32 devices in a mesh: groups: 2 (over y), wide: 4 (over z), narrow: 4 (over x, core).
Axes of the slice: x: 2, y: 2, z: 4, core: 2. Of those that a mesh axis runs over, the one named last changes fastest.
Arguments:
- zone_labels: int32 [512, 128, 128], P(('groups', 'wide'), 'narrow'), parts along dimension 0, may hold values from 0 to 2, as said below
- cell_scale: float32 [512, 128, 128], P(('groups', 'wide'), 'narrow'), parts along dimension 0, may hold values from 0.4 to 2.5
- diffusivity: float32 [3, 3], replicated, may hold values from 0.3 to 3
- decay_rates: float32 [3], replicated, may hold values from 0.0003 to 0.003
- load_field: float32 [512, 128, 128], P(('groups', 'wide'), 'narrow'), parts along dimension 0, may hold values from -4 to 4
Outputs:
- concentration: float32 [512, 128, 128], P(('groups', 'wide'), 'narrow'), parts along dimension 0
- residual: float32 [512, 128, 128], P(('groups', 'wide'), 'narrow'), parts along dimension 0
The draws below stay inside these ranges and needn't reach their ends.
There are 2 independent parts, one for each index of `groups`. The reference program is written for one: setup_inputs(seed, part) draws one part's arguments, and reference() takes and returns one part's arrays. A program takes and returns all parts, laid end to end along the dimension named above; an argument that names none is the same for every part. Nothing has to cross between parts.
Inputs may be any that keep to these rules, and one draw needn't show every extreme that they name: `zone_labels`: zone of each cell: 0 resting, 1 proliferative, 2 hypertrophic.
All inputs are finite; a program needn't handle non-finite values.
Results may differ from the reference program's by a relative error of at most 0.0003.
Values sent between devices are 32-bit elements; how exact they have to be, the bound alone decides.
No kernel may reach another device: no remote copies, remote signals or barrier semaphores. Data moves between devices by JAX's collectives and lax.ppermute only.
A program may use at most 64 MiB of HBM per device.

```python
import math
import jax
import jax.numpy as jnp
from jax import lax

CX = 64
CY = 32
NZ = 128
MARGIN = 4
ITERS = 2
ZONES = 3
BOXES_LONG = 4
BOXES_ACROSS = 4
BOXES = 16
NX = 256
NY = 128
EX = 72
EY = 40


def draw_zone_labels(key, part):
    key = jax.random.fold_in(key, 11)
    flip_key, pick_key = jax.random.split(key, 2)
    positions = jnp.arange(NX, dtype=jnp.int32)
    banded = jnp.broadcast_to((positions * ZONES // NX)[:, None, None], (NX, NY, NZ))
    flip_bits = jax.random.randint(flip_key, (NX, NY, NZ), 0, 2)
    pick_zone = jax.random.randint(pick_key, (NX, NY, NZ), 0, ZONES)
    return jnp.where(flip_bits == 1, pick_zone, banded).astype(jnp.int32)


def draw_load_field(key, part):
    key = jax.random.fold_in(key, 23)
    return jax.random.truncated_normal(key, -4.0, 4.0, (NX, NY, NZ), jnp.float32)


def shard_levels(key, shape, shards, low, largest):
    def one(dim, parts):
        draws = jax.random.uniform(jax.random.fold_in(jax.random.fold_in(key, 6), dim), (parts,), jnp.float32, low / len(shards), largest / len(shards))
        return jnp.repeat(jnp.exp(draws), shape[dim] // parts).reshape((-1,) + (1,) * (len(shape) - dim - 1))

    loudness = one(*shards[0])
    for cut in shards[1:]:
        loudness = loudness * one(*cut)
    return loudness


def setup_inputs(seed: int = 0, part: int = 0) -> dict:
    keys = jax.random.split(jax.random.key(seed), 6)
    part_keys = jax.random.split(jax.random.fold_in(keys[5], part), 6)
    zone_labels = draw_zone_labels(jax.random.fold_in(jax.random.fold_in(keys[5], part), 71), part)
    cell_scale = jnp.clip(jnp.exp(math.log(2.5) - 1.8325814 * jax.random.uniform(part_keys[1], (NX, NY, NZ), jnp.float32) ** shard_levels(part_keys[1], (NX, NY, NZ), ((0, 4), (1, 4)), -0.2, 0.2)), 0.4, 2.5)
    diffusivity = jnp.clip(jnp.exp(jax.random.uniform(keys[2], (ZONES, 3), jnp.float32, math.log(0.3), math.log(3.0))), 0.3, 3.0)
    decay_rates = jnp.clip(jnp.exp(jax.random.uniform(keys[3], (ZONES,), jnp.float32, math.log(0.0003), math.log(0.003))), 0.0003, 0.003)
    load_field = draw_load_field(jax.random.fold_in(jax.random.fold_in(keys[5], part), 71), part)
    return dict(zone_labels=zone_labels, cell_scale=cell_scale, diffusivity=diffusivity, decay_rates=decay_rates, load_field=load_field)


precise = lax.Precision.HIGHEST
cheb_center = 1.3
cheb_radius = 1.2
cheb_ratio = 1.3 / 1.2

def zone_lookup(zone_labels, zone_table):
    summed = jnp.zeros(zone_labels.shape, zone_table.dtype)
    for zone_id in range(zone_table.shape[0]):
        summed = summed + jnp.where(zone_labels == zone_id, zone_table[zone_id], jnp.zeros((), zone_table.dtype))
    return summed

def conductances(zone_labels, cell_scale, diffusivity):
    return jnp.stack([zone_lookup(zone_labels, diffusivity[:, direction]) * cell_scale for direction in range(3)])

def face_term(center, neighbour, own_cond, near_cond):
    return 0.5 * (own_cond + near_cond) * (center - neighbour)

def operate(window, cond_window, mass_term):
    center = window[1:-1, 1:-1]
    own_cond = cond_window[:, 1:-1, 1:-1]
    result = mass_term * center
    result = result + face_term(center, window[2:, 1:-1], own_cond[0], cond_window[0, 2:, 1:-1])
    result = result + face_term(center, window[:-2, 1:-1], own_cond[0], cond_window[0, :-2, 1:-1])
    result = result + face_term(center, window[1:-1, 2:], own_cond[1], cond_window[1, 1:-1, 2:])
    result = result + face_term(center, window[1:-1, :-2], own_cond[1], cond_window[1, 1:-1, :-2])
    deep_field = jnp.pad(center, ((0, 0), (0, 0), (1, 1)))
    deep_cond = jnp.pad(own_cond[2], ((0, 0), (0, 0), (1, 1)))
    result = result + face_term(center, deep_field[:, :, 2:], own_cond[2], deep_cond[:, :, 2:])
    result = result + face_term(center, deep_field[:, :, :-2], own_cond[2], deep_cond[:, :, :-2])
    return result

def sine_basis(length):
    indices = jnp.arange(1, length + 1, dtype=jnp.int32)
    phases = indices[:, None] * indices[None, :] % (2 * (length + 1))
    angles = jnp.pi * phases.astype(jnp.float32) / (length + 1)
    sine_table = jnp.sqrt(jnp.float32(2.0 / (length + 1))) * jnp.sin(angles)
    eigvals = 4.0 * jnp.sin(jnp.pi * indices.astype(jnp.float32) / (2.0 * (length + 1))) ** 2
    return (sine_table, eigvals)

def transform(source_field, tables):
    spectral = jnp.einsum('ai,ajk->ijk', tables[0][0], source_field, precision=precise)
    spectral = jnp.einsum('bj,ibk->ijk', tables[1][0], spectral, precision=precise)
    return jnp.einsum('ijc,ck->ijk', spectral, tables[2][0], precision=precise)

def box_solve(extended, box_means, tables):
    divisor = box_means[3] + box_means[0] * tables[0][1][:, None, None] + box_means[1] * tables[1][1][None, :, None] + box_means[2] * tables[2][1][None, None, :]
    return transform(transform(extended, tables) / divisor, tables)

def assemble(diagonal, couple_long, couple_across, across):
    box_count = diagonal.shape[0]
    row_ids = jnp.arange(box_count, dtype=jnp.int32)[:, None]
    col_ids = jnp.arange(box_count, dtype=jnp.int32)[None, :]
    nothing = jnp.zeros((), diagonal.dtype)
    matrix = jnp.where(row_ids == col_ids, diagonal[:, None], nothing)
    matrix = matrix - jnp.where(col_ids == row_ids + across, couple_long[:, None], nothing)
    matrix = matrix - jnp.where(row_ids == col_ids + across, couple_long[None, :], nothing)
    matrix = matrix - jnp.where(col_ids == row_ids + 1, couple_across[:, None], nothing)
    matrix = matrix - jnp.where(row_ids == col_ids + 1, couple_across[None, :], nothing)
    return matrix

def box_totals(source_field):
    return source_field.reshape(BOXES_LONG, CX, BOXES_ACROSS, CY, NZ).sum(axis=(1, 3, 4))

def box_average(source_field):
    return source_field.reshape(BOXES_LONG, CX, BOXES_ACROSS, CY, NZ).mean(axis=(1, 3, 4))

def reference(zone_labels, cell_scale, diffusivity, decay_rates, load_field):
    conduct = conductances(zone_labels, cell_scale, diffusivity)
    mass_term = zone_lookup(zone_labels, decay_rates)
    cond_window = jnp.pad(conduct, ((0, 0), (1, 1), (1, 1), (0, 0)))

    def apply_op(source_field):
        return operate(jnp.pad(source_field, ((1, 1), (1, 1), (0, 0))), cond_window, mass_term)
    ones_image = apply_op(jnp.ones_like(load_field))
    long_faces = 0.5 * (conduct[0, CX - 1::CX][:-1] + conduct[0, CX::CX])
    couple_long = long_faces.sum(axis=2).reshape(BOXES_LONG - 1, BOXES_ACROSS, CY).sum(axis=2)
    couple_long = jnp.pad(couple_long, ((0, 1), (0, 0)))
    across_faces = 0.5 * (conduct[1][:, CY - 1::CY][:, :-1] + conduct[1][:, CY::CY])
    couple_across = across_faces.sum(axis=2).reshape(BOXES_LONG, CX, BOXES_ACROSS - 1).sum(axis=1)
    couple_across = jnp.pad(couple_across, ((0, 0), (0, 1)))
    diagonal = box_totals(ones_image) + couple_long + jnp.pad(couple_long, ((1, 0), (0, 0)))[:-1]
    diagonal = diagonal + couple_across + jnp.pad(couple_across, ((0, 0), (1, 0)))[:, :-1]
    matrix = assemble(diagonal.reshape(-1), couple_long.reshape(-1), couple_across.reshape(-1), BOXES_ACROSS)
    factor = jnp.linalg.cholesky(matrix)
    box_means = jnp.stack([box_average(conduct[0]), box_average(conduct[1]), box_average(conduct[2]), box_average(mass_term)])
    tables = (sine_basis(EX), sine_basis(EY), sine_basis(NZ))

    def precondition(residual):
        padded = jnp.pad(residual, ((MARGIN, MARGIN), (MARGIN, MARGIN), (0, 0)))

        def one_box(box_index):
            box_row = box_index // BOXES_ACROSS
            box_col = box_index % BOXES_ACROSS
            anchor = jnp.zeros((), jnp.int32)
            extended = lax.dynamic_slice(padded, ((box_row * CX).astype(jnp.int32), (box_col * CY).astype(jnp.int32), anchor), (EX, EY, NZ))
            solved = box_solve(extended, box_means[:, box_row, box_col], tables)
            return solved[MARGIN:MARGIN + CX, MARGIN:MARGIN + CY]
        solved_boxes = lax.map(one_box, jnp.arange(BOXES, dtype=jnp.int32))
        local_field = solved_boxes.reshape(BOXES_LONG, BOXES_ACROSS, CX, CY, NZ).transpose(0, 2, 1, 3, 4).reshape(NX, NY, NZ)
        coarse = jax.scipy.linalg.cho_solve((factor, True), box_totals(residual).reshape(-1))
        coarse_field = jnp.repeat(jnp.repeat(coarse.reshape(BOXES_LONG, BOXES_ACROSS), CX, axis=0), CY, axis=1)
        return local_field + coarse_field[:, :, None]
    iterate = precondition(load_field) / cheb_center
    update = iterate
    rho_now = 1.0 / cheb_ratio
    for iteration in range(ITERS - 1):
        rho_next = 1.0 / (2.0 * cheb_ratio - rho_now)
        residual = load_field - apply_op(iterate)
        update = rho_next * rho_now * update + 2.0 * rho_next / cheb_radius * precondition(residual)
        iterate = iterate + update
        rho_now = rho_next
    return (iterate, load_field - apply_op(iterate))
```

```python
import jax
import jax.numpy as jnp
from jax import lax
from jax.sharding import PartitionSpec as P

MARGIN = 4


precise = lax.Precision.HIGHEST
cheb_center = 1.3
cheb_radius = 1.2
cheb_ratio = 1.3 / 1.2


def with_halo(array, sides, width):
    for axis, dim in sides:
        size, length = (lax.axis_size(axis), array.shape[dim])
        up = [(i, (i + 1) % size) for i in range(size - 1)]
        down = [(j, i) for i, j in up]
        last = lax.slice_in_dim(array, length - width, length, axis=dim)
        first = lax.slice_in_dim(array, 0, width, axis=dim)
        before = lax.ppermute(last, axis, up)
        after = lax.ppermute(first, axis, down)
        array = jnp.concatenate([before, array, after], axis=dim)
    return array


def with_faces(array, sides):
    for axis, dim in sides:
        size, length = (lax.axis_size(axis), array.shape[dim])
        own = lax.axis_index(axis)
        last = lax.slice_in_dim(array, length - 1, length, axis=dim)
        first = lax.slice_in_dim(array, 0, 1, axis=dim)
        place = jnp.arange(size, dtype=jnp.int32).reshape((size,) + (1,) * array.ndim)
        sent = jnp.where(place > own, last[None], first[None])
        got = lax.all_to_all(sent, axis, split_axis=0, concat_axis=0, tiled=True)
        nothing = jnp.zeros((), array.dtype)
        before = lax.dynamic_index_in_dim(got, jnp.maximum(own - 1, 0), 0, keepdims=False)
        after = lax.dynamic_index_in_dim(got, jnp.minimum(own + 1, size - 1), 0, keepdims=False)
        before = jnp.where(own > 0, before, nothing)
        after = jnp.where(own < size - 1, after, nothing)
        array = jnp.concatenate([before, array, after], axis=dim)
    return array


def zone_lookup(zone_labels, zone_table):
    summed = jnp.zeros(zone_labels.shape, zone_table.dtype)
    for zone_id in range(zone_table.shape[0]):
        summed = summed + jnp.where(
            zone_labels == zone_id, zone_table[zone_id], jnp.zeros((), zone_table.dtype)
        )
    return summed


def conductances(zone_labels, cell_scale, diffusivity):
    return jnp.stack(
        [zone_lookup(zone_labels, diffusivity[:, direction]) * cell_scale for direction in range(3)]
    )


def face_term(center, neighbour, own_cond, near_cond):
    return 0.5 * (own_cond + near_cond) * (center - neighbour)


def operate(window, cond_window, mass_term):
    center = window[1:-1, 1:-1]
    own_cond = cond_window[:, 1:-1, 1:-1]
    result = mass_term * center
    result = result + face_term(center, window[2:, 1:-1], own_cond[0], cond_window[0, 2:, 1:-1])
    result = result + face_term(center, window[:-2, 1:-1], own_cond[0], cond_window[0, :-2, 1:-1])
    result = result + face_term(center, window[1:-1, 2:], own_cond[1], cond_window[1, 1:-1, 2:])
    result = result + face_term(center, window[1:-1, :-2], own_cond[1], cond_window[1, 1:-1, :-2])
    deep_field = jnp.pad(center, ((0, 0), (0, 0), (1, 1)))
    deep_cond = jnp.pad(own_cond[2], ((0, 0), (0, 0), (1, 1)))
    result = result + face_term(center, deep_field[:, :, 2:], own_cond[2], deep_cond[:, :, 2:])
    result = result + face_term(center, deep_field[:, :, :-2], own_cond[2], deep_cond[:, :, :-2])
    return result


def sine_basis(length):
    indices = jnp.arange(1, length + 1, dtype=jnp.int32)
    phases = indices[:, None] * indices[None, :] % (2 * (length + 1))
    angles = jnp.pi * phases.astype(jnp.float32) / (length + 1)
    sine_table = jnp.sqrt(jnp.float32(2.0 / (length + 1))) * jnp.sin(angles)
    eigvals = 4.0 * jnp.sin(jnp.pi * indices.astype(jnp.float32) / (2.0 * (length + 1))) ** 2
    return (sine_table, eigvals)


def transform(source_field, tables):
    spectral = jnp.einsum("ai,ajk->ijk", tables[0][0], source_field, precision=precise)
    spectral = jnp.einsum("bj,ibk->ijk", tables[1][0], spectral, precision=precise)
    return jnp.einsum("ijc,ck->ijk", spectral, tables[2][0], precision=precise)


def box_solve(extended, box_means, tables):
    divisor = (
        box_means[3]
        + box_means[0] * tables[0][1][:, None, None]
        + box_means[1] * tables[1][1][None, :, None]
        + box_means[2] * tables[2][1][None, None, :]
    )
    return transform(transform(extended, tables) / divisor, tables)


def assemble(diagonal, couple_long, couple_across, across):
    box_count = diagonal.shape[0]
    row_ids = jnp.arange(box_count, dtype=jnp.int32)[:, None]
    col_ids = jnp.arange(box_count, dtype=jnp.int32)[None, :]
    nothing = jnp.zeros((), diagonal.dtype)
    matrix = jnp.where(row_ids == col_ids, diagonal[:, None], nothing)
    matrix = matrix - jnp.where(col_ids == row_ids + across, couple_long[:, None], nothing)
    matrix = matrix - jnp.where(row_ids == col_ids + across, couple_long[None, :], nothing)
    matrix = matrix - jnp.where(col_ids == row_ids + 1, couple_across[:, None], nothing)
    matrix = matrix - jnp.where(row_ids == col_ids + 1, couple_across[None, :], nothing)
    return matrix


def on_device(zone_labels, cell_scale, diffusivity, decay_rates, load_field):
    cells_long, cells_across, cells_deep = load_field.shape
    conduct = conductances(zone_labels, cell_scale, diffusivity)
    mass_term = zone_lookup(zone_labels, decay_rates)
    tables = (
        sine_basis(cells_long + 2 * MARGIN),
        sine_basis(cells_across + 2 * MARGIN),
        sine_basis(cells_deep),
    )
    box_means = jnp.stack(
        [jnp.mean(conduct[0]), jnp.mean(conduct[1]), jnp.mean(conduct[2]), jnp.mean(mass_term)]
    )
    long_count = lax.axis_size("wide")
    across_count = lax.axis_size("narrow")
    long_pos = lax.axis_index("wide")
    across_pos = lax.axis_index("narrow")
    own_box = long_pos * across_count + across_pos
    reach_width = 1
    cond_window = with_halo(conduct, (("wide", 1), ("narrow", 2)), 1)

    def margin_of(own_field):
        return with_halo(own_field, (("wide", 0), ("narrow", 1)), MARGIN)

    def final_residual(iterate):
        window = with_faces(iterate, (("wide", 0), ("narrow", 1)))
        return load_field - operate(window, cond_window, mass_term)

    first_pair = (load_field, margin_of(load_field))
    face_high_long = jnp.sum(
        0.5
        * (
            conduct[0, -1]
            + cond_window[0, reach_width + cells_long, reach_width : reach_width + cells_across]
        )
    )
    face_low_long = jnp.sum(
        0.5
        * (
            conduct[0, 0]
            + cond_window[0, reach_width - 1, reach_width : reach_width + cells_across]
        )
    )
    face_high_across = jnp.sum(
        0.5
        * (
            conduct[1][:, -1]
            + cond_window[1, reach_width : reach_width + cells_long, reach_width + cells_across]
        )
    )
    face_low_across = jnp.sum(
        0.5
        * (
            conduct[1][:, 0]
            + cond_window[1, reach_width : reach_width + cells_long, reach_width - 1]
        )
    )
    face_deep = jnp.sum(0.5 * conduct[2][:, :, 0]) + jnp.sum(0.5 * conduct[2][:, :, -1])
    diagonal = (
        jnp.sum(mass_term)
        + face_high_long
        + face_low_long
        + face_high_across
        + face_low_across
        + face_deep
    )
    couple_long = jnp.where(
        long_pos < long_count - 1, face_high_long, jnp.zeros((), face_high_long.dtype)
    )
    couple_across = jnp.where(
        across_pos < across_count - 1, face_high_across, jnp.zeros((), face_high_across.dtype)
    )
    box_count = long_count * across_count
    own_entries = jnp.pad(
        jnp.stack([diagonal, couple_long, couple_across])[None, None, :], ((0, 0), (0, 0), (0, 125))
    )
    entries = lax.all_to_all(
        jnp.broadcast_to(own_entries, (box_count, 1, 128)),
        ("wide", "narrow"),
        split_axis=0,
        concat_axis=0,
        tiled=True,
    )[:, 0, :3]
    factor = jnp.linalg.cholesky(
        assemble(entries[:, 0], entries[:, 1], entries[:, 2], across_count)
    )

    def coarse_value(own_part):
        all_sums = lax.all_gather(
            jnp.broadcast_to(jnp.sum(own_part), (8, 128)), ("wide", "narrow"), axis=0, tiled=True
        )[::8, 0]
        solved = jax.scipy.linalg.cho_solve((factor, True), all_sums)
        return lax.dynamic_index_in_dim(solved, own_box, 0, keepdims=False)

    def precondition(own_part, extended):
        coarse = coarse_value(own_part)
        solved = box_solve(extended, box_means, tables)[
            MARGIN : MARGIN + cells_long, MARGIN : MARGIN + cells_across
        ]
        return solved + coarse

    iterate = precondition(first_pair[0], first_pair[1]) / cheb_center
    update = iterate
    rho_now = 1.0 / cheb_ratio
    rho_next = 1.0 / (2.0 * cheb_ratio - rho_now)
    own_res = final_residual(iterate)
    own_res, ext_res = (own_res, margin_of(own_res))
    update = rho_next * rho_now * update + 2.0 * rho_next / cheb_radius * precondition(
        own_res, ext_res
    )
    iterate = iterate + update
    return (iterate, final_residual(iterate))


def solution(mesh):
    return jax.shard_map(
        on_device,
        mesh=mesh,
        in_specs=(
            P(("groups", "wide"), "narrow", None),
            P(("groups", "wide"), "narrow", None),
            P(),
            P(),
            P(("groups", "wide"), "narrow", None),
        ),
        out_specs=(P(("groups", "wide"), "narrow", None), P(("groups", "wide"), "narrow", None)),
        check_vma=False,
    )
```

```python
import functools

import jax
import jax.numpy as jnp
import numpy as np
from jax import lax
from jax.experimental import pallas as pl
from jax.experimental.pallas import tpu as pltpu
from jax.sharding import PartitionSpec as P

MARGIN = 4
REACH = MARGIN + 1
EDGE = 8

precise = lax.Precision.HIGHEST
cheb_center = 1.3
cheb_radius = 1.2
cheb_ratio = 1.3 / 1.2
rho_first = 1.0 / cheb_ratio
rho_second = 1.0 / (2.0 * cheb_ratio - rho_first)

DIAGONAL, LONG_HIGH, LONG_LOW, ACROSS_HIGH, ACROSS_LOW, LOAD_SUM, IMAGE_SUM = range(7)
FLOW_LONG_HIGH, FLOW_LONG_LOW, FLOW_ACROSS_HIGH, FLOW_ACROSS_LOW = range(7, 11)
MEANS = range(11, 15)

VMEM = pl.BlockSpec(memory_space=pltpu.VMEM)
SMEM = pl.BlockSpec(memory_space=pltpu.SMEM)


def sine_basis(length):
    indices = np.arange(1, length + 1)
    phases = indices[:, None] * indices[None, :] % (2 * (length + 1))
    table = np.sqrt(2.0 / (length + 1)) * np.sin(np.pi * phases / (length + 1))
    eigvals = 4.0 * np.sin(np.pi * indices / (2.0 * (length + 1))) ** 2
    return table.astype(np.float32), eigvals.astype(np.float32)


def call(body, out_shape, in_specs, scratch=(), flops=0, moved=0):
    return pl.pallas_call(
        body,
        out_shape=out_shape,
        in_specs=in_specs,
        out_specs=jax.tree.map(lambda _: VMEM, out_shape),
        scratch_shapes=list(scratch),
        compiler_params=pltpu.CompilerParams(vmem_limit_bytes=30 * 2**20),
        cost_estimate=pl.CostEstimate(flops=flops, bytes_accessed=moved, transcendentals=0),
    )


def f32(*shape):
    return jax.ShapeDtypeStruct(shape, jnp.float32)


def dot(left, right):
    return lax.dot_general(
        left, right, (((1,), (0,)), ((), ())), precision=precise, preferred_element_type=jnp.float32
    )


class Box:
    def __init__(self, shape):
        self.long, self.across, self.deep = shape
        self.ex = self.long + 2 * MARGIN
        self.ey = self.across + 2 * MARGIN
        self.rows = self.long + 2 * REACH
        self.cols = self.across + 2 * EDGE
        self.flat = self.rows * self.cols


def tables_of(box):
    sine_x, eig_x = sine_basis(box.ex)
    sine_y, eig_y = sine_basis(box.ey)
    sine_z, eig_z = sine_basis(box.deep)
    skip = EDGE - MARGIN
    into_y = np.zeros((box.ey, box.cols), np.float32)
    into_y[:, skip : skip + box.ey] = sine_y
    from_y = sine_y[MARGIN : MARGIN + box.across]
    from_x = sine_x[MARGIN : MARGIN + box.long]
    spread = np.broadcast_to(eig_x[:, None], (box.ex, box.deep))
    return [
        jnp.asarray(np.ascontiguousarray(t))
        for t in (into_y, sine_x, from_x, from_y, sine_z, spread, eig_z[None, :], eig_y[None, :])
    ]


def box_solve(box, source, means, tables, row_mask, col_mask, spectral, middle, emit):
    into_y, into_x, from_x, from_y, sine_z, spread, eig_z, eig_y = tables
    deep = box.deep
    into_y = into_y[...] * col_mask
    into_x = into_x[...] * row_mask
    from_x, from_y, sine_z = from_x[...], from_y[...], sine_z[...]
    spectral_flat = spectral.reshape(box.ey * box.ex, deep)
    middle_flat = middle.reshape(box.long * box.ey, deep)
    for start in range(0, box.ex, 8):
        block = source[start : start + 8].reshape(8 * box.cols, deep)
        block = dot(block, sine_z).reshape(8, box.cols, deep)
        for row in range(0, 8, 2):
            pair = jnp.concatenate([block[row], block[row + 1]], axis=1)
            pair = dot(into_y, pair)
            for part in range(2):
                spectral_flat[pl.ds(start + row + part, box.ey, stride=box.ex), :] = pair[
                    :, part * deep : (part + 1) * deep
                ]
    base = means[3] + means[0] * spread[...] + means[2] * eig_z[...]
    for col in range(0, box.ey, 2):
        pair = jnp.concatenate([spectral[col], spectral[col + 1]], axis=1)
        pair = dot(into_x, pair)
        pair = jnp.concatenate(
            [
                pair[:, part * deep : (part + 1) * deep]
                / (base + means[1] * eig_y[0, col + part])
                for part in range(2)
            ],
            axis=1,
        )
        pair = dot(from_x, pair)
        for part in range(2):
            middle_flat[pl.ds(col + part, box.long, stride=box.ey), :] = pair[
                :, part * deep : (part + 1) * deep
            ]
    for start in range(0, box.long, 8):
        parts = []
        for row in range(start, start + 8, 2):
            pair = jnp.concatenate([middle[row], middle[row + 1]], axis=1)
            pair = dot(from_y, pair)
            parts += [pair[:, :deep], pair[:, deep:]]
        emit(start, dot(jnp.concatenate(parts, axis=0), sine_z))


def position():
    long_pos, across_pos = lax.axis_index("wide"), lax.axis_index("narrow")
    return long_pos, across_pos, lax.axis_size("wide"), lax.axis_size("narrow")


def as_float(flag):
    return jnp.where(flag, jnp.float32(1.0), jnp.float32(0.0))


def row_of(stride, col, count, first=0):
    return pl.ds(first * stride + col, count, stride=stride)


def widths():
    return (MARGIN, REACH, REACH)


def pack_columns(box, fields, lows, highs, wides, up, down):
    total = sum(wides)
    corner = total * box.long
    place = 0
    for field, low, high, wide in zip(fields, lows, highs, wides):
        for step in range(wide):
            for target, col in ((up, box.across - wide + step), (down, step)):
                values = field[row_of(box.across, col, box.long), :]
                target[place * box.long : (place + 1) * box.long, :] = values.astype(jnp.float32)
                at = corner + 2 * REACH * place
                target[at : at + wide, :] = low[row_of(box.across, col, wide), :]
                target[at + REACH : at + REACH + wide, :] = high[row_of(box.across, col, wide), :]
            place += 1


def message_rows(box, wides):
    total = sum(wides)
    return -(-(total * (box.long + 2 * REACH)) // 8) * 8


def pack_inputs(box, zone, scale, load, low, high, up, down):
    edges = np.cumsum((0,) + widths())

    def part(ref, index):
        size = widths()[index] * box.across
        start = int(edges[index]) * box.across
        return ref.reshape(sum(widths()) * box.across, box.deep).at[start : start + size]

    flat = [ref.reshape(box.long * box.across, box.deep) for ref in (load, scale, zone)]
    lows = [part(low, index) for index in range(3)]
    highs = [part(high, index) for index in range(3)]
    pack_columns(box, flat, lows, highs, widths(), up, down)


def fill_window(box, window, own, low, high, left, right, wide, place, total, add=None):
    flat = window.reshape(box.flat, box.deep)
    nothing = jnp.zeros((box.rows, EDGE, box.deep), jnp.float32)
    window[:, :EDGE, :] = nothing
    window[:, EDGE + box.across :, :] = nothing
    if add is None:
        add = lambda values, row_side, col_side: values
    inner = slice(EDGE, EDGE + box.across)
    first, last = REACH, REACH + box.long
    if wide < REACH:
        blank = jnp.zeros((1, box.across, box.deep), jnp.float32)
        window[0:1, inner, :] = blank
        window[box.rows - 1 :, inner, :] = blank
    window[first:last, inner, :] = add(own[...].astype(jnp.float32), 0, 0)
    window[first - wide : first, inner, :] = add(low, -1, 0)
    window[last : last + wide, inner, :] = add(high, 1, 0)
    corner = total * box.long
    for step in range(wide):
        for source, col, side in (
            (left, EDGE - wide + step, -1),
            (right, EDGE + box.across + step, 1),
        ):
            at = (place + step) * box.long
            values = source[at : at + box.long, :]
            flat[row_of(box.cols, col, box.long, first), :] = add(values, 0, side)
            at = corner + 2 * REACH * (place + step)
            values = source[at : at + wide, :]
            flat[row_of(box.cols, col, wide, first - wide), :] = add(values, -1, side)
            values = source[at + REACH : at + REACH + wide, :]
            flat[row_of(box.cols, col, wide, last), :] = add(values, 1, side)


def negative_image(row, x, x_next, flow_before, weights):
    to_long, to_across, to_deep, mass = weights
    rows, lanes = x.shape
    flow_long = to_long[row] * (x_next - x)
    flow_across = to_across[row] * (pltpu.roll(x, rows - 1, 0) - x)
    flow_deep = to_deep[row] * (pltpu.roll(x, lanes - 1, 1) - x)
    total = flow_long - flow_before - mass[row] * x
    total = total + (flow_across - pltpu.roll(flow_across, 1, 0))
    total = total + (flow_deep - pltpu.roll(flow_deep, 1, 1))
    return total, flow_long


def first_solve(
    box,
    zone,
    scale,
    load,
    low,
    high,
    left,
    right,
    diffusivity,
    decay,
    *rest,
):
    tables = rest[:8]
    to_long, to_across, to_deep, mass, load_window, local, told = rest[8:15]
    zone_window, scale_window, spectral, middle = rest[15:]
    wides = widths()
    total = sum(wides)
    places = np.cumsum((0,) + wides)
    own = (load, scale, zone)
    for index, window in enumerate((load_window, scale_window, zone_window)):
        part = slice(int(places[index]), int(places[index + 1]))
        fill_window(
            box, window, own[index], low[part], high[part], left, right, wides[index], part.start, total
        )
    half = [[0.5 * diffusivity[z, d] for d in range(3)] for z in range(3)]
    rates = [decay[z] for z in range(3)]
    lane = lax.broadcasted_iota(jnp.int32, (box.cols, box.deep), 1)
    ends = jnp.where((lane == 0) | (lane == box.deep - 1), jnp.float32(1.0), jnp.float32(0.0))
    not_last = jnp.where(lane == box.deep - 1, jnp.float32(0.0), jnp.float32(1.0))

    def looked_up(labels, values):
        return jnp.where(labels == 0.0, values[0], jnp.where(labels == 1.0, values[1], values[2]))

    def halves(row):
        labels, factor = zone_window[row], scale_window[row]
        return [looked_up(labels, [half[z][d] for z in range(3)]) * factor for d in range(3)] + [
            looked_up(labels, rates)
        ]

    def set_row(row, own_halves, next_long):
        to_long[row] = own_halves[0] + next_long
        to_across[row] = own_halves[1] + pltpu.roll(own_halves[1], box.cols - 1, 0)
        to_deep[row] = (own_halves[2] + pltpu.roll(own_halves[2], box.deep - 1, 1)) * not_last
        mass[row] = own_halves[3] + own_halves[2] * ends

    def plain_row(row, now):
        later = halves(row + 1)
        set_row(row, now, later[0])
        return later

    def own_row(row, carry):
        now, sums = carry
        later = plain_row(row, now)
        inner = slice(EDGE, EDGE + box.across)
        sums = [s + v[inner] for s, v in zip(sums, now)]
        return later, sums

    first, last = REACH, REACH + box.long
    now = lax.fori_loop(0, first, plain_row, halves(0))
    nothing = jnp.zeros((box.across, box.deep), jnp.float32)
    now, sums = lax.fori_loop(first, last, own_row, (now, [nothing] * 4))
    now = lax.fori_loop(last, box.rows - 1, plain_row, now)
    set_row(box.rows - 1, now, jnp.zeros_like(now[0]))
    cells = box.long * box.across * box.deep
    totals = [jnp.sum(s, keepdims=True) for s in sums]
    means = [2.0 * t / cells for t in totals[:3]] + [totals[3] / cells]

    one = jnp.ones((1, 1), jnp.float32)
    collected = [jnp.zeros((8 * box.across, box.deep), jnp.float32)]

    def emit(start, values):
        values = values * (1.0 / cheb_center)
        rows = values.reshape(8, box.across, box.deep)
        local[start : start + 8] = rows
        own_mass = mass[first + start : first + start + 8, EDGE : EDGE + box.across, :]
        collected[0] = collected[0] + values * own_mass.reshape(values.shape)

    box_solve(
        box,
        load_window.at[1 : 1 + box.ex],
        means,
        tables,
        one,
        one,
        spectral,
        middle,
        emit,
    )
    long_pos, across_pos, long_count, across_count = position()
    has = [
        as_float(long_pos < long_count - 1),
        as_float(long_pos > 0),
        as_float(across_pos < across_count - 1),
        as_float(across_pos > 0),
    ]
    inner = slice(EDGE, EDGE + box.across)
    across_flat = to_across.reshape(box.flat, box.deep)
    local_flat = local.reshape(box.long * box.across, box.deep)
    faces = [
        (to_long[last - 1, inner], local[box.long - 1]),
        (to_long[first - 1, inner], local[0]),
        (
            across_flat[row_of(box.cols, EDGE + box.across - 1, box.long, first), :],
            local_flat[row_of(box.across, box.across - 1, box.long), :],
        ),
        (
            across_flat[row_of(box.cols, EDGE - 1, box.long, first), :],
            local_flat[row_of(box.across, 0, box.long), :],
        ),
    ]
    weights = [jnp.sum(w, keepdims=True) for w, _ in faces]
    flows = [jnp.sum(w * v, keepdims=True) for w, v in faces]
    own_mass = mass[first:last, inner, :]
    numbers = [jnp.sum(own_mass, keepdims=True).reshape(1, 1) + sum(weights)]
    numbers += [w * h for w, h in zip(weights, has)]
    numbers += [jnp.sum(load[...], keepdims=True).reshape(1, 1)]
    numbers += [jnp.sum(collected[0], keepdims=True) + sum(flows)]
    numbers += [f * h for f, h in zip(flows, has)]
    numbers += means
    lanes = lax.broadcasted_iota(jnp.int32, told.shape, 1)
    line = jnp.zeros(told.shape, jnp.float32)
    for index, number in enumerate(numbers):
        line = jnp.where(lanes == index, number, line)
    told[...] = line


def pack_iterate(box, own, low, high, up, down):
    flat = [own.reshape(box.long * box.across, box.deep)]
    low = low.reshape(REACH * box.across, box.deep)
    high = high.reshape(REACH * box.across, box.deep)
    pack_columns(box, flat, [low], [high], (REACH,), up, down)


def coarse_solve(told, answers, solved):
    count, width = solved.shape
    across = lax.axis_size("narrow")
    numbers = told[...]

    def column(index, values=numbers):
        return values[:, index : index + 1]

    image = column(IMAGE_SUM)
    image = image - column(FLOW_LONG_LOW, pltpu.roll(numbers, count - across, 0))
    image = image - column(FLOW_LONG_HIGH, pltpu.roll(numbers, across, 0))
    image = image - column(FLOW_ACROSS_LOW, pltpu.roll(numbers, count - 1, 0))
    image = image - column(FLOW_ACROSS_HIGH, pltpu.roll(numbers, 1, 0))
    rows = lax.broadcasted_iota(jnp.int32, (count, width), 0)
    cols = lax.broadcasted_iota(jnp.int32, (count, width), 1)
    nothing = jnp.zeros((count, width), jnp.float32)
    matrix = jnp.where(cols == rows, column(DIAGONAL), nothing)
    matrix = matrix - jnp.where(cols == rows + across, column(LONG_HIGH), nothing)
    matrix = matrix - jnp.where(cols == rows - across, column(LONG_LOW), nothing)
    matrix = matrix - jnp.where(cols == rows + 1, column(ACROSS_HIGH), nothing)
    matrix = matrix - jnp.where(cols == rows - 1, column(ACROSS_LOW), nothing)
    matrix = jnp.where(cols == count, column(LOAD_SUM), matrix)
    matrix = jnp.where(cols == count + 1, image, matrix)
    solved[...] = matrix

    def eliminate(step, _):
        values = solved[...]
        pivot_row = solved[pl.ds(step, 1), :]
        at_step = cols == step
        factors = jnp.sum(jnp.where(at_step, values, nothing), axis=1, keepdims=True)
        pivot = jnp.sum(jnp.where(at_step[:1], pivot_row, nothing[:1]), axis=1, keepdims=True)
        pivot_row = pivot_row / pivot
        solved[...] = jnp.where(rows == step, pivot_row, values - factors * pivot_row)
        return 0

    lax.fori_loop(0, count, eliminate, 0)
    values = solved[...]
    lanes = lax.broadcasted_iota(jnp.int32, answers.shape, 1)
    answers[...] = jnp.where(
        lanes == 0, values[:, count : count + 1], values[:, count + 1 : count + 2]
    )


def second_solve(box, local, low, high, left, right, solved, told, *rest):
    to_long, to_across, to_deep, mass, load_window = rest[:5]
    tables = rest[5:13]
    iterate, top, bottom, last_col, first_col = rest[13:18]
    window, residual, spectral, middle = rest[18:]
    long_pos, across_pos, long_count, across_count = position()
    count = long_count * across_count
    own_box = long_pos * across_count + across_pos

    def coarse(row_side, col_side, lane):
        there_long, there_across = long_pos + row_side, across_pos + col_side
        inside = (
            (there_long >= 0)
            & (there_long < long_count)
            & (there_across >= 0)
            & (there_across < across_count)
        )
        place = jnp.clip(there_long * across_count + there_across, 0, count - 1)
        return solved[pl.ds(place, 1), lane : lane + 1] * as_float(inside)

    shifts = {
        (row_side, col_side): coarse(row_side, col_side, 0) * (1.0 / cheb_center)
        for row_side in (-1, 0, 1)
        for col_side in (-1, 0, 1)
    }

    def add(values, row_side, col_side):
        shift = shifts[row_side, col_side]
        if values.ndim == 3:
            shift = shift.reshape(1, 1, 1)
        return values + shift

    fill_window(box, window, local, low[...], high[...], left, right, REACH, 0, REACH, add)
    weights = (to_long, to_across, to_deep, mass)

    def one_row(row, flow):
        image, flow = negative_image(row, window[row], window[row + 1], flow, weights)
        residual[row - 1] = load_window[row] + image
        return flow

    flow = to_long[0] * (window[1] - window[0])
    lax.fori_loop(1, 1 + box.ex, one_row, flow)
    inner = slice(EDGE, EDGE + box.across)
    first = REACH
    means = [told[0:1, index : index + 1] for index in MEANS]
    row_ids = lax.broadcasted_iota(jnp.int32, (1, box.ex), 1)
    col_ids = lax.broadcasted_iota(jnp.int32, (1, box.cols), 1)
    row_mask = jnp.where(row_ids < MARGIN, as_float(long_pos > 0), 1.0)
    row_mask = jnp.where(row_ids >= MARGIN + box.long, as_float(long_pos < long_count - 1), row_mask)
    col_mask = jnp.where(col_ids < EDGE, as_float(across_pos > 0), 1.0)
    col_mask = jnp.where(
        col_ids >= EDGE + box.across, as_float(across_pos < across_count - 1), col_mask
    )
    own_c = coarse(0, 0, 0) * (1.0 - 1.0 / cheb_center) - coarse(0, 0, 1)
    keep = 1.0 + rho_second * rho_first
    gain = 2.0 * rho_second / cheb_radius

    def emit(start, values):
        rows = (values + own_c).reshape(8, box.across, box.deep)
        before = window[first + start : first + start + 8, inner, :]
        iterate[start : start + 8] = keep * before + gain * rows

    box_solve(box, residual, means, tables, row_mask, col_mask, spectral, middle, emit)
    top[...] = iterate[box.long - 1]
    bottom[...] = iterate[0]
    flat = iterate.reshape(box.long * box.across, box.deep)
    last_col[...] = flat[row_of(box.across, box.across - 1, box.long), :]
    first_col[...] = flat[row_of(box.across, 0, box.long), :]


def last_residual(box, load, iterate, low, high, left, right, to_long, to_across, to_deep, mass, out):
    first = REACH
    left_col, right_col = left[...], right[...]
    rows = lax.broadcasted_iota(jnp.int32, (box.cols, box.deep), 0)
    inner = slice(EDGE, EDGE + box.across)
    blank = jnp.zeros((EDGE, box.deep), jnp.float32)
    weights = (to_long, to_across, to_deep, mass)

    def padded(values):
        return jnp.concatenate([blank, values, blank], axis=0)

    def own(row):
        values = padded(iterate[row])
        values = jnp.where(rows == EDGE - 1, left[pl.ds(row, 1), :], values)
        return jnp.where(rows == EDGE + box.across, right[pl.ds(row, 1), :], values)

    def one_row(row, carry):
        now, flow = carry
        later = own(row + 1)
        image, flow = negative_image(first + row, now, later, flow, weights)
        out[row] = load[row] + image[inner]
        return later, flow

    now = own(0)
    flow = to_long[first - 1] * (now - padded(low[...]))
    now, flow = lax.fori_loop(0, box.long - 1, one_row, (now, flow))
    row = box.long - 1
    image, _ = negative_image(first + row, now, padded(high[...]), flow, weights)
    out[row] = load[row] + image[inner]


def exchange(axis, last, first):
    size = lax.axis_size(axis)
    up = [(i, i + 1) for i in range(size - 1)]
    down = [(j, i) for i, j in up]
    return lax.ppermute(last, axis, up), lax.ppermute(first, axis, down)


def on_device(zone, scale, diffusivity, decay, load):
    box = Box(load.shape)
    long, across, deep = load.shape
    count = lax.axis_size("wide") * lax.axis_size("narrow")
    tables = tables_of(box)
    wides = widths()

    def edge(high):
        parts = []
        for field, wide in zip((load, scale, zone), wides):
            start = long - wide if high else 0
            parts.append(lax.slice_in_dim(field, start, start + wide, axis=0).astype(jnp.float32))
        return jnp.concatenate(parts, axis=0)

    low, high = exchange("wide", edge(True), edge(False))
    message = f32(message_rows(box, wides), deep)
    up, down = call(
        functools.partial(pack_inputs, box), (message, message), [VMEM] * 5
    )(zone, scale, load, low, high)
    left, right = exchange("narrow", up, down)
    window = f32(box.rows, box.cols, deep)
    window_scratch = pltpu.VMEM(window.shape, jnp.float32)
    spectral = pltpu.VMEM((box.ey, box.ex, deep), jnp.float32)
    middle = pltpu.VMEM((box.long, box.ey, deep), jnp.float32)
    to_long, to_across, to_deep, mass, load_window, local, told = call(
        functools.partial(first_solve, box),
        (window,) * 5 + (f32(long, across, deep), f32(count, 128)),
        [VMEM] * 7 + [SMEM] * 2 + [VMEM] * 8,
        [window_scratch] * 2 + [spectral, middle],
    )(zone, scale, load, low, high, left, right, diffusivity, decay, *tables)
    low, high = exchange("wide", local[long - REACH :], local[:REACH])
    all_told = lax.all_to_all(
        told.reshape(count, 1, 128), ("wide", "narrow"), split_axis=0, concat_axis=0, tiled=True
    ).reshape(count, 128)
    message = f32(message_rows(box, (REACH,)), deep)
    up, down = call(
        functools.partial(pack_iterate, box), (message, message), [VMEM] * 3
    )(local, low, high)
    left, right = exchange("narrow", up, down)
    solved_width = -(-(count + 2) // 128) * 128
    solved = call(
        coarse_solve,
        f32(count, 128),
        [VMEM],
        [pltpu.VMEM((count, solved_width), jnp.float32)],
    )(all_told)
    iterate, top, bottom, last_col, first_col = call(
        functools.partial(second_solve, box),
        (
            f32(long, across, deep),
            f32(across, deep),
            f32(across, deep),
            f32(long, deep),
            f32(long, deep),
        ),
        [VMEM] * 20,
        [window_scratch, pltpu.VMEM((box.ex, box.cols, deep), jnp.float32), spectral, middle],
    )(
        local,
        low,
        high,
        left,
        right,
        solved,
        told,
        to_long,
        to_across,
        to_deep,
        mass,
        load_window,
        *tables,
    )
    low, high = exchange("wide", top, bottom)
    left, right = exchange("narrow", last_col, first_col)
    residual = call(
        functools.partial(last_residual, box), f32(long, across, deep), [VMEM] * 10
    )(load, iterate, low, high, left, right, to_long, to_across, to_deep, mass)
    return iterate, residual


def solution(mesh):
    split = P(("groups", "wide"), "narrow", None)
    return jax.shard_map(
        on_device,
        mesh=mesh,
        in_specs=(split, split, P(), P(), split),
        out_specs=(split, split),
        check_vma=False,
    )
```

```python
import functools

import jax
import jax.numpy as jnp
import ml_dtypes
import numpy as np
from jax import lax
from jax.experimental import pallas as pl
from jax.experimental.pallas import tpu as pltpu
from jax.sharding import PartitionSpec as P

MARGIN = 4
REACH = MARGIN + 1
EDGE = 8

cheb_center = 1.3
cheb_radius = 1.2
cheb_ratio = 1.3 / 1.2
rho_first = 1.0 / cheb_ratio
rho_second = 1.0 / (2.0 * cheb_ratio - rho_first)

DIAGONAL, LONG_HIGH, LONG_LOW, ACROSS_HIGH, ACROSS_LOW, LOAD_SUM, IMAGE_SUM = range(7)
FLOW_LONG_HIGH, FLOW_LONG_LOW, FLOW_ACROSS_HIGH, FLOW_ACROSS_LOW = range(7, 11)

VMEM = pl.BlockSpec(memory_space=pltpu.VMEM)
SMEM = pl.BlockSpec(memory_space=pltpu.SMEM)


def sine_basis(length):
    indices = np.arange(1, length + 1)
    phases = indices[:, None] * indices[None, :] % (2 * (length + 1))
    table = np.sqrt(2.0 / (length + 1)) * np.sin(np.pi * phases / (length + 1))
    eigvals = 4.0 * np.sin(np.pi * indices / (2.0 * (length + 1))) ** 2
    return table.astype(np.float32), eigvals.astype(np.float32)


def call(body, out_shape, in_specs, scratch=(), flops=0, moved=0):
    return pl.pallas_call(
        body,
        out_shape=out_shape,
        in_specs=in_specs,
        out_specs=jax.tree.map(lambda _: VMEM, out_shape),
        scratch_shapes=list(scratch),
        compiler_params=pltpu.CompilerParams(vmem_limit_bytes=30 * 2**20),
        cost_estimate=pl.CostEstimate(flops=flops, bytes_accessed=moved, transcendentals=0),
    )


def f32(*shape):
    return jax.ShapeDtypeStruct(shape, jnp.float32)


class Box:
    def __init__(self, shape):
        self.long, self.across, self.deep = shape
        self.ex = self.long + 2 * MARGIN
        self.ey = self.across + 2 * MARGIN
        self.rows = self.long + 2 * REACH
        self.cols = self.across + 2 * EDGE
        self.flat = self.rows * self.cols


def pieces(values, count):
    parts = []
    for _ in range(count):
        part = values.astype(jnp.bfloat16)
        parts.append(part)
        values = values - part.astype(jnp.float32)
    return parts


def left_table(table, depth, count):
    rows, cols = table.shape
    wide = np.zeros((rows, depth), np.float32)
    wide[:, :cols] = table
    parts = []
    rest = wide
    for _ in range(count):
        part = rest.astype(ml_dtypes.bfloat16)
        parts.append(part)
        rest = rest - part.astype(np.float32)
    blank = np.zeros_like(parts[0])
    lines = []
    for index in range(count):
        used = count - index if count > 2 else count
        lines.append(np.concatenate([parts[index]] * used + [blank] * (count - used), axis=1))
    return np.concatenate(lines, axis=0)


def right_tables(table):
    rest, parts = table, []
    for _ in range(3):
        part = rest.astype(ml_dtypes.bfloat16)
        parts.append(part)
        rest = rest - part.astype(np.float32)
    both = np.concatenate([parts[0], parts[1]], axis=1)
    return np.concatenate([both, both], axis=0), np.concatenate([parts[2], parts[0]], axis=0)


def padded(size):
    return -(-size // 16) * 16


FORWARD, BACKWARD = 2, 3


def tables_of(box):
    sine_x, eig_x = sine_basis(box.ex)
    sine_y, eig_y = sine_basis(box.ey)
    sine_z, eig_z = sine_basis(box.deep)
    skip = EDGE - MARGIN
    into_y = np.zeros((box.ey, box.cols), np.float32)
    into_y[:, skip : skip + box.ey] = sine_y
    from_y = sine_y[MARGIN : MARGIN + box.across]
    from_x = sine_x[MARGIN : MARGIN + box.long]
    spread = np.broadcast_to(eig_x[:, None], (box.ex, box.deep))
    main_z, rest_z = right_tables(sine_z)
    return [
        jnp.asarray(np.ascontiguousarray(t))
        for t in (
            left_table(into_y, box.cols, FORWARD),
            left_table(sine_x, padded(box.ex), FORWARD),
            left_table(from_x, padded(box.ex), BACKWARD),
            left_table(from_y, padded(box.ey), BACKWARD),
            main_z,
            rest_z,
            spread,
            eig_z[None, :],
            eig_y[None, :],
        )
    ]


N_TABLES = 9


def bf16_dot(left, right):
    return lax.dot_general(
        left, right, (((1,), (0,)), ((), ())), preferred_element_type=jnp.float32
    )


def dot_left(table, values, count, rows):
    total = bf16_dot(table, jnp.concatenate(pieces(values, count), axis=0))
    return sum(total[index * rows : (index + 1) * rows] for index in range(1, count)) + total[:rows]


def dot_right(values, main, rest, count):
    deep = values.shape[1]
    parts = pieces(values, count)
    total = bf16_dot(jnp.concatenate(parts[:2], axis=1), main)
    result = total[:, :deep] + total[:, deep:]
    if count == 3:
        result = result + bf16_dot(jnp.concatenate([parts[0], parts[2]], axis=1), rest)
    return result


def with_rows(values, rows):
    if values.shape[0] == rows:
        return values
    blank = jnp.zeros((rows - values.shape[0],) + values.shape[1:], values.dtype)
    return jnp.concatenate([values, blank], axis=0)


def box_solve(box, source, means, tables, row_mask, col_mask, spectral, middle, emit):
    into_y, into_x, from_x, from_y, main_z, rest_z, spread, eig_z, eig_y = tables
    deep = box.deep
    deep_x, deep_y = padded(box.ex), padded(box.ey)
    into_y, into_x = into_y[...], into_x[...]
    if col_mask is not None:
        mask = jnp.concatenate([col_mask] * FORWARD, axis=1)
        into_y = (into_y.astype(jnp.float32) * mask).astype(jnp.bfloat16)
        mask = jnp.concatenate([row_mask] * FORWARD, axis=1)
        into_x = (into_x.astype(jnp.float32) * mask).astype(jnp.bfloat16)
    from_x, from_y, main_z, rest_z = from_x[...], from_y[...], main_z[...], rest_z[...]
    spectral_flat = spectral.reshape(box.ey * deep_x, deep)
    middle_flat = middle.reshape(box.long * deep_y, deep)
    if deep_x > box.ex:
        spectral[:, box.ex :, :] = jnp.zeros((box.ey, deep_x - box.ex, deep), jnp.float32)
    if deep_y > box.ey:
        middle[:, box.ey :, :] = jnp.zeros((box.long, deep_y - box.ey, deep), jnp.float32)
    for start in range(0, box.ex, 8):
        block = source[start : start + 8].reshape(8 * box.cols, deep)
        block = dot_right(block, main_z, rest_z, FORWARD).reshape(8, box.cols, deep)
        for row in range(0, 8, 2):
            pair = jnp.concatenate([block[row], block[row + 1]], axis=1)
            pair = dot_left(into_y, pair, FORWARD, box.ey)
            for part in range(2):
                spectral_flat[pl.ds(start + row + part, box.ey, stride=deep_x), :] = pair[
                    :, part * deep : (part + 1) * deep
                ]
    base = means[3] + means[0] * spread[...] + means[2] * eig_z[...]
    for col in range(0, box.ey, 2):
        pair = jnp.concatenate([spectral[col], spectral[col + 1]], axis=1)
        pair = dot_left(into_x, pair, FORWARD, box.ex)
        pair = jnp.concatenate(
            [
                pair[:, part * deep : (part + 1) * deep]
                / (base + means[1] * eig_y[0, col + part])
                for part in range(2)
            ],
            axis=1,
        )
        pair = dot_left(from_x, with_rows(pair, deep_x), BACKWARD, box.long)
        for part in range(2):
            middle_flat[pl.ds(col + part, box.long, stride=deep_y), :] = pair[
                :, part * deep : (part + 1) * deep
            ]
    for start in range(0, box.long, 8):
        parts = []
        for row in range(start, start + 8, 2):
            pair = jnp.concatenate([middle[row], middle[row + 1]], axis=1)
            pair = dot_left(from_y, pair, BACKWARD, box.across)
            parts += [pair[:, :deep], pair[:, deep:]]
        emit(start, dot_right(jnp.concatenate(parts, axis=0), main_z, rest_z, BACKWARD))


def position():
    long_pos, across_pos = lax.axis_index("wide"), lax.axis_index("narrow")
    return long_pos, across_pos, lax.axis_size("wide"), lax.axis_size("narrow")


def as_float(flag):
    return jnp.where(flag, jnp.float32(1.0), jnp.float32(0.0))


def row_of(stride, col, count, first=0):
    return pl.ds(first * stride + col, count, stride=stride)


def pack_columns(box, fields, lows, highs, wide, up, down):
    corner = len(fields) * wide * box.long
    place = 0
    for field, low, high in zip(fields, lows, highs):
        for step in range(wide):
            for target, col in ((up, box.across - wide + step), (down, step)):
                values = field[row_of(box.across, col, box.long), :]
                target[place * box.long : (place + 1) * box.long, :] = values.astype(jnp.float32)
                at = corner + 2 * REACH * place
                target[at : at + wide, :] = low[row_of(box.across, col, wide), :]
                target[at + REACH : at + REACH + wide, :] = high[row_of(box.across, col, wide), :]
            place += 1


def message_rows(box, count):
    return -(-(count * (box.long + 2 * REACH)) // 8) * 8


def pack_fields(box, wide, *refs):
    *fields, low, high, up, down = refs
    size = wide * box.across
    flat = [field.reshape(box.long * box.across, box.deep) for field in fields]
    sides = [
        [
            ref.reshape(len(fields) * size, box.deep).at[index * size : (index + 1) * size]
            for index in range(len(fields))
        ]
        for ref in (low, high)
    ]
    pack_columns(box, flat, sides[0], sides[1], wide, up, down)


def pack_edges(box, zone, scale, load, load_up, load_down, up, down, staged, sems):
    last = box.long
    copies = [
        (load.at[last - MARGIN :], load_up),
        (load.at[:MARGIN], load_down),
        (scale.at[last - REACH :], up.at[:REACH]),
        (scale.at[:REACH], down.at[:REACH]),
        (zone.at[last - REACH :], staged.at[0]),
        (zone.at[:REACH], staged.at[1]),
    ]
    copies = [
        pltpu.make_async_copy(source, target, sems.at[index])
        for index, (source, target) in enumerate(copies)
    ]
    for copy in copies:
        copy.start()
    for copy in copies:
        copy.wait()
    up[REACH:] = staged[0].astype(jnp.float32)
    down[REACH:] = staged[1].astype(jnp.float32)


def fill_window(box, window, own, low, high, left, right, wide, place, total, add=None):
    flat = window.reshape(box.flat, box.deep)
    nothing = jnp.zeros((box.rows, EDGE, box.deep), jnp.float32)
    window[:, :EDGE, :] = nothing
    window[:, EDGE + box.across :, :] = nothing
    if add is None:
        add = lambda values, row_side, col_side: values
    inner = slice(EDGE, EDGE + box.across)
    first, last = REACH, REACH + box.long
    if wide < REACH:
        blank = jnp.zeros((1, box.across, box.deep), jnp.float32)
        window[0:1, inner, :] = blank
        window[box.rows - 1 :, inner, :] = blank
    window[first:last, inner, :] = add(own[...].astype(jnp.float32), 0, 0)
    window[first - wide : first, inner, :] = add(low, -1, 0)
    window[last : last + wide, inner, :] = add(high, 1, 0)
    corner = total * box.long
    for step in range(wide):
        for source, col, side in (
            (left, EDGE - wide + step, -1),
            (right, EDGE + box.across + step, 1),
        ):
            at = (place + step) * box.long
            values = source[at : at + box.long, :]
            flat[row_of(box.cols, col, box.long, first), :] = add(values, 0, side)
            at = corner + 2 * REACH * (place + step)
            values = source[at : at + wide, :]
            flat[row_of(box.cols, col, wide, first - wide), :] = add(values, -1, side)
            values = source[at + REACH : at + REACH + wide, :]
            flat[row_of(box.cols, col, wide, last), :] = add(values, 1, side)


def negative_image(row, x, x_next, flow_before, weights):
    to_long, to_across, to_deep, mass = weights
    rows, lanes = x.shape
    flow_long = to_long[row] * (x_next - x)
    flow_across = to_across[row] * (pltpu.roll(x, rows - 1, 0) - x)
    flow_deep = to_deep[row] * (pltpu.roll(x, lanes - 1, 1) - x)
    total = flow_long - flow_before - mass[row] * x
    total = total + (flow_across - pltpu.roll(flow_across, 1, 0))
    total = total + (flow_deep - pltpu.roll(flow_deep, 1, 1))
    return total, flow_long


def looked_up(labels, values):
    return jnp.where(labels == 0, values[0], jnp.where(labels == 1, values[1], values[2]))


def box_means(box, zone, scale, diffusivity, decay, out):
    step = 4
    nothing = jnp.zeros((box.across, box.deep), jnp.float32)

    def some_rows(index, sums):
        for row in range(step):
            labels, factor = zone[index * step + row], scale[index * step + row]
            sums = [
                sums[d] + looked_up(labels, [diffusivity[z, d] for z in range(3)]) * factor
                for d in range(3)
            ] + [sums[3] + looked_up(labels, [decay[z] for z in range(3)])]
        return sums

    sums = lax.fori_loop(0, box.long // step, some_rows, [nothing] * 4)
    cells = box.long * box.across * box.deep
    lanes = lax.broadcasted_iota(jnp.int32, out.shape, 1)
    line = jnp.zeros(out.shape, jnp.float32)
    for index, values in enumerate(sums):
        line = jnp.where(lanes == index, jnp.sum(values, keepdims=True) / cells, line)
    out[...] = line


def means_of(ref):
    return [ref[0:1, index : index + 1] for index in range(4)]


def first_solve(box, load, low, high, left, right, means, *rest):
    tables = rest[:N_TABLES]
    window, local, spectral, middle = rest[N_TABLES:]
    fill_window(box, window, load, low[...], high[...], left, right, MARGIN, 0, MARGIN)

    def emit(start, values):
        values = values * (1.0 / cheb_center)
        local[start : start + 8] = values.reshape(8, box.across, box.deep)

    box_solve(
        box,
        window.at[1 : 1 + box.ex],
        means_of(means),
        tables,
        None,
        None,
        spectral,
        middle,
        emit,
    )


def weights_of(
    box,
    zone,
    scale,
    load,
    local,
    low,
    high,
    left,
    right,
    diffusivity,
    decay,
    to_long,
    to_across,
    to_deep,
    mass,
    told,
    zone_window,
    scale_window,
):
    for index, (window, own) in enumerate(((scale_window, scale), (zone_window, zone))):
        part = slice(index * REACH, (index + 1) * REACH)
        fill_window(
            box, window, own, low[part], high[part], left, right, REACH, part.start, 2 * REACH
        )
    half = [[0.5 * diffusivity[z, d] for d in range(3)] for z in range(3)]
    rates = [decay[z] for z in range(3)]
    lane = lax.broadcasted_iota(jnp.int32, (box.cols, box.deep), 1)
    ends = jnp.where((lane == 0) | (lane == box.deep - 1), jnp.float32(1.0), jnp.float32(0.0))
    not_last = jnp.where(lane == box.deep - 1, jnp.float32(0.0), jnp.float32(1.0))

    def one_row(row, before):
        labels, factor = zone_window[row], scale_window[row]
        now = [looked_up(labels, [half[z][d] for z in range(3)]) * factor for d in range(3)]
        to_across[row] = now[1] + pltpu.roll(now[1], box.cols - 1, 0)
        to_deep[row] = (now[2] + pltpu.roll(now[2], box.deep - 1, 1)) * not_last
        mass[row] = looked_up(labels, rates) + now[2] * ends
        to_long[jnp.maximum(row - 1, 0)] = before + now[0]
        return now[0]

    last_long = lax.fori_loop(0, box.rows - 2, one_row, jnp.zeros_like(ends), unroll=4)
    for row in range(box.rows - 2, box.rows):
        last_long = one_row(row, last_long)
    to_long[box.rows - 1] = last_long

    first, last = REACH, REACH + box.long
    inner = slice(EDGE, EDGE + box.across)
    step = 8
    nothing = jnp.zeros((box.across, box.deep), jnp.float32)

    def add_rows(index, sums):
        mass_sum, image_sum, load_sum = sums
        for row in range(step):
            row = index * step + row
            own_mass = mass[first + row, inner]
            mass_sum = mass_sum + own_mass
            image_sum = image_sum + own_mass * local[row]
            load_sum = load_sum + load[row]
        return mass_sum, image_sum, load_sum

    mass_sum, image_sum, load_sum = lax.fori_loop(0, box.long // step, add_rows, (nothing,) * 3)
    long_pos, across_pos, long_count, across_count = position()
    has = [
        as_float(long_pos < long_count - 1),
        as_float(long_pos > 0),
        as_float(across_pos < across_count - 1),
        as_float(across_pos > 0),
    ]
    across_flat = to_across.reshape(box.flat, box.deep)
    local_flat = local.reshape(box.long * box.across, box.deep)
    faces = [
        (to_long[last - 1, inner], local[box.long - 1]),
        (to_long[first - 1, inner], local[0]),
        (
            across_flat[row_of(box.cols, EDGE + box.across - 1, box.long, first), :],
            local_flat[row_of(box.across, box.across - 1, box.long), :],
        ),
        (
            across_flat[row_of(box.cols, EDGE - 1, box.long, first), :],
            local_flat[row_of(box.across, 0, box.long), :],
        ),
    ]
    weights = [jnp.sum(w, keepdims=True) for w, _ in faces]
    flows = [jnp.sum(w * v, keepdims=True) for w, v in faces]
    numbers = [jnp.sum(mass_sum, keepdims=True) + sum(weights)]
    numbers += [w * h for w, h in zip(weights, has)]
    numbers += [jnp.sum(load_sum, keepdims=True)]
    numbers += [jnp.sum(image_sum, keepdims=True) + sum(flows)]
    numbers += [f * h for f, h in zip(flows, has)]
    lanes = lax.broadcasted_iota(jnp.int32, told.shape, 1)
    line = jnp.zeros(told.shape, jnp.float32)
    for index, number in enumerate(numbers):
        line = jnp.where(lanes == index, number, line)
    told[...] = line


def coarse_solve(told, answers, solved):
    count, width = solved.shape
    across = lax.axis_size("narrow")
    numbers = told[...]

    def column(index, values=numbers):
        return values[:, index : index + 1]

    image = column(IMAGE_SUM)
    image = image - column(FLOW_LONG_LOW, pltpu.roll(numbers, count - across, 0))
    image = image - column(FLOW_LONG_HIGH, pltpu.roll(numbers, across, 0))
    image = image - column(FLOW_ACROSS_LOW, pltpu.roll(numbers, count - 1, 0))
    image = image - column(FLOW_ACROSS_HIGH, pltpu.roll(numbers, 1, 0))
    rows = lax.broadcasted_iota(jnp.int32, (count, width), 0)
    cols = lax.broadcasted_iota(jnp.int32, (count, width), 1)
    nothing = jnp.zeros((count, width), jnp.float32)
    matrix = jnp.where(cols == rows, column(DIAGONAL), nothing)
    matrix = matrix - jnp.where(cols == rows + across, column(LONG_HIGH), nothing)
    matrix = matrix - jnp.where(cols == rows - across, column(LONG_LOW), nothing)
    matrix = matrix - jnp.where(cols == rows + 1, column(ACROSS_HIGH), nothing)
    matrix = matrix - jnp.where(cols == rows - 1, column(ACROSS_LOW), nothing)
    matrix = jnp.where(cols == count, column(LOAD_SUM), matrix)
    matrix = jnp.where(cols == count + 1, image, matrix)
    solved[...] = matrix

    def eliminate(step, _):
        values = solved[...]
        pivot_row = solved[pl.ds(step, 1), :]
        at_step = cols == step
        factors = jnp.sum(jnp.where(at_step, values, nothing), axis=1, keepdims=True)
        pivot = jnp.sum(jnp.where(at_step[:1], pivot_row, nothing[:1]), axis=1, keepdims=True)
        pivot_row = pivot_row / pivot
        solved[...] = jnp.where(rows == step, pivot_row, values - factors * pivot_row)
        return 0

    lax.fori_loop(0, count, eliminate, 0)
    values = solved[...]
    lanes = lax.broadcasted_iota(jnp.int32, answers.shape, 1)
    answers[...] = jnp.where(
        lanes == 0, values[:, count : count + 1], values[:, count + 1 : count + 2]
    )


def second_solve(box, local, low, high, left, right, solved, means, *rest):
    to_long, to_across, to_deep, mass, load_window = rest[:5]
    tables = rest[5 : 5 + N_TABLES]
    iterate, top, bottom, last_col, first_col = rest[5 + N_TABLES : 10 + N_TABLES]
    window, residual, spectral, middle = rest[10 + N_TABLES :]
    long_pos, across_pos, long_count, across_count = position()
    count = long_count * across_count
    own_box = long_pos * across_count + across_pos

    def coarse(row_side, col_side, lane):
        there_long, there_across = long_pos + row_side, across_pos + col_side
        inside = (
            (there_long >= 0)
            & (there_long < long_count)
            & (there_across >= 0)
            & (there_across < across_count)
        )
        place = jnp.clip(there_long * across_count + there_across, 0, count - 1)
        return solved[pl.ds(place, 1), lane : lane + 1] * as_float(inside)

    shifts = {
        (row_side, col_side): coarse(row_side, col_side, 0) * (1.0 / cheb_center)
        for row_side in (-1, 0, 1)
        for col_side in (-1, 0, 1)
    }

    def add(values, row_side, col_side):
        shift = shifts[row_side, col_side]
        if values.ndim == 3:
            shift = shift.reshape(1, 1, 1)
        return values + shift

    fill_window(box, window, local, low[...], high[...], left, right, REACH, 0, REACH, add)
    weights = (to_long, to_across, to_deep, mass)

    def one_row(row, flow):
        image, flow = negative_image(row, window[row], window[row + 1], flow, weights)
        residual[row - 1] = load_window[row] + image
        return flow

    flow = to_long[0] * (window[1] - window[0])
    lax.fori_loop(1, 1 + box.ex, one_row, flow, unroll=4)
    inner = slice(EDGE, EDGE + box.across)
    first = REACH
    row_ids = lax.broadcasted_iota(jnp.int32, (1, padded(box.ex)), 1)
    col_ids = lax.broadcasted_iota(jnp.int32, (1, box.cols), 1)
    row_mask = jnp.where(row_ids < MARGIN, as_float(long_pos > 0), 1.0)
    row_mask = jnp.where(row_ids >= MARGIN + box.long, as_float(long_pos < long_count - 1), row_mask)
    col_mask = jnp.where(col_ids < EDGE, as_float(across_pos > 0), 1.0)
    col_mask = jnp.where(
        col_ids >= EDGE + box.across, as_float(across_pos < across_count - 1), col_mask
    )
    own_c = coarse(0, 0, 0) * (1.0 - 1.0 / cheb_center) - coarse(0, 0, 1)
    keep = 1.0 + rho_second * rho_first
    gain = 2.0 * rho_second / cheb_radius

    def emit(start, values):
        rows = (values + own_c).reshape(8, box.across, box.deep)
        before = window[first + start : first + start + 8, inner, :]
        iterate[start : start + 8] = keep * before + gain * rows

    box_solve(
        box, residual, means_of(means), tables, row_mask, col_mask, spectral, middle, emit
    )
    top[...] = iterate[box.long - 1]
    bottom[...] = iterate[0]
    flat = iterate.reshape(box.long * box.across, box.deep)
    last_col[...] = flat[row_of(box.across, box.across - 1, box.long), :]
    first_col[...] = flat[row_of(box.across, 0, box.long), :]


def last_residual(
    box, load, iterate, low, high, left, right, to_long, to_across, to_deep, mass, out, window
):
    inner = slice(EDGE, EDGE + box.across)
    flat = window.reshape((box.long + 2) * box.cols, box.deep)
    blank = jnp.zeros((box.long + 2, EDGE, box.deep), jnp.float32)
    window[:, :EDGE, :] = blank
    window[:, EDGE + box.across :, :] = blank
    window[1 : 1 + box.long, inner, :] = iterate[...]
    window[0, inner, :] = low[...]
    window[1 + box.long, inner, :] = high[...]
    flat[row_of(box.cols, EDGE - 1, box.long, 1), :] = left[...]
    flat[row_of(box.cols, EDGE + box.across, box.long, 1), :] = right[...]
    weights = (to_long, to_across, to_deep, mass)

    def one_row(row, flow):
        image, flow = negative_image(REACH + row, window[row + 1], window[row + 2], flow, weights)
        out[row] = load[row] + image[inner]
        return flow

    flow = to_long[REACH - 1] * (window[1] - window[0])
    lax.fori_loop(0, box.long, one_row, flow, unroll=4)


def exchange(axis, last, first):
    size = lax.axis_size(axis)
    up = [(i, i + 1) for i in range(size - 1)]
    down = [(j, i) for i, j in up]
    return lax.ppermute(last, axis, up), lax.ppermute(first, axis, down)


def on_device(zone, scale, diffusivity, decay, load):
    box = Box(load.shape)
    long, across, deep = load.shape
    count = lax.axis_size("wide") * lax.axis_size("narrow")
    tables = tables_of(box)
    cells = f32(long, across, deep)
    window = f32(box.rows, box.cols, deep)

    def scratch(shape):
        return pltpu.VMEM(shape, jnp.float32)

    spectral = scratch((box.ey, padded(box.ex), deep))
    middle = scratch((long, padded(box.ey), deep))

    def pack(wide, *fields):
        message = f32(message_rows(box, wide * (len(fields) - 2)), deep)
        body = functools.partial(pack_fields, box, wide)
        return call(body, (message, message), [VMEM] * len(fields))(*fields)

    near, far = f32(MARGIN, across, deep), f32(2 * REACH, across, deep)
    load_up, load_down, up, down = call(
        functools.partial(pack_edges, box),
        (near, near, far, far),
        [pl.BlockSpec(memory_space=pltpu.HBM)] * 3,
        [pltpu.VMEM((2, REACH, across, deep), jnp.int32), pltpu.SemaphoreType.DMA((6,))],
    )(zone, scale, load)
    load_low, load_high = exchange("wide", load_up, load_down)
    means = call(functools.partial(box_means, box), f32(8, 128), [VMEM] * 2 + [SMEM] * 2)(
        zone, scale, diffusivity, decay
    )
    low, high = exchange("wide", up, down)
    load_left, load_right = exchange("narrow", *pack(MARGIN, load, load_low, load_high))
    left, right = exchange("narrow", *pack(REACH, scale, zone, low, high))
    load_window, local = call(
        functools.partial(first_solve, box),
        (window, cells),
        [VMEM] * (6 + N_TABLES),
        [spectral, middle],
        flops=4 * 10**9,
    )(load, load_low, load_high, load_left, load_right, means, *tables)
    to_long, to_across, to_deep, mass, told = call(
        functools.partial(weights_of, box),
        (window,) * 4 + (f32(count, 128),),
        [VMEM] * 8 + [SMEM] * 2,
        [scratch(window.shape)] * 2,
        flops=10**9,
    )(zone, scale, load, local, low, high, left, right, diffusivity, decay)
    low, high = exchange("wide", local[long - REACH :], local[:REACH])
    all_told = lax.all_to_all(
        told.reshape(count, 1, 128), ("wide", "narrow"), split_axis=0, concat_axis=0, tiled=True
    ).reshape(count, 128)
    left, right = exchange("narrow", *pack(REACH, local, low, high))
    solved_width = -(-(count + 2) // 128) * 128
    solved = call(coarse_solve, f32(count, 128), [VMEM], [scratch((count, solved_width))])(all_told)
    row, col = f32(across, deep), f32(long, deep)
    iterate, top, bottom, last_col, first_col = call(
        functools.partial(second_solve, box),
        (cells, row, row, col, col),
        [VMEM] * (12 + N_TABLES),
        [scratch(window.shape), scratch((box.ex, box.cols, deep)), spectral, middle],
        flops=4 * 10**9,
    )(
        local,
        low,
        high,
        left,
        right,
        solved,
        means,
        to_long,
        to_across,
        to_deep,
        mass,
        load_window,
        *tables,
    )
    low, high = exchange("wide", top, bottom)
    left, right = exchange("narrow", last_col, first_col)
    residual = call(
        functools.partial(last_residual, box),
        cells,
        [VMEM] * 10,
        [scratch((long + 2, box.cols, deep))],
    )(load, iterate, low, high, left, right, to_long, to_across, to_deep, mass)
    return iterate, residual


def solution(mesh):
    split = P(("groups", "wide"), "narrow", None)
    return jax.shard_map(
        on_device,
        mesh=mesh,
        in_specs=(split, split, P(), P(), split),
        out_specs=(split, split),
        check_vma=False,
    )
```

```python
import functools

import jax
import jax.numpy as jnp
import ml_dtypes
import numpy as np
from jax import lax
from jax.experimental import pallas as pl
from jax.experimental.pallas import tpu as pltpu
from jax.sharding import PartitionSpec as P

MARGIN = 4
REACH = MARGIN + 1
EDGE = 8

cheb_center = 1.3
cheb_radius = 1.2
cheb_ratio = 1.3 / 1.2
rho_first = 1.0 / cheb_ratio
rho_second = 1.0 / (2.0 * cheb_ratio - rho_first)
gain = 2.0 * rho_second / cheb_radius

MEANS = range(4)
BOX_DIAGONAL, LONG_HIGH, LONG_LOW, ACROSS_HIGH, ACROSS_LOW, LOAD_SUM = range(4, 10)
IMAGE_SUM, FLOW_LONG_HIGH, FLOW_LONG_LOW, FLOW_ACROSS_HIGH, FLOW_ACROSS_LOW = range(5)

VMEM = pl.BlockSpec(memory_space=pltpu.VMEM)
SMEM = pl.BlockSpec(memory_space=pltpu.SMEM)


def sine_basis(length):
    indices = np.arange(1, length + 1)
    phases = indices[:, None] * indices[None, :] % (2 * (length + 1))
    table = np.sqrt(2.0 / (length + 1)) * np.sin(np.pi * phases / (length + 1))
    eigvals = 4.0 * np.sin(np.pi * indices / (2.0 * (length + 1))) ** 2
    return table.astype(np.float32), eigvals.astype(np.float32)


def call(body, out_shape, in_specs, scratch=(), flops=0, moved=0, out_spec=VMEM):
    return pl.pallas_call(
        body,
        out_shape=out_shape,
        in_specs=in_specs,
        out_specs=jax.tree.map(lambda _: out_spec, out_shape),
        scratch_shapes=list(scratch),
        compiler_params=pltpu.CompilerParams(vmem_limit_bytes=30 * 2**20),
        cost_estimate=pl.CostEstimate(flops=flops, bytes_accessed=moved, transcendentals=0),
    )


def f32(*shape):
    return jax.ShapeDtypeStruct(shape, jnp.float32)


class Box:
    def __init__(self, shape):
        self.long, self.across, self.deep = shape
        self.ex = self.long + 2 * MARGIN
        self.ey = self.across + 2 * MARGIN
        self.rows = self.long + 2 * REACH
        self.cols = self.across + 2 * EDGE
        self.flat = self.rows * self.cols


def pieces(values, count):
    parts = []
    for _ in range(count):
        part = values.astype(jnp.bfloat16)
        parts.append(part)
        values = values - part.astype(jnp.float32)
    return parts


def left_table(table, depth, count):
    rows, cols = table.shape
    wide = np.zeros((rows, depth), np.float32)
    wide[:, :cols] = table
    parts = []
    rest = wide
    for _ in range(count):
        part = rest.astype(ml_dtypes.bfloat16)
        parts.append(part)
        rest = rest - part.astype(np.float32)
    blank = np.zeros_like(parts[0])
    lines = []
    for index in range(count):
        used = count - index if count > 2 else count
        lines.append(np.concatenate([parts[index]] * used + [blank] * (count - used), axis=1))
    return np.concatenate(lines, axis=0)


def right_tables(table):
    rest, parts = table, []
    for _ in range(3):
        part = rest.astype(ml_dtypes.bfloat16)
        parts.append(part)
        rest = rest - part.astype(np.float32)
    both = np.concatenate([parts[0], parts[1]], axis=1)
    return np.concatenate([both, both], axis=0), np.concatenate([parts[2], parts[0]], axis=0)


def padded(size):
    return -(-size // 16) * 16


FORWARD, BACKWARD = 2, 3


def tables_of(box):
    sine_x, eig_x = sine_basis(box.ex)
    sine_y, eig_y = sine_basis(box.ey)
    sine_z, eig_z = sine_basis(box.deep)
    skip = EDGE - MARGIN
    into_y = np.zeros((box.ey, box.cols), np.float32)
    into_y[:, skip : skip + box.ey] = sine_y
    from_y = sine_y[MARGIN : MARGIN + box.across]
    from_x = sine_x[MARGIN : MARGIN + box.long]
    spread = np.broadcast_to(eig_x[:, None], (box.ex, box.deep))
    main_z, rest_z = right_tables(sine_z)
    return [
        jnp.asarray(np.ascontiguousarray(t))
        for t in (
            left_table(into_y, box.cols, FORWARD),
            left_table(sine_x, padded(box.ex), FORWARD),
            left_table(from_x, padded(box.ex), BACKWARD),
            left_table(from_y, padded(box.ey), BACKWARD),
            main_z,
            rest_z,
            spread,
            eig_z[None, :],
            eig_y[None, :],
        )
    ]


N_TABLES = 9


def bf16_dot(left, right):
    return lax.dot_general(
        left, right, (((1,), (0,)), ((), ())), preferred_element_type=jnp.float32
    )


def dot_left(table, values, count, rows):
    total = bf16_dot(table, jnp.concatenate(pieces(values, count), axis=0))
    return sum(total[index * rows : (index + 1) * rows] for index in range(1, count)) + total[:rows]


def dot_right(values, main, rest, count):
    deep = values.shape[1]
    parts = pieces(values, count)
    total = bf16_dot(jnp.concatenate(parts[:2], axis=1), main)
    result = total[:, :deep] + total[:, deep:]
    if count == 3:
        result = result + bf16_dot(jnp.concatenate([parts[0], parts[2]], axis=1), rest)
    return result


def with_rows(values, rows):
    if values.shape[0] == rows:
        return values
    blank = jnp.zeros((rows - values.shape[0],) + values.shape[1:], values.dtype)
    return jnp.concatenate([values, blank], axis=0)


def box_solve(box, source, means, tables, row_mask, col_mask, spectral, middle, emit):
    into_y, into_x, from_x, from_y, main_z, rest_z, spread, eig_z, eig_y = tables
    deep = box.deep
    deep_x, deep_y = padded(box.ex), padded(box.ey)
    into_y, into_x = into_y[...], into_x[...]
    if col_mask is not None:
        mask = jnp.concatenate([col_mask] * FORWARD, axis=1)
        into_y = (into_y.astype(jnp.float32) * mask).astype(jnp.bfloat16)
        mask = jnp.concatenate([row_mask] * FORWARD, axis=1)
        into_x = (into_x.astype(jnp.float32) * mask).astype(jnp.bfloat16)
    from_x, from_y, main_z, rest_z = from_x[...], from_y[...], main_z[...], rest_z[...]
    spectral_flat = spectral.reshape(box.ey * deep_x, deep)
    middle_flat = middle.reshape(box.long * deep_y, deep)
    if deep_x > box.ex:
        spectral[:, box.ex :, :] = jnp.zeros((box.ey, deep_x - box.ex, deep), jnp.float32)
    if deep_y > box.ey:
        middle[:, box.ey :, :] = jnp.zeros((box.long, deep_y - box.ey, deep), jnp.float32)
    for start in range(0, box.ex, 8):
        block = source[start : start + 8].reshape(8 * box.cols, deep)
        block = dot_right(block, main_z, rest_z, FORWARD).reshape(8, box.cols, deep)
        for row in range(0, 8, 2):
            pair = jnp.concatenate([block[row], block[row + 1]], axis=1)
            pair = dot_left(into_y, pair, FORWARD, box.ey)
            for part in range(2):
                spectral_flat[pl.ds(start + row + part, box.ey, stride=deep_x), :] = pair[
                    :, part * deep : (part + 1) * deep
                ]
    base = means[3] + means[0] * spread[...] + means[2] * eig_z[...]
    for col in range(0, box.ey, 2):
        pair = jnp.concatenate([spectral[col], spectral[col + 1]], axis=1)
        pair = dot_left(into_x, pair, FORWARD, box.ex)
        pair = jnp.concatenate(
            [
                pair[:, part * deep : (part + 1) * deep]
                / (base + means[1] * eig_y[0, col + part])
                for part in range(2)
            ],
            axis=1,
        )
        pair = dot_left(from_x, with_rows(pair, deep_x), BACKWARD, box.long)
        for part in range(2):
            middle_flat[pl.ds(col + part, box.long, stride=deep_y), :] = pair[
                :, part * deep : (part + 1) * deep
            ]
    for start in range(0, box.long, 8):
        parts = []
        for row in range(start, start + 8, 2):
            pair = jnp.concatenate([middle[row], middle[row + 1]], axis=1)
            pair = dot_left(from_y, pair, BACKWARD, box.across)
            parts += [pair[:, :deep], pair[:, deep:]]
        emit(start, dot_right(jnp.concatenate(parts, axis=0), main_z, rest_z, BACKWARD))


def position():
    long_pos, across_pos = lax.axis_index("wide"), lax.axis_index("narrow")
    return long_pos, across_pos, lax.axis_size("wide"), lax.axis_size("narrow")


def as_float(flag):
    return jnp.where(flag, jnp.float32(1.0), jnp.float32(0.0))


def row_of(stride, col, count, first=0):
    return pl.ds(first * stride + col, count, stride=stride)


def pack_columns(box, fields, lows, highs, wide, up, down):
    corner = len(fields) * wide * box.long
    place = 0
    for field, low, high in zip(fields, lows, highs):
        for step in range(wide):
            for target, col in ((up, box.across - wide + step), (down, step)):
                values = field[row_of(box.across, col, box.long), :]
                target[place * box.long : (place + 1) * box.long, :] = values.astype(jnp.float32)
                at = corner + 2 * REACH * place
                target[at : at + wide, :] = low[row_of(box.across, col, wide), :]
                target[at + REACH : at + REACH + wide, :] = high[row_of(box.across, col, wide), :]
            place += 1


def message_rows(box, count):
    return -(-(count * (box.long + 2 * REACH)) // 8) * 8


def pack_fields(box, wide, *refs):
    *fields, low, high, up, down = refs
    size = wide * box.across
    flat = [field.reshape(box.long * box.across, box.deep) for field in fields]
    sides = [
        [
            ref.reshape(len(fields) * size, box.deep).at[index * size : (index + 1) * size]
            for index in range(len(fields))
        ]
        for ref in (low, high)
    ]
    pack_columns(box, flat, sides[0], sides[1], wide, up, down)


def pack_edges(box, zone, scale, up, down):
    last = box.long
    up[:REACH] = scale[last - REACH :]
    down[:REACH] = scale[:REACH]
    up[REACH:] = zone[last - REACH :].astype(jnp.float32)
    down[REACH:] = zone[:REACH].astype(jnp.float32)


def fill_window(box, window, own, low, high, left, right, wide, place, total, add=None):
    flat = window.reshape(box.flat, box.deep)
    nothing = jnp.zeros((box.rows, EDGE, box.deep), jnp.float32)
    window[:, :EDGE, :] = nothing
    window[:, EDGE + box.across :, :] = nothing
    if add is None:
        add = lambda values, row_side, col_side: values
    inner = slice(EDGE, EDGE + box.across)
    first, last = REACH, REACH + box.long
    if wide < REACH:
        blank = jnp.zeros((1, box.across, box.deep), jnp.float32)
        window[0:1, inner, :] = blank
        window[box.rows - 1 :, inner, :] = blank
    window[first:last, inner, :] = add(own[...].astype(jnp.float32), 0, 0)
    window[first - wide : first, inner, :] = add(low, -1, 0)
    window[last : last + wide, inner, :] = add(high, 1, 0)
    corner = total * box.long
    for step in range(wide):
        for source, col, side in (
            (left, EDGE - wide + step, -1),
            (right, EDGE + box.across + step, 1),
        ):
            at = (place + step) * box.long
            values = source[at : at + box.long, :]
            flat[row_of(box.cols, col, box.long, first), :] = add(values, 0, side)
            at = corner + 2 * REACH * (place + step)
            values = source[at : at + wide, :]
            flat[row_of(box.cols, col, wide, first - wide), :] = add(values, -1, side)
            values = source[at + REACH : at + REACH + wide, :]
            flat[row_of(box.cols, col, wide, last), :] = add(values, 1, side)


def negative_image(row, x, x_next, flow_before, weights):
    to_long, to_across, to_deep, mass = weights
    rows, lanes = x.shape
    flow_long = to_long[row] * (x_next - x)
    flow_across = to_across[row] * (pltpu.roll(x, rows - 1, 0) - x)
    flow_deep = to_deep[row] * (pltpu.roll(x, lanes - 1, 1) - x)
    total = flow_long - flow_before - mass[row] * x
    total = total + (flow_across - pltpu.roll(flow_across, 1, 0))
    total = total + (flow_deep - pltpu.roll(flow_deep, 1, 1))
    return total, flow_long


def looked_up(labels, values):
    return jnp.where(labels == 0, values[0], jnp.where(labels == 1, values[1], values[2]))


def line_of(numbers, shape):
    lanes = lax.broadcasted_iota(jnp.int32, shape, 1)
    line = jnp.zeros(shape, jnp.float32)
    for index, number in numbers:
        line = jnp.where(lanes == index, number, line)
    return line


def box_sums(box, zone, scale, load, diffusivity, decay, out):
    step = 4
    nothing = jnp.zeros((box.across, box.deep), jnp.float32)
    half = [[0.5 * diffusivity[z, d] for z in range(3)] for d in range(3)]
    rates = [decay[z] for z in range(3)]

    def halves(row):
        labels, factor = zone[row], scale[row]
        return [looked_up(labels, half[d]) * factor for d in range(3)] + [looked_up(labels, rates)]

    def some_rows(index, sums):
        for row in range(step):
            row = index * step + row
            sums = [total + more for total, more in zip(sums, halves(row) + [load[row]])]
        return sums

    sums = lax.fori_loop(0, box.long // step, some_rows, [nothing] * 5)

    def total(values):
        return jnp.sum(values, keepdims=True).reshape(1, 1)

    cells = box.long * box.across * box.deep
    numbers = [(index, total(sums[index]) * (2.0 / cells)) for index in range(3)]
    mass = total(sums[3])
    numbers += [(3, mass / cells)]
    ends = total(sums[2][:, :1]) + total(sums[2][:, box.deep - 1 :])
    numbers += [
        (BOX_DIAGONAL, mass + ends),
        (LONG_HIGH, total(halves(box.long - 1)[0])),
        (LONG_LOW, total(halves(0)[0])),
        (ACROSS_HIGH, total(sums[1][box.across - 1 :])),
        (ACROSS_LOW, total(sums[1][:1])),
        (LOAD_SUM, total(sums[4])),
    ]
    out[...] = line_of(numbers, out.shape)


def means_of(ref):
    return [ref[0:1, index : index + 1] for index in range(4)]


def first_solve(box, load, low, high, left, right, means, *rest):
    tables = rest[:N_TABLES]
    window, local, spectral, middle = rest[N_TABLES:]
    fill_window(box, window, load, low[...], high[...], left, right, MARGIN, 0, MARGIN)

    def emit(start, values):
        values = values * (1.0 / cheb_center)
        local[start : start + 8] = values.reshape(8, box.across, box.deep)

    box_solve(
        box,
        window.at[1 : 1 + box.ex],
        means_of(means),
        tables,
        None,
        None,
        spectral,
        middle,
        emit,
    )


def weights_of(
    box,
    zone,
    scale,
    local,
    low,
    high,
    left,
    right,
    diffusivity,
    decay,
    to_long,
    to_across,
    to_deep,
    mass,
    told,
    zone_window,
    scale_window,
):
    for index, (window, own) in enumerate(((scale_window, scale), (zone_window, zone))):
        part = slice(index * REACH, (index + 1) * REACH)
        fill_window(
            box, window, own, low[part], high[part], left, right, REACH, part.start, 2 * REACH
        )
    half = [[0.5 * diffusivity[z, d] for d in range(3)] for z in range(3)]
    rates = [decay[z] for z in range(3)]
    lane = lax.broadcasted_iota(jnp.int32, (box.cols, box.deep), 1)
    ends = jnp.where((lane == 0) | (lane == box.deep - 1), jnp.float32(1.0), jnp.float32(0.0))
    not_last = jnp.where(lane == box.deep - 1, jnp.float32(0.0), jnp.float32(1.0))

    def one_row(row, before):
        labels, factor = zone_window[row], scale_window[row]
        now = [looked_up(labels, [half[z][d] for z in range(3)]) * factor for d in range(3)]
        to_across[row] = now[1] + pltpu.roll(now[1], box.cols - 1, 0)
        to_deep[row] = (now[2] + pltpu.roll(now[2], box.deep - 1, 1)) * not_last
        mass[row] = looked_up(labels, rates) + now[2] * ends
        to_long[jnp.maximum(row - 1, 0)] = before + now[0]
        return now[0]

    last_long = lax.fori_loop(0, box.rows - 2, one_row, jnp.zeros_like(ends), unroll=4)
    for row in range(box.rows - 2, box.rows):
        last_long = one_row(row, last_long)
    to_long[box.rows - 1] = last_long

    first, last = REACH, REACH + box.long
    inner = slice(EDGE, EDGE + box.across)
    step = 8

    def add_rows(index, total):
        for row in range(step):
            row = index * step + row
            total = total + mass[first + row, inner] * local[row]
        return total

    nothing = jnp.zeros((box.across, box.deep), jnp.float32)
    image_sum = lax.fori_loop(0, box.long // step, add_rows, nothing)
    long_pos, across_pos, long_count, across_count = position()
    across_flat = to_across.reshape(box.flat, box.deep)
    local_flat = local.reshape(box.long * box.across, box.deep)
    flows = [
        to_long[last - 1, inner] * local[box.long - 1],
        to_long[first - 1, inner] * local[0],
        across_flat[row_of(box.cols, EDGE + box.across - 1, box.long, first), :]
        * local_flat[row_of(box.across, box.across - 1, box.long), :],
        across_flat[row_of(box.cols, EDGE - 1, box.long, first), :]
        * local_flat[row_of(box.across, 0, box.long), :],
    ]
    flows = [jnp.sum(flow, keepdims=True) for flow in flows]
    numbers = [
        (IMAGE_SUM, jnp.sum(image_sum, keepdims=True) + sum(flows)),
        (FLOW_LONG_HIGH, flows[0] * as_float(long_pos < long_count - 1)),
        (FLOW_LONG_LOW, flows[1] * as_float(long_pos > 0)),
        (FLOW_ACROSS_HIGH, flows[2] * as_float(across_pos < across_count - 1)),
        (FLOW_ACROSS_LOW, flows[3] * as_float(across_pos > 0)),
    ]
    told[...] = line_of(numbers, told.shape)


def column(values, index):
    return values[:, index : index + 1]


def coarse_inverse(told, inverse, work):
    count, width = work.shape
    across = lax.axis_size("narrow")
    numbers = told[...]
    beyond = pltpu.roll(numbers, count - across, 0)
    beside = pltpu.roll(numbers, count - 1, 0)
    before = pltpu.roll(numbers, across, 0)
    ahead = pltpu.roll(numbers, 1, 0)
    place = lax.broadcasted_iota(jnp.int32, (count, 1), 0)
    across_pos = lax.rem(place, across)
    nothing = jnp.zeros((count, 1), jnp.float32)
    couplings = []
    diagonal = column(numbers, BOX_DIAGONAL)
    for own, other, there, inside in (
        (LONG_HIGH, LONG_LOW, beyond, place < count - across),
        (LONG_LOW, LONG_HIGH, before, place >= across),
        (ACROSS_HIGH, ACROSS_LOW, beside, across_pos < across - 1),
        (ACROSS_LOW, ACROSS_HIGH, ahead, across_pos > 0),
    ):
        shared = jnp.where(inside, column(there, other), nothing)
        diagonal = diagonal + column(numbers, own) + shared
        couplings.append(jnp.where(inside, column(numbers, own) + shared, nothing))
    rows = lax.broadcasted_iota(jnp.int32, (count, width), 0)
    cols = lax.broadcasted_iota(jnp.int32, (count, width), 1)
    blank = jnp.zeros((count, width), jnp.float32)
    matrix = jnp.where(cols == rows, diagonal, blank)
    for shift, coupling in zip((across, -across, 1, -1), couplings):
        matrix = matrix - jnp.where((cols == rows + shift) & (cols < count), coupling, blank)
    matrix = jnp.where(cols == rows + count, jnp.ones((count, 1), jnp.float32), matrix)
    work[...] = matrix

    def eliminate(step, _):
        values = work[...]
        pivot_row = work[pl.ds(step, 1), :]
        at_step = cols == step
        factors = jnp.sum(jnp.where(at_step, values, blank), axis=1, keepdims=True)
        pivot = jnp.sum(jnp.where(at_step[:1], pivot_row, blank[:1]), axis=1, keepdims=True)
        pivot_row = pivot_row / pivot
        work[...] = jnp.where(rows == step, pivot_row, values - factors * pivot_row)
        return 0

    lax.fori_loop(0, count, eliminate, 0)
    values = work[...]
    if count % 128:
        inverse[...] = pltpu.roll(values, width - count, 1)[:, : inverse.shape[1]]
    else:
        inverse[...] = values[:, count : 2 * count]


def answer(inverse, sums):
    return jnp.sum(inverse[...] * sums, axis=0, keepdims=True)


def at_box(values, row_side, col_side):
    long_pos, across_pos, long_count, across_count = position()
    there_long, there_across = long_pos + row_side, across_pos + col_side
    inside = (
        (there_long >= 0)
        & (there_long < long_count)
        & (there_across >= 0)
        & (there_across < across_count)
    )
    lanes = lax.broadcasted_iota(jnp.int32, values.shape, 1)
    wanted = (lanes == there_long * across_count + there_across) & inside
    return jnp.sum(jnp.where(wanted, values, jnp.zeros_like(values)), axis=1, keepdims=True)


def second_solve(box, local, low, high, left, right, inverse, told, means, *rest):
    to_long, to_across, to_deep, mass, load_window = rest[:5]
    tables = rest[5 : 5 + N_TABLES]
    iterate, top, bottom, last_col, first_col = rest[5 + N_TABLES : 10 + N_TABLES]
    window, residual, spectral, middle = rest[10 + N_TABLES :]
    long_pos, across_pos, long_count, across_count = position()
    coarse = answer(inverse, column(told, LOAD_SUM)) * (1.0 / cheb_center)
    shifts = {
        (row_side, col_side): at_box(coarse, row_side, col_side)
        for row_side in (-1, 0, 1)
        for col_side in (-1, 0, 1)
    }

    def add(values, row_side, col_side):
        shift = shifts[row_side, col_side]
        if values.ndim == 3:
            shift = shift.reshape(1, 1, 1)
        return values + shift

    fill_window(box, window, local, low[...], high[...], left, right, REACH, 0, REACH, add)
    weights = (to_long, to_across, to_deep, mass)

    def one_row(row, flow):
        image, flow = negative_image(row, window[row], window[row + 1], flow, weights)
        residual[row - 1] = load_window[row] + image
        return flow

    flow = to_long[0] * (window[1] - window[0])
    lax.fori_loop(1, 1 + box.ex, one_row, flow, unroll=4)
    inner = slice(EDGE, EDGE + box.across)
    first = REACH
    row_ids = lax.broadcasted_iota(jnp.int32, (1, padded(box.ex)), 1)
    col_ids = lax.broadcasted_iota(jnp.int32, (1, box.cols), 1)
    row_mask = jnp.where(row_ids < MARGIN, as_float(long_pos > 0), 1.0)
    row_mask = jnp.where(row_ids >= MARGIN + box.long, as_float(long_pos < long_count - 1), row_mask)
    col_mask = jnp.where(col_ids < EDGE, as_float(across_pos > 0), 1.0)
    col_mask = jnp.where(
        col_ids >= EDGE + box.across, as_float(across_pos < across_count - 1), col_mask
    )
    keep = 1.0 + rho_second * rho_first

    def emit(start, values):
        rows = values.reshape(8, box.across, box.deep)
        before = window[first + start : first + start + 8, inner, :]
        iterate[start : start + 8] = keep * before + gain * rows

    box_solve(
        box, residual, means_of(means), tables, row_mask, col_mask, spectral, middle, emit
    )
    top[...] = iterate[box.long - 1]
    bottom[...] = iterate[0]
    flat = iterate.reshape(box.long * box.across, box.deep)
    last_col[...] = flat[row_of(box.across, box.across - 1, box.long), :]
    first_col[...] = flat[row_of(box.across, 0, box.long), :]


def last_residual(
    box,
    load,
    partial,
    low,
    high,
    left,
    right,
    inverse,
    load_told,
    image_told,
    to_long,
    to_across,
    to_deep,
    mass,
    iterate,
    out,
    window,
    result,
    sems,
):
    count = load_told.shape[0]
    across_count = lax.axis_size("narrow")
    numbers = image_told[...]
    sums = column(numbers, IMAGE_SUM)
    sums = sums - column(pltpu.roll(numbers, count - across_count, 0), FLOW_LONG_LOW)
    sums = sums - column(pltpu.roll(numbers, across_count, 0), FLOW_LONG_HIGH)
    sums = sums - column(pltpu.roll(numbers, count - 1, 0), FLOW_ACROSS_LOW)
    sums = sums - column(pltpu.roll(numbers, 1, 0), FLOW_ACROSS_HIGH)
    sums = column(load_told, LOAD_SUM) * (1.0 - 1.0 / cheb_center) - sums
    coarse = answer(inverse, sums) * gain
    inner = slice(EDGE, EDGE + box.across)
    flat = window.reshape((box.long + 2) * box.cols, box.deep)
    blank = jnp.zeros((box.long + 2, EDGE, box.deep), jnp.float32)
    window[:, :EDGE, :] = blank
    window[:, EDGE + box.across :, :] = blank
    window[1 : 1 + box.long, inner, :] = partial[...] + at_box(coarse, 0, 0).reshape(1, 1, 1)
    own = pltpu.make_async_copy(window.at[1 : 1 + box.long, inner, :], iterate, sems.at[0])
    own.start()
    window[0, inner, :] = low[...] + at_box(coarse, -1, 0)
    window[1 + box.long, inner, :] = high[...] + at_box(coarse, 1, 0)
    flat[row_of(box.cols, EDGE - 1, box.long, 1), :] = left[...] + at_box(coarse, 0, -1)
    flat[row_of(box.cols, EDGE + box.across, box.long, 1), :] = right[...] + at_box(coarse, 0, 1)
    weights = (to_long, to_across, to_deep, mass)

    def one_row(row, flow):
        image, flow = negative_image(REACH + row, window[row + 1], window[row + 2], flow, weights)
        result[row] = load[row] + image[inner]
        return flow

    flow = to_long[REACH - 1] * (window[1] - window[0])
    chunk = box.long // 4
    copies = [own]
    for index in range(4):
        rows = slice(index * chunk, (index + 1) * chunk)
        flow = lax.fori_loop(rows.start, rows.stop, one_row, flow, unroll=4)
        copy = pltpu.make_async_copy(result.at[rows], out.at[rows], sems.at[1 + index])
        copy.start()
        copies.append(copy)
    for copy in copies:
        copy.wait()


def exchange(axis, last, first):
    size = lax.axis_size(axis)
    up = [(i, i + 1) for i in range(size - 1)]
    down = [(j, i) for i, j in up]
    return lax.ppermute(last, axis, up), lax.ppermute(first, axis, down)


def on_device(zone, scale, diffusivity, decay, load):
    box = Box(load.shape)
    long, across, deep = load.shape
    count = lax.axis_size("wide") * lax.axis_size("narrow")
    tables = tables_of(box)
    cells = f32(long, across, deep)
    window = f32(box.rows, box.cols, deep)

    def scratch(shape):
        return pltpu.VMEM(shape, jnp.float32)

    spectral = scratch((box.ey, padded(box.ex), deep))
    middle = scratch((long, padded(box.ey), deep))

    def pack(wide, *fields):
        message = f32(message_rows(box, wide * (len(fields) - 2)), deep)
        body = functools.partial(pack_fields, box, wide)
        return call(body, (message, message), [VMEM] * len(fields))(*fields)

    load_low, load_high = exchange("wide", load[long - MARGIN :], load[:MARGIN])
    own_told = call(functools.partial(box_sums, box), f32(8, 128), [VMEM] * 3 + [SMEM] * 2)(
        zone, scale, load, diffusivity, decay
    )
    load_told = lax.all_gather(own_told[:1], ("wide", "narrow"), axis=0, tiled=True)
    far = f32(2 * REACH, across, deep)
    up, down = call(functools.partial(pack_edges, box), (far, far), [VMEM] * 2)(zone, scale)
    low, high = exchange("wide", up, down)
    load_left, load_right = exchange("narrow", *pack(MARGIN, load, load_low, load_high))
    left, right = exchange("narrow", *pack(REACH, scale, zone, low, high))
    load_window, local = call(
        functools.partial(first_solve, box),
        (window, cells),
        [VMEM] * (6 + N_TABLES),
        [spectral, middle],
        flops=4 * 10**9,
    )(load, load_low, load_high, load_left, load_right, own_told, *tables)
    to_long, to_across, to_deep, mass, image_told = call(
        functools.partial(weights_of, box),
        (window,) * 4 + (f32(8, 128),),
        [VMEM] * 7 + [SMEM] * 2,
        [scratch(window.shape)] * 2,
        flops=10**9,
    )(zone, scale, local, low, high, left, right, diffusivity, decay)
    low, high = exchange("wide", local[long - REACH :], local[:REACH])
    image_told = lax.all_gather(image_told[:1], ("wide", "narrow"), axis=0, tiled=True)
    left, right = exchange("narrow", *pack(REACH, local, low, high))
    inverse = call(
        coarse_inverse,
        f32(count, -(-count // 128) * 128),
        [VMEM],
        [scratch((count, -(-2 * count // 128) * 128))],
    )(load_told)
    row, col = f32(across, deep), f32(long, deep)
    partial, top, bottom, last_col, first_col = call(
        functools.partial(second_solve, box),
        (cells, row, row, col, col),
        [VMEM] * (13 + N_TABLES),
        [scratch(window.shape), scratch((box.ex, box.cols, deep)), spectral, middle],
        flops=4 * 10**9,
    )(
        local,
        low,
        high,
        left,
        right,
        inverse,
        load_told,
        own_told,
        to_long,
        to_across,
        to_deep,
        mass,
        load_window,
        *tables,
    )
    low, high = exchange("wide", top, bottom)
    left, right = exchange("narrow", last_col, first_col)
    return call(
        functools.partial(last_residual, box),
        (cells, cells),
        [VMEM] * 13,
        [scratch((long + 2, box.cols, deep)), scratch(cells.shape), pltpu.SemaphoreType.DMA((5,))],
        out_spec=pl.BlockSpec(memory_space=pl.ANY),
    )(
        load,
        partial,
        low,
        high,
        left,
        right,
        inverse,
        load_told,
        image_told,
        to_long,
        to_across,
        to_deep,
        mass,
    )


def solution(mesh):
    split = P(("groups", "wide"), "narrow", None)
    return jax.shard_map(
        on_device,
        mesh=mesh,
        in_specs=(split, split, P(), P(), split),
        out_specs=(split, split),
        check_vma=False,
    )
```

```python
import functools

import jax
import jax.numpy as jnp
import ml_dtypes
import numpy as np
from jax import lax
from jax.experimental import pallas as pl
from jax.experimental.pallas import tpu as pltpu
from jax.sharding import PartitionSpec as P

MARGIN = 4
REACH = MARGIN + 1
EDGE = 8

cheb_center = 1.3
cheb_radius = 1.2
cheb_ratio = 1.3 / 1.2
rho_first = 1.0 / cheb_ratio
rho_second = 1.0 / (2.0 * cheb_ratio - rho_first)
gain = 2.0 * rho_second / cheb_radius

MEANS = range(4)
BOX_DIAGONAL, LONG_HIGH, LONG_LOW, ACROSS_HIGH, ACROSS_LOW, LOAD_SUM = range(4, 10)
IMAGE_SUM, FLOW_LONG_HIGH, FLOW_LONG_LOW, FLOW_ACROSS_HIGH, FLOW_ACROSS_LOW = range(16, 21)

VMEM = pl.BlockSpec(memory_space=pltpu.VMEM)
SMEM = pl.BlockSpec(memory_space=pltpu.SMEM)


def sine_basis(length):
    indices = np.arange(1, length + 1)
    phases = indices[:, None] * indices[None, :] % (2 * (length + 1))
    table = np.sqrt(2.0 / (length + 1)) * np.sin(np.pi * phases / (length + 1))
    eigvals = 4.0 * np.sin(np.pi * indices / (2.0 * (length + 1))) ** 2
    return table.astype(np.float32), eigvals.astype(np.float32)


def call(body, out_shape, in_specs, scratch=(), flops=0, moved=0, out_spec=VMEM):
    return pl.pallas_call(
        body,
        out_shape=out_shape,
        in_specs=in_specs,
        out_specs=jax.tree.map(lambda _: out_spec, out_shape),
        scratch_shapes=list(scratch),
        compiler_params=pltpu.CompilerParams(vmem_limit_bytes=30 * 2**20),
        cost_estimate=pl.CostEstimate(flops=flops, bytes_accessed=moved, transcendentals=0),
    )


def f32(*shape):
    return jax.ShapeDtypeStruct(shape, jnp.float32)


class Box:
    def __init__(self, shape):
        self.long, self.across, self.deep = shape
        self.ex = self.long + 2 * MARGIN
        self.ey = self.across + 2 * MARGIN
        self.rows = self.long + 2 * REACH
        self.cols = self.across + 2 * EDGE
        self.flat = self.rows * self.cols


def pieces(values, count):
    parts = []
    for _ in range(count):
        part = values.astype(jnp.bfloat16)
        parts.append(part)
        values = values - part.astype(jnp.float32)
    return parts


def left_table(table, depth, count):
    rows, cols = table.shape
    wide = np.zeros((rows, depth), np.float32)
    wide[:, :cols] = table
    parts = []
    rest = wide
    for _ in range(count):
        part = rest.astype(ml_dtypes.bfloat16)
        parts.append(part)
        rest = rest - part.astype(np.float32)
    blank = np.zeros_like(parts[0])
    lines = []
    for index in range(count):
        used = count - index if count > 2 else count
        lines.append(np.concatenate([parts[index]] * used + [blank] * (count - used), axis=1))
    return np.concatenate(lines, axis=0)


def right_tables(table):
    rest, parts = table, []
    for _ in range(3):
        part = rest.astype(ml_dtypes.bfloat16)
        parts.append(part)
        rest = rest - part.astype(np.float32)
    both = np.concatenate([parts[0], parts[1]], axis=1)
    return np.concatenate([both, both], axis=0), np.concatenate([parts[2], parts[0]], axis=0)


def padded(size):
    return -(-size // 16) * 16


FORWARD, BACKWARD = 2, 3


def tables_of(box):
    sine_x, eig_x = sine_basis(box.ex)
    sine_y, eig_y = sine_basis(box.ey)
    sine_z, eig_z = sine_basis(box.deep)
    skip = EDGE - MARGIN
    into_y = np.zeros((box.ey, box.cols), np.float32)
    into_y[:, skip : skip + box.ey] = sine_y
    from_y = sine_y[MARGIN : MARGIN + box.across]
    from_x = sine_x[MARGIN : MARGIN + box.long]
    spread = np.broadcast_to(eig_x[:, None], (box.ex, box.deep))
    main_z, rest_z = right_tables(sine_z)
    return [
        jnp.asarray(np.ascontiguousarray(t))
        for t in (
            left_table(into_y, box.cols, FORWARD),
            left_table(sine_x, padded(box.ex), FORWARD),
            left_table(from_x, padded(box.ex), BACKWARD),
            left_table(from_y, padded(box.ey), BACKWARD),
            main_z,
            rest_z,
            spread,
            eig_z[None, :],
            eig_y[None, :],
        )
    ]


N_TABLES = 9


def bf16_dot(left, right):
    return lax.dot_general(
        left, right, (((1,), (0,)), ((), ())), preferred_element_type=jnp.float32
    )


def dot_left(table, values, count, rows):
    total = bf16_dot(table, jnp.concatenate(pieces(values, count), axis=0))
    return sum(total[index * rows : (index + 1) * rows] for index in range(1, count)) + total[:rows]


def dot_right(values, main, rest, count):
    deep = values.shape[1]
    parts = pieces(values, count)
    total = bf16_dot(jnp.concatenate(parts[:2], axis=1), main)
    result = total[:, :deep] + total[:, deep:]
    if count == 3:
        result = result + bf16_dot(jnp.concatenate([parts[0], parts[2]], axis=1), rest)
    return result


def with_rows(values, rows):
    if values.shape[0] == rows:
        return values
    blank = jnp.zeros((rows - values.shape[0],) + values.shape[1:], values.dtype)
    return jnp.concatenate([values, blank], axis=0)


def box_solve(box, source, means, tables, row_mask, col_mask, spectral, middle, emit):
    into_y, into_x, from_x, from_y, main_z, rest_z, spread, eig_z, eig_y = tables
    deep = box.deep
    deep_x, deep_y = padded(box.ex), padded(box.ey)
    into_y, into_x = into_y[...], into_x[...]
    if col_mask is not None:
        mask = jnp.concatenate([col_mask] * FORWARD, axis=1)
        into_y = (into_y.astype(jnp.float32) * mask).astype(jnp.bfloat16)
        mask = jnp.concatenate([row_mask] * FORWARD, axis=1)
        into_x = (into_x.astype(jnp.float32) * mask).astype(jnp.bfloat16)
    from_x, from_y, main_z, rest_z = from_x[...], from_y[...], main_z[...], rest_z[...]
    spectral_flat = spectral.reshape(box.ey * deep_x, deep)
    middle_flat = middle.reshape(box.long * deep_y, deep)
    if deep_x > box.ex:
        spectral[:, box.ex :, :] = jnp.zeros((box.ey, deep_x - box.ex, deep), jnp.float32)
    if deep_y > box.ey:
        middle[:, box.ey :, :] = jnp.zeros((box.long, deep_y - box.ey, deep), jnp.float32)
    for start in range(0, box.ex, 8):
        block = source[start : start + 8].reshape(8 * box.cols, deep)
        block = dot_right(block, main_z, rest_z, FORWARD).reshape(8, box.cols, deep)
        for row in range(0, 8, 2):
            pair = jnp.concatenate([block[row], block[row + 1]], axis=1)
            pair = dot_left(into_y, pair, FORWARD, box.ey)
            for part in range(2):
                spectral_flat[pl.ds(start + row + part, box.ey, stride=deep_x), :] = pair[
                    :, part * deep : (part + 1) * deep
                ]
    base = means[3] + means[0] * spread[...] + means[2] * eig_z[...]
    for col in range(0, box.ey, 2):
        pair = jnp.concatenate([spectral[col], spectral[col + 1]], axis=1)
        pair = dot_left(into_x, pair, FORWARD, box.ex)
        pair = jnp.concatenate(
            [
                pair[:, part * deep : (part + 1) * deep]
                / (base + means[1] * eig_y[0, col + part])
                for part in range(2)
            ],
            axis=1,
        )
        pair = dot_left(from_x, with_rows(pair, deep_x), BACKWARD, box.long)
        for part in range(2):
            middle_flat[pl.ds(col + part, box.long, stride=deep_y), :] = pair[
                :, part * deep : (part + 1) * deep
            ]
    for start in range(0, box.long, 8):
        parts = []
        for row in range(start, start + 8, 2):
            pair = jnp.concatenate([middle[row], middle[row + 1]], axis=1)
            pair = dot_left(from_y, pair, BACKWARD, box.across)
            parts += [pair[:, :deep], pair[:, deep:]]
        emit(start, dot_right(jnp.concatenate(parts, axis=0), main_z, rest_z, BACKWARD))


def position():
    long_pos, across_pos = lax.axis_index("wide"), lax.axis_index("narrow")
    return long_pos, across_pos, lax.axis_size("wide"), lax.axis_size("narrow")


def as_float(flag):
    return jnp.where(flag, jnp.float32(1.0), jnp.float32(0.0))


def row_of(stride, col, count, first=0):
    return pl.ds(first * stride + col, count, stride=stride)


def pack_columns(box, fields, lows, highs, wide, up, down):
    corner = len(fields) * wide * box.long
    place = 0
    for field, low, high in zip(fields, lows, highs):
        for step in range(wide):
            for target, col in ((up, box.across - wide + step), (down, step)):
                values = field[row_of(box.across, col, box.long), :]
                target[place * box.long : (place + 1) * box.long, :] = values.astype(jnp.float32)
                at = corner + 2 * REACH * place
                target[at : at + wide, :] = low[row_of(box.across, col, wide), :]
                target[at + REACH : at + REACH + wide, :] = high[row_of(box.across, col, wide), :]
            place += 1


def message_rows(box, count):
    return -(-(count * (box.long + 2 * REACH)) // 8) * 8


def pack_fields(box, wide, count, fields, *refs):
    own, (low, high), tables = refs[:fields], refs[fields : fields + 2], refs[fields + 2 : -3]
    up, down, table = refs[-3:]
    size = wide * box.across
    flat = [field.reshape(box.long * box.across, box.deep) for field in own]
    low = low.reshape(low.size // box.deep, box.deep)
    high = high.reshape(high.size // box.deep, box.deep)
    sides = [
        [ref.at[index * size : (index + 1) * size] for index in range(fields)]
        for ref in (low, high)
    ]
    pack_columns(box, flat, sides[0], sides[1], wide, up, down)
    known = merged(*(ref[ref.shape[0] - count :, :] for ref in tables))
    table[...] = known
    up[up.shape[0] - count :, :] = known
    down[down.shape[0] - count :, :] = known


def bring_in(
    box, zone, scale, load, own_zone, own_scale, own_load, load_up, load_down, up, down, staged, sems
):
    last = box.long
    copies = [
        (load.at[last - MARGIN :], load_up),
        (load.at[:MARGIN], load_down),
        (zone.at[last - REACH :], staged.at[0]),
        (zone.at[:REACH], staged.at[1]),
        (scale.at[last - REACH :], up.at[:REACH]),
        (scale.at[:REACH], down.at[:REACH]),
        (load, own_load),
        (scale, own_scale),
        (zone, own_zone),
    ]
    copies = [
        pltpu.make_async_copy(source, target, sems.at[index])
        for index, (source, target) in enumerate(copies)
    ]
    for copy in copies:
        copy.start()
    for copy in copies[:4]:
        copy.wait()
    up[REACH:] = staged[0].astype(jnp.float32)
    down[REACH:] = staged[1].astype(jnp.float32)
    for copy in copies[4:]:
        copy.wait()


def fill_window(box, window, own, low, high, left, right, wide, place, total, add=None):
    flat = window.reshape(box.flat, box.deep)
    nothing = jnp.zeros((box.rows, EDGE, box.deep), jnp.float32)
    window[:, :EDGE, :] = nothing
    window[:, EDGE + box.across :, :] = nothing
    if add is None:
        add = lambda values, row_side, col_side: values
    inner = slice(EDGE, EDGE + box.across)
    first, last = REACH, REACH + box.long
    if wide < REACH:
        blank = jnp.zeros((1, box.across, box.deep), jnp.float32)
        window[0:1, inner, :] = blank
        window[box.rows - 1 :, inner, :] = blank
    window[first:last, inner, :] = add(own[...].astype(jnp.float32), 0, 0)
    window[first - wide : first, inner, :] = add(low, -1, 0)
    window[last : last + wide, inner, :] = add(high, 1, 0)
    corner = total * box.long
    for step in range(wide):
        for source, col, side in (
            (left, EDGE - wide + step, -1),
            (right, EDGE + box.across + step, 1),
        ):
            at = (place + step) * box.long
            values = source[at : at + box.long, :]
            flat[row_of(box.cols, col, box.long, first), :] = add(values, 0, side)
            at = corner + 2 * REACH * (place + step)
            values = source[at : at + wide, :]
            flat[row_of(box.cols, col, wide, first - wide), :] = add(values, -1, side)
            values = source[at + REACH : at + REACH + wide, :]
            flat[row_of(box.cols, col, wide, last), :] = add(values, 1, side)


def negative_image(row, x, x_next, flow_before, weights):
    to_long, to_across, to_deep, mass = weights
    rows, lanes = x.shape
    flow_long = to_long[row] * (x_next - x)
    flow_across = to_across[row] * (pltpu.roll(x, rows - 1, 0) - x)
    flow_deep = to_deep[row] * (pltpu.roll(x, lanes - 1, 1) - x)
    total = flow_long - flow_before - mass[row] * x
    total = total + (flow_across - pltpu.roll(flow_across, 1, 0))
    total = total + (flow_deep - pltpu.roll(flow_deep, 1, 1))
    return total, flow_long


def looked_up(labels, values):
    return jnp.where(labels == 0, values[0], jnp.where(labels == 1, values[1], values[2]))


def at_own_row(line, shape):
    long_pos, across_pos, _, across_count = position()
    rows = lax.broadcasted_iota(jnp.int32, shape, 0)
    own = rows == long_pos * across_count + across_pos
    return jnp.where(own, line[:1], jnp.zeros(shape, jnp.float32))


def merged(table, *others):
    for other in others:
        table = jnp.where(table != 0.0, table, other)
    return table


def merge(table, low, high, out):
    count = table.shape[0]
    out[...] = merged(
        table[...], low[low.shape[0] - count :, :], high[high.shape[0] - count :, :]
    )


def line_of(numbers, shape):
    lanes = lax.broadcasted_iota(jnp.int32, shape, 1)
    line = jnp.zeros(shape, jnp.float32)
    for index, number in numbers:
        line = jnp.where(lanes == index, number, line)
    return line


def box_sums(box, zone, scale, load, diffusivity, decay, out, table):
    step = 4
    nothing = jnp.zeros((box.across, box.deep), jnp.float32)
    half = [[0.5 * diffusivity[z, d] for z in range(3)] for d in range(3)]
    rates = [decay[z] for z in range(3)]

    def halves(row):
        labels, factor = zone[row], scale[row]
        return [looked_up(labels, half[d]) * factor for d in range(3)] + [looked_up(labels, rates)]

    def some_rows(index, sums):
        for row in range(step):
            row = index * step + row
            sums = [total + more for total, more in zip(sums, halves(row) + [load[row]])]
        return sums

    sums = lax.fori_loop(0, box.long // step, some_rows, [nothing] * 5)

    def total(values):
        return jnp.sum(values, keepdims=True).reshape(1, 1)

    cells = box.long * box.across * box.deep
    numbers = [(index, total(sums[index]) * (2.0 / cells)) for index in range(3)]
    mass = total(sums[3])
    numbers += [(3, mass / cells)]
    ends = total(sums[2][:, :1]) + total(sums[2][:, box.deep - 1 :])
    numbers += [
        (BOX_DIAGONAL, mass + ends),
        (LONG_HIGH, total(halves(box.long - 1)[0])),
        (LONG_LOW, total(halves(0)[0])),
        (ACROSS_HIGH, total(sums[1][box.across - 1 :])),
        (ACROSS_LOW, total(sums[1][:1])),
        (LOAD_SUM, total(sums[4])),
    ]
    line = line_of(numbers, out.shape)
    out[...] = line
    table[...] = at_own_row(line, table.shape)


def means_of(ref):
    return [ref[0:1, index : index + 1] for index in range(4)]


def first_solve(box, load, low, high, left, right, means, *rest):
    tables = rest[:N_TABLES]
    window, local, spectral, middle = rest[N_TABLES:]
    _, across_pos, _, across_count = position()
    has_left, has_right = as_float(across_pos > 0), as_float(across_pos < across_count - 1)

    def inside(values, row_side, col_side):
        if col_side == 0:
            return values
        return values * (has_left if col_side < 0 else has_right)

    fill_window(box, window, load, low[...], high[...], left, right, MARGIN, 0, MARGIN, inside)

    def emit(start, values):
        values = values * (1.0 / cheb_center)
        local[start : start + 8] = values.reshape(8, box.across, box.deep)

    box_solve(
        box,
        window.at[1 : 1 + box.ex],
        means_of(means),
        tables,
        None,
        None,
        spectral,
        middle,
        emit,
    )


def weights_of(
    box,
    zone,
    scale,
    low,
    high,
    left,
    right,
    diffusivity,
    decay,
    to_long,
    to_across,
    to_deep,
    mass,
    zone_window,
    scale_window,
):
    for index, (window, own) in enumerate(((scale_window, scale), (zone_window, zone))):
        part = slice(index * REACH, (index + 1) * REACH)
        fill_window(
            box, window, own, low[part], high[part], left, right, REACH, part.start, 2 * REACH
        )
    half = [[0.5 * diffusivity[z, d] for d in range(3)] for z in range(3)]
    rates = [decay[z] for z in range(3)]
    lane = lax.broadcasted_iota(jnp.int32, (box.cols, box.deep), 1)
    ends = jnp.where((lane == 0) | (lane == box.deep - 1), jnp.float32(1.0), jnp.float32(0.0))
    not_last = jnp.where(lane == box.deep - 1, jnp.float32(0.0), jnp.float32(1.0))

    def one_row(row, before):
        labels, factor = zone_window[row], scale_window[row]
        now = [looked_up(labels, [half[z][d] for z in range(3)]) * factor for d in range(3)]
        to_across[row] = now[1] + pltpu.roll(now[1], box.cols - 1, 0)
        to_deep[row] = (now[2] + pltpu.roll(now[2], box.deep - 1, 1)) * not_last
        mass[row] = looked_up(labels, rates) + now[2] * ends
        to_long[jnp.maximum(row - 1, 0)] = before + now[0]
        return now[0]

    last_long = lax.fori_loop(0, box.rows - 2, one_row, jnp.zeros_like(ends), unroll=4)
    for row in range(box.rows - 2, box.rows):
        last_long = one_row(row, last_long)
    to_long[box.rows - 1] = last_long


def image_sums(
    box, zone, scale, local, low, high, left, right, table, diffusivity, decay, out, up, down
):
    half = [[0.5 * diffusivity[z, d] for z in range(3)] for d in range(3)]
    rates = [decay[z] for z in range(3)]
    lane = lax.broadcasted_iota(jnp.int32, (box.across, box.deep), 1)
    ends = jnp.where((lane == 0) | (lane == box.deep - 1), jnp.float32(1.0), jnp.float32(0.0))
    step = 8

    def add_rows(index, total):
        for row in range(step):
            row = index * step + row
            labels = zone[row]
            mass = looked_up(labels, rates) + looked_up(labels, half[2]) * scale[row] * ends
            total = total + mass * local[row]
        return total

    nothing = jnp.zeros((box.across, box.deep), jnp.float32)
    image = lax.fori_loop(0, box.long // step, add_rows, nothing)
    shape = (box.long * box.across, box.deep)
    zone_flat, scale_flat, local_flat = zone.reshape(shape), scale.reshape(shape), local.reshape(shape)
    last_col = row_of(box.across, box.across - 1, box.long)
    first_col = row_of(box.across, 0, box.long)

    def side(ref, place):
        return ref[place * box.long : (place + 1) * box.long, :]

    faces = [
        (0, zone[box.long - 1], scale[box.long - 1], local[box.long - 1], high[REACH], high[0]),
        (0, zone[0], scale[0], local[0], low[2 * REACH - 1], low[REACH - 1]),
        (
            1,
            zone_flat[last_col, :],
            scale_flat[last_col, :],
            local_flat[last_col, :],
            side(right, REACH),
            side(right, 0),
        ),
        (
            1,
            zone_flat[first_col, :],
            scale_flat[first_col, :],
            local_flat[first_col, :],
            side(left, 2 * REACH - 1),
            side(left, REACH - 1),
        ),
    ]
    flows = []
    for direction, labels, factor, values, far_labels, far_factor in faces:
        weight = looked_up(labels, half[direction]) * factor
        weight = weight + looked_up(far_labels, half[direction]) * far_factor
        flows.append(jnp.sum(weight * values, keepdims=True))
    long_pos, across_pos, long_count, across_count = position()
    numbers = [
        (IMAGE_SUM, jnp.sum(image, keepdims=True) + sum(flows)),
        (FLOW_LONG_HIGH, flows[0] * as_float(long_pos < long_count - 1)),
        (FLOW_LONG_LOW, flows[1] * as_float(long_pos > 0)),
        (FLOW_ACROSS_HIGH, flows[2] * as_float(across_pos < across_count - 1)),
        (FLOW_ACROSS_LOW, flows[3] * as_float(across_pos > 0)),
    ]
    count = out.shape[0]
    known = merged(table[...], left[left.shape[0] - count :, :], right[right.shape[0] - count :, :])
    known = known + at_own_row(line_of(numbers, (8, known.shape[1])), known.shape)
    out[...] = known
    edge = REACH * box.across
    up[:edge] = local_flat[shape[0] - edge :, :]
    up[edge:] = known
    down[:edge] = local_flat[:edge, :]
    down[edge:] = known


def column(values, index):
    return values[:, index : index + 1]


def coarse_inverse(told, inverse, work):
    count, width = work.shape
    across = lax.axis_size("narrow")
    numbers = told[...]
    beyond = pltpu.roll(numbers, count - across, 0)
    beside = pltpu.roll(numbers, count - 1, 0)
    before = pltpu.roll(numbers, across, 0)
    ahead = pltpu.roll(numbers, 1, 0)
    place = lax.broadcasted_iota(jnp.int32, (count, 1), 0)
    across_pos = lax.rem(place, across)
    nothing = jnp.zeros((count, 1), jnp.float32)
    couplings = []
    diagonal = column(numbers, BOX_DIAGONAL)
    for own, other, there, inside in (
        (LONG_HIGH, LONG_LOW, beyond, place < count - across),
        (LONG_LOW, LONG_HIGH, before, place >= across),
        (ACROSS_HIGH, ACROSS_LOW, beside, across_pos < across - 1),
        (ACROSS_LOW, ACROSS_HIGH, ahead, across_pos > 0),
    ):
        shared = jnp.where(inside, column(there, other), nothing)
        diagonal = diagonal + column(numbers, own) + shared
        couplings.append(jnp.where(inside, column(numbers, own) + shared, nothing))
    rows = lax.broadcasted_iota(jnp.int32, (count, width), 0)
    cols = lax.broadcasted_iota(jnp.int32, (count, width), 1)
    blank = jnp.zeros((count, width), jnp.float32)
    matrix = jnp.where(cols == rows, diagonal, blank)
    for shift, coupling in zip((across, -across, 1, -1), couplings):
        matrix = matrix - jnp.where((cols == rows + shift) & (cols < count), coupling, blank)
    matrix = jnp.where(cols == rows + count, jnp.ones((count, 1), jnp.float32), matrix)
    work[...] = matrix

    def eliminate(step, _):
        values = work[...]
        pivot_row = work[pl.ds(step, 1), :]
        at_step = cols == step
        factors = jnp.sum(jnp.where(at_step, values, blank), axis=1, keepdims=True)
        pivot = jnp.sum(jnp.where(at_step[:1], pivot_row, blank[:1]), axis=1, keepdims=True)
        pivot_row = pivot_row / pivot
        work[...] = jnp.where(rows == step, pivot_row, values - factors * pivot_row)
        return 0

    lax.fori_loop(0, count, eliminate, 0)
    values = work[...]
    if count % 128:
        inverse[...] = pltpu.roll(values, width - count, 1)[:, : inverse.shape[1]]
    else:
        inverse[...] = values[:, count : 2 * count]


def answer(inverse, sums):
    return jnp.sum(inverse[...] * sums, axis=0, keepdims=True)


def at_box(values, row_side, col_side):
    long_pos, across_pos, long_count, across_count = position()
    there_long, there_across = long_pos + row_side, across_pos + col_side
    inside = (
        (there_long >= 0)
        & (there_long < long_count)
        & (there_across >= 0)
        & (there_across < across_count)
    )
    lanes = lax.broadcasted_iota(jnp.int32, values.shape, 1)
    wanted = (lanes == there_long * across_count + there_across) & inside
    return jnp.sum(jnp.where(wanted, values, jnp.zeros_like(values)), axis=1, keepdims=True)


def second_solve(box, local, low, high, left, right, inverse, told, means, *rest):
    to_long, to_across, to_deep, mass, load_window = rest[:5]
    tables = rest[5 : 5 + N_TABLES]
    iterate, window, residual, spectral, middle = rest[5 + N_TABLES :]
    long_pos, across_pos, long_count, across_count = position()
    coarse = answer(inverse, column(told, LOAD_SUM)) * (1.0 / cheb_center)
    shifts = {
        (row_side, col_side): at_box(coarse, row_side, col_side)
        for row_side in (-1, 0, 1)
        for col_side in (-1, 0, 1)
    }

    def add(values, row_side, col_side):
        shift = shifts[row_side, col_side]
        if values.ndim == 3:
            shift = shift.reshape(1, 1, 1)
        return values + shift

    edge = REACH * box.across
    low, high = (ref[:edge, :].reshape(REACH, box.across, box.deep) for ref in (low, high))
    fill_window(box, window, local, low, high, left, right, REACH, 0, REACH, add)
    weights = (to_long, to_across, to_deep, mass)

    def one_row(row, flow):
        image, flow = negative_image(row, window[row], window[row + 1], flow, weights)
        residual[row - 1] = load_window[row] + image
        return flow

    flow = to_long[0] * (window[1] - window[0])
    lax.fori_loop(1, 1 + box.ex, one_row, flow, unroll=4)
    inner = slice(EDGE, EDGE + box.across)
    first = REACH
    row_ids = lax.broadcasted_iota(jnp.int32, (1, padded(box.ex)), 1)
    col_ids = lax.broadcasted_iota(jnp.int32, (1, box.cols), 1)
    row_mask = jnp.where(row_ids < MARGIN, as_float(long_pos > 0), 1.0)
    row_mask = jnp.where(row_ids >= MARGIN + box.long, as_float(long_pos < long_count - 1), row_mask)
    col_mask = jnp.where(col_ids < EDGE, as_float(across_pos > 0), 1.0)
    col_mask = jnp.where(
        col_ids >= EDGE + box.across, as_float(across_pos < across_count - 1), col_mask
    )
    keep = 1.0 + rho_second * rho_first

    def emit(start, values):
        rows = values.reshape(8, box.across, box.deep)
        before = window[first + start : first + start + 8, inner, :]
        iterate[start : start + 8] = keep * before + gain * rows

    box_solve(
        box, residual, means_of(means), tables, row_mask, col_mask, spectral, middle, emit
    )


def correct_faces(
    box, partial, inverse, table, more, shift, top, bottom, last_col, first_col
):
    count = table.shape[0]
    across_count = lax.axis_size("narrow")
    numbers = merged(table[...], more[...])
    sums = column(numbers, IMAGE_SUM)
    sums = sums - column(pltpu.roll(numbers, count - across_count, 0), FLOW_LONG_LOW)
    sums = sums - column(pltpu.roll(numbers, across_count, 0), FLOW_LONG_HIGH)
    sums = sums - column(pltpu.roll(numbers, count - 1, 0), FLOW_ACROSS_LOW)
    sums = sums - column(pltpu.roll(numbers, 1, 0), FLOW_ACROSS_HIGH)
    sums = column(numbers, LOAD_SUM) * (1.0 - 1.0 / cheb_center) - sums
    own = at_box(answer(inverse, sums) * gain, 0, 0)
    shift[...] = jnp.broadcast_to(own, shift.shape)
    top[...] = partial[box.long - 1] + own
    bottom[...] = partial[0] + own
    flat = partial.reshape(box.long * box.across, box.deep)
    last_col[...] = flat[row_of(box.across, box.across - 1, box.long), :] + own
    first_col[...] = flat[row_of(box.across, 0, box.long), :] + own


def last_residual(
    box,
    load,
    partial,
    low,
    high,
    left,
    right,
    shift,
    to_long,
    to_across,
    to_deep,
    mass,
    iterate,
    out,
    window,
    result,
    sems,
):
    inner = slice(EDGE, EDGE + box.across)
    flat = window.reshape((box.long + 2) * box.cols, box.deep)
    blank = jnp.zeros((box.long + 2, EDGE, box.deep), jnp.float32)
    window[:, :EDGE, :] = blank
    window[:, EDGE + box.across :, :] = blank
    window[1 : 1 + box.long, inner, :] = partial[...] + shift[0:1, :].reshape(1, 1, box.deep)
    own = pltpu.make_async_copy(window.at[1 : 1 + box.long, inner, :], iterate, sems.at[0])
    own.start()
    window[0, inner, :] = low[...]
    window[1 + box.long, inner, :] = high[...]
    flat[row_of(box.cols, EDGE - 1, box.long, 1), :] = left[...]
    flat[row_of(box.cols, EDGE + box.across, box.long, 1), :] = right[...]
    weights = (to_long, to_across, to_deep, mass)

    def one_row(row, flow):
        image, flow = negative_image(REACH + row, window[row + 1], window[row + 2], flow, weights)
        result[row] = load[row] + image[inner]
        return flow

    flow = to_long[REACH - 1] * (window[1] - window[0])
    chunk = box.long // 4
    copies = [own]
    for index in range(4):
        rows = slice(index * chunk, (index + 1) * chunk)
        flow = lax.fori_loop(rows.start, rows.stop, one_row, flow, unroll=4)
        copy = pltpu.make_async_copy(result.at[rows], out.at[rows], sems.at[1 + index])
        copy.start()
        copies.append(copy)
    for copy in copies:
        copy.wait()


def exchange(axis, last, first, around=False):
    size = lax.axis_size(axis)
    up = [(i, (i + 1) % size) for i in range(size if around else size - 1)]
    down = [(j, i) for i, j in up]
    return lax.ppermute(last, axis, up), lax.ppermute(first, axis, down)


def two_away(axis, table):
    size = lax.axis_size(axis)
    return lax.ppermute(table, axis, [(i, (i + 2) % size) for i in range(size)])


def tell(table):
    count = table.shape[0]
    long_pos, across_pos, _, across_count = position()
    own = lax.dynamic_slice_in_dim(table, long_pos * across_count + across_pos, 1, axis=0)
    line = jnp.broadcast_to(own, (count, 1, 128))
    told = lax.all_to_all(line, ("wide", "narrow"), split_axis=0, concat_axis=0, tiled=True)
    return told.reshape(count, 128)


def on_device(zone, scale, diffusivity, decay, load):
    box = Box(load.shape)
    long, across, deep = load.shape
    count = lax.axis_size("wide") * lax.axis_size("narrow")
    by_margins = lax.axis_size("wide") == 4 and lax.axis_size("narrow") == 4
    tables = tables_of(box)
    cells = f32(long, across, deep)
    window = f32(box.rows, box.cols, deep)
    table_shape = f32(count, 128)

    def scratch(shape):
        return pltpu.VMEM(shape, jnp.float32)

    spectral = scratch((box.ey, padded(box.ex), deep))
    middle = scratch((long, padded(box.ey), deep))

    def pack(wide, fields, *refs):
        message = f32(message_rows(box, wide * fields) + count, deep)
        body = functools.partial(pack_fields, box, wide, count, fields)
        return call(body, (message, message, table_shape), [VMEM] * len(refs))(*refs)

    far = f32(2 * REACH, across, deep)
    zone, scale, load, load_up, load_down, up, down = call(
        functools.partial(bring_in, box),
        (jax.ShapeDtypeStruct(cells.shape, zone.dtype), cells, cells)
        + (f32(MARGIN, across, deep),) * 2
        + (far, far),
        [pl.BlockSpec(memory_space=pltpu.HBM)] * 3,
        [pltpu.VMEM((2, REACH, across, deep), zone.dtype), pltpu.SemaphoreType.DMA((9,))],
    )(*(pltpu.with_memory_space_constraint(field, pltpu.HBM) for field in (zone, scale, load)))
    load_low, load_high = exchange("wide", load_up, load_down)
    far_low, far_high = exchange("wide", up, down)
    sums, table = call(
        functools.partial(box_sums, box), (f32(8, 128), table_shape), [VMEM] * 3 + [SMEM] * 2
    )(zone, scale, load, diffusivity, decay)
    own_table = table
    up, down, _ = pack(MARGIN, 1, load, load_low, load_high, table)
    load_left, load_right = exchange("narrow", up, down, by_margins)
    up, down, table = pack(REACH, 2, scale, zone, far_low, far_high, table, load_left, load_right)
    far_left, far_right = exchange("narrow", up, down)
    load_window, local = call(
        functools.partial(first_solve, box),
        (window, cells),
        [VMEM] * (6 + N_TABLES),
        [spectral, middle],
        flops=4 * 10**9,
    )(load, load_low, load_high, load_left, load_right, sums, *tables)
    message = f32(REACH * across + count, deep)
    table, up, down = call(
        functools.partial(image_sums, box), (table_shape, message, message), [VMEM] * 8 + [SMEM] * 2
    )(zone, scale, local, far_low, far_high, far_left, far_right, table, diffusivity, decay)
    image_table = table
    low, high = exchange("wide", up, down)
    to_long, to_across, to_deep, mass = call(
        functools.partial(weights_of, box),
        (window,) * 4,
        [VMEM] * 6 + [SMEM] * 2,
        [scratch(window.shape)] * 2,
        flops=10**9,
    )(zone, scale, far_low, far_high, far_left, far_right, diffusivity, decay)
    joined = functools.partial(call, merge, table_shape, [VMEM] * 3)
    if by_margins:
        table = joined()(table, low, high)
        more = two_away("wide", table)
        up, down, table = pack(REACH, 1, local, low, high, table, more)
        load_table = table
    else:
        up, down, _ = pack(REACH, 1, local, low, high, table)
        load_table = tell(own_table)
    left, right = exchange("narrow", up, down)
    inverse = call(
        coarse_inverse,
        f32(count, -(-count // 128) * 128),
        [VMEM],
        [scratch((count, -(-2 * count // 128) * 128))],
    )(load_table)
    if by_margins:
        table = joined()(table, left, right)
        more = two_away("narrow", table)
    else:
        table = more = tell(image_table)
    row, col = f32(across, deep), f32(long, deep)
    partial = call(
        functools.partial(second_solve, box),
        cells,
        [VMEM] * (13 + N_TABLES),
        [scratch(window.shape), scratch((box.ex, box.cols, deep)), spectral, middle],
        flops=4 * 10**9,
    )(
        local,
        low,
        high,
        left,
        right,
        inverse,
        load_table,
        sums,
        to_long,
        to_across,
        to_deep,
        mass,
        load_window,
        *tables,
    )
    shift, top, bottom, last_col, first_col = call(
        functools.partial(correct_faces, box), (f32(8, deep), row, row, col, col), [VMEM] * 4
    )(partial, inverse, table, more)
    left, right = exchange("narrow", last_col, first_col)
    low, high = exchange("wide", top, bottom)
    return call(
        functools.partial(last_residual, box),
        (cells, cells),
        [VMEM] * 11,
        [scratch((long + 2, box.cols, deep)), scratch(cells.shape), pltpu.SemaphoreType.DMA((5,))],
        out_spec=pl.BlockSpec(memory_space=pl.ANY),
    )(
        load,
        partial,
        low,
        high,
        left,
        right,
        shift,
        to_long,
        to_across,
        to_deep,
        mass,
    )


def solution(mesh):
    split = P(("groups", "wide"), "narrow", None)
    return jax.shard_map(
        on_device,
        mesh=mesh,
        in_specs=(split, split, P(), P(), split),
        out_specs=(split, split),
        check_vma=False,
    )
```

```python
import functools

import jax
import jax.numpy as jnp
import ml_dtypes
import numpy as np
from jax import lax
from jax.experimental import pallas as pl
from jax.experimental.pallas import tpu as pltpu
from jax.sharding import PartitionSpec as P

MARGIN = 4
REACH = MARGIN + 1
EDGE = 8

cheb_center = 1.3
cheb_radius = 1.2
cheb_ratio = 1.3 / 1.2
rho_first = 1.0 / cheb_ratio
rho_second = 1.0 / (2.0 * cheb_ratio - rho_first)
gain = 2.0 * rho_second / cheb_radius

MEANS = range(4)
BOX_DIAGONAL, LONG_HIGH, LONG_LOW, ACROSS_HIGH, ACROSS_LOW, LOAD_SUM = range(4, 10)
IMAGE_SUM, FLOW_LONG_HIGH, FLOW_LONG_LOW, FLOW_ACROSS_HIGH, FLOW_ACROSS_LOW = range(16, 21)

VMEM = pl.BlockSpec(memory_space=pltpu.VMEM)
SMEM = pl.BlockSpec(memory_space=pltpu.SMEM)


def sine_basis(length):
    indices = np.arange(1, length + 1)
    phases = indices[:, None] * indices[None, :] % (2 * (length + 1))
    table = np.sqrt(2.0 / (length + 1)) * np.sin(np.pi * phases / (length + 1))
    eigvals = 4.0 * np.sin(np.pi * indices / (2.0 * (length + 1))) ** 2
    return table.astype(np.float32), eigvals.astype(np.float32)


def call(body, out_shape, in_specs, scratch=(), flops=0, moved=0, out_spec=VMEM):
    return pl.pallas_call(
        body,
        out_shape=out_shape,
        in_specs=in_specs,
        out_specs=jax.tree.map(lambda _: out_spec, out_shape),
        scratch_shapes=list(scratch),
        compiler_params=pltpu.CompilerParams(vmem_limit_bytes=30 * 2**20),
        cost_estimate=pl.CostEstimate(flops=flops, bytes_accessed=moved, transcendentals=0),
    )


def f32(*shape):
    return jax.ShapeDtypeStruct(shape, jnp.float32)


class Box:
    def __init__(self, shape):
        self.long, self.across, self.deep = shape
        self.ex = self.long + 2 * MARGIN
        self.ey = self.across + 2 * MARGIN
        self.rows = self.long + 2 * REACH
        self.cols = self.across + 2 * EDGE
        self.flat = self.rows * self.cols


def pieces(values, count):
    parts = []
    for _ in range(count):
        part = values.astype(jnp.bfloat16)
        parts.append(part)
        values = values - part.astype(jnp.float32)
    return parts


def left_table(table, depth, count):
    rows, cols = table.shape
    wide = np.zeros((rows, depth), np.float32)
    wide[:, :cols] = table
    parts = []
    rest = wide
    for _ in range(count):
        part = rest.astype(ml_dtypes.bfloat16)
        parts.append(part)
        rest = rest - part.astype(np.float32)
    blank = np.zeros_like(parts[0])
    lines = []
    for index in range(count):
        used = count - index if count > 2 else count
        lines.append(np.concatenate([parts[index]] * used + [blank] * (count - used), axis=1))
    return np.concatenate(lines, axis=0)


def right_tables(table):
    rest, parts = table, []
    for _ in range(3):
        part = rest.astype(ml_dtypes.bfloat16)
        parts.append(part)
        rest = rest - part.astype(np.float32)
    both = np.concatenate([parts[0], parts[1]], axis=1)
    return np.concatenate([both, both], axis=0), np.concatenate([parts[2], parts[0]], axis=0)


def padded(size):
    return -(-size // 16) * 16


FORWARD, BACKWARD = 2, 3


def tables_of(box):
    sine_x, eig_x = sine_basis(box.ex)
    sine_y, eig_y = sine_basis(box.ey)
    sine_z, eig_z = sine_basis(box.deep)
    skip = EDGE - MARGIN
    into_y = np.zeros((box.ey, box.cols), np.float32)
    into_y[:, skip : skip + box.ey] = sine_y
    from_y = sine_y[MARGIN : MARGIN + box.across]
    from_x = sine_x[MARGIN : MARGIN + box.long]
    spread = np.broadcast_to(eig_x[:, None], (box.ex, box.deep))
    main_z, rest_z = right_tables(sine_z)
    return [
        jnp.asarray(np.ascontiguousarray(t))
        for t in (
            left_table(into_y, box.cols, FORWARD),
            left_table(sine_x, padded(box.ex), FORWARD),
            left_table(from_x, padded(box.ex), BACKWARD),
            left_table(from_y, padded(box.ey), BACKWARD),
            main_z,
            rest_z,
            spread,
            eig_z[None, :],
            eig_y[None, :],
        )
    ]


N_TABLES = 9


def bf16_dot(left, right):
    return lax.dot_general(
        left, right, (((1,), (0,)), ((), ())), preferred_element_type=jnp.float32
    )


def dot_left(table, values, count, rows):
    total = bf16_dot(table, jnp.concatenate(pieces(values, count), axis=0))
    return sum(total[index * rows : (index + 1) * rows] for index in range(1, count)) + total[:rows]


def dot_right(values, main, rest, count):
    deep = values.shape[1]
    parts = pieces(values, count)
    total = bf16_dot(jnp.concatenate(parts[:2], axis=1), main)
    result = total[:, :deep] + total[:, deep:]
    if count == 3:
        result = result + bf16_dot(jnp.concatenate([parts[0], parts[2]], axis=1), rest)
    return result


def with_rows(values, rows):
    if values.shape[0] == rows:
        return values
    blank = jnp.zeros((rows - values.shape[0],) + values.shape[1:], values.dtype)
    return jnp.concatenate([values, blank], axis=0)


def box_solve(box, source, means, tables, row_mask, col_mask, spectral, middle, emit):
    into_y, into_x, from_x, from_y, main_z, rest_z, spread, eig_z, eig_y = tables
    deep = box.deep
    deep_x, deep_y = padded(box.ex), padded(box.ey)
    into_y, into_x = into_y[...], into_x[...]
    if col_mask is not None:
        mask = jnp.concatenate([col_mask] * FORWARD, axis=1)
        into_y = (into_y.astype(jnp.float32) * mask).astype(jnp.bfloat16)
        mask = jnp.concatenate([row_mask] * FORWARD, axis=1)
        into_x = (into_x.astype(jnp.float32) * mask).astype(jnp.bfloat16)
    from_x, from_y, main_z, rest_z = from_x[...], from_y[...], main_z[...], rest_z[...]
    spectral_flat = spectral.reshape(box.ey * deep_x, deep)
    middle_flat = middle.reshape(box.long * deep_y, deep)
    if deep_x > box.ex:
        spectral[:, box.ex :, :] = jnp.zeros((box.ey, deep_x - box.ex, deep), jnp.float32)
    if deep_y > box.ey:
        middle[:, box.ey :, :] = jnp.zeros((box.long, deep_y - box.ey, deep), jnp.float32)
    for start in range(0, box.ex, 8):
        block = source[start : start + 8].reshape(8 * box.cols, deep)
        block = dot_right(block, main_z, rest_z, FORWARD).reshape(8, box.cols, deep)
        for row in range(0, 8, 2):
            pair = jnp.concatenate([block[row], block[row + 1]], axis=1)
            pair = dot_left(into_y, pair, FORWARD, box.ey)
            for part in range(2):
                spectral_flat[pl.ds(start + row + part, box.ey, stride=deep_x), :] = pair[
                    :, part * deep : (part + 1) * deep
                ]
    base = means[3] + means[0] * spread[...] + means[2] * eig_z[...]
    for col in range(0, box.ey, 2):
        pair = jnp.concatenate([spectral[col], spectral[col + 1]], axis=1)
        pair = dot_left(into_x, pair, FORWARD, box.ex)
        pair = jnp.concatenate(
            [
                pair[:, part * deep : (part + 1) * deep]
                / (base + means[1] * eig_y[0, col + part])
                for part in range(2)
            ],
            axis=1,
        )
        pair = dot_left(from_x, with_rows(pair, deep_x), BACKWARD, box.long)
        for part in range(2):
            middle_flat[pl.ds(col + part, box.long, stride=deep_y), :] = pair[
                :, part * deep : (part + 1) * deep
            ]
    for start in range(0, box.long, 8):
        parts = []
        for row in range(start, start + 8, 2):
            pair = jnp.concatenate([middle[row], middle[row + 1]], axis=1)
            pair = dot_left(from_y, pair, BACKWARD, box.across)
            parts += [pair[:, :deep], pair[:, deep:]]
        emit(start, dot_right(jnp.concatenate(parts, axis=0), main_z, rest_z, BACKWARD))


def position():
    long_pos, across_pos = lax.axis_index("wide"), lax.axis_index("narrow")
    return long_pos, across_pos, lax.axis_size("wide"), lax.axis_size("narrow")


def as_float(flag):
    return jnp.where(flag, jnp.float32(1.0), jnp.float32(0.0))


def is_even(axis):
    return lax.rem(lax.axis_index(axis), 2) == 0


class Sides:
    def __init__(self, axis, first, second):
        position = lax.axis_index(axis)
        self.even = is_even(axis)
        self.has_low = as_float(position > 0)
        self.has_high = as_float(position < lax.axis_size(axis) - 1)
        self.first, self.second = first, second

    def low(self, *index):
        return jnp.where(self.even, self.second[index], self.first[index]) * self.has_low

    def high(self, *index):
        return jnp.where(self.even, self.first[index], self.second[index]) * self.has_high


def in_order(even, up, down):
    return jnp.where(even, up, down), jnp.where(even, down, up)


def row_of(stride, col, count, first=0):
    return pl.ds(first * stride + col, count, stride=stride)


def pack_columns(box, fields, wide_sides, wide, first, second):
    corner = len(fields) * wide * box.long
    even = is_even("narrow")
    place = 0
    for field, sides in zip(fields, wide_sides):
        for step in range(wide):
            cols = (box.across - wide + step, step)
            values = [field[row_of(box.across, col, box.long), :] for col in cols]
            low = [sides.low(row_of(box.across, col, wide), slice(None)) for col in cols]
            high = [sides.high(row_of(box.across, col, wide), slice(None)) for col in cols]
            at = corner + 2 * REACH * place
            for start, parts in ((place * box.long, values), (at, low), (at + REACH, high)):
                parts = in_order(even, *(part.astype(jnp.float32) for part in parts))
                size = parts[0].shape[0]
                first[start : start + size, :], second[start : start + size, :] = parts
            place += 1


def message_rows(box, count):
    return -(-(count * (box.long + 2 * REACH)) // 8) * 8


def pack_fields(box, wide, count, fields, *refs):
    own, (low, high), tables = refs[:fields], refs[fields : fields + 2], refs[fields + 2 : -3]
    up, down, table = refs[-3:]
    size = wide * box.across
    flat = [field.reshape(box.long * box.across, box.deep) for field in own]
    low = low.reshape(low.size // box.deep, box.deep)
    high = high.reshape(high.size // box.deep, box.deep)
    sides = [
        Sides("wide", *(ref.at[index * size : (index + 1) * size] for ref in (low, high)))
        for index in range(fields)
    ]
    pack_columns(box, flat, sides, wide, up, down)
    known = merged(*(ref[ref.shape[0] - count :, :] for ref in tables))
    table[...] = known
    up[up.shape[0] - count :, :] = known
    down[down.shape[0] - count :, :] = known


def bring_in(
    box, zone, scale, load, own_zone, own_scale, own_load, load_first, load_second, first, second,
    staged, sems
):
    even = is_even("wide")

    def edges(wide):
        up, down = box.long - wide, 0
        return [pl.ds(jnp.where(even, *pair), wide) for pair in ((up, down), (down, up))]

    copies = [
        (load.at[edges(MARGIN)[0]], load_first),
        (load.at[edges(MARGIN)[1]], load_second),
        (zone.at[edges(REACH)[0]], staged.at[0]),
        (zone.at[edges(REACH)[1]], staged.at[1]),
        (scale.at[edges(REACH)[0]], first.at[:REACH]),
        (scale.at[edges(REACH)[1]], second.at[:REACH]),
        (load, own_load),
        (scale, own_scale),
        (zone, own_zone),
    ]
    copies = [
        pltpu.make_async_copy(source, target, sems.at[index])
        for index, (source, target) in enumerate(copies)
    ]
    for copy in copies:
        copy.start()
    for copy in copies[:4]:
        copy.wait()
    first[REACH:] = staged[0].astype(jnp.float32)
    second[REACH:] = staged[1].astype(jnp.float32)
    for copy in copies[4:]:
        copy.wait()


def fill_window(box, window, own, wide_sides, narrow_sides, wide, place, total, add=None):
    flat = window.reshape(box.flat, box.deep)
    nothing = jnp.zeros((box.rows, EDGE, box.deep), jnp.float32)
    window[:, :EDGE, :] = nothing
    window[:, EDGE + box.across :, :] = nothing
    if add is None:
        add = lambda values, row_side, col_side: values
    inner = slice(EDGE, EDGE + box.across)
    first, last = REACH, REACH + box.long
    if wide < REACH:
        blank = jnp.zeros((1, box.across, box.deep), jnp.float32)
        window[0:1, inner, :] = blank
        window[box.rows - 1 :, inner, :] = blank
    window[first:last, inner, :] = add(own[...].astype(jnp.float32), 0, 0)
    window[first - wide : first, inner, :] = add(wide_sides.low(Ellipsis), -1, 0)
    window[last : last + wide, inner, :] = add(wide_sides.high(Ellipsis), 1, 0)
    corner = total * box.long
    for step in range(wide):
        for source, col, side in (
            (narrow_sides.low, EDGE - wide + step, -1),
            (narrow_sides.high, EDGE + box.across + step, 1),
        ):
            for start, size, row, row_side in (
                ((place + step) * box.long, box.long, first, 0),
                (corner + 2 * REACH * (place + step), wide, first - wide, -1),
                (corner + 2 * REACH * (place + step) + REACH, wide, last, 1),
            ):
                values = source(slice(start, start + size), slice(None))
                flat[row_of(box.cols, col, size, row), :] = add(values, row_side, side)


def negative_image(row, x, x_next, flow_before, weights):
    to_long, to_across, to_deep, mass = weights
    rows, lanes = x.shape
    flow_long = to_long[row] * (x_next - x)
    flow_across = to_across[row] * (pltpu.roll(x, rows - 1, 0) - x)
    flow_deep = to_deep[row] * (pltpu.roll(x, lanes - 1, 1) - x)
    total = flow_long - flow_before - mass[row] * x
    total = total + (flow_across - pltpu.roll(flow_across, 1, 0))
    total = total + (flow_deep - pltpu.roll(flow_deep, 1, 1))
    return total, flow_long


def looked_up(labels, values):
    return jnp.where(labels == 0, values[0], jnp.where(labels == 1, values[1], values[2]))


def at_own_row(line, shape):
    long_pos, across_pos, _, across_count = position()
    rows = lax.broadcasted_iota(jnp.int32, shape, 0)
    own = rows == long_pos * across_count + across_pos
    return jnp.where(own, line[:1], jnp.zeros(shape, jnp.float32))


def merged(table, *others):
    for other in others:
        table = jnp.where(table != 0.0, table, other)
    return table


def merge(table, low, high, out):
    count = table.shape[0]
    out[...] = merged(
        table[...], low[low.shape[0] - count :, :], high[high.shape[0] - count :, :]
    )


def line_of(numbers, shape):
    lanes = lax.broadcasted_iota(jnp.int32, shape, 1)
    line = jnp.zeros(shape, jnp.float32)
    for index, number in numbers:
        line = jnp.where(lanes == index, number, line)
    return line


def box_sums(box, zone, scale, load, diffusivity, decay, out, table):
    step = 4
    nothing = jnp.zeros((box.across, box.deep), jnp.float32)
    half = [[0.5 * diffusivity[z, d] for z in range(3)] for d in range(3)]
    rates = [decay[z] for z in range(3)]

    def halves(row):
        labels, factor = zone[row], scale[row]
        return [looked_up(labels, half[d]) * factor for d in range(3)] + [looked_up(labels, rates)]

    def some_rows(index, sums):
        for row in range(step):
            row = index * step + row
            sums = [total + more for total, more in zip(sums, halves(row) + [load[row]])]
        return sums

    sums = lax.fori_loop(0, box.long // step, some_rows, [nothing] * 5)

    def total(values):
        return jnp.sum(values, keepdims=True).reshape(1, 1)

    cells = box.long * box.across * box.deep
    numbers = [(index, total(sums[index]) * (2.0 / cells)) for index in range(3)]
    mass = total(sums[3])
    numbers += [(3, mass / cells)]
    ends = total(sums[2][:, :1]) + total(sums[2][:, box.deep - 1 :])
    numbers += [
        (BOX_DIAGONAL, mass + ends),
        (LONG_HIGH, total(halves(box.long - 1)[0])),
        (LONG_LOW, total(halves(0)[0])),
        (ACROSS_HIGH, total(sums[1][box.across - 1 :])),
        (ACROSS_LOW, total(sums[1][:1])),
        (LOAD_SUM, total(sums[4])),
    ]
    line = line_of(numbers, out.shape)
    out[...] = line
    table[...] = at_own_row(line, table.shape)


def means_of(ref):
    return [ref[0:1, index : index + 1] for index in range(4)]


def first_solve(box, load, low, high, left, right, means, *rest):
    tables = rest[:N_TABLES]
    window, local, spectral, middle = rest[N_TABLES:]
    wide_sides, narrow_sides = Sides("wide", low, high), Sides("narrow", left, right)
    fill_window(box, window, load, wide_sides, narrow_sides, MARGIN, 0, MARGIN)

    def emit(start, values):
        values = values * (1.0 / cheb_center)
        local[start : start + 8] = values.reshape(8, box.across, box.deep)

    box_solve(
        box,
        window.at[1 : 1 + box.ex],
        means_of(means),
        tables,
        None,
        None,
        spectral,
        middle,
        emit,
    )


def weights_of(
    box,
    zone,
    scale,
    low,
    high,
    left,
    right,
    diffusivity,
    decay,
    to_long,
    to_across,
    to_deep,
    mass,
    zone_window,
    scale_window,
):
    for index, (window, own) in enumerate(((scale_window, scale), (zone_window, zone))):
        start = index * REACH
        wide_sides = Sides("wide", *(ref.at[start : start + REACH] for ref in (low, high)))
        narrow_sides = Sides("narrow", left, right)
        fill_window(box, window, own, wide_sides, narrow_sides, REACH, start, 2 * REACH)
    half = [[0.5 * diffusivity[z, d] for d in range(3)] for z in range(3)]
    rates = [decay[z] for z in range(3)]
    lane = lax.broadcasted_iota(jnp.int32, (box.cols, box.deep), 1)
    ends = jnp.where((lane == 0) | (lane == box.deep - 1), jnp.float32(1.0), jnp.float32(0.0))
    not_last = jnp.where(lane == box.deep - 1, jnp.float32(0.0), jnp.float32(1.0))

    def one_row(row, before):
        labels, factor = zone_window[row], scale_window[row]
        now = [looked_up(labels, [half[z][d] for z in range(3)]) * factor for d in range(3)]
        to_across[row] = now[1] + pltpu.roll(now[1], box.cols - 1, 0)
        to_deep[row] = (now[2] + pltpu.roll(now[2], box.deep - 1, 1)) * not_last
        mass[row] = looked_up(labels, rates) + now[2] * ends
        to_long[jnp.maximum(row - 1, 0)] = before + now[0]
        return now[0]

    last_long = lax.fori_loop(0, box.rows - 2, one_row, jnp.zeros_like(ends), unroll=4)
    for row in range(box.rows - 2, box.rows):
        last_long = one_row(row, last_long)
    to_long[box.rows - 1] = last_long


def image_sums(
    box, zone, scale, local, low, high, left, right, table, diffusivity, decay, out, up, down
):
    half = [[0.5 * diffusivity[z, d] for z in range(3)] for d in range(3)]
    rates = [decay[z] for z in range(3)]
    lane = lax.broadcasted_iota(jnp.int32, (box.across, box.deep), 1)
    ends = jnp.where((lane == 0) | (lane == box.deep - 1), jnp.float32(1.0), jnp.float32(0.0))
    step = 8

    def add_rows(index, total):
        for row in range(step):
            row = index * step + row
            labels = zone[row]
            mass = looked_up(labels, rates) + looked_up(labels, half[2]) * scale[row] * ends
            total = total + mass * local[row]
        return total

    nothing = jnp.zeros((box.across, box.deep), jnp.float32)
    image = lax.fori_loop(0, box.long // step, add_rows, nothing)
    shape = (box.long * box.across, box.deep)
    zone_flat, scale_flat, local_flat = zone.reshape(shape), scale.reshape(shape), local.reshape(shape)
    last_col = row_of(box.across, box.across - 1, box.long)
    first_col = row_of(box.across, 0, box.long)

    wide_sides, narrow_sides = Sides("wide", low, high), Sides("narrow", left, right)

    def side(source, place):
        return source(slice(place * box.long, (place + 1) * box.long), slice(None))

    above, below = wide_sides.high, wide_sides.low
    faces = [
        (0, zone[box.long - 1], scale[box.long - 1], local[box.long - 1], above(REACH), above(0)),
        (0, zone[0], scale[0], local[0], below(2 * REACH - 1), below(REACH - 1)),
        (
            1,
            zone_flat[last_col, :],
            scale_flat[last_col, :],
            local_flat[last_col, :],
            side(narrow_sides.high, REACH),
            side(narrow_sides.high, 0),
        ),
        (
            1,
            zone_flat[first_col, :],
            scale_flat[first_col, :],
            local_flat[first_col, :],
            side(narrow_sides.low, 2 * REACH - 1),
            side(narrow_sides.low, REACH - 1),
        ),
    ]
    flows = []
    for direction, labels, factor, values, far_labels, far_factor in faces:
        weight = looked_up(labels, half[direction]) * factor
        weight = weight + looked_up(far_labels, half[direction]) * far_factor
        flows.append(jnp.sum(weight * values, keepdims=True))
    long_pos, across_pos, long_count, across_count = position()
    numbers = [
        (IMAGE_SUM, jnp.sum(image, keepdims=True) + sum(flows)),
        (FLOW_LONG_HIGH, flows[0] * as_float(long_pos < long_count - 1)),
        (FLOW_LONG_LOW, flows[1] * as_float(long_pos > 0)),
        (FLOW_ACROSS_HIGH, flows[2] * as_float(across_pos < across_count - 1)),
        (FLOW_ACROSS_LOW, flows[3] * as_float(across_pos > 0)),
    ]
    count = out.shape[0]
    known = merged(table[...], left[left.shape[0] - count :, :], right[right.shape[0] - count :, :])
    known = known + at_own_row(line_of(numbers, (8, known.shape[1])), known.shape)
    out[...] = known
    edge = REACH * box.across
    even = is_even("wide")
    for target, pair in ((up, (box.long - REACH, 0)), (down, (0, box.long - REACH))):
        target[:edge] = local[pl.ds(jnp.where(even, *pair), REACH)].reshape(edge, box.deep)
        target[edge:] = known


def column(values, index):
    return values[:, index : index + 1]


def coarse_inverse(told, inverse, work):
    count, width = work.shape
    across = lax.axis_size("narrow")
    numbers = told[...]
    beyond = pltpu.roll(numbers, count - across, 0)
    beside = pltpu.roll(numbers, count - 1, 0)
    before = pltpu.roll(numbers, across, 0)
    ahead = pltpu.roll(numbers, 1, 0)
    place = lax.broadcasted_iota(jnp.int32, (count, 1), 0)
    across_pos = lax.rem(place, across)
    nothing = jnp.zeros((count, 1), jnp.float32)
    couplings = []
    diagonal = column(numbers, BOX_DIAGONAL)
    for own, other, there, inside in (
        (LONG_HIGH, LONG_LOW, beyond, place < count - across),
        (LONG_LOW, LONG_HIGH, before, place >= across),
        (ACROSS_HIGH, ACROSS_LOW, beside, across_pos < across - 1),
        (ACROSS_LOW, ACROSS_HIGH, ahead, across_pos > 0),
    ):
        shared = jnp.where(inside, column(there, other), nothing)
        diagonal = diagonal + column(numbers, own) + shared
        couplings.append(jnp.where(inside, column(numbers, own) + shared, nothing))
    rows = lax.broadcasted_iota(jnp.int32, (count, width), 0)
    cols = lax.broadcasted_iota(jnp.int32, (count, width), 1)
    blank = jnp.zeros((count, width), jnp.float32)
    matrix = jnp.where(cols == rows, diagonal, blank)
    for shift, coupling in zip((across, -across, 1, -1), couplings):
        matrix = matrix - jnp.where((cols == rows + shift) & (cols < count), coupling, blank)
    matrix = jnp.where(cols == rows + count, jnp.ones((count, 1), jnp.float32), matrix)
    work[...] = matrix

    def eliminate(step, _):
        values = work[...]
        pivot_row = work[pl.ds(step, 1), :]
        at_step = cols == step
        factors = jnp.sum(jnp.where(at_step, values, blank), axis=1, keepdims=True)
        pivot = jnp.sum(jnp.where(at_step[:1], pivot_row, blank[:1]), axis=1, keepdims=True)
        pivot_row = pivot_row / pivot
        work[...] = jnp.where(rows == step, pivot_row, values - factors * pivot_row)
        return 0

    lax.fori_loop(0, count, eliminate, 0)
    values = work[...]
    if count % 128:
        inverse[...] = pltpu.roll(values, width - count, 1)[:, : inverse.shape[1]]
    else:
        inverse[...] = values[:, count : 2 * count]


def answer(inverse, sums):
    return jnp.sum(inverse[...] * sums, axis=0, keepdims=True)


def at_box(values, row_side, col_side):
    long_pos, across_pos, long_count, across_count = position()
    there_long, there_across = long_pos + row_side, across_pos + col_side
    inside = (
        (there_long >= 0)
        & (there_long < long_count)
        & (there_across >= 0)
        & (there_across < across_count)
    )
    lanes = lax.broadcasted_iota(jnp.int32, values.shape, 1)
    wanted = (lanes == there_long * across_count + there_across) & inside
    return jnp.sum(jnp.where(wanted, values, jnp.zeros_like(values)), axis=1, keepdims=True)


def second_solve(box, local, low, high, left, right, inverse, told, means, *rest):
    to_long, to_across, to_deep, mass, load_window = rest[:5]
    tables = rest[5 : 5 + N_TABLES]
    iterate, window, residual, spectral, middle = rest[5 + N_TABLES :]
    long_pos, across_pos, long_count, across_count = position()
    coarse = answer(inverse, column(told, LOAD_SUM)) * (1.0 / cheb_center)
    shifts = {
        (row_side, col_side): at_box(coarse, row_side, col_side)
        for row_side in (-1, 0, 1)
        for col_side in (-1, 0, 1)
    }

    def add(values, row_side, col_side):
        shift = shifts[row_side, col_side]
        if values.ndim == 3:
            shift = shift.reshape(1, 1, 1)
        return values + shift

    edge = REACH * box.across
    low, high = (
        ref.at[:edge].reshape(REACH, box.across, box.deep) for ref in (low, high)
    )
    wide_sides, narrow_sides = Sides("wide", low, high), Sides("narrow", left, right)
    fill_window(box, window, local, wide_sides, narrow_sides, REACH, 0, REACH, add)
    weights = (to_long, to_across, to_deep, mass)

    def one_row(row, flow):
        image, flow = negative_image(row, window[row], window[row + 1], flow, weights)
        residual[row - 1] = load_window[row] + image
        return flow

    flow = to_long[0] * (window[1] - window[0])
    lax.fori_loop(1, 1 + box.ex, one_row, flow, unroll=4)
    inner = slice(EDGE, EDGE + box.across)
    first = REACH
    row_ids = lax.broadcasted_iota(jnp.int32, (1, padded(box.ex)), 1)
    col_ids = lax.broadcasted_iota(jnp.int32, (1, box.cols), 1)
    row_mask = jnp.where(row_ids < MARGIN, as_float(long_pos > 0), 1.0)
    row_mask = jnp.where(row_ids >= MARGIN + box.long, as_float(long_pos < long_count - 1), row_mask)
    col_mask = jnp.where(col_ids < EDGE, as_float(across_pos > 0), 1.0)
    col_mask = jnp.where(
        col_ids >= EDGE + box.across, as_float(across_pos < across_count - 1), col_mask
    )
    keep = 1.0 + rho_second * rho_first

    def emit(start, values):
        rows = values.reshape(8, box.across, box.deep)
        before = window[first + start : first + start + 8, inner, :]
        iterate[start : start + 8] = keep * before + gain * rows

    box_solve(
        box, residual, means_of(means), tables, row_mask, col_mask, spectral, middle, emit
    )


def correct_faces(
    box, partial, inverse, table, more, shift, top, bottom, last_col, first_col
):
    count = table.shape[0]
    across_count = lax.axis_size("narrow")
    numbers = merged(table[...], more[...])
    sums = column(numbers, IMAGE_SUM)
    sums = sums - column(pltpu.roll(numbers, count - across_count, 0), FLOW_LONG_LOW)
    sums = sums - column(pltpu.roll(numbers, across_count, 0), FLOW_LONG_HIGH)
    sums = sums - column(pltpu.roll(numbers, count - 1, 0), FLOW_ACROSS_LOW)
    sums = sums - column(pltpu.roll(numbers, 1, 0), FLOW_ACROSS_HIGH)
    sums = column(numbers, LOAD_SUM) * (1.0 - 1.0 / cheb_center) - sums
    own = at_box(answer(inverse, sums) * gain, 0, 0)
    shift[...] = jnp.broadcast_to(own, shift.shape)
    rows = in_order(is_even("wide"), partial[box.long - 1], partial[0])
    top[...], bottom[...] = rows[0] + own, rows[1] + own
    flat = partial.reshape(box.long * box.across, box.deep)
    cols = [flat[row_of(box.across, col, box.long), :] for col in (box.across - 1, 0)]
    cols = in_order(is_even("narrow"), *cols)
    last_col[...], first_col[...] = cols[0] + own, cols[1] + own


def last_residual(
    box,
    load,
    partial,
    low,
    high,
    left,
    right,
    shift,
    to_long,
    to_across,
    to_deep,
    mass,
    iterate,
    out,
    window,
    result,
    sems,
):
    inner = slice(EDGE, EDGE + box.across)
    flat = window.reshape((box.long + 2) * box.cols, box.deep)
    blank = jnp.zeros((box.long + 2, EDGE, box.deep), jnp.float32)
    window[:, :EDGE, :] = blank
    window[:, EDGE + box.across :, :] = blank
    window[1 : 1 + box.long, inner, :] = partial[...] + shift[0:1, :].reshape(1, 1, box.deep)
    own = pltpu.make_async_copy(window.at[1 : 1 + box.long, inner, :], iterate, sems.at[0])
    own.start()
    wide_sides, narrow_sides = Sides("wide", low, high), Sides("narrow", left, right)
    window[0, inner, :] = wide_sides.low(Ellipsis)
    window[1 + box.long, inner, :] = wide_sides.high(Ellipsis)
    flat[row_of(box.cols, EDGE - 1, box.long, 1), :] = narrow_sides.low(Ellipsis)
    flat[row_of(box.cols, EDGE + box.across, box.long, 1), :] = narrow_sides.high(Ellipsis)
    weights = (to_long, to_across, to_deep, mass)

    def one_row(row, flow):
        image, flow = negative_image(REACH + row, window[row + 1], window[row + 2], flow, weights)
        result[row] = load[row] + image[inner]
        return flow

    flow = to_long[REACH - 1] * (window[1] - window[0])
    chunk = box.long // 4
    copies = [own]
    for index in range(4):
        rows = slice(index * chunk, (index + 1) * chunk)
        flow = lax.fori_loop(rows.start, rows.stop, one_row, flow, unroll=4)
        copy = pltpu.make_async_copy(result.at[rows], out.at[rows], sems.at[1 + index])
        copy.start()
        copies.append(copy)
    for copy in copies:
        copy.wait()


def exchange(axis, first, second, around=False):
    size = lax.axis_size(axis)
    swaps = []
    for way in range(2):
        pairs = []
        for place in range(size):
            other = place + 1 if place % 2 == way else place - 1
            if around and size % 2 == 0:
                other %= size
            pairs.append((place, other if 0 <= other < size else place))
        swaps.append(pairs)
    return lax.ppermute(first, axis, swaps[0]), lax.ppermute(second, axis, swaps[1])


def two_away(axis, table):
    size = lax.axis_size(axis)
    return lax.ppermute(table, axis, [(i, (i + 2) % size) for i in range(size)])


def tell(table):
    count = table.shape[0]
    long_pos, across_pos, _, across_count = position()
    own = lax.dynamic_slice_in_dim(table, long_pos * across_count + across_pos, 1, axis=0)
    line = jnp.broadcast_to(own, (count, 1, 128))
    told = lax.all_to_all(line, ("wide", "narrow"), split_axis=0, concat_axis=0, tiled=True)
    return told.reshape(count, 128)


def on_device(zone, scale, diffusivity, decay, load):
    box = Box(load.shape)
    long, across, deep = load.shape
    count = lax.axis_size("wide") * lax.axis_size("narrow")
    by_margins = lax.axis_size("wide") == 4 and lax.axis_size("narrow") == 4
    tables = tables_of(box)
    cells = f32(long, across, deep)
    window = f32(box.rows, box.cols, deep)
    table_shape = f32(count, 128)

    def scratch(shape):
        return pltpu.VMEM(shape, jnp.float32)

    spectral = scratch((box.ey, padded(box.ex), deep))
    middle = scratch((long, padded(box.ey), deep))

    def pack(wide, fields, *refs):
        message = f32(message_rows(box, wide * fields) + count, deep)
        body = functools.partial(pack_fields, box, wide, count, fields)
        return call(body, (message, message, table_shape), [VMEM] * len(refs))(*refs)

    far = f32(2 * REACH, across, deep)
    zone, scale, load, load_up, load_down, up, down = call(
        functools.partial(bring_in, box),
        (jax.ShapeDtypeStruct(cells.shape, zone.dtype), cells, cells)
        + (f32(MARGIN, across, deep),) * 2
        + (far, far),
        [pl.BlockSpec(memory_space=pltpu.HBM)] * 3,
        [pltpu.VMEM((2, REACH, across, deep), zone.dtype), pltpu.SemaphoreType.DMA((9,))],
    )(*(pltpu.with_memory_space_constraint(field, pltpu.HBM) for field in (zone, scale, load)))
    load_low, load_high = exchange("wide", load_up, load_down)
    far_low, far_high = exchange("wide", up, down)
    sums, table = call(
        functools.partial(box_sums, box), (f32(8, 128), table_shape), [VMEM] * 3 + [SMEM] * 2
    )(zone, scale, load, diffusivity, decay)
    own_table = table
    up, down, _ = pack(MARGIN, 1, load, load_low, load_high, table)
    load_left, load_right = exchange("narrow", up, down, by_margins)
    up, down, table = pack(REACH, 2, scale, zone, far_low, far_high, table, load_left, load_right)
    far_left, far_right = exchange("narrow", up, down)
    load_window, local = call(
        functools.partial(first_solve, box),
        (window, cells),
        [VMEM] * (6 + N_TABLES),
        [spectral, middle],
        flops=4 * 10**9,
    )(load, load_low, load_high, load_left, load_right, sums, *tables)
    message = f32(REACH * across + count, deep)
    table, up, down = call(
        functools.partial(image_sums, box), (table_shape, message, message), [VMEM] * 8 + [SMEM] * 2
    )(zone, scale, local, far_low, far_high, far_left, far_right, table, diffusivity, decay)
    image_table = table
    low, high = exchange("wide", up, down)
    to_long, to_across, to_deep, mass = call(
        functools.partial(weights_of, box),
        (window,) * 4,
        [VMEM] * 6 + [SMEM] * 2,
        [scratch(window.shape)] * 2,
        flops=10**9,
    )(zone, scale, far_low, far_high, far_left, far_right, diffusivity, decay)
    joined = functools.partial(call, merge, table_shape, [VMEM] * 3)
    if by_margins:
        table = joined()(table, low, high)
        more = two_away("wide", table)
        up, down, table = pack(REACH, 1, local, low, high, table, more)
        load_table = table
    else:
        up, down, _ = pack(REACH, 1, local, low, high, table)
        load_table = tell(own_table)
    left, right = exchange("narrow", up, down)
    inverse = call(
        coarse_inverse,
        f32(count, -(-count // 128) * 128),
        [VMEM],
        [scratch((count, -(-2 * count // 128) * 128))],
    )(load_table)
    if by_margins:
        table = joined()(table, left, right)
        more = two_away("narrow", table)
    else:
        table = more = tell(image_table)
    row, col = f32(across, deep), f32(long, deep)
    partial = call(
        functools.partial(second_solve, box),
        cells,
        [VMEM] * (13 + N_TABLES),
        [scratch(window.shape), scratch((box.ex, box.cols, deep)), spectral, middle],
        flops=4 * 10**9,
    )(
        local,
        low,
        high,
        left,
        right,
        inverse,
        load_table,
        sums,
        to_long,
        to_across,
        to_deep,
        mass,
        load_window,
        *tables,
    )
    shift, top, bottom, last_col, first_col = call(
        functools.partial(correct_faces, box), (f32(8, deep), row, row, col, col), [VMEM] * 4
    )(partial, inverse, table, more)
    left, right = exchange("narrow", last_col, first_col)
    low, high = exchange("wide", top, bottom)
    return call(
        functools.partial(last_residual, box),
        (cells, cells),
        [VMEM] * 11,
        [scratch((long + 2, box.cols, deep)), scratch(cells.shape), pltpu.SemaphoreType.DMA((5,))],
        out_spec=pl.BlockSpec(memory_space=pl.ANY),
    )(
        load,
        partial,
        low,
        high,
        left,
        right,
        shift,
        to_long,
        to_across,
        to_deep,
        mass,
    )


def solution(mesh):
    split = P(("groups", "wide"), "narrow", None)
    return jax.shard_map(
        on_device,
        mesh=mesh,
        in_specs=(split, split, P(), P(), split),
        out_specs=(split, split),
        check_vma=False,
    )
```

```python
import functools

import jax
import jax.numpy as jnp
import ml_dtypes
import numpy as np
from jax import lax
from jax.experimental import pallas as pl
from jax.experimental.pallas import tpu as pltpu
from jax.sharding import PartitionSpec as P

MARGIN = 4
REACH = MARGIN + 1
EDGE = 8

cheb_center = 1.3
cheb_radius = 1.2
cheb_ratio = 1.3 / 1.2
rho_first = 1.0 / cheb_ratio
rho_second = 1.0 / (2.0 * cheb_ratio - rho_first)
gain = 2.0 * rho_second / cheb_radius

MEANS = range(4)
BOX_DIAGONAL, LONG_HIGH, LONG_LOW, ACROSS_HIGH, ACROSS_LOW, LOAD_SUM = range(4, 10)
IMAGE_SUM, FLOW_LONG_HIGH, FLOW_LONG_LOW, FLOW_ACROSS_HIGH, FLOW_ACROSS_LOW = range(16, 21)

VMEM = pl.BlockSpec(memory_space=pltpu.VMEM)
SMEM = pl.BlockSpec(memory_space=pltpu.SMEM)


def sine_basis(length):
    indices = np.arange(1, length + 1)
    phases = indices[:, None] * indices[None, :] % (2 * (length + 1))
    table = np.sqrt(2.0 / (length + 1)) * np.sin(np.pi * phases / (length + 1))
    eigvals = 4.0 * np.sin(np.pi * indices / (2.0 * (length + 1))) ** 2
    return table.astype(np.float32), eigvals.astype(np.float32)


def call(body, out_shape, in_specs, scratch=(), flops=0, moved=0, out_spec=VMEM):
    return pl.pallas_call(
        body,
        out_shape=out_shape,
        in_specs=in_specs,
        out_specs=jax.tree.map(lambda _: out_spec, out_shape),
        scratch_shapes=list(scratch),
        compiler_params=pltpu.CompilerParams(vmem_limit_bytes=30 * 2**20),
        cost_estimate=pl.CostEstimate(flops=flops, bytes_accessed=moved, transcendentals=0),
    )


def f32(*shape):
    return jax.ShapeDtypeStruct(shape, jnp.float32)


class Box:
    def __init__(self, shape):
        self.long, self.across, self.deep = shape
        self.ex = self.long + 2 * MARGIN
        self.ey = self.across + 2 * MARGIN
        self.rows = self.long + 2 * REACH
        self.cols = self.across + 2 * EDGE
        self.flat = self.rows * self.cols


def pieces(values, count):
    parts = []
    for _ in range(count):
        part = values.astype(jnp.bfloat16)
        parts.append(part)
        values = values - part.astype(jnp.float32)
    return parts


def left_table(table, depth, count):
    rows, cols = table.shape
    wide = np.zeros((rows, depth), np.float32)
    wide[:, :cols] = table
    parts = []
    rest = wide
    for _ in range(count):
        part = rest.astype(ml_dtypes.bfloat16)
        parts.append(part)
        rest = rest - part.astype(np.float32)
    blank = np.zeros_like(parts[0])
    lines = []
    for index in range(count):
        used = count - index if count > 2 else count
        lines.append(np.concatenate([parts[index]] * used + [blank] * (count - used), axis=1))
    return np.concatenate(lines, axis=0)


def right_tables(table):
    rest, parts = table, []
    for _ in range(3):
        part = rest.astype(ml_dtypes.bfloat16)
        parts.append(part)
        rest = rest - part.astype(np.float32)
    both = np.concatenate([parts[0], parts[1]], axis=1)
    return np.concatenate([both, both], axis=0), np.concatenate([parts[2], parts[0]], axis=0)


def padded(size):
    return -(-size // 16) * 16


FORWARD, BACKWARD = 2, 3


def tables_of(box):
    sine_x, eig_x = sine_basis(box.ex)
    sine_y, eig_y = sine_basis(box.ey)
    sine_z, eig_z = sine_basis(box.deep)
    skip = EDGE - MARGIN
    into_y = np.zeros((box.ey, box.cols), np.float32)
    into_y[:, skip : skip + box.ey] = sine_y
    from_y = sine_y[MARGIN : MARGIN + box.across]
    from_x = sine_x[MARGIN : MARGIN + box.long]
    spread = np.broadcast_to(eig_x[:, None], (box.ex, box.deep))
    main_z, rest_z = right_tables(sine_z)
    return [
        jnp.asarray(np.ascontiguousarray(t))
        for t in (
            left_table(into_y, box.cols, FORWARD),
            left_table(sine_x, padded(box.ex), FORWARD),
            left_table(from_x, padded(box.ex), BACKWARD),
            left_table(from_y, padded(box.ey), BACKWARD),
            main_z,
            rest_z,
            spread,
            eig_z[None, :],
            eig_y[None, :],
        )
    ]


N_TABLES = 9


def bf16_dot(left, right):
    return lax.dot_general(
        left, right, (((1,), (0,)), ((), ())), preferred_element_type=jnp.float32
    )


def dot_left(table, values, count, rows):
    total = bf16_dot(table, jnp.concatenate(pieces(values, count), axis=0))
    return sum(total[index * rows : (index + 1) * rows] for index in range(1, count)) + total[:rows]


def dot_right(values, main, rest, count):
    deep = values.shape[1]
    parts = pieces(values, count)
    total = bf16_dot(jnp.concatenate(parts[:2], axis=1), main)
    result = total[:, :deep] + total[:, deep:]
    if count == 3:
        result = result + bf16_dot(jnp.concatenate([parts[0], parts[2]], axis=1), rest)
    return result


def with_rows(values, rows):
    if values.shape[0] == rows:
        return values
    blank = jnp.zeros((rows - values.shape[0],) + values.shape[1:], values.dtype)
    return jnp.concatenate([values, blank], axis=0)


def box_solve(box, source, means, tables, row_mask, col_mask, spectral, middle, emit):
    into_y, into_x, from_x, from_y, main_z, rest_z, spread, eig_z, eig_y = tables
    deep = box.deep
    deep_x, deep_y = padded(box.ex), padded(box.ey)
    into_y, into_x = into_y[...], into_x[...]
    if col_mask is not None:
        mask = jnp.concatenate([col_mask] * FORWARD, axis=1)
        into_y = (into_y.astype(jnp.float32) * mask).astype(jnp.bfloat16)
        mask = jnp.concatenate([row_mask] * FORWARD, axis=1)
        into_x = (into_x.astype(jnp.float32) * mask).astype(jnp.bfloat16)
    from_x, from_y, main_z, rest_z = from_x[...], from_y[...], main_z[...], rest_z[...]
    spectral_flat = spectral.reshape(box.ey * deep_x, deep)
    middle_flat = middle.reshape(box.long * deep_y, deep)
    if deep_x > box.ex:
        spectral[:, box.ex :, :] = jnp.zeros((box.ey, deep_x - box.ex, deep), jnp.float32)
    if deep_y > box.ey:
        middle[:, box.ey :, :] = jnp.zeros((box.long, deep_y - box.ey, deep), jnp.float32)
    for start in range(0, box.ex, 8):
        block = source[start : start + 8].reshape(8 * box.cols, deep)
        block = dot_right(block, main_z, rest_z, FORWARD).reshape(8, box.cols, deep)
        for row in range(0, 8, 2):
            pair = jnp.concatenate([block[row], block[row + 1]], axis=1)
            pair = dot_left(into_y, pair, FORWARD, box.ey)
            for part in range(2):
                spectral_flat[pl.ds(start + row + part, box.ey, stride=deep_x), :] = pair[
                    :, part * deep : (part + 1) * deep
                ]
    base = means[3] + means[0] * spread[...] + means[2] * eig_z[...]
    for col in range(0, box.ey, 2):
        pair = jnp.concatenate([spectral[col], spectral[col + 1]], axis=1)
        pair = dot_left(into_x, pair, FORWARD, box.ex)
        pair = jnp.concatenate(
            [
                pair[:, part * deep : (part + 1) * deep]
                / (base + means[1] * eig_y[0, col + part])
                for part in range(2)
            ],
            axis=1,
        )
        pair = dot_left(from_x, with_rows(pair, deep_x), BACKWARD, box.long)
        for part in range(2):
            middle_flat[pl.ds(col + part, box.long, stride=deep_y), :] = pair[
                :, part * deep : (part + 1) * deep
            ]
    for start in range(0, box.long, 8):
        parts = []
        for row in range(start, start + 8, 2):
            pair = jnp.concatenate([middle[row], middle[row + 1]], axis=1)
            pair = dot_left(from_y, pair, BACKWARD, box.across)
            parts += [pair[:, :deep], pair[:, deep:]]
        emit(start, dot_right(jnp.concatenate(parts, axis=0), main_z, rest_z, BACKWARD))


def position():
    long_pos, across_pos = lax.axis_index("wide"), lax.axis_index("narrow")
    return long_pos, across_pos, lax.axis_size("wide"), lax.axis_size("narrow")


def as_float(flag):
    return jnp.where(flag, jnp.float32(1.0), jnp.float32(0.0))


def is_even(axis):
    return lax.rem(lax.axis_index(axis), 2) == 0


class Sides:
    def __init__(self, axis, first, second):
        position = lax.axis_index(axis)
        self.even = is_even(axis)
        self.has_low = as_float(position > 0)
        self.has_high = as_float(position < lax.axis_size(axis) - 1)
        self.first, self.second = first, second

    def low(self, *index):
        return jnp.where(self.even, self.second[index], self.first[index]) * self.has_low

    def high(self, *index):
        return jnp.where(self.even, self.first[index], self.second[index]) * self.has_high


def in_order(even, up, down):
    return jnp.where(even, up, down), jnp.where(even, down, up)


def row_of(stride, col, count, first=0):
    return pl.ds(first * stride + col, count, stride=stride)


def pack_columns(box, fields, wide_sides, wide, first, second):
    corner = len(fields) * wide * box.long
    even = is_even("narrow")
    place = 0
    for field, sides in zip(fields, wide_sides):
        for step in range(wide):
            cols = (box.across - wide + step, step)
            values = [field[row_of(box.across, col, box.long), :] for col in cols]
            low = [sides.low(row_of(box.across, col, wide), slice(None)) for col in cols]
            high = [sides.high(row_of(box.across, col, wide), slice(None)) for col in cols]
            at = corner + 2 * REACH * place
            for start, parts in ((place * box.long, values), (at, low), (at + REACH, high)):
                parts = in_order(even, *(part.astype(jnp.float32) for part in parts))
                size = parts[0].shape[0]
                first[start : start + size, :], second[start : start + size, :] = parts
            place += 1


def message_rows(box, count):
    return -(-(count * (box.long + 2 * REACH)) // 8) * 8


def pack_fields(box, wide, fields, tables, after, *refs):
    own, (low, high), refs = refs[:fields], refs[fields : fields + 2], refs[fields + 2 :]
    parts, (first, second, *table) = refs[:tables], refs[tables + after :]
    size = wide * box.across
    flat = [field.reshape(box.long * box.across, box.deep) for field in own]
    low = low.reshape(low.size // box.deep, box.deep)
    high = high.reshape(high.size // box.deep, box.deep)
    sides = [
        Sides("wide", *(ref.at[index * size : (index + 1) * size] for ref in (low, high)))
        for index in range(fields)
    ]
    pack_columns(box, flat, sides, wide, first, second)
    if tables:
        known = last_rows_merged(parts, table[0].shape[0])
        table[0][...] = known
        first[first.shape[0] - known.shape[0] :, :] = known
        second[second.shape[0] - known.shape[0] :, :] = known


def bring_edges(
    box, zone, scale, load, own_load, load_first, load_second, first, second, staged, sems
):
    even = is_even("wide")

    def edges(wide):
        up, down = box.long - wide, 0
        return [pl.ds(jnp.where(even, *pair), wide) for pair in ((up, down), (down, up))]

    copies = [
        (load.at[edges(MARGIN)[0]], load_first),
        (load.at[edges(MARGIN)[1]], load_second),
        (zone.at[edges(REACH)[0]], staged.at[0]),
        (zone.at[edges(REACH)[1]], staged.at[1]),
        (scale.at[edges(REACH)[0]], first.at[:REACH]),
        (scale.at[edges(REACH)[1]], second.at[:REACH]),
        (load, own_load),
    ]
    copies = [
        pltpu.make_async_copy(source, target, sems.at[index])
        for index, (source, target) in enumerate(copies)
    ]
    for copy in copies:
        copy.start()
    for copy in copies[:4]:
        copy.wait()
    first[REACH:] = staged[0].astype(jnp.float32)
    second[REACH:] = staged[1].astype(jnp.float32)
    for copy in copies[4:]:
        copy.wait()


def fill_window(box, window, own, wide_sides, narrow_sides, wide, place, total, add=None):
    flat = window.reshape(box.flat, box.deep)
    nothing = jnp.zeros((box.rows, EDGE, box.deep), jnp.float32)
    window[:, :EDGE, :] = nothing
    window[:, EDGE + box.across :, :] = nothing
    if add is None:
        add = lambda values, row_side, col_side: values
    inner = slice(EDGE, EDGE + box.across)
    first, last = REACH, REACH + box.long
    if wide < REACH:
        blank = jnp.zeros((1, box.across, box.deep), jnp.float32)
        window[0:1, inner, :] = blank
        window[box.rows - 1 :, inner, :] = blank
    window[first:last, inner, :] = add(own[...].astype(jnp.float32), 0, 0)
    window[first - wide : first, inner, :] = add(wide_sides.low(Ellipsis), -1, 0)
    window[last : last + wide, inner, :] = add(wide_sides.high(Ellipsis), 1, 0)
    corner = total * box.long
    for step in range(wide):
        for source, col, side in (
            (narrow_sides.low, EDGE - wide + step, -1),
            (narrow_sides.high, EDGE + box.across + step, 1),
        ):
            for start, size, row, row_side in (
                ((place + step) * box.long, box.long, first, 0),
                (corner + 2 * REACH * (place + step), wide, first - wide, -1),
                (corner + 2 * REACH * (place + step) + REACH, wide, last, 1),
            ):
                values = source(slice(start, start + size), slice(None))
                flat[row_of(box.cols, col, size, row), :] = add(values, row_side, side)


def negative_image(row, x, x_next, flow_before, weights):
    to_long, to_across, to_deep, mass = weights
    rows, lanes = x.shape
    flow_long = to_long[row] * (x_next - x)
    flow_across = to_across[row] * (pltpu.roll(x, rows - 1, 0) - x)
    flow_deep = to_deep[row] * (pltpu.roll(x, lanes - 1, 1) - x)
    total = flow_long - flow_before - mass[row] * x
    total = total + (flow_across - pltpu.roll(flow_across, 1, 0))
    total = total + (flow_deep - pltpu.roll(flow_deep, 1, 1))
    return total, flow_long


def looked_up(labels, values):
    return jnp.where(labels == 0, values[0], jnp.where(labels == 1, values[1], values[2]))


def at_own_row(line, shape):
    long_pos, across_pos, _, across_count = position()
    rows = lax.broadcasted_iota(jnp.int32, shape, 0)
    own = rows == long_pos * across_count + across_pos
    return jnp.where(own, line[:1], jnp.zeros(shape, jnp.float32))


def merged(table, *others):
    for other in others:
        table = jnp.where(table != 0.0, table, other)
    return table


def last_rows_merged(refs, count):
    return merged(*(ref[ref.shape[0] - count :, :] for ref in refs))


def line_of(numbers, shape):
    lanes = lax.broadcasted_iota(jnp.int32, shape, 1)
    line = jnp.zeros(shape, jnp.float32)
    for index, number in numbers:
        line = jnp.where(lanes == index, number, line)
    return line


def box_sums(
    box, far_zone, far_scale, load, after, diffusivity, decay, zone, scale, out, table, sems
):
    del after
    parts = 2
    size = box.long // parts
    copies = []
    for part in range(parts):
        rows = slice(part * size, (part + 1) * size)
        for index, (source, target) in enumerate(((far_zone, zone), (far_scale, scale))):
            copy = pltpu.make_async_copy(
                source.at[rows], target.at[rows], sems.at[2 * part + index]
            )
            copy.start()
            copies.append(copy)
    step = 4
    nothing = jnp.zeros((box.across, box.deep), jnp.float32)
    half = [[0.5 * diffusivity[z, d] for z in range(3)] for d in range(3)]
    rates = [decay[z] for z in range(3)]

    def halves(row):
        labels, factor = zone[row], scale[row]
        return [looked_up(labels, half[d]) * factor for d in range(3)] + [looked_up(labels, rates)]

    def some_rows(index, sums):
        for row in range(step):
            row = index * step + row
            sums = [total + more for total, more in zip(sums, halves(row) + [load[row]])]
        return sums

    sums = [nothing] * 5
    for part in range(parts):
        for copy in copies[2 * part : 2 * part + 2]:
            copy.wait()
        per_part = size // step
        sums = lax.fori_loop(part * per_part, (part + 1) * per_part, some_rows, sums)

    def total(values):
        return jnp.sum(values, keepdims=True).reshape(1, 1)

    cells = box.long * box.across * box.deep
    numbers = [(index, total(sums[index]) * (2.0 / cells)) for index in range(3)]
    mass = total(sums[3])
    numbers += [(3, mass / cells)]
    ends = total(sums[2][:, :1]) + total(sums[2][:, box.deep - 1 :])
    numbers += [
        (BOX_DIAGONAL, mass + ends),
        (LONG_HIGH, total(halves(box.long - 1)[0])),
        (LONG_LOW, total(halves(0)[0])),
        (ACROSS_HIGH, total(sums[1][box.across - 1 :])),
        (ACROSS_LOW, total(sums[1][:1])),
        (LOAD_SUM, total(sums[4])),
    ]
    line = line_of(numbers, out.shape)
    out[...] = line
    table[...] = at_own_row(line, table.shape)


def means_of(ref):
    return [ref[0:1, index : index + 1] for index in range(4)]


def first_solve(box, load, low, high, left, right, means, *rest):
    tables = rest[:N_TABLES]
    window, local, spectral, middle = rest[N_TABLES:]
    wide_sides, narrow_sides = Sides("wide", low, high), Sides("narrow", left, right)
    fill_window(box, window, load, wide_sides, narrow_sides, MARGIN, 0, MARGIN)

    def emit(start, values):
        values = values * (1.0 / cheb_center)
        local[start : start + 8] = values.reshape(8, box.across, box.deep)

    box_solve(
        box,
        window.at[1 : 1 + box.ex],
        means_of(means),
        tables,
        None,
        None,
        spectral,
        middle,
        emit,
    )


def weights_of(
    box,
    zone,
    scale,
    low,
    high,
    left,
    right,
    diffusivity,
    decay,
    to_long,
    to_across,
    to_deep,
    mass,
    zone_window,
    scale_window,
):
    for index, (window, own) in enumerate(((scale_window, scale), (zone_window, zone))):
        start = index * REACH
        wide_sides = Sides("wide", *(ref.at[start : start + REACH] for ref in (low, high)))
        narrow_sides = Sides("narrow", left, right)
        fill_window(box, window, own, wide_sides, narrow_sides, REACH, start, 2 * REACH)
    half = [[0.5 * diffusivity[z, d] for d in range(3)] for z in range(3)]
    rates = [decay[z] for z in range(3)]
    lane = lax.broadcasted_iota(jnp.int32, (box.cols, box.deep), 1)
    ends = jnp.where((lane == 0) | (lane == box.deep - 1), jnp.float32(1.0), jnp.float32(0.0))
    not_last = jnp.where(lane == box.deep - 1, jnp.float32(0.0), jnp.float32(1.0))

    def one_row(row, before):
        labels, factor = zone_window[row], scale_window[row]
        now = [looked_up(labels, [half[z][d] for z in range(3)]) * factor for d in range(3)]
        to_across[row] = now[1] + pltpu.roll(now[1], box.cols - 1, 0)
        to_deep[row] = (now[2] + pltpu.roll(now[2], box.deep - 1, 1)) * not_last
        mass[row] = looked_up(labels, rates) + now[2] * ends
        to_long[jnp.maximum(row - 1, 0)] = before + now[0]
        return now[0]

    last_long = lax.fori_loop(0, box.rows - 2, one_row, jnp.zeros_like(ends), unroll=4)
    for row in range(box.rows - 2, box.rows):
        last_long = one_row(row, last_long)
    to_long[box.rows - 1] = last_long


def image_sums(
    box, zone, scale, local, low, high, left, right, table, diffusivity, decay, out, up, down
):
    half = [[0.5 * diffusivity[z, d] for z in range(3)] for d in range(3)]
    rates = [decay[z] for z in range(3)]
    lane = lax.broadcasted_iota(jnp.int32, (box.across, box.deep), 1)
    ends = jnp.where((lane == 0) | (lane == box.deep - 1), jnp.float32(1.0), jnp.float32(0.0))
    step = 8

    def add_rows(index, total):
        for row in range(step):
            row = index * step + row
            labels = zone[row]
            mass = looked_up(labels, rates) + looked_up(labels, half[2]) * scale[row] * ends
            total = total + mass * local[row]
        return total

    nothing = jnp.zeros((box.across, box.deep), jnp.float32)
    image = lax.fori_loop(0, box.long // step, add_rows, nothing)
    shape = (box.long * box.across, box.deep)
    zone_flat, scale_flat, local_flat = zone.reshape(shape), scale.reshape(shape), local.reshape(shape)
    last_col = row_of(box.across, box.across - 1, box.long)
    first_col = row_of(box.across, 0, box.long)

    wide_sides, narrow_sides = Sides("wide", low, high), Sides("narrow", left, right)

    def side(source, place):
        return source(slice(place * box.long, (place + 1) * box.long), slice(None))

    above, below = wide_sides.high, wide_sides.low
    faces = [
        (0, zone[box.long - 1], scale[box.long - 1], local[box.long - 1], above(REACH), above(0)),
        (0, zone[0], scale[0], local[0], below(2 * REACH - 1), below(REACH - 1)),
        (
            1,
            zone_flat[last_col, :],
            scale_flat[last_col, :],
            local_flat[last_col, :],
            side(narrow_sides.high, REACH),
            side(narrow_sides.high, 0),
        ),
        (
            1,
            zone_flat[first_col, :],
            scale_flat[first_col, :],
            local_flat[first_col, :],
            side(narrow_sides.low, 2 * REACH - 1),
            side(narrow_sides.low, REACH - 1),
        ),
    ]
    flows = []
    for direction, labels, factor, values, far_labels, far_factor in faces:
        weight = looked_up(labels, half[direction]) * factor
        weight = weight + looked_up(far_labels, half[direction]) * far_factor
        flows.append(jnp.sum(weight * values, keepdims=True))
    long_pos, across_pos, long_count, across_count = position()
    numbers = [
        (IMAGE_SUM, jnp.sum(image, keepdims=True) + sum(flows)),
        (FLOW_LONG_HIGH, flows[0] * as_float(long_pos < long_count - 1)),
        (FLOW_LONG_LOW, flows[1] * as_float(long_pos > 0)),
        (FLOW_ACROSS_HIGH, flows[2] * as_float(across_pos < across_count - 1)),
        (FLOW_ACROSS_LOW, flows[3] * as_float(across_pos > 0)),
    ]
    known = table[...] + at_own_row(line_of(numbers, (8, out.shape[1])), out.shape)
    out[...] = known
    edge = REACH * box.across
    even = is_even("wide")
    for target, pair in ((up, (box.long - REACH, 0)), (down, (0, box.long - REACH))):
        target[:edge] = local[pl.ds(jnp.where(even, *pair), REACH)].reshape(edge, box.deep)
        target[edge:] = known


def column(values, index):
    return values[:, index : index + 1]


def coarse_inverse(numbers, work):
    count, width = work.shape
    across = lax.axis_size("narrow")
    beyond = pltpu.roll(numbers, count - across, 0)
    beside = pltpu.roll(numbers, count - 1, 0)
    before = pltpu.roll(numbers, across, 0)
    ahead = pltpu.roll(numbers, 1, 0)
    place = lax.broadcasted_iota(jnp.int32, (count, 1), 0)
    across_pos = lax.rem(place, across)
    nothing = jnp.zeros((count, 1), jnp.float32)
    couplings = []
    diagonal = column(numbers, BOX_DIAGONAL)
    for own, other, there, inside in (
        (LONG_HIGH, LONG_LOW, beyond, place < count - across),
        (LONG_LOW, LONG_HIGH, before, place >= across),
        (ACROSS_HIGH, ACROSS_LOW, beside, across_pos < across - 1),
        (ACROSS_LOW, ACROSS_HIGH, ahead, across_pos > 0),
    ):
        shared = jnp.where(inside, column(there, other), nothing)
        diagonal = diagonal + column(numbers, own) + shared
        couplings.append(jnp.where(inside, column(numbers, own) + shared, nothing))
    rows = lax.broadcasted_iota(jnp.int32, (count, width), 0)
    cols = lax.broadcasted_iota(jnp.int32, (count, width), 1)
    blank = jnp.zeros((count, width), jnp.float32)
    matrix = jnp.where(cols == rows, diagonal, blank)
    for shift, coupling in zip((across, -across, 1, -1), couplings):
        matrix = matrix - jnp.where((cols == rows + shift) & (cols < count), coupling, blank)
    matrix = jnp.where(cols == rows + count, jnp.ones((count, 1), jnp.float32), matrix)
    if count <= 16:
        for step in range(count):
            pivot_row = matrix[step : step + 1, :] / matrix[step : step + 1, step : step + 1]
            rest = matrix - matrix[:, step : step + 1] * pivot_row
            matrix = jnp.where(rows == step, pivot_row, rest)
        return pltpu.roll(matrix, width - count, 1)
    work[...] = matrix

    def eliminate(step, _):
        values = work[...]
        pivot_row = work[pl.ds(step, 1), :]
        at_step = cols == step
        factors = jnp.sum(jnp.where(at_step, values, blank), axis=1, keepdims=True)
        pivot = jnp.sum(jnp.where(at_step[:1], pivot_row, blank[:1]), axis=1, keepdims=True)
        pivot_row = pivot_row / pivot
        work[...] = jnp.where(rows == step, pivot_row, values - factors * pivot_row)
        return 0

    lax.fori_loop(0, count, eliminate, 0)
    values = work[...]
    if count % 128:
        return pltpu.roll(values, width - count, 1)
    return values[:, count : 2 * count]


def answer(inverse, sums):
    return jnp.sum(inverse * sums, axis=0, keepdims=True)


def at_box(values, row_side, col_side):
    long_pos, across_pos, long_count, across_count = position()
    there_long, there_across = long_pos + row_side, across_pos + col_side
    inside = (
        (there_long >= 0)
        & (there_long < long_count)
        & (there_across >= 0)
        & (there_across < across_count)
    )
    lanes = lax.broadcasted_iota(jnp.int32, values.shape, 1)
    wanted = (lanes == there_long * across_count + there_across) & inside
    return jnp.sum(jnp.where(wanted, values, jnp.zeros_like(values)), axis=1, keepdims=True)


def coarse_corrections(box, numbers, work):
    count = numbers.shape[0]
    across_count = lax.axis_size("narrow")
    inverse = coarse_inverse(numbers, work)
    sums = column(numbers, IMAGE_SUM)
    sums = sums - column(pltpu.roll(numbers, count - across_count, 0), FLOW_LONG_LOW)
    sums = sums - column(pltpu.roll(numbers, across_count, 0), FLOW_LONG_HIGH)
    sums = sums - column(pltpu.roll(numbers, count - 1, 0), FLOW_ACROSS_LOW)
    sums = sums - column(pltpu.roll(numbers, 1, 0), FLOW_ACROSS_HIGH)
    load_sums = column(numbers, LOAD_SUM)
    sums = load_sums * (1.0 - 1.0 / cheb_center) - sums
    return answer(inverse, load_sums) * (1.0 / cheb_center), answer(inverse, sums) * gain


def second_solve(box, parts, local, low, high, left, right, means, *rest):
    table_parts, rest = rest[:parts], rest[parts:]
    to_long, to_across, to_deep, mass, load_window = rest[:5]
    tables = rest[5 : 5 + N_TABLES]
    iterate, top, bottom, last_col, first_col = rest[5 + N_TABLES : 10 + N_TABLES]
    window, residual, spectral, middle, work = rest[10 + N_TABLES :]
    long_pos, across_pos, long_count, across_count = position()
    numbers = last_rows_merged(table_parts, work.shape[0])
    coarse, second_coarse = coarse_corrections(box, numbers, work)
    own_shift = at_box(second_coarse, 0, 0)
    shifts = {
        (row_side, col_side): at_box(coarse, row_side, col_side)
        for row_side in (-1, 0, 1)
        for col_side in (-1, 0, 1)
    }

    def add(values, row_side, col_side):
        shift = shifts[row_side, col_side]
        if values.ndim == 3:
            shift = shift.reshape(1, 1, 1)
        return values + shift

    edge = REACH * box.across
    low, high = (
        ref.at[:edge].reshape(REACH, box.across, box.deep) for ref in (low, high)
    )
    wide_sides, narrow_sides = Sides("wide", low, high), Sides("narrow", left, right)
    fill_window(box, window, local, wide_sides, narrow_sides, REACH, 0, REACH, add)
    weights = (to_long, to_across, to_deep, mass)

    def one_row(row, flow):
        image, flow = negative_image(row, window[row], window[row + 1], flow, weights)
        residual[row - 1] = load_window[row] + image
        return flow

    flow = to_long[0] * (window[1] - window[0])
    lax.fori_loop(1, 1 + box.ex, one_row, flow, unroll=4)
    inner = slice(EDGE, EDGE + box.across)
    first = REACH
    row_ids = lax.broadcasted_iota(jnp.int32, (1, padded(box.ex)), 1)
    col_ids = lax.broadcasted_iota(jnp.int32, (1, box.cols), 1)
    row_mask = jnp.where(row_ids < MARGIN, as_float(long_pos > 0), 1.0)
    row_mask = jnp.where(row_ids >= MARGIN + box.long, as_float(long_pos < long_count - 1), row_mask)
    col_mask = jnp.where(col_ids < EDGE, as_float(across_pos > 0), 1.0)
    col_mask = jnp.where(
        col_ids >= EDGE + box.across, as_float(across_pos < across_count - 1), col_mask
    )
    keep = 1.0 + rho_second * rho_first

    def emit(start, values):
        rows = values.reshape(8, box.across, box.deep)
        before = window[first + start : first + start + 8, inner, :]
        shift = own_shift.reshape(1, 1, 1)
        iterate[start : start + 8] = keep * before + (gain * rows + shift)

    box_solve(
        box, residual, means_of(means), tables, row_mask, col_mask, spectral, middle, emit
    )
    rows = in_order(is_even("wide"), iterate[box.long - 1], iterate[0])
    top[...], bottom[...] = rows
    flat = iterate.reshape(box.long * box.across, box.deep)
    cols = [flat[row_of(box.across, col, box.long), :] for col in (box.across - 1, 0)]
    last_col[...], first_col[...] = in_order(is_even("narrow"), *cols)


def last_residual(
    box,
    load,
    partial,
    low,
    high,
    left,
    right,
    to_long,
    to_across,
    to_deep,
    mass,
    iterate,
    out,
    window,
    result,
    sems,
):
    inner = slice(EDGE, EDGE + box.across)
    flat = window.reshape((box.long + 2) * box.cols, box.deep)
    blank = jnp.zeros((box.long + 2, EDGE, box.deep), jnp.float32)
    window[:, :EDGE, :] = blank
    window[:, EDGE + box.across :, :] = blank
    window[1 : 1 + box.long, inner, :] = partial[...]
    own = pltpu.make_async_copy(window.at[1 : 1 + box.long, inner, :], iterate, sems.at[0])
    own.start()
    wide_sides, narrow_sides = Sides("wide", low, high), Sides("narrow", left, right)
    window[0, inner, :] = wide_sides.low(Ellipsis)
    window[1 + box.long, inner, :] = wide_sides.high(Ellipsis)
    flat[row_of(box.cols, EDGE - 1, box.long, 1), :] = narrow_sides.low(Ellipsis)
    flat[row_of(box.cols, EDGE + box.across, box.long, 1), :] = narrow_sides.high(Ellipsis)
    weights = (to_long, to_across, to_deep, mass)

    def one_row(row, flow):
        image, flow = negative_image(REACH + row, window[row + 1], window[row + 2], flow, weights)
        result[row] = load[row] + image[inner]
        return flow

    flow = to_long[REACH - 1] * (window[1] - window[0])
    chunk = box.long // 4
    copies = [own]
    for index in range(4):
        rows = slice(index * chunk, (index + 1) * chunk)
        flow = lax.fori_loop(rows.start, rows.stop, one_row, flow, unroll=4)
        copy = pltpu.make_async_copy(result.at[rows], out.at[rows], sems.at[1 + index])
        copy.start()
        copies.append(copy)
    for copy in copies:
        copy.wait()


def exchange(axis, first, second, around=False):
    size = lax.axis_size(axis)
    swaps = []
    for way in range(2):
        pairs = []
        for place in range(size):
            other = place + 1 if place % 2 == way else place - 1
            if around and size % 2 == 0:
                other %= size
            pairs.append((place, other if 0 <= other < size else place))
        swaps.append(pairs)
    return lax.ppermute(first, axis, swaps[0]), lax.ppermute(second, axis, swaps[1])


def two_away(axis, table):
    size = lax.axis_size(axis)
    return lax.ppermute(table, axis, [(i, (i + 2) % size) for i in range(size)])


def tell(table):
    count = table.shape[0]
    long_pos, across_pos, _, across_count = position()
    own = lax.dynamic_slice_in_dim(table, long_pos * across_count + across_pos, 1, axis=0)
    line = jnp.broadcast_to(own, (count, 1, 128))
    told = lax.all_to_all(line, ("wide", "narrow"), split_axis=0, concat_axis=0, tiled=True)
    return told.reshape(count, 128)


def on_device(zone, scale, diffusivity, decay, load):
    box = Box(load.shape)
    long, across, deep = load.shape
    count = lax.axis_size("wide") * lax.axis_size("narrow")
    by_margins = lax.axis_size("wide") == 4 and lax.axis_size("narrow") == 4
    tables = tables_of(box)
    cells = f32(long, across, deep)
    whole_zone = jax.ShapeDtypeStruct(cells.shape, zone.dtype)
    window = f32(box.rows, box.cols, deep)
    table_shape = f32(count, 128)
    anywhere = pl.BlockSpec(memory_space=pl.ANY)
    in_hbm = pl.BlockSpec(memory_space=pltpu.HBM)

    def scratch(shape):
        return pltpu.VMEM(shape, jnp.float32)

    def pinned(field):
        return pltpu.with_memory_space_constraint(field, pltpu.HBM)

    spectral = scratch((box.ey, padded(box.ex), deep))
    middle = scratch((long, padded(box.ey), deep))

    def pack(wide, fields, sides, parts=(), after=()):
        rows = message_rows(box, wide * len(fields)) + (count if parts else 0)
        message = f32(rows, deep)
        body = functools.partial(pack_fields, box, wide, len(fields), len(parts), len(after))
        return call(
            body,
            (message, message) + ((table_shape,) if parts else ()),
            [VMEM] * (len(fields) + 2 + len(parts)) + [anywhere] * len(after),
        )(*fields, *sides, *parts, *after)

    far = f32(2 * REACH, across, deep)
    far_zone, far_scale = zone, scale
    load, load_first, load_second, first, second = call(
        functools.partial(bring_edges, box),
        (cells,) + (f32(MARGIN, across, deep),) * 2 + (far, far),
        [in_hbm] * 3,
        [pltpu.VMEM((2, REACH, across, deep), zone.dtype), pltpu.SemaphoreType.DMA((7,))],
    )(pinned(zone), pinned(scale), pinned(load))
    load_wide = exchange("wide", load_first, load_second)
    far_wide = exchange("wide", first, second)
    load_first, load_second = pack(MARGIN, [load], load_wide)
    load_narrow = exchange("narrow", load_first, load_second)
    zone, scale, sums, table = call(
        functools.partial(box_sums, box),
        (whole_zone, cells, f32(8, 128), table_shape),
        [in_hbm] * 2 + [VMEM, anywhere] + [SMEM] * 2,
        [pltpu.SemaphoreType.DMA((4,))],
    )(pinned(far_zone), pinned(far_scale), load, load_first, diffusivity, decay)
    far_narrow = exchange("narrow", *pack(REACH, [scale, zone], far_wide))
    load_window, local = call(
        functools.partial(first_solve, box),
        (window, cells),
        [VMEM] * (6 + N_TABLES),
        [spectral, middle],
        flops=4 * 10**9,
    )(load, *load_wide, *load_narrow, sums, *tables)
    message = f32(REACH * across + count, deep)
    table, first, second = call(
        functools.partial(image_sums, box), (table_shape, message, message), [VMEM] * 8 + [SMEM] * 2
    )(zone, scale, local, *far_wide, *far_narrow, table, diffusivity, decay)
    own_table = table
    wide = exchange("wide", first, second, by_margins)
    parts = (table, *wide)
    if by_margins:
        parts += (two_away("wide", table),)
    weights = call(
        functools.partial(weights_of, box),
        (window,) * 4,
        [VMEM] * 6 + [SMEM] * 2,
        [scratch(window.shape)] * 2,
        flops=10**9,
    )(zone, scale, *far_wide, *far_narrow, diffusivity, decay)
    first, second, table = pack(REACH, [local], wide, parts, weights[3:])
    narrow = exchange("narrow", first, second, by_margins)
    if by_margins:
        parts = (table, *narrow, two_away("narrow", table))
    else:
        parts = (tell(own_table),)
    row, col = f32(across, deep), f32(long, deep)
    iterate, first_row, second_row, first_col, second_col = call(
        functools.partial(second_solve, box, len(parts)),
        (cells, row, row, col, col),
        [VMEM] * (11 + len(parts) + N_TABLES),
        [
            scratch(window.shape),
            scratch((box.ex, box.cols, deep)),
            spectral,
            middle,
            scratch((count, -(-2 * count // 128) * 128)),
        ],
        flops=4 * 10**9,
    )(local, *wide, *narrow, sums, *parts, *weights, load_window, *tables)
    narrow = exchange("narrow", first_col, second_col)
    wide = exchange("wide", first_row, second_row)
    return call(
        functools.partial(last_residual, box),
        (cells, cells),
        [VMEM] * 10,
        [scratch((long + 2, box.cols, deep)), scratch(cells.shape), pltpu.SemaphoreType.DMA((5,))],
        out_spec=anywhere,
    )(load, iterate, *wide, *narrow, *weights)


def solution(mesh):
    split = P(("groups", "wide"), "narrow", None)
    return jax.shard_map(
        on_device,
        mesh=mesh,
        in_specs=(split, split, P(), P(), split),
        out_specs=(split, split),
        check_vma=False,
    )
```

```python
import functools

import jax
import jax.numpy as jnp
import ml_dtypes
import numpy as np
from jax import lax
from jax.experimental import pallas as pl
from jax.experimental.pallas import tpu as pltpu
from jax.sharding import PartitionSpec as P

MARGIN = 4
REACH = MARGIN + 1
EDGE = 8

cheb_center = 1.3
cheb_radius = 1.2
cheb_ratio = 1.3 / 1.2
rho_first = 1.0 / cheb_ratio
rho_second = 1.0 / (2.0 * cheb_ratio - rho_first)
gain = 2.0 * rho_second / cheb_radius

MEANS = range(4)
BOX_DIAGONAL, LONG_HIGH, LONG_LOW, ACROSS_HIGH, ACROSS_LOW, LOAD_SUM = range(4, 10)
IMAGE_SUM, FLOW_LONG_HIGH, FLOW_LONG_LOW, FLOW_ACROSS_HIGH, FLOW_ACROSS_LOW = range(16, 21)

VMEM = pl.BlockSpec(memory_space=pltpu.VMEM)
SMEM = pl.BlockSpec(memory_space=pltpu.SMEM)


def sine_basis(length):
    indices = np.arange(1, length + 1)
    phases = indices[:, None] * indices[None, :] % (2 * (length + 1))
    table = np.sqrt(2.0 / (length + 1)) * np.sin(np.pi * phases / (length + 1))
    eigvals = 4.0 * np.sin(np.pi * indices / (2.0 * (length + 1))) ** 2
    return table.astype(np.float32), eigvals.astype(np.float32)


def call(body, out_shape, in_specs, scratch=(), flops=0, moved=0, out_spec=VMEM):
    return pl.pallas_call(
        body,
        out_shape=out_shape,
        in_specs=in_specs,
        out_specs=jax.tree.map(lambda _: out_spec, out_shape),
        scratch_shapes=list(scratch),
        compiler_params=pltpu.CompilerParams(vmem_limit_bytes=30 * 2**20),
        cost_estimate=pl.CostEstimate(flops=flops, bytes_accessed=moved, transcendentals=0),
    )


def f32(*shape):
    return jax.ShapeDtypeStruct(shape, jnp.float32)


class Box:
    def __init__(self, shape):
        self.long, self.across, self.deep = shape
        self.ex = self.long + 2 * MARGIN
        self.ey = self.across + 2 * MARGIN
        self.rows = self.long + 2 * REACH
        self.cols = self.across + 2 * EDGE
        self.flat = self.rows * self.cols


def pieces(values, count):
    parts = []
    for _ in range(count):
        part = values.astype(jnp.bfloat16)
        parts.append(part)
        values = values - part.astype(jnp.float32)
    return parts


def left_table(table, depth, count):
    rows, cols = table.shape
    wide = np.zeros((rows, depth), np.float32)
    wide[:, :cols] = table
    parts = []
    rest = wide
    for _ in range(count):
        part = rest.astype(ml_dtypes.bfloat16)
        parts.append(part)
        rest = rest - part.astype(np.float32)
    blank = np.zeros_like(parts[0])
    lines = []
    for index in range(count):
        used = count - index if count > 2 else count
        lines.append(np.concatenate([parts[index]] * used + [blank] * (count - used), axis=1))
    return np.concatenate(lines, axis=0)


def right_tables(table):
    rest, parts = table, []
    for _ in range(3):
        part = rest.astype(ml_dtypes.bfloat16)
        parts.append(part)
        rest = rest - part.astype(np.float32)
    both = np.concatenate([parts[0], parts[1]], axis=1)
    return np.concatenate([both, both], axis=0), np.concatenate([parts[2], parts[0]], axis=0)


def padded(size):
    return -(-size // 16) * 16


FORWARD, BACKWARD = 2, 3


def tables_of(box):
    sine_x, eig_x = sine_basis(box.ex)
    sine_y, eig_y = sine_basis(box.ey)
    sine_z, eig_z = sine_basis(box.deep)
    from_y = sine_y[MARGIN : MARGIN + box.across]
    from_x = sine_x[MARGIN : MARGIN + box.long]
    spread = np.broadcast_to(eig_x[:, None], (box.ex, box.deep))
    main_z, rest_z = right_tables(sine_z)
    return [
        jnp.asarray(np.ascontiguousarray(t))
        for t in (
            left_table(sine_y, padded(box.ey), FORWARD),
            left_table(sine_x, padded(box.ex), FORWARD),
            left_table(from_x, padded(box.ex), BACKWARD),
            left_table(from_y, padded(box.ey), BACKWARD),
            main_z,
            rest_z,
            spread,
            eig_z[None, :],
            eig_y[None, :],
        )
    ]


N_TABLES = 9


def bf16_dot(left, right):
    return lax.dot_general(
        left, right, (((1,), (0,)), ((), ())), preferred_element_type=jnp.float32
    )


def dot_left(table, values, count, rows):
    total = bf16_dot(table, jnp.concatenate(pieces(values, count), axis=0))
    return sum(total[index * rows : (index + 1) * rows] for index in range(1, count)) + total[:rows]


def dot_right(values, main, rest, count):
    deep = values.shape[1]
    parts = pieces(values, count)
    total = bf16_dot(jnp.concatenate(parts[:2], axis=1), main)
    result = total[:, :deep] + total[:, deep:]
    if count == 3:
        result = result + bf16_dot(jnp.concatenate([parts[0], parts[2]], axis=1), rest)
    return result


def with_rows(values, rows):
    if values.shape[0] == rows:
        return values
    blank = jnp.zeros((rows - values.shape[0],) + values.shape[1:], values.dtype)
    return jnp.concatenate([values, blank], axis=0)


def box_solve(box, source, skip, means, tables, row_mask, col_mask, spectral, middle, emit):
    into_y, into_x, from_x, from_y, main_z, rest_z, spread, eig_z, eig_y = tables
    deep = box.deep
    deep_x, deep_y = padded(box.ex), padded(box.ey)
    into_y, into_x = into_y[...], into_x[...]
    if col_mask is not None:
        mask = jnp.concatenate([col_mask] * FORWARD, axis=1)
        into_y = (into_y.astype(jnp.float32) * mask).astype(jnp.bfloat16)
        mask = jnp.concatenate([row_mask] * FORWARD, axis=1)
        into_x = (into_x.astype(jnp.float32) * mask).astype(jnp.bfloat16)
    from_x, from_y, main_z, rest_z = from_x[...], from_y[...], main_z[...], rest_z[...]
    spectral_flat = spectral.reshape(box.ey * deep_x, deep)
    middle_flat = middle.reshape(box.long * deep_y, deep)
    if deep_x > box.ex:
        spectral[:, box.ex :, :] = jnp.zeros((box.ey, deep_x - box.ex, deep), jnp.float32)
    if deep_y > box.ey:
        middle[:, box.ey :, :] = jnp.zeros((box.long, deep_y - box.ey, deep), jnp.float32)
    for start in range(0, box.ex, 8):
        block = source[start : start + 8, skip : skip + box.ey].reshape(8 * box.ey, deep)
        block = dot_right(block, main_z, rest_z, FORWARD).reshape(8, box.ey, deep)
        for row in range(0, 8, 2):
            pair = jnp.concatenate([block[row], block[row + 1]], axis=1)
            pair = dot_left(into_y, with_rows(pair, deep_y), FORWARD, box.ey)
            for part in range(2):
                spectral_flat[pl.ds(start + row + part, box.ey, stride=deep_x), :] = pair[
                    :, part * deep : (part + 1) * deep
                ]
    base = means[3] + means[0] * spread[...] + means[2] * eig_z[...]
    for col in range(0, box.ey, 2):
        pair = jnp.concatenate([spectral[col], spectral[col + 1]], axis=1)
        pair = dot_left(into_x, pair, FORWARD, box.ex)
        pair = jnp.concatenate(
            [
                pair[:, part * deep : (part + 1) * deep]
                / (base + means[1] * eig_y[0, col + part])
                for part in range(2)
            ],
            axis=1,
        )
        pair = dot_left(from_x, with_rows(pair, deep_x), BACKWARD, box.long)
        for part in range(2):
            middle_flat[pl.ds(col + part, box.long, stride=deep_y), :] = pair[
                :, part * deep : (part + 1) * deep
            ]
    for start in range(0, box.long, 8):
        parts = []
        for row in range(start, start + 8, 2):
            pair = jnp.concatenate([middle[row], middle[row + 1]], axis=1)
            pair = dot_left(from_y, pair, BACKWARD, box.across)
            parts += [pair[:, :deep], pair[:, deep:]]
        emit(start, dot_right(jnp.concatenate(parts, axis=0), main_z, rest_z, BACKWARD))


def position():
    long_pos, across_pos = lax.axis_index("wide"), lax.axis_index("narrow")
    return long_pos, across_pos, lax.axis_size("wide"), lax.axis_size("narrow")


def as_float(flag):
    return jnp.where(flag, jnp.float32(1.0), jnp.float32(0.0))


def is_even(axis):
    return lax.rem(lax.axis_index(axis), 2) == 0


class Sides:
    def __init__(self, axis, first, second):
        position = lax.axis_index(axis)
        self.even = is_even(axis)
        self.has_low = as_float(position > 0)
        self.has_high = as_float(position < lax.axis_size(axis) - 1)
        self.first, self.second = first, second

    def low(self, *index):
        return jnp.where(self.even, self.second[index], self.first[index]) * self.has_low

    def high(self, *index):
        return jnp.where(self.even, self.first[index], self.second[index]) * self.has_high


def in_order(even, up, down):
    return jnp.where(even, up, down), jnp.where(even, down, up)


def row_of(stride, col, count, first=0):
    return pl.ds(first * stride + col, count, stride=stride)


def pack_columns(box, fields, wide_sides, wide, first, second):
    corner = len(fields) * wide * box.long
    even = is_even("narrow")
    place = 0
    for field, sides in zip(fields, wide_sides):
        for step in range(wide):
            cols = (box.across - wide + step, step)
            values = [field[row_of(box.across, col, box.long), :] for col in cols]
            low = [sides.low(row_of(box.across, col, wide), slice(None)) for col in cols]
            high = [sides.high(row_of(box.across, col, wide), slice(None)) for col in cols]
            at = corner + 2 * REACH * place
            for start, parts in ((place * box.long, values), (at, low), (at + REACH, high)):
                parts = in_order(even, *(part.astype(jnp.float32) for part in parts))
                size = parts[0].shape[0]
                first[start : start + size, :], second[start : start + size, :] = parts
            place += 1


def message_rows(box, count):
    return -(-(count * (box.long + 2 * REACH)) // 8) * 8


def pack_fields(box, wide, fields, tables, after, *refs):
    own, (low, high), refs = refs[:fields], refs[fields : fields + 2], refs[fields + 2 :]
    parts, (first, second, *table) = refs[:tables], refs[tables + after :]
    size = wide * box.across
    flat = [field.reshape(box.long * box.across, box.deep) for field in own]
    low = low.reshape(low.size // box.deep, box.deep)
    high = high.reshape(high.size // box.deep, box.deep)
    sides = [
        Sides("wide", *(ref.at[index * size : (index + 1) * size] for ref in (low, high)))
        for index in range(fields)
    ]
    pack_columns(box, flat, sides, wide, first, second)
    if tables:
        known = last_rows_merged(parts, table[0].shape[0])
        table[0][...] = known
        first[first.shape[0] - known.shape[0] :, :] = known
        second[second.shape[0] - known.shape[0] :, :] = known


def bring_edges(
    box, zone, scale, load, own_load, load_first, load_second, first, second, staged, sems
):
    even = is_even("wide")

    def edges(wide):
        up, down = box.long - wide, 0
        return [pl.ds(jnp.where(even, *pair), wide) for pair in ((up, down), (down, up))]

    copies = [
        (load.at[edges(MARGIN)[0]], load_first),
        (load.at[edges(MARGIN)[1]], load_second),
        (zone.at[edges(REACH)[0]], staged.at[0]),
        (zone.at[edges(REACH)[1]], staged.at[1]),
        (scale.at[edges(REACH)[0]], first.at[:REACH]),
        (scale.at[edges(REACH)[1]], second.at[:REACH]),
        (load, own_load),
    ]
    copies = [
        pltpu.make_async_copy(source, target, sems.at[index])
        for index, (source, target) in enumerate(copies)
    ]
    for copy in copies:
        copy.start()
    for copy in copies[:4]:
        copy.wait()
    first[REACH:] = staged[0].astype(jnp.float32)
    second[REACH:] = staged[1].astype(jnp.float32)
    for copy in copies[4:]:
        copy.wait()


def fill_window(box, window, own, wide_sides, narrow_sides, wide, place, total, add=None):
    flat = window.reshape(box.flat, box.deep)
    nothing = jnp.zeros((box.rows, EDGE, box.deep), jnp.float32)
    window[:, :EDGE, :] = nothing
    window[:, EDGE + box.across :, :] = nothing
    if add is None:
        add = lambda values, row_side, col_side: values
    inner = slice(EDGE, EDGE + box.across)
    first, last = REACH, REACH + box.long
    if wide < REACH:
        blank = jnp.zeros((1, box.across, box.deep), jnp.float32)
        window[0:1, inner, :] = blank
        window[box.rows - 1 :, inner, :] = blank
    window[first:last, inner, :] = add(own[...].astype(jnp.float32), 0, 0)
    window[first - wide : first, inner, :] = add(wide_sides.low(Ellipsis), -1, 0)
    window[last : last + wide, inner, :] = add(wide_sides.high(Ellipsis), 1, 0)
    corner = total * box.long
    for step in range(wide):
        for source, col, side in (
            (narrow_sides.low, EDGE - wide + step, -1),
            (narrow_sides.high, EDGE + box.across + step, 1),
        ):
            for start, size, row, row_side in (
                ((place + step) * box.long, box.long, first, 0),
                (corner + 2 * REACH * (place + step), wide, first - wide, -1),
                (corner + 2 * REACH * (place + step) + REACH, wide, last, 1),
            ):
                values = source(slice(start, start + size), slice(None))
                flat[row_of(box.cols, col, size, row), :] = add(values, row_side, side)


def negative_image(window, row, at, first, last, flow_before, weights):
    to_long, to_across, to_deep, mass = weights
    x = window[row, first:last]
    flow_long = to_long[at, first:last] * (window[row + 1, first:last] - x)
    flow_across = to_across[at, first:last] * (window[row, first + 1 : last + 1] - x)
    flow_from = to_across[at, first - 1 : last - 1] * (x - window[row, first - 1 : last - 1])
    lanes = x.shape[1]
    flow_deep = to_deep[at, first:last] * (pltpu.roll(x, lanes - 1, 1) - x)
    total = flow_long - flow_before - mass[at, first:last] * x
    total = total + (flow_across - flow_from)
    total = total + (flow_deep - pltpu.roll(flow_deep, 1, 1))
    return total, flow_long


def looked_up(labels, values):
    return jnp.where(labels == 0, values[0], jnp.where(labels == 1, values[1], values[2]))


def at_own_row(line, shape):
    long_pos, across_pos, _, across_count = position()
    rows = lax.broadcasted_iota(jnp.int32, shape, 0)
    own = rows == long_pos * across_count + across_pos
    return jnp.where(own, line[:1], jnp.zeros(shape, jnp.float32))


def merged(table, *others):
    for other in others:
        table = jnp.where(table != 0.0, table, other)
    return table


def last_rows_merged(refs, count):
    return merged(*(ref[ref.shape[0] - count :, :] for ref in refs))


def join_rows(table, message, out):
    out[...] = last_rows_merged((table, message), out.shape[0])


def line_of(numbers, shape):
    lanes = lax.broadcasted_iota(jnp.int32, shape, 1)
    line = jnp.zeros(shape, jnp.float32)
    for index, number in numbers:
        line = jnp.where(lanes == index, number, line)
    return line


def box_sums(
    box, far_zone, far_scale, load, after, diffusivity, decay, zone, scale, out, table, sems
):
    del after
    parts = 2
    size = box.long // parts
    copies = []
    for part in range(parts):
        rows = slice(part * size, (part + 1) * size)
        for index, (source, target) in enumerate(((far_zone, zone), (far_scale, scale))):
            copy = pltpu.make_async_copy(
                source.at[rows], target.at[rows], sems.at[2 * part + index]
            )
            copy.start()
            copies.append(copy)
    step = 4
    nothing = jnp.zeros((box.across, box.deep), jnp.float32)
    half = [[0.5 * diffusivity[z, d] for z in range(3)] for d in range(3)]
    rates = [decay[z] for z in range(3)]

    def halves(row):
        labels, factor = zone[row], scale[row]
        return [looked_up(labels, half[d]) * factor for d in range(3)] + [looked_up(labels, rates)]

    def some_rows(index, sums):
        for row in range(step):
            row = index * step + row
            sums = [total + more for total, more in zip(sums, halves(row) + [load[row]])]
        return sums

    sums = [nothing] * 5
    for part in range(parts):
        for copy in copies[2 * part : 2 * part + 2]:
            copy.wait()
        per_part = size // step
        sums = lax.fori_loop(part * per_part, (part + 1) * per_part, some_rows, sums)

    def total(values):
        return jnp.sum(values, keepdims=True).reshape(1, 1)

    cells = box.long * box.across * box.deep
    numbers = [(index, total(sums[index]) * (2.0 / cells)) for index in range(3)]
    mass = total(sums[3])
    numbers += [(3, mass / cells)]
    ends = total(sums[2][:, :1]) + total(sums[2][:, box.deep - 1 :])
    numbers += [
        (BOX_DIAGONAL, mass + ends),
        (LONG_HIGH, total(halves(box.long - 1)[0])),
        (LONG_LOW, total(halves(0)[0])),
        (ACROSS_HIGH, total(sums[1][box.across - 1 :])),
        (ACROSS_LOW, total(sums[1][:1])),
        (LOAD_SUM, total(sums[4])),
    ]
    line = line_of(numbers, out.shape)
    out[...] = line
    table[...] = at_own_row(line, table.shape)


def means_of(ref):
    return [ref[0:1, index : index + 1] for index in range(4)]


def first_solve(box, load, low, high, left, right, means, zone, scale, diffusivity, decay, *rest):
    tables = rest[:N_TABLES]
    window, local, image, spectral, middle = rest[N_TABLES:]
    half = [0.5 * diffusivity[z, 2] for z in range(3)]
    rates = [decay[z] for z in range(3)]
    lane = lax.broadcasted_iota(jnp.int32, (box.across, box.deep), 1)
    ends = jnp.where((lane == 0) | (lane == box.deep - 1), jnp.float32(1.0), jnp.float32(0.0))
    image[...] = jnp.zeros((box.across, box.deep), jnp.float32)
    wide_sides, narrow_sides = Sides("wide", low, high), Sides("narrow", left, right)
    fill_window(box, window, load, wide_sides, narrow_sides, MARGIN, 0, MARGIN)

    def emit(start, values):
        values = values * (1.0 / cheb_center)
        values = values.reshape(8, box.across, box.deep)
        local[start : start + 8] = values
        total = image[...]
        for row in range(8):
            labels = zone[start + row]
            mass = looked_up(labels, rates) + looked_up(labels, half) * scale[start + row] * ends
            total = total + mass * values[row]
        image[...] = total

    box_solve(
        box,
        window.at[1 : 1 + box.ex],
        EDGE - MARGIN,
        means_of(means),
        tables,
        None,
        None,
        spectral,
        middle,
        emit,
    )


def weights_of(
    box,
    zone,
    scale,
    low,
    high,
    left,
    right,
    diffusivity,
    decay,
    to_long,
    to_across,
    to_deep,
    mass,
    zone_window,
    scale_window,
):
    for index, (window, own) in enumerate(((scale_window, scale), (zone_window, zone))):
        start = index * REACH
        wide_sides = Sides("wide", *(ref.at[start : start + REACH] for ref in (low, high)))
        narrow_sides = Sides("narrow", left, right)
        fill_window(box, window, own, wide_sides, narrow_sides, REACH, start, 2 * REACH)
    half = [[0.5 * diffusivity[z, d] for d in range(3)] for z in range(3)]
    rates = [decay[z] for z in range(3)]
    lane = lax.broadcasted_iota(jnp.int32, (box.cols, box.deep), 1)
    ends = jnp.where((lane == 0) | (lane == box.deep - 1), jnp.float32(1.0), jnp.float32(0.0))
    not_last = jnp.where(lane == box.deep - 1, jnp.float32(0.0), jnp.float32(1.0))

    def one_row(row, before):
        labels, factor = zone_window[row], scale_window[row]
        now = [looked_up(labels, [half[z][d] for z in range(3)]) * factor for d in range(3)]
        to_across[row] = now[1] + pltpu.roll(now[1], box.cols - 1, 0)
        to_deep[row] = (now[2] + pltpu.roll(now[2], box.deep - 1, 1)) * not_last
        mass[row] = looked_up(labels, rates) + now[2] * ends
        to_long[jnp.maximum(row - 1, 0)] = before + now[0]
        return now[0]

    last_long = lax.fori_loop(0, box.rows - 2, one_row, jnp.zeros_like(ends), unroll=4)
    for row in range(box.rows - 2, box.rows):
        last_long = one_row(row, last_long)
    to_long[box.rows - 1] = last_long


def image_sums(
    box, zone, scale, local, image, low, high, left, right, table, diffusivity, out, up, down
):
    half = [[0.5 * diffusivity[z, d] for z in range(3)] for d in range(3)]
    shape = (box.long * box.across, box.deep)
    zone_flat, scale_flat, local_flat = zone.reshape(shape), scale.reshape(shape), local.reshape(shape)
    last_col = row_of(box.across, box.across - 1, box.long)
    first_col = row_of(box.across, 0, box.long)

    wide_sides, narrow_sides = Sides("wide", low, high), Sides("narrow", left, right)

    def side(source, place):
        return source(slice(place * box.long, (place + 1) * box.long), slice(None))

    above, below = wide_sides.high, wide_sides.low
    faces = [
        (0, zone[box.long - 1], scale[box.long - 1], local[box.long - 1], above(REACH), above(0)),
        (0, zone[0], scale[0], local[0], below(2 * REACH - 1), below(REACH - 1)),
        (
            1,
            zone_flat[last_col, :],
            scale_flat[last_col, :],
            local_flat[last_col, :],
            side(narrow_sides.high, REACH),
            side(narrow_sides.high, 0),
        ),
        (
            1,
            zone_flat[first_col, :],
            scale_flat[first_col, :],
            local_flat[first_col, :],
            side(narrow_sides.low, 2 * REACH - 1),
            side(narrow_sides.low, REACH - 1),
        ),
    ]
    flows = []
    for direction, labels, factor, values, far_labels, far_factor in faces:
        weight = looked_up(labels, half[direction]) * factor
        weight = weight + looked_up(far_labels, half[direction]) * far_factor
        flows.append(jnp.sum(weight * values, keepdims=True))
    long_pos, across_pos, long_count, across_count = position()
    numbers = [
        (IMAGE_SUM, jnp.sum(image[...], keepdims=True) + sum(flows)),
        (FLOW_LONG_HIGH, flows[0] * as_float(long_pos < long_count - 1)),
        (FLOW_LONG_LOW, flows[1] * as_float(long_pos > 0)),
        (FLOW_ACROSS_HIGH, flows[2] * as_float(across_pos < across_count - 1)),
        (FLOW_ACROSS_LOW, flows[3] * as_float(across_pos > 0)),
    ]
    known = table[...] + at_own_row(line_of(numbers, (8, out.shape[1])), out.shape)
    out[...] = known
    edge = REACH * box.across
    even = is_even("wide")
    for target, pair in ((up, (box.long - REACH, 0)), (down, (0, box.long - REACH))):
        target[:edge] = local[pl.ds(jnp.where(even, *pair), REACH)].reshape(edge, box.deep)
        target[edge:] = known


def column(values, index):
    return values[:, index : index + 1]


def coarse_inverse(numbers, work):
    count, width = work.shape
    across = lax.axis_size("narrow")
    beyond = pltpu.roll(numbers, count - across, 0)
    beside = pltpu.roll(numbers, count - 1, 0)
    before = pltpu.roll(numbers, across, 0)
    ahead = pltpu.roll(numbers, 1, 0)
    place = lax.broadcasted_iota(jnp.int32, (count, 1), 0)
    across_pos = lax.rem(place, across)
    nothing = jnp.zeros((count, 1), jnp.float32)
    couplings = []
    diagonal = column(numbers, BOX_DIAGONAL)
    for own, other, there, inside in (
        (LONG_HIGH, LONG_LOW, beyond, place < count - across),
        (LONG_LOW, LONG_HIGH, before, place >= across),
        (ACROSS_HIGH, ACROSS_LOW, beside, across_pos < across - 1),
        (ACROSS_LOW, ACROSS_HIGH, ahead, across_pos > 0),
    ):
        shared = jnp.where(inside, column(there, other), nothing)
        diagonal = diagonal + column(numbers, own) + shared
        couplings.append(jnp.where(inside, column(numbers, own) + shared, nothing))
    rows = lax.broadcasted_iota(jnp.int32, (count, width), 0)
    cols = lax.broadcasted_iota(jnp.int32, (count, width), 1)
    blank = jnp.zeros((count, width), jnp.float32)
    matrix = jnp.where(cols == rows, diagonal, blank)
    for shift, coupling in zip((across, -across, 1, -1), couplings):
        matrix = matrix - jnp.where((cols == rows + shift) & (cols < count), coupling, blank)
    matrix = jnp.where(cols == rows + count, jnp.ones((count, 1), jnp.float32), matrix)
    if count <= 16:
        for step in range(count):
            pivot_row = matrix[step : step + 1, :] / matrix[step : step + 1, step : step + 1]
            rest = matrix - matrix[:, step : step + 1] * pivot_row
            matrix = jnp.where(rows == step, pivot_row, rest)
        return pltpu.roll(matrix, width - count, 1)
    work[...] = matrix

    def eliminate(step, _):
        values = work[...]
        pivot_row = work[pl.ds(step, 1), :]
        at_step = cols == step
        factors = jnp.sum(jnp.where(at_step, values, blank), axis=1, keepdims=True)
        pivot = jnp.sum(jnp.where(at_step[:1], pivot_row, blank[:1]), axis=1, keepdims=True)
        pivot_row = pivot_row / pivot
        work[...] = jnp.where(rows == step, pivot_row, values - factors * pivot_row)
        return 0

    lax.fori_loop(0, count, eliminate, 0)
    values = work[...]
    if count % 128:
        return pltpu.roll(values, width - count, 1)
    return values[:, count : 2 * count]


def answer(inverse, sums):
    return jnp.sum(inverse * sums, axis=0, keepdims=True)


def at_box(values, row_side, col_side):
    long_pos, across_pos, long_count, across_count = position()
    there_long, there_across = long_pos + row_side, across_pos + col_side
    inside = (
        (there_long >= 0)
        & (there_long < long_count)
        & (there_across >= 0)
        & (there_across < across_count)
    )
    lanes = lax.broadcasted_iota(jnp.int32, values.shape, 1)
    wanted = (lanes == there_long * across_count + there_across) & inside
    return jnp.sum(jnp.where(wanted, values, jnp.zeros_like(values)), axis=1, keepdims=True)


def coarse_corrections(box, numbers, work):
    count = numbers.shape[0]
    across_count = lax.axis_size("narrow")
    inverse = coarse_inverse(numbers, work)
    sums = column(numbers, IMAGE_SUM)
    sums = sums - column(pltpu.roll(numbers, count - across_count, 0), FLOW_LONG_LOW)
    sums = sums - column(pltpu.roll(numbers, across_count, 0), FLOW_LONG_HIGH)
    sums = sums - column(pltpu.roll(numbers, count - 1, 0), FLOW_ACROSS_LOW)
    sums = sums - column(pltpu.roll(numbers, 1, 0), FLOW_ACROSS_HIGH)
    load_sums = column(numbers, LOAD_SUM)
    sums = load_sums * (1.0 - 1.0 / cheb_center) - sums
    return answer(inverse, load_sums) * (1.0 / cheb_center), answer(inverse, sums) * gain


def second_solve(box, parts, local, low, high, left, right, means, *rest):
    table_parts, rest = rest[:parts], rest[parts:]
    to_long, to_across, to_deep, mass, load_window = rest[:5]
    tables = rest[5 : 5 + N_TABLES]
    iterate, top, bottom, last_col, first_col = rest[5 + N_TABLES : 10 + N_TABLES]
    window, residual, spectral, middle, work = rest[10 + N_TABLES :]
    long_pos, across_pos, long_count, across_count = position()
    numbers = last_rows_merged(table_parts, work.shape[0])
    coarse, second_coarse = coarse_corrections(box, numbers, work)
    own_shift = at_box(second_coarse, 0, 0)
    shifts = {
        (row_side, col_side): at_box(coarse, row_side, col_side)
        for row_side in (-1, 0, 1)
        for col_side in (-1, 0, 1)
    }

    def add(values, row_side, col_side):
        shift = shifts[row_side, col_side]
        if values.ndim == 3:
            shift = shift.reshape(1, 1, 1)
        return values + shift

    edge = REACH * box.across
    low, high = (
        ref.at[:edge].reshape(REACH, box.across, box.deep) for ref in (low, high)
    )
    wide_sides, narrow_sides = Sides("wide", low, high), Sides("narrow", left, right)
    fill_window(box, window, local, wide_sides, narrow_sides, REACH, 0, REACH, add)
    weights = (to_long, to_across, to_deep, mass)

    start, stop = EDGE - MARGIN, EDGE + box.across + MARGIN

    def one_row(row, flow):
        image, flow = negative_image(window, row, row, start, stop, flow, weights)
        residual[row - 1] = load_window[row, start:stop] + image
        return flow

    flow = to_long[0, start:stop] * (window[1, start:stop] - window[0, start:stop])
    lax.fori_loop(1, 1 + box.ex, one_row, flow, unroll=4)
    inner = slice(EDGE, EDGE + box.across)
    first = REACH
    row_ids = lax.broadcasted_iota(jnp.int32, (1, padded(box.ex)), 1)
    col_ids = lax.broadcasted_iota(jnp.int32, (1, padded(box.ey)), 1)
    row_mask = jnp.where(row_ids < MARGIN, as_float(long_pos > 0), 1.0)
    row_mask = jnp.where(row_ids >= MARGIN + box.long, as_float(long_pos < long_count - 1), row_mask)
    col_mask = jnp.where(col_ids < MARGIN, as_float(across_pos > 0), 1.0)
    col_mask = jnp.where(
        col_ids >= MARGIN + box.across, as_float(across_pos < across_count - 1), col_mask
    )
    keep = 1.0 + rho_second * rho_first

    def emit(start, values):
        rows = values.reshape(8, box.across, box.deep)
        before = window[first + start : first + start + 8, inner, :]
        shift = own_shift.reshape(1, 1, 1)
        iterate[start : start + 8] = keep * before + (gain * rows + shift)

    box_solve(
        box, residual, 0, means_of(means), tables, row_mask, col_mask, spectral, middle, emit
    )
    rows = in_order(is_even("wide"), iterate[box.long - 1], iterate[0])
    top[...], bottom[...] = rows
    flat = iterate.reshape(box.long * box.across, box.deep)
    cols = [flat[row_of(box.across, col, box.long), :] for col in (box.across - 1, 0)]
    last_col[...], first_col[...] = in_order(is_even("narrow"), *cols)


def last_residual(
    box,
    load,
    partial,
    low,
    high,
    left,
    right,
    to_long,
    to_across,
    to_deep,
    mass,
    iterate,
    out,
    window,
    result,
    sems,
):
    inner = slice(EDGE, EDGE + box.across)
    flat = window.reshape((box.long + 2) * box.cols, box.deep)
    blank = jnp.zeros((box.long + 2, EDGE, box.deep), jnp.float32)
    window[:, :EDGE, :] = blank
    window[:, EDGE + box.across :, :] = blank
    window[1 : 1 + box.long, inner, :] = partial[...]
    own = pltpu.make_async_copy(window.at[1 : 1 + box.long, inner, :], iterate, sems.at[0])
    own.start()
    wide_sides, narrow_sides = Sides("wide", low, high), Sides("narrow", left, right)
    window[0, inner, :] = wide_sides.low(Ellipsis)
    window[1 + box.long, inner, :] = wide_sides.high(Ellipsis)
    flat[row_of(box.cols, EDGE - 1, box.long, 1), :] = narrow_sides.low(Ellipsis)
    flat[row_of(box.cols, EDGE + box.across, box.long, 1), :] = narrow_sides.high(Ellipsis)
    weights = (to_long, to_across, to_deep, mass)

    def one_row(row, flow):
        image, flow = negative_image(
            window, row + 1, REACH + row, inner.start, inner.stop, flow, weights
        )
        result[row] = load[row] + image
        return flow

    flow = to_long[REACH - 1, inner] * (window[1, inner] - window[0, inner])
    chunk = box.long // 4
    copies = [own]
    for index in range(4):
        rows = slice(index * chunk, (index + 1) * chunk)
        flow = lax.fori_loop(rows.start, rows.stop, one_row, flow, unroll=4)
        copy = pltpu.make_async_copy(result.at[rows], out.at[rows], sems.at[1 + index])
        copy.start()
        copies.append(copy)
    for copy in copies:
        copy.wait()


def exchange(axis, first, second, around=False):
    size = lax.axis_size(axis)
    swaps = []
    for way in range(2):
        pairs = []
        for place in range(size):
            other = place + 1 if place % 2 == way else place - 1
            if around and size % 2 == 0:
                other %= size
            pairs.append((place, other if 0 <= other < size else place))
        swaps.append(pairs)
    return lax.ppermute(first, axis, swaps[0]), lax.ppermute(second, axis, swaps[1])


def two_away(axis, table):
    size = lax.axis_size(axis)
    return lax.ppermute(table, axis, [(i, (i + 2) % size) for i in range(size)])


def tell(table):
    count = table.shape[0]
    long_pos, across_pos, _, across_count = position()
    own = lax.dynamic_slice_in_dim(table, long_pos * across_count + across_pos, 1, axis=0)
    line = jnp.broadcast_to(own, (count, 1, 128))
    told = lax.all_to_all(line, ("wide", "narrow"), split_axis=0, concat_axis=0, tiled=True)
    return told.reshape(count, 128)


def on_device(zone, scale, diffusivity, decay, load):
    box = Box(load.shape)
    long, across, deep = load.shape
    count = lax.axis_size("wide") * lax.axis_size("narrow")
    by_margins = lax.axis_size("wide") == 4 and lax.axis_size("narrow") == 4
    tables = tables_of(box)
    cells = f32(long, across, deep)
    whole_zone = jax.ShapeDtypeStruct(cells.shape, zone.dtype)
    window = f32(box.rows, box.cols, deep)
    table_shape = f32(count, 128)
    anywhere = pl.BlockSpec(memory_space=pl.ANY)
    in_hbm = pl.BlockSpec(memory_space=pltpu.HBM)

    def scratch(shape):
        return pltpu.VMEM(shape, jnp.float32)

    def pinned(field):
        return pltpu.with_memory_space_constraint(field, pltpu.HBM)

    spectral = scratch((box.ey, padded(box.ex), deep))
    middle = scratch((long, padded(box.ey), deep))

    def pack(wide, fields, sides, parts=(), after=()):
        rows = message_rows(box, wide * len(fields)) + (count if parts else 0)
        message = f32(rows, deep)
        body = functools.partial(pack_fields, box, wide, len(fields), len(parts), len(after))
        return call(
            body,
            (message, message) + ((table_shape,) if parts else ()),
            [VMEM] * (len(fields) + 2 + len(parts)) + [anywhere] * len(after),
        )(*fields, *sides, *parts, *after)

    far = f32(2 * REACH, across, deep)
    far_zone, far_scale = zone, scale
    load, load_first, load_second, first, second = call(
        functools.partial(bring_edges, box),
        (cells,) + (f32(MARGIN, across, deep),) * 2 + (far, far),
        [in_hbm] * 3,
        [pltpu.VMEM((2, REACH, across, deep), zone.dtype), pltpu.SemaphoreType.DMA((7,))],
    )(pinned(zone), pinned(scale), pinned(load))
    load_wide = exchange("wide", load_first, load_second)
    far_wide = exchange("wide", first, second)
    load_first, load_second = pack(MARGIN, [load], load_wide)
    load_narrow = exchange("narrow", load_first, load_second)
    zone, scale, sums, table = call(
        functools.partial(box_sums, box),
        (whole_zone, cells, f32(8, 128), table_shape),
        [in_hbm] * 2 + [VMEM, anywhere] + [SMEM] * 2,
        [pltpu.SemaphoreType.DMA((4,))],
    )(pinned(far_zone), pinned(far_scale), load, load_first, diffusivity, decay)
    far_narrow = exchange("narrow", *pack(REACH, [scale, zone], far_wide))
    load_window, local, image = call(
        functools.partial(first_solve, box),
        (window, cells, f32(across, deep)),
        [VMEM] * 8 + [SMEM] * 2 + [VMEM] * N_TABLES,
        [spectral, middle],
        flops=4 * 10**9,
    )(load, *load_wide, *load_narrow, sums, zone, scale, diffusivity, decay, *tables)
    message = f32(REACH * across + count, deep)
    table, first, second = call(
        functools.partial(image_sums, box), (table_shape, message, message), [VMEM] * 9 + [SMEM]
    )(zone, scale, local, image, *far_wide, *far_narrow, table, diffusivity)
    own_table = table
    wide = exchange("wide", first, second, by_margins)
    parts = (table, *wide)
    if by_margins:
        parts += (two_away("wide", table),)
    weights = call(
        functools.partial(weights_of, box),
        (window,) * 4,
        [VMEM] * 6 + [SMEM] * 2,
        [scratch(window.shape)] * 2,
        flops=10**9,
    )(zone, scale, *far_wide, *far_narrow, diffusivity, decay)
    first, second, table = pack(REACH, [local], wide, parts, weights[3:])
    narrow = exchange("narrow", first, second)
    if by_margins:
        table = call(join_rows, table_shape, [VMEM] * 2)(table, narrow[0])
        parts = (table, two_away("narrow", table))
    else:
        parts = (tell(own_table),)
    row, col = f32(across, deep), f32(long, deep)
    iterate, first_row, second_row, first_col, second_col = call(
        functools.partial(second_solve, box, len(parts)),
        (cells, row, row, col, col),
        [VMEM] * (11 + len(parts) + N_TABLES),
        [
            scratch(window.shape),
            scratch((box.ex, box.ey, deep)),
            spectral,
            middle,
            scratch((count, -(-2 * count // 128) * 128)),
        ],
        flops=4 * 10**9,
    )(local, *wide, *narrow, sums, *parts, *weights, load_window, *tables)
    narrow = exchange("narrow", first_col, second_col)
    wide = exchange("wide", first_row, second_row)
    return call(
        functools.partial(last_residual, box),
        (cells, cells),
        [VMEM] * 10,
        [scratch((long + 2, box.cols, deep)), scratch(cells.shape), pltpu.SemaphoreType.DMA((5,))],
        out_spec=anywhere,
    )(load, iterate, *wide, *narrow, *weights)


def solution(mesh):
    split = P(("groups", "wide"), "narrow", None)
    return jax.shard_map(
        on_device,
        mesh=mesh,
        in_specs=(split, split, P(), P(), split),
        out_specs=(split, split),
        check_vma=False,
    )
```

```python
import functools

import jax
import jax.numpy as jnp
import ml_dtypes
import numpy as np
from jax import lax
from jax.experimental import pallas as pl
from jax.experimental.pallas import tpu as pltpu
from jax.sharding import PartitionSpec as P

MARGIN = 4
REACH = MARGIN + 1
EDGE = 8

cheb_center = 1.3
cheb_radius = 1.2
cheb_ratio = 1.3 / 1.2
rho_first = 1.0 / cheb_ratio
rho_second = 1.0 / (2.0 * cheb_ratio - rho_first)
gain = 2.0 * rho_second / cheb_radius

MEANS = range(4)
BOX_DIAGONAL, LONG_HIGH, LONG_LOW, ACROSS_HIGH, ACROSS_LOW, LOAD_SUM = range(4, 10)
IMAGE_SUM, FLOW_LONG_HIGH, FLOW_LONG_LOW, FLOW_ACROSS_HIGH, FLOW_ACROSS_LOW = range(16, 21)

VMEM = pl.BlockSpec(memory_space=pltpu.VMEM)
SMEM = pl.BlockSpec(memory_space=pltpu.SMEM)


def sine_basis(length):
    indices = np.arange(1, length + 1)
    phases = indices[:, None] * indices[None, :] % (2 * (length + 1))
    table = np.sqrt(2.0 / (length + 1)) * np.sin(np.pi * phases / (length + 1))
    eigvals = 4.0 * np.sin(np.pi * indices / (2.0 * (length + 1))) ** 2
    return table.astype(np.float32), eigvals.astype(np.float32)


def call(body, out_shape, in_specs, scratch=(), flops=0, moved=0, out_spec=None):
    return pl.pallas_call(
        body,
        out_shape=out_shape,
        in_specs=in_specs,
        out_specs=out_spec or jax.tree.map(lambda _: VMEM, out_shape),
        scratch_shapes=list(scratch),
        compiler_params=pltpu.CompilerParams(vmem_limit_bytes=30 * 2**20),
        cost_estimate=pl.CostEstimate(flops=flops, bytes_accessed=moved, transcendentals=0),
    )


def f32(*shape):
    return jax.ShapeDtypeStruct(shape, jnp.float32)


class Box:
    def __init__(self, shape):
        self.long, self.across, self.deep = shape
        self.ex = self.long + 2 * MARGIN
        self.ey = self.across + 2 * MARGIN
        self.rows = self.long + 2 * REACH
        self.cols = self.across + 2 * EDGE
        self.flat = self.rows * self.cols


def pieces(values, count):
    parts = []
    for _ in range(count):
        part = values.astype(jnp.bfloat16)
        parts.append(part)
        values = values - part.astype(jnp.float32)
    return parts


def left_table(table, depth, count):
    rows, cols = table.shape
    wide = np.zeros((rows, depth), np.float32)
    wide[:, :cols] = table
    parts = []
    rest = wide
    for _ in range(count):
        part = rest.astype(ml_dtypes.bfloat16)
        parts.append(part)
        rest = rest - part.astype(np.float32)
    blank = np.zeros_like(parts[0])
    lines = []
    for index in range(count):
        used = count - index if count > 2 else count
        lines.append(np.concatenate([parts[index]] * used + [blank] * (count - used), axis=1))
    return np.concatenate(lines, axis=0)


def right_tables(table):
    rest, parts = table, []
    for _ in range(3):
        part = rest.astype(ml_dtypes.bfloat16)
        parts.append(part)
        rest = rest - part.astype(np.float32)
    both = np.concatenate([parts[0], parts[1]], axis=1)
    return np.concatenate([both, both], axis=0), np.concatenate([parts[2], parts[0]], axis=0)


def padded(size):
    return -(-size // 16) * 16


FORWARD, BACKWARD = 2, 3


def tables_of(box):
    sine_x, eig_x = sine_basis(box.ex)
    sine_y, eig_y = sine_basis(box.ey)
    sine_z, eig_z = sine_basis(box.deep)
    from_y = sine_y[MARGIN : MARGIN + box.across]
    from_x = sine_x[MARGIN : MARGIN + box.long]
    spread = np.broadcast_to(eig_x[:, None], (box.ex, box.deep))
    main_z, rest_z = right_tables(sine_z)
    return [
        jnp.asarray(np.ascontiguousarray(t))
        for t in (
            left_table(sine_y, padded(box.ey), FORWARD),
            left_table(sine_x, padded(box.ex), FORWARD),
            left_table(from_x, padded(box.ex), BACKWARD),
            left_table(from_y, padded(box.ey), BACKWARD),
            main_z,
            rest_z,
            spread,
            eig_z[None, :],
            eig_y[None, :],
        )
    ]


N_TABLES = 9


def bf16_dot(left, right):
    return lax.dot_general(
        left, right, (((1,), (0,)), ((), ())), preferred_element_type=jnp.float32
    )


def dot_left(table, values, count, rows):
    total = bf16_dot(table, jnp.concatenate(pieces(values, count), axis=0))
    return sum(total[index * rows : (index + 1) * rows] for index in range(1, count)) + total[:rows]


def dot_right(values, main, rest, count):
    deep = values.shape[1]
    parts = pieces(values, count)
    total = bf16_dot(jnp.concatenate(parts[:2], axis=1), main)
    result = total[:, :deep] + total[:, deep:]
    if count == 3:
        result = result + bf16_dot(jnp.concatenate([parts[0], parts[2]], axis=1), rest)
    return result


def with_rows(values, rows):
    if values.shape[0] == rows:
        return values
    blank = jnp.zeros((rows - values.shape[0],) + values.shape[1:], values.dtype)
    return jnp.concatenate([values, blank], axis=0)


def box_solve(box, source, means, tables, row_mask, col_mask, spectral, middle, emit):
    into_y, into_x, from_x, from_y, main_z, rest_z, spread, eig_z, eig_y = tables
    deep = box.deep
    deep_x, deep_y = padded(box.ex), padded(box.ey)
    into_y, into_x = into_y[...], into_x[...]
    if col_mask is not None:
        mask = jnp.concatenate([col_mask] * FORWARD, axis=1)
        into_y = (into_y.astype(jnp.float32) * mask).astype(jnp.bfloat16)
        mask = jnp.concatenate([row_mask] * FORWARD, axis=1)
        into_x = (into_x.astype(jnp.float32) * mask).astype(jnp.bfloat16)
    from_x, from_y, main_z, rest_z = from_x[...], from_y[...], main_z[...], rest_z[...]
    spectral_flat = spectral.reshape(box.ey * deep_x, deep)
    middle_flat = middle.reshape(box.long * deep_y, deep)
    if deep_x > box.ex:
        spectral[:, box.ex :, :] = jnp.zeros((box.ey, deep_x - box.ex, deep), jnp.float32)
    if deep_y > box.ey:
        middle[:, box.ey :, :] = jnp.zeros((box.long, deep_y - box.ey, deep), jnp.float32)
    for start in range(0, box.ex, 8):
        block = source(start).reshape(8 * box.ey, deep)
        block = dot_right(block, main_z, rest_z, FORWARD).reshape(8, box.ey, deep)
        for row in range(0, 8, 2):
            pair = jnp.concatenate([block[row], block[row + 1]], axis=1)
            pair = dot_left(into_y, with_rows(pair, deep_y), FORWARD, box.ey)
            for part in range(2):
                spectral_flat[pl.ds(start + row + part, box.ey, stride=deep_x), :] = pair[
                    :, part * deep : (part + 1) * deep
                ]
    base = means[3] + means[0] * spread[...] + means[2] * eig_z[...]
    for col in range(0, box.ey, 2):
        pair = jnp.concatenate([spectral[col], spectral[col + 1]], axis=1)
        pair = dot_left(into_x, pair, FORWARD, box.ex)
        pair = jnp.concatenate(
            [
                pair[:, part * deep : (part + 1) * deep]
                / (base + means[1] * eig_y[0, col + part])
                for part in range(2)
            ],
            axis=1,
        )
        pair = dot_left(from_x, with_rows(pair, deep_x), BACKWARD, box.long)
        for part in range(2):
            middle_flat[pl.ds(col + part, box.long, stride=deep_y), :] = pair[
                :, part * deep : (part + 1) * deep
            ]
    for start in range(0, box.long, 8):
        parts = []
        for row in range(start, start + 8, 2):
            pair = jnp.concatenate([middle[row], middle[row + 1]], axis=1)
            pair = dot_left(from_y, pair, BACKWARD, box.across)
            parts += [pair[:, :deep], pair[:, deep:]]
        emit(start, dot_right(jnp.concatenate(parts, axis=0), main_z, rest_z, BACKWARD))


def position():
    long_pos, across_pos = lax.axis_index("wide"), lax.axis_index("narrow")
    return long_pos, across_pos, lax.axis_size("wide"), lax.axis_size("narrow")


def as_float(flag):
    return jnp.where(flag, jnp.float32(1.0), jnp.float32(0.0))


def is_even(axis):
    return lax.rem(lax.axis_index(axis), 2) == 0


class Sides:
    def __init__(self, axis, first, second):
        position = lax.axis_index(axis)
        self.even = is_even(axis)
        self.has_low = as_float(position > 0)
        self.has_high = as_float(position < lax.axis_size(axis) - 1)
        self.first, self.second = first, second

    def low(self, *index):
        return jnp.where(self.even, self.second[index], self.first[index]) * self.has_low

    def high(self, *index):
        return jnp.where(self.even, self.first[index], self.second[index]) * self.has_high


def in_order(even, up, down):
    return jnp.where(even, up, down), jnp.where(even, down, up)


def row_of(stride, col, count, first=0):
    return pl.ds(first * stride + col, count, stride=stride)


def pack_columns(box, fields, wide_sides, wide, first, second):
    corner = len(fields) * wide * box.long
    even = is_even("narrow")
    place = 0
    for field, sides in zip(fields, wide_sides):
        for step in range(wide):
            cols = (box.across - wide + step, step)
            values = [field[row_of(box.across, col, box.long), :] for col in cols]
            low = [sides.low(row_of(box.across, col, wide), slice(None)) for col in cols]
            high = [sides.high(row_of(box.across, col, wide), slice(None)) for col in cols]
            at = corner + 2 * REACH * place
            for start, parts in ((place * box.long, values), (at, low), (at + REACH, high)):
                parts = in_order(even, *(part.astype(jnp.float32) for part in parts))
                size = parts[0].shape[0]
                first[start : start + size, :], second[start : start + size, :] = parts
            place += 1


def message_rows(box, count):
    return -(-(count * (box.long + 2 * REACH)) // 8) * 8


def pack_fields(box, wide, fields, tables, after, *refs):
    own, (low, high), refs = refs[:fields], refs[fields : fields + 2], refs[fields + 2 :]
    parts, (first, second, *table) = refs[:tables], refs[tables + after :]
    size = wide * box.across
    flat = [field.reshape(box.long * box.across, box.deep) for field in own]
    low = low.reshape(low.size // box.deep, box.deep)
    high = high.reshape(high.size // box.deep, box.deep)
    sides = [
        Sides("wide", *(ref.at[index * size : (index + 1) * size] for ref in (low, high)))
        for index in range(fields)
    ]
    pack_columns(box, flat, sides, wide, first, second)
    if tables:
        known = last_rows_merged(parts, table[0].shape[0])
        table[0][...] = known
        first[first.shape[0] - known.shape[0] :, :] = known
        second[second.shape[0] - known.shape[0] :, :] = known


def bring_edges(
    box, zone, scale, load, own_load, load_first, load_second, first, second, staged, sems
):
    even = is_even("wide")

    def edges(wide):
        up, down = box.long - wide, 0
        return [pl.ds(jnp.where(even, *pair), wide) for pair in ((up, down), (down, up))]

    copies = [
        (load.at[edges(MARGIN)[0]], load_first),
        (load.at[edges(MARGIN)[1]], load_second),
        (zone.at[edges(REACH)[0]], staged.at[0]),
        (zone.at[edges(REACH)[1]], staged.at[1]),
        (scale.at[edges(REACH)[0]], first.at[:REACH]),
        (scale.at[edges(REACH)[1]], second.at[:REACH]),
        (load, own_load),
    ]
    copies = [
        pltpu.make_async_copy(source, target, sems.at[index])
        for index, (source, target) in enumerate(copies)
    ]
    for copy in copies:
        copy.start()
    for copy in copies[:4]:
        copy.wait()
    first[REACH:] = staged[0].astype(jnp.float32)
    second[REACH:] = staged[1].astype(jnp.float32)
    for copy in copies[4:]:
        copy.wait()


def fill_window(box, window, own, wide_sides, narrow_sides, wide, place, total, add=None):
    flat = window.reshape(box.flat, box.deep)
    nothing = jnp.zeros((box.rows, EDGE, box.deep), jnp.float32)
    window[:, :EDGE, :] = nothing
    window[:, EDGE + box.across :, :] = nothing
    if add is None:
        add = lambda values, row_side, col_side: values
    inner = slice(EDGE, EDGE + box.across)
    first, last = REACH, REACH + box.long
    if wide < REACH:
        blank = jnp.zeros((1, box.across, box.deep), jnp.float32)
        window[0:1, inner, :] = blank
        window[box.rows - 1 :, inner, :] = blank
    window[first:last, inner, :] = add(own[...].astype(jnp.float32), 0, 0)
    window[first - wide : first, inner, :] = add(wide_sides.low(Ellipsis), -1, 0)
    window[last : last + wide, inner, :] = add(wide_sides.high(Ellipsis), 1, 0)
    corner = total * box.long
    for step in range(wide):
        for source, col, side in (
            (narrow_sides.low, EDGE - wide + step, -1),
            (narrow_sides.high, EDGE + box.across + step, 1),
        ):
            for start, size, row, row_side in (
                ((place + step) * box.long, box.long, first, 0),
                (corner + 2 * REACH * (place + step), wide, first - wide, -1),
                (corner + 2 * REACH * (place + step) + REACH, wide, last, 1),
            ):
                values = source(slice(start, start + size), slice(None))
                flat[row_of(box.cols, col, size, row), :] = add(values, row_side, side)


def negative_image(window, row, at, first, last, flow_before, weights):
    to_long, to_across, to_deep, mass = weights
    x = window[row, first:last]
    flow_long = to_long[at, first:last] * (window[row + 1, first:last] - x)
    flow_across = to_across[at, first:last] * (window[row, first + 1 : last + 1] - x)
    flow_from = to_across[at, first - 1 : last - 1] * (x - window[row, first - 1 : last - 1])
    lanes = x.shape[1]
    flow_deep = to_deep[at, first:last] * (pltpu.roll(x, lanes - 1, 1) - x)
    total = flow_long - flow_before - mass[at, first:last] * x
    total = total + (flow_across - flow_from)
    total = total + (flow_deep - pltpu.roll(flow_deep, 1, 1))
    return total, flow_long


def looked_up(labels, values):
    return jnp.where(labels == 0, values[0], jnp.where(labels == 1, values[1], values[2]))


def at_own_row(line, shape):
    long_pos, across_pos, _, across_count = position()
    rows = lax.broadcasted_iota(jnp.int32, shape, 0)
    own = rows == long_pos * across_count + across_pos
    return jnp.where(own, line[:1], jnp.zeros(shape, jnp.float32))


def merged(table, *others):
    for other in others:
        table = jnp.where(table != 0.0, table, other)
    return table


def last_rows_merged(refs, count):
    return merged(*(ref[ref.shape[0] - count :, :] for ref in refs))


def join_rows(table, message, out):
    out[...] = last_rows_merged((table, message), out.shape[0])


def line_of(numbers, shape):
    lanes = lax.broadcasted_iota(jnp.int32, shape, 1)
    line = jnp.zeros(shape, jnp.float32)
    for index, number in numbers:
        line = jnp.where(lanes == index, number, line)
    return line


def box_sums(
    box, far_zone, far_scale, load, after, diffusivity, decay, zone, scale, out, table, sems
):
    del after
    parts = 2
    size = box.long // parts
    copies = []
    for part in range(parts):
        rows = slice(part * size, (part + 1) * size)
        for index, (source, target) in enumerate(((far_zone, zone), (far_scale, scale))):
            copy = pltpu.make_async_copy(
                source.at[rows], target.at[rows], sems.at[2 * part + index]
            )
            copy.start()
            copies.append(copy)
    step = 4
    nothing = jnp.zeros((box.across, box.deep), jnp.float32)
    half = [[0.5 * diffusivity[z, d] for z in range(3)] for d in range(3)]
    rates = [decay[z] for z in range(3)]

    def halves(row):
        labels, factor = zone[row], scale[row]
        return [looked_up(labels, half[d]) * factor for d in range(3)] + [looked_up(labels, rates)]

    def some_rows(index, sums):
        for row in range(step):
            row = index * step + row
            sums = [total + more for total, more in zip(sums, halves(row) + [load[row]])]
        return sums

    sums = [nothing] * 5
    for part in range(parts):
        for copy in copies[2 * part : 2 * part + 2]:
            copy.wait()
        per_part = size // step
        sums = lax.fori_loop(part * per_part, (part + 1) * per_part, some_rows, sums)

    def total(values):
        return jnp.sum(values, keepdims=True).reshape(1, 1)

    cells = box.long * box.across * box.deep
    numbers = [(index, total(sums[index]) * (2.0 / cells)) for index in range(3)]
    mass = total(sums[3])
    numbers += [(3, mass / cells)]
    ends = total(sums[2][:, :1]) + total(sums[2][:, box.deep - 1 :])
    numbers += [
        (BOX_DIAGONAL, mass + ends),
        (LONG_HIGH, total(halves(box.long - 1)[0])),
        (LONG_LOW, total(halves(0)[0])),
        (ACROSS_HIGH, total(sums[1][box.across - 1 :])),
        (ACROSS_LOW, total(sums[1][:1])),
        (LOAD_SUM, total(sums[4])),
    ]
    line = line_of(numbers, out.shape)
    out[...] = line
    table[...] = at_own_row(line, table.shape)


def means_of(ref):
    return [ref[0:1, index : index + 1] for index in range(4)]


def first_solve(box, load, low, high, left, right, means, zone, scale, diffusivity, decay, *rest):
    tables = rest[:N_TABLES]
    window, local, image, spectral, middle = rest[N_TABLES:]
    half = [0.5 * diffusivity[z, 2] for z in range(3)]
    rates = [decay[z] for z in range(3)]
    lane = lax.broadcasted_iota(jnp.int32, (box.across, box.deep), 1)
    ends = jnp.where((lane == 0) | (lane == box.deep - 1), jnp.float32(1.0), jnp.float32(0.0))
    image[...] = jnp.zeros((box.across, box.deep), jnp.float32)
    wide_sides, narrow_sides = Sides("wide", low, high), Sides("narrow", left, right)
    fill_window(box, window, load, wide_sides, narrow_sides, MARGIN, 0, MARGIN)

    def emit(start, values):
        values = values * (1.0 / cheb_center)
        values = values.reshape(8, box.across, box.deep)
        local[start : start + 8] = values
        total = image[...]
        for row in range(8):
            labels = zone[start + row]
            mass = looked_up(labels, rates) + looked_up(labels, half) * scale[start + row] * ends
            total = total + mass * values[row]
        image[...] = total

    box_solve(
        box,
        lambda row: window[1 + row : 9 + row, EDGE - MARGIN : EDGE + box.across + MARGIN],
        means_of(means),
        tables,
        None,
        None,
        spectral,
        middle,
        emit,
    )


def weights_of(
    box,
    zone,
    scale,
    low,
    high,
    left,
    right,
    diffusivity,
    decay,
    to_long,
    to_across,
    to_deep,
    mass,
    zone_window,
    scale_window,
):
    for index, (window, own) in enumerate(((scale_window, scale), (zone_window, zone))):
        start = index * REACH
        wide_sides = Sides("wide", *(ref.at[start : start + REACH] for ref in (low, high)))
        narrow_sides = Sides("narrow", left, right)
        fill_window(box, window, own, wide_sides, narrow_sides, REACH, start, 2 * REACH)
    half = [[0.5 * diffusivity[z, d] for d in range(3)] for z in range(3)]
    rates = [decay[z] for z in range(3)]
    lane = lax.broadcasted_iota(jnp.int32, (box.cols, box.deep), 1)
    ends = jnp.where((lane == 0) | (lane == box.deep - 1), jnp.float32(1.0), jnp.float32(0.0))
    not_last = jnp.where(lane == box.deep - 1, jnp.float32(0.0), jnp.float32(1.0))

    def one_row(row, before):
        labels, factor = zone_window[row], scale_window[row]
        now = [looked_up(labels, [half[z][d] for z in range(3)]) * factor for d in range(3)]
        to_across[row] = now[1] + pltpu.roll(now[1], box.cols - 1, 0)
        to_deep[row] = (now[2] + pltpu.roll(now[2], box.deep - 1, 1)) * not_last
        mass[row] = looked_up(labels, rates) + now[2] * ends
        to_long[jnp.maximum(row - 1, 0)] = before + now[0]
        return now[0]

    last_long = lax.fori_loop(0, box.rows - 2, one_row, jnp.zeros_like(ends), unroll=4)
    for row in range(box.rows - 2, box.rows):
        last_long = one_row(row, last_long)
    to_long[box.rows - 1] = last_long


def image_sums(
    box, zone, scale, local, image, low, high, left, right, table, diffusivity, out, up, down
):
    half = [[0.5 * diffusivity[z, d] for z in range(3)] for d in range(3)]
    shape = (box.long * box.across, box.deep)
    zone_flat, scale_flat, local_flat = zone.reshape(shape), scale.reshape(shape), local.reshape(shape)
    last_col = row_of(box.across, box.across - 1, box.long)
    first_col = row_of(box.across, 0, box.long)

    wide_sides, narrow_sides = Sides("wide", low, high), Sides("narrow", left, right)

    def side(source, place):
        return source(slice(place * box.long, (place + 1) * box.long), slice(None))

    above, below = wide_sides.high, wide_sides.low
    faces = [
        (0, zone[box.long - 1], scale[box.long - 1], local[box.long - 1], above(REACH), above(0)),
        (0, zone[0], scale[0], local[0], below(2 * REACH - 1), below(REACH - 1)),
        (
            1,
            zone_flat[last_col, :],
            scale_flat[last_col, :],
            local_flat[last_col, :],
            side(narrow_sides.high, REACH),
            side(narrow_sides.high, 0),
        ),
        (
            1,
            zone_flat[first_col, :],
            scale_flat[first_col, :],
            local_flat[first_col, :],
            side(narrow_sides.low, 2 * REACH - 1),
            side(narrow_sides.low, REACH - 1),
        ),
    ]
    flows = []
    for direction, labels, factor, values, far_labels, far_factor in faces:
        weight = looked_up(labels, half[direction]) * factor
        weight = weight + looked_up(far_labels, half[direction]) * far_factor
        flows.append(jnp.sum(weight * values, keepdims=True))
    long_pos, across_pos, long_count, across_count = position()
    numbers = [
        (IMAGE_SUM, jnp.sum(image[...], keepdims=True) + sum(flows)),
        (FLOW_LONG_HIGH, flows[0] * as_float(long_pos < long_count - 1)),
        (FLOW_LONG_LOW, flows[1] * as_float(long_pos > 0)),
        (FLOW_ACROSS_HIGH, flows[2] * as_float(across_pos < across_count - 1)),
        (FLOW_ACROSS_LOW, flows[3] * as_float(across_pos > 0)),
    ]
    known = table[...] + at_own_row(line_of(numbers, (8, out.shape[1])), out.shape)
    out[...] = known
    edge = REACH * box.across
    even = is_even("wide")
    for target, pair in ((up, (box.long - REACH, 0)), (down, (0, box.long - REACH))):
        target[:edge] = local[pl.ds(jnp.where(even, *pair), REACH)].reshape(edge, box.deep)
        target[edge:] = known


def column(values, index):
    return values[:, index : index + 1]


def coarse_inverse(numbers, work):
    count, width = work.shape
    across = lax.axis_size("narrow")
    beyond = pltpu.roll(numbers, count - across, 0)
    beside = pltpu.roll(numbers, count - 1, 0)
    before = pltpu.roll(numbers, across, 0)
    ahead = pltpu.roll(numbers, 1, 0)
    place = lax.broadcasted_iota(jnp.int32, (count, 1), 0)
    across_pos = lax.rem(place, across)
    nothing = jnp.zeros((count, 1), jnp.float32)
    couplings = []
    diagonal = column(numbers, BOX_DIAGONAL)
    for own, other, there, inside in (
        (LONG_HIGH, LONG_LOW, beyond, place < count - across),
        (LONG_LOW, LONG_HIGH, before, place >= across),
        (ACROSS_HIGH, ACROSS_LOW, beside, across_pos < across - 1),
        (ACROSS_LOW, ACROSS_HIGH, ahead, across_pos > 0),
    ):
        shared = jnp.where(inside, column(there, other), nothing)
        diagonal = diagonal + column(numbers, own) + shared
        couplings.append(jnp.where(inside, column(numbers, own) + shared, nothing))
    rows = lax.broadcasted_iota(jnp.int32, (count, width), 0)
    cols = lax.broadcasted_iota(jnp.int32, (count, width), 1)
    blank = jnp.zeros((count, width), jnp.float32)
    matrix = jnp.where(cols == rows, diagonal, blank)
    for shift, coupling in zip((across, -across, 1, -1), couplings):
        matrix = matrix - jnp.where((cols == rows + shift) & (cols < count), coupling, blank)
    matrix = jnp.where(cols == rows + count, jnp.ones((count, 1), jnp.float32), matrix)
    if count <= 16:
        for step in range(count):
            pivot_row = matrix[step : step + 1, :] / matrix[step : step + 1, step : step + 1]
            rest = matrix - matrix[:, step : step + 1] * pivot_row
            matrix = jnp.where(rows == step, pivot_row, rest)
        return pltpu.roll(matrix, width - count, 1)
    work[...] = matrix

    def eliminate(step, _):
        values = work[...]
        pivot_row = work[pl.ds(step, 1), :]
        at_step = cols == step
        factors = jnp.sum(jnp.where(at_step, values, blank), axis=1, keepdims=True)
        pivot = jnp.sum(jnp.where(at_step[:1], pivot_row, blank[:1]), axis=1, keepdims=True)
        pivot_row = pivot_row / pivot
        work[...] = jnp.where(rows == step, pivot_row, values - factors * pivot_row)
        return 0

    lax.fori_loop(0, count, eliminate, 0)
    values = work[...]
    if count % 128:
        return pltpu.roll(values, width - count, 1)
    return values[:, count : 2 * count]


def answer(inverse, sums):
    return jnp.sum(inverse * sums, axis=0, keepdims=True)


def at_box(values, row_side, col_side):
    long_pos, across_pos, long_count, across_count = position()
    there_long, there_across = long_pos + row_side, across_pos + col_side
    inside = (
        (there_long >= 0)
        & (there_long < long_count)
        & (there_across >= 0)
        & (there_across < across_count)
    )
    lanes = lax.broadcasted_iota(jnp.int32, values.shape, 1)
    wanted = (lanes == there_long * across_count + there_across) & inside
    return jnp.sum(jnp.where(wanted, values, jnp.zeros_like(values)), axis=1, keepdims=True)


def coarse_corrections(parts, *refs):
    table_parts, (out, work) = refs[:parts], refs[parts:]
    count = work.shape[0]
    numbers = last_rows_merged(table_parts, count)
    across_count = lax.axis_size("narrow")
    inverse = coarse_inverse(numbers, work)
    sums = column(numbers, IMAGE_SUM)
    sums = sums - column(pltpu.roll(numbers, count - across_count, 0), FLOW_LONG_LOW)
    sums = sums - column(pltpu.roll(numbers, across_count, 0), FLOW_LONG_HIGH)
    sums = sums - column(pltpu.roll(numbers, count - 1, 0), FLOW_ACROSS_LOW)
    sums = sums - column(pltpu.roll(numbers, 1, 0), FLOW_ACROSS_HIGH)
    load_sums = column(numbers, LOAD_SUM)
    sums = load_sums * (1.0 - 1.0 / cheb_center) - sums
    out[0:1, :] = answer(inverse, load_sums) * (1.0 / cheb_center)
    out[1:2, :] = answer(inverse, sums) * gain


def second_solve(box, local, low, high, left, right, means, answers, *rest):
    to_long, to_across, to_deep, mass, load_window = rest[:5]
    tables = rest[5 : 5 + N_TABLES]
    iterate, top, bottom, last_col, first_col, out = rest[5 + N_TABLES : 11 + N_TABLES]
    window, spectral, middle, sems = rest[11 + N_TABLES :]
    long_pos, across_pos, long_count, across_count = position()
    coarse = answers[0:1, :]
    own_shift = at_box(answers[1:2, :], 0, 0)
    shifts = {
        (row_side, col_side): at_box(coarse, row_side, col_side)
        for row_side in (-1, 0, 1)
        for col_side in (-1, 0, 1)
    }

    def add(values, row_side, col_side):
        shift = shifts[row_side, col_side]
        if values.ndim == 3:
            shift = shift.reshape(1, 1, 1)
        return values + shift

    edge = REACH * box.across
    low, high = (
        ref.at[:edge].reshape(REACH, box.across, box.deep) for ref in (low, high)
    )
    wide_sides, narrow_sides = Sides("wide", low, high), Sides("narrow", left, right)
    fill_window(box, window, local, wide_sides, narrow_sides, REACH, 0, REACH, add)
    weights = (to_long, to_across, to_deep, mass)

    start, stop = EDGE - MARGIN, EDGE + box.across + MARGIN

    flow = [to_long[0, start:stop] * (window[1, start:stop] - window[0, start:stop])]

    def residual(start_row):
        rows = []
        for row in range(start_row + 1, start_row + 9):
            image, flow[0] = negative_image(window, row, row, start, stop, flow[0], weights)
            rows.append((load_window[row, start:stop] + image)[None])
        return jnp.concatenate(rows, axis=0)

    inner = slice(EDGE, EDGE + box.across)
    first = REACH
    row_ids = lax.broadcasted_iota(jnp.int32, (1, padded(box.ex)), 1)
    col_ids = lax.broadcasted_iota(jnp.int32, (1, padded(box.ey)), 1)
    row_mask = jnp.where(row_ids < MARGIN, as_float(long_pos > 0), 1.0)
    row_mask = jnp.where(row_ids >= MARGIN + box.long, as_float(long_pos < long_count - 1), row_mask)
    col_mask = jnp.where(col_ids < MARGIN, as_float(across_pos > 0), 1.0)
    col_mask = jnp.where(
        col_ids >= MARGIN + box.across, as_float(across_pos < across_count - 1), col_mask
    )
    keep = 1.0 + rho_second * rho_first
    copies = []

    def emit(start, values):
        rows = values.reshape(8, box.across, box.deep)
        before = window[first + start : first + start + 8, inner, :]
        shift = own_shift.reshape(1, 1, 1)
        iterate[start : start + 8] = keep * before + (gain * rows + shift)
        copies.append(
            pltpu.make_async_copy(
                iterate.at[start : start + 8], out.at[start : start + 8], sems.at[len(copies)]
            )
        )
        copies[-1].start()

    box_solve(
        box, residual, means_of(means), tables, row_mask, col_mask, spectral, middle, emit
    )
    rows = in_order(is_even("wide"), iterate[box.long - 1], iterate[0])
    top[...], bottom[...] = rows
    flat = iterate.reshape(box.long * box.across, box.deep)
    cols = [flat[row_of(box.across, col, box.long), :] for col in (box.across - 1, 0)]
    last_col[...], first_col[...] = in_order(is_even("narrow"), *cols)
    for copy in copies:
        copy.wait()


def last_residual(
    box,
    load,
    partial,
    low,
    high,
    left,
    right,
    to_long,
    to_across,
    to_deep,
    mass,
    out,
    window,
    result,
    sems,
):
    inner = slice(EDGE, EDGE + box.across)
    flat = window.reshape((box.long + 2) * box.cols, box.deep)
    blank = jnp.zeros((box.long + 2, EDGE, box.deep), jnp.float32)
    window[:, :EDGE, :] = blank
    window[:, EDGE + box.across :, :] = blank
    window[1 : 1 + box.long, inner, :] = partial[...]
    wide_sides, narrow_sides = Sides("wide", low, high), Sides("narrow", left, right)
    window[0, inner, :] = wide_sides.low(Ellipsis)
    window[1 + box.long, inner, :] = wide_sides.high(Ellipsis)
    flat[row_of(box.cols, EDGE - 1, box.long, 1), :] = narrow_sides.low(Ellipsis)
    flat[row_of(box.cols, EDGE + box.across, box.long, 1), :] = narrow_sides.high(Ellipsis)
    weights = (to_long, to_across, to_deep, mass)

    def one_row(row, flow):
        image, flow = negative_image(
            window, row + 1, REACH + row, inner.start, inner.stop, flow, weights
        )
        result[row] = load[row] + image
        return flow

    flow = to_long[REACH - 1, inner] * (window[1, inner] - window[0, inner])
    chunk = box.long // 4
    copies = []
    for index in range(4):
        rows = slice(index * chunk, (index + 1) * chunk)
        flow = lax.fori_loop(rows.start, rows.stop, one_row, flow, unroll=4)
        copy = pltpu.make_async_copy(result.at[rows], out.at[rows], sems.at[index])
        copy.start()
        copies.append(copy)
    for copy in copies:
        copy.wait()


def swaps(axis, around):
    sizes = (lax.axis_size("wide"), lax.axis_size("narrow"))
    along = ("wide", "narrow").index(axis)
    size, beside = sizes[along], sizes[1 - along]

    def number(place, other_place):
        pair = (place, other_place) if along == 0 else (other_place, place)
        return pair[0] * sizes[1] + pair[1]

    ways = []
    for way in range(2):
        pairs = []
        for place in range(size):
            for other_place in range(beside):
                partner = place + 1 if place % 2 == way else place - 1
                there = other_place
                if around and size % 2 == 0:
                    partner %= size
                if not 0 <= partner < size:
                    partner = place
                    there = other_place ^ 1 if beside % 2 == 0 else other_place
                pairs.append((number(place, other_place), number(partner, there)))
        ways.append(pairs)
    return ways


def exchange(axis, first, second, around=False):
    ways = swaps(axis, around)
    axes = ("wide", "narrow")
    return lax.ppermute(first, axes, ways[0]), lax.ppermute(second, axes, ways[1])


def two_away(axis, table):
    size = lax.axis_size(axis)
    return lax.ppermute(table, axis, [(i, (i + 2) % size) for i in range(size)])


def tell(table):
    count = table.shape[0]
    long_pos, across_pos, _, across_count = position()
    own = lax.dynamic_slice_in_dim(table, long_pos * across_count + across_pos, 1, axis=0)
    line = jnp.broadcast_to(own, (count, 1, 128))
    told = lax.all_to_all(line, ("wide", "narrow"), split_axis=0, concat_axis=0, tiled=True)
    return told.reshape(count, 128)


def on_device(zone, scale, diffusivity, decay, load):
    box = Box(load.shape)
    long, across, deep = load.shape
    count = lax.axis_size("wide") * lax.axis_size("narrow")
    by_margins = lax.axis_size("wide") == 4 and lax.axis_size("narrow") == 4
    tables = tables_of(box)
    cells = f32(long, across, deep)
    whole_zone = jax.ShapeDtypeStruct(cells.shape, zone.dtype)
    window = f32(box.rows, box.cols, deep)
    table_shape = f32(count, 128)
    anywhere = pl.BlockSpec(memory_space=pl.ANY)
    in_hbm = pl.BlockSpec(memory_space=pltpu.HBM)

    def scratch(shape):
        return pltpu.VMEM(shape, jnp.float32)

    def pinned(field):
        return pltpu.with_memory_space_constraint(field, pltpu.HBM)

    spectral = scratch((box.ey, padded(box.ex), deep))
    middle = scratch((long, padded(box.ey), deep))

    def pack(wide, fields, sides, parts=(), after=()):
        rows = message_rows(box, wide * len(fields)) + (count if parts else 0)
        message = f32(rows, deep)
        body = functools.partial(pack_fields, box, wide, len(fields), len(parts), len(after))
        return call(
            body,
            (message, message) + ((table_shape,) if parts else ()),
            [VMEM] * (len(fields) + 2 + len(parts)) + [anywhere] * len(after),
        )(*fields, *sides, *parts, *after)

    far = f32(2 * REACH, across, deep)
    far_zone, far_scale = zone, scale
    load, load_first, load_second, first, second = call(
        functools.partial(bring_edges, box),
        (cells,) + (f32(MARGIN, across, deep),) * 2 + (far, far),
        [in_hbm] * 3,
        [pltpu.VMEM((2, REACH, across, deep), zone.dtype), pltpu.SemaphoreType.DMA((7,))],
    )(pinned(zone), pinned(scale), pinned(load))
    load_wide = exchange("wide", load_first, load_second)
    far_wide = exchange("wide", first, second)
    load_first, load_second = pack(MARGIN, [load], load_wide)
    load_narrow = exchange("narrow", load_first, load_second)
    zone, scale, sums, table = call(
        functools.partial(box_sums, box),
        (whole_zone, cells, f32(8, 128), table_shape),
        [in_hbm] * 2 + [VMEM, anywhere] + [SMEM] * 2,
        [pltpu.SemaphoreType.DMA((4,))],
    )(pinned(far_zone), pinned(far_scale), load, load_first, diffusivity, decay)
    far_narrow = exchange("narrow", *pack(REACH, [scale, zone], far_wide))
    load_window, local, image = call(
        functools.partial(first_solve, box),
        (window, cells, f32(across, deep)),
        [VMEM] * 8 + [SMEM] * 2 + [VMEM] * N_TABLES,
        [spectral, middle],
        flops=4 * 10**9,
    )(load, *load_wide, *load_narrow, sums, zone, scale, diffusivity, decay, *tables)
    message = f32(REACH * across + count, deep)
    table, first, second = call(
        functools.partial(image_sums, box), (table_shape, message, message), [VMEM] * 9 + [SMEM]
    )(zone, scale, local, image, *far_wide, *far_narrow, table, diffusivity)
    own_table = table
    wide = exchange("wide", first, second, by_margins)
    parts = (table, *wide)
    if by_margins:
        parts += (two_away("wide", table),)
    weights = call(
        functools.partial(weights_of, box),
        (window,) * 4,
        [VMEM] * 6 + [SMEM] * 2,
        [scratch(window.shape)] * 2,
        flops=10**9,
    )(zone, scale, *far_wide, *far_narrow, diffusivity, decay)
    first, second, table = pack(REACH, [local], wide, parts, weights[3:])
    narrow = exchange("narrow", first, second)
    if by_margins:
        table = call(join_rows, table_shape, [VMEM] * 2)(table, narrow[0])
        parts = (table, two_away("narrow", table))
    else:
        parts = (tell(own_table),)
    row, col = f32(across, deep), f32(long, deep)
    answers = call(
        functools.partial(coarse_corrections, len(parts)),
        f32(8, -(-count // 128) * 128),
        [VMEM] * len(parts),
        [scratch((count, -(-2 * count // 128) * 128))],
    )(*parts)
    iterate, first_row, second_row, first_col, second_col, result = call(
        functools.partial(second_solve, box),
        (cells, row, row, col, col, cells),
        [VMEM] * (12 + N_TABLES),
        [scratch(window.shape), spectral, middle, pltpu.SemaphoreType.DMA((long // 8,))],
        flops=4 * 10**9,
        out_spec=(VMEM,) * 5 + (anywhere,),
    )(local, *wide, *narrow, sums, answers, *weights, load_window, *tables)
    narrow = exchange("narrow", first_col, second_col)
    wide = exchange("wide", first_row, second_row)
    residual = call(
        functools.partial(last_residual, box),
        cells,
        [VMEM] * 10,
        [scratch((long + 2, box.cols, deep)), scratch(cells.shape), pltpu.SemaphoreType.DMA((4,))],
        out_spec=anywhere,
    )(load, iterate, *wide, *narrow, *weights)
    return result, residual


def solution(mesh):
    split = P(("groups", "wide"), "narrow", None)
    return jax.shard_map(
        on_device,
        mesh=mesh,
        in_specs=(split, split, P(), P(), split),
        out_specs=(split, split),
        check_vma=False,
    )
```

```python
import functools

import jax
import jax.numpy as jnp
import ml_dtypes
import numpy as np
from jax import lax
from jax.experimental import pallas as pl
from jax.experimental.pallas import tpu as pltpu
from jax.sharding import PartitionSpec as P

MARGIN = 4
REACH = MARGIN + 1
EDGE = 8

cheb_center = 1.3
cheb_radius = 1.2
cheb_ratio = 1.3 / 1.2
rho_first = 1.0 / cheb_ratio
rho_second = 1.0 / (2.0 * cheb_ratio - rho_first)
gain = 2.0 * rho_second / cheb_radius

MEANS = range(4)
BOX_DIAGONAL, LONG_HIGH, LONG_LOW, ACROSS_HIGH, ACROSS_LOW, LOAD_SUM = range(4, 10)
IMAGE_SUM, FLOW_LONG_HIGH, FLOW_LONG_LOW, FLOW_ACROSS_HIGH, FLOW_ACROSS_LOW = range(16, 21)

VMEM = pl.BlockSpec(memory_space=pltpu.VMEM)
SMEM = pl.BlockSpec(memory_space=pltpu.SMEM)


def sine_basis(length):
    indices = np.arange(1, length + 1)
    phases = indices[:, None] * indices[None, :] % (2 * (length + 1))
    table = np.sqrt(2.0 / (length + 1)) * np.sin(np.pi * phases / (length + 1))
    eigvals = 4.0 * np.sin(np.pi * indices / (2.0 * (length + 1))) ** 2
    return table.astype(np.float32), eigvals.astype(np.float32)


def call(body, out_shape, in_specs, scratch=(), flops=0, moved=0, out_spec=None):
    return pl.pallas_call(
        body,
        out_shape=out_shape,
        in_specs=in_specs,
        out_specs=out_spec or jax.tree.map(lambda _: VMEM, out_shape),
        scratch_shapes=list(scratch),
        compiler_params=pltpu.CompilerParams(vmem_limit_bytes=30 * 2**20),
        cost_estimate=pl.CostEstimate(flops=flops, bytes_accessed=moved, transcendentals=0),
    )


def f32(*shape):
    return jax.ShapeDtypeStruct(shape, jnp.float32)


class Box:
    def __init__(self, shape):
        self.long, self.across, self.deep = shape
        self.ex = self.long + 2 * MARGIN
        self.ey = self.across + 2 * MARGIN
        self.rows = self.long + 2 * REACH
        self.cols = self.across + 2 * EDGE
        self.flat = self.rows * self.cols


def pieces(values, count):
    parts = []
    for _ in range(count):
        part = values.astype(jnp.bfloat16)
        parts.append(part)
        values = values - part.astype(jnp.float32)
    return parts


def left_table(table, depth, count):
    rows, cols = table.shape
    wide = np.zeros((rows, depth), np.float32)
    wide[:, :cols] = table
    parts = []
    rest = wide
    for _ in range(count):
        part = rest.astype(ml_dtypes.bfloat16)
        parts.append(part)
        rest = rest - part.astype(np.float32)
    blank = np.zeros_like(parts[0])
    lines = []
    for index in range(count):
        used = count - index if count > 2 else count
        lines.append(np.concatenate([parts[index]] * used + [blank] * (count - used), axis=1))
    return np.concatenate(lines, axis=0)


def right_tables(table):
    rest, parts = table, []
    for _ in range(3):
        part = rest.astype(ml_dtypes.bfloat16)
        parts.append(part)
        rest = rest - part.astype(np.float32)
    both = np.concatenate([parts[0], parts[1]], axis=1)
    return np.concatenate([both, both], axis=0), np.concatenate([parts[2], parts[0]], axis=0)


def padded(size):
    return -(-size // 16) * 16


FORWARD, BACKWARD = 2, 3


def tables_of(box):
    sine_x, eig_x = sine_basis(box.ex)
    sine_y, eig_y = sine_basis(box.ey)
    sine_z, eig_z = sine_basis(box.deep)
    from_y = sine_y[MARGIN : MARGIN + box.across]
    from_x = sine_x[MARGIN : MARGIN + box.long]
    spread = np.broadcast_to(eig_x[:, None], (box.ex, box.deep))
    main_z, rest_z = right_tables(sine_z)
    return [
        jnp.asarray(np.ascontiguousarray(t))
        for t in (
            left_table(sine_y, padded(box.ey), FORWARD),
            left_table(sine_x, padded(box.ex), FORWARD),
            left_table(from_x, padded(box.ex), BACKWARD),
            left_table(from_y, padded(box.ey), BACKWARD),
            main_z,
            rest_z,
            spread,
            eig_z[None, :],
            eig_y[None, :],
        )
    ]


N_TABLES = 9


def bf16_dot(left, right):
    return lax.dot_general(
        left, right, (((1,), (0,)), ((), ())), preferred_element_type=jnp.float32
    )


def dot_left(table, values, count, rows):
    total = bf16_dot(table, jnp.concatenate(pieces(values, count), axis=0))
    return sum(total[index * rows : (index + 1) * rows] for index in range(1, count)) + total[:rows]


def dot_right(values, main, rest, count):
    deep = values.shape[1]
    parts = pieces(values, count)
    total = bf16_dot(jnp.concatenate(parts[:2], axis=1), main)
    result = total[:, :deep] + total[:, deep:]
    if count == 3:
        result = result + bf16_dot(jnp.concatenate([parts[0], parts[2]], axis=1), rest)
    return result


def with_rows(values, rows):
    if values.shape[0] == rows:
        return values
    blank = jnp.zeros((rows - values.shape[0],) + values.shape[1:], values.dtype)
    return jnp.concatenate([values, blank], axis=0)


def box_solve(box, source, means, tables, row_mask, col_mask, spectral, middle, emit):
    into_y, into_x, from_x, from_y, main_z, rest_z, spread, eig_z, eig_y = tables
    deep = box.deep
    deep_x, deep_y = padded(box.ex), padded(box.ey)
    into_y, into_x = into_y[...], into_x[...]
    if col_mask is not None:
        mask = jnp.concatenate([col_mask] * FORWARD, axis=1)
        into_y = (into_y.astype(jnp.float32) * mask).astype(jnp.bfloat16)
        mask = jnp.concatenate([row_mask] * FORWARD, axis=1)
        into_x = (into_x.astype(jnp.float32) * mask).astype(jnp.bfloat16)
    from_x, from_y, main_z, rest_z = from_x[...], from_y[...], main_z[...], rest_z[...]
    if deep_x > box.ex:
        spectral[:, box.ex :, :] = jnp.zeros((box.ey, deep_x - box.ex, deep), jnp.float32)
    if deep_y > box.ey:
        middle[:, box.ey :, :] = jnp.zeros((box.long, deep_y - box.ey, deep), jnp.float32)
    for start in range(0, box.ex, 8):
        block = source(start).reshape(8 * box.ey, deep)
        block = dot_right(block, main_z, rest_z, FORWARD).reshape(8, box.ey, deep)
        rows = []
        for row in range(0, 8, 2):
            pair = jnp.concatenate([block[row], block[row + 1]], axis=1)
            pair = dot_left(into_y, with_rows(pair, deep_y), FORWARD, box.ey)
            rows += [pair[:, :deep], pair[:, deep:]]
        spectral[:, start : start + 8, :] = jnp.swapaxes(jnp.stack(rows), 0, 1)
    base = means[3] + means[0] * spread[...] + means[2] * eig_z[...]
    cols = []
    for col in range(0, box.ey, 2):
        pair = jnp.concatenate([spectral[col], spectral[col + 1]], axis=1)
        pair = dot_left(into_x, pair, FORWARD, box.ex)
        pair = jnp.concatenate(
            [
                pair[:, part * deep : (part + 1) * deep]
                / (base + means[1] * eig_y[0, col + part])
                for part in range(2)
            ],
            axis=1,
        )
        pair = dot_left(from_x, with_rows(pair, deep_x), BACKWARD, box.long)
        cols += [pair[:, :deep], pair[:, deep:]]
        if len(cols) == 8:
            middle[:, col - 6 : col + 2, :] = jnp.swapaxes(jnp.stack(cols), 0, 1)
            cols = []
    for start in range(0, box.long, 8):
        parts = []
        for row in range(start, start + 8, 2):
            pair = jnp.concatenate([middle[row], middle[row + 1]], axis=1)
            pair = dot_left(from_y, pair, BACKWARD, box.across)
            parts += [pair[:, :deep], pair[:, deep:]]
        emit(start, dot_right(jnp.concatenate(parts, axis=0), main_z, rest_z, BACKWARD))


def position():
    long_pos, across_pos = lax.axis_index("wide"), lax.axis_index("narrow")
    return long_pos, across_pos, lax.axis_size("wide"), lax.axis_size("narrow")


def as_float(flag):
    return jnp.where(flag, jnp.float32(1.0), jnp.float32(0.0))


def is_even(axis):
    return lax.rem(lax.axis_index(axis), 2) == 0


class Sides:
    def __init__(self, axis, first, second):
        position = lax.axis_index(axis)
        self.even = is_even(axis)
        self.has_low = as_float(position > 0)
        self.has_high = as_float(position < lax.axis_size(axis) - 1)
        self.first, self.second = first, second

    def low(self, *index):
        return jnp.where(self.even, self.second[index], self.first[index]) * self.has_low

    def high(self, *index):
        return jnp.where(self.even, self.first[index], self.second[index]) * self.has_high


def in_order(even, up, down):
    return jnp.where(even, up, down), jnp.where(even, down, up)


def row_of(stride, col, count, first=0):
    return pl.ds(first * stride + col, count, stride=stride)


def pack_columns(box, fields, wide_sides, wide, first, second):
    corner = len(fields) * wide * box.long
    even = is_even("narrow")
    place = 0
    for field, sides in zip(fields, wide_sides):
        for step in range(wide):
            cols = (box.across - wide + step, step)
            values = [field[row_of(box.across, col, box.long), :] for col in cols]
            low = [sides.low(row_of(box.across, col, wide), slice(None)) for col in cols]
            high = [sides.high(row_of(box.across, col, wide), slice(None)) for col in cols]
            at = corner + 2 * REACH * place
            for start, parts in ((place * box.long, values), (at, low), (at + REACH, high)):
                parts = in_order(even, *(part.astype(jnp.float32) for part in parts))
                size = parts[0].shape[0]
                first[start : start + size, :], second[start : start + size, :] = parts
            place += 1


def message_rows(box, count):
    return -(-(count * (box.long + 2 * REACH)) // 8) * 8


def pack_fields(box, wide, fields, tables, after, *refs):
    own, (low, high), refs = refs[:fields], refs[fields : fields + 2], refs[fields + 2 :]
    parts, (first, second, *table) = refs[:tables], refs[tables + after :]
    size = wide * box.across
    flat = [field.reshape(box.long * box.across, box.deep) for field in own]
    low = low.reshape(low.size // box.deep, box.deep)
    high = high.reshape(high.size // box.deep, box.deep)
    sides = [
        Sides("wide", *(ref.at[index * size : (index + 1) * size] for ref in (low, high)))
        for index in range(fields)
    ]
    pack_columns(box, flat, sides, wide, first, second)
    if tables:
        known = last_rows_merged(parts, table[0].shape[0])
        table[0][...] = known
        first[first.shape[0] - known.shape[0] :, :] = known
        second[second.shape[0] - known.shape[0] :, :] = known


def bring_edges(
    box, zone, scale, load, own_load, load_first, load_second, first, second, staged, sems
):
    even = is_even("wide")

    def edges(wide):
        up, down = box.long - wide, 0
        return [pl.ds(jnp.where(even, *pair), wide) for pair in ((up, down), (down, up))]

    copies = [
        (load.at[edges(MARGIN)[0]], load_first),
        (load.at[edges(MARGIN)[1]], load_second),
        (zone.at[edges(REACH)[0]], staged.at[0]),
        (zone.at[edges(REACH)[1]], staged.at[1]),
        (scale.at[edges(REACH)[0]], first.at[:REACH]),
        (scale.at[edges(REACH)[1]], second.at[:REACH]),
        (load, own_load),
    ]
    copies = [
        pltpu.make_async_copy(source, target, sems.at[index])
        for index, (source, target) in enumerate(copies)
    ]
    for copy in copies:
        copy.start()
    for copy in copies[:4]:
        copy.wait()
    first[REACH:] = staged[0].astype(jnp.float32)
    second[REACH:] = staged[1].astype(jnp.float32)
    for copy in copies[4:]:
        copy.wait()


def fill_window(box, window, own, wide_sides, narrow_sides, wide, place, total, add=None):
    flat = window.reshape(box.flat, box.deep)
    nothing = jnp.zeros((box.rows, EDGE, box.deep), jnp.float32)
    window[:, :EDGE, :] = nothing
    window[:, EDGE + box.across :, :] = nothing
    if add is None:
        add = lambda values, row_side, col_side: values
    inner = slice(EDGE, EDGE + box.across)
    first, last = REACH, REACH + box.long
    if wide < REACH:
        blank = jnp.zeros((1, box.across, box.deep), jnp.float32)
        window[0:1, inner, :] = blank
        window[box.rows - 1 :, inner, :] = blank
    window[first:last, inner, :] = add(own[...].astype(jnp.float32), 0, 0)
    window[first - wide : first, inner, :] = add(wide_sides.low(Ellipsis), -1, 0)
    window[last : last + wide, inner, :] = add(wide_sides.high(Ellipsis), 1, 0)
    corner = total * box.long
    for step in range(wide):
        for source, col, side in (
            (narrow_sides.low, EDGE - wide + step, -1),
            (narrow_sides.high, EDGE + box.across + step, 1),
        ):
            for start, size, row, row_side in (
                ((place + step) * box.long, box.long, first, 0),
                (corner + 2 * REACH * (place + step), wide, first - wide, -1),
                (corner + 2 * REACH * (place + step) + REACH, wide, last, 1),
            ):
                values = source(slice(start, start + size), slice(None))
                flat[row_of(box.cols, col, size, row), :] = add(values, row_side, side)


def negative_image(window, row, at, first, last, flow_before, weights):
    to_long, to_across, to_deep, mass = weights
    x = window[row, first:last]
    flow_long = to_long[at, first:last] * (window[row + 1, first:last] - x)
    flow_across = to_across[at, first:last] * (window[row, first + 1 : last + 1] - x)
    flow_from = to_across[at, first - 1 : last - 1] * (x - window[row, first - 1 : last - 1])
    lanes = x.shape[1]
    flow_deep = to_deep[at, first:last] * (pltpu.roll(x, lanes - 1, 1) - x)
    total = flow_long - flow_before - mass[at, first:last] * x
    total = total + (flow_across - flow_from)
    total = total + (flow_deep - pltpu.roll(flow_deep, 1, 1))
    return total, flow_long


def looked_up(labels, values):
    return jnp.where(labels == 0, values[0], jnp.where(labels == 1, values[1], values[2]))


def at_own_row(line, shape):
    long_pos, across_pos, _, across_count = position()
    rows = lax.broadcasted_iota(jnp.int32, shape, 0)
    own = rows == long_pos * across_count + across_pos
    return jnp.where(own, line[:1], jnp.zeros(shape, jnp.float32))


def merged(table, *others):
    for other in others:
        table = jnp.where(table != 0.0, table, other)
    return table


def last_rows_merged(refs, count):
    return merged(*(ref[ref.shape[0] - count :, :] for ref in refs))


def join_rows(table, message, out):
    out[...] = last_rows_merged((table, message), out.shape[0])


def line_of(numbers, shape):
    lanes = lax.broadcasted_iota(jnp.int32, shape, 1)
    line = jnp.zeros(shape, jnp.float32)
    for index, number in numbers:
        line = jnp.where(lanes == index, number, line)
    return line


def box_sums(
    box, far_zone, far_scale, load, after, diffusivity, decay, zone, scale, out, table, sems
):
    del after
    parts = 2
    size = box.long // parts
    copies = []
    for part in range(parts):
        rows = slice(part * size, (part + 1) * size)
        for index, (source, target) in enumerate(((far_zone, zone), (far_scale, scale))):
            copy = pltpu.make_async_copy(
                source.at[rows], target.at[rows], sems.at[2 * part + index]
            )
            copy.start()
            copies.append(copy)
    step = 4
    nothing = jnp.zeros((box.across, box.deep), jnp.float32)
    half = [[0.5 * diffusivity[z, d] for z in range(3)] for d in range(3)]
    rates = [decay[z] for z in range(3)]

    def halves(row):
        labels, factor = zone[row], scale[row]
        return [looked_up(labels, half[d]) * factor for d in range(3)] + [looked_up(labels, rates)]

    def some_rows(index, sums):
        for row in range(step):
            row = index * step + row
            sums = [total + more for total, more in zip(sums, halves(row) + [load[row]])]
        return sums

    sums = [nothing] * 5
    for part in range(parts):
        for copy in copies[2 * part : 2 * part + 2]:
            copy.wait()
        per_part = size // step
        sums = lax.fori_loop(part * per_part, (part + 1) * per_part, some_rows, sums)

    def total(values):
        return jnp.sum(values, keepdims=True).reshape(1, 1)

    cells = box.long * box.across * box.deep
    numbers = [(index, total(sums[index]) * (2.0 / cells)) for index in range(3)]
    mass = total(sums[3])
    numbers += [(3, mass / cells)]
    ends = total(sums[2][:, :1]) + total(sums[2][:, box.deep - 1 :])
    numbers += [
        (BOX_DIAGONAL, mass + ends),
        (LONG_HIGH, total(halves(box.long - 1)[0])),
        (LONG_LOW, total(halves(0)[0])),
        (ACROSS_HIGH, total(sums[1][box.across - 1 :])),
        (ACROSS_LOW, total(sums[1][:1])),
        (LOAD_SUM, total(sums[4])),
    ]
    line = line_of(numbers, out.shape)
    out[...] = line
    table[...] = at_own_row(line, table.shape)


def means_of(ref):
    return [ref[0:1, index : index + 1] for index in range(4)]


def first_solve(box, load, low, high, left, right, means, zone, scale, diffusivity, decay, *rest):
    tables = rest[:N_TABLES]
    window, local, image, spectral, middle = rest[N_TABLES:]
    half = [0.5 * diffusivity[z, 2] for z in range(3)]
    rates = [decay[z] for z in range(3)]
    lane = lax.broadcasted_iota(jnp.int32, (box.across, box.deep), 1)
    ends = jnp.where((lane == 0) | (lane == box.deep - 1), jnp.float32(1.0), jnp.float32(0.0))
    image[...] = jnp.zeros((box.across, box.deep), jnp.float32)
    wide_sides, narrow_sides = Sides("wide", low, high), Sides("narrow", left, right)
    fill_window(box, window, load, wide_sides, narrow_sides, MARGIN, 0, MARGIN)

    def emit(start, values):
        values = values * (1.0 / cheb_center)
        values = values.reshape(8, box.across, box.deep)
        local[start : start + 8] = values
        total = image[...]
        for row in range(8):
            labels = zone[start + row]
            mass = looked_up(labels, rates) + looked_up(labels, half) * scale[start + row] * ends
            total = total + mass * values[row]
        image[...] = total

    box_solve(
        box,
        lambda row: window[1 + row : 9 + row, EDGE - MARGIN : EDGE + box.across + MARGIN],
        means_of(means),
        tables,
        None,
        None,
        spectral,
        middle,
        emit,
    )


def weights_of(
    box,
    zone,
    scale,
    low,
    high,
    left,
    right,
    diffusivity,
    decay,
    to_long,
    to_across,
    to_deep,
    mass,
    zone_window,
    scale_window,
):
    for index, (window, own) in enumerate(((scale_window, scale), (zone_window, zone))):
        start = index * REACH
        wide_sides = Sides("wide", *(ref.at[start : start + REACH] for ref in (low, high)))
        narrow_sides = Sides("narrow", left, right)
        fill_window(box, window, own, wide_sides, narrow_sides, REACH, start, 2 * REACH)
    half = [[0.5 * diffusivity[z, d] for d in range(3)] for z in range(3)]
    rates = [decay[z] for z in range(3)]
    lane = lax.broadcasted_iota(jnp.int32, (box.cols, box.deep), 1)
    ends = jnp.where((lane == 0) | (lane == box.deep - 1), jnp.float32(1.0), jnp.float32(0.0))
    not_last = jnp.where(lane == box.deep - 1, jnp.float32(0.0), jnp.float32(1.0))

    def one_row(row, before):
        labels, factor = zone_window[row], scale_window[row]
        now = [looked_up(labels, [half[z][d] for z in range(3)]) * factor for d in range(3)]
        to_across[row] = now[1] + pltpu.roll(now[1], box.cols - 1, 0)
        to_deep[row] = (now[2] + pltpu.roll(now[2], box.deep - 1, 1)) * not_last
        mass[row] = looked_up(labels, rates) + now[2] * ends
        to_long[jnp.maximum(row - 1, 0)] = before + now[0]
        return now[0]

    last_long = lax.fori_loop(0, box.rows - 2, one_row, jnp.zeros_like(ends), unroll=4)
    for row in range(box.rows - 2, box.rows):
        last_long = one_row(row, last_long)
    to_long[box.rows - 1] = last_long


def image_sums(
    box, zone, scale, local, image, low, high, left, right, table, diffusivity, out, up, down
):
    half = [[0.5 * diffusivity[z, d] for z in range(3)] for d in range(3)]
    shape = (box.long * box.across, box.deep)
    zone_flat, scale_flat, local_flat = zone.reshape(shape), scale.reshape(shape), local.reshape(shape)
    last_col = row_of(box.across, box.across - 1, box.long)
    first_col = row_of(box.across, 0, box.long)

    wide_sides, narrow_sides = Sides("wide", low, high), Sides("narrow", left, right)

    def side(source, place):
        return source(slice(place * box.long, (place + 1) * box.long), slice(None))

    above, below = wide_sides.high, wide_sides.low
    faces = [
        (0, zone[box.long - 1], scale[box.long - 1], local[box.long - 1], above(REACH), above(0)),
        (0, zone[0], scale[0], local[0], below(2 * REACH - 1), below(REACH - 1)),
        (
            1,
            zone_flat[last_col, :],
            scale_flat[last_col, :],
            local_flat[last_col, :],
            side(narrow_sides.high, REACH),
            side(narrow_sides.high, 0),
        ),
        (
            1,
            zone_flat[first_col, :],
            scale_flat[first_col, :],
            local_flat[first_col, :],
            side(narrow_sides.low, 2 * REACH - 1),
            side(narrow_sides.low, REACH - 1),
        ),
    ]
    flows = []
    for direction, labels, factor, values, far_labels, far_factor in faces:
        weight = looked_up(labels, half[direction]) * factor
        weight = weight + looked_up(far_labels, half[direction]) * far_factor
        flows.append(jnp.sum(weight * values, keepdims=True))
    long_pos, across_pos, long_count, across_count = position()
    numbers = [
        (IMAGE_SUM, jnp.sum(image[...], keepdims=True) + sum(flows)),
        (FLOW_LONG_HIGH, flows[0] * as_float(long_pos < long_count - 1)),
        (FLOW_LONG_LOW, flows[1] * as_float(long_pos > 0)),
        (FLOW_ACROSS_HIGH, flows[2] * as_float(across_pos < across_count - 1)),
        (FLOW_ACROSS_LOW, flows[3] * as_float(across_pos > 0)),
    ]
    known = table[...] + at_own_row(line_of(numbers, (8, out.shape[1])), out.shape)
    out[...] = known
    edge = REACH * box.across
    even = is_even("wide")
    for target, pair in ((up, (box.long - REACH, 0)), (down, (0, box.long - REACH))):
        target[:edge] = local[pl.ds(jnp.where(even, *pair), REACH)].reshape(edge, box.deep)
        target[edge:] = known


def column(values, index):
    return values[:, index : index + 1]


def coarse_inverse(numbers, work):
    count, width = work.shape
    across = lax.axis_size("narrow")
    beyond = pltpu.roll(numbers, count - across, 0)
    beside = pltpu.roll(numbers, count - 1, 0)
    before = pltpu.roll(numbers, across, 0)
    ahead = pltpu.roll(numbers, 1, 0)
    place = lax.broadcasted_iota(jnp.int32, (count, 1), 0)
    across_pos = lax.rem(place, across)
    nothing = jnp.zeros((count, 1), jnp.float32)
    couplings = []
    diagonal = column(numbers, BOX_DIAGONAL)
    for own, other, there, inside in (
        (LONG_HIGH, LONG_LOW, beyond, place < count - across),
        (LONG_LOW, LONG_HIGH, before, place >= across),
        (ACROSS_HIGH, ACROSS_LOW, beside, across_pos < across - 1),
        (ACROSS_LOW, ACROSS_HIGH, ahead, across_pos > 0),
    ):
        shared = jnp.where(inside, column(there, other), nothing)
        diagonal = diagonal + column(numbers, own) + shared
        couplings.append(jnp.where(inside, column(numbers, own) + shared, nothing))
    rows = lax.broadcasted_iota(jnp.int32, (count, width), 0)
    cols = lax.broadcasted_iota(jnp.int32, (count, width), 1)
    blank = jnp.zeros((count, width), jnp.float32)
    matrix = jnp.where(cols == rows, diagonal, blank)
    for shift, coupling in zip((across, -across, 1, -1), couplings):
        matrix = matrix - jnp.where((cols == rows + shift) & (cols < count), coupling, blank)
    matrix = jnp.where(cols == rows + count, jnp.ones((count, 1), jnp.float32), matrix)
    if count <= 16:
        for step in range(count):
            pivot_row = matrix[step : step + 1, :] / matrix[step : step + 1, step : step + 1]
            rest = matrix - matrix[:, step : step + 1] * pivot_row
            matrix = jnp.where(rows == step, pivot_row, rest)
        return pltpu.roll(matrix, width - count, 1)
    work[...] = matrix

    def eliminate(step, _):
        values = work[...]
        pivot_row = work[pl.ds(step, 1), :]
        at_step = cols == step
        factors = jnp.sum(jnp.where(at_step, values, blank), axis=1, keepdims=True)
        pivot = jnp.sum(jnp.where(at_step[:1], pivot_row, blank[:1]), axis=1, keepdims=True)
        pivot_row = pivot_row / pivot
        work[...] = jnp.where(rows == step, pivot_row, values - factors * pivot_row)
        return 0

    lax.fori_loop(0, count, eliminate, 0)
    values = work[...]
    if count % 128:
        return pltpu.roll(values, width - count, 1)
    return values[:, count : 2 * count]


def answer(inverse, sums):
    return jnp.sum(inverse * sums, axis=0, keepdims=True)


def at_box(values, row_side, col_side):
    long_pos, across_pos, long_count, across_count = position()
    there_long, there_across = long_pos + row_side, across_pos + col_side
    inside = (
        (there_long >= 0)
        & (there_long < long_count)
        & (there_across >= 0)
        & (there_across < across_count)
    )
    lanes = lax.broadcasted_iota(jnp.int32, values.shape, 1)
    wanted = (lanes == there_long * across_count + there_across) & inside
    return jnp.sum(jnp.where(wanted, values, jnp.zeros_like(values)), axis=1, keepdims=True)


def coarse_corrections(parts, *refs):
    table_parts, (out, work) = refs[:parts], refs[parts:]
    count = work.shape[0]
    numbers = last_rows_merged(table_parts, count)
    across_count = lax.axis_size("narrow")
    inverse = coarse_inverse(numbers, work)
    sums = column(numbers, IMAGE_SUM)
    sums = sums - column(pltpu.roll(numbers, count - across_count, 0), FLOW_LONG_LOW)
    sums = sums - column(pltpu.roll(numbers, across_count, 0), FLOW_LONG_HIGH)
    sums = sums - column(pltpu.roll(numbers, count - 1, 0), FLOW_ACROSS_LOW)
    sums = sums - column(pltpu.roll(numbers, 1, 0), FLOW_ACROSS_HIGH)
    load_sums = column(numbers, LOAD_SUM)
    sums = load_sums * (1.0 - 1.0 / cheb_center) - sums
    out[0:1, :] = answer(inverse, load_sums) * (1.0 / cheb_center)
    out[1:2, :] = answer(inverse, sums) * gain


def second_solve(box, local, low, high, left, right, means, answers, *rest):
    to_long, to_across, to_deep, mass, load_window = rest[:5]
    tables = rest[5 : 5 + N_TABLES]
    iterate, top, bottom, last_col, first_col, out = rest[5 + N_TABLES : 11 + N_TABLES]
    window, spectral, middle, sems = rest[11 + N_TABLES :]
    long_pos, across_pos, long_count, across_count = position()
    coarse = answers[0:1, :]
    own_shift = at_box(answers[1:2, :], 0, 0)
    shifts = {
        (row_side, col_side): at_box(coarse, row_side, col_side)
        for row_side in (-1, 0, 1)
        for col_side in (-1, 0, 1)
    }

    def add(values, row_side, col_side):
        shift = shifts[row_side, col_side]
        if values.ndim == 3:
            shift = shift.reshape(1, 1, 1)
        return values + shift

    edge = REACH * box.across
    low, high = (
        ref.at[:edge].reshape(REACH, box.across, box.deep) for ref in (low, high)
    )
    wide_sides, narrow_sides = Sides("wide", low, high), Sides("narrow", left, right)
    fill_window(box, window, local, wide_sides, narrow_sides, REACH, 0, REACH, add)
    weights = (to_long, to_across, to_deep, mass)

    start, stop = EDGE - MARGIN, EDGE + box.across + MARGIN

    flow = [to_long[0, start:stop] * (window[1, start:stop] - window[0, start:stop])]

    def residual(start_row):
        rows = []
        for row in range(start_row + 1, start_row + 9):
            image, flow[0] = negative_image(window, row, row, start, stop, flow[0], weights)
            rows.append((load_window[row, start:stop] + image)[None])
        return jnp.concatenate(rows, axis=0)

    inner = slice(EDGE, EDGE + box.across)
    first = REACH
    row_ids = lax.broadcasted_iota(jnp.int32, (1, padded(box.ex)), 1)
    col_ids = lax.broadcasted_iota(jnp.int32, (1, padded(box.ey)), 1)
    row_mask = jnp.where(row_ids < MARGIN, as_float(long_pos > 0), 1.0)
    row_mask = jnp.where(row_ids >= MARGIN + box.long, as_float(long_pos < long_count - 1), row_mask)
    col_mask = jnp.where(col_ids < MARGIN, as_float(across_pos > 0), 1.0)
    col_mask = jnp.where(
        col_ids >= MARGIN + box.across, as_float(across_pos < across_count - 1), col_mask
    )
    keep = 1.0 + rho_second * rho_first
    copies = []

    def emit(start, values):
        rows = values.reshape(8, box.across, box.deep)
        before = window[first + start : first + start + 8, inner, :]
        shift = own_shift.reshape(1, 1, 1)
        iterate[start : start + 8] = keep * before + (gain * rows + shift)
        copies.append(
            pltpu.make_async_copy(
                iterate.at[start : start + 8], out.at[start : start + 8], sems.at[len(copies)]
            )
        )
        copies[-1].start()

    box_solve(
        box, residual, means_of(means), tables, row_mask, col_mask, spectral, middle, emit
    )
    rows = in_order(is_even("wide"), iterate[box.long - 1], iterate[0])
    top[...], bottom[...] = rows
    flat = iterate.reshape(box.long * box.across, box.deep)
    cols = [flat[row_of(box.across, col, box.long), :] for col in (box.across - 1, 0)]
    last_col[...], first_col[...] = in_order(is_even("narrow"), *cols)
    for copy in copies:
        copy.wait()


def last_residual(
    box,
    load,
    partial,
    low,
    high,
    left,
    right,
    to_long,
    to_across,
    to_deep,
    mass,
    out,
    window,
    result,
    sems,
):
    inner = slice(EDGE, EDGE + box.across)
    flat = window.reshape((box.long + 2) * box.cols, box.deep)
    blank = jnp.zeros((box.long + 2, EDGE, box.deep), jnp.float32)
    window[:, :EDGE, :] = blank
    window[:, EDGE + box.across :, :] = blank
    window[1 : 1 + box.long, inner, :] = partial[...]
    wide_sides, narrow_sides = Sides("wide", low, high), Sides("narrow", left, right)
    window[0, inner, :] = wide_sides.low(Ellipsis)
    window[1 + box.long, inner, :] = wide_sides.high(Ellipsis)
    flat[row_of(box.cols, EDGE - 1, box.long, 1), :] = narrow_sides.low(Ellipsis)
    flat[row_of(box.cols, EDGE + box.across, box.long, 1), :] = narrow_sides.high(Ellipsis)
    weights = (to_long, to_across, to_deep, mass)

    def one_row(row, flow):
        image, flow = negative_image(
            window, row + 1, REACH + row, inner.start, inner.stop, flow, weights
        )
        result[row] = load[row] + image
        return flow

    flow = to_long[REACH - 1, inner] * (window[1, inner] - window[0, inner])
    chunk = box.long // 4
    copies = []
    for index in range(4):
        rows = slice(index * chunk, (index + 1) * chunk)
        flow = lax.fori_loop(rows.start, rows.stop, one_row, flow, unroll=4)
        copy = pltpu.make_async_copy(result.at[rows], out.at[rows], sems.at[index])
        copy.start()
        copies.append(copy)
    for copy in copies:
        copy.wait()


def swaps(axis, around):
    sizes = (lax.axis_size("wide"), lax.axis_size("narrow"))
    along = ("wide", "narrow").index(axis)
    size, beside = sizes[along], sizes[1 - along]

    def number(place, other_place):
        pair = (place, other_place) if along == 0 else (other_place, place)
        return pair[0] * sizes[1] + pair[1]

    ways = []
    for way in range(2):
        pairs = []
        for place in range(size):
            for other_place in range(beside):
                partner = place + 1 if place % 2 == way else place - 1
                there = other_place
                if around and size % 2 == 0:
                    partner %= size
                if not 0 <= partner < size:
                    partner = place
                    there = other_place ^ 1 if beside % 2 == 0 else other_place
                pairs.append((number(place, other_place), number(partner, there)))
        ways.append(pairs)
    return ways


def exchange(axis, first, second, around=False):
    ways = swaps(axis, around)
    axes = ("wide", "narrow")
    return lax.ppermute(first, axes, ways[0]), lax.ppermute(second, axes, ways[1])


def two_away(axis, table):
    size = lax.axis_size(axis)
    return lax.ppermute(table, axis, [(i, (i + 2) % size) for i in range(size)])


def tell(table):
    count = table.shape[0]
    long_pos, across_pos, _, across_count = position()
    own = lax.dynamic_slice_in_dim(table, long_pos * across_count + across_pos, 1, axis=0)
    line = jnp.broadcast_to(own, (count, 1, 128))
    told = lax.all_to_all(line, ("wide", "narrow"), split_axis=0, concat_axis=0, tiled=True)
    return told.reshape(count, 128)


def on_device(zone, scale, diffusivity, decay, load):
    box = Box(load.shape)
    long, across, deep = load.shape
    count = lax.axis_size("wide") * lax.axis_size("narrow")
    by_margins = lax.axis_size("wide") == 4 and lax.axis_size("narrow") == 4
    tables = tables_of(box)
    cells = f32(long, across, deep)
    whole_zone = jax.ShapeDtypeStruct(cells.shape, zone.dtype)
    window = f32(box.rows, box.cols, deep)
    table_shape = f32(count, 128)
    anywhere = pl.BlockSpec(memory_space=pl.ANY)
    in_hbm = pl.BlockSpec(memory_space=pltpu.HBM)

    def scratch(shape):
        return pltpu.VMEM(shape, jnp.float32)

    def pinned(field):
        return pltpu.with_memory_space_constraint(field, pltpu.HBM)

    spectral = scratch((box.ey, padded(box.ex), deep))
    middle = scratch((long, padded(box.ey), deep))

    def pack(wide, fields, sides, parts=(), after=()):
        rows = message_rows(box, wide * len(fields)) + (count if parts else 0)
        message = f32(rows, deep)
        body = functools.partial(pack_fields, box, wide, len(fields), len(parts), len(after))
        return call(
            body,
            (message, message) + ((table_shape,) if parts else ()),
            [VMEM] * (len(fields) + 2 + len(parts)) + [anywhere] * len(after),
        )(*fields, *sides, *parts, *after)

    far = f32(2 * REACH, across, deep)
    far_zone, far_scale = zone, scale
    load, load_first, load_second, first, second = call(
        functools.partial(bring_edges, box),
        (cells,) + (f32(MARGIN, across, deep),) * 2 + (far, far),
        [in_hbm] * 3,
        [pltpu.VMEM((2, REACH, across, deep), zone.dtype), pltpu.SemaphoreType.DMA((7,))],
    )(pinned(zone), pinned(scale), pinned(load))
    load_wide = exchange("wide", load_first, load_second)
    far_wide = exchange("wide", first, second)
    load_first, load_second = pack(MARGIN, [load], load_wide)
    load_narrow = exchange("narrow", load_first, load_second)
    zone, scale, sums, table = call(
        functools.partial(box_sums, box),
        (whole_zone, cells, f32(8, 128), table_shape),
        [in_hbm] * 2 + [VMEM, anywhere] + [SMEM] * 2,
        [pltpu.SemaphoreType.DMA((4,))],
    )(pinned(far_zone), pinned(far_scale), load, load_first, diffusivity, decay)
    far_narrow = exchange("narrow", *pack(REACH, [scale, zone], far_wide))
    load_window, local, image = call(
        functools.partial(first_solve, box),
        (window, cells, f32(across, deep)),
        [VMEM] * 8 + [SMEM] * 2 + [VMEM] * N_TABLES,
        [spectral, middle],
        flops=4 * 10**9,
    )(load, *load_wide, *load_narrow, sums, zone, scale, diffusivity, decay, *tables)
    message = f32(REACH * across + count, deep)
    table, first, second = call(
        functools.partial(image_sums, box), (table_shape, message, message), [VMEM] * 9 + [SMEM]
    )(zone, scale, local, image, *far_wide, *far_narrow, table, diffusivity)
    own_table = table
    wide = exchange("wide", first, second, by_margins)
    parts = (table, *wide)
    if by_margins:
        parts += (two_away("wide", table),)
    weights = call(
        functools.partial(weights_of, box),
        (window,) * 4,
        [VMEM] * 6 + [SMEM] * 2,
        [scratch(window.shape)] * 2,
        flops=10**9,
    )(zone, scale, *far_wide, *far_narrow, diffusivity, decay)
    first, second, table = pack(REACH, [local], wide, parts, weights[3:])
    narrow = exchange("narrow", first, second)
    if by_margins:
        table = call(join_rows, table_shape, [VMEM] * 2)(table, narrow[0])
        parts = (table, two_away("narrow", table))
    else:
        parts = (tell(own_table),)
    row, col = f32(across, deep), f32(long, deep)
    answers = call(
        functools.partial(coarse_corrections, len(parts)),
        f32(8, -(-count // 128) * 128),
        [VMEM] * len(parts),
        [scratch((count, -(-2 * count // 128) * 128))],
    )(*parts)
    iterate, first_row, second_row, first_col, second_col, result = call(
        functools.partial(second_solve, box),
        (cells, row, row, col, col, cells),
        [VMEM] * (12 + N_TABLES),
        [scratch(window.shape), spectral, middle, pltpu.SemaphoreType.DMA((long // 8,))],
        flops=4 * 10**9,
        out_spec=(VMEM,) * 5 + (anywhere,),
    )(local, *wide, *narrow, sums, answers, *weights, load_window, *tables)
    narrow = exchange("narrow", first_col, second_col)
    wide = exchange("wide", first_row, second_row)
    residual = call(
        functools.partial(last_residual, box),
        cells,
        [VMEM] * 10,
        [scratch((long + 2, box.cols, deep)), scratch(cells.shape), pltpu.SemaphoreType.DMA((4,))],
        out_spec=anywhere,
    )(load, iterate, *wide, *narrow, *weights)
    return result, residual


def solution(mesh):
    split = P(("groups", "wide"), "narrow", None)
    return jax.shard_map(
        on_device,
        mesh=mesh,
        in_specs=(split, split, P(), P(), split),
        out_specs=(split, split),
        check_vma=False,
    )
```

```python
import functools

import jax
import jax.numpy as jnp
import ml_dtypes
import numpy as np
from jax import lax
from jax.experimental import pallas as pl
from jax.experimental.pallas import tpu as pltpu
from jax.sharding import PartitionSpec as P

MARGIN = 4
REACH = MARGIN + 1
EDGE = 8

cheb_center = 1.3
cheb_radius = 1.2
cheb_ratio = 1.3 / 1.2
rho_first = 1.0 / cheb_ratio
rho_second = 1.0 / (2.0 * cheb_ratio - rho_first)
gain = 2.0 * rho_second / cheb_radius

MEANS = range(4)
BOX_DIAGONAL, LONG_HIGH, LONG_LOW, ACROSS_HIGH, ACROSS_LOW, LOAD_SUM = range(4, 10)
IMAGE_SUM, FLOW_LONG_HIGH, FLOW_LONG_LOW, FLOW_ACROSS_HIGH, FLOW_ACROSS_LOW = range(16, 21)

VMEM = pl.BlockSpec(memory_space=pltpu.VMEM)
SMEM = pl.BlockSpec(memory_space=pltpu.SMEM)


def sine_basis(length):
    indices = np.arange(1, length + 1)
    phases = indices[:, None] * indices[None, :] % (2 * (length + 1))
    table = np.sqrt(2.0 / (length + 1)) * np.sin(np.pi * phases / (length + 1))
    eigvals = 4.0 * np.sin(np.pi * indices / (2.0 * (length + 1))) ** 2
    return table.astype(np.float32), eigvals.astype(np.float32)


def call(body, out_shape, in_specs, scratch=(), flops=0, out_spec=None, aliases=None):
    return pl.pallas_call(
        body,
        out_shape=out_shape,
        in_specs=in_specs,
        out_specs=out_spec or jax.tree.map(lambda _: VMEM, out_shape),
        scratch_shapes=list(scratch),
        compiler_params=pltpu.CompilerParams(vmem_limit_bytes=30 * 2**20),
        cost_estimate=pl.CostEstimate(flops=flops, bytes_accessed=0, transcendentals=0),
        input_output_aliases=aliases or {},
    )


def f32(*shape):
    return jax.ShapeDtypeStruct(shape, jnp.float32)


class Box:
    def __init__(self, shape):
        self.long, self.across, self.deep = shape
        self.ex = self.long + 2 * MARGIN
        self.ey = self.across + 2 * MARGIN
        self.rows = self.long + 2 * REACH
        self.cols = self.across + 2 * EDGE
        self.flat = self.rows * self.cols


def pieces(values, count):
    parts = []
    for _ in range(count):
        part = values.astype(jnp.bfloat16)
        parts.append(part)
        values = values - part.astype(jnp.float32)
    return parts


def left_table(table, depth, count):
    rows, cols = table.shape
    wide = np.zeros((rows, depth), np.float32)
    wide[:, :cols] = table
    parts = []
    rest = wide
    for _ in range(count):
        part = rest.astype(ml_dtypes.bfloat16)
        parts.append(part)
        rest = rest - part.astype(np.float32)
    blank = np.zeros_like(parts[0])
    lines = []
    for index in range(count):
        used = count - index if count > 2 else count
        lines.append(np.concatenate([parts[index]] * used + [blank] * (count - used), axis=1))
    return np.concatenate(lines, axis=0)


def right_tables(table):
    rest, parts = table, []
    for _ in range(3):
        part = rest.astype(ml_dtypes.bfloat16)
        parts.append(part)
        rest = rest - part.astype(np.float32)
    both = np.concatenate([parts[0], parts[1]], axis=1)
    return np.concatenate([both, both], axis=0), np.concatenate([parts[2], parts[0]], axis=0)


def padded(size):
    return -(-size // 16) * 16


FORWARD, BACKWARD = 2, 3


def tables_of(box):
    sine_x, eig_x = sine_basis(box.ex)
    sine_y, eig_y = sine_basis(box.ey)
    sine_z, eig_z = sine_basis(box.deep)
    from_y = sine_y[MARGIN : MARGIN + box.across]
    from_x = sine_x[MARGIN : MARGIN + box.long]
    spread = np.broadcast_to(eig_x[:, None], (box.ex, box.deep))
    main_z, rest_z = right_tables(sine_z)
    return [
        jnp.asarray(np.ascontiguousarray(t))
        for t in (
            left_table(sine_y, padded(box.ey), FORWARD),
            left_table(sine_x, padded(box.ex), FORWARD),
            left_table(from_x, padded(box.ex), BACKWARD),
            left_table(from_y, padded(box.ey), BACKWARD),
            main_z,
            rest_z,
            spread,
            eig_z[None, :],
            eig_y[None, :],
        )
    ]


N_TABLES = 9


def bf16_dot(left, right):
    return lax.dot_general(
        left, right, (((1,), (0,)), ((), ())), preferred_element_type=jnp.float32
    )


def dot_left(table, values, count, rows):
    total = bf16_dot(table, jnp.concatenate(pieces(values, count), axis=0))
    return sum(total[index * rows : (index + 1) * rows] for index in range(1, count)) + total[:rows]


def dot_right(values, main, rest, count):
    deep = values.shape[1]
    parts = pieces(values, count)
    total = bf16_dot(jnp.concatenate(parts[:2], axis=1), main)
    result = total[:, :deep] + total[:, deep:]
    if count == 3:
        result = result + bf16_dot(jnp.concatenate([parts[0], parts[2]], axis=1), rest)
    return result


def with_rows(values, rows):
    if values.shape[0] == rows:
        return values
    blank = jnp.zeros((rows - values.shape[0],) + values.shape[1:], values.dtype)
    return jnp.concatenate([values, blank], axis=0)


def box_solve(box, source, divided, tables, row_mask, col_mask, spectral, middle, emit):
    into_y, into_x, from_x, from_y, main_z, rest_z = tables[:6]
    deep = box.deep
    deep_x, deep_y = padded(box.ex), padded(box.ey)
    into_y, into_x = into_y[...], into_x[...]
    if col_mask is not None:
        mask = jnp.concatenate([col_mask] * FORWARD, axis=1)
        into_y = (into_y.astype(jnp.float32) * mask).astype(jnp.bfloat16)
        mask = jnp.concatenate([row_mask] * FORWARD, axis=1)
        into_x = (into_x.astype(jnp.float32) * mask).astype(jnp.bfloat16)
    from_x, from_y, main_z, rest_z = from_x[...], from_y[...], main_z[...], rest_z[...]
    spectral_flat = spectral.reshape(box.ey * deep_x, deep)
    middle_flat = middle.reshape(box.long * deep_y, deep)
    if deep_x > box.ex:
        spectral[:, box.ex :, :] = jnp.zeros((box.ey, deep_x - box.ex, deep), jnp.float32)
    if deep_y > box.ey:
        middle[:, box.ey :, :] = jnp.zeros((box.long, deep_y - box.ey, deep), jnp.float32)
    for start in range(0, box.ex, 8):
        block = source(start).reshape(8 * box.ey, deep)
        block = dot_right(block, main_z, rest_z, FORWARD).reshape(8, box.ey, deep)
        for row in range(0, 8, 2):
            pair = jnp.concatenate([block[row], block[row + 1]], axis=1)
            pair = dot_left(into_y, with_rows(pair, deep_y), FORWARD, box.ey)
            for part in range(2):
                spectral_flat[pl.ds(start + row + part, box.ey, stride=deep_x), :] = pair[
                    :, part * deep : (part + 1) * deep
                ]
    for col in range(0, box.ey, 2):
        pair = jnp.concatenate([spectral[col], spectral[col + 1]], axis=1)
        pair = dot_left(into_x, pair, FORWARD, box.ex)
        pair = jnp.concatenate(
            [
                divided(pair[:, part * deep : (part + 1) * deep], col + part)
                for part in range(2)
            ],
            axis=1,
        )
        pair = dot_left(from_x, with_rows(pair, deep_x), BACKWARD, box.long)
        for part in range(2):
            middle_flat[pl.ds(col + part, box.long, stride=deep_y), :] = pair[
                :, part * deep : (part + 1) * deep
            ]
    for start in range(0, box.long, 8):
        parts = []
        for row in range(start, start + 8, 2):
            pair = jnp.concatenate([middle[row], middle[row + 1]], axis=1)
            pair = dot_left(from_y, pair, BACKWARD, box.across)
            parts += [pair[:, :deep], pair[:, deep:]]
        emit(start, dot_right(jnp.concatenate(parts, axis=0), main_z, rest_z, BACKWARD))


def position():
    long_pos, across_pos = lax.axis_index("wide"), lax.axis_index("narrow")
    return long_pos, across_pos, lax.axis_size("wide"), lax.axis_size("narrow")


def as_float(flag):
    return jnp.where(flag, jnp.float32(1.0), jnp.float32(0.0))


def is_even(axis):
    return lax.rem(lax.axis_index(axis), 2) == 0


class Sides:
    def __init__(self, axis, first, second):
        position = lax.axis_index(axis)
        self.even = is_even(axis)
        self.has_low = as_float(position > 0)
        self.has_high = as_float(position < lax.axis_size(axis) - 1)
        self.first, self.second = first, second

    def low(self, *index):
        return jnp.where(self.even, self.second[index], self.first[index]) * self.has_low

    def high(self, *index):
        return jnp.where(self.even, self.first[index], self.second[index]) * self.has_high


def in_order(even, up, down):
    return jnp.where(even, up, down), jnp.where(even, down, up)


def row_of(stride, col, count, first=0):
    return pl.ds(first * stride + col, count, stride=stride)


def pack_columns(box, fields, wide_sides, wide, first, second):
    corner = len(fields) * wide * box.long
    even = is_even("narrow")
    place = 0
    for field, sides in zip(fields, wide_sides):
        for step in range(wide):
            cols = (box.across - wide + step, step)
            values = [field[row_of(box.across, col, box.long), :] for col in cols]
            low = [sides.low(row_of(box.across, col, wide), slice(None)) for col in cols]
            high = [sides.high(row_of(box.across, col, wide), slice(None)) for col in cols]
            at = corner + 2 * REACH * place
            for start, parts in ((place * box.long, values), (at, low), (at + REACH, high)):
                parts = in_order(even, *(part.astype(jnp.float32) for part in parts))
                size = parts[0].shape[0]
                first[start : start + size, :], second[start : start + size, :] = parts
            place += 1


def message_rows(box, count):
    return -(-(count * (box.long + 2 * REACH)) // 8) * 8


def pack_fields(box, wide, fields, tables, after, *refs):
    own, (low, high), refs = refs[:fields], refs[fields : fields + 2], refs[fields + 2 :]
    parts, (first, second, *table) = refs[:tables], refs[tables + after :]
    size = wide * box.across
    flat = [field.reshape(box.long * box.across, box.deep) for field in own]
    low = low.reshape(low.size // box.deep, box.deep)
    high = high.reshape(high.size // box.deep, box.deep)
    sides = [
        Sides("wide", *(ref.at[index * size : (index + 1) * size] for ref in (low, high)))
        for index in range(fields)
    ]
    pack_columns(box, flat, sides, wide, first, second)
    if tables:
        known = last_rows_merged(parts, table[0].shape[0])
        table[0][...] = known
        first[first.shape[0] - known.shape[0] :, :] = known
        second[second.shape[0] - known.shape[0] :, :] = known


def bring_edges(
    box, zone, scale, load, own_load, load_first, load_second, first, second, staged, sems
):
    even = is_even("wide")

    def edges(wide):
        up, down = box.long - wide, 0
        return [pl.ds(jnp.where(even, *pair), wide) for pair in ((up, down), (down, up))]

    copies = [
        (load.at[edges(MARGIN)[0]], load_first),
        (load.at[edges(MARGIN)[1]], load_second),
        (zone.at[edges(REACH)[0]], staged.at[0]),
        (zone.at[edges(REACH)[1]], staged.at[1]),
        (scale.at[edges(REACH)[0]], first.at[:REACH]),
        (scale.at[edges(REACH)[1]], second.at[:REACH]),
        (load, own_load),
    ]
    copies = [
        pltpu.make_async_copy(source, target, sems.at[index])
        for index, (source, target) in enumerate(copies)
    ]
    for copy in copies:
        copy.start()
    for copy in copies[:4]:
        copy.wait()
    first[REACH:] = staged[0].astype(jnp.float32)
    second[REACH:] = staged[1].astype(jnp.float32)
    for copy in copies[4:]:
        copy.wait()


def fill_window(box, window, own, wide_sides, narrow_sides, wide, place, total, add=None):
    flat = window.reshape(box.flat, box.deep)
    nothing = jnp.zeros((box.rows, EDGE, box.deep), jnp.float32)
    window[:, :EDGE, :] = nothing
    window[:, EDGE + box.across :, :] = nothing
    if add is None:
        add = lambda values, row_side, col_side: values
    inner = slice(EDGE, EDGE + box.across)
    first, last = REACH, REACH + box.long
    if wide < REACH:
        blank = jnp.zeros((1, box.across, box.deep), jnp.float32)
        window[0:1, inner, :] = blank
        window[box.rows - 1 :, inner, :] = blank
    window[first:last, inner, :] = add(own[...].astype(jnp.float32), 0, 0)
    window[first - wide : first, inner, :] = add(wide_sides.low(Ellipsis), -1, 0)
    window[last : last + wide, inner, :] = add(wide_sides.high(Ellipsis), 1, 0)
    corner = total * box.long
    for step in range(wide):
        for source, col, side in (
            (narrow_sides.low, EDGE - wide + step, -1),
            (narrow_sides.high, EDGE + box.across + step, 1),
        ):
            for start, size, row, row_side in (
                ((place + step) * box.long, box.long, first, 0),
                (corner + 2 * REACH * (place + step), wide, first - wide, -1),
                (corner + 2 * REACH * (place + step) + REACH, wide, last, 1),
            ):
                values = source(slice(start, start + size), slice(None))
                flat[row_of(box.cols, col, size, row), :] = add(values, row_side, side)


def negative_image(window, row, at, first, last, flow_before, weights):
    to_long, to_across, to_deep, mass = weights
    x = window[row, first:last]
    flow_long = to_long[at, first:last] * (window[row + 1, first:last] - x)
    flow_across = to_across[at, first:last] * (window[row, first + 1 : last + 1] - x)
    flow_from = to_across[at, first - 1 : last - 1] * (x - window[row, first - 1 : last - 1])
    lanes = x.shape[1]
    flow_deep = to_deep[at, first:last] * (pltpu.roll(x, lanes - 1, 1) - x)
    total = flow_long - flow_before - mass[at, first:last] * x
    total = total + (flow_across - flow_from)
    total = total + (flow_deep - pltpu.roll(flow_deep, 1, 1))
    return total, flow_long


def looked_up(labels, values):
    return jnp.where(labels == 0, values[0], jnp.where(labels == 1, values[1], values[2]))


def at_own_row(line, shape):
    long_pos, across_pos, _, across_count = position()
    rows = lax.broadcasted_iota(jnp.int32, shape, 0)
    own = rows == long_pos * across_count + across_pos
    return jnp.where(own, line[:1], jnp.zeros(shape, jnp.float32))


def merged(table, *others):
    for other in others:
        table = jnp.where(table != 0.0, table, other)
    return table


def last_rows_merged(refs, count):
    return merged(*(ref[ref.shape[0] - count :, :] for ref in refs))


def join_rows(table, message, out):
    out[...] = last_rows_merged((table, message), out.shape[0])


def line_of(numbers, shape):
    lanes = lax.broadcasted_iota(jnp.int32, shape, 1)
    line = jnp.zeros(shape, jnp.float32)
    for index, number in numbers:
        line = jnp.where(lanes == index, number, line)
    return line


def box_sums(
    box, far_zone, far_scale, load, after, diffusivity, decay, zone, scale, out, table, sems
):
    del after
    size = 8
    parts = box.long // size
    copies = []
    for part in range(parts):
        rows = slice(part * size, (part + 1) * size)
        for index, (source, target) in enumerate(((far_zone, zone), (far_scale, scale))):
            copy = pltpu.make_async_copy(
                source.at[rows], target.at[rows], sems.at[2 * part + index]
            )
            copy.start()
            copies.append(copy)
    nothing = jnp.zeros((box.across, box.deep), jnp.float32)
    half = [[0.5 * diffusivity[z, d] for z in range(3)] for d in range(3)]
    rates = [decay[z] for z in range(3)]

    def halves(row):
        labels, factor = zone[row], scale[row]
        return [looked_up(labels, half[d]) * factor for d in range(3)] + [looked_up(labels, rates)]

    sums = [nothing] * 5
    for part in range(parts):
        for copy in copies[2 * part : 2 * part + 2]:
            copy.wait()
        for row in range(part * size, (part + 1) * size):
            sums = [total + more for total, more in zip(sums, halves(row) + [load[row]])]

    def total(values):
        return jnp.sum(values, keepdims=True).reshape(1, 1)

    cells = box.long * box.across * box.deep
    numbers = [(index, total(sums[index]) * (2.0 / cells)) for index in range(3)]
    mass = total(sums[3])
    numbers += [(3, mass / cells)]
    ends = total(sums[2][:, :1]) + total(sums[2][:, box.deep - 1 :])
    numbers += [
        (BOX_DIAGONAL, mass + ends),
        (LONG_HIGH, total(halves(box.long - 1)[0])),
        (LONG_LOW, total(halves(0)[0])),
        (ACROSS_HIGH, total(sums[1][box.across - 1 :])),
        (ACROSS_LOW, total(sums[1][:1])),
        (LOAD_SUM, total(sums[4])),
    ]
    line = line_of(numbers, out.shape)
    out[...] = line
    table[...] = at_own_row(line, table.shape)


def means_of(ref):
    return [ref[0:1, index : index + 1] for index in range(4)]


def first_solve(box, load, low, high, left, right, means, zone, scale, diffusivity, decay, *rest):
    tables = rest[:N_TABLES]
    window, local, image, inverses, spectral, middle = rest[N_TABLES:]
    spread, eig_z, eig_y = tables[6:]
    means = means_of(means)
    base = means[3] + means[0] * spread[...] + means[2] * eig_z[...]

    def divided(values, col):
        inverse = 1.0 / (base + means[1] * eig_y[0, col])
        inverses[col] = inverse
        return values * inverse

    half = [0.5 * diffusivity[z, 2] for z in range(3)]
    rates = [decay[z] for z in range(3)]
    lane = lax.broadcasted_iota(jnp.int32, (box.across, box.deep), 1)
    ends = jnp.where((lane == 0) | (lane == box.deep - 1), jnp.float32(1.0), jnp.float32(0.0))
    image[...] = jnp.zeros((box.across, box.deep), jnp.float32)
    wide_sides, narrow_sides = Sides("wide", low, high), Sides("narrow", left, right)
    fill_window(box, window, load, wide_sides, narrow_sides, MARGIN, 0, MARGIN)

    def emit(start, values):
        values = values * (1.0 / cheb_center)
        values = values.reshape(8, box.across, box.deep)
        local[start : start + 8] = values
        total = image[...]
        for row in range(8):
            labels = zone[start + row]
            mass = looked_up(labels, rates) + looked_up(labels, half) * scale[start + row] * ends
            total = total + mass * values[row]
        image[...] = total

    box_solve(
        box,
        lambda row: window[1 + row : 9 + row, EDGE - MARGIN : EDGE + box.across + MARGIN],
        divided,
        tables,
        None,
        None,
        spectral,
        middle,
        emit,
    )


def side_weights(
    box, zone, scale, low, high, left, right, diffusivity, to_long, to_across, zone_window,
    scale_window
):
    for index, (window, own) in enumerate(((scale_window, scale), (zone_window, zone))):
        start = index * REACH
        wide_sides = Sides("wide", *(ref.at[start : start + REACH] for ref in (low, high)))
        narrow_sides = Sides("narrow", left, right)
        fill_window(box, window, own, wide_sides, narrow_sides, REACH, start, 2 * REACH)
    half = [[0.5 * diffusivity[z, d] for z in range(3)] for d in range(2)]

    def one_row(row, before):
        labels, factor = zone_window[row], scale_window[row]
        now = [looked_up(labels, half[d]) * factor for d in range(2)]
        to_across[row] = now[1] + pltpu.roll(now[1], box.cols - 1, 0)
        to_long[jnp.maximum(row - 1, 0)] = before + now[0]
        return now[0]

    def some_rows(index, before):
        for row in range(8):
            before = one_row(index * 8 + row, before)
        return before

    before = jnp.zeros((box.cols, box.deep), jnp.float32)
    before = lax.fori_loop(0, box.rows // 8, some_rows, before)
    for row in range(box.rows // 8 * 8, box.rows):
        before = one_row(row, before)
    to_long[box.rows - 1] = before


def deep_weights(box, zone_window, scale_window, diffusivity, decay, to_deep, mass):
    half = [0.5 * diffusivity[z, 2] for z in range(3)]
    rates = [decay[z] for z in range(3)]
    lane = lax.broadcasted_iota(jnp.int32, (box.cols, box.deep), 1)
    ends = jnp.where((lane == 0) | (lane == box.deep - 1), jnp.float32(1.0), jnp.float32(0.0))
    not_last = jnp.where(lane == box.deep - 1, jnp.float32(0.0), jnp.float32(1.0))

    def one_row(row):
        labels = zone_window[row]
        now = looked_up(labels, half) * scale_window[row]
        to_deep[row] = (now + pltpu.roll(now, box.deep - 1, 1)) * not_last
        mass[row] = looked_up(labels, rates) + now * ends

    def some_rows(index, _):
        for row in range(8):
            one_row(index * 8 + row)
        return 0

    lax.fori_loop(0, box.rows // 8, some_rows, 0)
    for row in range(box.rows // 8 * 8, box.rows):
        one_row(row)


def image_sums(
    box, zone, scale, local, image, low, high, left, right, table, diffusivity, out, up, down
):
    half = [[0.5 * diffusivity[z, d] for z in range(3)] for d in range(3)]
    shape = (box.long * box.across, box.deep)
    zone_flat, scale_flat, local_flat = zone.reshape(shape), scale.reshape(shape), local.reshape(shape)
    last_col = row_of(box.across, box.across - 1, box.long)
    first_col = row_of(box.across, 0, box.long)

    wide_sides, narrow_sides = Sides("wide", low, high), Sides("narrow", left, right)

    def side(source, place):
        return source(slice(place * box.long, (place + 1) * box.long), slice(None))

    above, below = wide_sides.high, wide_sides.low
    faces = [
        (0, zone[box.long - 1], scale[box.long - 1], local[box.long - 1], above(REACH), above(0)),
        (0, zone[0], scale[0], local[0], below(2 * REACH - 1), below(REACH - 1)),
        (
            1,
            zone_flat[last_col, :],
            scale_flat[last_col, :],
            local_flat[last_col, :],
            side(narrow_sides.high, REACH),
            side(narrow_sides.high, 0),
        ),
        (
            1,
            zone_flat[first_col, :],
            scale_flat[first_col, :],
            local_flat[first_col, :],
            side(narrow_sides.low, 2 * REACH - 1),
            side(narrow_sides.low, REACH - 1),
        ),
    ]
    flows = []
    for direction, labels, factor, values, far_labels, far_factor in faces:
        weight = looked_up(labels, half[direction]) * factor
        weight = weight + looked_up(far_labels, half[direction]) * far_factor
        flows.append(jnp.sum(weight * values, keepdims=True))
    long_pos, across_pos, long_count, across_count = position()
    numbers = [
        (IMAGE_SUM, jnp.sum(image[...], keepdims=True) + sum(flows)),
        (FLOW_LONG_HIGH, flows[0] * as_float(long_pos < long_count - 1)),
        (FLOW_LONG_LOW, flows[1] * as_float(long_pos > 0)),
        (FLOW_ACROSS_HIGH, flows[2] * as_float(across_pos < across_count - 1)),
        (FLOW_ACROSS_LOW, flows[3] * as_float(across_pos > 0)),
    ]
    known = table[...] + at_own_row(line_of(numbers, (8, out.shape[1])), out.shape)
    out[...] = known
    edge = REACH * box.across
    even = is_even("wide")
    for target, pair in ((up, (box.long - REACH, 0)), (down, (0, box.long - REACH))):
        target[:edge] = local[pl.ds(jnp.where(even, *pair), REACH)].reshape(edge, box.deep)
        target[edge:] = known


def column(values, index):
    return values[:, index : index + 1]


def coarse_inverse(numbers, work):
    count, width = work.shape
    across = lax.axis_size("narrow")
    beyond = pltpu.roll(numbers, count - across, 0)
    beside = pltpu.roll(numbers, count - 1, 0)
    before = pltpu.roll(numbers, across, 0)
    ahead = pltpu.roll(numbers, 1, 0)
    place = lax.broadcasted_iota(jnp.int32, (count, 1), 0)
    across_pos = lax.rem(place, across)
    nothing = jnp.zeros((count, 1), jnp.float32)
    couplings = []
    diagonal = column(numbers, BOX_DIAGONAL)
    for own, other, there, inside in (
        (LONG_HIGH, LONG_LOW, beyond, place < count - across),
        (LONG_LOW, LONG_HIGH, before, place >= across),
        (ACROSS_HIGH, ACROSS_LOW, beside, across_pos < across - 1),
        (ACROSS_LOW, ACROSS_HIGH, ahead, across_pos > 0),
    ):
        shared = jnp.where(inside, column(there, other), nothing)
        diagonal = diagonal + column(numbers, own) + shared
        couplings.append(jnp.where(inside, column(numbers, own) + shared, nothing))
    rows = lax.broadcasted_iota(jnp.int32, (count, width), 0)
    cols = lax.broadcasted_iota(jnp.int32, (count, width), 1)
    blank = jnp.zeros((count, width), jnp.float32)
    matrix = jnp.where(cols == rows, diagonal, blank)
    for shift, coupling in zip((across, -across, 1, -1), couplings):
        matrix = matrix - jnp.where((cols == rows + shift) & (cols < count), coupling, blank)
    matrix = jnp.where(cols == rows + count, jnp.ones((count, 1), jnp.float32), matrix)
    if count <= 16:
        for step in range(count):
            pivot_row = matrix[step : step + 1, :] / matrix[step : step + 1, step : step + 1]
            rest = matrix - matrix[:, step : step + 1] * pivot_row
            matrix = jnp.where(rows == step, pivot_row, rest)
        return pltpu.roll(matrix, width - count, 1)
    work[...] = matrix

    def eliminate(step, _):
        values = work[...]
        pivot_row = work[pl.ds(step, 1), :]
        at_step = cols == step
        factors = jnp.sum(jnp.where(at_step, values, blank), axis=1, keepdims=True)
        pivot = jnp.sum(jnp.where(at_step[:1], pivot_row, blank[:1]), axis=1, keepdims=True)
        pivot_row = pivot_row / pivot
        work[...] = jnp.where(rows == step, pivot_row, values - factors * pivot_row)
        return 0

    lax.fori_loop(0, count, eliminate, 0)
    values = work[...]
    if count % 128:
        return pltpu.roll(values, width - count, 1)
    return values[:, count : 2 * count]


def answer(inverse, sums):
    return jnp.sum(inverse * sums, axis=0, keepdims=True)


def at_box(values, row_side, col_side):
    long_pos, across_pos, long_count, across_count = position()
    there_long, there_across = long_pos + row_side, across_pos + col_side
    inside = (
        (there_long >= 0)
        & (there_long < long_count)
        & (there_across >= 0)
        & (there_across < across_count)
    )
    lanes = lax.broadcasted_iota(jnp.int32, values.shape, 1)
    wanted = (lanes == there_long * across_count + there_across) & inside
    return jnp.sum(jnp.where(wanted, values, jnp.zeros_like(values)), axis=1, keepdims=True)


def coarse_corrections(parts, *refs):
    table_parts, (out, work) = refs[:parts], refs[parts:]
    count = work.shape[0]
    numbers = last_rows_merged(table_parts, count)
    across_count = lax.axis_size("narrow")
    inverse = coarse_inverse(numbers, work)
    sums = column(numbers, IMAGE_SUM)
    sums = sums - column(pltpu.roll(numbers, count - across_count, 0), FLOW_LONG_LOW)
    sums = sums - column(pltpu.roll(numbers, across_count, 0), FLOW_LONG_HIGH)
    sums = sums - column(pltpu.roll(numbers, count - 1, 0), FLOW_ACROSS_LOW)
    sums = sums - column(pltpu.roll(numbers, 1, 0), FLOW_ACROSS_HIGH)
    load_sums = column(numbers, LOAD_SUM)
    sums = load_sums * (1.0 - 1.0 / cheb_center) - sums
    out[0:1, :] = answer(inverse, load_sums) * (1.0 / cheb_center)
    out[1:2, :] = answer(inverse, sums) * gain


def second_solve(box, local, low, high, left, right, inverses, answers, *rest):
    to_long, to_across, to_deep, mass, load_window = rest[:5]
    tables = rest[5 : 5 + N_TABLES]
    iterate, top, bottom, last_col, first_col, out = rest[5 + N_TABLES : 11 + N_TABLES]
    window, spectral, middle, sems = rest[11 + N_TABLES :]
    long_pos, across_pos, long_count, across_count = position()
    coarse = answers[0:1, :]
    own_shift = at_box(answers[1:2, :], 0, 0)
    shifts = {
        (row_side, col_side): at_box(coarse, row_side, col_side)
        for row_side in (-1, 0, 1)
        for col_side in (-1, 0, 1)
    }

    def add(values, row_side, col_side):
        shift = shifts[row_side, col_side]
        if values.ndim == 3:
            shift = shift.reshape(1, 1, 1)
        return values + shift

    edge = REACH * box.across
    low, high = (
        ref.at[:edge].reshape(REACH, box.across, box.deep) for ref in (low, high)
    )
    wide_sides, narrow_sides = Sides("wide", low, high), Sides("narrow", left, right)
    fill_window(box, window, local, wide_sides, narrow_sides, REACH, 0, REACH, add)
    weights = (to_long, to_across, to_deep, mass)

    start, stop = EDGE - MARGIN, EDGE + box.across + MARGIN

    flow = [to_long[0, start:stop] * (window[1, start:stop] - window[0, start:stop])]

    def divided(values, col):
        return values * inverses[col]

    def residual(start_row):
        rows = []
        for row in range(start_row + 1, start_row + 9):
            image, flow[0] = negative_image(window, row, row, start, stop, flow[0], weights)
            rows.append((load_window[row, start:stop] + image)[None])
        return jnp.concatenate(rows, axis=0)

    inner = slice(EDGE, EDGE + box.across)
    first = REACH
    row_ids = lax.broadcasted_iota(jnp.int32, (1, padded(box.ex)), 1)
    col_ids = lax.broadcasted_iota(jnp.int32, (1, padded(box.ey)), 1)
    row_mask = jnp.where(row_ids < MARGIN, as_float(long_pos > 0), 1.0)
    row_mask = jnp.where(row_ids >= MARGIN + box.long, as_float(long_pos < long_count - 1), row_mask)
    col_mask = jnp.where(col_ids < MARGIN, as_float(across_pos > 0), 1.0)
    col_mask = jnp.where(
        col_ids >= MARGIN + box.across, as_float(across_pos < across_count - 1), col_mask
    )
    keep = 1.0 + rho_second * rho_first
    copies = []

    def emit(start, values):
        rows = values.reshape(8, box.across, box.deep)
        before = window[first + start : first + start + 8, inner, :]
        shift = own_shift.reshape(1, 1, 1)
        iterate[start : start + 8] = keep * before + (gain * rows + shift)
        copies.append(
            pltpu.make_async_copy(
                iterate.at[start : start + 8], out.at[start : start + 8], sems.at[len(copies)]
            )
        )
        copies[-1].start()

    box_solve(
        box, residual, divided, tables, row_mask, col_mask, spectral, middle, emit
    )
    rows = in_order(is_even("wide"), iterate[box.long - 1], iterate[0])
    top[...], bottom[...] = rows
    flat = iterate.reshape(box.long * box.across, box.deep)
    cols = [flat[row_of(box.across, col, box.long), :] for col in (box.across - 1, 0)]
    last_col[...], first_col[...] = in_order(is_even("narrow"), *cols)
    for copy in copies:
        copy.wait()


def inner_residual(
    box, load, iterate, to_long, to_across, to_deep, mass, rows, cols, out, window, result, sems
):
    inner = slice(EDGE, EDGE + box.across)
    flat = window.reshape((box.long + 2) * box.cols, box.deep)
    iterate_flat = iterate.reshape(box.long * box.across, box.deep)
    window[1 : 1 + box.long, inner, :] = iterate[...]
    window[0, inner, :] = iterate[0]
    window[1 + box.long, inner, :] = iterate[box.long - 1]
    for col, place in ((0, EDGE - 1), (box.across - 1, EDGE + box.across)):
        values = iterate_flat[row_of(box.across, col, box.long), :]
        flat[row_of(box.cols, place, box.long, 1), :] = values
    weights = (to_long, to_across, to_deep, mass)
    flow = jnp.zeros((box.across, box.deep), jnp.float32)
    middle = slice(8, box.across - 8)
    copies = []
    for row in range(box.long):
        image, flow = negative_image(
            window, row + 1, REACH + row, inner.start, inner.stop, flow, weights
        )
        values = load[row] + image
        result[row] = values[middle]
        cols[0, row] = values[:8]
        cols[1, row] = values[box.across - 8 :]
        if row == 0:
            rows[0] = values
        if row == box.long - 1:
            rows[1] = values
        if row % 8 == 7:
            part = slice(row - 7, row + 1)
            copy = pltpu.make_async_copy(result.at[part], out.at[part, middle], sems.at[row // 8])
            copy.start()
            copies.append(copy)
    for copy in copies:
        copy.wait()


def outer_residual(
    box, iterate, low, high, left, right, to_long, to_across, rows, cols, inner_out, out,
    row_part, col_part, sems
):
    del inner_out
    inner = slice(EDGE, EDGE + box.across)
    middle = slice(8, box.across - 8)
    wide_sides, narrow_sides = Sides("wide", low, high), Sides("narrow", left, right)
    last = box.long - 1
    iterate_flat = iterate.reshape(box.long * box.across, box.deep)
    across_flat = to_across.reshape(box.flat, box.deep)
    below = to_long[REACH - 1, inner] * (wide_sides.low(Ellipsis) - iterate[0])
    above = to_long[REACH + last, inner] * (wide_sides.high(Ellipsis) - iterate[last])
    row_part[0] = (rows[0] + below)[middle]
    row_part[1] = (rows[1] + above)[middle]
    copies = [
        pltpu.make_async_copy(row_part.at[0], out.at[0, middle], sems.at[0]),
        pltpu.make_async_copy(row_part.at[1], out.at[last, middle], sems.at[1]),
    ]
    for copy in copies:
        copy.start()
    col_part[...] = cols[...]
    flat = col_part.reshape(2 * box.long * 8, box.deep)
    for side, (from_side, col, face, tile) in enumerate(
        (
            (narrow_sides.low, 0, EDGE - 1, slice(0, 8)),
            (narrow_sides.high, box.across - 1, EDGE + box.across - 1, slice(box.across - 8, None)),
        )
    ):
        weight = across_flat[row_of(box.cols, face, box.long, REACH), :]
        own = iterate_flat[row_of(box.across, col, box.long), :]
        place = pl.ds(side * box.long * 8 + side * 7, box.long, stride=8)
        flat[place, :] = flat[place, :] + weight * (from_side(Ellipsis) - own)
        col_part[side, 0] = col_part[side, 0] + below[tile]
        col_part[side, last] = col_part[side, last] + above[tile]
        first_col = side * (box.across - 8)
        copy = pltpu.make_async_copy(
            col_part.at[side], out.at[:, first_col : first_col + 8], sems.at[2 + side]
        )
        copy.start()
        copies.append(copy)
    for copy in copies:
        copy.wait()


def swaps(axis, around):
    sizes = (lax.axis_size("wide"), lax.axis_size("narrow"))
    along = ("wide", "narrow").index(axis)
    size, beside = sizes[along], sizes[1 - along]

    def number(place, other_place):
        pair = (place, other_place) if along == 0 else (other_place, place)
        return pair[0] * sizes[1] + pair[1]

    ways = []
    for way in range(2):
        pairs = []
        for place in range(size):
            for other_place in range(beside):
                partner = place + 1 if place % 2 == way else place - 1
                there = other_place
                if around and size % 2 == 0:
                    partner %= size
                if not 0 <= partner < size:
                    partner = place
                    there = other_place ^ 1 if beside % 2 == 0 else other_place
                pairs.append((number(place, other_place), number(partner, there)))
        ways.append(pairs)
    return ways


def exchange(axis, first, second, around=False):
    ways = swaps(axis, around)
    axes = ("wide", "narrow")
    return lax.ppermute(first, axes, ways[0]), lax.ppermute(second, axes, ways[1])


def two_away(axis, table):
    size = lax.axis_size(axis)
    return lax.ppermute(table, axis, [(i, (i + 2) % size) for i in range(size)])


def tell(table):
    count = table.shape[0]
    long_pos, across_pos, _, across_count = position()
    own = lax.dynamic_slice_in_dim(table, long_pos * across_count + across_pos, 1, axis=0)
    line = jnp.broadcast_to(own, (count, 1, 128))
    told = lax.all_to_all(line, ("wide", "narrow"), split_axis=0, concat_axis=0, tiled=True)
    return told.reshape(count, 128)


def on_device(zone, scale, diffusivity, decay, load):
    box = Box(load.shape)
    long, across, deep = load.shape
    count = lax.axis_size("wide") * lax.axis_size("narrow")
    by_margins = lax.axis_size("wide") == 4 and lax.axis_size("narrow") == 4
    tables = tables_of(box)
    cells = f32(long, across, deep)
    whole_zone = jax.ShapeDtypeStruct(cells.shape, zone.dtype)
    window = f32(box.rows, box.cols, deep)
    table_shape = f32(count, 128)
    anywhere = pl.BlockSpec(memory_space=pl.ANY)
    in_hbm = pl.BlockSpec(memory_space=pltpu.HBM)

    def scratch(shape):
        return pltpu.VMEM(shape, jnp.float32)

    def pinned(field):
        return pltpu.with_memory_space_constraint(field, pltpu.HBM)

    spectral = scratch((box.ey, padded(box.ex), deep))
    middle = scratch((long, padded(box.ey), deep))

    def pack(wide, fields, sides, parts=(), after=()):
        rows = message_rows(box, wide * len(fields)) + (count if parts else 0)
        message = f32(rows, deep)
        body = functools.partial(pack_fields, box, wide, len(fields), len(parts), len(after))
        return call(
            body,
            (message, message) + ((table_shape,) if parts else ()),
            [VMEM] * (len(fields) + 2 + len(parts)) + [anywhere] * len(after),
        )(*fields, *sides, *parts, *after)

    far = f32(2 * REACH, across, deep)
    far_zone, far_scale = zone, scale
    load, load_first, load_second, first, second = call(
        functools.partial(bring_edges, box),
        (cells,) + (f32(MARGIN, across, deep),) * 2 + (far, far),
        [in_hbm] * 3,
        [pltpu.VMEM((2, REACH, across, deep), zone.dtype), pltpu.SemaphoreType.DMA((7,))],
    )(pinned(zone), pinned(scale), pinned(load))
    load_wide = exchange("wide", load_first, load_second)
    far_wide = exchange("wide", first, second)
    load_first, load_second = pack(MARGIN, [load], load_wide)
    load_narrow = exchange("narrow", load_first, load_second)
    zone, scale, sums, table = call(
        functools.partial(box_sums, box),
        (whole_zone, cells, f32(8, 128), table_shape),
        [in_hbm] * 2 + [VMEM, anywhere] + [SMEM] * 2,
        [pltpu.SemaphoreType.DMA((2 * (long // 8),))],
    )(pinned(far_zone), pinned(far_scale), load, load_first, diffusivity, decay)
    far_narrow = exchange("narrow", *pack(REACH, [scale, zone], far_wide))
    load_window, local, image, inverses = call(
        functools.partial(first_solve, box),
        (window, cells, f32(across, deep), f32(box.ey, box.ex, deep)),
        [VMEM] * 8 + [SMEM] * 2 + [VMEM] * N_TABLES,
        [spectral, middle],
        flops=4 * 10**9,
    )(load, *load_wide, *load_narrow, sums, zone, scale, diffusivity, decay, *tables)
    message = f32(REACH * across + count, deep)
    table, first, second = call(
        functools.partial(image_sums, box), (table_shape, message, message), [VMEM] * 9 + [SMEM]
    )(zone, scale, local, image, *far_wide, *far_narrow, table, diffusivity)
    own_table = table
    wide = exchange("wide", first, second, by_margins)
    parts = (table, *wide)
    if by_margins:
        parts += (two_away("wide", table),)
    to_long, to_across, *windows = call(
        functools.partial(side_weights, box),
        (window,) * 4,
        [VMEM] * 6 + [SMEM],
        flops=10**9,
    )(zone, scale, *far_wide, *far_narrow, diffusivity)
    to_deep, mass = call(
        functools.partial(deep_weights, box),
        (window,) * 2,
        [VMEM] * 2 + [SMEM] * 2,
        flops=10**9,
    )(*windows, diffusivity, decay)
    weights = (to_long, to_across, to_deep, mass)
    first, second, table = pack(REACH, [local], wide, parts, [to_long])
    narrow = exchange("narrow", first, second)
    if by_margins:
        table = call(join_rows, table_shape, [VMEM] * 2)(table, narrow[0])
        parts = (table, two_away("narrow", table))
    else:
        parts = (tell(own_table),)
    row, col = f32(across, deep), f32(long, deep)
    answers = call(
        functools.partial(coarse_corrections, len(parts)),
        f32(8, -(-count // 128) * 128),
        [VMEM] * len(parts),
        [scratch((count, -(-2 * count // 128) * 128))],
    )(*parts)
    iterate, first_row, second_row, first_col, second_col, result = call(
        functools.partial(second_solve, box),
        (cells, row, row, col, col, cells),
        [VMEM] * (12 + N_TABLES),
        [scratch(window.shape), spectral, middle, pltpu.SemaphoreType.DMA((long // 8,))],
        flops=4 * 10**9,
        out_spec=(VMEM,) * 5 + (anywhere,),
    )(local, *wide, *narrow, inverses, answers, *weights, load_window, *tables)
    narrow = exchange("narrow", first_col, second_col)
    wide = exchange("wide", first_row, second_row)
    rows, cols, inner = call(
        functools.partial(inner_residual, box),
        (f32(2, across, deep), f32(2, long, 8, deep), cells),
        [VMEM] * 6,
        [
            scratch((long + 2, box.cols, deep)),
            scratch((long, across - 16, deep)),
            pltpu.SemaphoreType.DMA((long // 8,)),
        ],
        flops=10**9,
        out_spec=(VMEM, VMEM, anywhere),
    )(load, iterate, *weights)
    residual = call(
        functools.partial(outer_residual, box),
        cells,
        [VMEM] * 9 + [anywhere],
        [
            scratch((2, across - 16, deep)),
            scratch((2, long, 8, deep)),
            pltpu.SemaphoreType.DMA((4,)),
        ],
        out_spec=anywhere,
        aliases={9: 0},
    )(iterate, *wide, *narrow, to_long, to_across, rows, cols, inner)
    return result, residual


def solution(mesh):
    split = P(("groups", "wide"), "narrow", None)
    return jax.shard_map(
        on_device,
        mesh=mesh,
        in_specs=(split, split, P(), P(), split),
        out_specs=(split, split),
        check_vma=False,
    )
```

```python
import functools

import jax
import jax.numpy as jnp
import ml_dtypes
import numpy as np
from jax import lax
from jax.experimental import pallas as pl
from jax.experimental.pallas import tpu as pltpu
from jax.sharding import PartitionSpec as P

MARGIN = 4
REACH = MARGIN + 1
EDGE = 8

cheb_center = 1.3
cheb_radius = 1.2
cheb_ratio = 1.3 / 1.2
rho_first = 1.0 / cheb_ratio
rho_second = 1.0 / (2.0 * cheb_ratio - rho_first)
gain = 2.0 * rho_second / cheb_radius

MEANS = range(4)
BOX_DIAGONAL, LONG_HIGH, LONG_LOW, ACROSS_HIGH, ACROSS_LOW, LOAD_SUM = range(4, 10)
IMAGE_SUM, FLOW_LONG_HIGH, FLOW_LONG_LOW, FLOW_ACROSS_HIGH, FLOW_ACROSS_LOW = range(16, 21)

VMEM = pl.BlockSpec(memory_space=pltpu.VMEM)
SMEM = pl.BlockSpec(memory_space=pltpu.SMEM)


def sine_basis(length):
    indices = np.arange(1, length + 1)
    phases = indices[:, None] * indices[None, :] % (2 * (length + 1))
    table = np.sqrt(2.0 / (length + 1)) * np.sin(np.pi * phases / (length + 1))
    eigvals = 4.0 * np.sin(np.pi * indices / (2.0 * (length + 1))) ** 2
    return table.astype(np.float32), eigvals.astype(np.float32)


def call(body, out_shape, in_specs, scratch=(), flops=0, out_spec=None, aliases=None):
    return pl.pallas_call(
        body,
        out_shape=out_shape,
        in_specs=in_specs,
        out_specs=out_spec or jax.tree.map(lambda _: VMEM, out_shape),
        scratch_shapes=list(scratch),
        compiler_params=pltpu.CompilerParams(vmem_limit_bytes=30 * 2**20),
        cost_estimate=pl.CostEstimate(flops=flops, bytes_accessed=0, transcendentals=0),
        input_output_aliases=aliases or {},
    )


def f32(*shape):
    return jax.ShapeDtypeStruct(shape, jnp.float32)


class Box:
    def __init__(self, shape):
        self.long, self.across, self.deep = shape
        self.ex = self.long + 2 * MARGIN
        self.ey = self.across + 2 * MARGIN
        self.rows = self.long + 2 * REACH
        self.cols = self.across + 2 * EDGE
        self.flat = self.rows * self.cols


def pieces(values, count):
    parts = []
    for _ in range(count):
        part = values.astype(jnp.bfloat16)
        parts.append(part)
        values = values - part.astype(jnp.float32)
    return parts


def left_table(table, depth, count):
    rows, cols = table.shape
    wide = np.zeros((rows, depth), np.float32)
    wide[:, :cols] = table
    parts = []
    rest = wide
    for _ in range(count):
        part = rest.astype(ml_dtypes.bfloat16)
        parts.append(part)
        rest = rest - part.astype(np.float32)
    blank = np.zeros_like(parts[0])
    lines = []
    for index in range(count):
        used = count - index if count > 2 else count
        lines.append(np.concatenate([parts[index]] * used + [blank] * (count - used), axis=1))
    return np.concatenate(lines, axis=0)


def right_tables(table):
    rest, parts = table, []
    for _ in range(3):
        part = rest.astype(ml_dtypes.bfloat16)
        parts.append(part)
        rest = rest - part.astype(np.float32)
    both = np.concatenate([parts[0], parts[1]], axis=1)
    return np.concatenate([both, both], axis=0), np.concatenate([parts[2], parts[0]], axis=0)


def padded(size):
    return -(-size // 16) * 16


FORWARD, BACKWARD = 2, 3


def tables_of(box):
    sine_x, eig_x = sine_basis(box.ex)
    sine_y, eig_y = sine_basis(box.ey)
    sine_z, eig_z = sine_basis(box.deep)
    in_order_of_steps = np.arange(box.ey).reshape(8, box.ey // 8).T.reshape(-1)
    from_y = sine_y[MARGIN : MARGIN + box.across]
    from_x = sine_x[MARGIN : MARGIN + box.long]
    spread = np.broadcast_to(eig_x[:, None], (box.ex, box.deep))
    main_z, rest_z = right_tables(sine_z)
    return [
        jnp.asarray(np.ascontiguousarray(t))
        for t in (
            left_table(sine_y[:, in_order_of_steps], padded(box.ey), FORWARD),
            left_table(sine_x, padded(box.ex), FORWARD),
            left_table(from_x, padded(box.ex), BACKWARD),
            left_table(from_y, padded(box.ey), BACKWARD),
            main_z,
            rest_z,
            spread,
            eig_z[None, :],
            eig_y[None, :],
        )
    ]


N_TABLES = 9


def bf16_dot(left, right):
    return lax.dot_general(
        left, right, (((1,), (0,)), ((), ())), preferred_element_type=jnp.float32
    )


def dot_left(table, values, count, rows):
    total = bf16_dot(table, jnp.concatenate(pieces(values, count), axis=0))
    return sum(total[index * rows : (index + 1) * rows] for index in range(1, count)) + total[:rows]


def dot_right(values, main, rest, count):
    deep = values.shape[1]
    parts = pieces(values, count)
    total = bf16_dot(jnp.concatenate(parts[:2], axis=1), main)
    result = total[:, :deep] + total[:, deep:]
    if count == 3:
        result = result + bf16_dot(jnp.concatenate([parts[0], parts[2]], axis=1), rest)
    return result


def with_rows(values, rows):
    if values.shape[0] == rows:
        return values
    blank = jnp.zeros((rows - values.shape[0],) + values.shape[1:], values.dtype)
    return jnp.concatenate([values, blank], axis=0)


def box_solve(box, source, divided, tables, row_mask, col_mask, spectral, middle, emit):
    into_y, into_x, from_x, from_y, main_z, rest_z = tables[:6]
    deep = box.deep
    deep_x, deep_y = padded(box.ex), padded(box.ey)
    into_y, into_x = into_y[...], into_x[...]
    if col_mask is not None:
        mask = jnp.concatenate([col_mask] * FORWARD, axis=1)
        into_y = (into_y.astype(jnp.float32) * mask).astype(jnp.bfloat16)
        mask = jnp.concatenate([row_mask] * FORWARD, axis=1)
        into_x = (into_x.astype(jnp.float32) * mask).astype(jnp.bfloat16)
    from_x, from_y, main_z, rest_z = from_x[...], from_y[...], main_z[...], rest_z[...]
    spectral_flat = spectral.reshape(box.ey * deep_x, deep)
    middle_flat = middle.reshape(box.long * deep_y, deep)
    if deep_x > box.ex:
        spectral[:, box.ex :, :] = jnp.zeros((box.ey, deep_x - box.ex, deep), jnp.float32)
    if deep_y > box.ey:
        middle[:, box.ey :, :] = jnp.zeros((box.long, deep_y - box.ey, deep), jnp.float32)
    for start in range(0, box.ex, 8):
        block = source(start).reshape(8 * box.ey, deep)
        block = dot_right(block, main_z, rest_z, FORWARD).reshape(8, box.ey, deep)
        for row in range(0, 8, 2):
            pair = jnp.concatenate([block[row], block[row + 1]], axis=1)
            pair = dot_left(into_y, with_rows(pair, deep_y), FORWARD, box.ey)
            for part in range(2):
                spectral_flat[pl.ds(start + row + part, box.ey, stride=deep_x), :] = pair[
                    :, part * deep : (part + 1) * deep
                ]
    for col in range(0, box.ey, 2):
        pair = jnp.concatenate([spectral[col], spectral[col + 1]], axis=1)
        pair = dot_left(into_x, pair, FORWARD, box.ex)
        pair = jnp.concatenate(
            [
                divided(pair[:, part * deep : (part + 1) * deep], col + part)
                for part in range(2)
            ],
            axis=1,
        )
        pair = dot_left(from_x, with_rows(pair, deep_x), BACKWARD, box.long)
        for part in range(2):
            middle_flat[pl.ds(col + part, box.long, stride=deep_y), :] = pair[
                :, part * deep : (part + 1) * deep
            ]
    for start in range(0, box.long, 8):
        parts = []
        for row in range(start, start + 8, 2):
            pair = jnp.concatenate([middle[row], middle[row + 1]], axis=1)
            pair = dot_left(from_y, pair, BACKWARD, box.across)
            parts += [pair[:, :deep], pair[:, deep:]]
        emit(start, dot_right(jnp.concatenate(parts, axis=0), main_z, rest_z, BACKWARD))


def position():
    long_pos, across_pos = lax.axis_index("wide"), lax.axis_index("narrow")
    return long_pos, across_pos, lax.axis_size("wide"), lax.axis_size("narrow")


def as_float(flag):
    return jnp.where(flag, jnp.float32(1.0), jnp.float32(0.0))


def is_even(axis):
    return lax.rem(lax.axis_index(axis), 2) == 0


class Sides:
    def __init__(self, axis, first, second):
        position = lax.axis_index(axis)
        self.even = is_even(axis)
        self.has_low = as_float(position > 0)
        self.has_high = as_float(position < lax.axis_size(axis) - 1)
        self.first, self.second = first, second

    def low(self, *index):
        return jnp.where(self.even, self.second[index], self.first[index]) * self.has_low

    def high(self, *index):
        return jnp.where(self.even, self.first[index], self.second[index]) * self.has_high


def in_order(even, up, down):
    return jnp.where(even, up, down), jnp.where(even, down, up)


def row_of(stride, col, count, first=0):
    return pl.ds(first * stride + col, count, stride=stride)


def pack_columns(box, fields, wide_sides, wide, first, second):
    corner = len(fields) * wide * box.long
    even = is_even("narrow")
    place = 0
    for field, sides in zip(fields, wide_sides):
        for step in range(wide):
            cols = (box.across - wide + step, step)
            values = [field[row_of(box.across, col, box.long), :] for col in cols]
            low = [sides.low(row_of(box.across, col, wide), slice(None)) for col in cols]
            high = [sides.high(row_of(box.across, col, wide), slice(None)) for col in cols]
            at = corner + 2 * REACH * place
            for start, parts in ((place * box.long, values), (at, low), (at + REACH, high)):
                parts = in_order(even, *(part.astype(jnp.float32) for part in parts))
                size = parts[0].shape[0]
                first[start : start + size, :], second[start : start + size, :] = parts
            place += 1


def message_rows(box, count):
    return -(-(count * (box.long + 2 * REACH)) // 8) * 8


def pack_fields(box, wide, fields, tables, after, *refs):
    own, (low, high), refs = refs[:fields], refs[fields : fields + 2], refs[fields + 2 :]
    parts, (first, second, *table) = refs[:tables], refs[tables + after :]
    size = wide * box.across
    flat = [field.reshape(box.long * box.across, box.deep) for field in own]
    low = low.reshape(low.size // box.deep, box.deep)
    high = high.reshape(high.size // box.deep, box.deep)
    sides = [
        Sides("wide", *(ref.at[index * size : (index + 1) * size] for ref in (low, high)))
        for index in range(fields)
    ]
    pack_columns(box, flat, sides, wide, first, second)
    if tables:
        known = last_rows_merged(parts, table[0].shape[0])
        table[0][...] = known
        first[first.shape[0] - known.shape[0] :, :] = known
        second[second.shape[0] - known.shape[0] :, :] = known


def bring_edges(
    box, zone, scale, load, own_zone, own_scale, own_load, load_first, load_second, first, second,
    staged, sems
):
    even = is_even("wide")

    def edges(wide):
        up, down = box.long - wide, 0
        return [pl.ds(jnp.where(even, *pair), wide) for pair in ((up, down), (down, up))]

    copies = [
        (load.at[edges(MARGIN)[0]], load_first),
        (load.at[edges(MARGIN)[1]], load_second),
        (zone.at[edges(REACH)[0]], staged.at[0]),
        (zone.at[edges(REACH)[1]], staged.at[1]),
        (scale.at[edges(REACH)[0]], first.at[:REACH]),
        (scale.at[edges(REACH)[1]], second.at[:REACH]),
        (load, own_load),
        (scale, own_scale),
        (zone, own_zone),
    ]
    copies = [
        pltpu.make_async_copy(source, target, sems.at[index])
        for index, (source, target) in enumerate(copies)
    ]
    for copy in copies:
        copy.start()
    for copy in copies[:4]:
        copy.wait()
    first[REACH:] = staged[0].astype(jnp.float32)
    second[REACH:] = staged[1].astype(jnp.float32)
    for copy in copies[4:]:
        copy.wait()


def fill_window(box, window, own, wide_sides, narrow_sides, wide, place, total, add=None):
    flat = window.reshape(box.flat, box.deep)
    nothing = jnp.zeros((box.rows, EDGE, box.deep), jnp.float32)
    window[:, :EDGE, :] = nothing
    window[:, EDGE + box.across :, :] = nothing
    if add is None:
        add = lambda values, row_side, col_side: values
    inner = slice(EDGE, EDGE + box.across)
    first, last = REACH, REACH + box.long
    if wide < REACH:
        blank = jnp.zeros((1, box.across, box.deep), jnp.float32)
        window[0:1, inner, :] = blank
        window[box.rows - 1 :, inner, :] = blank
    window[first:last, inner, :] = add(own[...].astype(jnp.float32), 0, 0)
    window[first - wide : first, inner, :] = add(wide_sides.low(Ellipsis), -1, 0)
    window[last : last + wide, inner, :] = add(wide_sides.high(Ellipsis), 1, 0)
    corner = total * box.long
    for step in range(wide):
        for source, col, side in (
            (narrow_sides.low, EDGE - wide + step, -1),
            (narrow_sides.high, EDGE + box.across + step, 1),
        ):
            for start, size, row, row_side in (
                ((place + step) * box.long, box.long, first, 0),
                (corner + 2 * REACH * (place + step), wide, first - wide, -1),
                (corner + 2 * REACH * (place + step) + REACH, wide, last, 1),
            ):
                values = source(slice(start, start + size), slice(None))
                flat[row_of(box.cols, col, size, row), :] = add(values, row_side, side)


def some_cols(box, ref, row, step):
    stride = box.ey // 8
    return ref[row, pl.ds(EDGE - MARGIN + step, 8, stride=stride), :]


def negative_image(box, window, row, at, x, flow_before, weights):
    to_long, to_across, to_deep, mass = weights
    steps = range(box.ey // 8)
    x_next = [some_cols(box, window, row + 1, step) for step in range(-1, len(steps) + 1)]
    flow_long = [
        some_cols(box, to_long, at, step) * (x_next[step + 1] - x[step + 1]) for step in steps
    ]
    flow_across = [
        some_cols(box, to_across, at, step) * (x[step + 2] - x[step + 1])
        for step in range(-1, len(steps))
    ]
    totals = []
    for step in steps:
        here = x[step + 1]
        lanes = here.shape[1]
        flow_deep = some_cols(box, to_deep, at, step) * (pltpu.roll(here, lanes - 1, 1) - here)
        total = flow_long[step] - flow_before[step] - some_cols(box, mass, at, step) * here
        total = total + (flow_across[step + 1] - flow_across[step])
        totals.append(total + (flow_deep - pltpu.roll(flow_deep, 1, 1)))
    return totals, x_next, flow_long


def in_steps(box, refs, rows):
    return jnp.stack(
        [
            jnp.concatenate([some_cols(box, ref, row, step) for step in range(box.ey // 8)], axis=0)
            for ref, row in zip(refs, rows)
        ]
    )


def looked_up(labels, values):
    return jnp.where(labels == 0, values[0], jnp.where(labels == 1, values[1], values[2]))


def at_own_row(line, shape):
    long_pos, across_pos, _, across_count = position()
    rows = lax.broadcasted_iota(jnp.int32, shape, 0)
    own = rows == long_pos * across_count + across_pos
    return jnp.where(own, line[:1], jnp.zeros(shape, jnp.float32))


def merged(table, *others):
    for other in others:
        table = jnp.where(table != 0.0, table, other)
    return table


def last_rows_merged(refs, count):
    return merged(*(ref[ref.shape[0] - count :, :] for ref in refs))


def join_rows(table, message, out):
    out[...] = last_rows_merged((table, message), out.shape[0])


def line_of(numbers, shape):
    lanes = lax.broadcasted_iota(jnp.int32, shape, 1)
    line = jnp.zeros(shape, jnp.float32)
    for index, number in numbers:
        line = jnp.where(lanes == index, number, line)
    return line


def box_sums(box, zone, scale, load, after, diffusivity, decay, out, table):
    del after
    nothing = jnp.zeros((box.across, box.deep), jnp.float32)
    half = [[0.5 * diffusivity[z, d] for z in range(3)] for d in range(3)]
    rates = [decay[z] for z in range(3)]

    def halves(row):
        labels, factor = zone[row], scale[row]
        return [looked_up(labels, half[d]) * factor for d in range(3)] + [looked_up(labels, rates)]

    sums = [nothing] * 5
    for row in range(box.long):
        sums = [total + more for total, more in zip(sums, halves(row) + [load[row]])]

    def total(values):
        return jnp.sum(values, keepdims=True).reshape(1, 1)

    cells = box.long * box.across * box.deep
    numbers = [(index, total(sums[index]) * (2.0 / cells)) for index in range(3)]
    mass = total(sums[3])
    numbers += [(3, mass / cells)]
    ends = total(sums[2][:, :1]) + total(sums[2][:, box.deep - 1 :])
    numbers += [
        (BOX_DIAGONAL, mass + ends),
        (LONG_HIGH, total(halves(box.long - 1)[0])),
        (LONG_LOW, total(halves(0)[0])),
        (ACROSS_HIGH, total(sums[1][box.across - 1 :])),
        (ACROSS_LOW, total(sums[1][:1])),
        (LOAD_SUM, total(sums[4])),
    ]
    line = line_of(numbers, out.shape)
    out[...] = line
    table[...] = at_own_row(line, table.shape)


def means_of(ref):
    return [ref[0:1, index : index + 1] for index in range(4)]


def first_solve(box, load, low, high, left, right, means, zone, scale, diffusivity, decay, *rest):
    tables = rest[:N_TABLES]
    window, local, image, inverses, spectral, middle = rest[N_TABLES:]
    spread, eig_z, eig_y = tables[6:]
    means = means_of(means)
    base = means[3] + means[0] * spread[...] + means[2] * eig_z[...]

    def divided(values, col):
        divisor = base + means[1] * eig_y[0, col]
        inverse = pl.reciprocal(divisor, approx=True)
        for _ in range(2):
            inverse = inverse * (2.0 - divisor * inverse)
        inverses[col] = inverse
        return values * inverse

    half = [0.5 * diffusivity[z, 2] for z in range(3)]
    rates = [decay[z] for z in range(3)]
    lane = lax.broadcasted_iota(jnp.int32, (box.across, box.deep), 1)
    ends = jnp.where((lane == 0) | (lane == box.deep - 1), jnp.float32(1.0), jnp.float32(0.0))
    image[...] = jnp.zeros((box.across, box.deep), jnp.float32)
    wide_sides, narrow_sides = Sides("wide", low, high), Sides("narrow", left, right)
    fill_window(box, window, load, wide_sides, narrow_sides, MARGIN, 0, MARGIN)

    def emit(start, values):
        values = values * (1.0 / cheb_center)
        values = values.reshape(8, box.across, box.deep)
        local[start : start + 8] = values
        total = image[...]
        for row in range(8):
            labels = zone[start + row]
            mass = looked_up(labels, rates) + looked_up(labels, half) * scale[start + row] * ends
            total = total + mass * values[row]
        image[...] = total

    box_solve(
        box,
        lambda start: in_steps(box, [window] * 8, range(1 + start, 9 + start)),
        divided,
        tables,
        None,
        None,
        spectral,
        middle,
        emit,
    )


def side_weights(
    box, zone, scale, low, high, left, right, diffusivity, to_long, to_across, zone_window,
    scale_window
):
    for index, (window, own) in enumerate(((scale_window, scale), (zone_window, zone))):
        start = index * REACH
        wide_sides = Sides("wide", *(ref.at[start : start + REACH] for ref in (low, high)))
        narrow_sides = Sides("narrow", left, right)
        fill_window(box, window, own, wide_sides, narrow_sides, REACH, start, 2 * REACH)
    half = [[0.5 * diffusivity[z, d] for z in range(3)] for d in range(2)]

    def one_row(row, before):
        labels, factor = zone_window[row], scale_window[row]
        now = [looked_up(labels, half[d]) * factor for d in range(2)]
        to_across[row] = now[1] + pltpu.roll(now[1], box.cols - 1, 0)
        to_long[jnp.maximum(row - 1, 0)] = before + now[0]
        return now[0]

    def some_rows(index, before):
        for row in range(8):
            before = one_row(index * 8 + row, before)
        return before

    before = jnp.zeros((box.cols, box.deep), jnp.float32)
    before = lax.fori_loop(0, box.rows // 8, some_rows, before)
    for row in range(box.rows // 8 * 8, box.rows):
        before = one_row(row, before)
    to_long[box.rows - 1] = before


def deep_weights(box, zone_window, scale_window, diffusivity, decay, to_deep, mass):
    half = [0.5 * diffusivity[z, 2] for z in range(3)]
    rates = [decay[z] for z in range(3)]
    lane = lax.broadcasted_iota(jnp.int32, (box.cols, box.deep), 1)
    ends = jnp.where((lane == 0) | (lane == box.deep - 1), jnp.float32(1.0), jnp.float32(0.0))
    not_last = jnp.where(lane == box.deep - 1, jnp.float32(0.0), jnp.float32(1.0))

    def one_row(row):
        labels = zone_window[row]
        now = looked_up(labels, half) * scale_window[row]
        to_deep[row] = (now + pltpu.roll(now, box.deep - 1, 1)) * not_last
        mass[row] = looked_up(labels, rates) + now * ends

    def some_rows(index, _):
        for row in range(8):
            one_row(index * 8 + row)
        return 0

    lax.fori_loop(0, box.rows // 8, some_rows, 0)
    for row in range(box.rows // 8 * 8, box.rows):
        one_row(row)


def image_sums(
    box, zone, scale, local, image, low, high, left, right, table, diffusivity, out, up, down
):
    half = [[0.5 * diffusivity[z, d] for z in range(3)] for d in range(3)]
    shape = (box.long * box.across, box.deep)
    zone_flat, scale_flat, local_flat = zone.reshape(shape), scale.reshape(shape), local.reshape(shape)
    last_col = row_of(box.across, box.across - 1, box.long)
    first_col = row_of(box.across, 0, box.long)

    wide_sides, narrow_sides = Sides("wide", low, high), Sides("narrow", left, right)

    def side(source, place):
        return source(slice(place * box.long, (place + 1) * box.long), slice(None))

    above, below = wide_sides.high, wide_sides.low
    faces = [
        (0, zone[box.long - 1], scale[box.long - 1], local[box.long - 1], above(REACH), above(0)),
        (0, zone[0], scale[0], local[0], below(2 * REACH - 1), below(REACH - 1)),
        (
            1,
            zone_flat[last_col, :],
            scale_flat[last_col, :],
            local_flat[last_col, :],
            side(narrow_sides.high, REACH),
            side(narrow_sides.high, 0),
        ),
        (
            1,
            zone_flat[first_col, :],
            scale_flat[first_col, :],
            local_flat[first_col, :],
            side(narrow_sides.low, 2 * REACH - 1),
            side(narrow_sides.low, REACH - 1),
        ),
    ]
    flows = []
    for direction, labels, factor, values, far_labels, far_factor in faces:
        weight = looked_up(labels, half[direction]) * factor
        weight = weight + looked_up(far_labels, half[direction]) * far_factor
        flows.append(jnp.sum(weight * values, keepdims=True))
    long_pos, across_pos, long_count, across_count = position()
    numbers = [
        (IMAGE_SUM, jnp.sum(image[...], keepdims=True) + sum(flows)),
        (FLOW_LONG_HIGH, flows[0] * as_float(long_pos < long_count - 1)),
        (FLOW_LONG_LOW, flows[1] * as_float(long_pos > 0)),
        (FLOW_ACROSS_HIGH, flows[2] * as_float(across_pos < across_count - 1)),
        (FLOW_ACROSS_LOW, flows[3] * as_float(across_pos > 0)),
    ]
    known = table[...] + at_own_row(line_of(numbers, (8, out.shape[1])), out.shape)
    out[...] = known
    edge = REACH * box.across
    even = is_even("wide")
    for target, pair in ((up, (box.long - REACH, 0)), (down, (0, box.long - REACH))):
        target[:edge] = local[pl.ds(jnp.where(even, *pair), REACH)].reshape(edge, box.deep)
        target[edge:] = known


def column(values, index):
    return values[:, index : index + 1]


def coarse_inverse(numbers, work):
    count, width = work.shape
    across = lax.axis_size("narrow")
    beyond = pltpu.roll(numbers, count - across, 0)
    beside = pltpu.roll(numbers, count - 1, 0)
    before = pltpu.roll(numbers, across, 0)
    ahead = pltpu.roll(numbers, 1, 0)
    place = lax.broadcasted_iota(jnp.int32, (count, 1), 0)
    across_pos = lax.rem(place, across)
    nothing = jnp.zeros((count, 1), jnp.float32)
    couplings = []
    diagonal = column(numbers, BOX_DIAGONAL)
    for own, other, there, inside in (
        (LONG_HIGH, LONG_LOW, beyond, place < count - across),
        (LONG_LOW, LONG_HIGH, before, place >= across),
        (ACROSS_HIGH, ACROSS_LOW, beside, across_pos < across - 1),
        (ACROSS_LOW, ACROSS_HIGH, ahead, across_pos > 0),
    ):
        shared = jnp.where(inside, column(there, other), nothing)
        diagonal = diagonal + column(numbers, own) + shared
        couplings.append(jnp.where(inside, column(numbers, own) + shared, nothing))
    rows = lax.broadcasted_iota(jnp.int32, (count, width), 0)
    cols = lax.broadcasted_iota(jnp.int32, (count, width), 1)
    blank = jnp.zeros((count, width), jnp.float32)
    matrix = jnp.where(cols == rows, diagonal, blank)
    for shift, coupling in zip((across, -across, 1, -1), couplings):
        matrix = matrix - jnp.where((cols == rows + shift) & (cols < count), coupling, blank)
    matrix = jnp.where(cols == rows + count, jnp.ones((count, 1), jnp.float32), matrix)
    if count <= 16:
        for step in range(count):
            pivot_row = matrix[step : step + 1, :] / matrix[step : step + 1, step : step + 1]
            rest = matrix - matrix[:, step : step + 1] * pivot_row
            matrix = jnp.where(rows == step, pivot_row, rest)
        return pltpu.roll(matrix, width - count, 1)
    work[...] = matrix

    def eliminate(step, _):
        values = work[...]
        pivot_row = work[pl.ds(step, 1), :]
        at_step = cols == step
        factors = jnp.sum(jnp.where(at_step, values, blank), axis=1, keepdims=True)
        pivot = jnp.sum(jnp.where(at_step[:1], pivot_row, blank[:1]), axis=1, keepdims=True)
        pivot_row = pivot_row / pivot
        work[...] = jnp.where(rows == step, pivot_row, values - factors * pivot_row)
        return 0

    lax.fori_loop(0, count, eliminate, 0)
    values = work[...]
    if count % 128:
        return pltpu.roll(values, width - count, 1)
    return values[:, count : 2 * count]


def answer(inverse, sums):
    return jnp.sum(inverse * sums, axis=0, keepdims=True)


def at_box(values, row_side, col_side):
    long_pos, across_pos, long_count, across_count = position()
    there_long, there_across = long_pos + row_side, across_pos + col_side
    inside = (
        (there_long >= 0)
        & (there_long < long_count)
        & (there_across >= 0)
        & (there_across < across_count)
    )
    lanes = lax.broadcasted_iota(jnp.int32, values.shape, 1)
    wanted = (lanes == there_long * across_count + there_across) & inside
    return jnp.sum(jnp.where(wanted, values, jnp.zeros_like(values)), axis=1, keepdims=True)


def coarse_corrections(parts, *refs):
    table_parts, (out, work) = refs[:parts], refs[parts:]
    count = work.shape[0]
    numbers = last_rows_merged(table_parts, count)
    across_count = lax.axis_size("narrow")
    inverse = coarse_inverse(numbers, work)
    sums = column(numbers, IMAGE_SUM)
    sums = sums - column(pltpu.roll(numbers, count - across_count, 0), FLOW_LONG_LOW)
    sums = sums - column(pltpu.roll(numbers, across_count, 0), FLOW_LONG_HIGH)
    sums = sums - column(pltpu.roll(numbers, count - 1, 0), FLOW_ACROSS_LOW)
    sums = sums - column(pltpu.roll(numbers, 1, 0), FLOW_ACROSS_HIGH)
    load_sums = column(numbers, LOAD_SUM)
    sums = load_sums * (1.0 - 1.0 / cheb_center) - sums
    out[0:1, :] = answer(inverse, load_sums) * (1.0 / cheb_center)
    out[1:2, :] = answer(inverse, sums) * gain


def second_solve(box, local, low, high, left, right, inverses, answers, *rest):
    to_long, to_across, to_deep, mass, load_window = rest[:5]
    tables = rest[5 : 5 + N_TABLES]
    iterate, top, bottom, last_col, first_col, out = rest[5 + N_TABLES : 11 + N_TABLES]
    window, spectral, middle, sems = rest[11 + N_TABLES :]
    long_pos, across_pos, long_count, across_count = position()
    coarse = answers[0:1, :]
    own_shift = at_box(answers[1:2, :], 0, 0)
    shifts = {
        (row_side, col_side): at_box(coarse, row_side, col_side)
        for row_side in (-1, 0, 1)
        for col_side in (-1, 0, 1)
    }

    def add(values, row_side, col_side):
        shift = shifts[row_side, col_side]
        if values.ndim == 3:
            shift = shift.reshape(1, 1, 1)
        return values + shift

    edge = REACH * box.across
    low, high = (
        ref.at[:edge].reshape(REACH, box.across, box.deep) for ref in (low, high)
    )
    wide_sides, narrow_sides = Sides("wide", low, high), Sides("narrow", left, right)
    fill_window(box, window, local, wide_sides, narrow_sides, REACH, 0, REACH, add)
    weights = (to_long, to_across, to_deep, mass)

    steps = range(box.ey // 8)
    x = [some_cols(box, window, 1, step) for step in range(-1, len(steps) + 1)]
    flow = [
        some_cols(box, to_long, 0, step) * (x[step + 1] - some_cols(box, window, 0, step))
        for step in steps
    ]
    state = [x, flow]

    def divided(values, col):
        return values * inverses[col]

    def residual(start_row):
        rows = []
        for row in range(start_row + 1, start_row + 9):
            image, *state[:] = negative_image(box, window, row, row, *state, weights)
            image = [some_cols(box, load_window, row, step) + image[step] for step in steps]
            rows.append(jnp.concatenate(image, axis=0))
        return jnp.stack(rows)

    inner = slice(EDGE, EDGE + box.across)
    first = REACH
    row_ids = lax.broadcasted_iota(jnp.int32, (1, padded(box.ex)), 1)
    col_ids = lax.broadcasted_iota(jnp.int32, (1, padded(box.ey)), 1)
    col_ids = (col_ids & 7) * (box.ey // 8) + lax.shift_right_logical(col_ids, 3)
    row_mask = jnp.where(row_ids < MARGIN, as_float(long_pos > 0), 1.0)
    row_mask = jnp.where(row_ids >= MARGIN + box.long, as_float(long_pos < long_count - 1), row_mask)
    col_mask = jnp.where(col_ids < MARGIN, as_float(across_pos > 0), 1.0)
    col_mask = jnp.where(
        col_ids >= MARGIN + box.across, as_float(across_pos < across_count - 1), col_mask
    )
    keep = 1.0 + rho_second * rho_first
    copies = []

    def emit(start, values):
        rows = values.reshape(8, box.across, box.deep)
        before = window[first + start : first + start + 8, inner, :]
        shift = own_shift.reshape(1, 1, 1)
        iterate[start : start + 8] = keep * before + (gain * rows + shift)
        copies.append(
            pltpu.make_async_copy(
                iterate.at[start : start + 8], out.at[start : start + 8], sems.at[len(copies)]
            )
        )
        copies[-1].start()

    box_solve(
        box, residual, divided, tables, row_mask, col_mask, spectral, middle, emit
    )
    rows = in_order(is_even("wide"), iterate[box.long - 1], iterate[0])
    top[...], bottom[...] = rows
    flat = iterate.reshape(box.long * box.across, box.deep)
    cols = [flat[row_of(box.across, col, box.long), :] for col in (box.across - 1, 0)]
    last_col[...], first_col[...] = in_order(is_even("narrow"), *cols)
    for copy in copies:
        copy.wait()


def inner_residual(
    box, load, iterate, to_long, to_across, to_deep, mass, rows, cols, out, window, result, sems
):
    inner = slice(EDGE, EDGE + box.across)
    flat = window.reshape((box.long + 2) * box.cols, box.deep)
    iterate_flat = iterate.reshape(box.long * box.across, box.deep)
    blank = jnp.zeros((box.long + 2, EDGE, box.deep), jnp.float32)
    window[:, :EDGE, :] = blank
    window[:, EDGE + box.across :, :] = blank
    window[1 : 1 + box.long, inner, :] = iterate[...]
    window[0, inner, :] = iterate[0]
    window[1 + box.long, inner, :] = iterate[box.long - 1]
    for col, place in ((0, EDGE - 1), (box.across - 1, EDGE + box.across)):
        values = iterate_flat[row_of(box.across, col, box.long), :]
        flat[row_of(box.cols, place, box.long, 1), :] = values
    weights = (to_long, to_across, to_deep, mass)
    steps = range(box.ey // 8)
    x = [some_cols(box, window, 1, step) for step in range(-1, len(steps) + 1)]
    flow = [jnp.zeros((8, box.deep), jnp.float32) for _ in steps]
    middle = slice(8, box.across - 8)
    copies = []
    for row in range(box.long):
        image, x, flow = negative_image(box, window, row + 1, REACH + row, x, flow, weights)
        for step in steps:
            place = pl.ds(EDGE - MARGIN + step, 8, stride=box.ey // 8)
            result[row, place, :] = image[step]
        values = load[row] + result[row, inner]
        result[row, inner] = values
        cols[0, row] = values[:8]
        cols[1, row] = values[box.across - 8 :]
        if row == 0:
            rows[0] = values
        if row == box.long - 1:
            rows[1] = values
        if row % 8 == 7:
            part = slice(row - 7, row + 1)
            copy = pltpu.make_async_copy(
                result.at[part, EDGE + 8 : EDGE + box.across - 8],
                out.at[part, middle],
                sems.at[row // 8],
            )
            copy.start()
            copies.append(copy)
    for copy in copies:
        copy.wait()


def outer_residual(
    box, iterate, low, high, left, right, to_long, to_across, rows, cols, inner_out, out,
    row_part, col_part, sems
):
    del inner_out
    inner = slice(EDGE, EDGE + box.across)
    middle = slice(8, box.across - 8)
    wide_sides, narrow_sides = Sides("wide", low, high), Sides("narrow", left, right)
    last = box.long - 1
    iterate_flat = iterate.reshape(box.long * box.across, box.deep)
    across_flat = to_across.reshape(box.flat, box.deep)
    below = to_long[REACH - 1, inner] * (wide_sides.low(Ellipsis) - iterate[0])
    above = to_long[REACH + last, inner] * (wide_sides.high(Ellipsis) - iterate[last])
    row_part[0] = (rows[0] + below)[middle]
    row_part[1] = (rows[1] + above)[middle]
    copies = [
        pltpu.make_async_copy(row_part.at[0], out.at[0, middle], sems.at[0]),
        pltpu.make_async_copy(row_part.at[1], out.at[last, middle], sems.at[1]),
    ]
    for copy in copies:
        copy.start()
    col_part[...] = cols[...]
    flat = col_part.reshape(2 * box.long * 8, box.deep)
    for side, (from_side, col, face, tile) in enumerate(
        (
            (narrow_sides.low, 0, EDGE - 1, slice(0, 8)),
            (narrow_sides.high, box.across - 1, EDGE + box.across - 1, slice(box.across - 8, None)),
        )
    ):
        weight = across_flat[row_of(box.cols, face, box.long, REACH), :]
        own = iterate_flat[row_of(box.across, col, box.long), :]
        place = pl.ds(side * box.long * 8 + side * 7, box.long, stride=8)
        flat[place, :] = flat[place, :] + weight * (from_side(Ellipsis) - own)
        col_part[side, 0] = col_part[side, 0] + below[tile]
        col_part[side, last] = col_part[side, last] + above[tile]
        first_col = side * (box.across - 8)
        copy = pltpu.make_async_copy(
            col_part.at[side], out.at[:, first_col : first_col + 8], sems.at[2 + side]
        )
        copy.start()
        copies.append(copy)
    for copy in copies:
        copy.wait()


def swaps(axis, around):
    sizes = (lax.axis_size("wide"), lax.axis_size("narrow"))
    along = ("wide", "narrow").index(axis)
    size, beside = sizes[along], sizes[1 - along]

    def number(place, other_place):
        pair = (place, other_place) if along == 0 else (other_place, place)
        return pair[0] * sizes[1] + pair[1]

    ways = []
    for way in range(2):
        pairs = []
        for place in range(size):
            for other_place in range(beside):
                partner = place + 1 if place % 2 == way else place - 1
                there = other_place
                if around and size % 2 == 0:
                    partner %= size
                if not 0 <= partner < size:
                    partner = place
                    there = other_place ^ 1 if beside % 2 == 0 else other_place
                pairs.append((number(place, other_place), number(partner, there)))
        ways.append(pairs)
    return ways


def exchange(axis, first, second, around=False):
    ways = swaps(axis, around)
    axes = ("wide", "narrow")
    return lax.ppermute(first, axes, ways[0]), lax.ppermute(second, axes, ways[1])


def two_away(axis, table):
    size = lax.axis_size(axis)
    return lax.ppermute(table, axis, [(i, (i + 2) % size) for i in range(size)])


def tell(table):
    count = table.shape[0]
    long_pos, across_pos, _, across_count = position()
    own = lax.dynamic_slice_in_dim(table, long_pos * across_count + across_pos, 1, axis=0)
    line = jnp.broadcast_to(own, (count, 1, 128))
    told = lax.all_to_all(line, ("wide", "narrow"), split_axis=0, concat_axis=0, tiled=True)
    return told.reshape(count, 128)


def on_device(zone, scale, diffusivity, decay, load):
    box = Box(load.shape)
    long, across, deep = load.shape
    count = lax.axis_size("wide") * lax.axis_size("narrow")
    by_margins = lax.axis_size("wide") == 4 and lax.axis_size("narrow") == 4
    tables = tables_of(box)
    cells = f32(long, across, deep)
    whole_zone = jax.ShapeDtypeStruct(cells.shape, zone.dtype)
    window = f32(box.rows, box.cols, deep)
    table_shape = f32(count, 128)
    anywhere = pl.BlockSpec(memory_space=pl.ANY)
    in_hbm = pl.BlockSpec(memory_space=pltpu.HBM)

    def scratch(shape):
        return pltpu.VMEM(shape, jnp.float32)

    def pinned(field):
        return pltpu.with_memory_space_constraint(field, pltpu.HBM)

    spectral = scratch((box.ey, padded(box.ex), deep))
    middle = scratch((long, padded(box.ey), deep))

    def pack(wide, fields, sides, parts=(), after=()):
        rows = message_rows(box, wide * len(fields)) + (count if parts else 0)
        message = f32(rows, deep)
        body = functools.partial(pack_fields, box, wide, len(fields), len(parts), len(after))
        return call(
            body,
            (message, message) + ((table_shape,) if parts else ()),
            [VMEM] * (len(fields) + 2 + len(parts)) + [anywhere] * len(after),
        )(*fields, *sides, *parts, *after)

    far = f32(2 * REACH, across, deep)
    zone, scale, load, load_first, load_second, first, second = call(
        functools.partial(bring_edges, box),
        (whole_zone, cells, cells) + (f32(MARGIN, across, deep),) * 2 + (far, far),
        [in_hbm] * 3,
        [pltpu.VMEM((2, REACH, across, deep), zone.dtype), pltpu.SemaphoreType.DMA((9,))],
    )(pinned(zone), pinned(scale), pinned(load))
    load_wide = exchange("wide", load_first, load_second)
    far_wide = exchange("wide", first, second)
    load_first, load_second = pack(MARGIN, [load], load_wide)
    load_narrow = exchange("narrow", load_first, load_second)
    sums, table = call(
        functools.partial(box_sums, box),
        (f32(8, 128), table_shape),
        [VMEM] * 3 + [anywhere] + [SMEM] * 2,
    )(zone, scale, load, load_first, diffusivity, decay)
    far_narrow = exchange("narrow", *pack(REACH, [scale, zone], far_wide))
    load_window, local, image, inverses = call(
        functools.partial(first_solve, box),
        (window, cells, f32(across, deep), f32(box.ey, box.ex, deep)),
        [VMEM] * 8 + [SMEM] * 2 + [VMEM] * N_TABLES,
        [spectral, middle],
        flops=4 * 10**9,
    )(load, *load_wide, *load_narrow, sums, zone, scale, diffusivity, decay, *tables)
    message = f32(REACH * across + count, deep)
    table, first, second = call(
        functools.partial(image_sums, box), (table_shape, message, message), [VMEM] * 9 + [SMEM]
    )(zone, scale, local, image, *far_wide, *far_narrow, table, diffusivity)
    own_table = table
    wide = exchange("wide", first, second, by_margins)
    parts = (table, *wide)
    if by_margins:
        parts += (two_away("wide", table),)
    to_long, to_across, *windows = call(
        functools.partial(side_weights, box),
        (window,) * 4,
        [VMEM] * 6 + [SMEM],
        flops=10**9,
    )(zone, scale, *far_wide, *far_narrow, diffusivity)
    to_deep, mass = call(
        functools.partial(deep_weights, box),
        (window,) * 2,
        [VMEM] * 2 + [SMEM] * 2,
        flops=10**9,
    )(*windows, diffusivity, decay)
    weights = (to_long, to_across, to_deep, mass)
    first, second, table = pack(REACH, [local], wide, parts, [to_long])
    narrow = exchange("narrow", first, second)
    if by_margins:
        table = call(join_rows, table_shape, [VMEM] * 2)(table, narrow[0])
        parts = (table, two_away("narrow", table))
    else:
        parts = (tell(own_table),)
    row, col = f32(across, deep), f32(long, deep)
    answers = call(
        functools.partial(coarse_corrections, len(parts)),
        f32(8, -(-count // 128) * 128),
        [VMEM] * len(parts),
        [scratch((count, -(-2 * count // 128) * 128))],
    )(*parts)
    iterate, first_row, second_row, first_col, second_col, result = call(
        functools.partial(second_solve, box),
        (cells, row, row, col, col, cells),
        [VMEM] * (12 + N_TABLES),
        [scratch(window.shape), spectral, middle, pltpu.SemaphoreType.DMA((long // 8,))],
        flops=4 * 10**9,
        out_spec=(VMEM,) * 5 + (anywhere,),
    )(local, *wide, *narrow, inverses, answers, *weights, load_window, *tables)
    narrow = exchange("narrow", first_col, second_col)
    wide = exchange("wide", first_row, second_row)
    rows, cols, inner = call(
        functools.partial(inner_residual, box),
        (f32(2, across, deep), f32(2, long, 8, deep), cells),
        [VMEM] * 6,
        [
            scratch((long + 2, box.cols, deep)),
            scratch((long, box.cols, deep)),
            pltpu.SemaphoreType.DMA((long // 8,)),
        ],
        flops=10**9,
        out_spec=(VMEM, VMEM, anywhere),
    )(load, iterate, *weights)
    residual = call(
        functools.partial(outer_residual, box),
        cells,
        [VMEM] * 9 + [anywhere],
        [
            scratch((2, across - 16, deep)),
            scratch((2, long, 8, deep)),
            pltpu.SemaphoreType.DMA((4,)),
        ],
        out_spec=anywhere,
        aliases={9: 0},
    )(iterate, *wide, *narrow, to_long, to_across, rows, cols, inner)
    return result, residual


def solution(mesh):
    split = P(("groups", "wide"), "narrow", None)
    return jax.shard_map(
        on_device,
        mesh=mesh,
        in_specs=(split, split, P(), P(), split),
        out_specs=(split, split),
        check_vma=False,
    )
```

```python
import functools

import jax
import jax.numpy as jnp
import ml_dtypes
import numpy as np
from jax import lax
from jax.experimental import pallas as pl
from jax.experimental.pallas import tpu as pltpu
from jax.sharding import PartitionSpec as P

MARGIN = 4
REACH = MARGIN + 1
EDGE = 8

cheb_center = 1.3
cheb_radius = 1.2
cheb_ratio = 1.3 / 1.2
rho_first = 1.0 / cheb_ratio
rho_second = 1.0 / (2.0 * cheb_ratio - rho_first)
gain = 2.0 * rho_second / cheb_radius

MEANS = range(4)
BOX_DIAGONAL, LONG_HIGH, LONG_LOW, ACROSS_HIGH, ACROSS_LOW, LOAD_SUM = range(4, 10)
IMAGE_SUM, FLOW_LONG_HIGH, FLOW_LONG_LOW, FLOW_ACROSS_HIGH, FLOW_ACROSS_LOW = range(16, 21)

VMEM = pl.BlockSpec(memory_space=pltpu.VMEM)
SMEM = pl.BlockSpec(memory_space=pltpu.SMEM)


def sine_basis(length):
    indices = np.arange(1, length + 1)
    phases = indices[:, None] * indices[None, :] % (2 * (length + 1))
    table = np.sqrt(2.0 / (length + 1)) * np.sin(np.pi * phases / (length + 1))
    eigvals = 4.0 * np.sin(np.pi * indices / (2.0 * (length + 1))) ** 2
    return table.astype(np.float32), eigvals.astype(np.float32)


def call(body, out_shape, in_specs, scratch=(), flops=0, out_spec=None, aliases=None):
    return pl.pallas_call(
        body,
        out_shape=out_shape,
        in_specs=in_specs,
        out_specs=out_spec or jax.tree.map(lambda _: VMEM, out_shape),
        scratch_shapes=list(scratch),
        compiler_params=pltpu.CompilerParams(vmem_limit_bytes=30 * 2**20),
        cost_estimate=pl.CostEstimate(flops=flops, bytes_accessed=0, transcendentals=0),
        input_output_aliases=aliases or {},
    )


def f32(*shape):
    return jax.ShapeDtypeStruct(shape, jnp.float32)


class Box:
    def __init__(self, shape):
        self.long, self.across, self.deep = shape
        self.ex = self.long + 2 * MARGIN
        self.ey = self.across + 2 * MARGIN
        self.rows = self.long + 2 * REACH
        self.cols = self.across + 2 * EDGE
        self.flat = self.rows * self.cols


def pieces(values, count):
    parts = []
    for _ in range(count - 1):
        scaled = values * 65537.0
        part = scaled - (scaled - values)
        parts.append(part)
        values = values - part
    return parts + [values]


def left_table(table, depth, count):
    rows, cols = table.shape
    wide = np.zeros((rows, depth), np.float32)
    wide[:, :cols] = table
    parts = []
    rest = wide
    for _ in range(count):
        part = rest.astype(ml_dtypes.bfloat16).astype(np.float32)
        parts.append(part)
        rest = rest - part
    blank = np.zeros_like(parts[0])
    lines = []
    for index in range(count):
        used = count - index if count > 2 else count
        lines.append(np.concatenate([parts[index]] * used + [blank] * (count - used), axis=1))
    return np.concatenate(lines, axis=0)


def right_tables(table):
    rest, parts = table, []
    for _ in range(3):
        part = rest.astype(ml_dtypes.bfloat16).astype(np.float32)
        parts.append(part)
        rest = rest - part
    both = np.concatenate([parts[0], parts[1]], axis=1)
    return np.concatenate([both, both], axis=0), np.concatenate([parts[2], parts[0]], axis=0)


def padded(size):
    return -(-size // 8) * 8


FORWARD, BACKWARD = 2, 3


def tables_of(box):
    sine_x, eig_x = sine_basis(box.ex)
    sine_y, eig_y = sine_basis(box.ey)
    sine_z, eig_z = sine_basis(box.deep)
    in_order_of_steps = np.arange(box.ey).reshape(8, box.ey // 8).T.reshape(-1)
    from_y = sine_y[MARGIN : MARGIN + box.across]
    from_x = sine_x[MARGIN : MARGIN + box.long]
    spread = np.broadcast_to(eig_x[:, None], (box.ex, box.deep))
    main_z, rest_z = right_tables(sine_z)
    return [
        jnp.asarray(np.ascontiguousarray(t))
        for t in (
            left_table(sine_y[:, in_order_of_steps], padded(box.ey), FORWARD),
            left_table(sine_x, padded(box.ex), FORWARD),
            left_table(from_x, padded(box.ex), BACKWARD),
            left_table(from_y, padded(box.ey), BACKWARD),
            main_z,
            rest_z,
            spread,
            eig_z[None, :],
            eig_y[None, :],
        )
    ]


N_TABLES = 9


def one_pass(left, right):
    return lax.dot_general(
        left,
        right,
        (((1,), (0,)), ((), ())),
        precision=lax.Precision.DEFAULT,
        preferred_element_type=jnp.float32,
    )


def dot_left(table, values, count, rows):
    total = one_pass(table, jnp.concatenate(pieces(values, count), axis=0))
    return sum(total[index * rows : (index + 1) * rows] for index in range(1, count)) + total[:rows]


def dot_right(values, main, rest, count):
    deep = values.shape[1]
    parts = pieces(values, count)
    total = one_pass(jnp.concatenate(parts[:2], axis=1), main)
    result = total[:, :deep] + total[:, deep:]
    if count == 3:
        result = result + one_pass(jnp.concatenate([parts[0], parts[2]], axis=1), rest)
    return result


def with_rows(values, rows):
    if values.shape[0] == rows:
        return values
    blank = jnp.zeros((rows - values.shape[0],) + values.shape[1:], values.dtype)
    return jnp.concatenate([values, blank], axis=0)


def box_solve(box, source, divided, tables, row_mask, col_mask, spectral, middle, emit):
    into_y, into_x, from_x, from_y, main_z, rest_z = tables[:6]
    deep = box.deep
    deep_x, deep_y = padded(box.ex), padded(box.ey)
    into_y, into_x = into_y[...], into_x[...]
    if col_mask is not None:
        mask = jnp.concatenate([col_mask] * FORWARD, axis=1)
        into_y = into_y * mask
        mask = jnp.concatenate([row_mask] * FORWARD, axis=1)
        into_x = into_x * mask
    from_x, from_y, main_z, rest_z = from_x[...], from_y[...], main_z[...], rest_z[...]
    spectral_flat = spectral.reshape(box.ey * deep_x, deep)
    middle_flat = middle.reshape(box.long * deep_y, deep)
    if deep_x > box.ex:
        spectral[:, box.ex :, :] = jnp.zeros((box.ey, deep_x - box.ex, deep), jnp.float32)
    if deep_y > box.ey:
        middle[:, box.ey :, :] = jnp.zeros((box.long, deep_y - box.ey, deep), jnp.float32)
    for start in range(0, box.ex, 8):
        block = source(start).reshape(8 * box.ey, deep)
        block = dot_right(block, main_z, rest_z, FORWARD).reshape(8, box.ey, deep)
        for row in range(0, 8, 2):
            pair = jnp.concatenate([block[row], block[row + 1]], axis=1)
            pair = dot_left(into_y, with_rows(pair, deep_y), FORWARD, box.ey)
            for part in range(2):
                spectral_flat[pl.ds(start + row + part, box.ey, stride=deep_x), :] = pair[
                    :, part * deep : (part + 1) * deep
                ]
    for col in range(0, box.ey, 2):
        pair = jnp.concatenate([spectral[col], spectral[col + 1]], axis=1)
        pair = dot_left(into_x, pair, FORWARD, box.ex)
        pair = jnp.concatenate(
            [
                divided(pair[:, part * deep : (part + 1) * deep], col + part)
                for part in range(2)
            ],
            axis=1,
        )
        pair = dot_left(from_x, with_rows(pair, deep_x), BACKWARD, box.long)
        for part in range(2):
            middle_flat[pl.ds(col + part, box.long, stride=deep_y), :] = pair[
                :, part * deep : (part + 1) * deep
            ]
    for start in range(0, box.long, 8):
        parts = []
        for row in range(start, start + 8, 2):
            pair = jnp.concatenate([middle[row], middle[row + 1]], axis=1)
            pair = dot_left(from_y, pair, BACKWARD, box.across)
            parts += [pair[:, :deep], pair[:, deep:]]
        emit(start, dot_right(jnp.concatenate(parts, axis=0), main_z, rest_z, BACKWARD))


def position():
    long_pos, across_pos = lax.axis_index("wide"), lax.axis_index("narrow")
    return long_pos, across_pos, lax.axis_size("wide"), lax.axis_size("narrow")


def as_float(flag):
    return jnp.where(flag, jnp.float32(1.0), jnp.float32(0.0))


def is_even(axis):
    return lax.rem(lax.axis_index(axis), 2) == 0


class Sides:
    def __init__(self, axis, first, second):
        position = lax.axis_index(axis)
        self.even = is_even(axis)
        self.has_low = as_float(position > 0)
        self.has_high = as_float(position < lax.axis_size(axis) - 1)
        self.first, self.second = first, second

    def low(self, *index):
        return jnp.where(self.even, self.second[index], self.first[index]) * self.has_low

    def high(self, *index):
        return jnp.where(self.even, self.first[index], self.second[index]) * self.has_high


def in_order(even, up, down):
    return jnp.where(even, up, down), jnp.where(even, down, up)


def row_of(stride, col, count, first=0):
    return pl.ds(first * stride + col, count, stride=stride)


def pack_columns(box, fields, wide_sides, wide, first, second):
    corner = len(fields) * wide * box.long
    even = is_even("narrow")
    place = 0
    for field, sides in zip(fields, wide_sides):
        for step in range(wide):
            cols = (box.across - wide + step, step)
            values = [field[row_of(box.across, col, box.long), :] for col in cols]
            low = [sides.low(row_of(box.across, col, wide), slice(None)) for col in cols]
            high = [sides.high(row_of(box.across, col, wide), slice(None)) for col in cols]
            at = corner + 2 * REACH * place
            for start, parts in ((place * box.long, values), (at, low), (at + REACH, high)):
                parts = in_order(even, *(part.astype(jnp.float32) for part in parts))
                size = parts[0].shape[0]
                first[start : start + size, :], second[start : start + size, :] = parts
            place += 1


def message_rows(box, count):
    return -(-(count * (box.long + 2 * REACH)) // 8) * 8


def pack_fields(box, wide, fields, tables, after, *refs):
    own, (low, high), refs = refs[:fields], refs[fields : fields + 2], refs[fields + 2 :]
    parts, (first, second, *table) = refs[:tables], refs[tables + after :]
    size = wide * box.across
    flat = [field.reshape(box.long * box.across, box.deep) for field in own]
    low = low.reshape(low.size // box.deep, box.deep)
    high = high.reshape(high.size // box.deep, box.deep)
    sides = [
        Sides("wide", *(ref.at[index * size : (index + 1) * size] for ref in (low, high)))
        for index in range(fields)
    ]
    pack_columns(box, flat, sides, wide, first, second)
    if tables:
        known = last_rows_merged(parts, table[0].shape[0])
        table[0][...] = known
        first[first.shape[0] - known.shape[0] :, :] = known
        second[second.shape[0] - known.shape[0] :, :] = known


def bring_edges(
    box, zone, scale, load, own_zone, own_scale, own_load, load_first, load_second, first, second,
    staged, sems
):
    even = is_even("wide")

    def edges(wide):
        up, down = box.long - wide, 0
        return [pl.ds(jnp.where(even, *pair), wide) for pair in ((up, down), (down, up))]

    copies = [
        (load.at[edges(MARGIN)[0]], load_first),
        (load.at[edges(MARGIN)[1]], load_second),
        (zone.at[edges(REACH)[0]], staged.at[0]),
        (zone.at[edges(REACH)[1]], staged.at[1]),
        (scale.at[edges(REACH)[0]], first.at[:REACH]),
        (scale.at[edges(REACH)[1]], second.at[:REACH]),
        (load, own_load),
        (scale, own_scale),
        (zone, own_zone),
    ]
    copies = [
        pltpu.make_async_copy(source, target, sems.at[index])
        for index, (source, target) in enumerate(copies)
    ]
    for copy in copies:
        copy.start()
    for copy in copies[:4]:
        copy.wait()
    first[REACH:] = staged[0].astype(jnp.float32)
    second[REACH:] = staged[1].astype(jnp.float32)
    for copy in copies[4:]:
        copy.wait()


def fill_window(box, window, own, wide_sides, narrow_sides, wide, place, total, add=None):
    flat = window.reshape(box.flat, box.deep)
    nothing = jnp.zeros((box.rows, EDGE, box.deep), jnp.float32)
    window[:, :EDGE, :] = nothing
    window[:, EDGE + box.across :, :] = nothing
    if add is None:
        add = lambda values, row_side, col_side: values
    inner = slice(EDGE, EDGE + box.across)
    first, last = REACH, REACH + box.long
    if wide < REACH:
        blank = jnp.zeros((1, box.across, box.deep), jnp.float32)
        window[0:1, inner, :] = blank
        window[box.rows - 1 :, inner, :] = blank
    window[first:last, inner, :] = add(own[...].astype(jnp.float32), 0, 0)
    window[first - wide : first, inner, :] = add(wide_sides.low(Ellipsis), -1, 0)
    window[last : last + wide, inner, :] = add(wide_sides.high(Ellipsis), 1, 0)
    corner = total * box.long
    for step in range(wide):
        for source, col, side in (
            (narrow_sides.low, EDGE - wide + step, -1),
            (narrow_sides.high, EDGE + box.across + step, 1),
        ):
            for start, size, row, row_side in (
                ((place + step) * box.long, box.long, first, 0),
                (corner + 2 * REACH * (place + step), wide, first - wide, -1),
                (corner + 2 * REACH * (place + step) + REACH, wide, last, 1),
            ):
                values = source(slice(start, start + size), slice(None))
                flat[row_of(box.cols, col, size, row), :] = add(values, row_side, side)


def some_cols(box, ref, row, step):
    stride = box.ey // 8
    return ref[row, pl.ds(EDGE - MARGIN + step, 8, stride=stride), :]


def negative_image(box, window, row, at, x, flow_before, weights):
    to_long, to_across, to_deep, mass = weights
    steps = range(box.ey // 8)
    x_next = [some_cols(box, window, row + 1, step) for step in range(-1, len(steps) + 1)]
    flow_long = [
        some_cols(box, to_long, at, step) * (x_next[step + 1] - x[step + 1]) for step in steps
    ]
    flow_across = [
        some_cols(box, to_across, at, step) * (x[step + 2] - x[step + 1])
        for step in range(-1, len(steps))
    ]
    totals = []
    for step in steps:
        here = x[step + 1]
        lanes = here.shape[1]
        flow_deep = some_cols(box, to_deep, at, step) * (pltpu.roll(here, lanes - 1, 1) - here)
        total = flow_long[step] - flow_before[step] - some_cols(box, mass, at, step) * here
        total = total + (flow_across[step + 1] - flow_across[step])
        totals.append(total + (flow_deep - pltpu.roll(flow_deep, 1, 1)))
    return totals, x_next, flow_long


def in_steps(box, refs, rows):
    return jnp.stack(
        [
            jnp.concatenate([some_cols(box, ref, row, step) for step in range(box.ey // 8)], axis=0)
            for ref, row in zip(refs, rows)
        ]
    )


def looked_up(labels, values):
    return jnp.where(labels == 0, values[0], jnp.where(labels == 1, values[1], values[2]))


def at_own_row(line, shape):
    long_pos, across_pos, _, across_count = position()
    rows = lax.broadcasted_iota(jnp.int32, shape, 0)
    own = rows == long_pos * across_count + across_pos
    return jnp.where(own, line[:1], jnp.zeros(shape, jnp.float32))


def merged(table, *others):
    for other in others:
        table = jnp.where(table != 0.0, table, other)
    return table


def last_rows_merged(refs, count):
    return merged(*(ref[ref.shape[0] - count :, :] for ref in refs))


def join_rows(table, message, out):
    out[...] = last_rows_merged((table, message), out.shape[0])


def line_of(numbers, shape):
    lanes = lax.broadcasted_iota(jnp.int32, shape, 1)
    line = jnp.zeros(shape, jnp.float32)
    for index, number in numbers:
        line = jnp.where(lanes == index, number, line)
    return line


def box_sums(box, zone, scale, load, after, diffusivity, decay, out, table):
    del after
    nothing = jnp.zeros((box.across, box.deep), jnp.float32)
    half = [[0.5 * diffusivity[z, d] for z in range(3)] for d in range(3)]
    rates = [decay[z] for z in range(3)]

    def halves(row):
        labels, factor = zone[row], scale[row]
        return [looked_up(labels, half[d]) * factor for d in range(3)] + [looked_up(labels, rates)]

    sums = [nothing] * 5
    for row in range(box.long):
        sums = [total + more for total, more in zip(sums, halves(row) + [load[row]])]

    def total(values):
        return jnp.sum(values, keepdims=True).reshape(1, 1)

    cells = box.long * box.across * box.deep
    numbers = [(index, total(sums[index]) * (2.0 / cells)) for index in range(3)]
    mass = total(sums[3])
    numbers += [(3, mass / cells)]
    ends = total(sums[2][:, :1]) + total(sums[2][:, box.deep - 1 :])
    numbers += [
        (BOX_DIAGONAL, mass + ends),
        (LONG_HIGH, total(halves(box.long - 1)[0])),
        (LONG_LOW, total(halves(0)[0])),
        (ACROSS_HIGH, total(sums[1][box.across - 1 :])),
        (ACROSS_LOW, total(sums[1][:1])),
        (LOAD_SUM, total(sums[4])),
    ]
    line = line_of(numbers, out.shape)
    out[...] = line
    table[...] = at_own_row(line, table.shape)


def means_of(ref):
    return [ref[0:1, index : index + 1] for index in range(4)]


def first_solve(box, load, low, high, left, right, means, zone, scale, diffusivity, decay, *rest):
    tables = rest[:N_TABLES]
    window, local, image, inverses, spectral, middle = rest[N_TABLES:]
    spread, eig_z, eig_y = tables[6:]
    means = means_of(means)
    base = means[3] + means[0] * spread[...] + means[2] * eig_z[...]

    def divided(values, col):
        divisor = base + means[1] * eig_y[0, col]
        inverse = pl.reciprocal(divisor, approx=True)
        for _ in range(2):
            inverse = inverse * (2.0 - divisor * inverse)
        inverses[col] = inverse
        return values * inverse

    half = [0.5 * diffusivity[z, 2] for z in range(3)]
    rates = [decay[z] for z in range(3)]
    lane = lax.broadcasted_iota(jnp.int32, (box.across, box.deep), 1)
    ends = jnp.where((lane == 0) | (lane == box.deep - 1), jnp.float32(1.0), jnp.float32(0.0))
    image[...] = jnp.zeros((box.across, box.deep), jnp.float32)
    wide_sides, narrow_sides = Sides("wide", low, high), Sides("narrow", left, right)
    fill_window(box, window, load, wide_sides, narrow_sides, MARGIN, 0, MARGIN)

    def emit(start, values):
        values = values * (1.0 / cheb_center)
        values = values.reshape(8, box.across, box.deep)
        local[start : start + 8] = values
        total = image[...]
        for row in range(8):
            labels = zone[start + row]
            mass = looked_up(labels, rates) + looked_up(labels, half) * scale[start + row] * ends
            total = total + mass * values[row]
        image[...] = total

    box_solve(
        box,
        lambda start: in_steps(box, [window] * 8, range(1 + start, 9 + start)),
        divided,
        tables,
        None,
        None,
        spectral,
        middle,
        emit,
    )


def side_weights(
    box, zone, scale, low, high, left, right, diffusivity, to_long, to_across, zone_window,
    scale_window
):
    for index, (window, own) in enumerate(((scale_window, scale), (zone_window, zone))):
        start = index * REACH
        wide_sides = Sides("wide", *(ref.at[start : start + REACH] for ref in (low, high)))
        narrow_sides = Sides("narrow", left, right)
        fill_window(box, window, own, wide_sides, narrow_sides, REACH, start, 2 * REACH)
    half = [[0.5 * diffusivity[z, d] for z in range(3)] for d in range(2)]

    def one_row(row, before):
        labels, factor = zone_window[row], scale_window[row]
        now = [looked_up(labels, half[d]) * factor for d in range(2)]
        to_across[row] = now[1] + pltpu.roll(now[1], box.cols - 1, 0)
        to_long[jnp.maximum(row - 1, 0)] = before + now[0]
        return now[0]

    def some_rows(index, before):
        for row in range(8):
            before = one_row(index * 8 + row, before)
        return before

    before = jnp.zeros((box.cols, box.deep), jnp.float32)
    before = lax.fori_loop(0, box.rows // 8, some_rows, before)
    for row in range(box.rows // 8 * 8, box.rows):
        before = one_row(row, before)
    to_long[box.rows - 1] = before


def deep_weights(box, zone_window, scale_window, diffusivity, decay, to_deep, mass):
    half = [0.5 * diffusivity[z, 2] for z in range(3)]
    rates = [decay[z] for z in range(3)]
    lane = lax.broadcasted_iota(jnp.int32, (box.cols, box.deep), 1)
    ends = jnp.where((lane == 0) | (lane == box.deep - 1), jnp.float32(1.0), jnp.float32(0.0))
    not_last = jnp.where(lane == box.deep - 1, jnp.float32(0.0), jnp.float32(1.0))

    def one_row(row):
        labels = zone_window[row]
        now = looked_up(labels, half) * scale_window[row]
        to_deep[row] = (now + pltpu.roll(now, box.deep - 1, 1)) * not_last
        mass[row] = looked_up(labels, rates) + now * ends

    def some_rows(index, _):
        for row in range(8):
            one_row(index * 8 + row)
        return 0

    lax.fori_loop(0, box.rows // 8, some_rows, 0)
    for row in range(box.rows // 8 * 8, box.rows):
        one_row(row)


def image_sums(
    box, zone, scale, local, image, low, high, left, right, table, diffusivity, out, up, down
):
    half = [[0.5 * diffusivity[z, d] for z in range(3)] for d in range(3)]
    shape = (box.long * box.across, box.deep)
    zone_flat, scale_flat, local_flat = zone.reshape(shape), scale.reshape(shape), local.reshape(shape)
    last_col = row_of(box.across, box.across - 1, box.long)
    first_col = row_of(box.across, 0, box.long)

    wide_sides, narrow_sides = Sides("wide", low, high), Sides("narrow", left, right)

    def side(source, place):
        return source(slice(place * box.long, (place + 1) * box.long), slice(None))

    above, below = wide_sides.high, wide_sides.low
    faces = [
        (0, zone[box.long - 1], scale[box.long - 1], local[box.long - 1], above(REACH), above(0)),
        (0, zone[0], scale[0], local[0], below(2 * REACH - 1), below(REACH - 1)),
        (
            1,
            zone_flat[last_col, :],
            scale_flat[last_col, :],
            local_flat[last_col, :],
            side(narrow_sides.high, REACH),
            side(narrow_sides.high, 0),
        ),
        (
            1,
            zone_flat[first_col, :],
            scale_flat[first_col, :],
            local_flat[first_col, :],
            side(narrow_sides.low, 2 * REACH - 1),
            side(narrow_sides.low, REACH - 1),
        ),
    ]
    flows = []
    for direction, labels, factor, values, far_labels, far_factor in faces:
        weight = looked_up(labels, half[direction]) * factor
        weight = weight + looked_up(far_labels, half[direction]) * far_factor
        flows.append(jnp.sum(weight * values, keepdims=True))
    long_pos, across_pos, long_count, across_count = position()
    numbers = [
        (IMAGE_SUM, jnp.sum(image[...], keepdims=True) + sum(flows)),
        (FLOW_LONG_HIGH, flows[0] * as_float(long_pos < long_count - 1)),
        (FLOW_LONG_LOW, flows[1] * as_float(long_pos > 0)),
        (FLOW_ACROSS_HIGH, flows[2] * as_float(across_pos < across_count - 1)),
        (FLOW_ACROSS_LOW, flows[3] * as_float(across_pos > 0)),
    ]
    known = table[...] + at_own_row(line_of(numbers, (8, out.shape[1])), out.shape)
    out[...] = known
    edge = REACH * box.across
    even = is_even("wide")
    for target, pair in ((up, (box.long - REACH, 0)), (down, (0, box.long - REACH))):
        target[:edge] = local[pl.ds(jnp.where(even, *pair), REACH)].reshape(edge, box.deep)
        target[edge:] = known


def column(values, index):
    return values[:, index : index + 1]


def coarse_inverse(numbers, work):
    count, width = work.shape
    across = lax.axis_size("narrow")
    beyond = pltpu.roll(numbers, count - across, 0)
    beside = pltpu.roll(numbers, count - 1, 0)
    before = pltpu.roll(numbers, across, 0)
    ahead = pltpu.roll(numbers, 1, 0)
    place = lax.broadcasted_iota(jnp.int32, (count, 1), 0)
    across_pos = lax.rem(place, across)
    nothing = jnp.zeros((count, 1), jnp.float32)
    couplings = []
    diagonal = column(numbers, BOX_DIAGONAL)
    for own, other, there, inside in (
        (LONG_HIGH, LONG_LOW, beyond, place < count - across),
        (LONG_LOW, LONG_HIGH, before, place >= across),
        (ACROSS_HIGH, ACROSS_LOW, beside, across_pos < across - 1),
        (ACROSS_LOW, ACROSS_HIGH, ahead, across_pos > 0),
    ):
        shared = jnp.where(inside, column(there, other), nothing)
        diagonal = diagonal + column(numbers, own) + shared
        couplings.append(jnp.where(inside, column(numbers, own) + shared, nothing))
    rows = lax.broadcasted_iota(jnp.int32, (count, width), 0)
    cols = lax.broadcasted_iota(jnp.int32, (count, width), 1)
    blank = jnp.zeros((count, width), jnp.float32)
    matrix = jnp.where(cols == rows, diagonal, blank)
    for shift, coupling in zip((across, -across, 1, -1), couplings):
        matrix = matrix - jnp.where((cols == rows + shift) & (cols < count), coupling, blank)
    matrix = jnp.where(cols == rows + count, jnp.ones((count, 1), jnp.float32), matrix)
    if count <= 16:
        for step in range(count):
            pivot_row = matrix[step : step + 1, :] / matrix[step : step + 1, step : step + 1]
            rest = matrix - matrix[:, step : step + 1] * pivot_row
            matrix = jnp.where(rows == step, pivot_row, rest)
        return pltpu.roll(matrix, width - count, 1)
    work[...] = matrix

    def eliminate(step, _):
        values = work[...]
        pivot_row = work[pl.ds(step, 1), :]
        at_step = cols == step
        factors = jnp.sum(jnp.where(at_step, values, blank), axis=1, keepdims=True)
        pivot = jnp.sum(jnp.where(at_step[:1], pivot_row, blank[:1]), axis=1, keepdims=True)
        pivot_row = pivot_row / pivot
        work[...] = jnp.where(rows == step, pivot_row, values - factors * pivot_row)
        return 0

    lax.fori_loop(0, count, eliminate, 0)
    values = work[...]
    if count % 128:
        return pltpu.roll(values, width - count, 1)
    return values[:, count : 2 * count]


def answer(inverse, sums):
    return jnp.sum(inverse * sums, axis=0, keepdims=True)


def at_box(values, row_side, col_side):
    long_pos, across_pos, long_count, across_count = position()
    there_long, there_across = long_pos + row_side, across_pos + col_side
    inside = (
        (there_long >= 0)
        & (there_long < long_count)
        & (there_across >= 0)
        & (there_across < across_count)
    )
    lanes = lax.broadcasted_iota(jnp.int32, values.shape, 1)
    wanted = (lanes == there_long * across_count + there_across) & inside
    return jnp.sum(jnp.where(wanted, values, jnp.zeros_like(values)), axis=1, keepdims=True)


def coarse_corrections(parts, *refs):
    table_parts, (out, work) = refs[:parts], refs[parts:]
    count = work.shape[0]
    numbers = last_rows_merged(table_parts, count)
    across_count = lax.axis_size("narrow")
    inverse = coarse_inverse(numbers, work)
    sums = column(numbers, IMAGE_SUM)
    sums = sums - column(pltpu.roll(numbers, count - across_count, 0), FLOW_LONG_LOW)
    sums = sums - column(pltpu.roll(numbers, across_count, 0), FLOW_LONG_HIGH)
    sums = sums - column(pltpu.roll(numbers, count - 1, 0), FLOW_ACROSS_LOW)
    sums = sums - column(pltpu.roll(numbers, 1, 0), FLOW_ACROSS_HIGH)
    load_sums = column(numbers, LOAD_SUM)
    sums = load_sums * (1.0 - 1.0 / cheb_center) - sums
    out[0:1, :] = answer(inverse, load_sums) * (1.0 / cheb_center)
    out[1:2, :] = answer(inverse, sums) * gain


def second_solve(box, local, low, high, left, right, inverses, answers, *rest):
    to_long, to_across, to_deep, mass, load_window = rest[:5]
    tables = rest[5 : 5 + N_TABLES]
    iterate, top, bottom, last_col, first_col, out = rest[5 + N_TABLES : 11 + N_TABLES]
    window, spectral, middle, sems = rest[11 + N_TABLES :]
    long_pos, across_pos, long_count, across_count = position()
    coarse = answers[0:1, :]
    own_shift = at_box(answers[1:2, :], 0, 0)
    shifts = {
        (row_side, col_side): at_box(coarse, row_side, col_side)
        for row_side in (-1, 0, 1)
        for col_side in (-1, 0, 1)
    }

    def add(values, row_side, col_side):
        shift = shifts[row_side, col_side]
        if values.ndim == 3:
            shift = shift.reshape(1, 1, 1)
        return values + shift

    edge = REACH * box.across
    low, high = (
        ref.at[:edge].reshape(REACH, box.across, box.deep) for ref in (low, high)
    )
    wide_sides, narrow_sides = Sides("wide", low, high), Sides("narrow", left, right)
    fill_window(box, window, local, wide_sides, narrow_sides, REACH, 0, REACH, add)
    weights = (to_long, to_across, to_deep, mass)

    steps = range(box.ey // 8)
    x = [some_cols(box, window, 1, step) for step in range(-1, len(steps) + 1)]
    flow = [
        some_cols(box, to_long, 0, step) * (x[step + 1] - some_cols(box, window, 0, step))
        for step in steps
    ]
    state = [x, flow]

    def divided(values, col):
        return values * inverses[col]

    def residual(start_row):
        rows = []
        for row in range(start_row + 1, start_row + 9):
            image, *state[:] = negative_image(box, window, row, row, *state, weights)
            image = [some_cols(box, load_window, row, step) + image[step] for step in steps]
            rows.append(jnp.concatenate(image, axis=0))
        return jnp.stack(rows)

    inner = slice(EDGE, EDGE + box.across)
    first = REACH
    row_ids = lax.broadcasted_iota(jnp.int32, (1, padded(box.ex)), 1)
    col_ids = lax.broadcasted_iota(jnp.int32, (1, padded(box.ey)), 1)
    col_ids = (col_ids & 7) * (box.ey // 8) + lax.shift_right_logical(col_ids, 3)
    row_mask = jnp.where(row_ids < MARGIN, as_float(long_pos > 0), 1.0)
    row_mask = jnp.where(row_ids >= MARGIN + box.long, as_float(long_pos < long_count - 1), row_mask)
    col_mask = jnp.where(col_ids < MARGIN, as_float(across_pos > 0), 1.0)
    col_mask = jnp.where(
        col_ids >= MARGIN + box.across, as_float(across_pos < across_count - 1), col_mask
    )
    keep = 1.0 + rho_second * rho_first
    copies = []

    def emit(start, values):
        rows = values.reshape(8, box.across, box.deep)
        before = window[first + start : first + start + 8, inner, :]
        shift = own_shift.reshape(1, 1, 1)
        iterate[start : start + 8] = keep * before + (gain * rows + shift)
        copies.append(
            pltpu.make_async_copy(
                iterate.at[start : start + 8], out.at[start : start + 8], sems.at[len(copies)]
            )
        )
        copies[-1].start()

    box_solve(
        box, residual, divided, tables, row_mask, col_mask, spectral, middle, emit
    )
    rows = in_order(is_even("wide"), iterate[box.long - 1], iterate[0])
    top[...], bottom[...] = rows
    flat = iterate.reshape(box.long * box.across, box.deep)
    cols = [flat[row_of(box.across, col, box.long), :] for col in (box.across - 1, 0)]
    last_col[...], first_col[...] = in_order(is_even("narrow"), *cols)
    for copy in copies:
        copy.wait()


def inner_residual(
    box, load, iterate, to_long, to_across, to_deep, mass, rows, cols, out, window, result, sems
):
    inner = slice(EDGE, EDGE + box.across)
    flat = window.reshape((box.long + 2) * box.cols, box.deep)
    iterate_flat = iterate.reshape(box.long * box.across, box.deep)
    blank = jnp.zeros((box.long + 2, EDGE, box.deep), jnp.float32)
    window[:, :EDGE, :] = blank
    window[:, EDGE + box.across :, :] = blank
    window[1 : 1 + box.long, inner, :] = iterate[...]
    window[0, inner, :] = iterate[0]
    window[1 + box.long, inner, :] = iterate[box.long - 1]
    for col, place in ((0, EDGE - 1), (box.across - 1, EDGE + box.across)):
        values = iterate_flat[row_of(box.across, col, box.long), :]
        flat[row_of(box.cols, place, box.long, 1), :] = values
    weights = (to_long, to_across, to_deep, mass)
    steps = range(box.ey // 8)
    x = [some_cols(box, window, 1, step) for step in range(-1, len(steps) + 1)]
    flow = [jnp.zeros((8, box.deep), jnp.float32) for _ in steps]
    middle = slice(8, box.across - 8)
    copies = []
    for row in range(box.long):
        image, x, flow = negative_image(box, window, row + 1, REACH + row, x, flow, weights)
        for step in steps:
            place = pl.ds(EDGE - MARGIN + step, 8, stride=box.ey // 8)
            result[row, place, :] = image[step]
        values = load[row] + result[row, inner]
        result[row, inner] = values
        cols[0, row] = values[:8]
        cols[1, row] = values[box.across - 8 :]
        if row == 0:
            rows[0] = values
        if row == box.long - 1:
            rows[1] = values
        if row % 8 == 7:
            part = slice(row - 7, row + 1)
            copy = pltpu.make_async_copy(
                result.at[part, EDGE + 8 : EDGE + box.across - 8],
                out.at[part, middle],
                sems.at[row // 8],
            )
            copy.start()
            copies.append(copy)
    for copy in copies:
        copy.wait()


def outer_residual(
    box, iterate, low, high, left, right, to_long, to_across, rows, cols, inner_out, out,
    row_part, col_part, sems
):
    del inner_out
    inner = slice(EDGE, EDGE + box.across)
    middle = slice(8, box.across - 8)
    wide_sides, narrow_sides = Sides("wide", low, high), Sides("narrow", left, right)
    last = box.long - 1
    iterate_flat = iterate.reshape(box.long * box.across, box.deep)
    across_flat = to_across.reshape(box.flat, box.deep)
    below = to_long[REACH - 1, inner] * (wide_sides.low(Ellipsis) - iterate[0])
    above = to_long[REACH + last, inner] * (wide_sides.high(Ellipsis) - iterate[last])
    row_part[0] = (rows[0] + below)[middle]
    row_part[1] = (rows[1] + above)[middle]
    copies = [
        pltpu.make_async_copy(row_part.at[0], out.at[0, middle], sems.at[0]),
        pltpu.make_async_copy(row_part.at[1], out.at[last, middle], sems.at[1]),
    ]
    for copy in copies:
        copy.start()
    col_part[...] = cols[...]
    flat = col_part.reshape(2 * box.long * 8, box.deep)
    for side, (from_side, col, face, tile) in enumerate(
        (
            (narrow_sides.low, 0, EDGE - 1, slice(0, 8)),
            (narrow_sides.high, box.across - 1, EDGE + box.across - 1, slice(box.across - 8, None)),
        )
    ):
        weight = across_flat[row_of(box.cols, face, box.long, REACH), :]
        own = iterate_flat[row_of(box.across, col, box.long), :]
        place = pl.ds(side * box.long * 8 + side * 7, box.long, stride=8)
        flat[place, :] = flat[place, :] + weight * (from_side(Ellipsis) - own)
        col_part[side, 0] = col_part[side, 0] + below[tile]
        col_part[side, last] = col_part[side, last] + above[tile]
        first_col = side * (box.across - 8)
        copy = pltpu.make_async_copy(
            col_part.at[side], out.at[:, first_col : first_col + 8], sems.at[2 + side]
        )
        copy.start()
        copies.append(copy)
    for copy in copies:
        copy.wait()


def swaps(axis, around):
    sizes = (lax.axis_size("wide"), lax.axis_size("narrow"))
    along = ("wide", "narrow").index(axis)
    size, beside = sizes[along], sizes[1 - along]

    def number(place, other_place):
        pair = (place, other_place) if along == 0 else (other_place, place)
        return pair[0] * sizes[1] + pair[1]

    ways = []
    for way in range(2):
        pairs = []
        for place in range(size):
            for other_place in range(beside):
                partner = place + 1 if place % 2 == way else place - 1
                there = other_place
                if around and size % 2 == 0:
                    partner %= size
                if not 0 <= partner < size:
                    partner = place
                    there = other_place ^ 1 if beside % 2 == 0 else other_place
                pairs.append((number(place, other_place), number(partner, there)))
        ways.append(pairs)
    return ways


def exchange(axis, first, second, around=False):
    ways = swaps(axis, around)
    axes = ("wide", "narrow")
    return lax.ppermute(first, axes, ways[0]), lax.ppermute(second, axes, ways[1])


def two_away(axis, table):
    size = lax.axis_size(axis)
    return lax.ppermute(table, axis, [(i, (i + 2) % size) for i in range(size)])


def tell(table):
    count = table.shape[0]
    long_pos, across_pos, _, across_count = position()
    own = lax.dynamic_slice_in_dim(table, long_pos * across_count + across_pos, 1, axis=0)
    line = jnp.broadcast_to(own, (count, 1, 128))
    told = lax.all_to_all(line, ("wide", "narrow"), split_axis=0, concat_axis=0, tiled=True)
    return told.reshape(count, 128)


def on_device(zone, scale, diffusivity, decay, load):
    box = Box(load.shape)
    long, across, deep = load.shape
    count = lax.axis_size("wide") * lax.axis_size("narrow")
    by_margins = lax.axis_size("wide") == 4 and lax.axis_size("narrow") == 4
    tables = tables_of(box)
    cells = f32(long, across, deep)
    whole_zone = jax.ShapeDtypeStruct(cells.shape, zone.dtype)
    window = f32(box.rows, box.cols, deep)
    table_shape = f32(count, 128)
    anywhere = pl.BlockSpec(memory_space=pl.ANY)
    in_hbm = pl.BlockSpec(memory_space=pltpu.HBM)

    def scratch(shape):
        return pltpu.VMEM(shape, jnp.float32)

    def pinned(field):
        return pltpu.with_memory_space_constraint(field, pltpu.HBM)

    spectral = scratch((box.ey, padded(box.ex), deep))
    middle = scratch((long, padded(box.ey), deep))

    def pack(wide, fields, sides, parts=(), after=()):
        rows = message_rows(box, wide * len(fields)) + (count if parts else 0)
        message = f32(rows, deep)
        body = functools.partial(pack_fields, box, wide, len(fields), len(parts), len(after))
        return call(
            body,
            (message, message) + ((table_shape,) if parts else ()),
            [VMEM] * (len(fields) + 2 + len(parts)) + [anywhere] * len(after),
        )(*fields, *sides, *parts, *after)

    far = f32(2 * REACH, across, deep)
    zone, scale, load, load_first, load_second, first, second = call(
        functools.partial(bring_edges, box),
        (whole_zone, cells, cells) + (f32(MARGIN, across, deep),) * 2 + (far, far),
        [in_hbm] * 3,
        [pltpu.VMEM((2, REACH, across, deep), zone.dtype), pltpu.SemaphoreType.DMA((9,))],
    )(pinned(zone), pinned(scale), pinned(load))
    load_wide = exchange("wide", load_first, load_second)
    far_wide = exchange("wide", first, second)
    load_first, load_second = pack(MARGIN, [load], load_wide)
    load_narrow = exchange("narrow", load_first, load_second)
    sums, table = call(
        functools.partial(box_sums, box),
        (f32(8, 128), table_shape),
        [VMEM] * 3 + [anywhere] + [SMEM] * 2,
    )(zone, scale, load, load_first, diffusivity, decay)
    far_narrow = exchange("narrow", *pack(REACH, [scale, zone], far_wide))
    load_window, local, image, inverses = call(
        functools.partial(first_solve, box),
        (window, cells, f32(across, deep), f32(box.ey, box.ex, deep)),
        [VMEM] * 8 + [SMEM] * 2 + [VMEM] * N_TABLES,
        [spectral, middle],
        flops=4 * 10**9,
    )(load, *load_wide, *load_narrow, sums, zone, scale, diffusivity, decay, *tables)
    message = f32(REACH * across + count, deep)
    table, first, second = call(
        functools.partial(image_sums, box), (table_shape, message, message), [VMEM] * 9 + [SMEM]
    )(zone, scale, local, image, *far_wide, *far_narrow, table, diffusivity)
    own_table = table
    wide = exchange("wide", first, second, by_margins)
    parts = (table, *wide)
    if by_margins:
        parts += (two_away("wide", table),)
    to_long, to_across, *windows = call(
        functools.partial(side_weights, box),
        (window,) * 4,
        [VMEM] * 6 + [SMEM],
        flops=10**9,
    )(zone, scale, *far_wide, *far_narrow, diffusivity)
    to_deep, mass = call(
        functools.partial(deep_weights, box),
        (window,) * 2,
        [VMEM] * 2 + [SMEM] * 2,
        flops=10**9,
    )(*windows, diffusivity, decay)
    weights = (to_long, to_across, to_deep, mass)
    first, second, table = pack(REACH, [local], wide, parts, [to_long])
    narrow = exchange("narrow", first, second)
    if by_margins:
        table = call(join_rows, table_shape, [VMEM] * 2)(table, narrow[0])
        parts = (table, two_away("narrow", table))
    else:
        parts = (tell(own_table),)
    row, col = f32(across, deep), f32(long, deep)
    answers = call(
        functools.partial(coarse_corrections, len(parts)),
        f32(8, -(-count // 128) * 128),
        [VMEM] * len(parts),
        [scratch((count, -(-2 * count // 128) * 128))],
    )(*parts)
    iterate, first_row, second_row, first_col, second_col, result = call(
        functools.partial(second_solve, box),
        (cells, row, row, col, col, cells),
        [VMEM] * (12 + N_TABLES),
        [scratch(window.shape), spectral, middle, pltpu.SemaphoreType.DMA((long // 8,))],
        flops=4 * 10**9,
        out_spec=(VMEM,) * 5 + (anywhere,),
    )(local, *wide, *narrow, inverses, answers, *weights, load_window, *tables)
    narrow = exchange("narrow", first_col, second_col)
    wide = exchange("wide", first_row, second_row)
    rows, cols, inner = call(
        functools.partial(inner_residual, box),
        (f32(2, across, deep), f32(2, long, 8, deep), cells),
        [VMEM] * 6,
        [
            scratch((long + 2, box.cols, deep)),
            scratch((long, box.cols, deep)),
            pltpu.SemaphoreType.DMA((long // 8,)),
        ],
        flops=10**9,
        out_spec=(VMEM, VMEM, anywhere),
    )(load, iterate, *weights)
    residual = call(
        functools.partial(outer_residual, box),
        cells,
        [VMEM] * 9 + [anywhere],
        [
            scratch((2, across - 16, deep)),
            scratch((2, long, 8, deep)),
            pltpu.SemaphoreType.DMA((4,)),
        ],
        out_spec=anywhere,
        aliases={9: 0},
    )(iterate, *wide, *narrow, to_long, to_across, rows, cols, inner)
    return result, residual


def solution(mesh):
    split = P(("groups", "wide"), "narrow", None)
    return jax.shard_map(
        on_device,
        mesh=mesh,
        in_specs=(split, split, P(), P(), split),
        out_specs=(split, split),
        check_vma=False,
    )
```

```python
import functools

import jax
import jax.numpy as jnp
import ml_dtypes
import numpy as np
from jax import lax
from jax.experimental import pallas as pl
from jax.experimental.pallas import tpu as pltpu
from jax.sharding import PartitionSpec as P

MARGIN = 4
REACH = MARGIN + 1
EDGE = 8

cheb_center = 1.3
cheb_radius = 1.2
cheb_ratio = 1.3 / 1.2
rho_first = 1.0 / cheb_ratio
rho_second = 1.0 / (2.0 * cheb_ratio - rho_first)
gain = 2.0 * rho_second / cheb_radius

MEANS = range(4)
BOX_DIAGONAL, LONG_HIGH, LONG_LOW, ACROSS_HIGH, ACROSS_LOW, LOAD_SUM = range(4, 10)
IMAGE_SUM, FLOW_LONG_HIGH, FLOW_LONG_LOW, FLOW_ACROSS_HIGH, FLOW_ACROSS_LOW = range(16, 21)

VMEM = pl.BlockSpec(memory_space=pltpu.VMEM)
SMEM = pl.BlockSpec(memory_space=pltpu.SMEM)


def sine_basis(length):
    indices = np.arange(1, length + 1)
    phases = indices[:, None] * indices[None, :] % (2 * (length + 1))
    table = np.sqrt(2.0 / (length + 1)) * np.sin(np.pi * phases / (length + 1))
    eigvals = 4.0 * np.sin(np.pi * indices / (2.0 * (length + 1))) ** 2
    return table.astype(np.float32), eigvals.astype(np.float32)


def call(body, out_shape, in_specs, scratch=(), flops=0, out_spec=None, aliases=None):
    return pl.pallas_call(
        body,
        out_shape=out_shape,
        in_specs=in_specs,
        out_specs=out_spec or jax.tree.map(lambda _: VMEM, out_shape),
        scratch_shapes=list(scratch),
        compiler_params=pltpu.CompilerParams(vmem_limit_bytes=30 * 2**20),
        cost_estimate=pl.CostEstimate(flops=flops, bytes_accessed=0, transcendentals=0),
        input_output_aliases=aliases or {},
    )


def f32(*shape):
    return jax.ShapeDtypeStruct(shape, jnp.float32)


class Box:
    def __init__(self, shape):
        self.long, self.across, self.deep = shape
        self.ex = self.long + 2 * MARGIN
        self.ey = self.across + 2 * MARGIN
        self.rows = self.long + 2 * REACH
        self.cols = self.across + 2 * EDGE
        self.flat = self.rows * self.cols


def pieces(values, count):
    parts = []
    for _ in range(count - 1):
        scaled = values * 65537.0
        part = scaled - (scaled - values)
        parts.append(part)
        values = values - part
    return parts + [values]


def products(count):
    return [(a, b) for a in range(count) for b in range(count - a)]


def left_table(table, depth, count):
    rows, cols = table.shape
    rest = np.zeros((rows, depth), np.float32)
    rest[:, :cols] = table
    parts = []
    for _ in range(count):
        part = rest.astype(ml_dtypes.bfloat16).astype(np.float32)
        parts.append(part)
        rest = rest - part
    return np.concatenate([parts[a] for a, _ in products(count)], axis=1)


def right_tables(table):
    rest, parts = table, []
    for _ in range(3):
        part = rest.astype(ml_dtypes.bfloat16).astype(np.float32)
        parts.append(part)
        rest = rest - part
    both = np.concatenate([parts[0], parts[1]], axis=1)
    return np.concatenate([both, both], axis=0), np.concatenate([parts[2], parts[0]], axis=0)


def padded(size):
    return -(-size // 8) * 8


FORWARD, BACKWARD = 2, 3


def tables_of(box):
    sine_x, eig_x = sine_basis(box.ex)
    sine_y, eig_y = sine_basis(box.ey)
    sine_z, eig_z = sine_basis(box.deep)
    in_order_of_steps = np.arange(box.ey).reshape(8, box.ey // 8).T.reshape(-1)
    from_y = sine_y[MARGIN : MARGIN + box.across]
    from_x = sine_x[MARGIN : MARGIN + box.long]
    spread = np.broadcast_to(eig_x[:, None], (box.ex, box.deep))
    main_z, rest_z = right_tables(sine_z)
    return [
        jnp.asarray(np.ascontiguousarray(t))
        for t in (
            left_table(sine_y[:, in_order_of_steps], padded(box.ey), FORWARD),
            left_table(sine_x, padded(box.ex), FORWARD),
            left_table(from_x, padded(box.ex), BACKWARD),
            left_table(from_y, padded(box.ey), BACKWARD),
            main_z,
            rest_z,
            spread,
            eig_z[None, :],
            eig_y[None, :],
        )
    ]


N_TABLES = 9


def one_pass(left, right):
    return lax.dot_general(
        left,
        right,
        (((1,), (0,)), ((), ())),
        precision=lax.Precision.DEFAULT,
        preferred_element_type=jnp.float32,
    )


def dot_left(table, values, count):
    parts = pieces(values, count)
    return one_pass(table, jnp.concatenate([parts[b] for _, b in products(count)], axis=0))


def dot_right(values, main, rest, count):
    deep = values.shape[1]
    parts = pieces(values, count)
    total = one_pass(jnp.concatenate(parts[:2], axis=1), main)
    result = total[:, :deep] + total[:, deep:]
    if count == 3:
        result = result + one_pass(jnp.concatenate([parts[0], parts[2]], axis=1), rest)
    return result


def with_rows(values, rows):
    if values.shape[0] == rows:
        return values
    blank = jnp.zeros((rows - values.shape[0],) + values.shape[1:], values.dtype)
    return jnp.concatenate([values, blank], axis=0)


def box_solve(box, source, divided, tables, row_mask, col_mask, spectral, middle, emit):
    into_y, into_x, from_x, from_y, main_z, rest_z = tables[:6]
    deep = box.deep
    deep_x, deep_y = padded(box.ex), padded(box.ey)
    into_y, into_x = into_y[...], into_x[...]
    if col_mask is not None:
        mask = jnp.concatenate([col_mask] * len(products(FORWARD)), axis=1)
        into_y = into_y * mask
        mask = jnp.concatenate([row_mask] * len(products(FORWARD)), axis=1)
        into_x = into_x * mask
    from_x, from_y, main_z, rest_z = from_x[...], from_y[...], main_z[...], rest_z[...]
    spectral_flat = spectral.reshape(box.ey * deep_x, deep)
    middle_flat = middle.reshape(box.long * deep_y, deep)
    if deep_x > box.ex:
        spectral[:, box.ex :, :] = jnp.zeros((box.ey, deep_x - box.ex, deep), jnp.float32)
    if deep_y > box.ey:
        middle[:, box.ey :, :] = jnp.zeros((box.long, deep_y - box.ey, deep), jnp.float32)
    for start in range(0, box.ex, 8):
        block = source(start).reshape(8 * box.ey, deep)
        block = dot_right(block, main_z, rest_z, FORWARD).reshape(8, box.ey, deep)
        for row in range(0, 8, 2):
            pair = jnp.concatenate([block[row], block[row + 1]], axis=1)
            pair = dot_left(into_y, with_rows(pair, deep_y), FORWARD)
            for part in range(2):
                spectral_flat[pl.ds(start + row + part, box.ey, stride=deep_x), :] = pair[
                    :, part * deep : (part + 1) * deep
                ]
    for col in range(0, box.ey, 2):
        pair = jnp.concatenate([spectral[col], spectral[col + 1]], axis=1)
        pair = dot_left(into_x, pair, FORWARD)
        pair = jnp.concatenate(
            [
                divided(pair[:, part * deep : (part + 1) * deep], col + part)
                for part in range(2)
            ],
            axis=1,
        )
        pair = dot_left(from_x, with_rows(pair, deep_x), BACKWARD)
        for part in range(2):
            middle_flat[pl.ds(col + part, box.long, stride=deep_y), :] = pair[
                :, part * deep : (part + 1) * deep
            ]
    for start in range(0, box.long, 8):
        parts = []
        for row in range(start, start + 8, 2):
            pair = jnp.concatenate([middle[row], middle[row + 1]], axis=1)
            pair = dot_left(from_y, pair, BACKWARD)
            parts += [pair[:, :deep], pair[:, deep:]]
        emit(start, dot_right(jnp.concatenate(parts, axis=0), main_z, rest_z, BACKWARD))


def position():
    long_pos, across_pos = lax.axis_index("wide"), lax.axis_index("narrow")
    return long_pos, across_pos, lax.axis_size("wide"), lax.axis_size("narrow")


def as_float(flag):
    return jnp.where(flag, jnp.float32(1.0), jnp.float32(0.0))


def is_even(axis):
    return lax.rem(lax.axis_index(axis), 2) == 0


class Sides:
    def __init__(self, axis, first, second):
        position = lax.axis_index(axis)
        self.even = is_even(axis)
        self.has_low = as_float(position > 0)
        self.has_high = as_float(position < lax.axis_size(axis) - 1)
        self.first, self.second = first, second

    def low(self, *index):
        return jnp.where(self.even, self.second[index], self.first[index]) * self.has_low

    def high(self, *index):
        return jnp.where(self.even, self.first[index], self.second[index]) * self.has_high


def in_order(even, up, down):
    return jnp.where(even, up, down), jnp.where(even, down, up)


def row_of(stride, col, count, first=0):
    return pl.ds(first * stride + col, count, stride=stride)


def pack_columns(box, fields, wide_sides, wide, first, second):
    corner = len(fields) * wide * box.long
    even = is_even("narrow")
    place = 0
    for field, sides in zip(fields, wide_sides):
        for step in range(wide):
            cols = (box.across - wide + step, step)
            values = [field[row_of(box.across, col, box.long), :] for col in cols]
            low = [sides.low(row_of(box.across, col, wide), slice(None)) for col in cols]
            high = [sides.high(row_of(box.across, col, wide), slice(None)) for col in cols]
            at = corner + 2 * REACH * place
            for start, parts in ((place * box.long, values), (at, low), (at + REACH, high)):
                parts = in_order(even, *(part.astype(jnp.float32) for part in parts))
                size = parts[0].shape[0]
                first[start : start + size, :], second[start : start + size, :] = parts
            place += 1


def message_rows(box, count):
    return -(-(count * (box.long + 2 * REACH)) // 8) * 8


def pack_fields(box, wide, fields, tables, after, *refs):
    own, (low, high), refs = refs[:fields], refs[fields : fields + 2], refs[fields + 2 :]
    parts, (first, second, *table) = refs[:tables], refs[tables + after :]
    size = wide * box.across
    flat = [field.reshape(box.long * box.across, box.deep) for field in own]
    low = low.reshape(low.size // box.deep, box.deep)
    high = high.reshape(high.size // box.deep, box.deep)
    sides = [
        Sides("wide", *(ref.at[index * size : (index + 1) * size] for ref in (low, high)))
        for index in range(fields)
    ]
    pack_columns(box, flat, sides, wide, first, second)
    if tables:
        known = last_rows_merged(parts, table[0].shape[0])
        table[0][...] = known
        first[first.shape[0] - known.shape[0] :, :] = known
        second[second.shape[0] - known.shape[0] :, :] = known


def bring_edges(
    box, zone, scale, load, own_zone, own_scale, own_load, load_first, load_second, first, second,
    staged, sems
):
    even = is_even("wide")

    def edges(wide):
        up, down = box.long - wide, 0
        return [pl.ds(jnp.where(even, *pair), wide) for pair in ((up, down), (down, up))]

    copies = [
        (load.at[edges(MARGIN)[0]], load_first),
        (load.at[edges(MARGIN)[1]], load_second),
        (zone.at[edges(REACH)[0]], staged.at[0]),
        (zone.at[edges(REACH)[1]], staged.at[1]),
        (scale.at[edges(REACH)[0]], first.at[:REACH]),
        (scale.at[edges(REACH)[1]], second.at[:REACH]),
        (load, own_load),
        (scale, own_scale),
        (zone, own_zone),
    ]
    copies = [
        pltpu.make_async_copy(source, target, sems.at[index])
        for index, (source, target) in enumerate(copies)
    ]
    for copy in copies:
        copy.start()
    for copy in copies[:4]:
        copy.wait()
    first[REACH:] = staged[0].astype(jnp.float32)
    second[REACH:] = staged[1].astype(jnp.float32)
    for copy in copies[4:]:
        copy.wait()


def fill_window(box, window, own, wide_sides, narrow_sides, wide, place, total, add=None):
    flat = window.reshape(box.flat, box.deep)
    nothing = jnp.zeros((box.rows, EDGE, box.deep), jnp.float32)
    window[:, :EDGE, :] = nothing
    window[:, EDGE + box.across :, :] = nothing
    if add is None:
        add = lambda values, row_side, col_side: values
    inner = slice(EDGE, EDGE + box.across)
    first, last = REACH, REACH + box.long
    if wide < REACH:
        blank = jnp.zeros((1, box.across, box.deep), jnp.float32)
        window[0:1, inner, :] = blank
        window[box.rows - 1 :, inner, :] = blank
    window[first:last, inner, :] = add(own[...].astype(jnp.float32), 0, 0)
    window[first - wide : first, inner, :] = add(wide_sides.low(Ellipsis), -1, 0)
    window[last : last + wide, inner, :] = add(wide_sides.high(Ellipsis), 1, 0)
    corner = total * box.long
    for step in range(wide):
        for source, col, side in (
            (narrow_sides.low, EDGE - wide + step, -1),
            (narrow_sides.high, EDGE + box.across + step, 1),
        ):
            for start, size, row, row_side in (
                ((place + step) * box.long, box.long, first, 0),
                (corner + 2 * REACH * (place + step), wide, first - wide, -1),
                (corner + 2 * REACH * (place + step) + REACH, wide, last, 1),
            ):
                values = source(slice(start, start + size), slice(None))
                flat[row_of(box.cols, col, size, row), :] = add(values, row_side, side)


def some_cols(box, ref, row, step):
    stride = box.ey // 8
    return ref[row, pl.ds(EDGE - MARGIN + step, 8, stride=stride), :]


def negative_image(box, window, row, at, x, flow_before, weights):
    to_long, to_across, to_deep, mass = weights
    steps = range(box.ey // 8)
    x_next = [some_cols(box, window, row + 1, step) for step in range(-1, len(steps) + 1)]
    flow_long = [
        some_cols(box, to_long, at, step) * (x_next[step + 1] - x[step + 1]) for step in steps
    ]
    flow_across = [
        some_cols(box, to_across, at, step) * (x[step + 2] - x[step + 1])
        for step in range(-1, len(steps))
    ]
    totals = []
    for step in steps:
        here = x[step + 1]
        lanes = here.shape[1]
        flow_deep = some_cols(box, to_deep, at, step) * (pltpu.roll(here, lanes - 1, 1) - here)
        total = flow_long[step] - flow_before[step] - some_cols(box, mass, at, step) * here
        total = total + (flow_across[step + 1] - flow_across[step])
        totals.append(total + (flow_deep - pltpu.roll(flow_deep, 1, 1)))
    return totals, x_next, flow_long


def in_steps(box, refs, rows):
    return jnp.stack(
        [
            jnp.concatenate([some_cols(box, ref, row, step) for step in range(box.ey // 8)], axis=0)
            for ref, row in zip(refs, rows)
        ]
    )


def looked_up(labels, values):
    return jnp.where(labels == 0, values[0], jnp.where(labels == 1, values[1], values[2]))


def at_own_row(line, shape):
    long_pos, across_pos, _, across_count = position()
    rows = lax.broadcasted_iota(jnp.int32, shape, 0)
    own = rows == long_pos * across_count + across_pos
    return jnp.where(own, line[:1], jnp.zeros(shape, jnp.float32))


def merged(table, *others):
    for other in others:
        table = jnp.where(table != 0.0, table, other)
    return table


def last_rows_merged(refs, count):
    return merged(*(ref[ref.shape[0] - count :, :] for ref in refs))


def join_rows(table, message, out):
    out[...] = last_rows_merged((table, message), out.shape[0])


def line_of(numbers, shape):
    lanes = lax.broadcasted_iota(jnp.int32, shape, 1)
    line = jnp.zeros(shape, jnp.float32)
    for index, number in numbers:
        line = jnp.where(lanes == index, number, line)
    return line


def box_sums(box, zone, scale, load, after, diffusivity, decay, out, table):
    del after
    nothing = jnp.zeros((box.across, box.deep), jnp.float32)
    half = [[0.5 * diffusivity[z, d] for z in range(3)] for d in range(3)]
    rates = [decay[z] for z in range(3)]

    def halves(row):
        labels, factor = zone[row], scale[row]
        return [looked_up(labels, half[d]) * factor for d in range(3)] + [looked_up(labels, rates)]

    sums = [nothing] * 5
    for row in range(box.long):
        sums = [total + more for total, more in zip(sums, halves(row) + [load[row]])]

    def total(values):
        return jnp.sum(values, keepdims=True).reshape(1, 1)

    cells = box.long * box.across * box.deep
    numbers = [(index, total(sums[index]) * (2.0 / cells)) for index in range(3)]
    mass = total(sums[3])
    numbers += [(3, mass / cells)]
    ends = total(sums[2][:, :1]) + total(sums[2][:, box.deep - 1 :])
    numbers += [
        (BOX_DIAGONAL, mass + ends),
        (LONG_HIGH, total(halves(box.long - 1)[0])),
        (LONG_LOW, total(halves(0)[0])),
        (ACROSS_HIGH, total(sums[1][box.across - 1 :])),
        (ACROSS_LOW, total(sums[1][:1])),
        (LOAD_SUM, total(sums[4])),
    ]
    line = line_of(numbers, out.shape)
    out[...] = line
    table[...] = at_own_row(line, table.shape)


def means_of(ref):
    return [ref[0:1, index : index + 1] for index in range(4)]


def first_solve(box, load, low, high, left, right, means, zone, scale, diffusivity, decay, *rest):
    tables = rest[:N_TABLES]
    window, local, image, inverses, spectral, middle = rest[N_TABLES:]
    spread, eig_z, eig_y = tables[6:]
    means = means_of(means)
    base = means[3] + means[0] * spread[...] + means[2] * eig_z[...]

    def divided(values, col):
        divisor = base + means[1] * eig_y[0, col]
        inverse = pl.reciprocal(divisor, approx=True)
        for _ in range(2):
            inverse = inverse * (2.0 - divisor * inverse)
        inverses[col] = inverse
        return values * inverse

    half = [0.5 * diffusivity[z, 2] for z in range(3)]
    rates = [decay[z] for z in range(3)]
    lane = lax.broadcasted_iota(jnp.int32, (box.across, box.deep), 1)
    ends = jnp.where((lane == 0) | (lane == box.deep - 1), jnp.float32(1.0), jnp.float32(0.0))
    image[...] = jnp.zeros((box.across, box.deep), jnp.float32)
    wide_sides, narrow_sides = Sides("wide", low, high), Sides("narrow", left, right)
    fill_window(box, window, load, wide_sides, narrow_sides, MARGIN, 0, MARGIN)

    def emit(start, values):
        values = values * (1.0 / cheb_center)
        values = values.reshape(8, box.across, box.deep)
        local[start : start + 8] = values
        total = image[...]
        for row in range(8):
            labels = zone[start + row]
            mass = looked_up(labels, rates) + looked_up(labels, half) * scale[start + row] * ends
            total = total + mass * values[row]
        image[...] = total

    box_solve(
        box,
        lambda start: in_steps(box, [window] * 8, range(1 + start, 9 + start)),
        divided,
        tables,
        None,
        None,
        spectral,
        middle,
        emit,
    )


def side_weights(
    box, zone, scale, low, high, left, right, diffusivity, to_long, to_across, zone_window,
    scale_window
):
    for index, (window, own) in enumerate(((scale_window, scale), (zone_window, zone))):
        start = index * REACH
        wide_sides = Sides("wide", *(ref.at[start : start + REACH] for ref in (low, high)))
        narrow_sides = Sides("narrow", left, right)
        fill_window(box, window, own, wide_sides, narrow_sides, REACH, start, 2 * REACH)
    half = [[0.5 * diffusivity[z, d] for z in range(3)] for d in range(2)]

    def one_row(row, before):
        labels, factor = zone_window[row], scale_window[row]
        now = [looked_up(labels, half[d]) * factor for d in range(2)]
        to_across[row] = now[1] + pltpu.roll(now[1], box.cols - 1, 0)
        to_long[jnp.maximum(row - 1, 0)] = before + now[0]
        return now[0]

    def some_rows(index, before):
        for row in range(8):
            before = one_row(index * 8 + row, before)
        return before

    before = jnp.zeros((box.cols, box.deep), jnp.float32)
    before = lax.fori_loop(0, box.rows // 8, some_rows, before)
    for row in range(box.rows // 8 * 8, box.rows):
        before = one_row(row, before)
    to_long[box.rows - 1] = before


def deep_weights(box, zone_window, scale_window, diffusivity, decay, to_deep, mass):
    half = [0.5 * diffusivity[z, 2] for z in range(3)]
    rates = [decay[z] for z in range(3)]
    lane = lax.broadcasted_iota(jnp.int32, (box.cols, box.deep), 1)
    ends = jnp.where((lane == 0) | (lane == box.deep - 1), jnp.float32(1.0), jnp.float32(0.0))
    not_last = jnp.where(lane == box.deep - 1, jnp.float32(0.0), jnp.float32(1.0))

    def one_row(row):
        labels = zone_window[row]
        now = looked_up(labels, half) * scale_window[row]
        to_deep[row] = (now + pltpu.roll(now, box.deep - 1, 1)) * not_last
        mass[row] = looked_up(labels, rates) + now * ends

    def some_rows(index, _):
        for row in range(8):
            one_row(index * 8 + row)
        return 0

    lax.fori_loop(0, box.rows // 8, some_rows, 0)
    for row in range(box.rows // 8 * 8, box.rows):
        one_row(row)


def image_sums(
    box, zone, scale, local, image, low, high, left, right, table, diffusivity, out, up, down
):
    half = [[0.5 * diffusivity[z, d] for z in range(3)] for d in range(3)]
    shape = (box.long * box.across, box.deep)
    zone_flat, scale_flat, local_flat = zone.reshape(shape), scale.reshape(shape), local.reshape(shape)
    last_col = row_of(box.across, box.across - 1, box.long)
    first_col = row_of(box.across, 0, box.long)

    wide_sides, narrow_sides = Sides("wide", low, high), Sides("narrow", left, right)

    def side(source, place):
        return source(slice(place * box.long, (place + 1) * box.long), slice(None))

    above, below = wide_sides.high, wide_sides.low
    faces = [
        (0, zone[box.long - 1], scale[box.long - 1], local[box.long - 1], above(REACH), above(0)),
        (0, zone[0], scale[0], local[0], below(2 * REACH - 1), below(REACH - 1)),
        (
            1,
            zone_flat[last_col, :],
            scale_flat[last_col, :],
            local_flat[last_col, :],
            side(narrow_sides.high, REACH),
            side(narrow_sides.high, 0),
        ),
        (
            1,
            zone_flat[first_col, :],
            scale_flat[first_col, :],
            local_flat[first_col, :],
            side(narrow_sides.low, 2 * REACH - 1),
            side(narrow_sides.low, REACH - 1),
        ),
    ]
    flows = []
    for direction, labels, factor, values, far_labels, far_factor in faces:
        weight = looked_up(labels, half[direction]) * factor
        weight = weight + looked_up(far_labels, half[direction]) * far_factor
        flows.append(jnp.sum(weight * values, keepdims=True))
    long_pos, across_pos, long_count, across_count = position()
    numbers = [
        (IMAGE_SUM, jnp.sum(image[...], keepdims=True) + sum(flows)),
        (FLOW_LONG_HIGH, flows[0] * as_float(long_pos < long_count - 1)),
        (FLOW_LONG_LOW, flows[1] * as_float(long_pos > 0)),
        (FLOW_ACROSS_HIGH, flows[2] * as_float(across_pos < across_count - 1)),
        (FLOW_ACROSS_LOW, flows[3] * as_float(across_pos > 0)),
    ]
    known = table[...] + at_own_row(line_of(numbers, (8, out.shape[1])), out.shape)
    out[...] = known
    edge = REACH * box.across
    even = is_even("wide")
    for target, pair in ((up, (box.long - REACH, 0)), (down, (0, box.long - REACH))):
        target[:edge] = local[pl.ds(jnp.where(even, *pair), REACH)].reshape(edge, box.deep)
        target[edge:] = known


def column(values, index):
    return values[:, index : index + 1]


def coarse_inverse(numbers, work):
    count, width = work.shape
    across = lax.axis_size("narrow")
    beyond = pltpu.roll(numbers, count - across, 0)
    beside = pltpu.roll(numbers, count - 1, 0)
    before = pltpu.roll(numbers, across, 0)
    ahead = pltpu.roll(numbers, 1, 0)
    place = lax.broadcasted_iota(jnp.int32, (count, 1), 0)
    across_pos = lax.rem(place, across)
    nothing = jnp.zeros((count, 1), jnp.float32)
    couplings = []
    diagonal = column(numbers, BOX_DIAGONAL)
    for own, other, there, inside in (
        (LONG_HIGH, LONG_LOW, beyond, place < count - across),
        (LONG_LOW, LONG_HIGH, before, place >= across),
        (ACROSS_HIGH, ACROSS_LOW, beside, across_pos < across - 1),
        (ACROSS_LOW, ACROSS_HIGH, ahead, across_pos > 0),
    ):
        shared = jnp.where(inside, column(there, other), nothing)
        diagonal = diagonal + column(numbers, own) + shared
        couplings.append(jnp.where(inside, column(numbers, own) + shared, nothing))
    rows = lax.broadcasted_iota(jnp.int32, (count, width), 0)
    cols = lax.broadcasted_iota(jnp.int32, (count, width), 1)
    blank = jnp.zeros((count, width), jnp.float32)
    matrix = jnp.where(cols == rows, diagonal, blank)
    for shift, coupling in zip((across, -across, 1, -1), couplings):
        matrix = matrix - jnp.where((cols == rows + shift) & (cols < count), coupling, blank)
    matrix = jnp.where(cols == rows + count, jnp.ones((count, 1), jnp.float32), matrix)
    if count <= 16:
        for step in range(count):
            pivot_row = matrix[step : step + 1, :] / matrix[step : step + 1, step : step + 1]
            rest = matrix - matrix[:, step : step + 1] * pivot_row
            matrix = jnp.where(rows == step, pivot_row, rest)
        return pltpu.roll(matrix, width - count, 1)
    work[...] = matrix

    def eliminate(step, _):
        values = work[...]
        pivot_row = work[pl.ds(step, 1), :]
        at_step = cols == step
        factors = jnp.sum(jnp.where(at_step, values, blank), axis=1, keepdims=True)
        pivot = jnp.sum(jnp.where(at_step[:1], pivot_row, blank[:1]), axis=1, keepdims=True)
        pivot_row = pivot_row / pivot
        work[...] = jnp.where(rows == step, pivot_row, values - factors * pivot_row)
        return 0

    lax.fori_loop(0, count, eliminate, 0)
    values = work[...]
    if count % 128:
        return pltpu.roll(values, width - count, 1)
    return values[:, count : 2 * count]


def answer(inverse, sums):
    return jnp.sum(inverse * sums, axis=0, keepdims=True)


def at_box(values, row_side, col_side):
    long_pos, across_pos, long_count, across_count = position()
    there_long, there_across = long_pos + row_side, across_pos + col_side
    inside = (
        (there_long >= 0)
        & (there_long < long_count)
        & (there_across >= 0)
        & (there_across < across_count)
    )
    lanes = lax.broadcasted_iota(jnp.int32, values.shape, 1)
    wanted = (lanes == there_long * across_count + there_across) & inside
    return jnp.sum(jnp.where(wanted, values, jnp.zeros_like(values)), axis=1, keepdims=True)


def coarse_corrections(parts, *refs):
    table_parts, (out, work) = refs[:parts], refs[parts:]
    count = work.shape[0]
    numbers = last_rows_merged(table_parts, count)
    across_count = lax.axis_size("narrow")
    inverse = coarse_inverse(numbers, work)
    sums = column(numbers, IMAGE_SUM)
    sums = sums - column(pltpu.roll(numbers, count - across_count, 0), FLOW_LONG_LOW)
    sums = sums - column(pltpu.roll(numbers, across_count, 0), FLOW_LONG_HIGH)
    sums = sums - column(pltpu.roll(numbers, count - 1, 0), FLOW_ACROSS_LOW)
    sums = sums - column(pltpu.roll(numbers, 1, 0), FLOW_ACROSS_HIGH)
    load_sums = column(numbers, LOAD_SUM)
    sums = load_sums * (1.0 - 1.0 / cheb_center) - sums
    out[0:1, :] = answer(inverse, load_sums) * (1.0 / cheb_center)
    out[1:2, :] = answer(inverse, sums) * gain


def second_solve(box, local, low, high, left, right, inverses, answers, *rest):
    to_long, to_across, to_deep, mass, load_window = rest[:5]
    tables = rest[5 : 5 + N_TABLES]
    iterate, top, bottom, last_col, first_col, out = rest[5 + N_TABLES : 11 + N_TABLES]
    window, spectral, middle, sems = rest[11 + N_TABLES :]
    long_pos, across_pos, long_count, across_count = position()
    coarse = answers[0:1, :]
    own_shift = at_box(answers[1:2, :], 0, 0)
    shifts = {
        (row_side, col_side): at_box(coarse, row_side, col_side)
        for row_side in (-1, 0, 1)
        for col_side in (-1, 0, 1)
    }

    def add(values, row_side, col_side):
        shift = shifts[row_side, col_side]
        if values.ndim == 3:
            shift = shift.reshape(1, 1, 1)
        return values + shift

    edge = REACH * box.across
    low, high = (
        ref.at[:edge].reshape(REACH, box.across, box.deep) for ref in (low, high)
    )
    wide_sides, narrow_sides = Sides("wide", low, high), Sides("narrow", left, right)
    fill_window(box, window, local, wide_sides, narrow_sides, REACH, 0, REACH, add)
    weights = (to_long, to_across, to_deep, mass)

    steps = range(box.ey // 8)
    x = [some_cols(box, window, 1, step) for step in range(-1, len(steps) + 1)]
    flow = [
        some_cols(box, to_long, 0, step) * (x[step + 1] - some_cols(box, window, 0, step))
        for step in steps
    ]
    state = [x, flow]

    def divided(values, col):
        return values * inverses[col]

    def residual(start_row):
        rows = []
        for row in range(start_row + 1, start_row + 9):
            image, *state[:] = negative_image(box, window, row, row, *state, weights)
            image = [some_cols(box, load_window, row, step) + image[step] for step in steps]
            rows.append(jnp.concatenate(image, axis=0))
        return jnp.stack(rows)

    inner = slice(EDGE, EDGE + box.across)
    first = REACH
    row_ids = lax.broadcasted_iota(jnp.int32, (1, padded(box.ex)), 1)
    col_ids = lax.broadcasted_iota(jnp.int32, (1, padded(box.ey)), 1)
    col_ids = (col_ids & 7) * (box.ey // 8) + lax.shift_right_logical(col_ids, 3)
    row_mask = jnp.where(row_ids < MARGIN, as_float(long_pos > 0), 1.0)
    row_mask = jnp.where(row_ids >= MARGIN + box.long, as_float(long_pos < long_count - 1), row_mask)
    col_mask = jnp.where(col_ids < MARGIN, as_float(across_pos > 0), 1.0)
    col_mask = jnp.where(
        col_ids >= MARGIN + box.across, as_float(across_pos < across_count - 1), col_mask
    )
    keep = 1.0 + rho_second * rho_first
    copies = []

    def emit(start, values):
        rows = values.reshape(8, box.across, box.deep)
        before = window[first + start : first + start + 8, inner, :]
        shift = own_shift.reshape(1, 1, 1)
        iterate[start : start + 8] = keep * before + (gain * rows + shift)
        copies.append(
            pltpu.make_async_copy(
                iterate.at[start : start + 8], out.at[start : start + 8], sems.at[len(copies)]
            )
        )
        copies[-1].start()

    box_solve(
        box, residual, divided, tables, row_mask, col_mask, spectral, middle, emit
    )
    rows = in_order(is_even("wide"), iterate[box.long - 1], iterate[0])
    top[...], bottom[...] = rows
    flat = iterate.reshape(box.long * box.across, box.deep)
    cols = [flat[row_of(box.across, col, box.long), :] for col in (box.across - 1, 0)]
    last_col[...], first_col[...] = in_order(is_even("narrow"), *cols)
    for copy in copies:
        copy.wait()


def inner_residual(
    box, load, iterate, to_long, to_across, to_deep, mass, rows, cols, out, window, result, sems
):
    inner = slice(EDGE, EDGE + box.across)
    flat = window.reshape((box.long + 2) * box.cols, box.deep)
    iterate_flat = iterate.reshape(box.long * box.across, box.deep)
    blank = jnp.zeros((box.long + 2, EDGE, box.deep), jnp.float32)
    window[:, :EDGE, :] = blank
    window[:, EDGE + box.across :, :] = blank
    window[1 : 1 + box.long, inner, :] = iterate[...]
    window[0, inner, :] = iterate[0]
    window[1 + box.long, inner, :] = iterate[box.long - 1]
    for col, place in ((0, EDGE - 1), (box.across - 1, EDGE + box.across)):
        values = iterate_flat[row_of(box.across, col, box.long), :]
        flat[row_of(box.cols, place, box.long, 1), :] = values
    weights = (to_long, to_across, to_deep, mass)
    steps = range(box.ey // 8)
    x = [some_cols(box, window, 1, step) for step in range(-1, len(steps) + 1)]
    flow = [jnp.zeros((8, box.deep), jnp.float32) for _ in steps]
    middle = slice(8, box.across - 8)
    copies = []
    for row in range(box.long):
        image, x, flow = negative_image(box, window, row + 1, REACH + row, x, flow, weights)
        for step in steps:
            place = pl.ds(EDGE - MARGIN + step, 8, stride=box.ey // 8)
            result[row, place, :] = image[step]
        values = load[row] + result[row, inner]
        result[row, inner] = values
        cols[0, row] = values[:8]
        cols[1, row] = values[box.across - 8 :]
        if row == 0:
            rows[0] = values
        if row == box.long - 1:
            rows[1] = values
        if row % 8 == 7:
            part = slice(row - 7, row + 1)
            copy = pltpu.make_async_copy(
                result.at[part, EDGE + 8 : EDGE + box.across - 8],
                out.at[part, middle],
                sems.at[row // 8],
            )
            copy.start()
            copies.append(copy)
    for copy in copies:
        copy.wait()


def outer_residual(
    box, iterate, low, high, left, right, to_long, to_across, rows, cols, inner_out, out,
    row_part, col_part, sems
):
    del inner_out
    inner = slice(EDGE, EDGE + box.across)
    middle = slice(8, box.across - 8)
    wide_sides, narrow_sides = Sides("wide", low, high), Sides("narrow", left, right)
    last = box.long - 1
    iterate_flat = iterate.reshape(box.long * box.across, box.deep)
    across_flat = to_across.reshape(box.flat, box.deep)
    below = to_long[REACH - 1, inner] * (wide_sides.low(Ellipsis) - iterate[0])
    above = to_long[REACH + last, inner] * (wide_sides.high(Ellipsis) - iterate[last])
    row_part[0] = (rows[0] + below)[middle]
    row_part[1] = (rows[1] + above)[middle]
    copies = [
        pltpu.make_async_copy(row_part.at[0], out.at[0, middle], sems.at[0]),
        pltpu.make_async_copy(row_part.at[1], out.at[last, middle], sems.at[1]),
    ]
    for copy in copies:
        copy.start()
    col_part[...] = cols[...]
    flat = col_part.reshape(2 * box.long * 8, box.deep)
    for side, (from_side, col, face, tile) in enumerate(
        (
            (narrow_sides.low, 0, EDGE - 1, slice(0, 8)),
            (narrow_sides.high, box.across - 1, EDGE + box.across - 1, slice(box.across - 8, None)),
        )
    ):
        weight = across_flat[row_of(box.cols, face, box.long, REACH), :]
        own = iterate_flat[row_of(box.across, col, box.long), :]
        place = pl.ds(side * box.long * 8 + side * 7, box.long, stride=8)
        flat[place, :] = flat[place, :] + weight * (from_side(Ellipsis) - own)
        col_part[side, 0] = col_part[side, 0] + below[tile]
        col_part[side, last] = col_part[side, last] + above[tile]
        first_col = side * (box.across - 8)
        copy = pltpu.make_async_copy(
            col_part.at[side], out.at[:, first_col : first_col + 8], sems.at[2 + side]
        )
        copy.start()
        copies.append(copy)
    for copy in copies:
        copy.wait()


def swaps(axis, around):
    sizes = (lax.axis_size("wide"), lax.axis_size("narrow"))
    along = ("wide", "narrow").index(axis)
    size, beside = sizes[along], sizes[1 - along]

    def number(place, other_place):
        pair = (place, other_place) if along == 0 else (other_place, place)
        return pair[0] * sizes[1] + pair[1]

    ways = []
    for way in range(2):
        pairs = []
        for place in range(size):
            for other_place in range(beside):
                partner = place + 1 if place % 2 == way else place - 1
                there = other_place
                if around and size % 2 == 0:
                    partner %= size
                if not 0 <= partner < size:
                    partner = place
                    there = other_place ^ 1 if beside % 2 == 0 else other_place
                pairs.append((number(place, other_place), number(partner, there)))
        ways.append(pairs)
    return ways


def exchange(axis, first, second, around=False):
    ways = swaps(axis, around)
    axes = ("wide", "narrow")
    return lax.ppermute(first, axes, ways[0]), lax.ppermute(second, axes, ways[1])


def two_away(axis, table):
    size = lax.axis_size(axis)
    return lax.ppermute(table, axis, [(i, (i + 2) % size) for i in range(size)])


def tell(table):
    count = table.shape[0]
    long_pos, across_pos, _, across_count = position()
    own = lax.dynamic_slice_in_dim(table, long_pos * across_count + across_pos, 1, axis=0)
    line = jnp.broadcast_to(own, (count, 1, 128))
    told = lax.all_to_all(line, ("wide", "narrow"), split_axis=0, concat_axis=0, tiled=True)
    return told.reshape(count, 128)


def on_device(zone, scale, diffusivity, decay, load):
    box = Box(load.shape)
    long, across, deep = load.shape
    count = lax.axis_size("wide") * lax.axis_size("narrow")
    by_margins = lax.axis_size("wide") == 4 and lax.axis_size("narrow") == 4
    tables = tables_of(box)
    cells = f32(long, across, deep)
    whole_zone = jax.ShapeDtypeStruct(cells.shape, zone.dtype)
    window = f32(box.rows, box.cols, deep)
    table_shape = f32(count, 128)
    anywhere = pl.BlockSpec(memory_space=pl.ANY)
    in_hbm = pl.BlockSpec(memory_space=pltpu.HBM)

    def scratch(shape):
        return pltpu.VMEM(shape, jnp.float32)

    def pinned(field):
        return pltpu.with_memory_space_constraint(field, pltpu.HBM)

    spectral = scratch((box.ey, padded(box.ex), deep))
    middle = scratch((long, padded(box.ey), deep))

    def pack(wide, fields, sides, parts=(), after=()):
        rows = message_rows(box, wide * len(fields)) + (count if parts else 0)
        message = f32(rows, deep)
        body = functools.partial(pack_fields, box, wide, len(fields), len(parts), len(after))
        return call(
            body,
            (message, message) + ((table_shape,) if parts else ()),
            [VMEM] * (len(fields) + 2 + len(parts)) + [anywhere] * len(after),
        )(*fields, *sides, *parts, *after)

    far = f32(2 * REACH, across, deep)
    zone, scale, load, load_first, load_second, first, second = call(
        functools.partial(bring_edges, box),
        (whole_zone, cells, cells) + (f32(MARGIN, across, deep),) * 2 + (far, far),
        [in_hbm] * 3,
        [pltpu.VMEM((2, REACH, across, deep), zone.dtype), pltpu.SemaphoreType.DMA((9,))],
    )(pinned(zone), pinned(scale), pinned(load))
    load_wide = exchange("wide", load_first, load_second)
    far_wide = exchange("wide", first, second)
    load_first, load_second = pack(MARGIN, [load], load_wide)
    load_narrow = exchange("narrow", load_first, load_second)
    sums, table = call(
        functools.partial(box_sums, box),
        (f32(8, 128), table_shape),
        [VMEM] * 3 + [anywhere] + [SMEM] * 2,
    )(zone, scale, load, load_first, diffusivity, decay)
    far_narrow = exchange("narrow", *pack(REACH, [scale, zone], far_wide))
    load_window, local, image, inverses = call(
        functools.partial(first_solve, box),
        (window, cells, f32(across, deep), f32(box.ey, box.ex, deep)),
        [VMEM] * 8 + [SMEM] * 2 + [VMEM] * N_TABLES,
        [spectral, middle],
        flops=4 * 10**9,
    )(load, *load_wide, *load_narrow, sums, zone, scale, diffusivity, decay, *tables)
    message = f32(REACH * across + count, deep)
    table, first, second = call(
        functools.partial(image_sums, box), (table_shape, message, message), [VMEM] * 9 + [SMEM]
    )(zone, scale, local, image, *far_wide, *far_narrow, table, diffusivity)
    own_table = table
    wide = exchange("wide", first, second, by_margins)
    parts = (table, *wide)
    if by_margins:
        parts += (two_away("wide", table),)
    to_long, to_across, *windows = call(
        functools.partial(side_weights, box),
        (window,) * 4,
        [VMEM] * 6 + [SMEM],
        flops=10**9,
    )(zone, scale, *far_wide, *far_narrow, diffusivity)
    to_deep, mass = call(
        functools.partial(deep_weights, box),
        (window,) * 2,
        [VMEM] * 2 + [SMEM] * 2,
        flops=10**9,
    )(*windows, diffusivity, decay)
    weights = (to_long, to_across, to_deep, mass)
    first, second, table = pack(REACH, [local], wide, parts, [to_long])
    narrow = exchange("narrow", first, second)
    if by_margins:
        table = call(join_rows, table_shape, [VMEM] * 2)(table, narrow[0])
        parts = (table, two_away("narrow", table))
    else:
        parts = (tell(own_table),)
    row, col = f32(across, deep), f32(long, deep)
    answers = call(
        functools.partial(coarse_corrections, len(parts)),
        f32(8, -(-count // 128) * 128),
        [VMEM] * len(parts),
        [scratch((count, -(-2 * count // 128) * 128))],
    )(*parts)
    iterate, first_row, second_row, first_col, second_col, result = call(
        functools.partial(second_solve, box),
        (cells, row, row, col, col, cells),
        [VMEM] * (12 + N_TABLES),
        [scratch(window.shape), spectral, middle, pltpu.SemaphoreType.DMA((long // 8,))],
        flops=4 * 10**9,
        out_spec=(VMEM,) * 5 + (anywhere,),
    )(local, *wide, *narrow, inverses, answers, *weights, load_window, *tables)
    narrow = exchange("narrow", first_col, second_col)
    wide = exchange("wide", first_row, second_row)
    rows, cols, inner = call(
        functools.partial(inner_residual, box),
        (f32(2, across, deep), f32(2, long, 8, deep), cells),
        [VMEM] * 6,
        [
            scratch((long + 2, box.cols, deep)),
            scratch((long, box.cols, deep)),
            pltpu.SemaphoreType.DMA((long // 8,)),
        ],
        flops=10**9,
        out_spec=(VMEM, VMEM, anywhere),
    )(load, iterate, *weights)
    residual = call(
        functools.partial(outer_residual, box),
        cells,
        [VMEM] * 9 + [anywhere],
        [
            scratch((2, across - 16, deep)),
            scratch((2, long, 8, deep)),
            pltpu.SemaphoreType.DMA((4,)),
        ],
        out_spec=anywhere,
        aliases={9: 0},
    )(iterate, *wide, *narrow, to_long, to_across, rows, cols, inner)
    return result, residual


def solution(mesh):
    split = P(("groups", "wide"), "narrow", None)
    return jax.shard_map(
        on_device,
        mesh=mesh,
        in_specs=(split, split, P(), P(), split),
        out_specs=(split, split),
        check_vma=False,
    )
```

```python
import functools

import jax
import jax.numpy as jnp
import ml_dtypes
import numpy as np
from jax import lax
from jax.experimental import pallas as pl
from jax.experimental.pallas import tpu as pltpu
from jax.sharding import PartitionSpec as P

MARGIN = 4
REACH = MARGIN + 1
EDGE = 8

cheb_center = 1.3
cheb_radius = 1.2
cheb_ratio = 1.3 / 1.2
rho_first = 1.0 / cheb_ratio
rho_second = 1.0 / (2.0 * cheb_ratio - rho_first)
gain = 2.0 * rho_second / cheb_radius

MEANS = range(4)
BOX_DIAGONAL, LONG_HIGH, LONG_LOW, ACROSS_HIGH, ACROSS_LOW, LOAD_SUM = range(4, 10)
IMAGE_SUM, FLOW_LONG_HIGH, FLOW_LONG_LOW, FLOW_ACROSS_HIGH, FLOW_ACROSS_LOW = range(16, 21)

VMEM = pl.BlockSpec(memory_space=pltpu.VMEM)
SMEM = pl.BlockSpec(memory_space=pltpu.SMEM)


def sine_basis(length):
    indices = np.arange(1, length + 1)
    phases = indices[:, None] * indices[None, :] % (2 * (length + 1))
    table = np.sqrt(2.0 / (length + 1)) * np.sin(np.pi * phases / (length + 1))
    eigvals = 4.0 * np.sin(np.pi * indices / (2.0 * (length + 1))) ** 2
    return table.astype(np.float32), eigvals.astype(np.float32)


def call(body, out_shape, in_specs, scratch=(), flops=0, out_spec=None, aliases=None):
    return pl.pallas_call(
        body,
        out_shape=out_shape,
        in_specs=in_specs,
        out_specs=out_spec or jax.tree.map(lambda _: VMEM, out_shape),
        scratch_shapes=list(scratch),
        compiler_params=pltpu.CompilerParams(vmem_limit_bytes=30 * 2**20),
        cost_estimate=pl.CostEstimate(flops=flops, bytes_accessed=0, transcendentals=0),
        input_output_aliases=aliases or {},
    )


def f32(*shape):
    return jax.ShapeDtypeStruct(shape, jnp.float32)


class Box:
    def __init__(self, shape):
        self.long, self.across, self.deep = shape
        self.ex = self.long + 2 * MARGIN
        self.ey = self.across + 2 * MARGIN
        self.rows = self.long + 2 * REACH
        self.cols = self.across + 2 * EDGE
        self.flat = self.rows * self.cols


def pieces(values, count):
    parts = []
    for _ in range(count - 1):
        scaled = values * 65537.0
        part = scaled - (scaled - values)
        parts.append(part)
        values = values - part
    return parts + [values]


def left_table(table, depth, count):
    rows, cols = table.shape
    wide = np.zeros((rows, depth), np.float32)
    wide[:, :cols] = table
    parts = []
    rest = wide
    for _ in range(count):
        part = rest.astype(ml_dtypes.bfloat16).astype(np.float32)
        parts.append(part)
        rest = rest - part
    blank = np.zeros_like(parts[0])
    lines = []
    for index in range(count):
        used = count - index if count > 2 else count
        lines.append(np.concatenate([parts[index]] * used + [blank] * (count - used), axis=1))
    return np.concatenate(lines, axis=0)


def right_tables(table):
    rest, parts = table, []
    for _ in range(3):
        part = rest.astype(ml_dtypes.bfloat16).astype(np.float32)
        parts.append(part)
        rest = rest - part
    both = np.concatenate([parts[0], parts[1]], axis=1)
    return np.concatenate([both, both], axis=0), np.concatenate([parts[2], parts[0]], axis=0)


def padded(size):
    return -(-size // 8) * 8


FORWARD, BACKWARD = 2, 3


def tables_of(box):
    sine_x, eig_x = sine_basis(box.ex)
    sine_y, eig_y = sine_basis(box.ey)
    sine_z, eig_z = sine_basis(box.deep)
    in_order_of_steps = np.arange(box.ey).reshape(8, box.ey // 8).T.reshape(-1)
    from_y = sine_y[MARGIN : MARGIN + box.across]
    from_x = sine_x[MARGIN : MARGIN + box.long]
    spread = np.broadcast_to(eig_x[:, None], (box.ex, box.deep))
    main_z, rest_z = right_tables(sine_z)
    return [
        jnp.asarray(np.ascontiguousarray(t))
        for t in (
            left_table(sine_y[:, in_order_of_steps], padded(box.ey), FORWARD),
            left_table(sine_x, padded(box.ex), FORWARD),
            left_table(from_x, padded(box.ex), BACKWARD),
            left_table(from_y, padded(box.ey), BACKWARD),
            main_z,
            rest_z,
            spread,
            eig_z[None, :],
            eig_y[None, :],
        )
    ]


N_TABLES = 9


def one_pass(left, right):
    return lax.dot_general(
        left,
        right,
        (((1,), (0,)), ((), ())),
        precision=lax.Precision.DEFAULT,
        preferred_element_type=jnp.float32,
    )


def dot_left(table, values, count, rows):
    total = one_pass(table, jnp.concatenate(pieces(values, count), axis=0))
    return sum(total[index * rows : (index + 1) * rows] for index in range(1, count)) + total[:rows]


def dot_right(values, main, rest, count):
    deep = values.shape[1]
    parts = pieces(values, count)
    total = one_pass(jnp.concatenate(parts[:2], axis=1), main)
    result = total[:, :deep] + total[:, deep:]
    if count == 3:
        result = result + one_pass(jnp.concatenate([parts[0], parts[2]], axis=1), rest)
    return result


def with_rows(values, rows):
    if values.shape[0] == rows:
        return values
    blank = jnp.zeros((rows - values.shape[0],) + values.shape[1:], values.dtype)
    return jnp.concatenate([values, blank], axis=0)


ABREAST = 8


def beside(values):
    return jnp.concatenate(values, axis=1)


def apart(values, lanes):
    return [values[:, start : start + lanes] for start in range(0, values.shape[1], lanes)]


def box_solve(box, source, divided, tables, row_mask, col_mask, spectral, middle, emit):
    into_y, into_x, from_x, from_y, main_z, rest_z = tables[:6]
    deep = box.deep
    deep_x, deep_y = padded(box.ex), padded(box.ey)
    into_y, into_x = into_y[...], into_x[...]
    if col_mask is not None:
        mask = jnp.concatenate([col_mask] * FORWARD, axis=1)
        into_y = into_y * mask
        mask = jnp.concatenate([row_mask] * FORWARD, axis=1)
        into_x = into_x * mask
    from_x, from_y, main_z, rest_z = from_x[...], from_y[...], main_z[...], rest_z[...]
    spectral_flat = spectral.reshape(box.ey * deep_x, deep)
    middle_flat = middle.reshape(box.long * deep_y, deep)
    if deep_x > box.ex:
        spectral[:, box.ex :, :] = jnp.zeros((box.ey, deep_x - box.ex, deep), jnp.float32)
    if deep_y > box.ey:
        middle[:, box.ey :, :] = jnp.zeros((box.long, deep_y - box.ey, deep), jnp.float32)
    for start in range(0, box.ex, 8):
        block = source(start).reshape(8 * box.ey, deep)
        block = dot_right(block, main_z, rest_z, FORWARD).reshape(8, box.ey, deep)
        for row in range(0, 8, ABREAST):
            wide = beside([block[row + part] for part in range(ABREAST)])
            wide = dot_left(into_y, with_rows(wide, deep_y), FORWARD, box.ey)
            for part, values in enumerate(apart(wide, deep)):
                place = pl.ds(start + row + part, box.ey, stride=deep_x)
                spectral_flat[place, :] = values
    for col in range(0, box.ey, ABREAST):
        wide = beside([spectral[col + part] for part in range(ABREAST)])
        wide = apart(dot_left(into_x, wide, FORWARD, box.ex), deep)
        wide = beside([divided(values, col + part) for part, values in enumerate(wide)])
        wide = dot_left(from_x, with_rows(wide, deep_x), BACKWARD, box.long)
        for part, values in enumerate(apart(wide, deep)):
            middle_flat[pl.ds(col + part, box.long, stride=deep_y), :] = values
    for start in range(0, box.long, 8):
        parts = []
        for row in range(start, start + 8, ABREAST):
            wide = beside([middle[row + part] for part in range(ABREAST)])
            parts += apart(dot_left(from_y, wide, BACKWARD, box.across), deep)
        emit(start, dot_right(jnp.concatenate(parts, axis=0), main_z, rest_z, BACKWARD))


def position():
    long_pos, across_pos = lax.axis_index("wide"), lax.axis_index("narrow")
    return long_pos, across_pos, lax.axis_size("wide"), lax.axis_size("narrow")


def as_float(flag):
    return jnp.where(flag, jnp.float32(1.0), jnp.float32(0.0))


def is_even(axis):
    return lax.rem(lax.axis_index(axis), 2) == 0


class Sides:
    def __init__(self, axis, first, second):
        position = lax.axis_index(axis)
        self.even = is_even(axis)
        self.has_low = as_float(position > 0)
        self.has_high = as_float(position < lax.axis_size(axis) - 1)
        self.first, self.second = first, second

    def low(self, *index):
        return jnp.where(self.even, self.second[index], self.first[index]) * self.has_low

    def high(self, *index):
        return jnp.where(self.even, self.first[index], self.second[index]) * self.has_high


def in_order(even, up, down):
    return jnp.where(even, up, down), jnp.where(even, down, up)


def row_of(stride, col, count, first=0):
    return pl.ds(first * stride + col, count, stride=stride)


def pack_columns(box, fields, wide_sides, wide, first, second):
    corner = len(fields) * wide * box.long
    even = is_even("narrow")
    place = 0
    for field, sides in zip(fields, wide_sides):
        for step in range(wide):
            cols = (box.across - wide + step, step)
            values = [field[row_of(box.across, col, box.long), :] for col in cols]
            low = [sides.low(row_of(box.across, col, wide), slice(None)) for col in cols]
            high = [sides.high(row_of(box.across, col, wide), slice(None)) for col in cols]
            at = corner + 2 * REACH * place
            for start, parts in ((place * box.long, values), (at, low), (at + REACH, high)):
                parts = in_order(even, *(part.astype(jnp.float32) for part in parts))
                size = parts[0].shape[0]
                first[start : start + size, :], second[start : start + size, :] = parts
            place += 1


def message_rows(box, count):
    return -(-(count * (box.long + 2 * REACH)) // 8) * 8


def pack_fields(box, wide, fields, tables, after, *refs):
    own, (low, high), refs = refs[:fields], refs[fields : fields + 2], refs[fields + 2 :]
    parts, (first, second, *table) = refs[:tables], refs[tables + after :]
    size = wide * box.across
    flat = [field.reshape(box.long * box.across, box.deep) for field in own]
    low = low.reshape(low.size // box.deep, box.deep)
    high = high.reshape(high.size // box.deep, box.deep)
    sides = [
        Sides("wide", *(ref.at[index * size : (index + 1) * size] for ref in (low, high)))
        for index in range(fields)
    ]
    pack_columns(box, flat, sides, wide, first, second)
    if tables:
        known = last_rows_merged(parts, table[0].shape[0])
        table[0][...] = known
        first[first.shape[0] - known.shape[0] :, :] = known
        second[second.shape[0] - known.shape[0] :, :] = known


def bring_edges(
    box, zone, scale, load, own_zone, own_scale, own_load, load_first, load_second, first, second,
    staged, sems
):
    even = is_even("wide")

    def edges(wide):
        up, down = box.long - wide, 0
        return [pl.ds(jnp.where(even, *pair), wide) for pair in ((up, down), (down, up))]

    copies = [
        (load.at[edges(MARGIN)[0]], load_first),
        (load.at[edges(MARGIN)[1]], load_second),
        (zone.at[edges(REACH)[0]], staged.at[0]),
        (zone.at[edges(REACH)[1]], staged.at[1]),
        (scale.at[edges(REACH)[0]], first.at[:REACH]),
        (scale.at[edges(REACH)[1]], second.at[:REACH]),
        (load, own_load),
        (scale, own_scale),
        (zone, own_zone),
    ]
    copies = [
        pltpu.make_async_copy(source, target, sems.at[index])
        for index, (source, target) in enumerate(copies)
    ]
    for copy in copies:
        copy.start()
    for copy in copies[:4]:
        copy.wait()
    first[REACH:] = staged[0].astype(jnp.float32)
    second[REACH:] = staged[1].astype(jnp.float32)
    for copy in copies[4:]:
        copy.wait()


def fill_window(box, window, own, wide_sides, narrow_sides, wide, place, total, add=None):
    flat = window.reshape(box.flat, box.deep)
    nothing = jnp.zeros((box.rows, EDGE, box.deep), jnp.float32)
    window[:, :EDGE, :] = nothing
    window[:, EDGE + box.across :, :] = nothing
    if add is None:
        add = lambda values, row_side, col_side: values
    inner = slice(EDGE, EDGE + box.across)
    first, last = REACH, REACH + box.long
    if wide < REACH:
        blank = jnp.zeros((1, box.across, box.deep), jnp.float32)
        window[0:1, inner, :] = blank
        window[box.rows - 1 :, inner, :] = blank
    window[first:last, inner, :] = add(own[...].astype(jnp.float32), 0, 0)
    window[first - wide : first, inner, :] = add(wide_sides.low(Ellipsis), -1, 0)
    window[last : last + wide, inner, :] = add(wide_sides.high(Ellipsis), 1, 0)
    corner = total * box.long
    for step in range(wide):
        for source, col, side in (
            (narrow_sides.low, EDGE - wide + step, -1),
            (narrow_sides.high, EDGE + box.across + step, 1),
        ):
            for start, size, row, row_side in (
                ((place + step) * box.long, box.long, first, 0),
                (corner + 2 * REACH * (place + step), wide, first - wide, -1),
                (corner + 2 * REACH * (place + step) + REACH, wide, last, 1),
            ):
                values = source(slice(start, start + size), slice(None))
                flat[row_of(box.cols, col, size, row), :] = add(values, row_side, side)


def some_cols(box, ref, row, step):
    stride = box.ey // 8
    return ref[row, pl.ds(EDGE - MARGIN + step, 8, stride=stride), :]


def negative_image(box, window, row, at, x, flow_before, weights):
    to_long, to_across, to_deep, mass = weights
    steps = range(box.ey // 8)
    x_next = [some_cols(box, window, row + 1, step) for step in range(-1, len(steps) + 1)]
    flow_long = [
        some_cols(box, to_long, at, step) * (x_next[step + 1] - x[step + 1]) for step in steps
    ]
    flow_across = [
        some_cols(box, to_across, at, step) * (x[step + 2] - x[step + 1])
        for step in range(-1, len(steps))
    ]
    totals = []
    for step in steps:
        here = x[step + 1]
        lanes = here.shape[1]
        flow_deep = some_cols(box, to_deep, at, step) * (pltpu.roll(here, lanes - 1, 1) - here)
        total = flow_long[step] - flow_before[step] - some_cols(box, mass, at, step) * here
        total = total + (flow_across[step + 1] - flow_across[step])
        totals.append(total + (flow_deep - pltpu.roll(flow_deep, 1, 1)))
    return totals, x_next, flow_long


def in_steps(box, refs, rows):
    return jnp.stack(
        [
            jnp.concatenate([some_cols(box, ref, row, step) for step in range(box.ey // 8)], axis=0)
            for ref, row in zip(refs, rows)
        ]
    )


def looked_up(labels, values):
    return jnp.where(labels == 0, values[0], jnp.where(labels == 1, values[1], values[2]))


def at_own_row(line, shape):
    long_pos, across_pos, _, across_count = position()
    rows = lax.broadcasted_iota(jnp.int32, shape, 0)
    own = rows == long_pos * across_count + across_pos
    return jnp.where(own, line[:1], jnp.zeros(shape, jnp.float32))


def merged(table, *others):
    for other in others:
        table = jnp.where(table != 0.0, table, other)
    return table


def last_rows_merged(refs, count):
    return merged(*(ref[ref.shape[0] - count :, :] for ref in refs))


def join_rows(table, message, out):
    out[...] = last_rows_merged((table, message), out.shape[0])


def line_of(numbers, shape):
    lanes = lax.broadcasted_iota(jnp.int32, shape, 1)
    line = jnp.zeros(shape, jnp.float32)
    for index, number in numbers:
        line = jnp.where(lanes == index, number, line)
    return line


def box_sums(box, zone, scale, load, after, diffusivity, decay, out, table):
    del after
    nothing = jnp.zeros((box.across, box.deep), jnp.float32)
    half = [[0.5 * diffusivity[z, d] for z in range(3)] for d in range(3)]
    rates = [decay[z] for z in range(3)]

    def halves(row):
        labels, factor = zone[row], scale[row]
        return [looked_up(labels, half[d]) * factor for d in range(3)] + [looked_up(labels, rates)]

    sums = [nothing] * 5
    for row in range(box.long):
        sums = [total + more for total, more in zip(sums, halves(row) + [load[row]])]

    def total(values):
        return jnp.sum(values, keepdims=True).reshape(1, 1)

    cells = box.long * box.across * box.deep
    numbers = [(index, total(sums[index]) * (2.0 / cells)) for index in range(3)]
    mass = total(sums[3])
    numbers += [(3, mass / cells)]
    ends = total(sums[2][:, :1]) + total(sums[2][:, box.deep - 1 :])
    numbers += [
        (BOX_DIAGONAL, mass + ends),
        (LONG_HIGH, total(halves(box.long - 1)[0])),
        (LONG_LOW, total(halves(0)[0])),
        (ACROSS_HIGH, total(sums[1][box.across - 1 :])),
        (ACROSS_LOW, total(sums[1][:1])),
        (LOAD_SUM, total(sums[4])),
    ]
    line = line_of(numbers, out.shape)
    out[...] = line
    table[...] = at_own_row(line, table.shape)


def means_of(ref):
    return [ref[0:1, index : index + 1] for index in range(4)]


def first_solve(box, load, low, high, left, right, means, zone, scale, diffusivity, decay, *rest):
    tables = rest[:N_TABLES]
    window, local, image, inverses, spectral, middle = rest[N_TABLES:]
    spread, eig_z, eig_y = tables[6:]
    means = means_of(means)
    base = means[3] + means[0] * spread[...] + means[2] * eig_z[...]

    def divided(values, col):
        divisor = base + means[1] * eig_y[0, col]
        inverse = pl.reciprocal(divisor, approx=True)
        for _ in range(2):
            inverse = inverse * (2.0 - divisor * inverse)
        inverses[col] = inverse
        return values * inverse

    half = [0.5 * diffusivity[z, 2] for z in range(3)]
    rates = [decay[z] for z in range(3)]
    lane = lax.broadcasted_iota(jnp.int32, (box.across, box.deep), 1)
    ends = jnp.where((lane == 0) | (lane == box.deep - 1), jnp.float32(1.0), jnp.float32(0.0))
    image[...] = jnp.zeros((box.across, box.deep), jnp.float32)
    wide_sides, narrow_sides = Sides("wide", low, high), Sides("narrow", left, right)
    fill_window(box, window, load, wide_sides, narrow_sides, MARGIN, 0, MARGIN)

    def emit(start, values):
        values = values * (1.0 / cheb_center)
        values = values.reshape(8, box.across, box.deep)
        local[start : start + 8] = values
        total = image[...]
        for row in range(8):
            labels = zone[start + row]
            mass = looked_up(labels, rates) + looked_up(labels, half) * scale[start + row] * ends
            total = total + mass * values[row]
        image[...] = total

    box_solve(
        box,
        lambda start: in_steps(box, [window] * 8, range(1 + start, 9 + start)),
        divided,
        tables,
        None,
        None,
        spectral,
        middle,
        emit,
    )


def side_weights(
    box, zone, scale, low, high, left, right, diffusivity, to_long, to_across, zone_window,
    scale_window
):
    for index, (window, own) in enumerate(((scale_window, scale), (zone_window, zone))):
        start = index * REACH
        wide_sides = Sides("wide", *(ref.at[start : start + REACH] for ref in (low, high)))
        narrow_sides = Sides("narrow", left, right)
        fill_window(box, window, own, wide_sides, narrow_sides, REACH, start, 2 * REACH)
    half = [[0.5 * diffusivity[z, d] for z in range(3)] for d in range(2)]

    def one_row(row, before):
        labels, factor = zone_window[row], scale_window[row]
        now = [looked_up(labels, half[d]) * factor for d in range(2)]
        to_across[row] = now[1] + pltpu.roll(now[1], box.cols - 1, 0)
        to_long[jnp.maximum(row - 1, 0)] = before + now[0]
        return now[0]

    def some_rows(index, before):
        for row in range(8):
            before = one_row(index * 8 + row, before)
        return before

    before = jnp.zeros((box.cols, box.deep), jnp.float32)
    before = lax.fori_loop(0, box.rows // 8, some_rows, before)
    for row in range(box.rows // 8 * 8, box.rows):
        before = one_row(row, before)
    to_long[box.rows - 1] = before


def deep_weights(box, zone_window, scale_window, diffusivity, decay, to_deep, mass):
    half = [0.5 * diffusivity[z, 2] for z in range(3)]
    rates = [decay[z] for z in range(3)]
    lane = lax.broadcasted_iota(jnp.int32, (box.cols, box.deep), 1)
    ends = jnp.where((lane == 0) | (lane == box.deep - 1), jnp.float32(1.0), jnp.float32(0.0))
    not_last = jnp.where(lane == box.deep - 1, jnp.float32(0.0), jnp.float32(1.0))

    def one_row(row):
        labels = zone_window[row]
        now = looked_up(labels, half) * scale_window[row]
        to_deep[row] = (now + pltpu.roll(now, box.deep - 1, 1)) * not_last
        mass[row] = looked_up(labels, rates) + now * ends

    def some_rows(index, _):
        for row in range(8):
            one_row(index * 8 + row)
        return 0

    lax.fori_loop(0, box.rows // 8, some_rows, 0)
    for row in range(box.rows // 8 * 8, box.rows):
        one_row(row)


def image_sums(
    box, zone, scale, local, image, low, high, left, right, table, diffusivity, out, up, down
):
    half = [[0.5 * diffusivity[z, d] for z in range(3)] for d in range(3)]
    shape = (box.long * box.across, box.deep)
    zone_flat, scale_flat, local_flat = zone.reshape(shape), scale.reshape(shape), local.reshape(shape)
    last_col = row_of(box.across, box.across - 1, box.long)
    first_col = row_of(box.across, 0, box.long)

    wide_sides, narrow_sides = Sides("wide", low, high), Sides("narrow", left, right)

    def side(source, place):
        return source(slice(place * box.long, (place + 1) * box.long), slice(None))

    above, below = wide_sides.high, wide_sides.low
    faces = [
        (0, zone[box.long - 1], scale[box.long - 1], local[box.long - 1], above(REACH), above(0)),
        (0, zone[0], scale[0], local[0], below(2 * REACH - 1), below(REACH - 1)),
        (
            1,
            zone_flat[last_col, :],
            scale_flat[last_col, :],
            local_flat[last_col, :],
            side(narrow_sides.high, REACH),
            side(narrow_sides.high, 0),
        ),
        (
            1,
            zone_flat[first_col, :],
            scale_flat[first_col, :],
            local_flat[first_col, :],
            side(narrow_sides.low, 2 * REACH - 1),
            side(narrow_sides.low, REACH - 1),
        ),
    ]
    flows = []
    for direction, labels, factor, values, far_labels, far_factor in faces:
        weight = looked_up(labels, half[direction]) * factor
        weight = weight + looked_up(far_labels, half[direction]) * far_factor
        flows.append(jnp.sum(weight * values, keepdims=True))
    long_pos, across_pos, long_count, across_count = position()
    numbers = [
        (IMAGE_SUM, jnp.sum(image[...], keepdims=True) + sum(flows)),
        (FLOW_LONG_HIGH, flows[0] * as_float(long_pos < long_count - 1)),
        (FLOW_LONG_LOW, flows[1] * as_float(long_pos > 0)),
        (FLOW_ACROSS_HIGH, flows[2] * as_float(across_pos < across_count - 1)),
        (FLOW_ACROSS_LOW, flows[3] * as_float(across_pos > 0)),
    ]
    known = table[...] + at_own_row(line_of(numbers, (8, out.shape[1])), out.shape)
    out[...] = known
    edge = REACH * box.across
    even = is_even("wide")
    for target, pair in ((up, (box.long - REACH, 0)), (down, (0, box.long - REACH))):
        target[:edge] = local[pl.ds(jnp.where(even, *pair), REACH)].reshape(edge, box.deep)
        target[edge:] = known


def column(values, index):
    return values[:, index : index + 1]


def coarse_inverse(numbers, work):
    count, width = work.shape
    across = lax.axis_size("narrow")
    beyond = pltpu.roll(numbers, count - across, 0)
    beside = pltpu.roll(numbers, count - 1, 0)
    before = pltpu.roll(numbers, across, 0)
    ahead = pltpu.roll(numbers, 1, 0)
    place = lax.broadcasted_iota(jnp.int32, (count, 1), 0)
    across_pos = lax.rem(place, across)
    nothing = jnp.zeros((count, 1), jnp.float32)
    couplings = []
    diagonal = column(numbers, BOX_DIAGONAL)
    for own, other, there, inside in (
        (LONG_HIGH, LONG_LOW, beyond, place < count - across),
        (LONG_LOW, LONG_HIGH, before, place >= across),
        (ACROSS_HIGH, ACROSS_LOW, beside, across_pos < across - 1),
        (ACROSS_LOW, ACROSS_HIGH, ahead, across_pos > 0),
    ):
        shared = jnp.where(inside, column(there, other), nothing)
        diagonal = diagonal + column(numbers, own) + shared
        couplings.append(jnp.where(inside, column(numbers, own) + shared, nothing))
    rows = lax.broadcasted_iota(jnp.int32, (count, width), 0)
    cols = lax.broadcasted_iota(jnp.int32, (count, width), 1)
    blank = jnp.zeros((count, width), jnp.float32)
    matrix = jnp.where(cols == rows, diagonal, blank)
    for shift, coupling in zip((across, -across, 1, -1), couplings):
        matrix = matrix - jnp.where((cols == rows + shift) & (cols < count), coupling, blank)
    matrix = jnp.where(cols == rows + count, jnp.ones((count, 1), jnp.float32), matrix)
    if count <= 16:
        for step in range(count):
            pivot_row = matrix[step : step + 1, :] / matrix[step : step + 1, step : step + 1]
            rest = matrix - matrix[:, step : step + 1] * pivot_row
            matrix = jnp.where(rows == step, pivot_row, rest)
        return pltpu.roll(matrix, width - count, 1)
    work[...] = matrix

    def eliminate(step, _):
        values = work[...]
        pivot_row = work[pl.ds(step, 1), :]
        at_step = cols == step
        factors = jnp.sum(jnp.where(at_step, values, blank), axis=1, keepdims=True)
        pivot = jnp.sum(jnp.where(at_step[:1], pivot_row, blank[:1]), axis=1, keepdims=True)
        pivot_row = pivot_row / pivot
        work[...] = jnp.where(rows == step, pivot_row, values - factors * pivot_row)
        return 0

    lax.fori_loop(0, count, eliminate, 0)
    values = work[...]
    if count % 128:
        return pltpu.roll(values, width - count, 1)
    return values[:, count : 2 * count]


def answer(inverse, sums):
    return jnp.sum(inverse * sums, axis=0, keepdims=True)


def at_box(values, row_side, col_side):
    long_pos, across_pos, long_count, across_count = position()
    there_long, there_across = long_pos + row_side, across_pos + col_side
    inside = (
        (there_long >= 0)
        & (there_long < long_count)
        & (there_across >= 0)
        & (there_across < across_count)
    )
    lanes = lax.broadcasted_iota(jnp.int32, values.shape, 1)
    wanted = (lanes == there_long * across_count + there_across) & inside
    return jnp.sum(jnp.where(wanted, values, jnp.zeros_like(values)), axis=1, keepdims=True)


def coarse_corrections(parts, *refs):
    table_parts, (out, work) = refs[:parts], refs[parts:]
    count = work.shape[0]
    numbers = last_rows_merged(table_parts, count)
    across_count = lax.axis_size("narrow")
    inverse = coarse_inverse(numbers, work)
    sums = column(numbers, IMAGE_SUM)
    sums = sums - column(pltpu.roll(numbers, count - across_count, 0), FLOW_LONG_LOW)
    sums = sums - column(pltpu.roll(numbers, across_count, 0), FLOW_LONG_HIGH)
    sums = sums - column(pltpu.roll(numbers, count - 1, 0), FLOW_ACROSS_LOW)
    sums = sums - column(pltpu.roll(numbers, 1, 0), FLOW_ACROSS_HIGH)
    load_sums = column(numbers, LOAD_SUM)
    sums = load_sums * (1.0 - 1.0 / cheb_center) - sums
    out[0:1, :] = answer(inverse, load_sums) * (1.0 / cheb_center)
    out[1:2, :] = answer(inverse, sums) * gain


def second_solve(box, local, low, high, left, right, inverses, answers, *rest):
    to_long, to_across, to_deep, mass, load_window = rest[:5]
    tables = rest[5 : 5 + N_TABLES]
    iterate, top, bottom, last_col, first_col, out = rest[5 + N_TABLES : 11 + N_TABLES]
    window, spectral, middle, sems = rest[11 + N_TABLES :]
    long_pos, across_pos, long_count, across_count = position()
    coarse = answers[0:1, :]
    own_shift = at_box(answers[1:2, :], 0, 0)
    shifts = {
        (row_side, col_side): at_box(coarse, row_side, col_side)
        for row_side in (-1, 0, 1)
        for col_side in (-1, 0, 1)
    }

    def add(values, row_side, col_side):
        shift = shifts[row_side, col_side]
        if values.ndim == 3:
            shift = shift.reshape(1, 1, 1)
        return values + shift

    edge = REACH * box.across
    low, high = (
        ref.at[:edge].reshape(REACH, box.across, box.deep) for ref in (low, high)
    )
    wide_sides, narrow_sides = Sides("wide", low, high), Sides("narrow", left, right)
    fill_window(box, window, local, wide_sides, narrow_sides, REACH, 0, REACH, add)
    weights = (to_long, to_across, to_deep, mass)

    steps = range(box.ey // 8)
    x = [some_cols(box, window, 1, step) for step in range(-1, len(steps) + 1)]
    flow = [
        some_cols(box, to_long, 0, step) * (x[step + 1] - some_cols(box, window, 0, step))
        for step in steps
    ]
    state = [x, flow]

    def divided(values, col):
        return values * inverses[col]

    def residual(start_row):
        rows = []
        for row in range(start_row + 1, start_row + 9):
            image, *state[:] = negative_image(box, window, row, row, *state, weights)
            image = [some_cols(box, load_window, row, step) + image[step] for step in steps]
            rows.append(jnp.concatenate(image, axis=0))
        return jnp.stack(rows)

    inner = slice(EDGE, EDGE + box.across)
    first = REACH
    row_ids = lax.broadcasted_iota(jnp.int32, (1, padded(box.ex)), 1)
    col_ids = lax.broadcasted_iota(jnp.int32, (1, padded(box.ey)), 1)
    col_ids = (col_ids & 7) * (box.ey // 8) + lax.shift_right_logical(col_ids, 3)
    row_mask = jnp.where(row_ids < MARGIN, as_float(long_pos > 0), 1.0)
    row_mask = jnp.where(row_ids >= MARGIN + box.long, as_float(long_pos < long_count - 1), row_mask)
    col_mask = jnp.where(col_ids < MARGIN, as_float(across_pos > 0), 1.0)
    col_mask = jnp.where(
        col_ids >= MARGIN + box.across, as_float(across_pos < across_count - 1), col_mask
    )
    keep = 1.0 + rho_second * rho_first
    copies = []

    def emit(start, values):
        rows = values.reshape(8, box.across, box.deep)
        before = window[first + start : first + start + 8, inner, :]
        shift = own_shift.reshape(1, 1, 1)
        iterate[start : start + 8] = keep * before + (gain * rows + shift)
        copies.append(
            pltpu.make_async_copy(
                iterate.at[start : start + 8], out.at[start : start + 8], sems.at[len(copies)]
            )
        )
        copies[-1].start()

    box_solve(
        box, residual, divided, tables, row_mask, col_mask, spectral, middle, emit
    )
    rows = in_order(is_even("wide"), iterate[box.long - 1], iterate[0])
    top[...], bottom[...] = rows
    flat = iterate.reshape(box.long * box.across, box.deep)
    cols = [flat[row_of(box.across, col, box.long), :] for col in (box.across - 1, 0)]
    last_col[...], first_col[...] = in_order(is_even("narrow"), *cols)
    for copy in copies:
        copy.wait()


def inner_residual(
    box, load, iterate, to_long, to_across, to_deep, mass, rows, cols, out, window, result, sems
):
    inner = slice(EDGE, EDGE + box.across)
    flat = window.reshape((box.long + 2) * box.cols, box.deep)
    iterate_flat = iterate.reshape(box.long * box.across, box.deep)
    blank = jnp.zeros((box.long + 2, EDGE, box.deep), jnp.float32)
    window[:, :EDGE, :] = blank
    window[:, EDGE + box.across :, :] = blank
    window[1 : 1 + box.long, inner, :] = iterate[...]
    window[0, inner, :] = iterate[0]
    window[1 + box.long, inner, :] = iterate[box.long - 1]
    for col, place in ((0, EDGE - 1), (box.across - 1, EDGE + box.across)):
        values = iterate_flat[row_of(box.across, col, box.long), :]
        flat[row_of(box.cols, place, box.long, 1), :] = values
    weights = (to_long, to_across, to_deep, mass)
    steps = range(box.ey // 8)
    x = [some_cols(box, window, 1, step) for step in range(-1, len(steps) + 1)]
    flow = [jnp.zeros((8, box.deep), jnp.float32) for _ in steps]
    middle = slice(8, box.across - 8)
    copies = []
    for row in range(box.long):
        image, x, flow = negative_image(box, window, row + 1, REACH + row, x, flow, weights)
        for step in steps:
            place = pl.ds(EDGE - MARGIN + step, 8, stride=box.ey // 8)
            result[row, place, :] = image[step]
        values = load[row] + result[row, inner]
        result[row, inner] = values
        cols[0, row] = values[:8]
        cols[1, row] = values[box.across - 8 :]
        if row == 0:
            rows[0] = values
        if row == box.long - 1:
            rows[1] = values
        if row % 8 == 7:
            part = slice(row - 7, row + 1)
            copy = pltpu.make_async_copy(
                result.at[part, EDGE + 8 : EDGE + box.across - 8],
                out.at[part, middle],
                sems.at[row // 8],
            )
            copy.start()
            copies.append(copy)
    for copy in copies:
        copy.wait()


def outer_residual(
    box, iterate, low, high, left, right, to_long, to_across, rows, cols, inner_out, out,
    row_part, col_part, sems
):
    del inner_out
    inner = slice(EDGE, EDGE + box.across)
    middle = slice(8, box.across - 8)
    wide_sides, narrow_sides = Sides("wide", low, high), Sides("narrow", left, right)
    last = box.long - 1
    iterate_flat = iterate.reshape(box.long * box.across, box.deep)
    across_flat = to_across.reshape(box.flat, box.deep)
    below = to_long[REACH - 1, inner] * (wide_sides.low(Ellipsis) - iterate[0])
    above = to_long[REACH + last, inner] * (wide_sides.high(Ellipsis) - iterate[last])
    row_part[0] = (rows[0] + below)[middle]
    row_part[1] = (rows[1] + above)[middle]
    copies = [
        pltpu.make_async_copy(row_part.at[0], out.at[0, middle], sems.at[0]),
        pltpu.make_async_copy(row_part.at[1], out.at[last, middle], sems.at[1]),
    ]
    for copy in copies:
        copy.start()
    col_part[...] = cols[...]
    flat = col_part.reshape(2 * box.long * 8, box.deep)
    for side, (from_side, col, face, tile) in enumerate(
        (
            (narrow_sides.low, 0, EDGE - 1, slice(0, 8)),
            (narrow_sides.high, box.across - 1, EDGE + box.across - 1, slice(box.across - 8, None)),
        )
    ):
        weight = across_flat[row_of(box.cols, face, box.long, REACH), :]
        own = iterate_flat[row_of(box.across, col, box.long), :]
        place = pl.ds(side * box.long * 8 + side * 7, box.long, stride=8)
        flat[place, :] = flat[place, :] + weight * (from_side(Ellipsis) - own)
        col_part[side, 0] = col_part[side, 0] + below[tile]
        col_part[side, last] = col_part[side, last] + above[tile]
        first_col = side * (box.across - 8)
        copy = pltpu.make_async_copy(
            col_part.at[side], out.at[:, first_col : first_col + 8], sems.at[2 + side]
        )
        copy.start()
        copies.append(copy)
    for copy in copies:
        copy.wait()


def swaps(axis, around):
    sizes = (lax.axis_size("wide"), lax.axis_size("narrow"))
    along = ("wide", "narrow").index(axis)
    size, beside = sizes[along], sizes[1 - along]

    def number(place, other_place):
        pair = (place, other_place) if along == 0 else (other_place, place)
        return pair[0] * sizes[1] + pair[1]

    ways = []
    for way in range(2):
        pairs = []
        for place in range(size):
            for other_place in range(beside):
                partner = place + 1 if place % 2 == way else place - 1
                there = other_place
                if around and size % 2 == 0:
                    partner %= size
                if not 0 <= partner < size:
                    partner = place
                    there = other_place ^ 1 if beside % 2 == 0 else other_place
                pairs.append((number(place, other_place), number(partner, there)))
        ways.append(pairs)
    return ways


def exchange(axis, first, second, around=False):
    ways = swaps(axis, around)
    axes = ("wide", "narrow")
    return lax.ppermute(first, axes, ways[0]), lax.ppermute(second, axes, ways[1])


def two_away(axis, table):
    size = lax.axis_size(axis)
    return lax.ppermute(table, axis, [(i, (i + 2) % size) for i in range(size)])


def tell(table):
    count = table.shape[0]
    long_pos, across_pos, _, across_count = position()
    own = lax.dynamic_slice_in_dim(table, long_pos * across_count + across_pos, 1, axis=0)
    line = jnp.broadcast_to(own, (count, 1, 128))
    told = lax.all_to_all(line, ("wide", "narrow"), split_axis=0, concat_axis=0, tiled=True)
    return told.reshape(count, 128)


def on_device(zone, scale, diffusivity, decay, load):
    box = Box(load.shape)
    long, across, deep = load.shape
    count = lax.axis_size("wide") * lax.axis_size("narrow")
    by_margins = lax.axis_size("wide") == 4 and lax.axis_size("narrow") == 4
    tables = tables_of(box)
    cells = f32(long, across, deep)
    whole_zone = jax.ShapeDtypeStruct(cells.shape, zone.dtype)
    window = f32(box.rows, box.cols, deep)
    table_shape = f32(count, 128)
    anywhere = pl.BlockSpec(memory_space=pl.ANY)
    in_hbm = pl.BlockSpec(memory_space=pltpu.HBM)

    def scratch(shape):
        return pltpu.VMEM(shape, jnp.float32)

    def pinned(field):
        return pltpu.with_memory_space_constraint(field, pltpu.HBM)

    spectral = scratch((box.ey, padded(box.ex), deep))
    middle = scratch((long, padded(box.ey), deep))

    def pack(wide, fields, sides, parts=(), after=()):
        rows = message_rows(box, wide * len(fields)) + (count if parts else 0)
        message = f32(rows, deep)
        body = functools.partial(pack_fields, box, wide, len(fields), len(parts), len(after))
        return call(
            body,
            (message, message) + ((table_shape,) if parts else ()),
            [VMEM] * (len(fields) + 2 + len(parts)) + [anywhere] * len(after),
        )(*fields, *sides, *parts, *after)

    far = f32(2 * REACH, across, deep)
    zone, scale, load, load_first, load_second, first, second = call(
        functools.partial(bring_edges, box),
        (whole_zone, cells, cells) + (f32(MARGIN, across, deep),) * 2 + (far, far),
        [in_hbm] * 3,
        [pltpu.VMEM((2, REACH, across, deep), zone.dtype), pltpu.SemaphoreType.DMA((9,))],
    )(pinned(zone), pinned(scale), pinned(load))
    load_wide = exchange("wide", load_first, load_second)
    far_wide = exchange("wide", first, second)
    load_first, load_second = pack(MARGIN, [load], load_wide)
    load_narrow = exchange("narrow", load_first, load_second)
    sums, table = call(
        functools.partial(box_sums, box),
        (f32(8, 128), table_shape),
        [VMEM] * 3 + [anywhere] + [SMEM] * 2,
    )(zone, scale, load, load_first, diffusivity, decay)
    far_narrow = exchange("narrow", *pack(REACH, [scale, zone], far_wide))
    load_window, local, image, inverses = call(
        functools.partial(first_solve, box),
        (window, cells, f32(across, deep), f32(box.ey, box.ex, deep)),
        [VMEM] * 8 + [SMEM] * 2 + [VMEM] * N_TABLES,
        [spectral, middle],
        flops=4 * 10**9,
    )(load, *load_wide, *load_narrow, sums, zone, scale, diffusivity, decay, *tables)
    message = f32(REACH * across + count, deep)
    table, first, second = call(
        functools.partial(image_sums, box), (table_shape, message, message), [VMEM] * 9 + [SMEM]
    )(zone, scale, local, image, *far_wide, *far_narrow, table, diffusivity)
    own_table = table
    wide = exchange("wide", first, second, by_margins)
    parts = (table, *wide)
    if by_margins:
        parts += (two_away("wide", table),)
    to_long, to_across, *windows = call(
        functools.partial(side_weights, box),
        (window,) * 4,
        [VMEM] * 6 + [SMEM],
        flops=10**9,
    )(zone, scale, *far_wide, *far_narrow, diffusivity)
    to_deep, mass = call(
        functools.partial(deep_weights, box),
        (window,) * 2,
        [VMEM] * 2 + [SMEM] * 2,
        flops=10**9,
    )(*windows, diffusivity, decay)
    weights = (to_long, to_across, to_deep, mass)
    first, second, table = pack(REACH, [local], wide, parts, [to_long])
    narrow = exchange("narrow", first, second)
    if by_margins:
        table = call(join_rows, table_shape, [VMEM] * 2)(table, narrow[0])
        parts = (table, two_away("narrow", table))
    else:
        parts = (tell(own_table),)
    row, col = f32(across, deep), f32(long, deep)
    answers = call(
        functools.partial(coarse_corrections, len(parts)),
        f32(8, -(-count // 128) * 128),
        [VMEM] * len(parts),
        [scratch((count, -(-2 * count // 128) * 128))],
    )(*parts)
    iterate, first_row, second_row, first_col, second_col, result = call(
        functools.partial(second_solve, box),
        (cells, row, row, col, col, cells),
        [VMEM] * (12 + N_TABLES),
        [scratch(window.shape), spectral, middle, pltpu.SemaphoreType.DMA((long // 8,))],
        flops=4 * 10**9,
        out_spec=(VMEM,) * 5 + (anywhere,),
    )(local, *wide, *narrow, inverses, answers, *weights, load_window, *tables)
    narrow = exchange("narrow", first_col, second_col)
    wide = exchange("wide", first_row, second_row)
    rows, cols, inner = call(
        functools.partial(inner_residual, box),
        (f32(2, across, deep), f32(2, long, 8, deep), cells),
        [VMEM] * 6,
        [
            scratch((long + 2, box.cols, deep)),
            scratch((long, box.cols, deep)),
            pltpu.SemaphoreType.DMA((long // 8,)),
        ],
        flops=10**9,
        out_spec=(VMEM, VMEM, anywhere),
    )(load, iterate, *weights)
    residual = call(
        functools.partial(outer_residual, box),
        cells,
        [VMEM] * 9 + [anywhere],
        [
            scratch((2, across - 16, deep)),
            scratch((2, long, 8, deep)),
            pltpu.SemaphoreType.DMA((4,)),
        ],
        out_spec=anywhere,
        aliases={9: 0},
    )(iterate, *wide, *narrow, to_long, to_across, rows, cols, inner)
    return result, residual


def solution(mesh):
    split = P(("groups", "wide"), "narrow", None)
    return jax.shard_map(
        on_device,
        mesh=mesh,
        in_specs=(split, split, P(), P(), split),
        out_specs=(split, split),
        check_vma=False,
    )
```

```python
import functools

import jax
import jax.numpy as jnp
import ml_dtypes
import numpy as np
from jax import lax
from jax.experimental import pallas as pl
from jax.experimental.pallas import tpu as pltpu
from jax.sharding import PartitionSpec as P

MARGIN = 4
REACH = MARGIN + 1
EDGE = 8

cheb_center = 1.3
cheb_radius = 1.2
cheb_ratio = 1.3 / 1.2
rho_first = 1.0 / cheb_ratio
rho_second = 1.0 / (2.0 * cheb_ratio - rho_first)
gain = 2.0 * rho_second / cheb_radius

MEANS = range(4)
BOX_DIAGONAL, LONG_HIGH, LONG_LOW, ACROSS_HIGH, ACROSS_LOW, LOAD_SUM = range(4, 10)
IMAGE_SUM, FLOW_LONG_HIGH, FLOW_LONG_LOW, FLOW_ACROSS_HIGH, FLOW_ACROSS_LOW = range(16, 21)

VMEM = pl.BlockSpec(memory_space=pltpu.VMEM)
SMEM = pl.BlockSpec(memory_space=pltpu.SMEM)


def sine_basis(length):
    indices = np.arange(1, length + 1)
    phases = indices[:, None] * indices[None, :] % (2 * (length + 1))
    table = np.sqrt(2.0 / (length + 1)) * np.sin(np.pi * phases / (length + 1))
    eigvals = 4.0 * np.sin(np.pi * indices / (2.0 * (length + 1))) ** 2
    return table.astype(np.float32), eigvals.astype(np.float32)


def call(body, out_shape, in_specs, scratch=(), flops=0, out_spec=None, aliases=None):
    return pl.pallas_call(
        body,
        out_shape=out_shape,
        in_specs=in_specs,
        out_specs=out_spec or jax.tree.map(lambda _: VMEM, out_shape),
        scratch_shapes=list(scratch),
        compiler_params=pltpu.CompilerParams(vmem_limit_bytes=30 * 2**20),
        cost_estimate=pl.CostEstimate(flops=flops, bytes_accessed=0, transcendentals=0),
        input_output_aliases=aliases or {},
    )


def f32(*shape):
    return jax.ShapeDtypeStruct(shape, jnp.float32)


class Box:
    def __init__(self, shape):
        self.long, self.across, self.deep = shape
        self.ex = self.long + 2 * MARGIN
        self.ey = self.across + 2 * MARGIN
        self.rows = self.long + 2 * REACH
        self.cols = self.across + 2 * EDGE
        self.flat = self.rows * self.cols


def pieces(values, count):
    parts = []
    for _ in range(count - 1):
        scaled = values * 65537.0
        part = scaled - (scaled - values)
        parts.append(part)
        values = values - part
    return parts + [values]


def left_table(table, depth, count):
    rows, cols = table.shape
    wide = np.zeros((rows, depth), np.float32)
    wide[:, :cols] = table
    parts = []
    rest = wide
    for _ in range(count):
        part = rest.astype(ml_dtypes.bfloat16).astype(np.float32)
        parts.append(part)
        rest = rest - part
    blank = np.zeros_like(parts[0])
    lines = []
    for index in range(count):
        used = count - index if count > 2 else count
        lines.append(np.concatenate([parts[index]] * used + [blank] * (count - used), axis=1))
    return np.concatenate(lines, axis=0)


def right_tables(table):
    rest, parts = table, []
    for _ in range(3):
        part = rest.astype(ml_dtypes.bfloat16).astype(np.float32)
        parts.append(part)
        rest = rest - part
    both = np.concatenate([parts[0], parts[1]], axis=1)
    return np.concatenate([both, both], axis=0), np.concatenate([parts[2], parts[0]], axis=0)


def padded(size):
    return -(-size // 8) * 8


FORWARD, BACKWARD = 2, 3


def tables_of(box):
    sine_x, eig_x = sine_basis(box.ex)
    sine_y, eig_y = sine_basis(box.ey)
    sine_z, eig_z = sine_basis(box.deep)
    in_order_of_steps = np.arange(box.ey).reshape(8, box.ey // 8).T.reshape(-1)
    from_y = sine_y[MARGIN : MARGIN + box.across]
    from_x = sine_x[MARGIN : MARGIN + box.long]
    spread_x = np.broadcast_to(eig_x[:, None], (box.ex, box.deep))
    spread_y = np.broadcast_to(eig_y[:, None], (box.ey, box.deep))
    main_z, rest_z = right_tables(sine_z)
    return [
        jnp.asarray(np.ascontiguousarray(t))
        for t in (
            left_table(sine_y[:, in_order_of_steps], padded(box.ey), FORWARD),
            left_table(sine_x, padded(box.ex), FORWARD),
            left_table(from_x, padded(box.ex), BACKWARD),
            left_table(from_y, padded(box.ey), BACKWARD),
            main_z,
            rest_z,
            spread_x,
            spread_y,
            eig_z[None, :],
        )
    ]


N_TABLES = 9


def one_pass(left, right):
    return lax.dot_general(
        left,
        right,
        (((1,), (0,)), ((), ())),
        precision=lax.Precision.DEFAULT,
        preferred_element_type=jnp.float32,
    )


def dot_left(table, values, count, rows):
    total = one_pass(table, jnp.concatenate(pieces(values, count), axis=0))
    return sum(total[index * rows : (index + 1) * rows] for index in range(1, count)) + total[:rows]


def dot_right(values, main, rest, count):
    deep = values.shape[1]
    parts = pieces(values, count)
    total = one_pass(jnp.concatenate(parts[:2], axis=1), main)
    result = total[:, :deep] + total[:, deep:]
    if count == 3:
        result = result + one_pass(jnp.concatenate([parts[0], parts[2]], axis=1), rest)
    return result


def with_rows(values, rows):
    if values.shape[0] == rows:
        return values
    blank = jnp.zeros((rows - values.shape[0],) + values.shape[1:], values.dtype)
    return jnp.concatenate([values, blank], axis=0)


ABREAST = 8


def beside(values):
    return jnp.concatenate(values, axis=1)


def apart(values, lanes):
    return [values[:, start : start + lanes] for start in range(0, values.shape[1], lanes)]


def box_solve(box, source, divided, tables, row_mask, col_mask, spectral, middle, emit):
    into_y, into_x, from_x, from_y, main_z, rest_z = tables[:6]
    deep = box.deep
    deep_x, deep_y = padded(box.ex), padded(box.ey)
    into_y, into_x = into_y[...], into_x[...]
    if col_mask is not None:
        mask = jnp.concatenate([col_mask] * FORWARD, axis=1)
        into_y = into_y * mask
        mask = jnp.concatenate([row_mask] * FORWARD, axis=1)
        into_x = into_x * mask
    from_x, from_y, main_z, rest_z = from_x[...], from_y[...], main_z[...], rest_z[...]
    spectral_flat = spectral.reshape(box.ey * deep_x, deep)
    middle_flat = middle.reshape(box.long * deep_y, deep)
    if deep_x > box.ex:
        spectral[:, box.ex :, :] = jnp.zeros((box.ey, deep_x - box.ex, deep), jnp.float32)
    if deep_y > box.ey:
        middle[:, box.ey :, :] = jnp.zeros((box.long, deep_y - box.ey, deep), jnp.float32)
    for start in range(0, box.ex, 8):
        block = source(start).reshape(8 * box.ey, deep)
        block = dot_right(block, main_z, rest_z, FORWARD).reshape(8, box.ey, deep)
        for row in range(0, 8, ABREAST):
            wide = beside([block[row + part] for part in range(ABREAST)])
            wide = dot_left(into_y, with_rows(wide, deep_y), FORWARD, box.ey)
            for part, values in enumerate(apart(wide, deep)):
                place = pl.ds(start + row + part, box.ey, stride=deep_x)
                spectral_flat[place, :] = values
    for col in range(0, box.ey, ABREAST):
        wide = beside([spectral[col + part] for part in range(ABREAST)])
        wide = apart(dot_left(into_x, wide, FORWARD, box.ex), deep)
        wide = beside([divided(values, col + part) for part, values in enumerate(wide)])
        wide = dot_left(from_x, with_rows(wide, deep_x), BACKWARD, box.long)
        for part, values in enumerate(apart(wide, deep)):
            middle_flat[pl.ds(col + part, box.long, stride=deep_y), :] = values
    for start in range(0, box.long, 8):
        parts = []
        for row in range(start, start + 8, ABREAST):
            wide = beside([middle[row + part] for part in range(ABREAST)])
            parts += apart(dot_left(from_y, wide, BACKWARD, box.across), deep)
        emit(start, dot_right(jnp.concatenate(parts, axis=0), main_z, rest_z, BACKWARD))


def position():
    long_pos, across_pos = lax.axis_index("wide"), lax.axis_index("narrow")
    return long_pos, across_pos, lax.axis_size("wide"), lax.axis_size("narrow")


def as_float(flag):
    return jnp.where(flag, jnp.float32(1.0), jnp.float32(0.0))


def is_even(axis):
    return lax.rem(lax.axis_index(axis), 2) == 0


class Sides:
    def __init__(self, axis, first, second):
        position = lax.axis_index(axis)
        self.even = is_even(axis)
        self.has_low = as_float(position > 0)
        self.has_high = as_float(position < lax.axis_size(axis) - 1)
        self.first, self.second = first, second

    def low(self, *index):
        return jnp.where(self.even, self.second[index], self.first[index]) * self.has_low

    def high(self, *index):
        return jnp.where(self.even, self.first[index], self.second[index]) * self.has_high


def in_order(even, up, down):
    return jnp.where(even, up, down), jnp.where(even, down, up)


def row_of(stride, col, count, first=0):
    return pl.ds(first * stride + col, count, stride=stride)


def pack_columns(box, fields, wide_sides, wide, first, second):
    corner = len(fields) * wide * box.long
    even = is_even("narrow")
    place = 0
    for field, sides in zip(fields, wide_sides):
        for step in range(wide):
            cols = (box.across - wide + step, step)
            values = [field[row_of(box.across, col, box.long), :] for col in cols]
            low = [sides.low(row_of(box.across, col, wide), slice(None)) for col in cols]
            high = [sides.high(row_of(box.across, col, wide), slice(None)) for col in cols]
            at = corner + 2 * REACH * place
            for start, parts in ((place * box.long, values), (at, low), (at + REACH, high)):
                parts = in_order(even, *(part.astype(jnp.float32) for part in parts))
                size = parts[0].shape[0]
                first[start : start + size, :], second[start : start + size, :] = parts
            place += 1


def message_rows(box, count):
    return -(-(count * (box.long + 2 * REACH)) // 8) * 8


def pack_fields(box, wide, fields, tables, after, *refs):
    own, (low, high), refs = refs[:fields], refs[fields : fields + 2], refs[fields + 2 :]
    parts, (first, second, *table) = refs[:tables], refs[tables + after :]
    size = wide * box.across
    flat = [field.reshape(box.long * box.across, box.deep) for field in own]
    low = low.reshape(low.size // box.deep, box.deep)
    high = high.reshape(high.size // box.deep, box.deep)
    sides = [
        Sides("wide", *(ref.at[index * size : (index + 1) * size] for ref in (low, high)))
        for index in range(fields)
    ]
    pack_columns(box, flat, sides, wide, first, second)
    if tables:
        known = last_rows_merged(parts, table[0].shape[0])
        table[0][...] = known
        first[first.shape[0] - known.shape[0] :, :] = known
        second[second.shape[0] - known.shape[0] :, :] = known


def bring_edges(
    box, zone, scale, load, own_zone, own_scale, own_load, load_first, load_second, first, second,
    staged, sems
):
    even = is_even("wide")

    def edges(wide):
        up, down = box.long - wide, 0
        return [pl.ds(jnp.where(even, *pair), wide) for pair in ((up, down), (down, up))]

    copies = [
        (load.at[edges(MARGIN)[0]], load_first),
        (load.at[edges(MARGIN)[1]], load_second),
        (zone.at[edges(REACH)[0]], staged.at[0]),
        (zone.at[edges(REACH)[1]], staged.at[1]),
        (scale.at[edges(REACH)[0]], first.at[:REACH]),
        (scale.at[edges(REACH)[1]], second.at[:REACH]),
        (load, own_load),
        (scale, own_scale),
        (zone, own_zone),
    ]
    copies = [
        pltpu.make_async_copy(source, target, sems.at[index])
        for index, (source, target) in enumerate(copies)
    ]
    for copy in copies:
        copy.start()
    for copy in copies[:4]:
        copy.wait()
    first[REACH:] = staged[0].astype(jnp.float32)
    second[REACH:] = staged[1].astype(jnp.float32)
    for copy in copies[4:]:
        copy.wait()


def fill_window(box, window, own, wide_sides, narrow_sides, wide, place, total, add=None):
    flat = window.reshape(box.flat, box.deep)
    nothing = jnp.zeros((box.rows, EDGE, box.deep), jnp.float32)
    window[:, :EDGE, :] = nothing
    window[:, EDGE + box.across :, :] = nothing
    if add is None:
        add = lambda values, row_side, col_side: values
    inner = slice(EDGE, EDGE + box.across)
    first, last = REACH, REACH + box.long
    if wide < REACH:
        blank = jnp.zeros((1, box.across, box.deep), jnp.float32)
        window[0:1, inner, :] = blank
        window[box.rows - 1 :, inner, :] = blank
    window[first:last, inner, :] = add(own[...].astype(jnp.float32), 0, 0)
    window[first - wide : first, inner, :] = add(wide_sides.low(Ellipsis), -1, 0)
    window[last : last + wide, inner, :] = add(wide_sides.high(Ellipsis), 1, 0)
    corner = total * box.long
    for step in range(wide):
        for source, col, side in (
            (narrow_sides.low, EDGE - wide + step, -1),
            (narrow_sides.high, EDGE + box.across + step, 1),
        ):
            for start, size, row, row_side in (
                ((place + step) * box.long, box.long, first, 0),
                (corner + 2 * REACH * (place + step), wide, first - wide, -1),
                (corner + 2 * REACH * (place + step) + REACH, wide, last, 1),
            ):
                values = source(slice(start, start + size), slice(None))
                flat[row_of(box.cols, col, size, row), :] = add(values, row_side, side)


def some_cols(box, ref, row, step):
    stride = box.ey // 8
    return ref[row, pl.ds(EDGE - MARGIN + step, 8, stride=stride), :]


def negative_image(box, window, row, at, x, flow_before, weights):
    to_long, to_across, to_deep, mass = weights
    steps = range(box.ey // 8)
    x_next = [some_cols(box, window, row + 1, step) for step in range(-1, len(steps) + 1)]
    flow_long = [
        some_cols(box, to_long, at, step) * (x_next[step + 1] - x[step + 1]) for step in steps
    ]
    flow_across = [
        some_cols(box, to_across, at, step) * (x[step + 2] - x[step + 1])
        for step in range(-1, len(steps))
    ]
    totals = []
    for step in steps:
        here = x[step + 1]
        lanes = here.shape[1]
        flow_deep = some_cols(box, to_deep, at, step) * (pltpu.roll(here, lanes - 1, 1) - here)
        total = flow_long[step] - flow_before[step] - some_cols(box, mass, at, step) * here
        total = total + (flow_across[step + 1] - flow_across[step])
        totals.append(total + (flow_deep - pltpu.roll(flow_deep, 1, 1)))
    return totals, x_next, flow_long


def in_steps(box, refs, rows):
    return jnp.stack(
        [
            jnp.concatenate([some_cols(box, ref, row, step) for step in range(box.ey // 8)], axis=0)
            for ref, row in zip(refs, rows)
        ]
    )


def looked_up(labels, values):
    return jnp.where(labels == 0, values[0], jnp.where(labels == 1, values[1], values[2]))


def at_own_row(line, shape):
    long_pos, across_pos, _, across_count = position()
    rows = lax.broadcasted_iota(jnp.int32, shape, 0)
    own = rows == long_pos * across_count + across_pos
    return jnp.where(own, line[:1], jnp.zeros(shape, jnp.float32))


def merged(table, *others):
    for other in others:
        table = jnp.where(table != 0.0, table, other)
    return table


def last_rows_merged(refs, count):
    return merged(*(ref[ref.shape[0] - count :, :] for ref in refs))


def join_rows(table, message, out):
    out[...] = last_rows_merged((table, message), out.shape[0])


def line_of(numbers, shape):
    count = -(-len(numbers) // 8) * 8
    rows = lax.broadcasted_iota(jnp.int32, (count, shape[1]), 0)
    lanes = lax.broadcasted_iota(jnp.int32, (count, shape[1]), 1)
    stacked = jnp.zeros((count, shape[1]), jnp.float32)
    place = jnp.zeros((count, shape[1]), jnp.bool_)
    for row, (index, values) in enumerate(numbers):
        stacked = jnp.where(rows == row, values, stacked)
        place = place | ((rows == row) & (lanes == index))
    sums = jnp.sum(stacked, axis=1, keepdims=True)
    line = jnp.sum(jnp.where(place, sums, jnp.zeros_like(stacked)), axis=0, keepdims=True)
    return jnp.broadcast_to(line, shape)


def box_sums(box, zone, scale, load, after, diffusivity, decay, out, table):
    del after
    nothing = jnp.zeros((box.across, box.deep), jnp.float32)
    half = [[0.5 * diffusivity[z, d] for z in range(3)] for d in range(3)]
    rates = [decay[z] for z in range(3)]

    def halves(row):
        labels, factor = zone[row], scale[row]
        return [looked_up(labels, half[d]) * factor for d in range(3)] + [looked_up(labels, rates)]

    sums = [nothing] * 5
    for row in range(box.long):
        sums = [total + more for total, more in zip(sums, halves(row) + [load[row]])]

    def total(values):
        return jnp.sum(values, axis=0, keepdims=True)

    cells = box.long * box.across * box.deep
    numbers = [(index, total(sums[index]) * (2.0 / cells)) for index in range(3)]
    mass = total(sums[3])
    numbers += [(3, mass / cells)]
    lane = lax.broadcasted_iota(jnp.int32, (1, box.deep), 1)
    ends = jnp.where((lane == 0) | (lane == box.deep - 1), total(sums[2]), 0.0)
    numbers += [
        (BOX_DIAGONAL, mass + ends),
        (LONG_HIGH, total(halves(box.long - 1)[0])),
        (LONG_LOW, total(halves(0)[0])),
        (ACROSS_HIGH, sums[1][box.across - 1 :]),
        (ACROSS_LOW, sums[1][:1]),
        (LOAD_SUM, total(sums[4])),
    ]
    line = line_of(numbers, out.shape)
    out[...] = line
    table[...] = at_own_row(line, table.shape)


def means_of(ref):
    return [ref[0:1, index : index + 1] for index in range(4)]


def first_solve(box, load, low, high, left, right, means, zone, scale, diffusivity, decay, *rest):
    tables = rest[:N_TABLES]
    window, local, image, inverses, spectral, middle = rest[N_TABLES:]
    spread_x, spread_y, eig_z = tables[6:]
    means = means_of(means)
    base = means[3] + means[0] * spread_x[...] + means[2] * eig_z[...]

    def divided(values, col):
        divisor = base + means[1] * spread_y[col : col + 1, :]
        inverse = pl.reciprocal(divisor, approx=True)
        for _ in range(2):
            inverse = inverse * (2.0 - divisor * inverse)
        inverses[col] = inverse
        return values * inverse

    half = [0.5 * diffusivity[z, 2] for z in range(3)]
    rates = [decay[z] for z in range(3)]
    lane = lax.broadcasted_iota(jnp.int32, (box.across, box.deep), 1)
    ends = jnp.where((lane == 0) | (lane == box.deep - 1), jnp.float32(1.0), jnp.float32(0.0))
    image[...] = jnp.zeros((box.across, box.deep), jnp.float32)
    wide_sides, narrow_sides = Sides("wide", low, high), Sides("narrow", left, right)
    fill_window(box, window, load, wide_sides, narrow_sides, MARGIN, 0, MARGIN)

    def emit(start, values):
        values = values * (1.0 / cheb_center)
        values = values.reshape(8, box.across, box.deep)
        local[start : start + 8] = values
        total = image[...]
        for row in range(8):
            labels = zone[start + row]
            mass = looked_up(labels, rates) + looked_up(labels, half) * scale[start + row] * ends
            total = total + mass * values[row]
        image[...] = total

    box_solve(
        box,
        lambda start: in_steps(box, [window] * 8, range(1 + start, 9 + start)),
        divided,
        tables,
        None,
        None,
        spectral,
        middle,
        emit,
    )


def side_weights(
    box, zone, scale, low, high, left, right, diffusivity, to_long, to_across, zone_window,
    scale_window
):
    for index, (window, own) in enumerate(((scale_window, scale), (zone_window, zone))):
        start = index * REACH
        wide_sides = Sides("wide", *(ref.at[start : start + REACH] for ref in (low, high)))
        narrow_sides = Sides("narrow", left, right)
        fill_window(box, window, own, wide_sides, narrow_sides, REACH, start, 2 * REACH)
    half = [[0.5 * diffusivity[z, d] for z in range(3)] for d in range(2)]

    def one_row(row, before):
        labels, factor = zone_window[row], scale_window[row]
        now = [looked_up(labels, half[d]) * factor for d in range(2)]
        to_across[row] = now[1] + pltpu.roll(now[1], box.cols - 1, 0)
        to_long[jnp.maximum(row - 1, 0)] = before + now[0]
        return now[0]

    def some_rows(index, before):
        for row in range(8):
            before = one_row(index * 8 + row, before)
        return before

    before = jnp.zeros((box.cols, box.deep), jnp.float32)
    before = lax.fori_loop(0, box.rows // 8, some_rows, before)
    for row in range(box.rows // 8 * 8, box.rows):
        before = one_row(row, before)
    to_long[box.rows - 1] = before


def deep_weights(box, zone_window, scale_window, diffusivity, decay, to_deep, mass):
    half = [0.5 * diffusivity[z, 2] for z in range(3)]
    rates = [decay[z] for z in range(3)]
    lane = lax.broadcasted_iota(jnp.int32, (box.cols, box.deep), 1)
    ends = jnp.where((lane == 0) | (lane == box.deep - 1), jnp.float32(1.0), jnp.float32(0.0))
    not_last = jnp.where(lane == box.deep - 1, jnp.float32(0.0), jnp.float32(1.0))

    def one_row(row):
        labels = zone_window[row]
        now = looked_up(labels, half) * scale_window[row]
        to_deep[row] = (now + pltpu.roll(now, box.deep - 1, 1)) * not_last
        mass[row] = looked_up(labels, rates) + now * ends

    def some_rows(index, _):
        for row in range(8):
            one_row(index * 8 + row)
        return 0

    lax.fori_loop(0, box.rows // 8, some_rows, 0)
    for row in range(box.rows // 8 * 8, box.rows):
        one_row(row)


def image_sums(
    box, zone, scale, local, image, low, high, left, right, table, diffusivity, out, up, down
):
    half = [[0.5 * diffusivity[z, d] for z in range(3)] for d in range(3)]
    shape = (box.long * box.across, box.deep)
    zone_flat, scale_flat, local_flat = zone.reshape(shape), scale.reshape(shape), local.reshape(shape)
    last_col = row_of(box.across, box.across - 1, box.long)
    first_col = row_of(box.across, 0, box.long)

    wide_sides, narrow_sides = Sides("wide", low, high), Sides("narrow", left, right)

    def side(source, place):
        return source(slice(place * box.long, (place + 1) * box.long), slice(None))

    above, below = wide_sides.high, wide_sides.low
    faces = [
        (0, zone[box.long - 1], scale[box.long - 1], local[box.long - 1], above(REACH), above(0)),
        (0, zone[0], scale[0], local[0], below(2 * REACH - 1), below(REACH - 1)),
        (
            1,
            zone_flat[last_col, :],
            scale_flat[last_col, :],
            local_flat[last_col, :],
            side(narrow_sides.high, REACH),
            side(narrow_sides.high, 0),
        ),
        (
            1,
            zone_flat[first_col, :],
            scale_flat[first_col, :],
            local_flat[first_col, :],
            side(narrow_sides.low, 2 * REACH - 1),
            side(narrow_sides.low, REACH - 1),
        ),
    ]
    flows = []
    for direction, labels, factor, values, far_labels, far_factor in faces:
        weight = looked_up(labels, half[direction]) * factor
        weight = weight + looked_up(far_labels, half[direction]) * far_factor
        flows.append(jnp.sum(weight * values, axis=0, keepdims=True))
    long_pos, across_pos, long_count, across_count = position()
    numbers = [
        (IMAGE_SUM, jnp.sum(image[...], axis=0, keepdims=True) + sum(flows)),
        (FLOW_LONG_HIGH, flows[0] * as_float(long_pos < long_count - 1)),
        (FLOW_LONG_LOW, flows[1] * as_float(long_pos > 0)),
        (FLOW_ACROSS_HIGH, flows[2] * as_float(across_pos < across_count - 1)),
        (FLOW_ACROSS_LOW, flows[3] * as_float(across_pos > 0)),
    ]
    known = table[...] + at_own_row(line_of(numbers, (8, out.shape[1])), out.shape)
    out[...] = known
    edge = REACH * box.across
    even = is_even("wide")
    for target, pair in ((up, (box.long - REACH, 0)), (down, (0, box.long - REACH))):
        target[:edge] = local[pl.ds(jnp.where(even, *pair), REACH)].reshape(edge, box.deep)
        target[edge:] = known


def column(values, index):
    return values[:, index : index + 1]


def uncoupled_groups(count, across):
    places = np.arange(count)
    long_step = np.abs(places[:, None] // across - places[None, :] // across)
    across_step = np.abs(places[:, None] % across - places[None, :] % across)
    coupled = long_step + across_step == 1
    left = list(range(count))
    groups = []
    while left:
        group = []
        for place in sorted(left, key=lambda p: (coupled[p][left].sum(), p)):
            if not coupled[place][group].any():
                group.append(place)
        left = [place for place in left if place not in group]
        for place in group:
            beside = [other for other in left if coupled[place][other]]
            for other in beside:
                coupled[other][beside] = True
                coupled[other][other] = False
        groups.append(group)
    return groups


def coarse_inverse(numbers, work):
    count, width = work.shape
    across = lax.axis_size("narrow")
    beyond = pltpu.roll(numbers, count - across, 0)
    beside = pltpu.roll(numbers, count - 1, 0)
    before = pltpu.roll(numbers, across, 0)
    ahead = pltpu.roll(numbers, 1, 0)
    place = lax.broadcasted_iota(jnp.int32, (count, 1), 0)
    across_pos = lax.rem(place, across)
    nothing = jnp.zeros((count, 1), jnp.float32)
    couplings = []
    diagonal = column(numbers, BOX_DIAGONAL)
    for own, other, there, inside in (
        (LONG_HIGH, LONG_LOW, beyond, place < count - across),
        (LONG_LOW, LONG_HIGH, before, place >= across),
        (ACROSS_HIGH, ACROSS_LOW, beside, across_pos < across - 1),
        (ACROSS_LOW, ACROSS_HIGH, ahead, across_pos > 0),
    ):
        shared = jnp.where(inside, column(there, other), nothing)
        diagonal = diagonal + column(numbers, own) + shared
        couplings.append(jnp.where(inside, column(numbers, own) + shared, nothing))
    rows = lax.broadcasted_iota(jnp.int32, (count, width), 0)
    cols = lax.broadcasted_iota(jnp.int32, (count, width), 1)
    blank = jnp.zeros((count, width), jnp.float32)
    matrix = jnp.where(cols == rows, diagonal, blank)
    for shift, coupling in zip((across, -across, 1, -1), couplings):
        matrix = matrix - jnp.where((cols == rows + shift) & (cols < count), coupling, blank)
    matrix = jnp.where(cols == rows + count, jnp.ones((count, 1), jnp.float32), matrix)
    if count <= 16:
        for group in uncoupled_groups(count, across):
            rest = matrix
            for step in group:
                pivot_row = matrix[step : step + 1, :] / matrix[step : step + 1, step : step + 1]
                rest = rest - matrix[:, step : step + 1] * pivot_row
                rest = jnp.where(rows == step, pivot_row, rest)
            matrix = rest
        return pltpu.roll(matrix, width - count, 1)
    work[...] = matrix

    def eliminate(step, _):
        values = work[...]
        pivot_row = work[pl.ds(step, 1), :]
        at_step = cols == step
        factors = jnp.sum(jnp.where(at_step, values, blank), axis=1, keepdims=True)
        pivot = jnp.sum(jnp.where(at_step[:1], pivot_row, blank[:1]), axis=1, keepdims=True)
        pivot_row = pivot_row / pivot
        work[...] = jnp.where(rows == step, pivot_row, values - factors * pivot_row)
        return 0

    lax.fori_loop(0, count, eliminate, 0)
    values = work[...]
    if count % 128:
        return pltpu.roll(values, width - count, 1)
    return values[:, count : 2 * count]


def answer(inverse, sums):
    return jnp.sum(inverse * sums, axis=0, keepdims=True)


def at_box(values, row_side, col_side):
    long_pos, across_pos, long_count, across_count = position()
    there_long, there_across = long_pos + row_side, across_pos + col_side
    inside = (
        (there_long >= 0)
        & (there_long < long_count)
        & (there_across >= 0)
        & (there_across < across_count)
    )
    lanes = lax.broadcasted_iota(jnp.int32, values.shape, 1)
    wanted = (lanes == there_long * across_count + there_across) & inside
    return jnp.sum(jnp.where(wanted, values, jnp.zeros_like(values)), axis=1, keepdims=True)


def coarse_corrections(parts, *refs):
    table_parts, (out, work) = refs[:parts], refs[parts:]
    count = work.shape[0]
    numbers = last_rows_merged(table_parts, count)
    across_count = lax.axis_size("narrow")
    inverse = coarse_inverse(numbers, work)
    sums = column(numbers, IMAGE_SUM)
    sums = sums - column(pltpu.roll(numbers, count - across_count, 0), FLOW_LONG_LOW)
    sums = sums - column(pltpu.roll(numbers, across_count, 0), FLOW_LONG_HIGH)
    sums = sums - column(pltpu.roll(numbers, count - 1, 0), FLOW_ACROSS_LOW)
    sums = sums - column(pltpu.roll(numbers, 1, 0), FLOW_ACROSS_HIGH)
    load_sums = column(numbers, LOAD_SUM)
    sums = load_sums * (1.0 - 1.0 / cheb_center) - sums
    out[0:1, :] = answer(inverse, load_sums) * (1.0 / cheb_center)
    out[1:2, :] = answer(inverse, sums) * gain


def second_solve(box, local, low, high, left, right, inverses, answers, *rest):
    to_long, to_across, to_deep, mass, load_window = rest[:5]
    tables = rest[5 : 5 + N_TABLES]
    iterate, top, bottom, last_col, first_col, out = rest[5 + N_TABLES : 11 + N_TABLES]
    window, spectral, middle, sems = rest[11 + N_TABLES :]
    long_pos, across_pos, long_count, across_count = position()
    coarse = answers[0:1, :]
    own_shift = at_box(answers[1:2, :], 0, 0)
    shifts = {
        (row_side, col_side): at_box(coarse, row_side, col_side)
        for row_side in (-1, 0, 1)
        for col_side in (-1, 0, 1)
    }

    def add(values, row_side, col_side):
        shift = shifts[row_side, col_side]
        if values.ndim == 3:
            shift = shift.reshape(1, 1, 1)
        return values + shift

    edge = REACH * box.across
    low, high = (
        ref.at[:edge].reshape(REACH, box.across, box.deep) for ref in (low, high)
    )
    wide_sides, narrow_sides = Sides("wide", low, high), Sides("narrow", left, right)
    fill_window(box, window, local, wide_sides, narrow_sides, REACH, 0, REACH, add)
    weights = (to_long, to_across, to_deep, mass)

    steps = range(box.ey // 8)
    x = [some_cols(box, window, 1, step) for step in range(-1, len(steps) + 1)]
    flow = [
        some_cols(box, to_long, 0, step) * (x[step + 1] - some_cols(box, window, 0, step))
        for step in steps
    ]
    state = [x, flow]

    def divided(values, col):
        return values * inverses[col]

    def residual(start_row):
        rows = []
        for row in range(start_row + 1, start_row + 9):
            image, *state[:] = negative_image(box, window, row, row, *state, weights)
            image = [some_cols(box, load_window, row, step) + image[step] for step in steps]
            rows.append(jnp.concatenate(image, axis=0))
        return jnp.stack(rows)

    inner = slice(EDGE, EDGE + box.across)
    first = REACH
    row_ids = lax.broadcasted_iota(jnp.int32, (1, padded(box.ex)), 1)
    col_ids = lax.broadcasted_iota(jnp.int32, (1, padded(box.ey)), 1)
    col_ids = (col_ids & 7) * (box.ey // 8) + lax.shift_right_logical(col_ids, 3)
    row_mask = jnp.where(row_ids < MARGIN, as_float(long_pos > 0), 1.0)
    row_mask = jnp.where(row_ids >= MARGIN + box.long, as_float(long_pos < long_count - 1), row_mask)
    col_mask = jnp.where(col_ids < MARGIN, as_float(across_pos > 0), 1.0)
    col_mask = jnp.where(
        col_ids >= MARGIN + box.across, as_float(across_pos < across_count - 1), col_mask
    )
    keep = 1.0 + rho_second * rho_first
    copies = []

    def emit(start, values):
        rows = values.reshape(8, box.across, box.deep)
        before = window[first + start : first + start + 8, inner, :]
        shift = own_shift.reshape(1, 1, 1)
        iterate[start : start + 8] = keep * before + (gain * rows + shift)
        copies.append(
            pltpu.make_async_copy(
                iterate.at[start : start + 8], out.at[start : start + 8], sems.at[len(copies)]
            )
        )
        copies[-1].start()

    box_solve(
        box, residual, divided, tables, row_mask, col_mask, spectral, middle, emit
    )
    rows = in_order(is_even("wide"), iterate[box.long - 1], iterate[0])
    top[...], bottom[...] = rows
    flat = iterate.reshape(box.long * box.across, box.deep)
    cols = [flat[row_of(box.across, col, box.long), :] for col in (box.across - 1, 0)]
    last_col[...], first_col[...] = in_order(is_even("narrow"), *cols)
    for copy in copies:
        copy.wait()


def inner_residual(
    box, load, iterate, to_long, to_across, to_deep, mass, rows, cols, out, window, result, sems
):
    inner = slice(EDGE, EDGE + box.across)
    flat = window.reshape((box.long + 2) * box.cols, box.deep)
    iterate_flat = iterate.reshape(box.long * box.across, box.deep)
    blank = jnp.zeros((box.long + 2, EDGE, box.deep), jnp.float32)
    window[:, :EDGE, :] = blank
    window[:, EDGE + box.across :, :] = blank
    window[1 : 1 + box.long, inner, :] = iterate[...]
    window[0, inner, :] = iterate[0]
    window[1 + box.long, inner, :] = iterate[box.long - 1]
    for col, place in ((0, EDGE - 1), (box.across - 1, EDGE + box.across)):
        values = iterate_flat[row_of(box.across, col, box.long), :]
        flat[row_of(box.cols, place, box.long, 1), :] = values
    weights = (to_long, to_across, to_deep, mass)
    steps = range(box.ey // 8)
    x = [some_cols(box, window, 1, step) for step in range(-1, len(steps) + 1)]
    flow = [jnp.zeros((8, box.deep), jnp.float32) for _ in steps]
    middle = slice(8, box.across - 8)
    copies = []
    for row in range(box.long):
        image, x, flow = negative_image(box, window, row + 1, REACH + row, x, flow, weights)
        for step in steps:
            place = pl.ds(EDGE - MARGIN + step, 8, stride=box.ey // 8)
            result[row, place, :] = image[step]
        values = load[row] + result[row, inner]
        result[row, inner] = values
        cols[0, row] = values[:8]
        cols[1, row] = values[box.across - 8 :]
        if row == 0:
            rows[0] = values
        if row == box.long - 1:
            rows[1] = values
        if row % 8 == 7:
            part = slice(row - 7, row + 1)
            copy = pltpu.make_async_copy(
                result.at[part, EDGE + 8 : EDGE + box.across - 8],
                out.at[part, middle],
                sems.at[row // 8],
            )
            copy.start()
            copies.append(copy)
    for copy in copies:
        copy.wait()


def outer_residual(
    box, iterate, low, high, left, right, to_long, to_across, rows, cols, inner_out, out,
    row_part, col_part, sems
):
    del inner_out
    inner = slice(EDGE, EDGE + box.across)
    middle = slice(8, box.across - 8)
    wide_sides, narrow_sides = Sides("wide", low, high), Sides("narrow", left, right)
    last = box.long - 1
    iterate_flat = iterate.reshape(box.long * box.across, box.deep)
    across_flat = to_across.reshape(box.flat, box.deep)
    below = to_long[REACH - 1, inner] * (wide_sides.low(Ellipsis) - iterate[0])
    above = to_long[REACH + last, inner] * (wide_sides.high(Ellipsis) - iterate[last])
    row_part[0] = (rows[0] + below)[middle]
    row_part[1] = (rows[1] + above)[middle]
    copies = [
        pltpu.make_async_copy(row_part.at[0], out.at[0, middle], sems.at[0]),
        pltpu.make_async_copy(row_part.at[1], out.at[last, middle], sems.at[1]),
    ]
    for copy in copies:
        copy.start()
    col_part[...] = cols[...]
    flat = col_part.reshape(2 * box.long * 8, box.deep)
    for side, (from_side, col, face, tile) in enumerate(
        (
            (narrow_sides.low, 0, EDGE - 1, slice(0, 8)),
            (narrow_sides.high, box.across - 1, EDGE + box.across - 1, slice(box.across - 8, None)),
        )
    ):
        weight = across_flat[row_of(box.cols, face, box.long, REACH), :]
        own = iterate_flat[row_of(box.across, col, box.long), :]
        place = pl.ds(side * box.long * 8 + side * 7, box.long, stride=8)
        flat[place, :] = flat[place, :] + weight * (from_side(Ellipsis) - own)
        col_part[side, 0] = col_part[side, 0] + below[tile]
        col_part[side, last] = col_part[side, last] + above[tile]
        first_col = side * (box.across - 8)
        copy = pltpu.make_async_copy(
            col_part.at[side], out.at[:, first_col : first_col + 8], sems.at[2 + side]
        )
        copy.start()
        copies.append(copy)
    for copy in copies:
        copy.wait()


def swaps(axis, around):
    sizes = (lax.axis_size("wide"), lax.axis_size("narrow"))
    along = ("wide", "narrow").index(axis)
    size, beside = sizes[along], sizes[1 - along]

    def number(place, other_place):
        pair = (place, other_place) if along == 0 else (other_place, place)
        return pair[0] * sizes[1] + pair[1]

    ways = []
    for way in range(2):
        pairs = []
        for place in range(size):
            for other_place in range(beside):
                partner = place + 1 if place % 2 == way else place - 1
                there = other_place
                if around and size % 2 == 0:
                    partner %= size
                if not 0 <= partner < size:
                    partner = place
                    there = other_place ^ 1 if beside % 2 == 0 else other_place
                pairs.append((number(place, other_place), number(partner, there)))
        ways.append(pairs)
    return ways


def exchange(axis, first, second, around=False):
    ways = swaps(axis, around)
    axes = ("wide", "narrow")
    return lax.ppermute(first, axes, ways[0]), lax.ppermute(second, axes, ways[1])


def two_away(axis, table):
    size = lax.axis_size(axis)
    return lax.ppermute(table, axis, [(i, (i + 2) % size) for i in range(size)])


def tell(table):
    count = table.shape[0]
    long_pos, across_pos, _, across_count = position()
    own = lax.dynamic_slice_in_dim(table, long_pos * across_count + across_pos, 1, axis=0)
    line = jnp.broadcast_to(own, (count, 1, 128))
    told = lax.all_to_all(line, ("wide", "narrow"), split_axis=0, concat_axis=0, tiled=True)
    return told.reshape(count, 128)


def on_device(zone, scale, diffusivity, decay, load):
    box = Box(load.shape)
    long, across, deep = load.shape
    count = lax.axis_size("wide") * lax.axis_size("narrow")
    by_margins = lax.axis_size("wide") == 4 and lax.axis_size("narrow") == 4
    tables = tables_of(box)
    cells = f32(long, across, deep)
    whole_zone = jax.ShapeDtypeStruct(cells.shape, zone.dtype)
    window = f32(box.rows, box.cols, deep)
    table_shape = f32(count, 128)
    anywhere = pl.BlockSpec(memory_space=pl.ANY)
    in_hbm = pl.BlockSpec(memory_space=pltpu.HBM)

    def scratch(shape):
        return pltpu.VMEM(shape, jnp.float32)

    def pinned(field):
        return pltpu.with_memory_space_constraint(field, pltpu.HBM)

    spectral = scratch((box.ey, padded(box.ex), deep))
    middle = scratch((long, padded(box.ey), deep))

    def pack(wide, fields, sides, parts=(), after=()):
        rows = message_rows(box, wide * len(fields)) + (count if parts else 0)
        message = f32(rows, deep)
        body = functools.partial(pack_fields, box, wide, len(fields), len(parts), len(after))
        return call(
            body,
            (message, message) + ((table_shape,) if parts else ()),
            [VMEM] * (len(fields) + 2 + len(parts)) + [anywhere] * len(after),
        )(*fields, *sides, *parts, *after)

    far = f32(2 * REACH, across, deep)
    zone, scale, load, load_first, load_second, first, second = call(
        functools.partial(bring_edges, box),
        (whole_zone, cells, cells) + (f32(MARGIN, across, deep),) * 2 + (far, far),
        [in_hbm] * 3,
        [pltpu.VMEM((2, REACH, across, deep), zone.dtype), pltpu.SemaphoreType.DMA((9,))],
    )(pinned(zone), pinned(scale), pinned(load))
    load_wide = exchange("wide", load_first, load_second)
    far_wide = exchange("wide", first, second)
    load_first, load_second = pack(MARGIN, [load], load_wide)
    load_narrow = exchange("narrow", load_first, load_second)
    sums, table = call(
        functools.partial(box_sums, box),
        (f32(8, 128), table_shape),
        [VMEM] * 3 + [anywhere] + [SMEM] * 2,
    )(zone, scale, load, load_first, diffusivity, decay)
    far_narrow = exchange("narrow", *pack(REACH, [scale, zone], far_wide))
    load_window, local, image, inverses = call(
        functools.partial(first_solve, box),
        (window, cells, f32(across, deep), f32(box.ey, box.ex, deep)),
        [VMEM] * 8 + [SMEM] * 2 + [VMEM] * N_TABLES,
        [spectral, middle],
        flops=4 * 10**9,
    )(load, *load_wide, *load_narrow, sums, zone, scale, diffusivity, decay, *tables)
    message = f32(REACH * across + count, deep)
    table, first, second = call(
        functools.partial(image_sums, box), (table_shape, message, message), [VMEM] * 9 + [SMEM]
    )(zone, scale, local, image, *far_wide, *far_narrow, table, diffusivity)
    own_table = table
    wide = exchange("wide", first, second, by_margins)
    parts = (table, *wide)
    if by_margins:
        parts += (two_away("wide", table),)
    to_long, to_across, *windows = call(
        functools.partial(side_weights, box),
        (window,) * 4,
        [VMEM] * 6 + [SMEM],
        flops=10**9,
    )(zone, scale, *far_wide, *far_narrow, diffusivity)
    to_deep, mass = call(
        functools.partial(deep_weights, box),
        (window,) * 2,
        [VMEM] * 2 + [SMEM] * 2,
        flops=10**9,
    )(*windows, diffusivity, decay)
    weights = (to_long, to_across, to_deep, mass)
    first, second, table = pack(REACH, [local], wide, parts, [to_long])
    narrow = exchange("narrow", first, second)
    if by_margins:
        table = call(join_rows, table_shape, [VMEM] * 2)(table, narrow[0])
        parts = (table, two_away("narrow", table))
    else:
        parts = (tell(own_table),)
    row, col = f32(across, deep), f32(long, deep)
    answers = call(
        functools.partial(coarse_corrections, len(parts)),
        f32(8, -(-count // 128) * 128),
        [VMEM] * len(parts),
        [scratch((count, -(-2 * count // 128) * 128))],
    )(*parts)
    iterate, first_row, second_row, first_col, second_col, result = call(
        functools.partial(second_solve, box),
        (cells, row, row, col, col, cells),
        [VMEM] * (12 + N_TABLES),
        [scratch(window.shape), spectral, middle, pltpu.SemaphoreType.DMA((long // 8,))],
        flops=4 * 10**9,
        out_spec=(VMEM,) * 5 + (anywhere,),
    )(local, *wide, *narrow, inverses, answers, *weights, load_window, *tables)
    narrow = exchange("narrow", first_col, second_col)
    wide = exchange("wide", first_row, second_row)
    rows, cols, inner = call(
        functools.partial(inner_residual, box),
        (f32(2, across, deep), f32(2, long, 8, deep), cells),
        [VMEM] * 6,
        [
            scratch((long + 2, box.cols, deep)),
            scratch((long, box.cols, deep)),
            pltpu.SemaphoreType.DMA((long // 8,)),
        ],
        flops=10**9,
        out_spec=(VMEM, VMEM, anywhere),
    )(load, iterate, *weights)
    residual = call(
        functools.partial(outer_residual, box),
        cells,
        [VMEM] * 9 + [anywhere],
        [
            scratch((2, across - 16, deep)),
            scratch((2, long, 8, deep)),
            pltpu.SemaphoreType.DMA((4,)),
        ],
        out_spec=anywhere,
        aliases={9: 0},
    )(iterate, *wide, *narrow, to_long, to_across, rows, cols, inner)
    return result, residual


def solution(mesh):
    split = P(("groups", "wide"), "narrow", None)
    return jax.shard_map(
        on_device,
        mesh=mesh,
        in_specs=(split, split, P(), P(), split),
        out_specs=(split, split),
        check_vma=False,
    )
```

```python
import functools

import jax
import jax.numpy as jnp
import ml_dtypes
import numpy as np
from jax import lax
from jax.experimental import pallas as pl
from jax.experimental.pallas import tpu as pltpu
from jax.sharding import PartitionSpec as P

MARGIN = 4
REACH = MARGIN + 1
EDGE = 8

cheb_center = 1.3
cheb_radius = 1.2
cheb_ratio = 1.3 / 1.2
rho_first = 1.0 / cheb_ratio
rho_second = 1.0 / (2.0 * cheb_ratio - rho_first)
gain = 2.0 * rho_second / cheb_radius

MEANS = range(4)
BOX_DIAGONAL, LONG_HIGH, LONG_LOW, ACROSS_HIGH, ACROSS_LOW, LOAD_SUM = range(4, 10)
IMAGE_SUM, FLOW_LONG_HIGH, FLOW_LONG_LOW, FLOW_ACROSS_HIGH, FLOW_ACROSS_LOW = range(16, 21)

VMEM = pl.BlockSpec(memory_space=pltpu.VMEM)


def sine_basis(length):
    indices = np.arange(1, length + 1)
    phases = indices[:, None] * indices[None, :] % (2 * (length + 1))
    table = np.sqrt(2.0 / (length + 1)) * np.sin(np.pi * phases / (length + 1))
    eigvals = 4.0 * np.sin(np.pi * indices / (2.0 * (length + 1))) ** 2
    return table.astype(np.float32), eigvals.astype(np.float32)


def call(body, out_shape, in_specs, scratch=(), flops=0, out_spec=None, aliases=None):
    return pl.pallas_call(
        body,
        out_shape=out_shape,
        in_specs=in_specs,
        out_specs=out_spec or jax.tree.map(lambda _: VMEM, out_shape),
        scratch_shapes=list(scratch),
        compiler_params=pltpu.CompilerParams(vmem_limit_bytes=30 * 2**20),
        cost_estimate=pl.CostEstimate(flops=flops, bytes_accessed=0, transcendentals=0),
        input_output_aliases=aliases or {},
    )


def f32(*shape):
    return jax.ShapeDtypeStruct(shape, jnp.float32)


class Box:
    def __init__(self, shape):
        self.long, self.across, self.deep = shape
        self.ex = self.long + 2 * MARGIN
        self.ey = self.across + 2 * MARGIN
        self.rows = self.long + 2 * REACH
        self.cols = self.across + 2 * EDGE
        self.flat = self.rows * self.cols


def pieces(values, count):
    parts = []
    for _ in range(count - 1):
        scaled = values * 65537.0
        part = scaled - (scaled - values)
        parts.append(part)
        values = values - part
    return parts + [values]


def left_table(table, depth, count):
    rows, cols = table.shape
    wide = np.zeros((rows, depth), np.float32)
    wide[:, :cols] = table
    parts = []
    rest = wide
    for _ in range(count):
        part = rest.astype(ml_dtypes.bfloat16).astype(np.float32)
        parts.append(part)
        rest = rest - part
    blank = np.zeros_like(parts[0])
    lines = []
    for index in range(count):
        used = count - index if count > 2 else count
        lines.append(np.concatenate([parts[index]] * used + [blank] * (count - used), axis=1))
    return np.concatenate(lines, axis=0)


def right_tables(table):
    rest, parts = table, []
    for _ in range(3):
        part = rest.astype(ml_dtypes.bfloat16).astype(np.float32)
        parts.append(part)
        rest = rest - part
    both = np.concatenate([parts[0], parts[1]], axis=1)
    return np.concatenate([both, both], axis=0), np.concatenate([parts[2], parts[0]], axis=0)


def padded(size):
    return -(-size // 8) * 8


FORWARD, BACKWARD = 2, 3


def tables_of(box):
    sine_x, eig_x = sine_basis(box.ex)
    sine_y, eig_y = sine_basis(box.ey)
    sine_z, eig_z = sine_basis(box.deep)
    in_order_of_steps = np.arange(box.ey).reshape(8, box.ey // 8).T.reshape(-1)
    from_y = sine_y[MARGIN : MARGIN + box.across]
    from_x = sine_x[MARGIN : MARGIN + box.long]
    spread_x = np.broadcast_to(eig_x[:, None], (box.ex, box.deep))
    spread_y = np.broadcast_to(eig_y[:, None], (box.ey, box.deep))
    main_z, rest_z = right_tables(sine_z)
    return [
        jnp.asarray(np.ascontiguousarray(t))
        for t in (
            left_table(sine_y[:, in_order_of_steps], padded(box.ey), FORWARD),
            left_table(sine_x, padded(box.ex), FORWARD),
            left_table(from_x, padded(box.ex), BACKWARD),
            left_table(from_y, padded(box.ey), BACKWARD),
            main_z,
            rest_z,
            spread_x,
            spread_y,
            eig_z[None, :],
        )
    ]


N_TABLES = 9


def one_pass(left, right):
    return lax.dot_general(
        left,
        right,
        (((1,), (0,)), ((), ())),
        precision=lax.Precision.DEFAULT,
        preferred_element_type=jnp.float32,
    )


def dot_left(table, values, count, rows):
    total = one_pass(table, jnp.concatenate(pieces(values, count), axis=0))
    return sum(total[index * rows : (index + 1) * rows] for index in range(1, count)) + total[:rows]


def dot_right(values, main, rest, count):
    deep = values.shape[1]
    parts = pieces(values, count)
    total = one_pass(jnp.concatenate(parts[:2], axis=1), main)
    result = total[:, :deep] + total[:, deep:]
    if count == 3:
        result = result + one_pass(jnp.concatenate([parts[0], parts[2]], axis=1), rest)
    return result


def with_rows(values, rows):
    if values.shape[0] == rows:
        return values
    blank = jnp.zeros((rows - values.shape[0],) + values.shape[1:], values.dtype)
    return jnp.concatenate([values, blank], axis=0)


ABREAST = 8


def beside(values):
    return jnp.concatenate(values, axis=1)


def apart(values, lanes):
    return [values[:, start : start + lanes] for start in range(0, values.shape[1], lanes)]


def box_solve(box, source, divided, tables, row_mask, col_mask, spectral, middle, emit):
    into_y, into_x, from_x, from_y, main_z, rest_z = tables[:6]
    deep = box.deep
    deep_x, deep_y = padded(box.ex), padded(box.ey)
    into_y, into_x = into_y[...], into_x[...]
    if col_mask is not None:
        mask = jnp.concatenate([col_mask] * FORWARD, axis=1)
        into_y = into_y * mask
        mask = jnp.concatenate([row_mask] * FORWARD, axis=1)
        into_x = into_x * mask
    from_x, from_y, main_z, rest_z = from_x[...], from_y[...], main_z[...], rest_z[...]
    spectral_flat = spectral.reshape(box.ey * deep_x, deep)
    middle_flat = middle.reshape(box.long * deep_y, deep)
    if deep_x > box.ex:
        spectral[:, box.ex :, :] = jnp.zeros((box.ey, deep_x - box.ex, deep), jnp.float32)
    if deep_y > box.ey:
        middle[:, box.ey :, :] = jnp.zeros((box.long, deep_y - box.ey, deep), jnp.float32)
    for start in range(0, box.ex, 8):
        block = source(start).reshape(8 * box.ey, deep)
        block = dot_right(block, main_z, rest_z, FORWARD).reshape(8, box.ey, deep)
        for row in range(0, 8, ABREAST):
            wide = beside([block[row + part] for part in range(ABREAST)])
            wide = dot_left(into_y, with_rows(wide, deep_y), FORWARD, box.ey)
            for part, values in enumerate(apart(wide, deep)):
                place = pl.ds(start + row + part, box.ey, stride=deep_x)
                spectral_flat[place, :] = values
    for col in range(0, box.ey, ABREAST):
        wide = beside([spectral[col + part] for part in range(ABREAST)])
        wide = apart(dot_left(into_x, wide, FORWARD, box.ex), deep)
        wide = beside([divided(values, col + part) for part, values in enumerate(wide)])
        wide = dot_left(from_x, with_rows(wide, deep_x), BACKWARD, box.long)
        for part, values in enumerate(apart(wide, deep)):
            middle_flat[pl.ds(col + part, box.long, stride=deep_y), :] = values
    for start in range(0, box.long, 8):
        parts = []
        for row in range(start, start + 8, ABREAST):
            wide = beside([middle[row + part] for part in range(ABREAST)])
            parts += apart(dot_left(from_y, wide, BACKWARD, box.across), deep)
        emit(start, dot_right(jnp.concatenate(parts, axis=0), main_z, rest_z, BACKWARD))


def position():
    long_pos, across_pos = lax.axis_index("wide"), lax.axis_index("narrow")
    return long_pos, across_pos, lax.axis_size("wide"), lax.axis_size("narrow")


def as_float(flag):
    return jnp.where(flag, jnp.float32(1.0), jnp.float32(0.0))


def is_even(axis):
    return lax.rem(lax.axis_index(axis), 2) == 0


class Sides:
    def __init__(self, axis, first, second):
        position = lax.axis_index(axis)
        self.even = is_even(axis)
        self.has_low = as_float(position > 0)
        self.has_high = as_float(position < lax.axis_size(axis) - 1)
        self.first, self.second = first, second

    def low(self, *index):
        return jnp.where(self.even, self.second[index], self.first[index]) * self.has_low

    def high(self, *index):
        return jnp.where(self.even, self.first[index], self.second[index]) * self.has_high


def in_order(even, up, down):
    return jnp.where(even, up, down), jnp.where(even, down, up)


def row_of(stride, col, count, first=0):
    return pl.ds(first * stride + col, count, stride=stride)


def pack_columns(box, fields, wide_sides, wide, first, second):
    corner = len(fields) * wide * box.long
    even = is_even("narrow")
    place = 0
    for field, sides in zip(fields, wide_sides):
        for step in range(wide):
            cols = (box.across - wide + step, step)
            values = [field[row_of(box.across, col, box.long), :] for col in cols]
            low = [sides.low(row_of(box.across, col, wide), slice(None)) for col in cols]
            high = [sides.high(row_of(box.across, col, wide), slice(None)) for col in cols]
            at = corner + 2 * REACH * place
            for start, parts in ((place * box.long, values), (at, low), (at + REACH, high)):
                parts = in_order(even, *(part.astype(jnp.float32) for part in parts))
                size = parts[0].shape[0]
                first[start : start + size, :], second[start : start + size, :] = parts
            place += 1


def message_rows(box, count):
    return -(-(count * (box.long + 2 * REACH)) // 8) * 8


def pack_fields(box, wide, fields, tables, after, *refs):
    own, (low, high), refs = refs[:fields], refs[fields : fields + 2], refs[fields + 2 :]
    parts, (first, second, *table) = refs[:tables], refs[tables + after :]
    size = wide * box.across
    flat = [field.reshape(box.long * box.across, box.deep) for field in own]
    low = low.reshape(low.size // box.deep, box.deep)
    high = high.reshape(high.size // box.deep, box.deep)
    sides = [
        Sides("wide", *(ref.at[index * size : (index + 1) * size] for ref in (low, high)))
        for index in range(fields)
    ]
    pack_columns(box, flat, sides, wide, first, second)
    if tables:
        known = last_rows_merged(parts, table[0].shape[0])
        table[0][...] = known
        first[first.shape[0] - known.shape[0] :, :] = known
        second[second.shape[0] - known.shape[0] :, :] = known


def bring_edges(box, zone, scale, load, load_first, load_second, first, second, staged, sems):
    even = is_even("wide")

    def edges(wide):
        up, down = box.long - wide, 0
        return [pl.ds(jnp.where(even, *pair), wide) for pair in ((up, down), (down, up))]

    copies = [
        (zone.at[edges(REACH)[0]], staged.at[0]),
        (zone.at[edges(REACH)[1]], staged.at[1]),
        (load.at[edges(MARGIN)[0]], load_first),
        (load.at[edges(MARGIN)[1]], load_second),
        (scale.at[edges(REACH)[0]], first.at[:REACH]),
        (scale.at[edges(REACH)[1]], second.at[:REACH]),
    ]
    copies = [
        pltpu.make_async_copy(source, target, sems.at[index])
        for index, (source, target) in enumerate(copies)
    ]
    for copy in copies:
        copy.start()
    for copy in copies[:2]:
        copy.wait()
    first[REACH:] = staged[0].astype(jnp.float32)
    second[REACH:] = staged[1].astype(jnp.float32)
    for copy in copies[2:]:
        copy.wait()


def bring_box(load, scale, zone, after, own_load, own_scale, own_zone, sems):
    del after
    pairs = ((load, own_load), (scale, own_scale), (zone, own_zone))
    copies = [
        pltpu.make_async_copy(source, target, sems.at[index])
        for index, (source, target) in enumerate(pairs)
    ]
    for copy in copies:
        copy.start()
    for copy in copies:
        copy.wait()


def fill_window(box, window, own, wide_sides, narrow_sides, wide, place, total, add=None):
    flat = window.reshape(box.flat, box.deep)
    nothing = jnp.zeros((box.rows, EDGE, box.deep), jnp.float32)
    window[:, :EDGE, :] = nothing
    window[:, EDGE + box.across :, :] = nothing
    if add is None:
        add = lambda values, row_side, col_side: values
    inner = slice(EDGE, EDGE + box.across)
    first, last = REACH, REACH + box.long
    if wide < REACH:
        blank = jnp.zeros((1, box.across, box.deep), jnp.float32)
        window[0:1, inner, :] = blank
        window[box.rows - 1 :, inner, :] = blank
    window[first:last, inner, :] = add(own[...].astype(jnp.float32), 0, 0)
    window[first - wide : first, inner, :] = add(wide_sides.low(Ellipsis), -1, 0)
    window[last : last + wide, inner, :] = add(wide_sides.high(Ellipsis), 1, 0)
    corner = total * box.long
    for step in range(wide):
        for source, col, side in (
            (narrow_sides.low, EDGE - wide + step, -1),
            (narrow_sides.high, EDGE + box.across + step, 1),
        ):
            for start, size, row, row_side in (
                ((place + step) * box.long, box.long, first, 0),
                (corner + 2 * REACH * (place + step), wide, first - wide, -1),
                (corner + 2 * REACH * (place + step) + REACH, wide, last, 1),
            ):
                values = source(slice(start, start + size), slice(None))
                flat[row_of(box.cols, col, size, row), :] = add(values, row_side, side)


def some_cols(box, ref, row, step):
    stride = box.ey // 8
    return ref[row, pl.ds(EDGE - MARGIN + step, 8, stride=stride), :]


def negative_image(box, window, row, at, x, flow_before, weights):
    to_long, to_across, to_deep, mass = weights
    steps = range(box.ey // 8)
    x_next = [some_cols(box, window, row + 1, step) for step in range(-1, len(steps) + 1)]
    flow_long = [
        some_cols(box, to_long, at, step) * (x_next[step + 1] - x[step + 1]) for step in steps
    ]
    flow_across = [
        some_cols(box, to_across, at, step) * (x[step + 2] - x[step + 1])
        for step in range(-1, len(steps))
    ]
    totals = []
    for step in steps:
        here = x[step + 1]
        lanes = here.shape[1]
        flow_deep = some_cols(box, to_deep, at, step) * (pltpu.roll(here, lanes - 1, 1) - here)
        total = flow_long[step] - flow_before[step] - some_cols(box, mass, at, step) * here
        total = total + (flow_across[step + 1] - flow_across[step])
        totals.append(total + (flow_deep - pltpu.roll(flow_deep, 1, 1)))
    return totals, x_next, flow_long


def in_steps(box, refs, rows):
    return jnp.stack(
        [
            jnp.concatenate([some_cols(box, ref, row, step) for step in range(box.ey // 8)], axis=0)
            for ref, row in zip(refs, rows)
        ]
    )


def looked_up(labels, values):
    return jnp.where(labels == 0, values[0], jnp.where(labels == 1, values[1], values[2]))


def at_own_row(line, shape):
    long_pos, across_pos, _, across_count = position()
    rows = lax.broadcasted_iota(jnp.int32, shape, 0)
    own = rows == long_pos * across_count + across_pos
    return jnp.where(own, line[:1], jnp.zeros(shape, jnp.float32))


def merged(table, *others):
    for other in others:
        table = jnp.where(table != 0.0, table, other)
    return table


def last_rows_merged(refs, count):
    return merged(*(ref[ref.shape[0] - count :, :] for ref in refs))


def join_rows(table, message, out):
    out[...] = last_rows_merged((table, message), out.shape[0])


def line_of(numbers, shape):
    count = -(-len(numbers) // 8) * 8
    rows = lax.broadcasted_iota(jnp.int32, (count, shape[1]), 0)
    lanes = lax.broadcasted_iota(jnp.int32, (count, shape[1]), 1)
    stacked = jnp.zeros((count, shape[1]), jnp.float32)
    place = jnp.zeros((count, shape[1]), jnp.bool_)
    for row, (index, values) in enumerate(numbers):
        stacked = jnp.where(rows == row, values, stacked)
        place = place | ((rows == row) & (lanes == index))
    sums = jnp.sum(stacked, axis=1, keepdims=True)
    line = jnp.sum(jnp.where(place, sums, jnp.zeros_like(stacked)), axis=0, keepdims=True)
    return jnp.broadcast_to(line, shape)


def box_sums(box, zone, scale, load, after, diffusivity, decay, out, table):
    del after
    nothing = jnp.zeros((box.across, box.deep), jnp.float32)
    half = [[0.5 * diffusivity[z : z + 1, d : d + 1] for z in range(3)] for d in range(3)]
    rates = [decay[0:1, z : z + 1] for z in range(3)]

    def halves(row):
        labels, factor = zone[row], scale[row]
        return [looked_up(labels, half[d]) * factor for d in range(3)] + [looked_up(labels, rates)]

    sums = [nothing] * 5
    for row in range(box.long):
        sums = [total + more for total, more in zip(sums, halves(row) + [load[row]])]

    def total(values):
        return jnp.sum(values, axis=0, keepdims=True)

    cells = box.long * box.across * box.deep
    numbers = [(index, total(sums[index]) * (2.0 / cells)) for index in range(3)]
    mass = total(sums[3])
    numbers += [(3, mass / cells)]
    lane = lax.broadcasted_iota(jnp.int32, (1, box.deep), 1)
    ends = jnp.where((lane == 0) | (lane == box.deep - 1), total(sums[2]), 0.0)
    numbers += [
        (BOX_DIAGONAL, mass + ends),
        (LONG_HIGH, total(halves(box.long - 1)[0])),
        (LONG_LOW, total(halves(0)[0])),
        (ACROSS_HIGH, sums[1][box.across - 1 :]),
        (ACROSS_LOW, sums[1][:1]),
        (LOAD_SUM, total(sums[4])),
    ]
    line = line_of(numbers, out.shape)
    out[...] = line
    table[...] = at_own_row(line, table.shape)


def means_of(ref):
    return [ref[0:1, index : index + 1] for index in range(4)]


def first_solve(box, load, low, high, left, right, means, zone, scale, diffusivity, decay, *rest):
    tables = rest[:N_TABLES]
    window, local, image, inverses, spectral, middle = rest[N_TABLES:]
    spread_x, spread_y, eig_z = tables[6:]
    means = means_of(means)
    base = means[3] + means[0] * spread_x[...] + means[2] * eig_z[...]

    def divided(values, col):
        divisor = base + means[1] * spread_y[col : col + 1, :]
        inverse = pl.reciprocal(divisor, approx=True)
        for _ in range(2):
            inverse = inverse * (2.0 - divisor * inverse)
        inverses[col] = inverse
        return values * inverse

    half = [0.5 * diffusivity[z : z + 1, 2:3] for z in range(3)]
    rates = [decay[0:1, z : z + 1] for z in range(3)]
    lane = lax.broadcasted_iota(jnp.int32, (box.across, box.deep), 1)
    ends = jnp.where((lane == 0) | (lane == box.deep - 1), jnp.float32(1.0), jnp.float32(0.0))
    image[...] = jnp.zeros((box.across, box.deep), jnp.float32)
    wide_sides, narrow_sides = Sides("wide", low, high), Sides("narrow", left, right)
    fill_window(box, window, load, wide_sides, narrow_sides, MARGIN, 0, MARGIN)

    def emit(start, values):
        values = values * (1.0 / cheb_center)
        values = values.reshape(8, box.across, box.deep)
        local[start : start + 8] = values
        total = image[...]
        for row in range(8):
            labels = zone[start + row]
            mass = looked_up(labels, rates) + looked_up(labels, half) * scale[start + row] * ends
            total = total + mass * values[row]
        image[...] = total

    box_solve(
        box,
        lambda start: in_steps(box, [window] * 8, range(1 + start, 9 + start)),
        divided,
        tables,
        None,
        None,
        spectral,
        middle,
        emit,
    )


def side_weights(
    box, zone, scale, low, high, left, right, diffusivity, to_long, to_across, zone_window,
    scale_window
):
    for index, (window, own) in enumerate(((scale_window, scale), (zone_window, zone))):
        start = index * REACH
        wide_sides = Sides("wide", *(ref.at[start : start + REACH] for ref in (low, high)))
        narrow_sides = Sides("narrow", left, right)
        fill_window(box, window, own, wide_sides, narrow_sides, REACH, start, 2 * REACH)
    half = [[0.5 * diffusivity[z : z + 1, d : d + 1] for z in range(3)] for d in range(2)]

    def one_row(row, before):
        labels, factor = zone_window[row], scale_window[row]
        now = [looked_up(labels, half[d]) * factor for d in range(2)]
        to_across[row] = now[1] + pltpu.roll(now[1], box.cols - 1, 0)
        to_long[jnp.maximum(row - 1, 0)] = before + now[0]
        return now[0]

    def some_rows(index, before):
        for row in range(8):
            before = one_row(index * 8 + row, before)
        return before

    before = jnp.zeros((box.cols, box.deep), jnp.float32)
    before = lax.fori_loop(0, box.rows // 8, some_rows, before)
    for row in range(box.rows // 8 * 8, box.rows):
        before = one_row(row, before)
    to_long[box.rows - 1] = before


def deep_weights(box, zone_window, scale_window, diffusivity, decay, to_deep, mass):
    half = [0.5 * diffusivity[z : z + 1, 2:3] for z in range(3)]
    rates = [decay[0:1, z : z + 1] for z in range(3)]
    lane = lax.broadcasted_iota(jnp.int32, (box.cols, box.deep), 1)
    ends = jnp.where((lane == 0) | (lane == box.deep - 1), jnp.float32(1.0), jnp.float32(0.0))
    not_last = jnp.where(lane == box.deep - 1, jnp.float32(0.0), jnp.float32(1.0))

    def one_row(row):
        labels = zone_window[row]
        now = looked_up(labels, half) * scale_window[row]
        to_deep[row] = (now + pltpu.roll(now, box.deep - 1, 1)) * not_last
        mass[row] = looked_up(labels, rates) + now * ends

    def some_rows(index, _):
        for row in range(8):
            one_row(index * 8 + row)
        return 0

    lax.fori_loop(0, box.rows // 8, some_rows, 0)
    for row in range(box.rows // 8 * 8, box.rows):
        one_row(row)


def image_sums(
    box, zone, scale, local, image, low, high, left, right, table, diffusivity, out, up, down
):
    half = [[0.5 * diffusivity[z : z + 1, d : d + 1] for z in range(3)] for d in range(3)]
    shape = (box.long * box.across, box.deep)
    zone_flat, scale_flat, local_flat = zone.reshape(shape), scale.reshape(shape), local.reshape(shape)
    last_col = row_of(box.across, box.across - 1, box.long)
    first_col = row_of(box.across, 0, box.long)

    wide_sides, narrow_sides = Sides("wide", low, high), Sides("narrow", left, right)

    def side(source, place):
        return source(slice(place * box.long, (place + 1) * box.long), slice(None))

    above, below = wide_sides.high, wide_sides.low
    faces = [
        (0, zone[box.long - 1], scale[box.long - 1], local[box.long - 1], above(REACH), above(0)),
        (0, zone[0], scale[0], local[0], below(2 * REACH - 1), below(REACH - 1)),
        (
            1,
            zone_flat[last_col, :],
            scale_flat[last_col, :],
            local_flat[last_col, :],
            side(narrow_sides.high, REACH),
            side(narrow_sides.high, 0),
        ),
        (
            1,
            zone_flat[first_col, :],
            scale_flat[first_col, :],
            local_flat[first_col, :],
            side(narrow_sides.low, 2 * REACH - 1),
            side(narrow_sides.low, REACH - 1),
        ),
    ]
    flows = []
    for direction, labels, factor, values, far_labels, far_factor in faces:
        weight = looked_up(labels, half[direction]) * factor
        weight = weight + looked_up(far_labels, half[direction]) * far_factor
        flows.append(jnp.sum(weight * values, axis=0, keepdims=True))
    long_pos, across_pos, long_count, across_count = position()
    numbers = [
        (IMAGE_SUM, jnp.sum(image[...], axis=0, keepdims=True) + sum(flows)),
        (FLOW_LONG_HIGH, flows[0] * as_float(long_pos < long_count - 1)),
        (FLOW_LONG_LOW, flows[1] * as_float(long_pos > 0)),
        (FLOW_ACROSS_HIGH, flows[2] * as_float(across_pos < across_count - 1)),
        (FLOW_ACROSS_LOW, flows[3] * as_float(across_pos > 0)),
    ]
    known = table[...] + at_own_row(line_of(numbers, (8, out.shape[1])), out.shape)
    out[...] = known
    edge = REACH * box.across
    even = is_even("wide")
    for target, pair in ((up, (box.long - REACH, 0)), (down, (0, box.long - REACH))):
        target[:edge] = local[pl.ds(jnp.where(even, *pair), REACH)].reshape(edge, box.deep)
        target[edge:] = known


def column(values, index):
    return values[:, index : index + 1]


def uncoupled_groups(count, across):
    places = np.arange(count)
    long_step = np.abs(places[:, None] // across - places[None, :] // across)
    across_step = np.abs(places[:, None] % across - places[None, :] % across)
    coupled = long_step + across_step == 1
    left = list(range(count))
    groups = []
    while left:
        group = []
        for place in sorted(left, key=lambda p: (coupled[p][left].sum(), p)):
            if not coupled[place][group].any():
                group.append(place)
        left = [place for place in left if place not in group]
        for place in group:
            beside = [other for other in left if coupled[place][other]]
            for other in beside:
                coupled[other][beside] = True
                coupled[other][other] = False
        groups.append(group)
    return groups


def coarse_inverse(numbers, work):
    count, width = work.shape
    across = lax.axis_size("narrow")
    beyond = pltpu.roll(numbers, count - across, 0)
    beside = pltpu.roll(numbers, count - 1, 0)
    before = pltpu.roll(numbers, across, 0)
    ahead = pltpu.roll(numbers, 1, 0)
    place = lax.broadcasted_iota(jnp.int32, (count, 1), 0)
    across_pos = lax.rem(place, across)
    nothing = jnp.zeros((count, 1), jnp.float32)
    couplings = []
    diagonal = column(numbers, BOX_DIAGONAL)
    for own, other, there, inside in (
        (LONG_HIGH, LONG_LOW, beyond, place < count - across),
        (LONG_LOW, LONG_HIGH, before, place >= across),
        (ACROSS_HIGH, ACROSS_LOW, beside, across_pos < across - 1),
        (ACROSS_LOW, ACROSS_HIGH, ahead, across_pos > 0),
    ):
        shared = jnp.where(inside, column(there, other), nothing)
        diagonal = diagonal + column(numbers, own) + shared
        couplings.append(jnp.where(inside, column(numbers, own) + shared, nothing))
    rows = lax.broadcasted_iota(jnp.int32, (count, width), 0)
    cols = lax.broadcasted_iota(jnp.int32, (count, width), 1)
    blank = jnp.zeros((count, width), jnp.float32)
    matrix = jnp.where(cols == rows, diagonal, blank)
    for shift, coupling in zip((across, -across, 1, -1), couplings):
        matrix = matrix - jnp.where((cols == rows + shift) & (cols < count), coupling, blank)
    matrix = jnp.where(cols == rows + count, jnp.ones((count, 1), jnp.float32), matrix)
    if count <= 16:
        for group in uncoupled_groups(count, across):
            rest = matrix
            for step in group:
                pivot_row = matrix[step : step + 1, :] / matrix[step : step + 1, step : step + 1]
                rest = rest - matrix[:, step : step + 1] * pivot_row
                rest = jnp.where(rows == step, pivot_row, rest)
            matrix = rest
        return pltpu.roll(matrix, width - count, 1)
    work[...] = matrix

    def eliminate(step, _):
        values = work[...]
        pivot_row = work[pl.ds(step, 1), :]
        at_step = cols == step
        factors = jnp.sum(jnp.where(at_step, values, blank), axis=1, keepdims=True)
        pivot = jnp.sum(jnp.where(at_step[:1], pivot_row, blank[:1]), axis=1, keepdims=True)
        pivot_row = pivot_row / pivot
        work[...] = jnp.where(rows == step, pivot_row, values - factors * pivot_row)
        return 0

    lax.fori_loop(0, count, eliminate, 0)
    values = work[...]
    if count % 128:
        return pltpu.roll(values, width - count, 1)
    return values[:, count : 2 * count]


def answer(inverse, sums):
    return jnp.sum(inverse * sums, axis=0, keepdims=True)


def at_box(values, row_side, col_side):
    long_pos, across_pos, long_count, across_count = position()
    there_long, there_across = long_pos + row_side, across_pos + col_side
    inside = (
        (there_long >= 0)
        & (there_long < long_count)
        & (there_across >= 0)
        & (there_across < across_count)
    )
    lanes = lax.broadcasted_iota(jnp.int32, values.shape, 1)
    wanted = (lanes == there_long * across_count + there_across) & inside
    return jnp.sum(jnp.where(wanted, values, jnp.zeros_like(values)), axis=1, keepdims=True)


def coarse_corrections(parts, *refs):
    table_parts, (out, work) = refs[:parts], refs[parts:]
    count = work.shape[0]
    numbers = last_rows_merged(table_parts, count)
    across_count = lax.axis_size("narrow")
    inverse = coarse_inverse(numbers, work)
    sums = column(numbers, IMAGE_SUM)
    sums = sums - column(pltpu.roll(numbers, count - across_count, 0), FLOW_LONG_LOW)
    sums = sums - column(pltpu.roll(numbers, across_count, 0), FLOW_LONG_HIGH)
    sums = sums - column(pltpu.roll(numbers, count - 1, 0), FLOW_ACROSS_LOW)
    sums = sums - column(pltpu.roll(numbers, 1, 0), FLOW_ACROSS_HIGH)
    load_sums = column(numbers, LOAD_SUM)
    sums = load_sums * (1.0 - 1.0 / cheb_center) - sums
    out[0:1, :] = answer(inverse, load_sums) * (1.0 / cheb_center)
    out[1:2, :] = answer(inverse, sums) * gain


def second_solve(box, local, low, high, left, right, inverses, answers, *rest):
    to_long, to_across, to_deep, mass, load_window = rest[:5]
    tables = rest[5 : 5 + N_TABLES]
    iterate, top, bottom, last_col, first_col, out = rest[5 + N_TABLES : 11 + N_TABLES]
    window, spectral, middle, sems = rest[11 + N_TABLES :]
    long_pos, across_pos, long_count, across_count = position()
    coarse = answers[0:1, :]
    own_shift = at_box(answers[1:2, :], 0, 0)
    shifts = {
        (row_side, col_side): at_box(coarse, row_side, col_side)
        for row_side in (-1, 0, 1)
        for col_side in (-1, 0, 1)
    }

    def add(values, row_side, col_side):
        shift = shifts[row_side, col_side]
        if values.ndim == 3:
            shift = shift.reshape(1, 1, 1)
        return values + shift

    edge = REACH * box.across
    low, high = (
        ref.at[:edge].reshape(REACH, box.across, box.deep) for ref in (low, high)
    )
    wide_sides, narrow_sides = Sides("wide", low, high), Sides("narrow", left, right)
    fill_window(box, window, local, wide_sides, narrow_sides, REACH, 0, REACH, add)
    weights = (to_long, to_across, to_deep, mass)

    steps = range(box.ey // 8)
    x = [some_cols(box, window, 1, step) for step in range(-1, len(steps) + 1)]
    flow = [
        some_cols(box, to_long, 0, step) * (x[step + 1] - some_cols(box, window, 0, step))
        for step in steps
    ]
    state = [x, flow]

    def divided(values, col):
        return values * inverses[col]

    def residual(start_row):
        rows = []
        for row in range(start_row + 1, start_row + 9):
            image, *state[:] = negative_image(box, window, row, row, *state, weights)
            image = [some_cols(box, load_window, row, step) + image[step] for step in steps]
            rows.append(jnp.concatenate(image, axis=0))
        return jnp.stack(rows)

    inner = slice(EDGE, EDGE + box.across)
    first = REACH
    row_ids = lax.broadcasted_iota(jnp.int32, (1, padded(box.ex)), 1)
    col_ids = lax.broadcasted_iota(jnp.int32, (1, padded(box.ey)), 1)
    col_ids = (col_ids & 7) * (box.ey // 8) + lax.shift_right_logical(col_ids, 3)
    row_mask = jnp.where(row_ids < MARGIN, as_float(long_pos > 0), 1.0)
    row_mask = jnp.where(row_ids >= MARGIN + box.long, as_float(long_pos < long_count - 1), row_mask)
    col_mask = jnp.where(col_ids < MARGIN, as_float(across_pos > 0), 1.0)
    col_mask = jnp.where(
        col_ids >= MARGIN + box.across, as_float(across_pos < across_count - 1), col_mask
    )
    keep = 1.0 + rho_second * rho_first
    copies = []

    def emit(start, values):
        rows = values.reshape(8, box.across, box.deep)
        before = window[first + start : first + start + 8, inner, :]
        shift = own_shift.reshape(1, 1, 1)
        iterate[start : start + 8] = keep * before + (gain * rows + shift)
        copies.append(
            pltpu.make_async_copy(
                iterate.at[start : start + 8], out.at[start : start + 8], sems.at[len(copies)]
            )
        )
        copies[-1].start()

    box_solve(
        box, residual, divided, tables, row_mask, col_mask, spectral, middle, emit
    )
    rows = in_order(is_even("wide"), iterate[box.long - 1], iterate[0])
    top[...], bottom[...] = rows
    flat = iterate.reshape(box.long * box.across, box.deep)
    cols = [flat[row_of(box.across, col, box.long), :] for col in (box.across - 1, 0)]
    last_col[...], first_col[...] = in_order(is_even("narrow"), *cols)
    for copy in copies:
        copy.wait()


def inner_residual(
    box, load, iterate, to_long, to_across, to_deep, mass, rows, cols, out, window, result, sems
):
    inner = slice(EDGE, EDGE + box.across)
    flat = window.reshape((box.long + 2) * box.cols, box.deep)
    iterate_flat = iterate.reshape(box.long * box.across, box.deep)
    blank = jnp.zeros((box.long + 2, EDGE, box.deep), jnp.float32)
    window[:, :EDGE, :] = blank
    window[:, EDGE + box.across :, :] = blank
    window[1 : 1 + box.long, inner, :] = iterate[...]
    window[0, inner, :] = iterate[0]
    window[1 + box.long, inner, :] = iterate[box.long - 1]
    for col, place in ((0, EDGE - 1), (box.across - 1, EDGE + box.across)):
        values = iterate_flat[row_of(box.across, col, box.long), :]
        flat[row_of(box.cols, place, box.long, 1), :] = values
    weights = (to_long, to_across, to_deep, mass)
    steps = range(box.ey // 8)
    x = [some_cols(box, window, 1, step) for step in range(-1, len(steps) + 1)]
    flow = [jnp.zeros((8, box.deep), jnp.float32) for _ in steps]
    middle = slice(8, box.across - 8)
    copies = []
    for row in range(box.long):
        image, x, flow = negative_image(box, window, row + 1, REACH + row, x, flow, weights)
        for step in steps:
            place = pl.ds(EDGE - MARGIN + step, 8, stride=box.ey // 8)
            result[row, place, :] = image[step]
        values = load[row] + result[row, inner]
        result[row, inner] = values
        cols[0, row] = values[:8]
        cols[1, row] = values[box.across - 8 :]
        if row == 0:
            rows[0] = values
        if row == box.long - 1:
            rows[1] = values
        if row % 8 == 7:
            part = slice(row - 7, row + 1)
            copy = pltpu.make_async_copy(
                result.at[part, EDGE + 8 : EDGE + box.across - 8],
                out.at[part, middle],
                sems.at[row // 8],
            )
            copy.start()
            copies.append(copy)
    for copy in copies:
        copy.wait()


def outer_residual(
    box, iterate, low, high, left, right, to_long, to_across, rows, cols, inner_out, out,
    row_part, col_part, sems
):
    del inner_out
    inner = slice(EDGE, EDGE + box.across)
    middle = slice(8, box.across - 8)
    wide_sides, narrow_sides = Sides("wide", low, high), Sides("narrow", left, right)
    last = box.long - 1
    iterate_flat = iterate.reshape(box.long * box.across, box.deep)
    across_flat = to_across.reshape(box.flat, box.deep)
    below = to_long[REACH - 1, inner] * (wide_sides.low(Ellipsis) - iterate[0])
    above = to_long[REACH + last, inner] * (wide_sides.high(Ellipsis) - iterate[last])
    row_part[0] = (rows[0] + below)[middle]
    row_part[1] = (rows[1] + above)[middle]
    copies = [
        pltpu.make_async_copy(row_part.at[0], out.at[0, middle], sems.at[0]),
        pltpu.make_async_copy(row_part.at[1], out.at[last, middle], sems.at[1]),
    ]
    for copy in copies:
        copy.start()
    col_part[...] = cols[...]
    flat = col_part.reshape(2 * box.long * 8, box.deep)
    for side, (from_side, col, face, tile) in enumerate(
        (
            (narrow_sides.low, 0, EDGE - 1, slice(0, 8)),
            (narrow_sides.high, box.across - 1, EDGE + box.across - 1, slice(box.across - 8, None)),
        )
    ):
        weight = across_flat[row_of(box.cols, face, box.long, REACH), :]
        own = iterate_flat[row_of(box.across, col, box.long), :]
        place = pl.ds(side * box.long * 8 + side * 7, box.long, stride=8)
        flat[place, :] = flat[place, :] + weight * (from_side(Ellipsis) - own)
        col_part[side, 0] = col_part[side, 0] + below[tile]
        col_part[side, last] = col_part[side, last] + above[tile]
        first_col = side * (box.across - 8)
        copy = pltpu.make_async_copy(
            col_part.at[side], out.at[:, first_col : first_col + 8], sems.at[2 + side]
        )
        copy.start()
        copies.append(copy)
    for copy in copies:
        copy.wait()


def swaps(axis):
    sizes = (lax.axis_size("wide"), lax.axis_size("narrow"))
    along = ("wide", "narrow").index(axis)
    size, beside = sizes[along], sizes[1 - along]

    def number(place, other_place):
        pair = (place, other_place) if along == 0 else (other_place, place)
        return pair[0] * sizes[1] + pair[1]

    ways = []
    for way in range(2):
        pairs = []
        for place in range(size):
            for other_place in range(beside):
                partner = place + 1 if place % 2 == way else place - 1
                there = other_place
                if not 0 <= partner < size:
                    partner = place
                    there = other_place ^ 1 if beside % 2 == 0 else other_place
                pairs.append((number(place, other_place), number(partner, there)))
        ways.append(pairs)
    return ways


def exchange(axis, first, second):
    ways = swaps(axis)
    axes = ("wide", "narrow")
    return lax.ppermute(first, axes, ways[0]), lax.ppermute(second, axes, ways[1])


def from_other_end(axis, table):
    size = lax.axis_size(axis)
    return lax.ppermute(table, axis, [(i, size - 1 - i) for i in range(size)])


def two_away(axis, table):
    size = lax.axis_size(axis)
    return lax.ppermute(table, axis, [(i, (i + 2) % size) for i in range(size)])


def tell(table):
    count = table.shape[0]
    long_pos, across_pos, _, across_count = position()
    own = lax.dynamic_slice_in_dim(table, long_pos * across_count + across_pos, 1, axis=0)
    line = jnp.broadcast_to(own, (count, 1, 128))
    told = lax.all_to_all(line, ("wide", "narrow"), split_axis=0, concat_axis=0, tiled=True)
    return told.reshape(count, 128)


def on_device(zone, scale, diffusivity, decay, load):
    box = Box(load.shape)
    long, across, deep = load.shape
    count = lax.axis_size("wide") * lax.axis_size("narrow")
    by_margins = lax.axis_size("wide") == 4 and lax.axis_size("narrow") == 4
    tables = tables_of(box)
    decay = decay.reshape(1, -1)
    cells = f32(long, across, deep)
    whole_zone = jax.ShapeDtypeStruct(cells.shape, zone.dtype)
    window = f32(box.rows, box.cols, deep)
    table_shape = f32(count, 128)
    anywhere = pl.BlockSpec(memory_space=pl.ANY)
    in_hbm = pl.BlockSpec(memory_space=pltpu.HBM)

    def scratch(shape):
        return pltpu.VMEM(shape, jnp.float32)

    def pinned(field):
        return pltpu.with_memory_space_constraint(field, pltpu.HBM)

    spectral = scratch((box.ey, padded(box.ex), deep))
    middle = scratch((long, padded(box.ey), deep))

    def pack(wide, fields, sides, parts=(), after=()):
        rows = message_rows(box, wide * len(fields)) + (count if parts else 0)
        message = f32(rows, deep)
        body = functools.partial(pack_fields, box, wide, len(fields), len(parts), len(after))
        return call(
            body,
            (message, message) + ((table_shape,) if parts else ()),
            [VMEM] * (len(fields) + 2 + len(parts)) + [anywhere] * len(after),
        )(*fields, *sides, *parts, *after)

    far = f32(2 * REACH, across, deep)
    far_zone, far_scale, far_load = pinned(zone), pinned(scale), pinned(load)
    load_first, load_second, first, second = call(
        functools.partial(bring_edges, box),
        (f32(MARGIN, across, deep),) * 2 + (far, far),
        [in_hbm] * 3,
        [pltpu.VMEM((2, REACH, across, deep), zone.dtype), pltpu.SemaphoreType.DMA((6,))],
    )(far_zone, far_scale, far_load)
    load, scale, zone = call(
        bring_box,
        (cells, cells, whole_zone),
        [in_hbm] * 3 + [anywhere],
        [pltpu.SemaphoreType.DMA((3,))],
    )(far_load, far_scale, far_zone, load_first)
    load_wide = exchange("wide", load_first, load_second)
    far_wide = exchange("wide", first, second)
    load_first, load_second = pack(MARGIN, [load], load_wide)
    load_narrow = exchange("narrow", load_first, load_second)
    sums, table = call(
        functools.partial(box_sums, box),
        (f32(8, 128), table_shape),
        [VMEM] * 3 + [anywhere] + [VMEM] * 2,
    )(zone, scale, load, load_first, diffusivity, decay)
    far_narrow = exchange("narrow", *pack(REACH, [scale, zone], far_wide))
    load_window, local, image, inverses = call(
        functools.partial(first_solve, box),
        (window, cells, f32(across, deep), f32(box.ey, box.ex, deep)),
        [VMEM] * 8 + [VMEM] * 2 + [VMEM] * N_TABLES,
        [spectral, middle],
        flops=4 * 10**9,
    )(load, *load_wide, *load_narrow, sums, zone, scale, diffusivity, decay, *tables)
    message = f32(REACH * across + count, deep)
    table, first, second = call(
        functools.partial(image_sums, box), (table_shape, message, message), [VMEM] * 9 + [VMEM]
    )(zone, scale, local, image, *far_wide, *far_narrow, table, diffusivity)
    own_table = table
    wide = exchange("wide", first, second)
    parts = (table, wide[0])
    if by_margins:
        parts += (two_away("wide", table), from_other_end("wide", table))
    to_long, to_across, *windows = call(
        functools.partial(side_weights, box),
        (window,) * 4,
        [VMEM] * 6 + [VMEM],
        flops=10**9,
    )(zone, scale, *far_wide, *far_narrow, diffusivity)
    to_deep, mass = call(
        functools.partial(deep_weights, box),
        (window,) * 2,
        [VMEM] * 2 + [VMEM] * 2,
        flops=10**9,
    )(*windows, diffusivity, decay)
    weights = (to_long, to_across, to_deep, mass)
    first, second, table = pack(REACH, [local], wide, parts, [to_long])
    narrow = exchange("narrow", first, second)
    if by_margins:
        table = call(join_rows, table_shape, [VMEM] * 2)(table, narrow[0])
        parts = (table, two_away("narrow", table))
    else:
        parts = (tell(own_table),)
    row, col = f32(across, deep), f32(long, deep)
    answers = call(
        functools.partial(coarse_corrections, len(parts)),
        f32(8, -(-count // 128) * 128),
        [VMEM] * len(parts),
        [scratch((count, -(-2 * count // 128) * 128))],
    )(*parts)
    iterate, first_row, second_row, first_col, second_col, result = call(
        functools.partial(second_solve, box),
        (cells, row, row, col, col, cells),
        [VMEM] * (12 + N_TABLES),
        [scratch(window.shape), spectral, middle, pltpu.SemaphoreType.DMA((long // 8,))],
        flops=4 * 10**9,
        out_spec=(VMEM,) * 5 + (anywhere,),
    )(local, *wide, *narrow, inverses, answers, *weights, load_window, *tables)
    narrow = exchange("narrow", first_col, second_col)
    wide = exchange("wide", first_row, second_row)
    rows, cols, inner = call(
        functools.partial(inner_residual, box),
        (f32(2, across, deep), f32(2, long, 8, deep), cells),
        [VMEM] * 6,
        [
            scratch((long + 2, box.cols, deep)),
            scratch((long, box.cols, deep)),
            pltpu.SemaphoreType.DMA((long // 8,)),
        ],
        flops=10**9,
        out_spec=(VMEM, VMEM, anywhere),
    )(load, iterate, *weights)
    residual = call(
        functools.partial(outer_residual, box),
        cells,
        [VMEM] * 9 + [anywhere],
        [
            scratch((2, across - 16, deep)),
            scratch((2, long, 8, deep)),
            pltpu.SemaphoreType.DMA((4,)),
        ],
        out_spec=anywhere,
        aliases={9: 0},
    )(iterate, *wide, *narrow, to_long, to_across, rows, cols, inner)
    return result, residual


def solution(mesh):
    split = P(("groups", "wide"), "narrow", None)
    return jax.shard_map(
        on_device,
        mesh=mesh,
        in_specs=(split, split, P(), P(), split),
        out_specs=(split, split),
        check_vma=False,
    )
```

```python
import functools

import jax
import jax.numpy as jnp
import ml_dtypes
import numpy as np
from jax import lax
from jax.experimental import pallas as pl
from jax.experimental.pallas import tpu as pltpu
from jax.sharding import PartitionSpec as P

MARGIN = 4
REACH = MARGIN + 1
EDGE = 8

cheb_center = 1.3
cheb_radius = 1.2
cheb_ratio = 1.3 / 1.2
rho_first = 1.0 / cheb_ratio
rho_second = 1.0 / (2.0 * cheb_ratio - rho_first)
gain = 2.0 * rho_second / cheb_radius

MEANS = range(4)
BOX_DIAGONAL, LONG_HIGH, LONG_LOW, ACROSS_HIGH, ACROSS_LOW, LOAD_SUM = range(4, 10)
IMAGE_SUM, FLOW_LONG_HIGH, FLOW_LONG_LOW, FLOW_ACROSS_HIGH, FLOW_ACROSS_LOW = range(16, 21)

VMEM = pl.BlockSpec(memory_space=pltpu.VMEM)


def sine_basis(length):
    indices = np.arange(1, length + 1)
    phases = indices[:, None] * indices[None, :] % (2 * (length + 1))
    table = np.sqrt(2.0 / (length + 1)) * np.sin(np.pi * phases / (length + 1))
    eigvals = 4.0 * np.sin(np.pi * indices / (2.0 * (length + 1))) ** 2
    return table.astype(np.float32), eigvals.astype(np.float32)


def call(body, out_shape, in_specs, scratch=(), flops=0, out_spec=None, aliases=None):
    return pl.pallas_call(
        body,
        out_shape=out_shape,
        in_specs=in_specs,
        out_specs=out_spec or jax.tree.map(lambda _: VMEM, out_shape),
        scratch_shapes=list(scratch),
        compiler_params=pltpu.CompilerParams(vmem_limit_bytes=30 * 2**20),
        cost_estimate=pl.CostEstimate(flops=flops, bytes_accessed=0, transcendentals=0),
        input_output_aliases=aliases or {},
    )


def f32(*shape):
    return jax.ShapeDtypeStruct(shape, jnp.float32)


class Box:
    def __init__(self, shape):
        self.long, self.across, self.deep = shape
        self.ex = self.long + 2 * MARGIN
        self.ey = self.across + 2 * MARGIN
        self.rows = self.long + 2 * REACH
        self.cols = self.across + 2 * EDGE
        self.flat = self.rows * self.cols


def pieces(values, count):
    parts = []
    for _ in range(count - 1):
        scaled = values * 65537.0
        part = scaled - (scaled - values)
        parts.append(part)
        values = values - part
    return parts + [values]


def left_table(table, depth, count):
    rows, cols = table.shape
    wide = np.zeros((rows, depth), np.float32)
    wide[:, :cols] = table
    parts = []
    rest = wide
    for _ in range(count):
        part = rest.astype(ml_dtypes.bfloat16).astype(np.float32)
        parts.append(part)
        rest = rest - part
    blank = np.zeros_like(parts[0])
    lines = []
    for index in range(count):
        used = count - index if count > 2 else count
        lines.append(np.concatenate([parts[index]] * used + [blank] * (count - used), axis=1))
    return np.concatenate(lines, axis=0)


def right_tables(table):
    rest, parts = table, []
    for _ in range(3):
        part = rest.astype(ml_dtypes.bfloat16).astype(np.float32)
        parts.append(part)
        rest = rest - part
    both = np.concatenate([parts[0], parts[1]], axis=1)
    return np.concatenate([both, both], axis=0), np.concatenate([parts[2], parts[0]], axis=0)


def padded(size):
    return -(-size // 8) * 8


FORWARD, BACKWARD = 2, 3


def tables_of(box):
    sine_x, eig_x = sine_basis(box.ex)
    sine_y, eig_y = sine_basis(box.ey)
    sine_z, eig_z = sine_basis(box.deep)
    in_order_of_steps = np.arange(box.ey).reshape(8, box.ey // 8).T.reshape(-1)
    from_y = sine_y[MARGIN : MARGIN + box.across]
    from_x = sine_x[MARGIN : MARGIN + box.long]
    spread_x = np.broadcast_to(eig_x[:, None], (box.ex, box.deep))
    spread_y = np.broadcast_to(eig_y[:, None], (box.ey, box.deep))
    main_z, rest_z = right_tables(sine_z)
    return [
        jnp.asarray(np.ascontiguousarray(t))
        for t in (
            left_table(sine_y[:, in_order_of_steps], padded(box.ey), FORWARD),
            left_table(sine_x, padded(box.ex), FORWARD),
            left_table(from_x, padded(box.ex), BACKWARD),
            left_table(from_y, padded(box.ey), BACKWARD),
            main_z,
            rest_z,
            spread_x,
            spread_y,
            eig_z[None, :],
        )
    ]


N_TABLES = 9


def one_pass(left, right):
    return lax.dot_general(
        left,
        right,
        (((1,), (0,)), ((), ())),
        precision=lax.Precision.DEFAULT,
        preferred_element_type=jnp.float32,
    )


def dot_left(table, values, count, rows):
    total = one_pass(table, jnp.concatenate(pieces(values, count), axis=0))
    return sum(total[index * rows : (index + 1) * rows] for index in range(1, count)) + total[:rows]


def dot_right(values, main, rest, count):
    deep = values.shape[1]
    parts = pieces(values, count)
    total = one_pass(jnp.concatenate(parts[:2], axis=1), main)
    result = total[:, :deep] + total[:, deep:]
    if count == 3:
        result = result + one_pass(jnp.concatenate([parts[0], parts[2]], axis=1), rest)
    return result


def with_rows(values, rows):
    if values.shape[0] == rows:
        return values
    blank = jnp.zeros((rows - values.shape[0],) + values.shape[1:], values.dtype)
    return jnp.concatenate([values, blank], axis=0)


FORWARD_ROWS, COLS_ABREAST, BACKWARD_ROWS = 24, 40, 32


def fitting(size, wanted):
    return max(part for part in range(8, wanted + 1, 8) if size % part == 0)


def beside(values):
    return jnp.concatenate(values, axis=1)


def apart(values, lanes):
    return [values[:, start : start + lanes] for start in range(0, values.shape[1], lanes)]


def box_solve(box, source, divided, tables, row_mask, col_mask, spectral, middle, emit):
    into_y, into_x, from_x, from_y, main_z, rest_z = tables[:6]
    deep = box.deep
    deep_x, deep_y = padded(box.ex), padded(box.ey)
    into_y, into_x = into_y[...], into_x[...]
    if col_mask is not None:
        mask = jnp.concatenate([col_mask] * FORWARD, axis=1)
        into_y = into_y * mask
        mask = jnp.concatenate([row_mask] * FORWARD, axis=1)
        into_x = into_x * mask
    from_x, from_y, main_z, rest_z = from_x[...], from_y[...], main_z[...], rest_z[...]
    spectral_flat = spectral.reshape(box.ey * deep_x, deep)
    middle_flat = middle.reshape(box.long * deep_y, deep)
    if deep_x > box.ex:
        spectral[:, box.ex :, :] = jnp.zeros((box.ey, deep_x - box.ex, deep), jnp.float32)
    if deep_y > box.ey:
        middle[:, box.ey :, :] = jnp.zeros((box.long, deep_y - box.ey, deep), jnp.float32)
    step = fitting(box.ex, FORWARD_ROWS)
    for start in range(0, box.ex, step):
        block = jnp.concatenate([source(row) for row in range(start, start + step, 8)], axis=0)
        block = dot_right(block.reshape(step * box.ey, deep), main_z, rest_z, FORWARD)
        block = block.reshape(step, box.ey, deep)
        wide = beside([block[row] for row in range(step)])
        wide = dot_left(into_y, with_rows(wide, deep_y), FORWARD, box.ey)
        for row, values in enumerate(apart(wide, deep)):
            spectral_flat[pl.ds(start + row, box.ey, stride=deep_x), :] = values
    step = fitting(box.ey, COLS_ABREAST)
    for start in range(0, box.ey, step):
        wide = beside([spectral[col] for col in range(start, start + step)])
        wide = apart(dot_left(into_x, wide, FORWARD, box.ex), deep)
        wide = beside([divided(values, start + part) for part, values in enumerate(wide)])
        wide = dot_left(from_x, with_rows(wide, deep_x), BACKWARD, box.long)
        for part, values in enumerate(apart(wide, deep)):
            middle_flat[pl.ds(start + part, box.long, stride=deep_y), :] = values
    step = fitting(box.long, BACKWARD_ROWS)
    for start in range(0, box.long, step):
        wide = beside([middle[row] for row in range(start, start + step)])
        parts = apart(dot_left(from_y, wide, BACKWARD, box.across), deep)
        values = dot_right(jnp.concatenate(parts, axis=0), main_z, rest_z, BACKWARD)
        for row in range(0, step, 8):
            emit(start + row, values[row * box.across : (row + 8) * box.across])


def position():
    long_pos, across_pos = lax.axis_index("wide"), lax.axis_index("narrow")
    return long_pos, across_pos, lax.axis_size("wide"), lax.axis_size("narrow")


def as_float(flag):
    return jnp.where(flag, jnp.float32(1.0), jnp.float32(0.0))


def is_even(axis):
    return lax.rem(lax.axis_index(axis), 2) == 0


class Sides:
    def __init__(self, axis, first, second):
        position = lax.axis_index(axis)
        self.even = is_even(axis)
        self.has_low = as_float(position > 0)
        self.has_high = as_float(position < lax.axis_size(axis) - 1)
        self.first, self.second = first, second

    def low(self, *index):
        return jnp.where(self.even, self.second[index], self.first[index]) * self.has_low

    def high(self, *index):
        return jnp.where(self.even, self.first[index], self.second[index]) * self.has_high


def in_order(even, up, down):
    return jnp.where(even, up, down), jnp.where(even, down, up)


def row_of(stride, col, count, first=0):
    return pl.ds(first * stride + col, count, stride=stride)


def pack_columns(box, fields, wide_sides, wide, first, second):
    corner = len(fields) * wide * box.long
    even = is_even("narrow")
    place = 0
    for field, sides in zip(fields, wide_sides):
        for step in range(wide):
            cols = (box.across - wide + step, step)
            values = [field[row_of(box.across, col, box.long), :] for col in cols]
            low = [sides.low(row_of(box.across, col, wide), slice(None)) for col in cols]
            high = [sides.high(row_of(box.across, col, wide), slice(None)) for col in cols]
            at = corner + 2 * REACH * place
            for start, parts in ((place * box.long, values), (at, low), (at + REACH, high)):
                parts = in_order(even, *(part.astype(jnp.float32) for part in parts))
                size = parts[0].shape[0]
                first[start : start + size, :], second[start : start + size, :] = parts
            place += 1


def message_rows(box, count):
    return -(-(count * (box.long + 2 * REACH)) // 8) * 8


def pack_fields(box, wide, fields, tables, after, *refs):
    own, (low, high), refs = refs[:fields], refs[fields : fields + 2], refs[fields + 2 :]
    parts, (first, second, *table) = refs[:tables], refs[tables + after :]
    size = wide * box.across
    flat = [field.reshape(box.long * box.across, box.deep) for field in own]
    low = low.reshape(low.size // box.deep, box.deep)
    high = high.reshape(high.size // box.deep, box.deep)
    sides = [
        Sides("wide", *(ref.at[index * size : (index + 1) * size] for ref in (low, high)))
        for index in range(fields)
    ]
    pack_columns(box, flat, sides, wide, first, second)
    if tables:
        known = last_rows_merged(parts, table[0].shape[0])
        table[0][...] = known
        first[first.shape[0] - known.shape[0] :, :] = known
        second[second.shape[0] - known.shape[0] :, :] = known


def bring_edges(box, zone, scale, load, load_first, load_second, first, second, staged, sems):
    even = is_even("wide")

    def edges(wide):
        up, down = box.long - wide, 0
        return [pl.ds(jnp.where(even, *pair), wide) for pair in ((up, down), (down, up))]

    copies = [
        (zone.at[edges(REACH)[0]], staged.at[0]),
        (zone.at[edges(REACH)[1]], staged.at[1]),
        (load.at[edges(MARGIN)[0]], load_first),
        (load.at[edges(MARGIN)[1]], load_second),
        (scale.at[edges(REACH)[0]], first.at[:REACH]),
        (scale.at[edges(REACH)[1]], second.at[:REACH]),
    ]
    copies = [
        pltpu.make_async_copy(source, target, sems.at[index])
        for index, (source, target) in enumerate(copies)
    ]
    for copy in copies:
        copy.start()
    for copy in copies[:2]:
        copy.wait()
    first[REACH:] = staged[0].astype(jnp.float32)
    second[REACH:] = staged[1].astype(jnp.float32)
    for copy in copies[2:]:
        copy.wait()


def bring_box(load, scale, zone, after, own_load, own_scale, own_zone, sems):
    del after
    parts = 4
    size = own_load.shape[0] // parts
    copies = []
    for part in range(parts):
        rows = slice(part * size, (part + 1) * size)
        for source, target in ((load, own_load), (scale, own_scale), (zone, own_zone)):
            copies.append(
                pltpu.make_async_copy(source.at[rows], target.at[rows], sems.at[len(copies)])
            )
            copies[-1].start()
    for copy in copies:
        copy.wait()


def fill_window(box, window, own, wide_sides, narrow_sides, wide, place, total, add=None):
    flat = window.reshape(box.flat, box.deep)
    nothing = jnp.zeros((box.rows, EDGE, box.deep), jnp.float32)
    window[:, :EDGE, :] = nothing
    window[:, EDGE + box.across :, :] = nothing
    if add is None:
        add = lambda values, row_side, col_side: values
    inner = slice(EDGE, EDGE + box.across)
    first, last = REACH, REACH + box.long
    if wide < REACH:
        blank = jnp.zeros((1, box.across, box.deep), jnp.float32)
        window[0:1, inner, :] = blank
        window[box.rows - 1 :, inner, :] = blank
    window[first:last, inner, :] = add(own[...].astype(jnp.float32), 0, 0)
    window[first - wide : first, inner, :] = add(wide_sides.low(Ellipsis), -1, 0)
    window[last : last + wide, inner, :] = add(wide_sides.high(Ellipsis), 1, 0)
    corner = total * box.long
    for step in range(wide):
        for source, col, side in (
            (narrow_sides.low, EDGE - wide + step, -1),
            (narrow_sides.high, EDGE + box.across + step, 1),
        ):
            for start, size, row, row_side in (
                ((place + step) * box.long, box.long, first, 0),
                (corner + 2 * REACH * (place + step), wide, first - wide, -1),
                (corner + 2 * REACH * (place + step) + REACH, wide, last, 1),
            ):
                values = source(slice(start, start + size), slice(None))
                flat[row_of(box.cols, col, size, row), :] = add(values, row_side, side)


def some_cols(box, ref, row, step):
    stride = box.ey // 8
    return ref[row, pl.ds(EDGE - MARGIN + step, 8, stride=stride), :]


def negative_image(box, window, row, at, x, flow_before, weights):
    to_long, to_across, to_deep, mass = weights
    steps = range(box.ey // 8)
    x_next = [some_cols(box, window, row + 1, step) for step in range(-1, len(steps) + 1)]
    flow_long = [
        some_cols(box, to_long, at, step) * (x_next[step + 1] - x[step + 1]) for step in steps
    ]
    flow_across = [
        some_cols(box, to_across, at, step) * (x[step + 2] - x[step + 1])
        for step in range(-1, len(steps))
    ]
    totals = []
    for step in steps:
        here = x[step + 1]
        lanes = here.shape[1]
        flow_deep = some_cols(box, to_deep, at, step) * (pltpu.roll(here, lanes - 1, 1) - here)
        total = flow_long[step] - flow_before[step] - some_cols(box, mass, at, step) * here
        total = total + (flow_across[step + 1] - flow_across[step])
        totals.append(total + (flow_deep - pltpu.roll(flow_deep, 1, 1)))
    return totals, x_next, flow_long


def in_steps(box, refs, rows):
    return jnp.stack(
        [
            jnp.concatenate([some_cols(box, ref, row, step) for step in range(box.ey // 8)], axis=0)
            for ref, row in zip(refs, rows)
        ]
    )


def looked_up(labels, values):
    return jnp.where(labels == 0, values[0], jnp.where(labels == 1, values[1], values[2]))


def at_own_row(line, shape):
    long_pos, across_pos, _, across_count = position()
    rows = lax.broadcasted_iota(jnp.int32, shape, 0)
    own = rows == long_pos * across_count + across_pos
    return jnp.where(own, line[:1], jnp.zeros(shape, jnp.float32))


def merged(table, *others):
    for other in others:
        table = jnp.where(table != 0.0, table, other)
    return table


def last_rows_merged(refs, count):
    return merged(*(ref[ref.shape[0] - count :, :] for ref in refs))


def join_rows(table, message, out):
    out[...] = last_rows_merged((table, message), out.shape[0])


def line_of(numbers, shape):
    count = -(-len(numbers) // 8) * 8
    rows = lax.broadcasted_iota(jnp.int32, (count, shape[1]), 0)
    lanes = lax.broadcasted_iota(jnp.int32, (count, shape[1]), 1)
    stacked = jnp.zeros((count, shape[1]), jnp.float32)
    place = jnp.zeros((count, shape[1]), jnp.bool_)
    for row, (index, values) in enumerate(numbers):
        stacked = jnp.where(rows == row, values, stacked)
        place = place | ((rows == row) & (lanes == index))
    sums = jnp.sum(stacked, axis=1, keepdims=True)
    line = jnp.sum(jnp.where(place, sums, jnp.zeros_like(stacked)), axis=0, keepdims=True)
    return jnp.broadcast_to(line, shape)


def box_sums(box, zone, scale, load, after, diffusivity, decay, out, table):
    del after
    nothing = jnp.zeros((box.across, box.deep), jnp.float32)
    half = [[0.5 * diffusivity[z : z + 1, d : d + 1] for z in range(3)] for d in range(3)]
    rates = [decay[0:1, z : z + 1] for z in range(3)]

    def halves(row):
        labels, factor = zone[row], scale[row]
        return [looked_up(labels, half[d]) * factor for d in range(3)] + [looked_up(labels, rates)]

    sums = [nothing] * 5
    for row in range(box.long):
        sums = [total + more for total, more in zip(sums, halves(row) + [load[row]])]

    def total(values):
        return jnp.sum(values, axis=0, keepdims=True)

    cells = box.long * box.across * box.deep
    numbers = [(index, total(sums[index]) * (2.0 / cells)) for index in range(3)]
    mass = total(sums[3])
    numbers += [(3, mass / cells)]
    lane = lax.broadcasted_iota(jnp.int32, (1, box.deep), 1)
    ends = jnp.where((lane == 0) | (lane == box.deep - 1), total(sums[2]), 0.0)
    numbers += [
        (BOX_DIAGONAL, mass + ends),
        (LONG_HIGH, total(halves(box.long - 1)[0])),
        (LONG_LOW, total(halves(0)[0])),
        (ACROSS_HIGH, sums[1][box.across - 1 :]),
        (ACROSS_LOW, sums[1][:1]),
        (LOAD_SUM, total(sums[4])),
    ]
    line = line_of(numbers, out.shape)
    out[...] = line
    table[...] = at_own_row(line, table.shape)


def means_of(ref):
    return [ref[0:1, index : index + 1] for index in range(4)]


def first_solve(box, load, low, high, left, right, means, zone, scale, diffusivity, decay, *rest):
    tables = rest[:N_TABLES]
    window, local, image, inverses, spectral, middle = rest[N_TABLES:]
    spread_x, spread_y, eig_z = tables[6:]
    means = means_of(means)
    base = means[3] + means[0] * spread_x[...] + means[2] * eig_z[...]

    def divided(values, col):
        divisor = base + means[1] * spread_y[col : col + 1, :]
        inverse = pl.reciprocal(divisor, approx=True)
        for _ in range(2):
            inverse = inverse * (2.0 - divisor * inverse)
        inverses[col] = inverse
        return values * inverse

    half = [0.5 * diffusivity[z : z + 1, 2:3] for z in range(3)]
    rates = [decay[0:1, z : z + 1] for z in range(3)]
    lane = lax.broadcasted_iota(jnp.int32, (box.across, box.deep), 1)
    ends = jnp.where((lane == 0) | (lane == box.deep - 1), jnp.float32(1.0), jnp.float32(0.0))
    image[...] = jnp.zeros((box.across, box.deep), jnp.float32)
    wide_sides, narrow_sides = Sides("wide", low, high), Sides("narrow", left, right)
    fill_window(box, window, load, wide_sides, narrow_sides, MARGIN, 0, MARGIN)

    def emit(start, values):
        values = values * (1.0 / cheb_center)
        values = values.reshape(8, box.across, box.deep)
        local[start : start + 8] = values
        total = image[...]
        for row in range(8):
            labels = zone[start + row]
            mass = looked_up(labels, rates) + looked_up(labels, half) * scale[start + row] * ends
            total = total + mass * values[row]
        image[...] = total

    box_solve(
        box,
        lambda start: in_steps(box, [window] * 8, range(1 + start, 9 + start)),
        divided,
        tables,
        None,
        None,
        spectral,
        middle,
        emit,
    )


def side_weights(
    box, zone, scale, low, high, left, right, diffusivity, to_long, to_across, zone_window,
    scale_window
):
    for index, (window, own) in enumerate(((scale_window, scale), (zone_window, zone))):
        start = index * REACH
        wide_sides = Sides("wide", *(ref.at[start : start + REACH] for ref in (low, high)))
        narrow_sides = Sides("narrow", left, right)
        fill_window(box, window, own, wide_sides, narrow_sides, REACH, start, 2 * REACH)
    half = [[0.5 * diffusivity[z : z + 1, d : d + 1] for z in range(3)] for d in range(2)]

    def one_row(row, before):
        labels, factor = zone_window[row], scale_window[row]
        now = [looked_up(labels, half[d]) * factor for d in range(2)]
        to_across[row] = now[1] + pltpu.roll(now[1], box.cols - 1, 0)
        to_long[jnp.maximum(row - 1, 0)] = before + now[0]
        return now[0]

    def some_rows(index, before):
        for row in range(8):
            before = one_row(index * 8 + row, before)
        return before

    before = jnp.zeros((box.cols, box.deep), jnp.float32)
    before = lax.fori_loop(0, box.rows // 8, some_rows, before)
    for row in range(box.rows // 8 * 8, box.rows):
        before = one_row(row, before)
    to_long[box.rows - 1] = before


def deep_weights(box, zone_window, scale_window, diffusivity, decay, to_deep, mass):
    half = [0.5 * diffusivity[z : z + 1, 2:3] for z in range(3)]
    rates = [decay[0:1, z : z + 1] for z in range(3)]
    lane = lax.broadcasted_iota(jnp.int32, (box.cols, box.deep), 1)
    ends = jnp.where((lane == 0) | (lane == box.deep - 1), jnp.float32(1.0), jnp.float32(0.0))
    not_last = jnp.where(lane == box.deep - 1, jnp.float32(0.0), jnp.float32(1.0))

    def one_row(row):
        labels = zone_window[row]
        now = looked_up(labels, half) * scale_window[row]
        to_deep[row] = (now + pltpu.roll(now, box.deep - 1, 1)) * not_last
        mass[row] = looked_up(labels, rates) + now * ends

    def some_rows(index, _):
        for row in range(8):
            one_row(index * 8 + row)
        return 0

    lax.fori_loop(0, box.rows // 8, some_rows, 0)
    for row in range(box.rows // 8 * 8, box.rows):
        one_row(row)


def image_sums(
    box, zone, scale, local, image, low, high, left, right, table, diffusivity, out, up, down
):
    half = [[0.5 * diffusivity[z : z + 1, d : d + 1] for z in range(3)] for d in range(3)]
    shape = (box.long * box.across, box.deep)
    zone_flat, scale_flat, local_flat = zone.reshape(shape), scale.reshape(shape), local.reshape(shape)
    last_col = row_of(box.across, box.across - 1, box.long)
    first_col = row_of(box.across, 0, box.long)

    wide_sides, narrow_sides = Sides("wide", low, high), Sides("narrow", left, right)

    def side(source, place):
        return source(slice(place * box.long, (place + 1) * box.long), slice(None))

    above, below = wide_sides.high, wide_sides.low
    faces = [
        (0, zone[box.long - 1], scale[box.long - 1], local[box.long - 1], above(REACH), above(0)),
        (0, zone[0], scale[0], local[0], below(2 * REACH - 1), below(REACH - 1)),
        (
            1,
            zone_flat[last_col, :],
            scale_flat[last_col, :],
            local_flat[last_col, :],
            side(narrow_sides.high, REACH),
            side(narrow_sides.high, 0),
        ),
        (
            1,
            zone_flat[first_col, :],
            scale_flat[first_col, :],
            local_flat[first_col, :],
            side(narrow_sides.low, 2 * REACH - 1),
            side(narrow_sides.low, REACH - 1),
        ),
    ]
    flows = []
    for direction, labels, factor, values, far_labels, far_factor in faces:
        weight = looked_up(labels, half[direction]) * factor
        weight = weight + looked_up(far_labels, half[direction]) * far_factor
        flows.append(jnp.sum(weight * values, axis=0, keepdims=True))
    long_pos, across_pos, long_count, across_count = position()
    numbers = [
        (IMAGE_SUM, jnp.sum(image[...], axis=0, keepdims=True) + sum(flows)),
        (FLOW_LONG_HIGH, flows[0] * as_float(long_pos < long_count - 1)),
        (FLOW_LONG_LOW, flows[1] * as_float(long_pos > 0)),
        (FLOW_ACROSS_HIGH, flows[2] * as_float(across_pos < across_count - 1)),
        (FLOW_ACROSS_LOW, flows[3] * as_float(across_pos > 0)),
    ]
    known = table[...] + at_own_row(line_of(numbers, (8, out.shape[1])), out.shape)
    out[...] = known
    edge = REACH * box.across
    even = is_even("wide")
    for target, pair in ((up, (box.long - REACH, 0)), (down, (0, box.long - REACH))):
        target[:edge] = local[pl.ds(jnp.where(even, *pair), REACH)].reshape(edge, box.deep)
        target[edge:] = known


def column(values, index):
    return values[:, index : index + 1]


def uncoupled_groups(count, across):
    places = np.arange(count)
    long_step = np.abs(places[:, None] // across - places[None, :] // across)
    across_step = np.abs(places[:, None] % across - places[None, :] % across)
    coupled = long_step + across_step == 1
    left = list(range(count))
    groups = []
    while left:
        group = []
        for place in sorted(left, key=lambda p: (coupled[p][left].sum(), p)):
            if not coupled[place][group].any():
                group.append(place)
        left = [place for place in left if place not in group]
        for place in group:
            beside = [other for other in left if coupled[place][other]]
            for other in beside:
                coupled[other][beside] = True
                coupled[other][other] = False
        groups.append(group)
    return groups


def coarse_inverse(numbers, work):
    count, width = work.shape
    across = lax.axis_size("narrow")
    beyond = pltpu.roll(numbers, count - across, 0)
    beside = pltpu.roll(numbers, count - 1, 0)
    before = pltpu.roll(numbers, across, 0)
    ahead = pltpu.roll(numbers, 1, 0)
    place = lax.broadcasted_iota(jnp.int32, (count, 1), 0)
    across_pos = lax.rem(place, across)
    nothing = jnp.zeros((count, 1), jnp.float32)
    couplings = []
    diagonal = column(numbers, BOX_DIAGONAL)
    for own, other, there, inside in (
        (LONG_HIGH, LONG_LOW, beyond, place < count - across),
        (LONG_LOW, LONG_HIGH, before, place >= across),
        (ACROSS_HIGH, ACROSS_LOW, beside, across_pos < across - 1),
        (ACROSS_LOW, ACROSS_HIGH, ahead, across_pos > 0),
    ):
        shared = jnp.where(inside, column(there, other), nothing)
        diagonal = diagonal + column(numbers, own) + shared
        couplings.append(jnp.where(inside, column(numbers, own) + shared, nothing))
    rows = lax.broadcasted_iota(jnp.int32, (count, width), 0)
    cols = lax.broadcasted_iota(jnp.int32, (count, width), 1)
    blank = jnp.zeros((count, width), jnp.float32)
    matrix = jnp.where(cols == rows, diagonal, blank)
    for shift, coupling in zip((across, -across, 1, -1), couplings):
        matrix = matrix - jnp.where((cols == rows + shift) & (cols < count), coupling, blank)
    matrix = jnp.where(cols == rows + count, jnp.ones((count, 1), jnp.float32), matrix)
    if count <= 16:
        for group in uncoupled_groups(count, across):
            rest = matrix
            for step in group:
                pivot_row = matrix[step : step + 1, :] / matrix[step : step + 1, step : step + 1]
                rest = rest - matrix[:, step : step + 1] * pivot_row
                rest = jnp.where(rows == step, pivot_row, rest)
            matrix = rest
        return pltpu.roll(matrix, width - count, 1)
    work[...] = matrix

    def eliminate(step, _):
        values = work[...]
        pivot_row = work[pl.ds(step, 1), :]
        at_step = cols == step
        factors = jnp.sum(jnp.where(at_step, values, blank), axis=1, keepdims=True)
        pivot = jnp.sum(jnp.where(at_step[:1], pivot_row, blank[:1]), axis=1, keepdims=True)
        pivot_row = pivot_row / pivot
        work[...] = jnp.where(rows == step, pivot_row, values - factors * pivot_row)
        return 0

    lax.fori_loop(0, count, eliminate, 0)
    values = work[...]
    if count % 128:
        return pltpu.roll(values, width - count, 1)
    return values[:, count : 2 * count]


def answer(inverse, sums):
    return jnp.sum(inverse * sums, axis=0, keepdims=True)


def at_box(values, row_side, col_side):
    long_pos, across_pos, long_count, across_count = position()
    there_long, there_across = long_pos + row_side, across_pos + col_side
    inside = (
        (there_long >= 0)
        & (there_long < long_count)
        & (there_across >= 0)
        & (there_across < across_count)
    )
    lanes = lax.broadcasted_iota(jnp.int32, values.shape, 1)
    wanted = (lanes == there_long * across_count + there_across) & inside
    return jnp.sum(jnp.where(wanted, values, jnp.zeros_like(values)), axis=1, keepdims=True)


def coarse_corrections(parts, *refs):
    table_parts, (out, work) = refs[:parts], refs[parts:]
    count = work.shape[0]
    numbers = last_rows_merged(table_parts, count)
    across_count = lax.axis_size("narrow")
    inverse = coarse_inverse(numbers, work)
    sums = column(numbers, IMAGE_SUM)
    sums = sums - column(pltpu.roll(numbers, count - across_count, 0), FLOW_LONG_LOW)
    sums = sums - column(pltpu.roll(numbers, across_count, 0), FLOW_LONG_HIGH)
    sums = sums - column(pltpu.roll(numbers, count - 1, 0), FLOW_ACROSS_LOW)
    sums = sums - column(pltpu.roll(numbers, 1, 0), FLOW_ACROSS_HIGH)
    load_sums = column(numbers, LOAD_SUM)
    sums = load_sums * (1.0 - 1.0 / cheb_center) - sums
    out[0:1, :] = answer(inverse, load_sums) * (1.0 / cheb_center)
    out[1:2, :] = answer(inverse, sums) * gain


def second_solve(box, local, low, high, left, right, inverses, answers, *rest):
    to_long, to_across, to_deep, mass, load_window = rest[:5]
    tables = rest[5 : 5 + N_TABLES]
    iterate, top, bottom, last_col, first_col, out = rest[5 + N_TABLES : 11 + N_TABLES]
    window, spectral, middle, sems = rest[11 + N_TABLES :]
    long_pos, across_pos, long_count, across_count = position()
    coarse = answers[0:1, :]
    own_shift = at_box(answers[1:2, :], 0, 0)
    shifts = {
        (row_side, col_side): at_box(coarse, row_side, col_side)
        for row_side in (-1, 0, 1)
        for col_side in (-1, 0, 1)
    }

    def add(values, row_side, col_side):
        shift = shifts[row_side, col_side]
        if values.ndim == 3:
            shift = shift.reshape(1, 1, 1)
        return values + shift

    edge = REACH * box.across
    low, high = (
        ref.at[:edge].reshape(REACH, box.across, box.deep) for ref in (low, high)
    )
    wide_sides, narrow_sides = Sides("wide", low, high), Sides("narrow", left, right)
    fill_window(box, window, local, wide_sides, narrow_sides, REACH, 0, REACH, add)
    weights = (to_long, to_across, to_deep, mass)

    steps = range(box.ey // 8)
    x = [some_cols(box, window, 1, step) for step in range(-1, len(steps) + 1)]
    flow = [
        some_cols(box, to_long, 0, step) * (x[step + 1] - some_cols(box, window, 0, step))
        for step in steps
    ]
    state = [x, flow]

    def divided(values, col):
        return values * inverses[col]

    def residual(start_row):
        rows = []
        for row in range(start_row + 1, start_row + 9):
            image, *state[:] = negative_image(box, window, row, row, *state, weights)
            image = [some_cols(box, load_window, row, step) + image[step] for step in steps]
            rows.append(jnp.concatenate(image, axis=0))
        return jnp.stack(rows)

    inner = slice(EDGE, EDGE + box.across)
    first = REACH
    row_ids = lax.broadcasted_iota(jnp.int32, (1, padded(box.ex)), 1)
    col_ids = lax.broadcasted_iota(jnp.int32, (1, padded(box.ey)), 1)
    col_ids = (col_ids & 7) * (box.ey // 8) + lax.shift_right_logical(col_ids, 3)
    row_mask = jnp.where(row_ids < MARGIN, as_float(long_pos > 0), 1.0)
    row_mask = jnp.where(row_ids >= MARGIN + box.long, as_float(long_pos < long_count - 1), row_mask)
    col_mask = jnp.where(col_ids < MARGIN, as_float(across_pos > 0), 1.0)
    col_mask = jnp.where(
        col_ids >= MARGIN + box.across, as_float(across_pos < across_count - 1), col_mask
    )
    keep = 1.0 + rho_second * rho_first
    copies = []

    def emit(start, values):
        rows = values.reshape(8, box.across, box.deep)
        before = window[first + start : first + start + 8, inner, :]
        shift = own_shift.reshape(1, 1, 1)
        iterate[start : start + 8] = keep * before + (gain * rows + shift)
        copies.append(
            pltpu.make_async_copy(
                iterate.at[start : start + 8], out.at[start : start + 8], sems.at[len(copies)]
            )
        )
        copies[-1].start()

    box_solve(
        box, residual, divided, tables, row_mask, col_mask, spectral, middle, emit
    )
    rows = in_order(is_even("wide"), iterate[box.long - 1], iterate[0])
    top[...], bottom[...] = rows
    flat = iterate.reshape(box.long * box.across, box.deep)
    cols = [flat[row_of(box.across, col, box.long), :] for col in (box.across - 1, 0)]
    last_col[...], first_col[...] = in_order(is_even("narrow"), *cols)
    for copy in copies:
        copy.wait()


def inner_residual(
    box, load, iterate, to_long, to_across, to_deep, mass, rows, cols, out, window, result, sems
):
    inner = slice(EDGE, EDGE + box.across)
    flat = window.reshape((box.long + 2) * box.cols, box.deep)
    iterate_flat = iterate.reshape(box.long * box.across, box.deep)
    blank = jnp.zeros((box.long + 2, EDGE, box.deep), jnp.float32)
    window[:, :EDGE, :] = blank
    window[:, EDGE + box.across :, :] = blank
    window[1 : 1 + box.long, inner, :] = iterate[...]
    window[0, inner, :] = iterate[0]
    window[1 + box.long, inner, :] = iterate[box.long - 1]
    for col, place in ((0, EDGE - 1), (box.across - 1, EDGE + box.across)):
        values = iterate_flat[row_of(box.across, col, box.long), :]
        flat[row_of(box.cols, place, box.long, 1), :] = values
    weights = (to_long, to_across, to_deep, mass)
    steps = range(box.ey // 8)
    x = [some_cols(box, window, 1, step) for step in range(-1, len(steps) + 1)]
    flow = [jnp.zeros((8, box.deep), jnp.float32) for _ in steps]
    middle = slice(8, box.across - 8)
    copies = []
    for row in range(box.long):
        image, x, flow = negative_image(box, window, row + 1, REACH + row, x, flow, weights)
        for step in steps:
            place = pl.ds(EDGE - MARGIN + step, 8, stride=box.ey // 8)
            result[row, place, :] = image[step]
        values = load[row] + result[row, inner]
        result[row, inner] = values
        cols[0, row] = values[:8]
        cols[1, row] = values[box.across - 8 :]
        if row == 0:
            rows[0] = values
        if row == box.long - 1:
            rows[1] = values
        if row % 8 == 7:
            part = slice(row - 7, row + 1)
            copy = pltpu.make_async_copy(
                result.at[part, EDGE + 8 : EDGE + box.across - 8],
                out.at[part, middle],
                sems.at[row // 8],
            )
            copy.start()
            copies.append(copy)
    for copy in copies:
        copy.wait()


def outer_residual(
    box, iterate, low, high, left, right, to_long, to_across, rows, cols, inner_out, out,
    row_part, col_part, sems
):
    del inner_out
    inner = slice(EDGE, EDGE + box.across)
    middle = slice(8, box.across - 8)
    wide_sides, narrow_sides = Sides("wide", low, high), Sides("narrow", left, right)
    last = box.long - 1
    iterate_flat = iterate.reshape(box.long * box.across, box.deep)
    across_flat = to_across.reshape(box.flat, box.deep)
    below = to_long[REACH - 1, inner] * (wide_sides.low(Ellipsis) - iterate[0])
    above = to_long[REACH + last, inner] * (wide_sides.high(Ellipsis) - iterate[last])
    row_part[0] = (rows[0] + below)[middle]
    row_part[1] = (rows[1] + above)[middle]
    copies = [
        pltpu.make_async_copy(row_part.at[0], out.at[0, middle], sems.at[0]),
        pltpu.make_async_copy(row_part.at[1], out.at[last, middle], sems.at[1]),
    ]
    for copy in copies:
        copy.start()
    col_part[...] = cols[...]
    flat = col_part.reshape(2 * box.long * 8, box.deep)
    for side, (from_side, col, face, tile) in enumerate(
        (
            (narrow_sides.low, 0, EDGE - 1, slice(0, 8)),
            (narrow_sides.high, box.across - 1, EDGE + box.across - 1, slice(box.across - 8, None)),
        )
    ):
        weight = across_flat[row_of(box.cols, face, box.long, REACH), :]
        own = iterate_flat[row_of(box.across, col, box.long), :]
        place = pl.ds(side * box.long * 8 + side * 7, box.long, stride=8)
        flat[place, :] = flat[place, :] + weight * (from_side(Ellipsis) - own)
        col_part[side, 0] = col_part[side, 0] + below[tile]
        col_part[side, last] = col_part[side, last] + above[tile]
        first_col = side * (box.across - 8)
        copy = pltpu.make_async_copy(
            col_part.at[side], out.at[:, first_col : first_col + 8], sems.at[2 + side]
        )
        copy.start()
        copies.append(copy)
    for copy in copies:
        copy.wait()


def swaps(axis):
    sizes = (lax.axis_size("wide"), lax.axis_size("narrow"))
    along = ("wide", "narrow").index(axis)
    size, beside = sizes[along], sizes[1 - along]

    def number(place, other_place):
        pair = (place, other_place) if along == 0 else (other_place, place)
        return pair[0] * sizes[1] + pair[1]

    ways = []
    for way in range(2):
        pairs = []
        for place in range(size):
            for other_place in range(beside):
                partner = place + 1 if place % 2 == way else place - 1
                there = other_place
                if not 0 <= partner < size:
                    partner = place
                    there = other_place ^ 1 if beside % 2 == 0 else other_place
                pairs.append((number(place, other_place), number(partner, there)))
        ways.append(pairs)
    return ways


def exchange(axis, first, second):
    ways = swaps(axis)
    axes = ("wide", "narrow")
    return lax.ppermute(first, axes, ways[0]), lax.ppermute(second, axes, ways[1])


def from_other_end(axis, table):
    size = lax.axis_size(axis)
    return lax.ppermute(table, axis, [(i, size - 1 - i) for i in range(size)])


def two_away(axis, table):
    size = lax.axis_size(axis)
    return lax.ppermute(table, axis, [(i, (i + 2) % size) for i in range(size)])


def tell(table):
    count = table.shape[0]
    long_pos, across_pos, _, across_count = position()
    own = lax.dynamic_slice_in_dim(table, long_pos * across_count + across_pos, 1, axis=0)
    line = jnp.broadcast_to(own, (count, 1, 128))
    told = lax.all_to_all(line, ("wide", "narrow"), split_axis=0, concat_axis=0, tiled=True)
    return told.reshape(count, 128)


def on_device(zone, scale, diffusivity, decay, load):
    box = Box(load.shape)
    long, across, deep = load.shape
    count = lax.axis_size("wide") * lax.axis_size("narrow")
    by_margins = lax.axis_size("wide") == 4 and lax.axis_size("narrow") == 4
    tables = tables_of(box)
    decay = decay.reshape(1, -1)
    cells = f32(long, across, deep)
    whole_zone = jax.ShapeDtypeStruct(cells.shape, zone.dtype)
    window = f32(box.rows, box.cols, deep)
    table_shape = f32(count, 128)
    anywhere = pl.BlockSpec(memory_space=pl.ANY)
    in_hbm = pl.BlockSpec(memory_space=pltpu.HBM)

    def scratch(shape):
        return pltpu.VMEM(shape, jnp.float32)

    def pinned(field):
        return pltpu.with_memory_space_constraint(field, pltpu.HBM)

    spectral = scratch((box.ey, padded(box.ex), deep))
    middle = scratch((long, padded(box.ey), deep))

    def pack(wide, fields, sides, parts=(), after=()):
        rows = message_rows(box, wide * len(fields)) + (count if parts else 0)
        message = f32(rows, deep)
        body = functools.partial(pack_fields, box, wide, len(fields), len(parts), len(after))
        return call(
            body,
            (message, message) + ((table_shape,) if parts else ()),
            [VMEM] * (len(fields) + 2 + len(parts)) + [anywhere] * len(after),
        )(*fields, *sides, *parts, *after)

    far = f32(2 * REACH, across, deep)
    far_zone, far_scale, far_load = pinned(zone), pinned(scale), pinned(load)
    load_first, load_second, first, second = call(
        functools.partial(bring_edges, box),
        (f32(MARGIN, across, deep),) * 2 + (far, far),
        [in_hbm] * 3,
        [pltpu.VMEM((2, REACH, across, deep), zone.dtype), pltpu.SemaphoreType.DMA((6,))],
    )(far_zone, far_scale, far_load)
    load, scale, zone = call(
        bring_box,
        (cells, cells, whole_zone),
        [in_hbm] * 3 + [anywhere],
        [pltpu.SemaphoreType.DMA((12,))],
    )(far_load, far_scale, far_zone, load_first)
    load_wide = exchange("wide", load_first, load_second)
    far_wide = exchange("wide", first, second)
    load_first, load_second = pack(MARGIN, [load], load_wide)
    load_narrow = exchange("narrow", load_first, load_second)
    sums, table = call(
        functools.partial(box_sums, box),
        (f32(8, 128), table_shape),
        [VMEM] * 3 + [anywhere] + [VMEM] * 2,
    )(zone, scale, load, load_first, diffusivity, decay)
    far_narrow = exchange("narrow", *pack(REACH, [scale, zone], far_wide))
    load_window, local, image, inverses = call(
        functools.partial(first_solve, box),
        (window, cells, f32(across, deep), f32(box.ey, box.ex, deep)),
        [VMEM] * 8 + [VMEM] * 2 + [VMEM] * N_TABLES,
        [spectral, middle],
        flops=4 * 10**9,
    )(load, *load_wide, *load_narrow, sums, zone, scale, diffusivity, decay, *tables)
    message = f32(REACH * across + count, deep)
    table, first, second = call(
        functools.partial(image_sums, box), (table_shape, message, message), [VMEM] * 9 + [VMEM]
    )(zone, scale, local, image, *far_wide, *far_narrow, table, diffusivity)
    own_table = table
    wide = exchange("wide", first, second)
    parts = (table, wide[0])
    if by_margins:
        parts += (two_away("wide", table), from_other_end("wide", table))
    to_long, to_across, *windows = call(
        functools.partial(side_weights, box),
        (window,) * 4,
        [VMEM] * 6 + [VMEM],
        flops=10**9,
    )(zone, scale, *far_wide, *far_narrow, diffusivity)
    to_deep, mass = call(
        functools.partial(deep_weights, box),
        (window,) * 2,
        [VMEM] * 2 + [VMEM] * 2,
        flops=10**9,
    )(*windows, diffusivity, decay)
    weights = (to_long, to_across, to_deep, mass)
    first, second, table = pack(REACH, [local], wide, parts, [to_long])
    narrow = exchange("narrow", first, second)
    if by_margins:
        table = call(join_rows, table_shape, [VMEM] * 2)(table, narrow[0])
        parts = (table, two_away("narrow", table))
    else:
        parts = (tell(own_table),)
    row, col = f32(across, deep), f32(long, deep)
    answers = call(
        functools.partial(coarse_corrections, len(parts)),
        f32(8, -(-count // 128) * 128),
        [VMEM] * len(parts),
        [scratch((count, -(-2 * count // 128) * 128))],
    )(*parts)
    iterate, first_row, second_row, first_col, second_col, result = call(
        functools.partial(second_solve, box),
        (cells, row, row, col, col, cells),
        [VMEM] * (12 + N_TABLES),
        [scratch(window.shape), spectral, middle, pltpu.SemaphoreType.DMA((long // 8,))],
        flops=4 * 10**9,
        out_spec=(VMEM,) * 5 + (anywhere,),
    )(local, *wide, *narrow, inverses, answers, *weights, load_window, *tables)
    narrow = exchange("narrow", first_col, second_col)
    wide = exchange("wide", first_row, second_row)
    rows, cols, inner = call(
        functools.partial(inner_residual, box),
        (f32(2, across, deep), f32(2, long, 8, deep), cells),
        [VMEM] * 6,
        [
            scratch((long + 2, box.cols, deep)),
            scratch((long, box.cols, deep)),
            pltpu.SemaphoreType.DMA((long // 8,)),
        ],
        flops=10**9,
        out_spec=(VMEM, VMEM, anywhere),
    )(load, iterate, *weights)
    residual = call(
        functools.partial(outer_residual, box),
        cells,
        [VMEM] * 9 + [anywhere],
        [
            scratch((2, across - 16, deep)),
            scratch((2, long, 8, deep)),
            pltpu.SemaphoreType.DMA((4,)),
        ],
        out_spec=anywhere,
        aliases={9: 0},
    )(iterate, *wide, *narrow, to_long, to_across, rows, cols, inner)
    return result, residual


def solution(mesh):
    split = P(("groups", "wide"), "narrow", None)
    return jax.shard_map(
        on_device,
        mesh=mesh,
        in_specs=(split, split, P(), P(), split),
        out_specs=(split, split),
        check_vma=False,
    )
```

```python
import functools

import jax
import jax.numpy as jnp
import ml_dtypes
import numpy as np
from jax import lax
from jax.experimental import pallas as pl
from jax.experimental.pallas import tpu as pltpu
from jax.sharding import PartitionSpec as P

MARGIN = 4
REACH = MARGIN + 1
EDGE = 8

cheb_center = 1.3
cheb_radius = 1.2
cheb_ratio = 1.3 / 1.2
rho_first = 1.0 / cheb_ratio
rho_second = 1.0 / (2.0 * cheb_ratio - rho_first)
gain = 2.0 * rho_second / cheb_radius

MEANS = range(4)
BOX_DIAGONAL, LONG_HIGH, LONG_LOW, ACROSS_HIGH, ACROSS_LOW, LOAD_SUM = range(4, 10)
IMAGE_SUM, FLOW_LONG_HIGH, FLOW_LONG_LOW, FLOW_ACROSS_HIGH, FLOW_ACROSS_LOW = range(16, 21)

VMEM = pl.BlockSpec(memory_space=pltpu.VMEM)


def sine_basis(length):
    indices = np.arange(1, length + 1)
    phases = indices[:, None] * indices[None, :] % (2 * (length + 1))
    table = np.sqrt(2.0 / (length + 1)) * np.sin(np.pi * phases / (length + 1))
    eigvals = 4.0 * np.sin(np.pi * indices / (2.0 * (length + 1))) ** 2
    return table.astype(np.float32), eigvals.astype(np.float32)


def call(body, out_shape, in_specs, scratch=(), flops=0, out_spec=None, aliases=None):
    return pl.pallas_call(
        body,
        out_shape=out_shape,
        in_specs=in_specs,
        out_specs=out_spec or jax.tree.map(lambda _: VMEM, out_shape),
        scratch_shapes=list(scratch),
        compiler_params=pltpu.CompilerParams(vmem_limit_bytes=30 * 2**20),
        cost_estimate=pl.CostEstimate(flops=flops, bytes_accessed=0, transcendentals=0),
        input_output_aliases=aliases or {},
    )


def f32(*shape):
    return jax.ShapeDtypeStruct(shape, jnp.float32)


class Box:
    def __init__(self, shape):
        self.long, self.across, self.deep = shape
        self.ex = self.long + 2 * MARGIN
        self.ey = self.across + 2 * MARGIN
        self.rows = self.long + 2 * REACH
        self.cols = self.across + 2 * EDGE
        self.flat = self.rows * self.cols


def pieces(values, count):
    parts = []
    for _ in range(count - 1):
        scaled = values * 65537.0
        part = scaled - (scaled - values)
        parts.append(part)
        values = values - part
    return parts + [values]


def products(count):
    return [(a, b) for a in range(count) for b in range(count - a)]


def left_table(table, depth, count):
    rows, cols = table.shape
    rest = np.zeros((rows, depth), np.float32)
    rest[:, :cols] = table
    parts = []
    for _ in range(count):
        part = rest.astype(ml_dtypes.bfloat16).astype(np.float32)
        parts.append(part)
        rest = rest - part
    return np.concatenate([parts[a] for a, _ in products(count)], axis=1)


def right_tables(table):
    rest, parts = table, []
    for _ in range(3):
        part = rest.astype(ml_dtypes.bfloat16).astype(np.float32)
        parts.append(part)
        rest = rest - part
    both = np.concatenate([parts[0], parts[1]], axis=1)
    return np.concatenate([both, both], axis=0), np.concatenate([parts[2], parts[0]], axis=0)


def padded(size):
    return -(-size // 8) * 8


FORWARD, BACKWARD = 2, 3


def tables_of(box):
    sine_x, eig_x = sine_basis(box.ex)
    sine_y, eig_y = sine_basis(box.ey)
    sine_z, eig_z = sine_basis(box.deep)
    in_order_of_steps = np.arange(box.ey).reshape(8, box.ey // 8).T.reshape(-1)
    from_y = sine_y[MARGIN : MARGIN + box.across]
    from_x = sine_x[MARGIN : MARGIN + box.long]
    spread_x = np.broadcast_to(eig_x[:, None], (box.ex, box.deep))
    spread_y = np.broadcast_to(eig_y[:, None], (box.ey, box.deep))
    main_z, rest_z = right_tables(sine_z)
    return [
        jnp.asarray(np.ascontiguousarray(t))
        for t in (
            left_table(sine_y[:, in_order_of_steps], padded(box.ey), FORWARD),
            left_table(sine_x, padded(box.ex), FORWARD),
            left_table(from_x, padded(box.ex), BACKWARD),
            left_table(from_y, padded(box.ey), BACKWARD),
            main_z,
            rest_z,
            spread_x,
            spread_y,
            eig_z[None, :],
        )
    ]


N_TABLES = 9


def one_pass(left, right):
    return lax.dot_general(
        left,
        right,
        (((1,), (0,)), ((), ())),
        precision=lax.Precision.DEFAULT,
        preferred_element_type=jnp.float32,
    )


def dot_left(table, values, count):
    parts = pieces(values, count)
    return one_pass(table, jnp.concatenate([parts[b] for _, b in products(count)], axis=0))


def dot_right(values, main, rest, count):
    deep = values.shape[1]
    parts = pieces(values, count)
    total = one_pass(jnp.concatenate(parts[:2], axis=1), main)
    result = total[:, :deep] + total[:, deep:]
    if count == 3:
        result = result + one_pass(jnp.concatenate([parts[0], parts[2]], axis=1), rest)
    return result


def with_rows(values, rows):
    if values.shape[0] == rows:
        return values
    blank = jnp.zeros((rows - values.shape[0],) + values.shape[1:], values.dtype)
    return jnp.concatenate([values, blank], axis=0)


FORWARD_ROWS, COLS_ABREAST, BACKWARD_ROWS = 24, 40, 32


def fitting(size, wanted):
    return max(part for part in range(8, wanted + 1, 8) if size % part == 0)


def beside(values):
    return jnp.concatenate(values, axis=1)


def apart(values, lanes):
    return [values[:, start : start + lanes] for start in range(0, values.shape[1], lanes)]


def box_solve(box, source, divided, tables, row_mask, col_mask, spectral, middle, emit):
    into_y, into_x, from_x, from_y, main_z, rest_z = tables[:6]
    deep = box.deep
    deep_x, deep_y = padded(box.ex), padded(box.ey)
    into_y, into_x = into_y[...], into_x[...]
    if col_mask is not None:
        mask = jnp.concatenate([col_mask] * len(products(FORWARD)), axis=1)
        into_y = into_y * mask
        mask = jnp.concatenate([row_mask] * len(products(FORWARD)), axis=1)
        into_x = into_x * mask
    from_x, from_y, main_z, rest_z = from_x[...], from_y[...], main_z[...], rest_z[...]
    spectral_flat = spectral.reshape(box.ey * deep_x, deep)
    middle_flat = middle.reshape(box.long * deep_y, deep)
    if deep_x > box.ex:
        spectral[:, box.ex :, :] = jnp.zeros((box.ey, deep_x - box.ex, deep), jnp.float32)
    if deep_y > box.ey:
        middle[:, box.ey :, :] = jnp.zeros((box.long, deep_y - box.ey, deep), jnp.float32)
    step = fitting(box.ex, FORWARD_ROWS)
    for start in range(0, box.ex, step):
        block = jnp.concatenate([source(row) for row in range(start, start + step, 8)], axis=0)
        block = dot_right(block.reshape(step * box.ey, deep), main_z, rest_z, FORWARD)
        block = block.reshape(step, box.ey, deep)
        wide = beside([block[row] for row in range(step)])
        wide = dot_left(into_y, with_rows(wide, deep_y), FORWARD)
        for row, values in enumerate(apart(wide, deep)):
            spectral_flat[pl.ds(start + row, box.ey, stride=deep_x), :] = values
    step = fitting(box.ey, COLS_ABREAST)
    for start in range(0, box.ey, step):
        wide = beside([spectral[col] for col in range(start, start + step)])
        wide = apart(dot_left(into_x, wide, FORWARD), deep)
        wide = beside([divided(values, start + part) for part, values in enumerate(wide)])
        wide = dot_left(from_x, with_rows(wide, deep_x), BACKWARD)
        for part, values in enumerate(apart(wide, deep)):
            middle_flat[pl.ds(start + part, box.long, stride=deep_y), :] = values
    step = fitting(box.long, BACKWARD_ROWS)
    for start in range(0, box.long, step):
        wide = beside([middle[row] for row in range(start, start + step)])
        parts = apart(dot_left(from_y, wide, BACKWARD), deep)
        values = dot_right(jnp.concatenate(parts, axis=0), main_z, rest_z, BACKWARD)
        for row in range(0, step, 8):
            emit(start + row, values[row * box.across : (row + 8) * box.across])


def position():
    long_pos, across_pos = lax.axis_index("wide"), lax.axis_index("narrow")
    return long_pos, across_pos, lax.axis_size("wide"), lax.axis_size("narrow")


def as_float(flag):
    return jnp.where(flag, jnp.float32(1.0), jnp.float32(0.0))


def is_even(axis):
    return lax.rem(lax.axis_index(axis), 2) == 0


class Sides:
    def __init__(self, axis, first, second):
        position = lax.axis_index(axis)
        self.even = is_even(axis)
        self.has_low = as_float(position > 0)
        self.has_high = as_float(position < lax.axis_size(axis) - 1)
        self.first, self.second = first, second

    def low(self, *index):
        return jnp.where(self.even, self.second[index], self.first[index]) * self.has_low

    def high(self, *index):
        return jnp.where(self.even, self.first[index], self.second[index]) * self.has_high


def in_order(even, up, down):
    return jnp.where(even, up, down), jnp.where(even, down, up)


def row_of(stride, col, count, first=0):
    return pl.ds(first * stride + col, count, stride=stride)


def pack_columns(box, fields, wide_sides, wide, first, second):
    corner = len(fields) * wide * box.long
    even = is_even("narrow")
    place = 0
    for field, sides in zip(fields, wide_sides):
        for step in range(wide):
            cols = (box.across - wide + step, step)
            values = [field[row_of(box.across, col, box.long), :] for col in cols]
            low = [sides.low(row_of(box.across, col, wide), slice(None)) for col in cols]
            high = [sides.high(row_of(box.across, col, wide), slice(None)) for col in cols]
            at = corner + 2 * REACH * place
            for start, parts in ((place * box.long, values), (at, low), (at + REACH, high)):
                parts = in_order(even, *(part.astype(jnp.float32) for part in parts))
                size = parts[0].shape[0]
                first[start : start + size, :], second[start : start + size, :] = parts
            place += 1


def message_rows(box, count):
    return -(-(count * (box.long + 2 * REACH)) // 8) * 8


def pack_fields(box, wide, fields, tables, after, *refs):
    own, (low, high), refs = refs[:fields], refs[fields : fields + 2], refs[fields + 2 :]
    parts, (first, second, *table) = refs[:tables], refs[tables + after :]
    size = wide * box.across
    flat = [field.reshape(box.long * box.across, box.deep) for field in own]
    low = low.reshape(low.size // box.deep, box.deep)
    high = high.reshape(high.size // box.deep, box.deep)
    sides = [
        Sides("wide", *(ref.at[index * size : (index + 1) * size] for ref in (low, high)))
        for index in range(fields)
    ]
    pack_columns(box, flat, sides, wide, first, second)
    if tables:
        known = last_rows_merged(parts, table[0].shape[0])
        table[0][...] = known
        first[first.shape[0] - known.shape[0] :, :] = known
        second[second.shape[0] - known.shape[0] :, :] = known


def bring_edges(box, zone, scale, load, load_first, load_second, first, second, staged, sems):
    even = is_even("wide")

    def edges(wide):
        up, down = box.long - wide, 0
        return [pl.ds(jnp.where(even, *pair), wide) for pair in ((up, down), (down, up))]

    copies = [
        (zone.at[edges(REACH)[0]], staged.at[0]),
        (zone.at[edges(REACH)[1]], staged.at[1]),
        (load.at[edges(MARGIN)[0]], load_first),
        (load.at[edges(MARGIN)[1]], load_second),
        (scale.at[edges(REACH)[0]], first.at[:REACH]),
        (scale.at[edges(REACH)[1]], second.at[:REACH]),
    ]
    copies = [
        pltpu.make_async_copy(source, target, sems.at[index])
        for index, (source, target) in enumerate(copies)
    ]
    for copy in copies:
        copy.start()
    for copy in copies[:2]:
        copy.wait()
    first[REACH:] = staged[0].astype(jnp.float32)
    second[REACH:] = staged[1].astype(jnp.float32)
    for copy in copies[2:]:
        copy.wait()


def bring_box(load, scale, zone, after, own_load, own_scale, own_zone, sems):
    del after
    parts = 4
    size = own_load.shape[0] // parts
    copies = []
    for part in range(parts):
        rows = slice(part * size, (part + 1) * size)
        for source, target in ((load, own_load), (scale, own_scale), (zone, own_zone)):
            copies.append(
                pltpu.make_async_copy(source.at[rows], target.at[rows], sems.at[len(copies)])
            )
            copies[-1].start()
    for copy in copies:
        copy.wait()


def fill_window(box, window, own, wide_sides, narrow_sides, wide, place, total, add=None):
    flat = window.reshape(box.flat, box.deep)
    nothing = jnp.zeros((box.rows, EDGE, box.deep), jnp.float32)
    window[:, :EDGE, :] = nothing
    window[:, EDGE + box.across :, :] = nothing
    if add is None:
        add = lambda values, row_side, col_side: values
    inner = slice(EDGE, EDGE + box.across)
    first, last = REACH, REACH + box.long
    if wide < REACH:
        blank = jnp.zeros((1, box.across, box.deep), jnp.float32)
        window[0:1, inner, :] = blank
        window[box.rows - 1 :, inner, :] = blank
    window[first:last, inner, :] = add(own[...].astype(jnp.float32), 0, 0)
    window[first - wide : first, inner, :] = add(wide_sides.low(Ellipsis), -1, 0)
    window[last : last + wide, inner, :] = add(wide_sides.high(Ellipsis), 1, 0)
    corner = total * box.long
    for step in range(wide):
        for source, col, side in (
            (narrow_sides.low, EDGE - wide + step, -1),
            (narrow_sides.high, EDGE + box.across + step, 1),
        ):
            for start, size, row, row_side in (
                ((place + step) * box.long, box.long, first, 0),
                (corner + 2 * REACH * (place + step), wide, first - wide, -1),
                (corner + 2 * REACH * (place + step) + REACH, wide, last, 1),
            ):
                values = source(slice(start, start + size), slice(None))
                flat[row_of(box.cols, col, size, row), :] = add(values, row_side, side)


def some_cols(box, ref, row, step):
    stride = box.ey // 8
    return ref[row, pl.ds(EDGE - MARGIN + step, 8, stride=stride), :]


def negative_image(box, window, row, at, x, flow_before, weights):
    to_long, to_across, to_deep, mass = weights
    steps = range(box.ey // 8)
    x_next = [some_cols(box, window, row + 1, step) for step in range(-1, len(steps) + 1)]
    flow_long = [
        some_cols(box, to_long, at, step) * (x_next[step + 1] - x[step + 1]) for step in steps
    ]
    flow_across = [
        some_cols(box, to_across, at, step) * (x[step + 2] - x[step + 1])
        for step in range(-1, len(steps))
    ]
    totals = []
    for step in steps:
        here = x[step + 1]
        lanes = here.shape[1]
        flow_deep = some_cols(box, to_deep, at, step) * (pltpu.roll(here, lanes - 1, 1) - here)
        total = flow_long[step] - flow_before[step] - some_cols(box, mass, at, step) * here
        total = total + (flow_across[step + 1] - flow_across[step])
        totals.append(total + (flow_deep - pltpu.roll(flow_deep, 1, 1)))
    return totals, x_next, flow_long


def in_steps(box, refs, rows):
    return jnp.stack(
        [
            jnp.concatenate([some_cols(box, ref, row, step) for step in range(box.ey // 8)], axis=0)
            for ref, row in zip(refs, rows)
        ]
    )


def looked_up(labels, values):
    return jnp.where(labels == 0, values[0], jnp.where(labels == 1, values[1], values[2]))


def at_own_row(line, shape):
    long_pos, across_pos, _, across_count = position()
    rows = lax.broadcasted_iota(jnp.int32, shape, 0)
    own = rows == long_pos * across_count + across_pos
    return jnp.where(own, line[:1], jnp.zeros(shape, jnp.float32))


def merged(table, *others):
    for other in others:
        table = jnp.where(table != 0.0, table, other)
    return table


def last_rows_merged(refs, count):
    return merged(*(ref[ref.shape[0] - count :, :] for ref in refs))


def join_rows(table, message, out):
    out[...] = last_rows_merged((table, message), out.shape[0])


def line_of(numbers, shape):
    count = -(-len(numbers) // 8) * 8
    rows = lax.broadcasted_iota(jnp.int32, (count, shape[1]), 0)
    lanes = lax.broadcasted_iota(jnp.int32, (count, shape[1]), 1)
    stacked = jnp.zeros((count, shape[1]), jnp.float32)
    place = jnp.zeros((count, shape[1]), jnp.bool_)
    for row, (index, values) in enumerate(numbers):
        stacked = jnp.where(rows == row, values, stacked)
        place = place | ((rows == row) & (lanes == index))
    sums = jnp.sum(stacked, axis=1, keepdims=True)
    line = jnp.sum(jnp.where(place, sums, jnp.zeros_like(stacked)), axis=0, keepdims=True)
    return jnp.broadcast_to(line, shape)


def box_sums(box, zone, scale, load, after, diffusivity, decay, out, table):
    del after
    nothing = jnp.zeros((box.across, box.deep), jnp.float32)
    half = [[0.5 * diffusivity[z : z + 1, d : d + 1] for z in range(3)] for d in range(3)]
    rates = [decay[0:1, z : z + 1] for z in range(3)]

    def halves(row):
        labels, factor = zone[row], scale[row]
        return [looked_up(labels, half[d]) * factor for d in range(3)] + [looked_up(labels, rates)]

    sums = [nothing] * 5
    for row in range(box.long):
        sums = [total + more for total, more in zip(sums, halves(row) + [load[row]])]

    def total(values):
        return jnp.sum(values, axis=0, keepdims=True)

    cells = box.long * box.across * box.deep
    numbers = [(index, total(sums[index]) * (2.0 / cells)) for index in range(3)]
    mass = total(sums[3])
    numbers += [(3, mass / cells)]
    lane = lax.broadcasted_iota(jnp.int32, (1, box.deep), 1)
    ends = jnp.where((lane == 0) | (lane == box.deep - 1), total(sums[2]), 0.0)
    numbers += [
        (BOX_DIAGONAL, mass + ends),
        (LONG_HIGH, total(halves(box.long - 1)[0])),
        (LONG_LOW, total(halves(0)[0])),
        (ACROSS_HIGH, sums[1][box.across - 1 :]),
        (ACROSS_LOW, sums[1][:1]),
        (LOAD_SUM, total(sums[4])),
    ]
    line = line_of(numbers, out.shape)
    out[...] = line
    table[...] = at_own_row(line, table.shape)


def means_of(ref):
    return [ref[0:1, index : index + 1] for index in range(4)]


def first_solve(box, load, low, high, left, right, means, zone, scale, diffusivity, decay, *rest):
    tables = rest[:N_TABLES]
    window, local, image, inverses, spectral, middle = rest[N_TABLES:]
    spread_x, spread_y, eig_z = tables[6:]
    means = means_of(means)
    base = means[3] + means[0] * spread_x[...] + means[2] * eig_z[...]

    def divided(values, col):
        divisor = base + means[1] * spread_y[col : col + 1, :]
        inverse = pl.reciprocal(divisor, approx=True)
        for _ in range(2):
            inverse = inverse * (2.0 - divisor * inverse)
        inverses[col] = inverse
        return values * inverse

    half = [0.5 * diffusivity[z : z + 1, 2:3] for z in range(3)]
    rates = [decay[0:1, z : z + 1] for z in range(3)]
    lane = lax.broadcasted_iota(jnp.int32, (box.across, box.deep), 1)
    ends = jnp.where((lane == 0) | (lane == box.deep - 1), jnp.float32(1.0), jnp.float32(0.0))
    image[...] = jnp.zeros((box.across, box.deep), jnp.float32)
    wide_sides, narrow_sides = Sides("wide", low, high), Sides("narrow", left, right)
    fill_window(box, window, load, wide_sides, narrow_sides, MARGIN, 0, MARGIN)

    def emit(start, values):
        values = values * (1.0 / cheb_center)
        values = values.reshape(8, box.across, box.deep)
        local[start : start + 8] = values
        total = image[...]
        for row in range(8):
            labels = zone[start + row]
            mass = looked_up(labels, rates) + looked_up(labels, half) * scale[start + row] * ends
            total = total + mass * values[row]
        image[...] = total

    box_solve(
        box,
        lambda start: in_steps(box, [window] * 8, range(1 + start, 9 + start)),
        divided,
        tables,
        None,
        None,
        spectral,
        middle,
        emit,
    )


def side_weights(
    box, zone, scale, low, high, left, right, diffusivity, to_long, to_across, zone_window,
    scale_window
):
    for index, (window, own) in enumerate(((scale_window, scale), (zone_window, zone))):
        start = index * REACH
        wide_sides = Sides("wide", *(ref.at[start : start + REACH] for ref in (low, high)))
        narrow_sides = Sides("narrow", left, right)
        fill_window(box, window, own, wide_sides, narrow_sides, REACH, start, 2 * REACH)
    half = [[0.5 * diffusivity[z : z + 1, d : d + 1] for z in range(3)] for d in range(2)]

    def one_row(row, before):
        labels, factor = zone_window[row], scale_window[row]
        now = [looked_up(labels, half[d]) * factor for d in range(2)]
        to_across[row] = now[1] + pltpu.roll(now[1], box.cols - 1, 0)
        to_long[max(row - 1, 0)] = before + now[0]
        return now[0]

    before = jnp.zeros((box.cols, box.deep), jnp.float32)
    for row in range(box.rows):
        before = one_row(row, before)
    to_long[box.rows - 1] = before


def deep_weights(box, zone_window, scale_window, diffusivity, decay, to_deep, mass):
    half = [0.5 * diffusivity[z : z + 1, 2:3] for z in range(3)]
    rates = [decay[0:1, z : z + 1] for z in range(3)]
    lane = lax.broadcasted_iota(jnp.int32, (box.cols, box.deep), 1)
    ends = jnp.where((lane == 0) | (lane == box.deep - 1), jnp.float32(1.0), jnp.float32(0.0))
    not_last = jnp.where(lane == box.deep - 1, jnp.float32(0.0), jnp.float32(1.0))

    def one_row(row):
        labels = zone_window[row]
        now = looked_up(labels, half) * scale_window[row]
        to_deep[row] = (now + pltpu.roll(now, box.deep - 1, 1)) * not_last
        mass[row] = looked_up(labels, rates) + now * ends

    for row in range(box.rows):
        one_row(row)


def image_sums(
    box, zone, scale, local, image, low, high, left, right, table, diffusivity, out, up, down
):
    half = [[0.5 * diffusivity[z : z + 1, d : d + 1] for z in range(3)] for d in range(3)]
    shape = (box.long * box.across, box.deep)
    zone_flat, scale_flat, local_flat = zone.reshape(shape), scale.reshape(shape), local.reshape(shape)
    last_col = row_of(box.across, box.across - 1, box.long)
    first_col = row_of(box.across, 0, box.long)

    wide_sides, narrow_sides = Sides("wide", low, high), Sides("narrow", left, right)

    def side(source, place):
        return source(slice(place * box.long, (place + 1) * box.long), slice(None))

    above, below = wide_sides.high, wide_sides.low
    faces = [
        (0, zone[box.long - 1], scale[box.long - 1], local[box.long - 1], above(REACH), above(0)),
        (0, zone[0], scale[0], local[0], below(2 * REACH - 1), below(REACH - 1)),
        (
            1,
            zone_flat[last_col, :],
            scale_flat[last_col, :],
            local_flat[last_col, :],
            side(narrow_sides.high, REACH),
            side(narrow_sides.high, 0),
        ),
        (
            1,
            zone_flat[first_col, :],
            scale_flat[first_col, :],
            local_flat[first_col, :],
            side(narrow_sides.low, 2 * REACH - 1),
            side(narrow_sides.low, REACH - 1),
        ),
    ]
    flows = []
    for direction, labels, factor, values, far_labels, far_factor in faces:
        weight = looked_up(labels, half[direction]) * factor
        weight = weight + looked_up(far_labels, half[direction]) * far_factor
        flows.append(jnp.sum(weight * values, axis=0, keepdims=True))
    long_pos, across_pos, long_count, across_count = position()
    numbers = [
        (IMAGE_SUM, jnp.sum(image[...], axis=0, keepdims=True) + sum(flows)),
        (FLOW_LONG_HIGH, flows[0] * as_float(long_pos < long_count - 1)),
        (FLOW_LONG_LOW, flows[1] * as_float(long_pos > 0)),
        (FLOW_ACROSS_HIGH, flows[2] * as_float(across_pos < across_count - 1)),
        (FLOW_ACROSS_LOW, flows[3] * as_float(across_pos > 0)),
    ]
    known = table[...] + at_own_row(line_of(numbers, (8, out.shape[1])), out.shape)
    out[...] = known
    edge = REACH * box.across
    even = is_even("wide")
    for target, pair in ((up, (box.long - REACH, 0)), (down, (0, box.long - REACH))):
        target[:edge] = local[pl.ds(jnp.where(even, *pair), REACH)].reshape(edge, box.deep)
        target[edge:] = known


def column(values, index):
    return values[:, index : index + 1]


def uncoupled_groups(count, across):
    places = np.arange(count)
    long_step = np.abs(places[:, None] // across - places[None, :] // across)
    across_step = np.abs(places[:, None] % across - places[None, :] % across)
    coupled = long_step + across_step == 1
    left = list(range(count))
    groups = []
    while left:
        group = []
        for place in sorted(left, key=lambda p: (coupled[p][left].sum(), p)):
            if not coupled[place][group].any():
                group.append(place)
        left = [place for place in left if place not in group]
        for place in group:
            beside = [other for other in left if coupled[place][other]]
            for other in beside:
                coupled[other][beside] = True
                coupled[other][other] = False
        groups.append(group)
    return groups


def coarse_inverse(numbers, work):
    count, width = work.shape
    across = lax.axis_size("narrow")
    beyond = pltpu.roll(numbers, count - across, 0)
    beside = pltpu.roll(numbers, count - 1, 0)
    before = pltpu.roll(numbers, across, 0)
    ahead = pltpu.roll(numbers, 1, 0)
    place = lax.broadcasted_iota(jnp.int32, (count, 1), 0)
    across_pos = lax.rem(place, across)
    nothing = jnp.zeros((count, 1), jnp.float32)
    couplings = []
    diagonal = column(numbers, BOX_DIAGONAL)
    for own, other, there, inside in (
        (LONG_HIGH, LONG_LOW, beyond, place < count - across),
        (LONG_LOW, LONG_HIGH, before, place >= across),
        (ACROSS_HIGH, ACROSS_LOW, beside, across_pos < across - 1),
        (ACROSS_LOW, ACROSS_HIGH, ahead, across_pos > 0),
    ):
        shared = jnp.where(inside, column(there, other), nothing)
        diagonal = diagonal + column(numbers, own) + shared
        couplings.append(jnp.where(inside, column(numbers, own) + shared, nothing))
    rows = lax.broadcasted_iota(jnp.int32, (count, width), 0)
    cols = lax.broadcasted_iota(jnp.int32, (count, width), 1)
    blank = jnp.zeros((count, width), jnp.float32)
    matrix = jnp.where(cols == rows, diagonal, blank)
    for shift, coupling in zip((across, -across, 1, -1), couplings):
        matrix = matrix - jnp.where((cols == rows + shift) & (cols < count), coupling, blank)
    matrix = jnp.where(cols == rows + count, jnp.ones((count, 1), jnp.float32), matrix)
    if count <= 16:
        for group in uncoupled_groups(count, across):
            rest = matrix
            for step in group:
                pivot_row = matrix[step : step + 1, :] / matrix[step : step + 1, step : step + 1]
                rest = rest - matrix[:, step : step + 1] * pivot_row
                rest = jnp.where(rows == step, pivot_row, rest)
            matrix = rest
        return pltpu.roll(matrix, width - count, 1)
    work[...] = matrix

    def eliminate(step, _):
        values = work[...]
        pivot_row = work[pl.ds(step, 1), :]
        at_step = cols == step
        factors = jnp.sum(jnp.where(at_step, values, blank), axis=1, keepdims=True)
        pivot = jnp.sum(jnp.where(at_step[:1], pivot_row, blank[:1]), axis=1, keepdims=True)
        pivot_row = pivot_row / pivot
        work[...] = jnp.where(rows == step, pivot_row, values - factors * pivot_row)
        return 0

    lax.fori_loop(0, count, eliminate, 0)
    values = work[...]
    if count % 128:
        return pltpu.roll(values, width - count, 1)
    return values[:, count : 2 * count]


def answer(inverse, sums):
    return jnp.sum(inverse * sums, axis=0, keepdims=True)


def at_box(values, row_side, col_side):
    long_pos, across_pos, long_count, across_count = position()
    there_long, there_across = long_pos + row_side, across_pos + col_side
    inside = (
        (there_long >= 0)
        & (there_long < long_count)
        & (there_across >= 0)
        & (there_across < across_count)
    )
    lanes = lax.broadcasted_iota(jnp.int32, values.shape, 1)
    wanted = (lanes == there_long * across_count + there_across) & inside
    return jnp.sum(jnp.where(wanted, values, jnp.zeros_like(values)), axis=1, keepdims=True)


def coarse_corrections(table_parts, work):
    count = work.shape[0]
    numbers = last_rows_merged(table_parts, count)
    across_count = lax.axis_size("narrow")
    inverse = coarse_inverse(numbers, work)
    sums = column(numbers, IMAGE_SUM)
    sums = sums - column(pltpu.roll(numbers, count - across_count, 0), FLOW_LONG_LOW)
    sums = sums - column(pltpu.roll(numbers, across_count, 0), FLOW_LONG_HIGH)
    sums = sums - column(pltpu.roll(numbers, count - 1, 0), FLOW_ACROSS_LOW)
    sums = sums - column(pltpu.roll(numbers, 1, 0), FLOW_ACROSS_HIGH)
    load_sums = column(numbers, LOAD_SUM)
    sums = load_sums * (1.0 - 1.0 / cheb_center) - sums
    return answer(inverse, load_sums) * (1.0 / cheb_center), answer(inverse, sums) * gain


def second_solve(box, parts, local, low, high, left, right, inverses, *rest):
    table_parts, rest = rest[:parts], rest[parts:]
    to_long, to_across, to_deep, mass, load_window = rest[:5]
    tables = rest[5 : 5 + N_TABLES]
    iterate, top, bottom, last_col, first_col, out = rest[5 + N_TABLES : 11 + N_TABLES]
    window, spectral, middle, sems, work = rest[11 + N_TABLES :]
    long_pos, across_pos, long_count, across_count = position()
    coarse, second_coarse = coarse_corrections(table_parts, work)
    own_coarse = at_box(coarse, 0, 0)
    shifts = {
        (row_side, col_side): at_box(coarse, row_side, col_side) - own_coarse
        for row_side in (-1, 0, 1)
        for col_side in (-1, 0, 1)
    }

    def add(values, row_side, col_side):
        if row_side == 0 and col_side == 0:
            return values
        shift = shifts[row_side, col_side]
        if values.ndim == 3:
            shift = shift.reshape(1, 1, 1)
        return values + shift

    edge = REACH * box.across
    low, high = (
        ref.at[:edge].reshape(REACH, box.across, box.deep) for ref in (low, high)
    )
    wide_sides, narrow_sides = Sides("wide", low, high), Sides("narrow", left, right)
    fill_window(box, window, local, wide_sides, narrow_sides, REACH, 0, REACH, add)
    weights = (to_long, to_across, to_deep, mass)

    steps = range(box.ey // 8)
    x = [some_cols(box, window, 1, step) for step in range(-1, len(steps) + 1)]
    flow = [
        some_cols(box, to_long, 0, step) * (x[step + 1] - some_cols(box, window, 0, step))
        for step in steps
    ]
    state = [x, flow]

    def divided(values, col):
        return values * inverses[col]

    def residual(start_row):
        rows = []
        for row in range(start_row + 1, start_row + 9):
            image, *state[:] = negative_image(box, window, row, row, *state, weights)
            image = [
                some_cols(box, load_window, row, step)
                + (image[step] - some_cols(box, mass, row, step) * own_coarse)
                for step in steps
            ]
            rows.append(jnp.concatenate(image, axis=0))
        return jnp.stack(rows)

    inner = slice(EDGE, EDGE + box.across)
    first = REACH
    row_ids = lax.broadcasted_iota(jnp.int32, (1, padded(box.ex)), 1)
    col_ids = lax.broadcasted_iota(jnp.int32, (1, padded(box.ey)), 1)
    col_ids = (col_ids & 7) * (box.ey // 8) + lax.shift_right_logical(col_ids, 3)
    row_mask = jnp.where(row_ids < MARGIN, as_float(long_pos > 0), 1.0)
    row_mask = jnp.where(row_ids >= MARGIN + box.long, as_float(long_pos < long_count - 1), row_mask)
    col_mask = jnp.where(col_ids < MARGIN, as_float(across_pos > 0), 1.0)
    col_mask = jnp.where(
        col_ids >= MARGIN + box.across, as_float(across_pos < across_count - 1), col_mask
    )
    keep = 1.0 + rho_second * rho_first
    shift = (at_box(second_coarse, 0, 0) + keep * own_coarse).reshape(1, 1, 1)
    copies = []

    def emit(start, values):
        rows = values.reshape(8, box.across, box.deep)
        before = window[first + start : first + start + 8, inner, :]
        iterate[start : start + 8] = keep * before + (gain * rows + shift)
        copies.append(
            pltpu.make_async_copy(
                iterate.at[start : start + 8], out.at[start : start + 8], sems.at[len(copies)]
            )
        )
        copies[-1].start()

    box_solve(
        box, residual, divided, tables, row_mask, col_mask, spectral, middle, emit
    )
    rows = in_order(is_even("wide"), iterate[box.long - 1], iterate[0])
    top[...], bottom[...] = rows
    flat = iterate.reshape(box.long * box.across, box.deep)
    cols = [flat[row_of(box.across, col, box.long), :] for col in (box.across - 1, 0)]
    last_col[...], first_col[...] = in_order(is_even("narrow"), *cols)
    for copy in copies:
        copy.wait()


def inner_residual(
    box, load, iterate, to_long, to_across, to_deep, mass, rows, cols, out, window, result, sems
):
    inner = slice(EDGE, EDGE + box.across)
    flat = window.reshape((box.long + 2) * box.cols, box.deep)
    iterate_flat = iterate.reshape(box.long * box.across, box.deep)
    blank = jnp.zeros((box.long + 2, EDGE, box.deep), jnp.float32)
    window[:, :EDGE, :] = blank
    window[:, EDGE + box.across :, :] = blank
    window[1 : 1 + box.long, inner, :] = iterate[...]
    window[0, inner, :] = iterate[0]
    window[1 + box.long, inner, :] = iterate[box.long - 1]
    for col, place in ((0, EDGE - 1), (box.across - 1, EDGE + box.across)):
        values = iterate_flat[row_of(box.across, col, box.long), :]
        flat[row_of(box.cols, place, box.long, 1), :] = values
    weights = (to_long, to_across, to_deep, mass)
    steps = range(box.ey // 8)
    x = [some_cols(box, window, 1, step) for step in range(-1, len(steps) + 1)]
    flow = [jnp.zeros((8, box.deep), jnp.float32) for _ in steps]
    middle = slice(8, box.across - 8)
    copies = []
    for row in range(box.long):
        image, x, flow = negative_image(box, window, row + 1, REACH + row, x, flow, weights)
        for step in steps:
            place = pl.ds(EDGE - MARGIN + step, 8, stride=box.ey // 8)
            result[row, place, :] = image[step]
        values = load[row] + result[row, inner]
        result[row, inner] = values
        cols[0, row] = values[:8]
        cols[1, row] = values[box.across - 8 :]
        if row == 0:
            rows[0] = values
        if row == box.long - 1:
            rows[1] = values
        if row % 8 == 7:
            part = slice(row - 7, row + 1)
            copy = pltpu.make_async_copy(
                result.at[part, EDGE + 8 : EDGE + box.across - 8],
                out.at[part, middle],
                sems.at[row // 8],
            )
            copy.start()
            copies.append(copy)
    for copy in copies:
        copy.wait()


def outer_residual(
    box, iterate, low, high, left, right, to_long, to_across, rows, cols, inner_out, out,
    row_part, col_part, sems
):
    del inner_out
    inner = slice(EDGE, EDGE + box.across)
    middle = slice(8, box.across - 8)
    wide_sides, narrow_sides = Sides("wide", low, high), Sides("narrow", left, right)
    last = box.long - 1
    iterate_flat = iterate.reshape(box.long * box.across, box.deep)
    across_flat = to_across.reshape(box.flat, box.deep)
    below = to_long[REACH - 1, inner] * (wide_sides.low(Ellipsis) - iterate[0])
    above = to_long[REACH + last, inner] * (wide_sides.high(Ellipsis) - iterate[last])
    row_part[0] = (rows[0] + below)[middle]
    row_part[1] = (rows[1] + above)[middle]
    copies = [
        pltpu.make_async_copy(row_part.at[0], out.at[0, middle], sems.at[0]),
        pltpu.make_async_copy(row_part.at[1], out.at[last, middle], sems.at[1]),
    ]
    for copy in copies:
        copy.start()
    col_part[...] = cols[...]
    flat = col_part.reshape(2 * box.long * 8, box.deep)
    for side, (from_side, col, face, tile) in enumerate(
        (
            (narrow_sides.low, 0, EDGE - 1, slice(0, 8)),
            (narrow_sides.high, box.across - 1, EDGE + box.across - 1, slice(box.across - 8, None)),
        )
    ):
        weight = across_flat[row_of(box.cols, face, box.long, REACH), :]
        own = iterate_flat[row_of(box.across, col, box.long), :]
        place = pl.ds(side * box.long * 8 + side * 7, box.long, stride=8)
        flat[place, :] = flat[place, :] + weight * (from_side(Ellipsis) - own)
        col_part[side, 0] = col_part[side, 0] + below[tile]
        col_part[side, last] = col_part[side, last] + above[tile]
        first_col = side * (box.across - 8)
        copy = pltpu.make_async_copy(
            col_part.at[side], out.at[:, first_col : first_col + 8], sems.at[2 + side]
        )
        copy.start()
        copies.append(copy)
    for copy in copies:
        copy.wait()


def swaps(axis):
    sizes = (lax.axis_size("wide"), lax.axis_size("narrow"))
    along = ("wide", "narrow").index(axis)
    size, beside = sizes[along], sizes[1 - along]

    def number(place, other_place):
        pair = (place, other_place) if along == 0 else (other_place, place)
        return pair[0] * sizes[1] + pair[1]

    ways = []
    for way in range(2):
        pairs = []
        for place in range(size):
            for other_place in range(beside):
                partner = place + 1 if place % 2 == way else place - 1
                there = other_place
                if not 0 <= partner < size:
                    partner = place
                    there = other_place ^ 1 if beside % 2 == 0 else other_place
                pairs.append((number(place, other_place), number(partner, there)))
        ways.append(pairs)
    return ways


def exchange(axis, first, second):
    ways = swaps(axis)
    axes = ("wide", "narrow")
    return lax.ppermute(first, axes, ways[0]), lax.ppermute(second, axes, ways[1])


def from_other_end(axis, table):
    size = lax.axis_size(axis)
    return lax.ppermute(table, axis, [(i, size - 1 - i) for i in range(size)])


def two_away(axis, table):
    size = lax.axis_size(axis)
    return lax.ppermute(table, axis, [(i, (i + 2) % size) for i in range(size)])


def tell(table):
    count = table.shape[0]
    long_pos, across_pos, _, across_count = position()
    own = lax.dynamic_slice_in_dim(table, long_pos * across_count + across_pos, 1, axis=0)
    line = jnp.broadcast_to(own, (count, 1, 128))
    told = lax.all_to_all(line, ("wide", "narrow"), split_axis=0, concat_axis=0, tiled=True)
    return told.reshape(count, 128)


def on_device(zone, scale, diffusivity, decay, load):
    box = Box(load.shape)
    long, across, deep = load.shape
    count = lax.axis_size("wide") * lax.axis_size("narrow")
    by_margins = lax.axis_size("wide") == 4 and lax.axis_size("narrow") == 4
    tables = tables_of(box)
    decay = decay.reshape(1, -1)
    cells = f32(long, across, deep)
    whole_zone = jax.ShapeDtypeStruct(cells.shape, zone.dtype)
    window = f32(box.rows, box.cols, deep)
    table_shape = f32(count, 128)
    anywhere = pl.BlockSpec(memory_space=pl.ANY)
    in_hbm = pl.BlockSpec(memory_space=pltpu.HBM)

    def scratch(shape):
        return pltpu.VMEM(shape, jnp.float32)

    def pinned(field):
        return pltpu.with_memory_space_constraint(field, pltpu.HBM)

    spectral = scratch((box.ey, padded(box.ex), deep))
    middle = scratch((long, padded(box.ey), deep))

    def pack(wide, fields, sides, parts=(), after=()):
        rows = message_rows(box, wide * len(fields)) + (count if parts else 0)
        message = f32(rows, deep)
        body = functools.partial(pack_fields, box, wide, len(fields), len(parts), len(after))
        return call(
            body,
            (message, message) + ((table_shape,) if parts else ()),
            [VMEM] * (len(fields) + 2 + len(parts)) + [anywhere] * len(after),
        )(*fields, *sides, *parts, *after)

    far = f32(2 * REACH, across, deep)
    far_zone, far_scale, far_load = pinned(zone), pinned(scale), pinned(load)
    load_first, load_second, first, second = call(
        functools.partial(bring_edges, box),
        (f32(MARGIN, across, deep),) * 2 + (far, far),
        [in_hbm] * 3,
        [pltpu.VMEM((2, REACH, across, deep), zone.dtype), pltpu.SemaphoreType.DMA((6,))],
    )(far_zone, far_scale, far_load)
    load, scale, zone = call(
        bring_box,
        (cells, cells, whole_zone),
        [in_hbm] * 3 + [anywhere],
        [pltpu.SemaphoreType.DMA((12,))],
    )(far_load, far_scale, far_zone, load_first)
    load_wide = exchange("wide", load_first, load_second)
    far_wide = exchange("wide", first, second)
    load_first, load_second = pack(MARGIN, [load], load_wide)
    load_narrow = exchange("narrow", load_first, load_second)
    sums, table = call(
        functools.partial(box_sums, box),
        (f32(8, 128), table_shape),
        [VMEM] * 3 + [anywhere] + [VMEM] * 2,
    )(zone, scale, load, load_first, diffusivity, decay)
    far_narrow = exchange("narrow", *pack(REACH, [scale, zone], far_wide))
    load_window, local, image, inverses = call(
        functools.partial(first_solve, box),
        (window, cells, f32(across, deep), f32(box.ey, box.ex, deep)),
        [VMEM] * 8 + [VMEM] * 2 + [VMEM] * N_TABLES,
        [spectral, middle],
        flops=4 * 10**9,
    )(load, *load_wide, *load_narrow, sums, zone, scale, diffusivity, decay, *tables)
    message = f32(REACH * across + count, deep)
    table, first, second = call(
        functools.partial(image_sums, box), (table_shape, message, message), [VMEM] * 9 + [VMEM]
    )(zone, scale, local, image, *far_wide, *far_narrow, table, diffusivity)
    own_table = table
    wide = exchange("wide", first, second)
    parts = (table, wide[0])
    if by_margins:
        parts += (two_away("wide", table), from_other_end("wide", table))
    to_long, to_across, *windows = call(
        functools.partial(side_weights, box),
        (window,) * 4,
        [VMEM] * 6 + [VMEM],
        flops=10**9,
    )(zone, scale, *far_wide, *far_narrow, diffusivity)
    to_deep, mass = call(
        functools.partial(deep_weights, box),
        (window,) * 2,
        [VMEM] * 2 + [VMEM] * 2,
        flops=10**9,
    )(*windows, diffusivity, decay)
    weights = (to_long, to_across, to_deep, mass)
    first, second, table = pack(REACH, [local], wide, parts, [to_long])
    narrow = exchange("narrow", first, second)
    if by_margins:
        table = call(join_rows, table_shape, [VMEM] * 2)(table, narrow[0])
        parts = (table, two_away("narrow", table))
    else:
        parts = (tell(own_table),)
    row, col = f32(across, deep), f32(long, deep)
    iterate, first_row, second_row, first_col, second_col, result = call(
        functools.partial(second_solve, box, len(parts)),
        (cells, row, row, col, col, cells),
        [VMEM] * (11 + len(parts) + N_TABLES),
        [
            scratch(window.shape),
            spectral,
            middle,
            pltpu.SemaphoreType.DMA((long // 8,)),
            scratch((count, -(-2 * count // 128) * 128)),
        ],
        flops=4 * 10**9,
        out_spec=(VMEM,) * 5 + (anywhere,),
    )(local, *wide, *narrow, inverses, *parts, *weights, load_window, *tables)
    narrow = exchange("narrow", first_col, second_col)
    wide = exchange("wide", first_row, second_row)
    rows, cols, inner = call(
        functools.partial(inner_residual, box),
        (f32(2, across, deep), f32(2, long, 8, deep), cells),
        [VMEM] * 6,
        [
            scratch((long + 2, box.cols, deep)),
            scratch((long, box.cols, deep)),
            pltpu.SemaphoreType.DMA((long // 8,)),
        ],
        flops=10**9,
        out_spec=(VMEM, VMEM, anywhere),
    )(load, iterate, *weights)
    residual = call(
        functools.partial(outer_residual, box),
        cells,
        [VMEM] * 9 + [anywhere],
        [
            scratch((2, across - 16, deep)),
            scratch((2, long, 8, deep)),
            pltpu.SemaphoreType.DMA((4,)),
        ],
        out_spec=anywhere,
        aliases={9: 0},
    )(iterate, *wide, *narrow, to_long, to_across, rows, cols, inner)
    return result, residual


def solution(mesh):
    split = P(("groups", "wide"), "narrow", None)
    return jax.shard_map(
        on_device,
        mesh=mesh,
        in_specs=(split, split, P(), P(), split),
        out_specs=(split, split),
        check_vma=False,
    )
```

```python
import functools

import jax
import jax.numpy as jnp
import ml_dtypes
import numpy as np
from jax import lax
from jax.experimental import pallas as pl
from jax.experimental.pallas import tpu as pltpu
from jax.sharding import PartitionSpec as P

MARGIN = 4
REACH = MARGIN + 1
EDGE = 8

cheb_center = 1.3
cheb_radius = 1.2
cheb_ratio = 1.3 / 1.2
rho_first = 1.0 / cheb_ratio
rho_second = 1.0 / (2.0 * cheb_ratio - rho_first)
gain = 2.0 * rho_second / cheb_radius

MEANS = range(4)
BOX_DIAGONAL, LONG_HIGH, LONG_LOW, ACROSS_HIGH, ACROSS_LOW, LOAD_SUM = range(4, 10)
IMAGE_SUM, FLOW_LONG_HIGH, FLOW_LONG_LOW, FLOW_ACROSS_HIGH, FLOW_ACROSS_LOW = range(16, 21)

VMEM = pl.BlockSpec(memory_space=pltpu.VMEM)


def sine_basis(length):
    indices = np.arange(1, length + 1)
    phases = indices[:, None] * indices[None, :] % (2 * (length + 1))
    table = np.sqrt(2.0 / (length + 1)) * np.sin(np.pi * phases / (length + 1))
    eigvals = 4.0 * np.sin(np.pi * indices / (2.0 * (length + 1))) ** 2
    return table.astype(np.float32), eigvals.astype(np.float32)


def call(body, out_shape, in_specs, scratch=(), flops=0, out_spec=None, aliases=None):
    return pl.pallas_call(
        body,
        out_shape=out_shape,
        in_specs=in_specs,
        out_specs=out_spec or jax.tree.map(lambda _: VMEM, out_shape),
        scratch_shapes=list(scratch),
        compiler_params=pltpu.CompilerParams(vmem_limit_bytes=30 * 2**20),
        cost_estimate=pl.CostEstimate(flops=flops, bytes_accessed=0, transcendentals=0),
        input_output_aliases=aliases or {},
    )


def f32(*shape):
    return jax.ShapeDtypeStruct(shape, jnp.float32)


class Box:
    def __init__(self, shape):
        self.long, self.across, self.deep = shape
        self.ex = self.long + 2 * MARGIN
        self.ey = self.across + 2 * MARGIN
        self.rows = self.long + 2 * REACH
        self.cols = self.across + 2 * EDGE
        self.flat = self.rows * self.cols


def pieces(values, count):
    parts = []
    for _ in range(count - 1):
        scaled = values * 65537.0
        part = scaled - (scaled - values)
        parts.append(part)
        values = values - part
    return parts + [values]


def left_table(table, depth, count):
    rows, cols = table.shape
    wide = np.zeros((rows, depth), np.float32)
    wide[:, :cols] = table
    parts = []
    rest = wide
    for _ in range(count):
        part = rest.astype(ml_dtypes.bfloat16).astype(np.float32)
        parts.append(part)
        rest = rest - part
    blank = np.zeros_like(parts[0])
    lines = []
    for index in range(count):
        used = count - index if count > 2 else count
        lines.append(np.concatenate([parts[index]] * used + [blank] * (count - used), axis=1))
    return np.concatenate(lines, axis=0)


def right_tables(table):
    rest, parts = table, []
    for _ in range(3):
        part = rest.astype(ml_dtypes.bfloat16).astype(np.float32)
        parts.append(part)
        rest = rest - part
    both = np.concatenate([parts[0], parts[1]], axis=1)
    return np.concatenate([both, both], axis=0), np.concatenate([parts[2], parts[0]], axis=0)


def padded(size):
    return -(-size // 8) * 8


FORWARD, BACKWARD = 2, 3


def tables_of(box):
    sine_x, eig_x = sine_basis(box.ex)
    sine_y, eig_y = sine_basis(box.ey)
    sine_z, eig_z = sine_basis(box.deep)
    in_order_of_steps = np.arange(box.ey).reshape(8, box.ey // 8).T.reshape(-1)
    from_y = sine_y[MARGIN : MARGIN + box.across]
    from_x = sine_x[MARGIN : MARGIN + box.long]
    spread_x = np.broadcast_to(eig_x[:, None], (box.ex, box.deep))
    spread_y = np.broadcast_to(eig_y[:, None], (box.ey, box.deep))
    main_z, rest_z = right_tables(sine_z)
    return [
        jnp.asarray(np.ascontiguousarray(t))
        for t in (
            left_table(sine_y[:, in_order_of_steps], padded(box.ey), FORWARD),
            left_table(sine_x, padded(box.ex), FORWARD),
            left_table(from_x, padded(box.ex), BACKWARD),
            left_table(from_y, padded(box.ey), BACKWARD),
            main_z,
            rest_z,
            spread_x,
            spread_y,
            eig_z[None, :],
        )
    ]


N_TABLES = 9


def one_pass(left, right):
    return lax.dot_general(
        left,
        right,
        (((1,), (0,)), ((), ())),
        precision=lax.Precision.DEFAULT,
        preferred_element_type=jnp.float32,
    )


def dot_left(table, values, count, rows):
    total = one_pass(table, jnp.concatenate(pieces(values, count), axis=0))
    return sum(total[index * rows : (index + 1) * rows] for index in range(1, count)) + total[:rows]


def dot_right(values, main, rest, count):
    deep = values.shape[1]
    parts = pieces(values, count)
    total = one_pass(jnp.concatenate(parts[:2], axis=1), main)
    result = total[:, :deep] + total[:, deep:]
    if count == 3:
        result = result + one_pass(jnp.concatenate([parts[0], parts[2]], axis=1), rest)
    return result


def with_rows(values, rows):
    if values.shape[0] == rows:
        return values
    blank = jnp.zeros((rows - values.shape[0],) + values.shape[1:], values.dtype)
    return jnp.concatenate([values, blank], axis=0)


FORWARD_ROWS, COLS_ABREAST, BACKWARD_ROWS = 72, 40, 64


def fitting(size, wanted):
    return max(part for part in range(8, wanted + 1, 8) if size % part == 0)


def beside(values):
    return jnp.concatenate(values, axis=1)


def apart(values, lanes):
    return [values[:, start : start + lanes] for start in range(0, values.shape[1], lanes)]


def box_solve(box, source, divided, tables, row_mask, col_mask, spectral, middle, emit):
    into_y, into_x, from_x, from_y, main_z, rest_z = tables[:6]
    deep = box.deep
    deep_x, deep_y = padded(box.ex), padded(box.ey)
    into_y, into_x = into_y[...], into_x[...]
    if col_mask is not None:
        mask = jnp.concatenate([col_mask] * FORWARD, axis=1)
        into_y = into_y * mask
        mask = jnp.concatenate([row_mask] * FORWARD, axis=1)
        into_x = into_x * mask
    from_x, from_y, main_z, rest_z = from_x[...], from_y[...], main_z[...], rest_z[...]
    spectral_flat = spectral.reshape(box.ey * deep_x, deep)
    middle_flat = middle.reshape(box.long * deep_y, deep)
    if deep_x > box.ex:
        spectral[:, box.ex :, :] = jnp.zeros((box.ey, deep_x - box.ex, deep), jnp.float32)
    if deep_y > box.ey:
        middle[:, box.ey :, :] = jnp.zeros((box.long, deep_y - box.ey, deep), jnp.float32)
    step = fitting(box.ex, FORWARD_ROWS)
    for start in range(0, box.ex, step):
        block = jnp.concatenate([source(row) for row in range(start, start + step, 8)], axis=0)
        block = dot_right(block.reshape(step * box.ey, deep), main_z, rest_z, FORWARD)
        block = block.reshape(step, box.ey, deep)
        wide = beside([block[row] for row in range(step)])
        wide = dot_left(into_y, with_rows(wide, deep_y), FORWARD, box.ey)
        for row, values in enumerate(apart(wide, deep)):
            spectral_flat[pl.ds(start + row, box.ey, stride=deep_x), :] = values
    step = fitting(box.ey, COLS_ABREAST)
    for start in range(0, box.ey, step):
        wide = beside([spectral[col] for col in range(start, start + step)])
        wide = apart(dot_left(into_x, wide, FORWARD, box.ex), deep)
        wide = beside([divided(values, start + part) for part, values in enumerate(wide)])
        wide = dot_left(from_x, with_rows(wide, deep_x), BACKWARD, box.long)
        for part, values in enumerate(apart(wide, deep)):
            middle_flat[pl.ds(start + part, box.long, stride=deep_y), :] = values
    step = fitting(box.long, BACKWARD_ROWS)
    for start in range(0, box.long, step):
        wide = beside([middle[row] for row in range(start, start + step)])
        parts = apart(dot_left(from_y, wide, BACKWARD, box.across), deep)
        values = dot_right(jnp.concatenate(parts, axis=0), main_z, rest_z, BACKWARD)
        for row in range(0, step, 8):
            emit(start + row, values[row * box.across : (row + 8) * box.across])


def position():
    long_pos, across_pos = lax.axis_index("wide"), lax.axis_index("narrow")
    return long_pos, across_pos, lax.axis_size("wide"), lax.axis_size("narrow")


def as_float(flag):
    return jnp.where(flag, jnp.float32(1.0), jnp.float32(0.0))


def is_even(axis):
    return lax.rem(lax.axis_index(axis), 2) == 0


class Sides:
    def __init__(self, axis, first, second):
        position = lax.axis_index(axis)
        self.even = is_even(axis)
        self.has_low = as_float(position > 0)
        self.has_high = as_float(position < lax.axis_size(axis) - 1)
        self.first, self.second = first, second

    def low(self, *index):
        return jnp.where(self.even, self.second[index], self.first[index]) * self.has_low

    def high(self, *index):
        return jnp.where(self.even, self.first[index], self.second[index]) * self.has_high


def in_order(even, up, down):
    return jnp.where(even, up, down), jnp.where(even, down, up)


def row_of(stride, col, count, first=0):
    return pl.ds(first * stride + col, count, stride=stride)


def pack_columns(box, fields, wide_sides, wide, first, second):
    corner = len(fields) * wide * box.long
    even = is_even("narrow")
    place = 0
    for field, sides in zip(fields, wide_sides):
        for step in range(wide):
            cols = (box.across - wide + step, step)
            values = [field[row_of(box.across, col, box.long), :] for col in cols]
            low = [sides.low(row_of(box.across, col, wide), slice(None)) for col in cols]
            high = [sides.high(row_of(box.across, col, wide), slice(None)) for col in cols]
            at = corner + 2 * REACH * place
            for start, parts in ((place * box.long, values), (at, low), (at + REACH, high)):
                parts = in_order(even, *(part.astype(jnp.float32) for part in parts))
                size = parts[0].shape[0]
                first[start : start + size, :], second[start : start + size, :] = parts
            place += 1


def message_rows(box, count):
    return -(-(count * (box.long + 2 * REACH)) // 8) * 8


def pack_fields(box, wide, fields, tables, after, *refs):
    own, (low, high), refs = refs[:fields], refs[fields : fields + 2], refs[fields + 2 :]
    parts, (first, second, *table) = refs[:tables], refs[tables + after :]
    size = wide * box.across
    flat = [field.reshape(box.long * box.across, box.deep) for field in own]
    low = low.reshape(low.size // box.deep, box.deep)
    high = high.reshape(high.size // box.deep, box.deep)
    sides = [
        Sides("wide", *(ref.at[index * size : (index + 1) * size] for ref in (low, high)))
        for index in range(fields)
    ]
    pack_columns(box, flat, sides, wide, first, second)
    if tables:
        known = last_rows_merged(parts, table[0].shape[0])
        table[0][...] = known
        first[first.shape[0] - known.shape[0] :, :] = known
        second[second.shape[0] - known.shape[0] :, :] = known


def bring_edges(box, zone, scale, load, load_first, load_second, first, second, staged, sems):
    even = is_even("wide")

    def edges(wide):
        up, down = box.long - wide, 0
        return [pl.ds(jnp.where(even, *pair), wide) for pair in ((up, down), (down, up))]

    copies = [
        (zone.at[edges(REACH)[0]], staged.at[0]),
        (zone.at[edges(REACH)[1]], staged.at[1]),
        (load.at[edges(MARGIN)[0]], load_first),
        (load.at[edges(MARGIN)[1]], load_second),
        (scale.at[edges(REACH)[0]], first.at[:REACH]),
        (scale.at[edges(REACH)[1]], second.at[:REACH]),
    ]
    copies = [
        pltpu.make_async_copy(source, target, sems.at[index])
        for index, (source, target) in enumerate(copies)
    ]
    for copy in copies:
        copy.start()
    for copy in copies[:2]:
        copy.wait()
    first[REACH:] = staged[0].astype(jnp.float32)
    second[REACH:] = staged[1].astype(jnp.float32)
    for copy in copies[2:]:
        copy.wait()


def bring_box(load, scale, zone, after, own_load, own_scale, own_zone, sems):
    del after
    parts = 4
    size = own_load.shape[0] // parts
    copies = []
    for part in range(parts):
        rows = slice(part * size, (part + 1) * size)
        for source, target in ((load, own_load), (scale, own_scale), (zone, own_zone)):
            copies.append(
                pltpu.make_async_copy(source.at[rows], target.at[rows], sems.at[len(copies)])
            )
            copies[-1].start()
    for copy in copies:
        copy.wait()


def fill_window(box, window, own, wide_sides, narrow_sides, wide, place, total, add=None):
    flat = window.reshape(box.flat, box.deep)
    nothing = jnp.zeros((box.rows, EDGE, box.deep), jnp.float32)
    window[:, :EDGE, :] = nothing
    window[:, EDGE + box.across :, :] = nothing
    if add is None:
        add = lambda values, row_side, col_side: values
    inner = slice(EDGE, EDGE + box.across)
    first, last = REACH, REACH + box.long
    if wide < REACH:
        blank = jnp.zeros((1, box.across, box.deep), jnp.float32)
        window[0:1, inner, :] = blank
        window[box.rows - 1 :, inner, :] = blank
    window[first:last, inner, :] = add(own[...].astype(jnp.float32), 0, 0)
    window[first - wide : first, inner, :] = add(wide_sides.low(Ellipsis), -1, 0)
    window[last : last + wide, inner, :] = add(wide_sides.high(Ellipsis), 1, 0)
    corner = total * box.long
    for step in range(wide):
        for source, col, side in (
            (narrow_sides.low, EDGE - wide + step, -1),
            (narrow_sides.high, EDGE + box.across + step, 1),
        ):
            for start, size, row, row_side in (
                ((place + step) * box.long, box.long, first, 0),
                (corner + 2 * REACH * (place + step), wide, first - wide, -1),
                (corner + 2 * REACH * (place + step) + REACH, wide, last, 1),
            ):
                values = source(slice(start, start + size), slice(None))
                flat[row_of(box.cols, col, size, row), :] = add(values, row_side, side)


def some_cols(box, ref, row, step):
    stride = box.ey // 8
    return ref[row, pl.ds(EDGE - MARGIN + step, 8, stride=stride), :]


def negative_image(box, window, row, at, x, flow_before, weights):
    to_long, to_across, to_deep, mass = weights
    steps = range(box.ey // 8)
    x_next = [some_cols(box, window, row + 1, step) for step in range(-1, len(steps) + 1)]
    flow_long = [
        some_cols(box, to_long, at, step) * (x_next[step + 1] - x[step + 1]) for step in steps
    ]
    flow_across = [
        some_cols(box, to_across, at, step) * (x[step + 2] - x[step + 1])
        for step in range(-1, len(steps))
    ]
    totals = []
    for step in steps:
        here = x[step + 1]
        lanes = here.shape[1]
        flow_deep = some_cols(box, to_deep, at, step) * (pltpu.roll(here, lanes - 1, 1) - here)
        total = flow_long[step] - flow_before[step] - some_cols(box, mass, at, step) * here
        total = total + (flow_across[step + 1] - flow_across[step])
        totals.append(total + (flow_deep - pltpu.roll(flow_deep, 1, 1)))
    return totals, x_next, flow_long


def in_steps(box, refs, rows):
    return jnp.stack(
        [
            jnp.concatenate([some_cols(box, ref, row, step) for step in range(box.ey // 8)], axis=0)
            for ref, row in zip(refs, rows)
        ]
    )


def looked_up(labels, values):
    return jnp.where(labels == 0, values[0], jnp.where(labels == 1, values[1], values[2]))


def at_own_row(line, shape):
    long_pos, across_pos, _, across_count = position()
    rows = lax.broadcasted_iota(jnp.int32, shape, 0)
    own = rows == long_pos * across_count + across_pos
    return jnp.where(own, line[:1], jnp.zeros(shape, jnp.float32))


def merged(table, *others):
    for other in others:
        table = jnp.where(table != 0.0, table, other)
    return table


def last_rows_merged(refs, count):
    return merged(*(ref[ref.shape[0] - count :, :] for ref in refs))


def join_rows(table, message, out):
    out[...] = last_rows_merged((table, message), out.shape[0])


def line_of(numbers, shape):
    count = -(-len(numbers) // 8) * 8
    rows = lax.broadcasted_iota(jnp.int32, (count, shape[1]), 0)
    lanes = lax.broadcasted_iota(jnp.int32, (count, shape[1]), 1)
    stacked = jnp.zeros((count, shape[1]), jnp.float32)
    place = jnp.zeros((count, shape[1]), jnp.bool_)
    for row, (index, values) in enumerate(numbers):
        stacked = jnp.where(rows == row, values, stacked)
        place = place | ((rows == row) & (lanes == index))
    sums = jnp.sum(stacked, axis=1, keepdims=True)
    line = jnp.sum(jnp.where(place, sums, jnp.zeros_like(stacked)), axis=0, keepdims=True)
    return jnp.broadcast_to(line, shape)


def box_sums(box, zone, scale, load, after, diffusivity, decay, out, table):
    del after
    nothing = jnp.zeros((box.across, box.deep), jnp.float32)
    half = [[0.5 * diffusivity[z : z + 1, d : d + 1] for z in range(3)] for d in range(3)]
    rates = [decay[0:1, z : z + 1] for z in range(3)]

    def halves(row):
        labels, factor = zone[row], scale[row]
        return [looked_up(labels, half[d]) * factor for d in range(3)] + [looked_up(labels, rates)]

    sums = [nothing] * 5
    for row in range(box.long):
        sums = [total + more for total, more in zip(sums, halves(row) + [load[row]])]

    def total(values):
        return jnp.sum(values, axis=0, keepdims=True)

    cells = box.long * box.across * box.deep
    numbers = [(index, total(sums[index]) * (2.0 / cells)) for index in range(3)]
    mass = total(sums[3])
    numbers += [(3, mass / cells)]
    lane = lax.broadcasted_iota(jnp.int32, (1, box.deep), 1)
    ends = jnp.where((lane == 0) | (lane == box.deep - 1), total(sums[2]), 0.0)
    numbers += [
        (BOX_DIAGONAL, mass + ends),
        (LONG_HIGH, total(halves(box.long - 1)[0])),
        (LONG_LOW, total(halves(0)[0])),
        (ACROSS_HIGH, sums[1][box.across - 1 :]),
        (ACROSS_LOW, sums[1][:1]),
        (LOAD_SUM, total(sums[4])),
    ]
    line = line_of(numbers, out.shape)
    out[...] = line
    table[...] = at_own_row(line, table.shape)


def means_of(ref):
    return [ref[0:1, index : index + 1] for index in range(4)]


def first_solve(box, load, low, high, left, right, means, zone, scale, diffusivity, decay, *rest):
    tables = rest[:N_TABLES]
    window, local, image, inverses, spectral, middle = rest[N_TABLES:]
    spread_x, spread_y, eig_z = tables[6:]
    means = means_of(means)
    base = means[3] + means[0] * spread_x[...] + means[2] * eig_z[...]

    def divided(values, col):
        divisor = base + means[1] * spread_y[col : col + 1, :]
        inverse = pl.reciprocal(divisor, approx=True)
        for _ in range(2):
            inverse = inverse * (2.0 - divisor * inverse)
        inverses[col] = inverse
        return values * inverse

    half = [0.5 * diffusivity[z : z + 1, 2:3] for z in range(3)]
    rates = [decay[0:1, z : z + 1] for z in range(3)]
    lane = lax.broadcasted_iota(jnp.int32, (box.across, box.deep), 1)
    ends = jnp.where((lane == 0) | (lane == box.deep - 1), jnp.float32(1.0), jnp.float32(0.0))
    image[...] = jnp.zeros((box.across, box.deep), jnp.float32)
    wide_sides, narrow_sides = Sides("wide", low, high), Sides("narrow", left, right)
    fill_window(box, window, load, wide_sides, narrow_sides, MARGIN, 0, MARGIN)

    def emit(start, values):
        values = values * (1.0 / cheb_center)
        values = values.reshape(8, box.across, box.deep)
        local[start : start + 8] = values
        total = image[...]
        for row in range(8):
            labels = zone[start + row]
            mass = looked_up(labels, rates) + looked_up(labels, half) * scale[start + row] * ends
            total = total + mass * values[row]
        image[...] = total

    box_solve(
        box,
        lambda start: in_steps(box, [window] * 8, range(1 + start, 9 + start)),
        divided,
        tables,
        None,
        None,
        spectral,
        middle,
        emit,
    )


def side_weights(
    box, zone, scale, low, high, left, right, diffusivity, to_long, to_across, zone_window,
    scale_window
):
    for index, (window, own) in enumerate(((scale_window, scale), (zone_window, zone))):
        start = index * REACH
        wide_sides = Sides("wide", *(ref.at[start : start + REACH] for ref in (low, high)))
        narrow_sides = Sides("narrow", left, right)
        fill_window(box, window, own, wide_sides, narrow_sides, REACH, start, 2 * REACH)
    half = [[0.5 * diffusivity[z : z + 1, d : d + 1] for z in range(3)] for d in range(2)]

    def one_row(row, before):
        labels, factor = zone_window[row], scale_window[row]
        now = [looked_up(labels, half[d]) * factor for d in range(2)]
        to_across[row] = now[1] + pltpu.roll(now[1], box.cols - 1, 0)
        to_long[max(row - 1, 0)] = before + now[0]
        return now[0]

    before = jnp.zeros((box.cols, box.deep), jnp.float32)
    for row in range(box.rows):
        before = one_row(row, before)
    to_long[box.rows - 1] = before


def deep_weights(box, zone_window, scale_window, diffusivity, decay, to_deep, mass):
    half = [0.5 * diffusivity[z : z + 1, 2:3] for z in range(3)]
    rates = [decay[0:1, z : z + 1] for z in range(3)]
    lane = lax.broadcasted_iota(jnp.int32, (box.cols, box.deep), 1)
    ends = jnp.where((lane == 0) | (lane == box.deep - 1), jnp.float32(1.0), jnp.float32(0.0))
    not_last = jnp.where(lane == box.deep - 1, jnp.float32(0.0), jnp.float32(1.0))

    def one_row(row):
        labels = zone_window[row]
        now = looked_up(labels, half) * scale_window[row]
        to_deep[row] = (now + pltpu.roll(now, box.deep - 1, 1)) * not_last
        mass[row] = looked_up(labels, rates) + now * ends

    for row in range(box.rows):
        one_row(row)


def image_sums(
    box, zone, scale, local, image, low, high, left, right, table, diffusivity, out, up, down
):
    half = [[0.5 * diffusivity[z : z + 1, d : d + 1] for z in range(3)] for d in range(3)]
    shape = (box.long * box.across, box.deep)
    zone_flat, scale_flat, local_flat = zone.reshape(shape), scale.reshape(shape), local.reshape(shape)
    last_col = row_of(box.across, box.across - 1, box.long)
    first_col = row_of(box.across, 0, box.long)

    wide_sides, narrow_sides = Sides("wide", low, high), Sides("narrow", left, right)

    def side(source, place):
        return source(slice(place * box.long, (place + 1) * box.long), slice(None))

    above, below = wide_sides.high, wide_sides.low
    faces = [
        (0, zone[box.long - 1], scale[box.long - 1], local[box.long - 1], above(REACH), above(0)),
        (0, zone[0], scale[0], local[0], below(2 * REACH - 1), below(REACH - 1)),
        (
            1,
            zone_flat[last_col, :],
            scale_flat[last_col, :],
            local_flat[last_col, :],
            side(narrow_sides.high, REACH),
            side(narrow_sides.high, 0),
        ),
        (
            1,
            zone_flat[first_col, :],
            scale_flat[first_col, :],
            local_flat[first_col, :],
            side(narrow_sides.low, 2 * REACH - 1),
            side(narrow_sides.low, REACH - 1),
        ),
    ]
    flows = []
    for direction, labels, factor, values, far_labels, far_factor in faces:
        weight = looked_up(labels, half[direction]) * factor
        weight = weight + looked_up(far_labels, half[direction]) * far_factor
        flows.append(jnp.sum(weight * values, axis=0, keepdims=True))
    long_pos, across_pos, long_count, across_count = position()
    numbers = [
        (IMAGE_SUM, jnp.sum(image[...], axis=0, keepdims=True) + sum(flows)),
        (FLOW_LONG_HIGH, flows[0] * as_float(long_pos < long_count - 1)),
        (FLOW_LONG_LOW, flows[1] * as_float(long_pos > 0)),
        (FLOW_ACROSS_HIGH, flows[2] * as_float(across_pos < across_count - 1)),
        (FLOW_ACROSS_LOW, flows[3] * as_float(across_pos > 0)),
    ]
    known = table[...] + at_own_row(line_of(numbers, (8, out.shape[1])), out.shape)
    out[...] = known
    edge = REACH * box.across
    even = is_even("wide")
    for target, pair in ((up, (box.long - REACH, 0)), (down, (0, box.long - REACH))):
        target[:edge] = local[pl.ds(jnp.where(even, *pair), REACH)].reshape(edge, box.deep)
        target[edge:] = known


def column(values, index):
    return values[:, index : index + 1]


def uncoupled_groups(count, across):
    places = np.arange(count)
    long_step = np.abs(places[:, None] // across - places[None, :] // across)
    across_step = np.abs(places[:, None] % across - places[None, :] % across)
    coupled = long_step + across_step == 1
    left = list(range(count))
    groups = []
    while left:
        group = []
        for place in sorted(left, key=lambda p: (coupled[p][left].sum(), p)):
            if not coupled[place][group].any():
                group.append(place)
        left = [place for place in left if place not in group]
        for place in group:
            beside = [other for other in left if coupled[place][other]]
            for other in beside:
                coupled[other][beside] = True
                coupled[other][other] = False
        groups.append(group)
    return groups


def coarse_inverse(numbers, work):
    count, width = work.shape
    across = lax.axis_size("narrow")
    beyond = pltpu.roll(numbers, count - across, 0)
    beside = pltpu.roll(numbers, count - 1, 0)
    before = pltpu.roll(numbers, across, 0)
    ahead = pltpu.roll(numbers, 1, 0)
    place = lax.broadcasted_iota(jnp.int32, (count, 1), 0)
    across_pos = lax.rem(place, across)
    nothing = jnp.zeros((count, 1), jnp.float32)
    couplings = []
    diagonal = column(numbers, BOX_DIAGONAL)
    for own, other, there, inside in (
        (LONG_HIGH, LONG_LOW, beyond, place < count - across),
        (LONG_LOW, LONG_HIGH, before, place >= across),
        (ACROSS_HIGH, ACROSS_LOW, beside, across_pos < across - 1),
        (ACROSS_LOW, ACROSS_HIGH, ahead, across_pos > 0),
    ):
        shared = jnp.where(inside, column(there, other), nothing)
        diagonal = diagonal + column(numbers, own) + shared
        couplings.append(jnp.where(inside, column(numbers, own) + shared, nothing))
    rows = lax.broadcasted_iota(jnp.int32, (count, width), 0)
    cols = lax.broadcasted_iota(jnp.int32, (count, width), 1)
    blank = jnp.zeros((count, width), jnp.float32)
    matrix = jnp.where(cols == rows, diagonal, blank)
    for shift, coupling in zip((across, -across, 1, -1), couplings):
        matrix = matrix - jnp.where((cols == rows + shift) & (cols < count), coupling, blank)
    matrix = jnp.where(cols == rows + count, jnp.ones((count, 1), jnp.float32), matrix)
    if count <= 16:
        for group in uncoupled_groups(count, across):
            rest = matrix
            for step in group:
                pivot_row = matrix[step : step + 1, :] / matrix[step : step + 1, step : step + 1]
                rest = rest - matrix[:, step : step + 1] * pivot_row
                rest = jnp.where(rows == step, pivot_row, rest)
            matrix = rest
        return pltpu.roll(matrix, width - count, 1)
    work[...] = matrix

    def eliminate(step, _):
        values = work[...]
        pivot_row = work[pl.ds(step, 1), :]
        at_step = cols == step
        factors = jnp.sum(jnp.where(at_step, values, blank), axis=1, keepdims=True)
        pivot = jnp.sum(jnp.where(at_step[:1], pivot_row, blank[:1]), axis=1, keepdims=True)
        pivot_row = pivot_row / pivot
        work[...] = jnp.where(rows == step, pivot_row, values - factors * pivot_row)
        return 0

    lax.fori_loop(0, count, eliminate, 0)
    values = work[...]
    if count % 128:
        return pltpu.roll(values, width - count, 1)
    return values[:, count : 2 * count]


def answer(inverse, sums):
    return jnp.sum(inverse * sums, axis=0, keepdims=True)


def at_box(values, row_side, col_side):
    long_pos, across_pos, long_count, across_count = position()
    there_long, there_across = long_pos + row_side, across_pos + col_side
    inside = (
        (there_long >= 0)
        & (there_long < long_count)
        & (there_across >= 0)
        & (there_across < across_count)
    )
    lanes = lax.broadcasted_iota(jnp.int32, values.shape, 1)
    wanted = (lanes == there_long * across_count + there_across) & inside
    return jnp.sum(jnp.where(wanted, values, jnp.zeros_like(values)), axis=1, keepdims=True)


def coarse_corrections(parts, *refs):
    table_parts, (out, work) = refs[:parts], refs[parts:]
    count = work.shape[0]
    numbers = last_rows_merged(table_parts, count)
    across_count = lax.axis_size("narrow")
    inverse = coarse_inverse(numbers, work)
    sums = column(numbers, IMAGE_SUM)
    sums = sums - column(pltpu.roll(numbers, count - across_count, 0), FLOW_LONG_LOW)
    sums = sums - column(pltpu.roll(numbers, across_count, 0), FLOW_LONG_HIGH)
    sums = sums - column(pltpu.roll(numbers, count - 1, 0), FLOW_ACROSS_LOW)
    sums = sums - column(pltpu.roll(numbers, 1, 0), FLOW_ACROSS_HIGH)
    load_sums = column(numbers, LOAD_SUM)
    sums = load_sums * (1.0 - 1.0 / cheb_center) - sums
    out[0:1, :] = answer(inverse, load_sums) * (1.0 / cheb_center)
    out[1:2, :] = answer(inverse, sums) * gain


def second_solve(box, local, low, high, left, right, inverses, answers, *rest):
    to_long, to_across, to_deep, mass, load_window = rest[:5]
    tables = rest[5 : 5 + N_TABLES]
    iterate, top, bottom, last_col, first_col, out = rest[5 + N_TABLES : 11 + N_TABLES]
    window, spectral, middle, sems = rest[11 + N_TABLES :]
    long_pos, across_pos, long_count, across_count = position()
    coarse = answers[0:1, :]
    own_shift = at_box(answers[1:2, :], 0, 0)
    shifts = {
        (row_side, col_side): at_box(coarse, row_side, col_side)
        for row_side in (-1, 0, 1)
        for col_side in (-1, 0, 1)
    }

    def add(values, row_side, col_side):
        shift = shifts[row_side, col_side]
        if values.ndim == 3:
            shift = shift.reshape(1, 1, 1)
        return values + shift

    edge = REACH * box.across
    low, high = (
        ref.at[:edge].reshape(REACH, box.across, box.deep) for ref in (low, high)
    )
    wide_sides, narrow_sides = Sides("wide", low, high), Sides("narrow", left, right)
    fill_window(box, window, local, wide_sides, narrow_sides, REACH, 0, REACH, add)
    weights = (to_long, to_across, to_deep, mass)

    steps = range(box.ey // 8)
    x = [some_cols(box, window, 1, step) for step in range(-1, len(steps) + 1)]
    flow = [
        some_cols(box, to_long, 0, step) * (x[step + 1] - some_cols(box, window, 0, step))
        for step in steps
    ]
    state = [x, flow]

    def divided(values, col):
        return values * inverses[col]

    def residual(start_row):
        rows = []
        for row in range(start_row + 1, start_row + 9):
            image, *state[:] = negative_image(box, window, row, row, *state, weights)
            image = [some_cols(box, load_window, row, step) + image[step] for step in steps]
            rows.append(jnp.concatenate(image, axis=0))
        return jnp.stack(rows)

    inner = slice(EDGE, EDGE + box.across)
    first = REACH
    row_ids = lax.broadcasted_iota(jnp.int32, (1, padded(box.ex)), 1)
    col_ids = lax.broadcasted_iota(jnp.int32, (1, padded(box.ey)), 1)
    col_ids = (col_ids & 7) * (box.ey // 8) + lax.shift_right_logical(col_ids, 3)
    row_mask = jnp.where(row_ids < MARGIN, as_float(long_pos > 0), 1.0)
    row_mask = jnp.where(row_ids >= MARGIN + box.long, as_float(long_pos < long_count - 1), row_mask)
    col_mask = jnp.where(col_ids < MARGIN, as_float(across_pos > 0), 1.0)
    col_mask = jnp.where(
        col_ids >= MARGIN + box.across, as_float(across_pos < across_count - 1), col_mask
    )
    keep = 1.0 + rho_second * rho_first
    copies = []

    def emit(start, values):
        rows = values.reshape(8, box.across, box.deep)
        before = window[first + start : first + start + 8, inner, :]
        shift = own_shift.reshape(1, 1, 1)
        iterate[start : start + 8] = keep * before + (gain * rows + shift)
        copies.append(
            pltpu.make_async_copy(
                iterate.at[start : start + 8], out.at[start : start + 8], sems.at[len(copies)]
            )
        )
        copies[-1].start()

    box_solve(
        box, residual, divided, tables, row_mask, col_mask, spectral, middle, emit
    )
    rows = in_order(is_even("wide"), iterate[box.long - 1], iterate[0])
    top[...], bottom[...] = rows
    flat = iterate.reshape(box.long * box.across, box.deep)
    cols = [flat[row_of(box.across, col, box.long), :] for col in (box.across - 1, 0)]
    last_col[...], first_col[...] = in_order(is_even("narrow"), *cols)
    for copy in copies:
        copy.wait()


def inner_residual(
    box, load, iterate, to_long, to_across, to_deep, mass, rows, cols, out, window, result, sems
):
    inner = slice(EDGE, EDGE + box.across)
    flat = window.reshape((box.long + 2) * box.cols, box.deep)
    iterate_flat = iterate.reshape(box.long * box.across, box.deep)
    blank = jnp.zeros((box.long + 2, EDGE, box.deep), jnp.float32)
    window[:, :EDGE, :] = blank
    window[:, EDGE + box.across :, :] = blank
    window[1 : 1 + box.long, inner, :] = iterate[...]
    window[0, inner, :] = iterate[0]
    window[1 + box.long, inner, :] = iterate[box.long - 1]
    for col, place in ((0, EDGE - 1), (box.across - 1, EDGE + box.across)):
        values = iterate_flat[row_of(box.across, col, box.long), :]
        flat[row_of(box.cols, place, box.long, 1), :] = values
    weights = (to_long, to_across, to_deep, mass)
    steps = range(box.ey // 8)
    x = [some_cols(box, window, 1, step) for step in range(-1, len(steps) + 1)]
    flow = [jnp.zeros((8, box.deep), jnp.float32) for _ in steps]
    middle = slice(8, box.across - 8)
    copies = []
    for row in range(box.long):
        image, x, flow = negative_image(box, window, row + 1, REACH + row, x, flow, weights)
        for step in steps:
            place = pl.ds(EDGE - MARGIN + step, 8, stride=box.ey // 8)
            result[row, place, :] = image[step]
        values = load[row] + result[row, inner]
        result[row, inner] = values
        cols[0, row] = values[:8]
        cols[1, row] = values[box.across - 8 :]
        if row == 0:
            rows[0] = values
        if row == box.long - 1:
            rows[1] = values
        if row % 8 == 7:
            part = slice(row - 7, row + 1)
            copy = pltpu.make_async_copy(
                result.at[part, EDGE + 8 : EDGE + box.across - 8],
                out.at[part, middle],
                sems.at[row // 8],
            )
            copy.start()
            copies.append(copy)
    for copy in copies:
        copy.wait()


def outer_residual(
    box, iterate, low, high, left, right, to_long, to_across, rows, cols, inner_out, out,
    row_part, col_part, sems
):
    del inner_out
    inner = slice(EDGE, EDGE + box.across)
    middle = slice(8, box.across - 8)
    wide_sides, narrow_sides = Sides("wide", low, high), Sides("narrow", left, right)
    last = box.long - 1
    iterate_flat = iterate.reshape(box.long * box.across, box.deep)
    across_flat = to_across.reshape(box.flat, box.deep)
    below = to_long[REACH - 1, inner] * (wide_sides.low(Ellipsis) - iterate[0])
    above = to_long[REACH + last, inner] * (wide_sides.high(Ellipsis) - iterate[last])
    row_part[0] = (rows[0] + below)[middle]
    row_part[1] = (rows[1] + above)[middle]
    copies = [
        pltpu.make_async_copy(row_part.at[0], out.at[0, middle], sems.at[0]),
        pltpu.make_async_copy(row_part.at[1], out.at[last, middle], sems.at[1]),
    ]
    for copy in copies:
        copy.start()
    col_part[...] = cols[...]
    flat = col_part.reshape(2 * box.long * 8, box.deep)
    for side, (from_side, col, face, tile) in enumerate(
        (
            (narrow_sides.low, 0, EDGE - 1, slice(0, 8)),
            (narrow_sides.high, box.across - 1, EDGE + box.across - 1, slice(box.across - 8, None)),
        )
    ):
        weight = across_flat[row_of(box.cols, face, box.long, REACH), :]
        own = iterate_flat[row_of(box.across, col, box.long), :]
        place = pl.ds(side * box.long * 8 + side * 7, box.long, stride=8)
        flat[place, :] = flat[place, :] + weight * (from_side(Ellipsis) - own)
        col_part[side, 0] = col_part[side, 0] + below[tile]
        col_part[side, last] = col_part[side, last] + above[tile]
        first_col = side * (box.across - 8)
        copy = pltpu.make_async_copy(
            col_part.at[side], out.at[:, first_col : first_col + 8], sems.at[2 + side]
        )
        copy.start()
        copies.append(copy)
    for copy in copies:
        copy.wait()


def swaps(axis):
    sizes = (lax.axis_size("wide"), lax.axis_size("narrow"))
    along = ("wide", "narrow").index(axis)
    size, beside = sizes[along], sizes[1 - along]

    def number(place, other_place):
        pair = (place, other_place) if along == 0 else (other_place, place)
        return pair[0] * sizes[1] + pair[1]

    ways = []
    for way in range(2):
        pairs = []
        for place in range(size):
            for other_place in range(beside):
                partner = place + 1 if place % 2 == way else place - 1
                there = other_place
                if not 0 <= partner < size:
                    partner = place
                    there = other_place ^ 1 if beside % 2 == 0 else other_place
                pairs.append((number(place, other_place), number(partner, there)))
        ways.append(pairs)
    return ways


def exchange(axis, first, second):
    ways = swaps(axis)
    axes = ("wide", "narrow")
    return lax.ppermute(first, axes, ways[0]), lax.ppermute(second, axes, ways[1])


def from_other_end(axis, table):
    size = lax.axis_size(axis)
    return lax.ppermute(table, axis, [(i, size - 1 - i) for i in range(size)])


def two_away(axis, table):
    size = lax.axis_size(axis)
    return lax.ppermute(table, axis, [(i, (i + 2) % size) for i in range(size)])


def tell(table):
    count = table.shape[0]
    long_pos, across_pos, _, across_count = position()
    own = lax.dynamic_slice_in_dim(table, long_pos * across_count + across_pos, 1, axis=0)
    line = jnp.broadcast_to(own, (count, 1, 128))
    told = lax.all_to_all(line, ("wide", "narrow"), split_axis=0, concat_axis=0, tiled=True)
    return told.reshape(count, 128)


def on_device(zone, scale, diffusivity, decay, load):
    box = Box(load.shape)
    long, across, deep = load.shape
    count = lax.axis_size("wide") * lax.axis_size("narrow")
    by_margins = lax.axis_size("wide") == 4 and lax.axis_size("narrow") == 4
    tables = tables_of(box)
    decay = decay.reshape(1, -1)
    cells = f32(long, across, deep)
    whole_zone = jax.ShapeDtypeStruct(cells.shape, zone.dtype)
    window = f32(box.rows, box.cols, deep)
    table_shape = f32(count, 128)
    anywhere = pl.BlockSpec(memory_space=pl.ANY)
    in_hbm = pl.BlockSpec(memory_space=pltpu.HBM)

    def scratch(shape):
        return pltpu.VMEM(shape, jnp.float32)

    def pinned(field):
        return pltpu.with_memory_space_constraint(field, pltpu.HBM)

    spectral = scratch((box.ey, padded(box.ex), deep))
    middle = scratch((long, padded(box.ey), deep))

    def pack(wide, fields, sides, parts=(), after=()):
        rows = message_rows(box, wide * len(fields)) + (count if parts else 0)
        message = f32(rows, deep)
        body = functools.partial(pack_fields, box, wide, len(fields), len(parts), len(after))
        return call(
            body,
            (message, message) + ((table_shape,) if parts else ()),
            [VMEM] * (len(fields) + 2 + len(parts)) + [anywhere] * len(after),
        )(*fields, *sides, *parts, *after)

    far = f32(2 * REACH, across, deep)
    far_zone, far_scale, far_load = pinned(zone), pinned(scale), pinned(load)
    load_first, load_second, first, second = call(
        functools.partial(bring_edges, box),
        (f32(MARGIN, across, deep),) * 2 + (far, far),
        [in_hbm] * 3,
        [pltpu.VMEM((2, REACH, across, deep), zone.dtype), pltpu.SemaphoreType.DMA((6,))],
    )(far_zone, far_scale, far_load)
    load, scale, zone = call(
        bring_box,
        (cells, cells, whole_zone),
        [in_hbm] * 3 + [anywhere],
        [pltpu.SemaphoreType.DMA((12,))],
    )(far_load, far_scale, far_zone, load_first)
    load_wide = exchange("wide", load_first, load_second)
    far_wide = exchange("wide", first, second)
    load_first, load_second = pack(MARGIN, [load], load_wide)
    load_narrow = exchange("narrow", load_first, load_second)
    sums, table = call(
        functools.partial(box_sums, box),
        (f32(8, 128), table_shape),
        [VMEM] * 3 + [anywhere] + [VMEM] * 2,
    )(zone, scale, load, load_first, diffusivity, decay)
    far_narrow = exchange("narrow", *pack(REACH, [scale, zone], far_wide))
    load_window, local, image, inverses = call(
        functools.partial(first_solve, box),
        (window, cells, f32(across, deep), f32(box.ey, box.ex, deep)),
        [VMEM] * 8 + [VMEM] * 2 + [VMEM] * N_TABLES,
        [spectral, middle],
        flops=4 * 10**9,
    )(load, *load_wide, *load_narrow, sums, zone, scale, diffusivity, decay, *tables)
    message = f32(REACH * across + count, deep)
    table, first, second = call(
        functools.partial(image_sums, box), (table_shape, message, message), [VMEM] * 9 + [VMEM]
    )(zone, scale, local, image, *far_wide, *far_narrow, table, diffusivity)
    own_table = table
    wide = exchange("wide", first, second)
    parts = (table, wide[0])
    if by_margins:
        parts += (two_away("wide", table), from_other_end("wide", table))
    to_long, to_across, *windows = call(
        functools.partial(side_weights, box),
        (window,) * 4,
        [VMEM] * 6 + [VMEM],
        flops=10**9,
    )(zone, scale, *far_wide, *far_narrow, diffusivity)
    to_deep, mass = call(
        functools.partial(deep_weights, box),
        (window,) * 2,
        [VMEM] * 2 + [VMEM] * 2,
        flops=10**9,
    )(*windows, diffusivity, decay)
    weights = (to_long, to_across, to_deep, mass)
    first, second, table = pack(REACH, [local], wide, parts, [to_long])
    narrow = exchange("narrow", first, second)
    if by_margins:
        table = call(join_rows, table_shape, [VMEM] * 2)(table, narrow[0])
        parts = (table, two_away("narrow", table))
    else:
        parts = (tell(own_table),)
    row, col = f32(across, deep), f32(long, deep)
    answers = call(
        functools.partial(coarse_corrections, len(parts)),
        f32(8, -(-count // 128) * 128),
        [VMEM] * len(parts),
        [scratch((count, -(-2 * count // 128) * 128))],
    )(*parts)
    iterate, first_row, second_row, first_col, second_col, result = call(
        functools.partial(second_solve, box),
        (cells, row, row, col, col, cells),
        [VMEM] * (12 + N_TABLES),
        [scratch(window.shape), spectral, middle, pltpu.SemaphoreType.DMA((long // 8,))],
        flops=4 * 10**9,
        out_spec=(VMEM,) * 5 + (anywhere,),
    )(local, *wide, *narrow, inverses, answers, *weights, load_window, *tables)
    narrow = exchange("narrow", first_col, second_col)
    wide = exchange("wide", first_row, second_row)
    rows, cols, inner = call(
        functools.partial(inner_residual, box),
        (f32(2, across, deep), f32(2, long, 8, deep), cells),
        [VMEM] * 6,
        [
            scratch((long + 2, box.cols, deep)),
            scratch((long, box.cols, deep)),
            pltpu.SemaphoreType.DMA((long // 8,)),
        ],
        flops=10**9,
        out_spec=(VMEM, VMEM, anywhere),
    )(load, iterate, *weights)
    residual = call(
        functools.partial(outer_residual, box),
        cells,
        [VMEM] * 9 + [anywhere],
        [
            scratch((2, across - 16, deep)),
            scratch((2, long, 8, deep)),
            pltpu.SemaphoreType.DMA((4,)),
        ],
        out_spec=anywhere,
        aliases={9: 0},
    )(iterate, *wide, *narrow, to_long, to_across, rows, cols, inner)
    return result, residual


def solution(mesh):
    split = P(("groups", "wide"), "narrow", None)
    return jax.shard_map(
        on_device,
        mesh=mesh,
        in_specs=(split, split, P(), P(), split),
        out_specs=(split, split),
        check_vma=False,
    )
```

```python
import functools

import jax
import jax.numpy as jnp
import ml_dtypes
import numpy as np
from jax import lax
from jax.experimental import pallas as pl
from jax.experimental.pallas import tpu as pltpu
from jax.sharding import PartitionSpec as P

MARGIN = 4
REACH = MARGIN + 1
EDGE = 8

cheb_center = 1.3
cheb_radius = 1.2
cheb_ratio = 1.3 / 1.2
rho_first = 1.0 / cheb_ratio
rho_second = 1.0 / (2.0 * cheb_ratio - rho_first)
gain = 2.0 * rho_second / cheb_radius

MEANS = range(4)
BOX_DIAGONAL, LONG_HIGH, LONG_LOW, ACROSS_HIGH, ACROSS_LOW, LOAD_SUM = range(4, 10)
IMAGE_SUM, FLOW_LONG_HIGH, FLOW_LONG_LOW, FLOW_ACROSS_HIGH, FLOW_ACROSS_LOW = range(16, 21)

VMEM = pl.BlockSpec(memory_space=pltpu.VMEM)


def sine_basis(length):
    indices = np.arange(1, length + 1)
    phases = indices[:, None] * indices[None, :] % (2 * (length + 1))
    table = np.sqrt(2.0 / (length + 1)) * np.sin(np.pi * phases / (length + 1))
    eigvals = 4.0 * np.sin(np.pi * indices / (2.0 * (length + 1))) ** 2
    return table.astype(np.float32), eigvals.astype(np.float32)


def call(body, out_shape, in_specs, scratch=(), flops=0, out_spec=None, aliases=None):
    return pl.pallas_call(
        body,
        out_shape=out_shape,
        in_specs=in_specs,
        out_specs=out_spec or jax.tree.map(lambda _: VMEM, out_shape),
        scratch_shapes=list(scratch),
        compiler_params=pltpu.CompilerParams(vmem_limit_bytes=30 * 2**20),
        cost_estimate=pl.CostEstimate(flops=flops, bytes_accessed=0, transcendentals=0),
        input_output_aliases=aliases or {},
    )


def f32(*shape):
    return jax.ShapeDtypeStruct(shape, jnp.float32)


class Box:
    def __init__(self, shape):
        self.long, self.across, self.deep = shape
        self.ex = self.long + 2 * MARGIN
        self.ey = self.across + 2 * MARGIN
        self.rows = self.long + 2 * REACH
        self.cols = self.across + 2 * EDGE
        self.flat = self.rows * self.cols


def pieces(values, count):
    parts = []
    for _ in range(count - 1):
        scaled = values * 65537.0
        part = scaled - (scaled - values)
        parts.append(part)
        values = values - part
    return parts + [values]


def left_table(table, depth, count):
    rows, cols = table.shape
    wide = np.zeros((rows, depth), np.float32)
    wide[:, :cols] = table
    parts = []
    rest = wide
    for _ in range(count):
        part = rest.astype(ml_dtypes.bfloat16).astype(np.float32)
        parts.append(part)
        rest = rest - part
    blank = np.zeros_like(parts[0])
    lines = []
    for index in range(count):
        used = count - index if count > 2 else count
        lines.append(np.concatenate([parts[index]] * used + [blank] * (count - used), axis=1))
    return np.concatenate(lines, axis=0)


def right_tables(table):
    rest, parts = table, []
    for _ in range(3):
        part = rest.astype(ml_dtypes.bfloat16).astype(np.float32)
        parts.append(part)
        rest = rest - part
    both = np.concatenate([parts[0], parts[1]], axis=1)
    return np.concatenate([both, both], axis=0), np.concatenate([parts[2], parts[0]], axis=0)


def padded(size):
    return -(-size // 8) * 8


FORWARD, BACKWARD = 2, 3


def tables_of(box):
    sine_x, eig_x = sine_basis(box.ex)
    sine_y, eig_y = sine_basis(box.ey)
    sine_z, eig_z = sine_basis(box.deep)
    in_order_of_steps = np.arange(box.ey).reshape(8, box.ey // 8).T.reshape(-1)
    from_y = sine_y[MARGIN : MARGIN + box.across]
    from_x = sine_x[MARGIN : MARGIN + box.long]
    spread_x = np.broadcast_to(eig_x[:, None], (box.ex, box.deep))
    spread_y = np.broadcast_to(eig_y[:, None], (box.ey, box.deep))
    main_z, rest_z = right_tables(sine_z)
    return [
        jnp.asarray(np.ascontiguousarray(t))
        for t in (
            left_table(sine_y[:, in_order_of_steps], padded(box.ey), FORWARD),
            left_table(sine_x, padded(box.ex), FORWARD),
            left_table(from_x, padded(box.ex), BACKWARD),
            left_table(from_y, padded(box.ey), BACKWARD),
            main_z,
            rest_z,
            spread_x,
            spread_y,
            eig_z[None, :],
        )
    ]


N_TABLES = 9


def one_pass(left, right):
    return lax.dot_general(
        left,
        right,
        (((1,), (0,)), ((), ())),
        precision=lax.Precision.DEFAULT,
        preferred_element_type=jnp.float32,
    )


def dot_left(table, values, count, rows):
    total = one_pass(table, jnp.concatenate(pieces(values, count), axis=0))
    return sum(total[index * rows : (index + 1) * rows] for index in range(1, count)) + total[:rows]


def dot_right(values, main, rest, count):
    deep = values.shape[1]
    parts = pieces(values, count)
    total = one_pass(jnp.concatenate(parts[:2], axis=1), main)
    result = total[:, :deep] + total[:, deep:]
    if count == 3:
        result = result + one_pass(jnp.concatenate([parts[0], parts[2]], axis=1), rest)
    return result


def with_rows(values, rows):
    if values.shape[0] == rows:
        return values
    blank = jnp.zeros((rows - values.shape[0],) + values.shape[1:], values.dtype)
    return jnp.concatenate([values, blank], axis=0)


FORWARD_ROWS, COLS_ABREAST, BACKWARD_ROWS = 24, 40, 32


def fitting(size, wanted):
    return max(part for part in range(8, wanted + 1, 8) if size % part == 0)


def beside(values):
    return jnp.concatenate(values, axis=1)


def apart(values, lanes):
    return [values[:, start : start + lanes] for start in range(0, values.shape[1], lanes)]


def box_solve(box, source, divided, tables, row_mask, col_mask, spectral, middle, emit):
    into_y, into_x, from_x, from_y, main_z, rest_z = tables[:6]
    deep = box.deep
    deep_x, deep_y = padded(box.ex), padded(box.ey)
    into_y, into_x = into_y[...], into_x[...]
    if col_mask is not None:
        mask = jnp.concatenate([col_mask] * FORWARD, axis=1)
        into_y = into_y * mask
        mask = jnp.concatenate([row_mask] * FORWARD, axis=1)
        into_x = into_x * mask
    from_x, from_y, main_z, rest_z = from_x[...], from_y[...], main_z[...], rest_z[...]
    spectral_flat = spectral.reshape(box.ey * deep_x, deep)
    middle_flat = middle.reshape(box.long * deep_y, deep)
    if deep_x > box.ex:
        spectral[:, box.ex :, :] = jnp.zeros((box.ey, deep_x - box.ex, deep), jnp.float32)
    if deep_y > box.ey:
        middle[:, box.ey :, :] = jnp.zeros((box.long, deep_y - box.ey, deep), jnp.float32)
    step = fitting(box.ex, FORWARD_ROWS)
    for start in range(0, box.ex, step):
        block = jnp.concatenate([source(row) for row in range(start, start + step, 8)], axis=0)
        block = dot_right(block.reshape(step * box.ey, deep), main_z, rest_z, FORWARD)
        block = block.reshape(step, box.ey, deep)
        wide = beside([block[row] for row in range(step)])
        wide = dot_left(into_y, with_rows(wide, deep_y), FORWARD, box.ey)
        for row, values in enumerate(apart(wide, deep)):
            spectral_flat[pl.ds(start + row, box.ey, stride=deep_x), :] = values
    step = fitting(box.ey, COLS_ABREAST)
    for start in range(0, box.ey, step):
        wide = beside([spectral[col] for col in range(start, start + step)])
        wide = apart(dot_left(into_x, wide, FORWARD, box.ex), deep)
        wide = beside([divided(values, start + part) for part, values in enumerate(wide)])
        wide = dot_left(from_x, with_rows(wide, deep_x), BACKWARD, box.long)
        for part, values in enumerate(apart(wide, deep)):
            middle_flat[pl.ds(start + part, box.long, stride=deep_y), :] = values
    step = fitting(box.long, BACKWARD_ROWS)
    for start in range(0, box.long, step):
        wide = beside([middle[row] for row in range(start, start + step)])
        parts = apart(dot_left(from_y, wide, BACKWARD, box.across), deep)
        values = dot_right(jnp.concatenate(parts, axis=0), main_z, rest_z, BACKWARD)
        for row in range(0, step, 8):
            emit(start + row, values[row * box.across : (row + 8) * box.across])


def position():
    long_pos, across_pos = lax.axis_index("wide"), lax.axis_index("narrow")
    return long_pos, across_pos, lax.axis_size("wide"), lax.axis_size("narrow")


def as_float(flag):
    return jnp.where(flag, jnp.float32(1.0), jnp.float32(0.0))


def is_even(axis):
    return lax.rem(lax.axis_index(axis), 2) == 0


class Sides:
    def __init__(self, axis, first, second):
        position = lax.axis_index(axis)
        self.even = is_even(axis)
        self.has_low = as_float(position > 0)
        self.has_high = as_float(position < lax.axis_size(axis) - 1)
        self.first, self.second = first, second

    def low(self, *index):
        return jnp.where(self.even, self.second[index], self.first[index]) * self.has_low

    def high(self, *index):
        return jnp.where(self.even, self.first[index], self.second[index]) * self.has_high


def in_order(even, up, down):
    return jnp.where(even, up, down), jnp.where(even, down, up)


def row_of(stride, col, count, first=0):
    return pl.ds(first * stride + col, count, stride=stride)


def pack_columns(box, fields, wide_sides, wide, first, second):
    corner = len(fields) * wide * box.long
    even = is_even("narrow")
    place = 0
    for field, sides in zip(fields, wide_sides):
        for step in range(wide):
            cols = (box.across - wide + step, step)
            values = [field[row_of(box.across, col, box.long), :] for col in cols]
            low = [sides.low(row_of(box.across, col, wide), slice(None)) for col in cols]
            high = [sides.high(row_of(box.across, col, wide), slice(None)) for col in cols]
            at = corner + 2 * REACH * place
            for start, parts in ((place * box.long, values), (at, low), (at + REACH, high)):
                parts = in_order(even, *(part.astype(jnp.float32) for part in parts))
                size = parts[0].shape[0]
                first[start : start + size, :], second[start : start + size, :] = parts
            place += 1


def message_rows(box, count):
    return -(-(count * (box.long + 2 * REACH)) // 8) * 8


def pack_fields(box, wide, fields, tables, after, *refs):
    own, (low, high), refs = refs[:fields], refs[fields : fields + 2], refs[fields + 2 :]
    parts, (first, second, *table) = refs[:tables], refs[tables + after :]
    size = wide * box.across
    flat = [field.reshape(box.long * box.across, box.deep) for field in own]
    low = low.reshape(low.size // box.deep, box.deep)
    high = high.reshape(high.size // box.deep, box.deep)
    sides = [
        Sides("wide", *(ref.at[index * size : (index + 1) * size] for ref in (low, high)))
        for index in range(fields)
    ]
    pack_columns(box, flat, sides, wide, first, second)
    if tables:
        known = last_rows_merged(parts, table[0].shape[0])
        table[0][...] = known
        first[first.shape[0] - known.shape[0] :, :] = known
        second[second.shape[0] - known.shape[0] :, :] = known


def bring_edges(box, zone, scale, load, load_first, load_second, first, second, staged, sems):
    even = is_even("wide")

    def edges(wide):
        up, down = box.long - wide, 0
        return [pl.ds(jnp.where(even, *pair), wide) for pair in ((up, down), (down, up))]

    copies = [
        (zone.at[edges(REACH)[0]], staged.at[0]),
        (zone.at[edges(REACH)[1]], staged.at[1]),
        (load.at[edges(MARGIN)[0]], load_first),
        (load.at[edges(MARGIN)[1]], load_second),
        (scale.at[edges(REACH)[0]], first.at[:REACH]),
        (scale.at[edges(REACH)[1]], second.at[:REACH]),
    ]
    copies = [
        pltpu.make_async_copy(source, target, sems.at[index])
        for index, (source, target) in enumerate(copies)
    ]
    for copy in copies:
        copy.start()
    for copy in copies[:2]:
        copy.wait()
    first[REACH:] = staged[0].astype(jnp.float32)
    second[REACH:] = staged[1].astype(jnp.float32)
    for copy in copies[2:]:
        copy.wait()


def fill_window(box, window, own, wide_sides, narrow_sides, wide, place, total, add=None):
    flat = window.reshape(box.flat, box.deep)
    nothing = jnp.zeros((box.rows, EDGE, box.deep), jnp.float32)
    window[:, :EDGE, :] = nothing
    window[:, EDGE + box.across :, :] = nothing
    if add is None:
        add = lambda values, row_side, col_side: values
    inner = slice(EDGE, EDGE + box.across)
    first, last = REACH, REACH + box.long
    if wide < REACH:
        blank = jnp.zeros((1, box.across, box.deep), jnp.float32)
        window[0:1, inner, :] = blank
        window[box.rows - 1 :, inner, :] = blank
    window[first:last, inner, :] = add(own[...].astype(jnp.float32), 0, 0)
    window[first - wide : first, inner, :] = add(wide_sides.low(Ellipsis), -1, 0)
    window[last : last + wide, inner, :] = add(wide_sides.high(Ellipsis), 1, 0)
    corner = total * box.long
    for step in range(wide):
        for source, col, side in (
            (narrow_sides.low, EDGE - wide + step, -1),
            (narrow_sides.high, EDGE + box.across + step, 1),
        ):
            for start, size, row, row_side in (
                ((place + step) * box.long, box.long, first, 0),
                (corner + 2 * REACH * (place + step), wide, first - wide, -1),
                (corner + 2 * REACH * (place + step) + REACH, wide, last, 1),
            ):
                values = source(slice(start, start + size), slice(None))
                flat[row_of(box.cols, col, size, row), :] = add(values, row_side, side)


def some_cols(box, ref, row, step):
    stride = box.ey // 8
    return ref[row, pl.ds(EDGE - MARGIN + step, 8, stride=stride), :]


def negative_image(box, window, row, at, x, flow_before, weights):
    to_long, to_across, to_deep, mass = weights
    steps = range(box.ey // 8)
    x_next = [some_cols(box, window, row + 1, step) for step in range(-1, len(steps) + 1)]
    flow_long = [
        some_cols(box, to_long, at, step) * (x_next[step + 1] - x[step + 1]) for step in steps
    ]
    flow_across = [
        some_cols(box, to_across, at, step) * (x[step + 2] - x[step + 1])
        for step in range(-1, len(steps))
    ]
    totals = []
    for step in steps:
        here = x[step + 1]
        lanes = here.shape[1]
        flow_deep = some_cols(box, to_deep, at, step) * (pltpu.roll(here, lanes - 1, 1) - here)
        total = flow_long[step] - flow_before[step] - some_cols(box, mass, at, step) * here
        total = total + (flow_across[step + 1] - flow_across[step])
        totals.append(total + (flow_deep - pltpu.roll(flow_deep, 1, 1)))
    return totals, x_next, flow_long


def in_steps(box, refs, rows):
    return jnp.stack(
        [
            jnp.concatenate([some_cols(box, ref, row, step) for step in range(box.ey // 8)], axis=0)
            for ref, row in zip(refs, rows)
        ]
    )


def looked_up(labels, values):
    return jnp.where(labels == 0, values[0], jnp.where(labels == 1, values[1], values[2]))


def at_own_row(line, shape):
    long_pos, across_pos, _, across_count = position()
    rows = lax.broadcasted_iota(jnp.int32, shape, 0)
    own = rows == long_pos * across_count + across_pos
    return jnp.where(own, line[:1], jnp.zeros(shape, jnp.float32))


def merged(table, *others):
    for other in others:
        table = jnp.where(table != 0.0, table, other)
    return table


def last_rows_merged(refs, count):
    return merged(*(ref[ref.shape[0] - count :, :] for ref in refs))


def join_rows(table, message, out):
    out[...] = last_rows_merged((table, message), out.shape[0])


def line_of(numbers, shape):
    count = -(-len(numbers) // 8) * 8
    rows = lax.broadcasted_iota(jnp.int32, (count, shape[1]), 0)
    lanes = lax.broadcasted_iota(jnp.int32, (count, shape[1]), 1)
    stacked = jnp.zeros((count, shape[1]), jnp.float32)
    place = jnp.zeros((count, shape[1]), jnp.bool_)
    for row, (index, values) in enumerate(numbers):
        stacked = jnp.where(rows == row, values, stacked)
        place = place | ((rows == row) & (lanes == index))
    sums = jnp.sum(stacked, axis=1, keepdims=True)
    line = jnp.sum(jnp.where(place, sums, jnp.zeros_like(stacked)), axis=0, keepdims=True)
    return jnp.broadcast_to(line, shape)


def bring_box(
    box, far_load, far_scale, far_zone, after, diffusivity, decay, load, scale, zone, out, table, sems
):
    del after
    size = 8
    copies = []
    for start in range(0, box.long, size):
        rows = slice(start, start + size)
        for source, target in ((far_load, load), (far_scale, scale), (far_zone, zone)):
            copies.append(
                pltpu.make_async_copy(source.at[rows], target.at[rows], sems.at[len(copies)])
            )
            copies[-1].start()
    nothing = jnp.zeros((box.across, box.deep), jnp.float32)
    half = [[0.5 * diffusivity[z : z + 1, d : d + 1] for z in range(3)] for d in range(3)]
    rates = [decay[0:1, z : z + 1] for z in range(3)]

    def halves(row):
        labels, factor = zone[row], scale[row]
        return [looked_up(labels, half[d]) * factor for d in range(3)] + [looked_up(labels, rates)]

    sums = [nothing] * 5
    for start in range(0, box.long, size):
        for copy in copies[start // size * 3 : start // size * 3 + 3]:
            copy.wait()
        for row in range(start, start + size):
            sums = [total + more for total, more in zip(sums, halves(row) + [load[row]])]

    def total(values):
        return jnp.sum(values, axis=0, keepdims=True)

    cells = box.long * box.across * box.deep
    numbers = [(index, total(sums[index]) * (2.0 / cells)) for index in range(3)]
    mass = total(sums[3])
    numbers += [(3, mass / cells)]
    lane = lax.broadcasted_iota(jnp.int32, (1, box.deep), 1)
    ends = jnp.where((lane == 0) | (lane == box.deep - 1), total(sums[2]), 0.0)
    numbers += [
        (BOX_DIAGONAL, mass + ends),
        (LONG_HIGH, total(halves(box.long - 1)[0])),
        (LONG_LOW, total(halves(0)[0])),
        (ACROSS_HIGH, sums[1][box.across - 1 :]),
        (ACROSS_LOW, sums[1][:1]),
        (LOAD_SUM, total(sums[4])),
    ]
    line = line_of(numbers, out.shape)
    out[...] = line
    table[...] = at_own_row(line, table.shape)


def means_of(ref):
    return [ref[0:1, index : index + 1] for index in range(4)]


def first_solve(box, load, low, high, left, right, means, zone, scale, diffusivity, decay, *rest):
    tables = rest[:N_TABLES]
    window, local, image, inverses, spectral, middle = rest[N_TABLES:]
    spread_x, spread_y, eig_z = tables[6:]
    means = means_of(means)
    base = means[3] + means[0] * spread_x[...] + means[2] * eig_z[...]

    def divided(values, col):
        divisor = base + means[1] * spread_y[col : col + 1, :]
        inverse = pl.reciprocal(divisor, approx=True)
        for _ in range(2):
            inverse = inverse * (2.0 - divisor * inverse)
        inverses[col] = inverse
        return values * inverse

    half = [0.5 * diffusivity[z : z + 1, 2:3] for z in range(3)]
    rates = [decay[0:1, z : z + 1] for z in range(3)]
    lane = lax.broadcasted_iota(jnp.int32, (box.across, box.deep), 1)
    ends = jnp.where((lane == 0) | (lane == box.deep - 1), jnp.float32(1.0), jnp.float32(0.0))
    image[...] = jnp.zeros((box.across, box.deep), jnp.float32)
    wide_sides, narrow_sides = Sides("wide", low, high), Sides("narrow", left, right)
    fill_window(box, window, load, wide_sides, narrow_sides, MARGIN, 0, MARGIN)

    def emit(start, values):
        values = values * (1.0 / cheb_center)
        values = values.reshape(8, box.across, box.deep)
        local[start : start + 8] = values
        total = image[...]
        for row in range(8):
            labels = zone[start + row]
            mass = looked_up(labels, rates) + looked_up(labels, half) * scale[start + row] * ends
            total = total + mass * values[row]
        image[...] = total

    box_solve(
        box,
        lambda start: in_steps(box, [window] * 8, range(1 + start, 9 + start)),
        divided,
        tables,
        None,
        None,
        spectral,
        middle,
        emit,
    )


def side_weights(
    box, zone, scale, low, high, left, right, diffusivity, to_long, to_across, zone_window,
    scale_window
):
    for index, (window, own) in enumerate(((scale_window, scale), (zone_window, zone))):
        start = index * REACH
        wide_sides = Sides("wide", *(ref.at[start : start + REACH] for ref in (low, high)))
        narrow_sides = Sides("narrow", left, right)
        fill_window(box, window, own, wide_sides, narrow_sides, REACH, start, 2 * REACH)
    half = [[0.5 * diffusivity[z : z + 1, d : d + 1] for z in range(3)] for d in range(2)]

    def one_row(row, before):
        labels, factor = zone_window[row], scale_window[row]
        now = [looked_up(labels, half[d]) * factor for d in range(2)]
        to_across[row] = now[1] + pltpu.roll(now[1], box.cols - 1, 0)
        to_long[max(row - 1, 0)] = before + now[0]
        return now[0]

    before = jnp.zeros((box.cols, box.deep), jnp.float32)
    for row in range(box.rows):
        before = one_row(row, before)
    to_long[box.rows - 1] = before


def deep_weights(box, zone_window, scale_window, diffusivity, decay, to_deep, mass):
    half = [0.5 * diffusivity[z : z + 1, 2:3] for z in range(3)]
    rates = [decay[0:1, z : z + 1] for z in range(3)]
    lane = lax.broadcasted_iota(jnp.int32, (box.cols, box.deep), 1)
    ends = jnp.where((lane == 0) | (lane == box.deep - 1), jnp.float32(1.0), jnp.float32(0.0))
    not_last = jnp.where(lane == box.deep - 1, jnp.float32(0.0), jnp.float32(1.0))

    def one_row(row):
        labels = zone_window[row]
        now = looked_up(labels, half) * scale_window[row]
        to_deep[row] = (now + pltpu.roll(now, box.deep - 1, 1)) * not_last
        mass[row] = looked_up(labels, rates) + now * ends

    for row in range(box.rows):
        one_row(row)


def image_sums(
    box, zone, scale, local, image, low, high, left, right, table, diffusivity, out, up, down
):
    half = [[0.5 * diffusivity[z : z + 1, d : d + 1] for z in range(3)] for d in range(3)]
    shape = (box.long * box.across, box.deep)
    zone_flat, scale_flat, local_flat = zone.reshape(shape), scale.reshape(shape), local.reshape(shape)
    last_col = row_of(box.across, box.across - 1, box.long)
    first_col = row_of(box.across, 0, box.long)

    wide_sides, narrow_sides = Sides("wide", low, high), Sides("narrow", left, right)

    def side(source, place):
        return source(slice(place * box.long, (place + 1) * box.long), slice(None))

    above, below = wide_sides.high, wide_sides.low
    faces = [
        (0, zone[box.long - 1], scale[box.long - 1], local[box.long - 1], above(REACH), above(0)),
        (0, zone[0], scale[0], local[0], below(2 * REACH - 1), below(REACH - 1)),
        (
            1,
            zone_flat[last_col, :],
            scale_flat[last_col, :],
            local_flat[last_col, :],
            side(narrow_sides.high, REACH),
            side(narrow_sides.high, 0),
        ),
        (
            1,
            zone_flat[first_col, :],
            scale_flat[first_col, :],
            local_flat[first_col, :],
            side(narrow_sides.low, 2 * REACH - 1),
            side(narrow_sides.low, REACH - 1),
        ),
    ]
    flows = []
    for direction, labels, factor, values, far_labels, far_factor in faces:
        weight = looked_up(labels, half[direction]) * factor
        weight = weight + looked_up(far_labels, half[direction]) * far_factor
        flows.append(jnp.sum(weight * values, axis=0, keepdims=True))
    long_pos, across_pos, long_count, across_count = position()
    numbers = [
        (IMAGE_SUM, jnp.sum(image[...], axis=0, keepdims=True) + sum(flows)),
        (FLOW_LONG_HIGH, flows[0] * as_float(long_pos < long_count - 1)),
        (FLOW_LONG_LOW, flows[1] * as_float(long_pos > 0)),
        (FLOW_ACROSS_HIGH, flows[2] * as_float(across_pos < across_count - 1)),
        (FLOW_ACROSS_LOW, flows[3] * as_float(across_pos > 0)),
    ]
    known = table[...] + at_own_row(line_of(numbers, (8, out.shape[1])), out.shape)
    out[...] = known
    edge = REACH * box.across
    even = is_even("wide")
    for target, pair in ((up, (box.long - REACH, 0)), (down, (0, box.long - REACH))):
        target[:edge] = local[pl.ds(jnp.where(even, *pair), REACH)].reshape(edge, box.deep)
        target[edge:] = known


def column(values, index):
    return values[:, index : index + 1]


def uncoupled_groups(count, across):
    places = np.arange(count)
    long_step = np.abs(places[:, None] // across - places[None, :] // across)
    across_step = np.abs(places[:, None] % across - places[None, :] % across)
    coupled = long_step + across_step == 1
    left = list(range(count))
    groups = []
    while left:
        group = []
        for place in sorted(left, key=lambda p: (coupled[p][left].sum(), p)):
            if not coupled[place][group].any():
                group.append(place)
        left = [place for place in left if place not in group]
        for place in group:
            beside = [other for other in left if coupled[place][other]]
            for other in beside:
                coupled[other][beside] = True
                coupled[other][other] = False
        groups.append(group)
    return groups


def coarse_inverse(numbers, work):
    count, width = work.shape
    across = lax.axis_size("narrow")
    beyond = pltpu.roll(numbers, count - across, 0)
    beside = pltpu.roll(numbers, count - 1, 0)
    before = pltpu.roll(numbers, across, 0)
    ahead = pltpu.roll(numbers, 1, 0)
    place = lax.broadcasted_iota(jnp.int32, (count, 1), 0)
    across_pos = lax.rem(place, across)
    nothing = jnp.zeros((count, 1), jnp.float32)
    couplings = []
    diagonal = column(numbers, BOX_DIAGONAL)
    for own, other, there, inside in (
        (LONG_HIGH, LONG_LOW, beyond, place < count - across),
        (LONG_LOW, LONG_HIGH, before, place >= across),
        (ACROSS_HIGH, ACROSS_LOW, beside, across_pos < across - 1),
        (ACROSS_LOW, ACROSS_HIGH, ahead, across_pos > 0),
    ):
        shared = jnp.where(inside, column(there, other), nothing)
        diagonal = diagonal + column(numbers, own) + shared
        couplings.append(jnp.where(inside, column(numbers, own) + shared, nothing))
    rows = lax.broadcasted_iota(jnp.int32, (count, width), 0)
    cols = lax.broadcasted_iota(jnp.int32, (count, width), 1)
    blank = jnp.zeros((count, width), jnp.float32)
    matrix = jnp.where(cols == rows, diagonal, blank)
    for shift, coupling in zip((across, -across, 1, -1), couplings):
        matrix = matrix - jnp.where((cols == rows + shift) & (cols < count), coupling, blank)
    matrix = jnp.where(cols == rows + count, jnp.ones((count, 1), jnp.float32), matrix)
    if count <= 16:
        for group in uncoupled_groups(count, across):
            rest = matrix
            for step in group:
                pivot_row = matrix[step : step + 1, :] / matrix[step : step + 1, step : step + 1]
                rest = rest - matrix[:, step : step + 1] * pivot_row
                rest = jnp.where(rows == step, pivot_row, rest)
            matrix = rest
        return pltpu.roll(matrix, width - count, 1)
    work[...] = matrix

    def eliminate(step, _):
        values = work[...]
        pivot_row = work[pl.ds(step, 1), :]
        at_step = cols == step
        factors = jnp.sum(jnp.where(at_step, values, blank), axis=1, keepdims=True)
        pivot = jnp.sum(jnp.where(at_step[:1], pivot_row, blank[:1]), axis=1, keepdims=True)
        pivot_row = pivot_row / pivot
        work[...] = jnp.where(rows == step, pivot_row, values - factors * pivot_row)
        return 0

    lax.fori_loop(0, count, eliminate, 0)
    values = work[...]
    if count % 128:
        return pltpu.roll(values, width - count, 1)
    return values[:, count : 2 * count]


def answer(inverse, sums):
    return jnp.sum(inverse * sums, axis=0, keepdims=True)


def at_box(values, row_side, col_side):
    long_pos, across_pos, long_count, across_count = position()
    there_long, there_across = long_pos + row_side, across_pos + col_side
    inside = (
        (there_long >= 0)
        & (there_long < long_count)
        & (there_across >= 0)
        & (there_across < across_count)
    )
    lanes = lax.broadcasted_iota(jnp.int32, values.shape, 1)
    wanted = (lanes == there_long * across_count + there_across) & inside
    return jnp.sum(jnp.where(wanted, values, jnp.zeros_like(values)), axis=1, keepdims=True)


def coarse_corrections(parts, *refs):
    table_parts, (out, work) = refs[:parts], refs[parts:]
    count = work.shape[0]
    numbers = last_rows_merged(table_parts, count)
    across_count = lax.axis_size("narrow")
    inverse = coarse_inverse(numbers, work)
    sums = column(numbers, IMAGE_SUM)
    sums = sums - column(pltpu.roll(numbers, count - across_count, 0), FLOW_LONG_LOW)
    sums = sums - column(pltpu.roll(numbers, across_count, 0), FLOW_LONG_HIGH)
    sums = sums - column(pltpu.roll(numbers, count - 1, 0), FLOW_ACROSS_LOW)
    sums = sums - column(pltpu.roll(numbers, 1, 0), FLOW_ACROSS_HIGH)
    load_sums = column(numbers, LOAD_SUM)
    sums = load_sums * (1.0 - 1.0 / cheb_center) - sums
    out[0:1, :] = answer(inverse, load_sums) * (1.0 / cheb_center)
    out[1:2, :] = answer(inverse, sums) * gain


def second_solve(box, local, low, high, left, right, inverses, answers, *rest):
    to_long, to_across, to_deep, mass, load_window = rest[:5]
    tables = rest[5 : 5 + N_TABLES]
    iterate, top, bottom, last_col, first_col, out = rest[5 + N_TABLES : 11 + N_TABLES]
    window, spectral, middle, sems = rest[11 + N_TABLES :]
    long_pos, across_pos, long_count, across_count = position()
    coarse = answers[0:1, :]
    own_shift = at_box(answers[1:2, :], 0, 0)
    shifts = {
        (row_side, col_side): at_box(coarse, row_side, col_side)
        for row_side in (-1, 0, 1)
        for col_side in (-1, 0, 1)
    }

    def add(values, row_side, col_side):
        shift = shifts[row_side, col_side]
        if values.ndim == 3:
            shift = shift.reshape(1, 1, 1)
        return values + shift

    edge = REACH * box.across
    low, high = (
        ref.at[:edge].reshape(REACH, box.across, box.deep) for ref in (low, high)
    )
    wide_sides, narrow_sides = Sides("wide", low, high), Sides("narrow", left, right)
    fill_window(box, window, local, wide_sides, narrow_sides, REACH, 0, REACH, add)
    weights = (to_long, to_across, to_deep, mass)

    steps = range(box.ey // 8)
    x = [some_cols(box, window, 1, step) for step in range(-1, len(steps) + 1)]
    flow = [
        some_cols(box, to_long, 0, step) * (x[step + 1] - some_cols(box, window, 0, step))
        for step in steps
    ]
    state = [x, flow]

    def divided(values, col):
        return values * inverses[col]

    def residual(start_row):
        rows = []
        for row in range(start_row + 1, start_row + 9):
            image, *state[:] = negative_image(box, window, row, row, *state, weights)
            image = [some_cols(box, load_window, row, step) + image[step] for step in steps]
            rows.append(jnp.concatenate(image, axis=0))
        return jnp.stack(rows)

    inner = slice(EDGE, EDGE + box.across)
    first = REACH
    row_ids = lax.broadcasted_iota(jnp.int32, (1, padded(box.ex)), 1)
    col_ids = lax.broadcasted_iota(jnp.int32, (1, padded(box.ey)), 1)
    col_ids = (col_ids & 7) * (box.ey // 8) + lax.shift_right_logical(col_ids, 3)
    row_mask = jnp.where(row_ids < MARGIN, as_float(long_pos > 0), 1.0)
    row_mask = jnp.where(row_ids >= MARGIN + box.long, as_float(long_pos < long_count - 1), row_mask)
    col_mask = jnp.where(col_ids < MARGIN, as_float(across_pos > 0), 1.0)
    col_mask = jnp.where(
        col_ids >= MARGIN + box.across, as_float(across_pos < across_count - 1), col_mask
    )
    keep = 1.0 + rho_second * rho_first
    copies = []

    def emit(start, values):
        rows = values.reshape(8, box.across, box.deep)
        before = window[first + start : first + start + 8, inner, :]
        shift = own_shift.reshape(1, 1, 1)
        iterate[start : start + 8] = keep * before + (gain * rows + shift)
        copies.append(
            pltpu.make_async_copy(
                iterate.at[start : start + 8], out.at[start : start + 8], sems.at[len(copies)]
            )
        )
        copies[-1].start()

    box_solve(
        box, residual, divided, tables, row_mask, col_mask, spectral, middle, emit
    )
    rows = in_order(is_even("wide"), iterate[box.long - 1], iterate[0])
    top[...], bottom[...] = rows
    flat = iterate.reshape(box.long * box.across, box.deep)
    cols = [flat[row_of(box.across, col, box.long), :] for col in (box.across - 1, 0)]
    last_col[...], first_col[...] = in_order(is_even("narrow"), *cols)
    for copy in copies:
        copy.wait()


def inner_residual(
    box, load, iterate, to_long, to_across, to_deep, mass, rows, cols, out, window, result, sems
):
    inner = slice(EDGE, EDGE + box.across)
    flat = window.reshape((box.long + 2) * box.cols, box.deep)
    iterate_flat = iterate.reshape(box.long * box.across, box.deep)
    blank = jnp.zeros((box.long + 2, EDGE, box.deep), jnp.float32)
    window[:, :EDGE, :] = blank
    window[:, EDGE + box.across :, :] = blank
    window[1 : 1 + box.long, inner, :] = iterate[...]
    window[0, inner, :] = iterate[0]
    window[1 + box.long, inner, :] = iterate[box.long - 1]
    for col, place in ((0, EDGE - 1), (box.across - 1, EDGE + box.across)):
        values = iterate_flat[row_of(box.across, col, box.long), :]
        flat[row_of(box.cols, place, box.long, 1), :] = values
    weights = (to_long, to_across, to_deep, mass)
    steps = range(box.ey // 8)
    x = [some_cols(box, window, 1, step) for step in range(-1, len(steps) + 1)]
    flow = [jnp.zeros((8, box.deep), jnp.float32) for _ in steps]
    middle = slice(8, box.across - 8)
    copies = []
    for row in range(box.long):
        image, x, flow = negative_image(box, window, row + 1, REACH + row, x, flow, weights)
        for step in steps:
            place = pl.ds(EDGE - MARGIN + step, 8, stride=box.ey // 8)
            result[row, place, :] = image[step]
        values = load[row] + result[row, inner]
        result[row, inner] = values
        cols[0, row] = values[:8]
        cols[1, row] = values[box.across - 8 :]
        if row == 0:
            rows[0] = values
        if row == box.long - 1:
            rows[1] = values
        if row % 8 == 7:
            part = slice(row - 7, row + 1)
            copy = pltpu.make_async_copy(
                result.at[part, EDGE + 8 : EDGE + box.across - 8],
                out.at[part, middle],
                sems.at[row // 8],
            )
            copy.start()
            copies.append(copy)
    for copy in copies:
        copy.wait()


def outer_residual(
    box, iterate, low, high, left, right, to_long, to_across, rows, cols, inner_out, out,
    row_part, col_part, sems
):
    del inner_out
    inner = slice(EDGE, EDGE + box.across)
    middle = slice(8, box.across - 8)
    wide_sides, narrow_sides = Sides("wide", low, high), Sides("narrow", left, right)
    last = box.long - 1
    iterate_flat = iterate.reshape(box.long * box.across, box.deep)
    across_flat = to_across.reshape(box.flat, box.deep)
    below = to_long[REACH - 1, inner] * (wide_sides.low(Ellipsis) - iterate[0])
    above = to_long[REACH + last, inner] * (wide_sides.high(Ellipsis) - iterate[last])
    row_part[0] = (rows[0] + below)[middle]
    row_part[1] = (rows[1] + above)[middle]
    copies = [
        pltpu.make_async_copy(row_part.at[0], out.at[0, middle], sems.at[0]),
        pltpu.make_async_copy(row_part.at[1], out.at[last, middle], sems.at[1]),
    ]
    for copy in copies:
        copy.start()
    col_part[...] = cols[...]
    flat = col_part.reshape(2 * box.long * 8, box.deep)
    for side, (from_side, col, face, tile) in enumerate(
        (
            (narrow_sides.low, 0, EDGE - 1, slice(0, 8)),
            (narrow_sides.high, box.across - 1, EDGE + box.across - 1, slice(box.across - 8, None)),
        )
    ):
        weight = across_flat[row_of(box.cols, face, box.long, REACH), :]
        own = iterate_flat[row_of(box.across, col, box.long), :]
        place = pl.ds(side * box.long * 8 + side * 7, box.long, stride=8)
        flat[place, :] = flat[place, :] + weight * (from_side(Ellipsis) - own)
        col_part[side, 0] = col_part[side, 0] + below[tile]
        col_part[side, last] = col_part[side, last] + above[tile]
        first_col = side * (box.across - 8)
        copy = pltpu.make_async_copy(
            col_part.at[side], out.at[:, first_col : first_col + 8], sems.at[2 + side]
        )
        copy.start()
        copies.append(copy)
    for copy in copies:
        copy.wait()


def swaps(axis):
    sizes = (lax.axis_size("wide"), lax.axis_size("narrow"))
    along = ("wide", "narrow").index(axis)
    size, beside = sizes[along], sizes[1 - along]

    def number(place, other_place):
        pair = (place, other_place) if along == 0 else (other_place, place)
        return pair[0] * sizes[1] + pair[1]

    ways = []
    for way in range(2):
        pairs = []
        for place in range(size):
            for other_place in range(beside):
                partner = place + 1 if place % 2 == way else place - 1
                there = other_place
                if not 0 <= partner < size:
                    partner = place
                    there = other_place ^ 1 if beside % 2 == 0 else other_place
                pairs.append((number(place, other_place), number(partner, there)))
        ways.append(pairs)
    return ways


def exchange(axis, first, second):
    ways = swaps(axis)
    axes = ("wide", "narrow")
    return lax.ppermute(first, axes, ways[0]), lax.ppermute(second, axes, ways[1])


def from_other_end(axis, table):
    size = lax.axis_size(axis)
    return lax.ppermute(table, axis, [(i, size - 1 - i) for i in range(size)])


def two_away(axis, table):
    size = lax.axis_size(axis)
    return lax.ppermute(table, axis, [(i, (i + 2) % size) for i in range(size)])


def tell(table):
    count = table.shape[0]
    long_pos, across_pos, _, across_count = position()
    own = lax.dynamic_slice_in_dim(table, long_pos * across_count + across_pos, 1, axis=0)
    line = jnp.broadcast_to(own, (count, 1, 128))
    told = lax.all_to_all(line, ("wide", "narrow"), split_axis=0, concat_axis=0, tiled=True)
    return told.reshape(count, 128)


def on_device(zone, scale, diffusivity, decay, load):
    box = Box(load.shape)
    long, across, deep = load.shape
    count = lax.axis_size("wide") * lax.axis_size("narrow")
    by_margins = lax.axis_size("wide") == 4 and lax.axis_size("narrow") == 4
    tables = tables_of(box)
    decay = decay.reshape(1, -1)
    cells = f32(long, across, deep)
    whole_zone = jax.ShapeDtypeStruct(cells.shape, zone.dtype)
    window = f32(box.rows, box.cols, deep)
    table_shape = f32(count, 128)
    anywhere = pl.BlockSpec(memory_space=pl.ANY)
    in_hbm = pl.BlockSpec(memory_space=pltpu.HBM)

    def scratch(shape):
        return pltpu.VMEM(shape, jnp.float32)

    def pinned(field):
        return pltpu.with_memory_space_constraint(field, pltpu.HBM)

    spectral = scratch((box.ey, padded(box.ex), deep))
    middle = scratch((long, padded(box.ey), deep))

    def pack(wide, fields, sides, parts=(), after=()):
        rows = message_rows(box, wide * len(fields)) + (count if parts else 0)
        message = f32(rows, deep)
        body = functools.partial(pack_fields, box, wide, len(fields), len(parts), len(after))
        return call(
            body,
            (message, message) + ((table_shape,) if parts else ()),
            [VMEM] * (len(fields) + 2 + len(parts)) + [anywhere] * len(after),
        )(*fields, *sides, *parts, *after)

    far = f32(2 * REACH, across, deep)
    far_zone, far_scale, far_load = pinned(zone), pinned(scale), pinned(load)
    load_first, load_second, first, second = call(
        functools.partial(bring_edges, box),
        (f32(MARGIN, across, deep),) * 2 + (far, far),
        [in_hbm] * 3,
        [pltpu.VMEM((2, REACH, across, deep), zone.dtype), pltpu.SemaphoreType.DMA((6,))],
    )(far_zone, far_scale, far_load)
    load, scale, zone, sums, table = call(
        functools.partial(bring_box, box),
        (cells, cells, whole_zone, f32(8, 128), table_shape),
        [in_hbm] * 3 + [anywhere] + [VMEM] * 2,
        [pltpu.SemaphoreType.DMA((3 * (long // 8),))],
    )(far_load, far_scale, far_zone, load_first, diffusivity, decay)
    load_wide = exchange("wide", load_first, load_second)
    far_wide = exchange("wide", first, second)
    load_first, load_second = pack(MARGIN, [load], load_wide)
    load_narrow = exchange("narrow", load_first, load_second)
    far_narrow = exchange("narrow", *pack(REACH, [scale, zone], far_wide))
    load_window, local, image, inverses = call(
        functools.partial(first_solve, box),
        (window, cells, f32(across, deep), f32(box.ey, box.ex, deep)),
        [VMEM] * 8 + [VMEM] * 2 + [VMEM] * N_TABLES,
        [spectral, middle],
        flops=4 * 10**9,
    )(load, *load_wide, *load_narrow, sums, zone, scale, diffusivity, decay, *tables)
    message = f32(REACH * across + count, deep)
    table, first, second = call(
        functools.partial(image_sums, box), (table_shape, message, message), [VMEM] * 9 + [VMEM]
    )(zone, scale, local, image, *far_wide, *far_narrow, table, diffusivity)
    own_table = table
    wide = exchange("wide", first, second)
    parts = (table, wide[0])
    if by_margins:
        parts += (two_away("wide", table), from_other_end("wide", table))
    to_long, to_across, *windows = call(
        functools.partial(side_weights, box),
        (window,) * 4,
        [VMEM] * 6 + [VMEM],
        flops=10**9,
    )(zone, scale, *far_wide, *far_narrow, diffusivity)
    to_deep, mass = call(
        functools.partial(deep_weights, box),
        (window,) * 2,
        [VMEM] * 2 + [VMEM] * 2,
        flops=10**9,
    )(*windows, diffusivity, decay)
    weights = (to_long, to_across, to_deep, mass)
    first, second, table = pack(REACH, [local], wide, parts, [to_long])
    narrow = exchange("narrow", first, second)
    if by_margins:
        table = call(join_rows, table_shape, [VMEM] * 2)(table, narrow[0])
        parts = (table, two_away("narrow", table))
    else:
        parts = (tell(own_table),)
    row, col = f32(across, deep), f32(long, deep)
    answers = call(
        functools.partial(coarse_corrections, len(parts)),
        f32(8, -(-count // 128) * 128),
        [VMEM] * len(parts),
        [scratch((count, -(-2 * count // 128) * 128))],
    )(*parts)
    iterate, first_row, second_row, first_col, second_col, result = call(
        functools.partial(second_solve, box),
        (cells, row, row, col, col, cells),
        [VMEM] * (12 + N_TABLES),
        [scratch(window.shape), spectral, middle, pltpu.SemaphoreType.DMA((long // 8,))],
        flops=4 * 10**9,
        out_spec=(VMEM,) * 5 + (anywhere,),
    )(local, *wide, *narrow, inverses, answers, *weights, load_window, *tables)
    narrow = exchange("narrow", first_col, second_col)
    wide = exchange("wide", first_row, second_row)
    rows, cols, inner = call(
        functools.partial(inner_residual, box),
        (f32(2, across, deep), f32(2, long, 8, deep), cells),
        [VMEM] * 6,
        [
            scratch((long + 2, box.cols, deep)),
            scratch((long, box.cols, deep)),
            pltpu.SemaphoreType.DMA((long // 8,)),
        ],
        flops=10**9,
        out_spec=(VMEM, VMEM, anywhere),
    )(load, iterate, *weights)
    residual = call(
        functools.partial(outer_residual, box),
        cells,
        [VMEM] * 9 + [anywhere],
        [
            scratch((2, across - 16, deep)),
            scratch((2, long, 8, deep)),
            pltpu.SemaphoreType.DMA((4,)),
        ],
        out_spec=anywhere,
        aliases={9: 0},
    )(iterate, *wide, *narrow, to_long, to_across, rows, cols, inner)
    return result, residual


def solution(mesh):
    split = P(("groups", "wide"), "narrow", None)
    return jax.shard_map(
        on_device,
        mesh=mesh,
        in_specs=(split, split, P(), P(), split),
        out_specs=(split, split),
        check_vma=False,
    )
```

```python
import functools

import jax
import jax.numpy as jnp
import ml_dtypes
import numpy as np
from jax import lax
from jax.experimental import pallas as pl
from jax.experimental.pallas import tpu as pltpu
from jax.sharding import PartitionSpec as P

MARGIN = 4
REACH = MARGIN + 1
EDGE = 8

cheb_center = 1.3
cheb_radius = 1.2
cheb_ratio = 1.3 / 1.2
rho_first = 1.0 / cheb_ratio
rho_second = 1.0 / (2.0 * cheb_ratio - rho_first)
gain = 2.0 * rho_second / cheb_radius

MEANS = range(4)
BOX_DIAGONAL, LONG_HIGH, LONG_LOW, ACROSS_HIGH, ACROSS_LOW, LOAD_SUM = range(4, 10)
IMAGE_SUM, FLOW_LONG_HIGH, FLOW_LONG_LOW, FLOW_ACROSS_HIGH, FLOW_ACROSS_LOW = range(16, 21)

VMEM = pl.BlockSpec(memory_space=pltpu.VMEM)


def sine_basis(length):
    indices = np.arange(1, length + 1)
    phases = indices[:, None] * indices[None, :] % (2 * (length + 1))
    table = np.sqrt(2.0 / (length + 1)) * np.sin(np.pi * phases / (length + 1))
    eigvals = 4.0 * np.sin(np.pi * indices / (2.0 * (length + 1))) ** 2
    return table.astype(np.float32), eigvals.astype(np.float32)


def call(body, out_shape, in_specs, scratch=(), flops=0, out_spec=None, aliases=None):
    return pl.pallas_call(
        body,
        out_shape=out_shape,
        in_specs=in_specs,
        out_specs=out_spec or jax.tree.map(lambda _: VMEM, out_shape),
        scratch_shapes=list(scratch),
        compiler_params=pltpu.CompilerParams(vmem_limit_bytes=30 * 2**20),
        cost_estimate=pl.CostEstimate(flops=flops, bytes_accessed=0, transcendentals=0),
        input_output_aliases=aliases or {},
    )


def f32(*shape):
    return jax.ShapeDtypeStruct(shape, jnp.float32)


class Box:
    def __init__(self, shape):
        self.long, self.across, self.deep = shape
        self.ex = self.long + 2 * MARGIN
        self.ey = self.across + 2 * MARGIN
        self.rows = self.long + 2 * REACH
        self.cols = self.across + 2 * EDGE
        self.flat = self.rows * self.cols


def pieces(values, count):
    parts = []
    for _ in range(count - 1):
        scaled = values * 65537.0
        part = scaled - (scaled - values)
        parts.append(part)
        values = values - part
    return parts + [values]


def left_table(table, depth, count):
    rows, cols = table.shape
    wide = np.zeros((rows, depth), np.float32)
    wide[:, :cols] = table
    parts = []
    rest = wide
    for _ in range(count):
        part = rest.astype(ml_dtypes.bfloat16).astype(np.float32)
        parts.append(part)
        rest = rest - part
    blank = np.zeros_like(parts[0])
    lines = []
    for index in range(count):
        used = count - index if count > 2 else count
        lines.append(np.concatenate([parts[index]] * used + [blank] * (count - used), axis=1))
    return np.concatenate(lines, axis=0)


def right_tables(table):
    rest, parts = table, []
    for _ in range(3):
        part = rest.astype(ml_dtypes.bfloat16).astype(np.float32)
        parts.append(part)
        rest = rest - part
    both = np.concatenate([parts[0], parts[1]], axis=1)
    return np.concatenate([both, both], axis=0), np.concatenate([parts[2], parts[0]], axis=0)


def padded(size):
    return -(-size // 8) * 8


FORWARD, BACKWARD = 2, 3


def tables_of(box):
    sine_x, eig_x = sine_basis(box.ex)
    sine_y, eig_y = sine_basis(box.ey)
    sine_z, eig_z = sine_basis(box.deep)
    in_order_of_steps = np.arange(box.ey).reshape(8, box.ey // 8).T.reshape(-1)
    from_y = sine_y[MARGIN : MARGIN + box.across]
    from_x = sine_x[MARGIN : MARGIN + box.long]
    spread_x = np.broadcast_to(eig_x[:, None], (box.ex, box.deep))
    spread_y = np.broadcast_to(eig_y[:, None], (box.ey, box.deep))
    main_z, rest_z = right_tables(sine_z)
    return [
        jnp.asarray(np.ascontiguousarray(t))
        for t in (
            left_table(sine_y[:, in_order_of_steps], padded(box.ey), FORWARD),
            left_table(sine_x, padded(box.ex), FORWARD),
            left_table(from_x, padded(box.ex), BACKWARD),
            left_table(from_y, padded(box.ey), BACKWARD),
            main_z,
            rest_z,
            spread_x,
            spread_y,
            eig_z[None, :],
        )
    ]


N_TABLES = 9


def one_pass(left, right):
    return lax.dot_general(
        left,
        right,
        (((1,), (0,)), ((), ())),
        precision=lax.Precision.DEFAULT,
        preferred_element_type=jnp.float32,
    )


def dot_left(table, values, count, rows):
    total = one_pass(table, jnp.concatenate(pieces(values, count), axis=0))
    return sum(total[index * rows : (index + 1) * rows] for index in range(1, count)) + total[:rows]


def dot_right(values, main, rest, count):
    deep = values.shape[1]
    parts = pieces(values, count)
    total = one_pass(jnp.concatenate(parts[:2], axis=1), main)
    result = total[:, :deep] + total[:, deep:]
    if count == 3:
        result = result + one_pass(jnp.concatenate([parts[0], parts[2]], axis=1), rest)
    return result


def with_rows(values, rows):
    if values.shape[0] == rows:
        return values
    blank = jnp.zeros((rows - values.shape[0],) + values.shape[1:], values.dtype)
    return jnp.concatenate([values, blank], axis=0)


FORWARD_ROWS, COLS_ABREAST, BACKWARD_ROWS = 24, 40, 32


def fitting(size, wanted):
    return max(part for part in range(8, wanted + 1, 8) if size % part == 0)


def beside(values):
    return jnp.concatenate(values, axis=1)


def apart(values, lanes):
    return [values[:, start : start + lanes] for start in range(0, values.shape[1], lanes)]


def box_solve(box, source, divided, tables, row_mask, col_mask, spectral, middle, emit):
    into_y, into_x, from_x, from_y, main_z, rest_z = tables[:6]
    deep = box.deep
    deep_x, deep_y = padded(box.ex), padded(box.ey)
    into_y, into_x = into_y[...], into_x[...]
    if col_mask is not None:
        mask = jnp.concatenate([col_mask] * FORWARD, axis=1)
        into_y = into_y * mask
        mask = jnp.concatenate([row_mask] * FORWARD, axis=1)
        into_x = into_x * mask
    from_x, from_y, main_z, rest_z = from_x[...], from_y[...], main_z[...], rest_z[...]
    spectral_flat = spectral.reshape(box.ey * deep_x, deep)
    middle_flat = middle.reshape(box.long * deep_y, deep)
    if deep_x > box.ex:
        spectral[:, box.ex :, :] = jnp.zeros((box.ey, deep_x - box.ex, deep), jnp.float32)
    if deep_y > box.ey:
        middle[:, box.ey :, :] = jnp.zeros((box.long, deep_y - box.ey, deep), jnp.float32)
    step = fitting(box.ex, FORWARD_ROWS)
    for start in range(0, box.ex, step):
        block = jnp.concatenate([source(row) for row in range(start, start + step, 8)], axis=0)
        block = dot_right(block.reshape(step * box.ey, deep), main_z, rest_z, FORWARD)
        block = block.reshape(step, box.ey, deep)
        wide = beside([block[row] for row in range(step)])
        wide = dot_left(into_y, with_rows(wide, deep_y), FORWARD, box.ey)
        for row, values in enumerate(apart(wide, deep)):
            spectral_flat[pl.ds(start + row, box.ey, stride=deep_x), :] = values
    step = fitting(box.ey, COLS_ABREAST)
    for start in range(0, box.ey, step):
        wide = beside([spectral[col] for col in range(start, start + step)])
        wide = apart(dot_left(into_x, wide, FORWARD, box.ex), deep)
        wide = beside([divided(values, start + part) for part, values in enumerate(wide)])
        wide = dot_left(from_x, with_rows(wide, deep_x), BACKWARD, box.long)
        for part, values in enumerate(apart(wide, deep)):
            middle_flat[pl.ds(start + part, box.long, stride=deep_y), :] = values
    step = fitting(box.long, BACKWARD_ROWS)
    for start in range(0, box.long, step):
        wide = beside([middle[row] for row in range(start, start + step)])
        parts = apart(dot_left(from_y, wide, BACKWARD, box.across), deep)
        values = dot_right(jnp.concatenate(parts, axis=0), main_z, rest_z, BACKWARD)
        for row in range(0, step, 8):
            emit(start + row, values[row * box.across : (row + 8) * box.across])


def position():
    long_pos, across_pos = lax.axis_index("wide"), lax.axis_index("narrow")
    return long_pos, across_pos, lax.axis_size("wide"), lax.axis_size("narrow")


def as_float(flag):
    return jnp.where(flag, jnp.float32(1.0), jnp.float32(0.0))


def is_even(axis):
    return lax.rem(lax.axis_index(axis), 2) == 0


class Sides:
    def __init__(self, axis, first, second):
        position = lax.axis_index(axis)
        self.even = is_even(axis)
        self.has_low = as_float(position > 0)
        self.has_high = as_float(position < lax.axis_size(axis) - 1)
        self.first, self.second = first, second

    def low(self, *index):
        return jnp.where(self.even, self.second[index], self.first[index]) * self.has_low

    def high(self, *index):
        return jnp.where(self.even, self.first[index], self.second[index]) * self.has_high


def in_order(even, up, down):
    return jnp.where(even, up, down), jnp.where(even, down, up)


def row_of(stride, col, count, first=0):
    return pl.ds(first * stride + col, count, stride=stride)


def pack_columns(box, fields, wide_sides, wide, first, second):
    corner = len(fields) * wide * box.long
    even = is_even("narrow")
    place = 0
    for field, sides in zip(fields, wide_sides):
        for step in range(wide):
            cols = (box.across - wide + step, step)
            values = [field[row_of(box.across, col, box.long), :] for col in cols]
            low = [sides.low(row_of(box.across, col, wide), slice(None)) for col in cols]
            high = [sides.high(row_of(box.across, col, wide), slice(None)) for col in cols]
            at = corner + 2 * REACH * place
            for start, parts in ((place * box.long, values), (at, low), (at + REACH, high)):
                parts = in_order(even, *(part.astype(jnp.float32) for part in parts))
                size = parts[0].shape[0]
                first[start : start + size, :], second[start : start + size, :] = parts
            place += 1


def message_rows(box, count):
    return -(-(count * (box.long + 2 * REACH)) // 8) * 8


def pack_fields(box, wide, fields, tables, after, *refs):
    own, (low, high), refs = refs[:fields], refs[fields : fields + 2], refs[fields + 2 :]
    parts, (first, second, *table) = refs[:tables], refs[tables + after :]
    size = wide * box.across
    flat = [field.reshape(box.long * box.across, box.deep) for field in own]
    low = low.reshape(low.size // box.deep, box.deep)
    high = high.reshape(high.size // box.deep, box.deep)
    sides = [
        Sides("wide", *(ref.at[index * size : (index + 1) * size] for ref in (low, high)))
        for index in range(fields)
    ]
    pack_columns(box, flat, sides, wide, first, second)
    if tables:
        known = last_rows_merged(parts, table[0].shape[0])
        table[0][...] = known
        first[first.shape[0] - known.shape[0] :, :] = known
        second[second.shape[0] - known.shape[0] :, :] = known


def bring_edges(box, zone, scale, load, load_first, load_second, first, second, staged, sems):
    even = is_even("wide")

    def edges(wide):
        up, down = box.long - wide, 0
        return [pl.ds(jnp.where(even, *pair), wide) for pair in ((up, down), (down, up))]

    copies = [
        (zone.at[edges(REACH)[0]], staged.at[0]),
        (zone.at[edges(REACH)[1]], staged.at[1]),
        (load.at[edges(MARGIN)[0]], load_first),
        (load.at[edges(MARGIN)[1]], load_second),
        (scale.at[edges(REACH)[0]], first.at[:REACH]),
        (scale.at[edges(REACH)[1]], second.at[:REACH]),
    ]
    copies = [
        pltpu.make_async_copy(source, target, sems.at[index])
        for index, (source, target) in enumerate(copies)
    ]
    for copy in copies:
        copy.start()
    for copy in copies[:2]:
        copy.wait()
    first[REACH:] = staged[0].astype(jnp.float32)
    second[REACH:] = staged[1].astype(jnp.float32)
    for copy in copies[2:]:
        copy.wait()


def fill_window(box, window, own, wide_sides, narrow_sides, wide, place, total, add=None):
    flat = window.reshape(box.flat, box.deep)
    nothing = jnp.zeros((box.rows, EDGE, box.deep), jnp.float32)
    window[:, :EDGE, :] = nothing
    window[:, EDGE + box.across :, :] = nothing
    if add is None:
        add = lambda values, row_side, col_side: values
    inner = slice(EDGE, EDGE + box.across)
    first, last = REACH, REACH + box.long
    if wide < REACH:
        blank = jnp.zeros((1, box.across, box.deep), jnp.float32)
        window[0:1, inner, :] = blank
        window[box.rows - 1 :, inner, :] = blank
    window[first:last, inner, :] = add(own[...].astype(jnp.float32), 0, 0)
    window[first - wide : first, inner, :] = add(wide_sides.low(Ellipsis), -1, 0)
    window[last : last + wide, inner, :] = add(wide_sides.high(Ellipsis), 1, 0)
    corner = total * box.long
    for step in range(wide):
        for source, col, side in (
            (narrow_sides.low, EDGE - wide + step, -1),
            (narrow_sides.high, EDGE + box.across + step, 1),
        ):
            for start, size, row, row_side in (
                ((place + step) * box.long, box.long, first, 0),
                (corner + 2 * REACH * (place + step), wide, first - wide, -1),
                (corner + 2 * REACH * (place + step) + REACH, wide, last, 1),
            ):
                values = source(slice(start, start + size), slice(None))
                flat[row_of(box.cols, col, size, row), :] = add(values, row_side, side)


def some_cols(box, ref, row, step):
    stride = box.ey // 8
    return ref[row, pl.ds(EDGE - MARGIN + step, 8, stride=stride), :]


def negative_image(box, window, row, at, x, flow_before, weights):
    to_long, to_across, to_deep, mass = weights
    steps = range(box.ey // 8)
    x_next = [some_cols(box, window, row + 1, step) for step in range(-1, len(steps) + 1)]
    flow_long = [
        some_cols(box, to_long, at, step) * (x_next[step + 1] - x[step + 1]) for step in steps
    ]
    flow_across = [
        some_cols(box, to_across, at, step) * (x[step + 2] - x[step + 1])
        for step in range(-1, len(steps))
    ]
    totals = []
    for step in steps:
        here = x[step + 1]
        lanes = here.shape[1]
        flow_deep = some_cols(box, to_deep, at, step) * (pltpu.roll(here, lanes - 1, 1) - here)
        total = flow_long[step] - flow_before[step] - some_cols(box, mass, at, step) * here
        total = total + (flow_across[step + 1] - flow_across[step])
        totals.append(total + (flow_deep - pltpu.roll(flow_deep, 1, 1)))
    return totals, x_next, flow_long


def in_steps(box, refs, rows):
    return jnp.stack(
        [
            jnp.concatenate([some_cols(box, ref, row, step) for step in range(box.ey // 8)], axis=0)
            for ref, row in zip(refs, rows)
        ]
    )


def looked_up(labels, values):
    return jnp.where(labels == 0, values[0], jnp.where(labels == 1, values[1], values[2]))


def at_own_row(line, shape):
    long_pos, across_pos, _, across_count = position()
    rows = lax.broadcasted_iota(jnp.int32, shape, 0)
    own = rows == long_pos * across_count + across_pos
    return jnp.where(own, line[:1], jnp.zeros(shape, jnp.float32))


def merged(table, *others):
    for other in others:
        table = jnp.where(table != 0.0, table, other)
    return table


def last_rows_merged(refs, count):
    return merged(*(ref[ref.shape[0] - count :, :] for ref in refs))


def join_rows(table, message, out):
    out[...] = last_rows_merged((table, message), out.shape[0])


def line_of(numbers, shape):
    count = -(-len(numbers) // 8) * 8
    rows = lax.broadcasted_iota(jnp.int32, (count, shape[1]), 0)
    lanes = lax.broadcasted_iota(jnp.int32, (count, shape[1]), 1)
    stacked = jnp.zeros((count, shape[1]), jnp.float32)
    place = jnp.zeros((count, shape[1]), jnp.bool_)
    for row, (index, values) in enumerate(numbers):
        stacked = jnp.where(rows == row, values, stacked)
        place = place | ((rows == row) & (lanes == index))
    sums = jnp.sum(stacked, axis=1, keepdims=True)
    line = jnp.sum(jnp.where(place, sums, jnp.zeros_like(stacked)), axis=0, keepdims=True)
    return jnp.broadcast_to(line, shape)


def bring_box(
    box, far_load, far_scale, far_zone, after, diffusivity, decay, load, scale, zone, out, table, sems
):
    del after
    size = 8
    copies = []
    for start in range(0, box.long, size):
        rows = slice(start, start + size)
        for source, target in ((far_load, load), (far_scale, scale), (far_zone, zone)):
            copies.append(
                pltpu.make_async_copy(source.at[rows], target.at[rows], sems.at[len(copies)])
            )
            copies[-1].start()
    nothing = jnp.zeros((box.across, box.deep), jnp.float32)
    half = [[0.5 * diffusivity[z : z + 1, d : d + 1] for z in range(3)] for d in range(3)]
    rates = [decay[0:1, z : z + 1] for z in range(3)]

    def halves(row):
        labels, factor = zone[row], scale[row]
        return [looked_up(labels, half[d]) * factor for d in range(3)] + [looked_up(labels, rates)]

    sums = [nothing] * 5
    for start in range(0, box.long, size):
        for copy in copies[start // size * 3 : start // size * 3 + 3]:
            copy.wait()
        for row in range(start, start + size):
            sums = [total + more for total, more in zip(sums, halves(row) + [load[row]])]

    def total(values):
        return jnp.sum(values, axis=0, keepdims=True)

    cells = box.long * box.across * box.deep
    numbers = [(index, total(sums[index]) * (2.0 / cells)) for index in range(3)]
    mass = total(sums[3])
    numbers += [(3, mass / cells)]
    lane = lax.broadcasted_iota(jnp.int32, (1, box.deep), 1)
    ends = jnp.where((lane == 0) | (lane == box.deep - 1), total(sums[2]), 0.0)
    numbers += [
        (BOX_DIAGONAL, mass + ends),
        (LONG_HIGH, total(halves(box.long - 1)[0])),
        (LONG_LOW, total(halves(0)[0])),
        (ACROSS_HIGH, sums[1][box.across - 1 :]),
        (ACROSS_LOW, sums[1][:1]),
        (LOAD_SUM, total(sums[4])),
    ]
    line = line_of(numbers, out.shape)
    out[...] = line
    table[...] = at_own_row(line, table.shape)


def means_of(ref):
    return [ref[0:1, index : index + 1] for index in range(4)]


def first_solve(box, load, low, high, left, right, means, zone, scale, diffusivity, decay, *rest):
    tables = rest[:N_TABLES]
    window, local, image, inverses, first, second, spectral, middle = rest[N_TABLES:]
    spread_x, spread_y, eig_z = tables[6:]
    means = means_of(means)
    base = means[3] + means[0] * spread_x[...] + means[2] * eig_z[...]

    def divided(values, col):
        divisor = base + means[1] * spread_y[col : col + 1, :]
        inverse = pl.reciprocal(divisor, approx=True)
        for _ in range(2):
            inverse = inverse * (2.0 - divisor * inverse)
        inverses[col] = inverse
        return values * inverse

    half = [0.5 * diffusivity[z : z + 1, 2:3] for z in range(3)]
    rates = [decay[0:1, z : z + 1] for z in range(3)]
    lane = lax.broadcasted_iota(jnp.int32, (box.across, box.deep), 1)
    ends = jnp.where((lane == 0) | (lane == box.deep - 1), jnp.float32(1.0), jnp.float32(0.0))
    image[...] = jnp.zeros((box.across, box.deep), jnp.float32)
    wide_sides, narrow_sides = Sides("wide", low, high), Sides("narrow", left, right)
    fill_window(box, window, load, wide_sides, narrow_sides, MARGIN, 0, MARGIN)

    def emit(start, values):
        values = values * (1.0 / cheb_center)
        values = values.reshape(8, box.across, box.deep)
        local[start : start + 8] = values
        total = image[...]
        for row in range(8):
            labels = zone[start + row]
            mass = looked_up(labels, rates) + looked_up(labels, half) * scale[start + row] * ends
            total = total + mass * values[row]
        image[...] = total

    box_solve(
        box,
        lambda start: in_steps(box, [window] * 8, range(1 + start, 9 + start)),
        divided,
        tables,
        None,
        None,
        spectral,
        middle,
        emit,
    )
    even = is_even("wide")
    for target, pair in ((first, (box.long - REACH, 0)), (second, (0, box.long - REACH))):
        rows = local[pl.ds(jnp.where(even, *pair), REACH)]
        target[...] = rows.reshape(REACH * box.across, box.deep)


def side_weights(
    box, zone, scale, low, high, left, right, diffusivity, to_long, to_across, zone_window,
    scale_window
):
    for index, (window, own) in enumerate(((scale_window, scale), (zone_window, zone))):
        start = index * REACH
        wide_sides = Sides("wide", *(ref.at[start : start + REACH] for ref in (low, high)))
        narrow_sides = Sides("narrow", left, right)
        fill_window(box, window, own, wide_sides, narrow_sides, REACH, start, 2 * REACH)
    half = [[0.5 * diffusivity[z : z + 1, d : d + 1] for z in range(3)] for d in range(2)]

    def one_row(row, before):
        labels, factor = zone_window[row], scale_window[row]
        now = [looked_up(labels, half[d]) * factor for d in range(2)]
        to_across[row] = now[1] + pltpu.roll(now[1], box.cols - 1, 0)
        to_long[max(row - 1, 0)] = before + now[0]
        return now[0]

    before = jnp.zeros((box.cols, box.deep), jnp.float32)
    for row in range(box.rows):
        before = one_row(row, before)
    to_long[box.rows - 1] = before


def deep_weights(box, zone_window, scale_window, diffusivity, decay, to_deep, mass):
    half = [0.5 * diffusivity[z : z + 1, 2:3] for z in range(3)]
    rates = [decay[0:1, z : z + 1] for z in range(3)]
    lane = lax.broadcasted_iota(jnp.int32, (box.cols, box.deep), 1)
    ends = jnp.where((lane == 0) | (lane == box.deep - 1), jnp.float32(1.0), jnp.float32(0.0))
    not_last = jnp.where(lane == box.deep - 1, jnp.float32(0.0), jnp.float32(1.0))

    def one_row(row):
        labels = zone_window[row]
        now = looked_up(labels, half) * scale_window[row]
        to_deep[row] = (now + pltpu.roll(now, box.deep - 1, 1)) * not_last
        mass[row] = looked_up(labels, rates) + now * ends

    for row in range(box.rows):
        one_row(row)


def image_sums(
    box, zone, scale, local, image, low, high, left, right, table, diffusivity, out
):
    half = [[0.5 * diffusivity[z : z + 1, d : d + 1] for z in range(3)] for d in range(3)]
    shape = (box.long * box.across, box.deep)
    zone_flat, scale_flat, local_flat = zone.reshape(shape), scale.reshape(shape), local.reshape(shape)
    last_col = row_of(box.across, box.across - 1, box.long)
    first_col = row_of(box.across, 0, box.long)

    wide_sides, narrow_sides = Sides("wide", low, high), Sides("narrow", left, right)

    def side(source, place):
        return source(slice(place * box.long, (place + 1) * box.long), slice(None))

    above, below = wide_sides.high, wide_sides.low
    faces = [
        (0, zone[box.long - 1], scale[box.long - 1], local[box.long - 1], above(REACH), above(0)),
        (0, zone[0], scale[0], local[0], below(2 * REACH - 1), below(REACH - 1)),
        (
            1,
            zone_flat[last_col, :],
            scale_flat[last_col, :],
            local_flat[last_col, :],
            side(narrow_sides.high, REACH),
            side(narrow_sides.high, 0),
        ),
        (
            1,
            zone_flat[first_col, :],
            scale_flat[first_col, :],
            local_flat[first_col, :],
            side(narrow_sides.low, 2 * REACH - 1),
            side(narrow_sides.low, REACH - 1),
        ),
    ]
    flows = []
    for direction, labels, factor, values, far_labels, far_factor in faces:
        weight = looked_up(labels, half[direction]) * factor
        weight = weight + looked_up(far_labels, half[direction]) * far_factor
        flows.append(jnp.sum(weight * values, axis=0, keepdims=True))
    long_pos, across_pos, long_count, across_count = position()
    numbers = [
        (IMAGE_SUM, jnp.sum(image[...], axis=0, keepdims=True) + sum(flows)),
        (FLOW_LONG_HIGH, flows[0] * as_float(long_pos < long_count - 1)),
        (FLOW_LONG_LOW, flows[1] * as_float(long_pos > 0)),
        (FLOW_ACROSS_HIGH, flows[2] * as_float(across_pos < across_count - 1)),
        (FLOW_ACROSS_LOW, flows[3] * as_float(across_pos > 0)),
    ]
    known = table[...] + at_own_row(line_of(numbers, (8, out.shape[1])), out.shape)
    out[...] = known

def column(values, index):
    return values[:, index : index + 1]


def uncoupled_groups(count, across):
    places = np.arange(count)
    long_step = np.abs(places[:, None] // across - places[None, :] // across)
    across_step = np.abs(places[:, None] % across - places[None, :] % across)
    coupled = long_step + across_step == 1
    left = list(range(count))
    groups = []
    while left:
        group = []
        for place in sorted(left, key=lambda p: (coupled[p][left].sum(), p)):
            if not coupled[place][group].any():
                group.append(place)
        left = [place for place in left if place not in group]
        for place in group:
            beside = [other for other in left if coupled[place][other]]
            for other in beside:
                coupled[other][beside] = True
                coupled[other][other] = False
        groups.append(group)
    return groups


def coarse_inverse(numbers, work):
    count, width = work.shape
    across = lax.axis_size("narrow")
    beyond = pltpu.roll(numbers, count - across, 0)
    beside = pltpu.roll(numbers, count - 1, 0)
    before = pltpu.roll(numbers, across, 0)
    ahead = pltpu.roll(numbers, 1, 0)
    place = lax.broadcasted_iota(jnp.int32, (count, 1), 0)
    across_pos = lax.rem(place, across)
    nothing = jnp.zeros((count, 1), jnp.float32)
    couplings = []
    diagonal = column(numbers, BOX_DIAGONAL)
    for own, other, there, inside in (
        (LONG_HIGH, LONG_LOW, beyond, place < count - across),
        (LONG_LOW, LONG_HIGH, before, place >= across),
        (ACROSS_HIGH, ACROSS_LOW, beside, across_pos < across - 1),
        (ACROSS_LOW, ACROSS_HIGH, ahead, across_pos > 0),
    ):
        shared = jnp.where(inside, column(there, other), nothing)
        diagonal = diagonal + column(numbers, own) + shared
        couplings.append(jnp.where(inside, column(numbers, own) + shared, nothing))
    rows = lax.broadcasted_iota(jnp.int32, (count, width), 0)
    cols = lax.broadcasted_iota(jnp.int32, (count, width), 1)
    blank = jnp.zeros((count, width), jnp.float32)
    matrix = jnp.where(cols == rows, diagonal, blank)
    for shift, coupling in zip((across, -across, 1, -1), couplings):
        matrix = matrix - jnp.where((cols == rows + shift) & (cols < count), coupling, blank)
    matrix = jnp.where(cols == rows + count, jnp.ones((count, 1), jnp.float32), matrix)
    if count <= 16:
        for group in uncoupled_groups(count, across):
            rest = matrix
            for step in group:
                pivot_row = matrix[step : step + 1, :] / matrix[step : step + 1, step : step + 1]
                rest = rest - matrix[:, step : step + 1] * pivot_row
                rest = jnp.where(rows == step, pivot_row, rest)
            matrix = rest
        return pltpu.roll(matrix, width - count, 1)
    work[...] = matrix

    def eliminate(step, _):
        values = work[...]
        pivot_row = work[pl.ds(step, 1), :]
        at_step = cols == step
        factors = jnp.sum(jnp.where(at_step, values, blank), axis=1, keepdims=True)
        pivot = jnp.sum(jnp.where(at_step[:1], pivot_row, blank[:1]), axis=1, keepdims=True)
        pivot_row = pivot_row / pivot
        work[...] = jnp.where(rows == step, pivot_row, values - factors * pivot_row)
        return 0

    lax.fori_loop(0, count, eliminate, 0)
    values = work[...]
    if count % 128:
        return pltpu.roll(values, width - count, 1)
    return values[:, count : 2 * count]


def answer(inverse, sums):
    return jnp.sum(inverse * sums, axis=0, keepdims=True)


def at_box(values, row_side, col_side):
    long_pos, across_pos, long_count, across_count = position()
    there_long, there_across = long_pos + row_side, across_pos + col_side
    inside = (
        (there_long >= 0)
        & (there_long < long_count)
        & (there_across >= 0)
        & (there_across < across_count)
    )
    lanes = lax.broadcasted_iota(jnp.int32, values.shape, 1)
    wanted = (lanes == there_long * across_count + there_across) & inside
    return jnp.sum(jnp.where(wanted, values, jnp.zeros_like(values)), axis=1, keepdims=True)


def coarse_corrections(parts, *refs):
    table_parts, (out, work) = refs[:parts], refs[parts:]
    count = work.shape[0]
    numbers = last_rows_merged(table_parts, count)
    across_count = lax.axis_size("narrow")
    inverse = coarse_inverse(numbers, work)
    sums = column(numbers, IMAGE_SUM)
    sums = sums - column(pltpu.roll(numbers, count - across_count, 0), FLOW_LONG_LOW)
    sums = sums - column(pltpu.roll(numbers, across_count, 0), FLOW_LONG_HIGH)
    sums = sums - column(pltpu.roll(numbers, count - 1, 0), FLOW_ACROSS_LOW)
    sums = sums - column(pltpu.roll(numbers, 1, 0), FLOW_ACROSS_HIGH)
    load_sums = column(numbers, LOAD_SUM)
    sums = load_sums * (1.0 - 1.0 / cheb_center) - sums
    out[0:1, :] = answer(inverse, load_sums) * (1.0 / cheb_center)
    out[1:2, :] = answer(inverse, sums) * gain


def second_solve(box, local, low, high, left, right, inverses, answers, *rest):
    to_long, to_across, to_deep, mass, load_window = rest[:5]
    tables = rest[5 : 5 + N_TABLES]
    iterate, top, bottom, last_col, first_col, out = rest[5 + N_TABLES : 11 + N_TABLES]
    window, spectral, middle, sems = rest[11 + N_TABLES :]
    long_pos, across_pos, long_count, across_count = position()
    coarse = answers[0:1, :]
    own_shift = at_box(answers[1:2, :], 0, 0)
    shifts = {
        (row_side, col_side): at_box(coarse, row_side, col_side)
        for row_side in (-1, 0, 1)
        for col_side in (-1, 0, 1)
    }

    def add(values, row_side, col_side):
        shift = shifts[row_side, col_side]
        if values.ndim == 3:
            shift = shift.reshape(1, 1, 1)
        return values + shift

    edge = REACH * box.across
    low, high = (
        ref.at[:edge].reshape(REACH, box.across, box.deep) for ref in (low, high)
    )
    wide_sides, narrow_sides = Sides("wide", low, high), Sides("narrow", left, right)
    fill_window(box, window, local, wide_sides, narrow_sides, REACH, 0, REACH, add)
    weights = (to_long, to_across, to_deep, mass)

    steps = range(box.ey // 8)
    x = [some_cols(box, window, 1, step) for step in range(-1, len(steps) + 1)]
    flow = [
        some_cols(box, to_long, 0, step) * (x[step + 1] - some_cols(box, window, 0, step))
        for step in steps
    ]
    state = [x, flow]

    def divided(values, col):
        return values * inverses[col]

    def residual(start_row):
        rows = []
        for row in range(start_row + 1, start_row + 9):
            image, *state[:] = negative_image(box, window, row, row, *state, weights)
            image = [some_cols(box, load_window, row, step) + image[step] for step in steps]
            rows.append(jnp.concatenate(image, axis=0))
        return jnp.stack(rows)

    inner = slice(EDGE, EDGE + box.across)
    first = REACH
    row_ids = lax.broadcasted_iota(jnp.int32, (1, padded(box.ex)), 1)
    col_ids = lax.broadcasted_iota(jnp.int32, (1, padded(box.ey)), 1)
    col_ids = (col_ids & 7) * (box.ey // 8) + lax.shift_right_logical(col_ids, 3)
    row_mask = jnp.where(row_ids < MARGIN, as_float(long_pos > 0), 1.0)
    row_mask = jnp.where(row_ids >= MARGIN + box.long, as_float(long_pos < long_count - 1), row_mask)
    col_mask = jnp.where(col_ids < MARGIN, as_float(across_pos > 0), 1.0)
    col_mask = jnp.where(
        col_ids >= MARGIN + box.across, as_float(across_pos < across_count - 1), col_mask
    )
    keep = 1.0 + rho_second * rho_first
    copies = []

    def emit(start, values):
        rows = values.reshape(8, box.across, box.deep)
        before = window[first + start : first + start + 8, inner, :]
        shift = own_shift.reshape(1, 1, 1)
        iterate[start : start + 8] = keep * before + (gain * rows + shift)
        copies.append(
            pltpu.make_async_copy(
                iterate.at[start : start + 8], out.at[start : start + 8], sems.at[len(copies)]
            )
        )
        copies[-1].start()

    box_solve(
        box, residual, divided, tables, row_mask, col_mask, spectral, middle, emit
    )
    rows = in_order(is_even("wide"), iterate[box.long - 1], iterate[0])
    top[...], bottom[...] = rows
    flat = iterate.reshape(box.long * box.across, box.deep)
    cols = [flat[row_of(box.across, col, box.long), :] for col in (box.across - 1, 0)]
    last_col[...], first_col[...] = in_order(is_even("narrow"), *cols)
    for copy in copies:
        copy.wait()


def inner_residual(
    box, load, iterate, to_long, to_across, to_deep, mass, rows, cols, out, window, result, sems
):
    inner = slice(EDGE, EDGE + box.across)
    flat = window.reshape((box.long + 2) * box.cols, box.deep)
    iterate_flat = iterate.reshape(box.long * box.across, box.deep)
    blank = jnp.zeros((box.long + 2, EDGE, box.deep), jnp.float32)
    window[:, :EDGE, :] = blank
    window[:, EDGE + box.across :, :] = blank
    window[1 : 1 + box.long, inner, :] = iterate[...]
    window[0, inner, :] = iterate[0]
    window[1 + box.long, inner, :] = iterate[box.long - 1]
    for col, place in ((0, EDGE - 1), (box.across - 1, EDGE + box.across)):
        values = iterate_flat[row_of(box.across, col, box.long), :]
        flat[row_of(box.cols, place, box.long, 1), :] = values
    weights = (to_long, to_across, to_deep, mass)
    steps = range(box.ey // 8)
    x = [some_cols(box, window, 1, step) for step in range(-1, len(steps) + 1)]
    flow = [jnp.zeros((8, box.deep), jnp.float32) for _ in steps]
    middle = slice(8, box.across - 8)
    copies = []
    for row in range(box.long):
        image, x, flow = negative_image(box, window, row + 1, REACH + row, x, flow, weights)
        for step in steps:
            place = pl.ds(EDGE - MARGIN + step, 8, stride=box.ey // 8)
            result[row, place, :] = image[step]
        values = load[row] + result[row, inner]
        result[row, inner] = values
        cols[0, row] = values[:8]
        cols[1, row] = values[box.across - 8 :]
        if row == 0:
            rows[0] = values
        if row == box.long - 1:
            rows[1] = values
        if row % 8 == 7:
            part = slice(row - 7, row + 1)
            copy = pltpu.make_async_copy(
                result.at[part, EDGE + 8 : EDGE + box.across - 8],
                out.at[part, middle],
                sems.at[row // 8],
            )
            copy.start()
            copies.append(copy)
    for copy in copies:
        copy.wait()


def outer_residual(
    box, iterate, low, high, left, right, to_long, to_across, rows, cols, inner_out, out,
    row_part, col_part, sems
):
    del inner_out
    inner = slice(EDGE, EDGE + box.across)
    middle = slice(8, box.across - 8)
    wide_sides, narrow_sides = Sides("wide", low, high), Sides("narrow", left, right)
    last = box.long - 1
    iterate_flat = iterate.reshape(box.long * box.across, box.deep)
    across_flat = to_across.reshape(box.flat, box.deep)
    below = to_long[REACH - 1, inner] * (wide_sides.low(Ellipsis) - iterate[0])
    above = to_long[REACH + last, inner] * (wide_sides.high(Ellipsis) - iterate[last])
    row_part[0] = (rows[0] + below)[middle]
    row_part[1] = (rows[1] + above)[middle]
    copies = [
        pltpu.make_async_copy(row_part.at[0], out.at[0, middle], sems.at[0]),
        pltpu.make_async_copy(row_part.at[1], out.at[last, middle], sems.at[1]),
    ]
    for copy in copies:
        copy.start()
    col_part[...] = cols[...]
    flat = col_part.reshape(2 * box.long * 8, box.deep)
    for side, (from_side, col, face, tile) in enumerate(
        (
            (narrow_sides.low, 0, EDGE - 1, slice(0, 8)),
            (narrow_sides.high, box.across - 1, EDGE + box.across - 1, slice(box.across - 8, None)),
        )
    ):
        weight = across_flat[row_of(box.cols, face, box.long, REACH), :]
        own = iterate_flat[row_of(box.across, col, box.long), :]
        place = pl.ds(side * box.long * 8 + side * 7, box.long, stride=8)
        flat[place, :] = flat[place, :] + weight * (from_side(Ellipsis) - own)
        col_part[side, 0] = col_part[side, 0] + below[tile]
        col_part[side, last] = col_part[side, last] + above[tile]
        first_col = side * (box.across - 8)
        copy = pltpu.make_async_copy(
            col_part.at[side], out.at[:, first_col : first_col + 8], sems.at[2 + side]
        )
        copy.start()
        copies.append(copy)
    for copy in copies:
        copy.wait()


def swaps(axis):
    sizes = (lax.axis_size("wide"), lax.axis_size("narrow"))
    along = ("wide", "narrow").index(axis)
    size, beside = sizes[along], sizes[1 - along]

    def number(place, other_place):
        pair = (place, other_place) if along == 0 else (other_place, place)
        return pair[0] * sizes[1] + pair[1]

    ways = []
    for way in range(2):
        pairs = []
        for place in range(size):
            for other_place in range(beside):
                partner = place + 1 if place % 2 == way else place - 1
                there = other_place
                if not 0 <= partner < size:
                    partner = place
                    there = other_place ^ 1 if beside % 2 == 0 else other_place
                pairs.append((number(place, other_place), number(partner, there)))
        ways.append(pairs)
    return ways


def exchange(axis, first, second):
    ways = swaps(axis)
    axes = ("wide", "narrow")
    return lax.ppermute(first, axes, ways[0]), lax.ppermute(second, axes, ways[1])


def from_other_end(axis, table):
    size = lax.axis_size(axis)
    return lax.ppermute(table, axis, [(i, size - 1 - i) for i in range(size)])


def two_away(axis, table):
    size = lax.axis_size(axis)
    return lax.ppermute(table, axis, [(i, (i + 2) % size) for i in range(size)])


def tell(table):
    count = table.shape[0]
    long_pos, across_pos, _, across_count = position()
    own = lax.dynamic_slice_in_dim(table, long_pos * across_count + across_pos, 1, axis=0)
    line = jnp.broadcast_to(own, (count, 1, 128))
    told = lax.all_to_all(line, ("wide", "narrow"), split_axis=0, concat_axis=0, tiled=True)
    return told.reshape(count, 128)


def on_device(zone, scale, diffusivity, decay, load):
    box = Box(load.shape)
    long, across, deep = load.shape
    count = lax.axis_size("wide") * lax.axis_size("narrow")
    by_margins = lax.axis_size("wide") == 4 and lax.axis_size("narrow") == 4
    tables = tables_of(box)
    decay = decay.reshape(1, -1)
    cells = f32(long, across, deep)
    whole_zone = jax.ShapeDtypeStruct(cells.shape, zone.dtype)
    window = f32(box.rows, box.cols, deep)
    table_shape = f32(count, 128)
    anywhere = pl.BlockSpec(memory_space=pl.ANY)
    in_hbm = pl.BlockSpec(memory_space=pltpu.HBM)

    def scratch(shape):
        return pltpu.VMEM(shape, jnp.float32)

    def pinned(field):
        return pltpu.with_memory_space_constraint(field, pltpu.HBM)

    spectral = scratch((box.ey, padded(box.ex), deep))
    middle = scratch((long, padded(box.ey), deep))

    def pack(wide, fields, sides, parts=(), after=()):
        rows = message_rows(box, wide * len(fields)) + (count if parts else 0)
        message = f32(rows, deep)
        body = functools.partial(pack_fields, box, wide, len(fields), len(parts), len(after))
        return call(
            body,
            (message, message) + ((table_shape,) if parts else ()),
            [VMEM] * (len(fields) + 2 + len(parts)) + [anywhere] * len(after),
        )(*fields, *sides, *parts, *after)

    far = f32(2 * REACH, across, deep)
    far_zone, far_scale, far_load = pinned(zone), pinned(scale), pinned(load)
    load_first, load_second, first, second = call(
        functools.partial(bring_edges, box),
        (f32(MARGIN, across, deep),) * 2 + (far, far),
        [in_hbm] * 3,
        [pltpu.VMEM((2, REACH, across, deep), zone.dtype), pltpu.SemaphoreType.DMA((6,))],
    )(far_zone, far_scale, far_load)
    load, scale, zone, sums, table = call(
        functools.partial(bring_box, box),
        (cells, cells, whole_zone, f32(8, 128), table_shape),
        [in_hbm] * 3 + [anywhere] + [VMEM] * 2,
        [pltpu.SemaphoreType.DMA((3 * (long // 8),))],
    )(far_load, far_scale, far_zone, load_first, diffusivity, decay)
    load_wide = exchange("wide", load_first, load_second)
    far_wide = exchange("wide", first, second)
    load_first, load_second = pack(MARGIN, [load], load_wide)
    load_narrow = exchange("narrow", load_first, load_second)
    far_narrow = exchange("narrow", *pack(REACH, [scale, zone], far_wide))
    message = f32(REACH * across, deep)
    load_window, local, image, inverses, first, second = call(
        functools.partial(first_solve, box),
        (window, cells, f32(across, deep), f32(box.ey, box.ex, deep), message, message),
        [VMEM] * 8 + [VMEM] * 2 + [VMEM] * N_TABLES,
        [spectral, middle],
        flops=4 * 10**9,
    )(load, *load_wide, *load_narrow, sums, zone, scale, diffusivity, decay, *tables)
    wide = exchange("wide", first, second)
    table = call(functools.partial(image_sums, box), table_shape, [VMEM] * 10)(
        zone, scale, local, image, *far_wide, *far_narrow, table, diffusivity
    )
    own_table = table
    parts = (table,)
    if by_margins:
        partner = lax.ppermute(table, ("wide", "narrow"), swaps("wide")[0])
        parts += (partner, two_away("wide", table), from_other_end("wide", table))
    to_long, to_across, *windows = call(
        functools.partial(side_weights, box),
        (window,) * 4,
        [VMEM] * 6 + [VMEM],
        flops=10**9,
    )(zone, scale, *far_wide, *far_narrow, diffusivity)
    to_deep, mass = call(
        functools.partial(deep_weights, box),
        (window,) * 2,
        [VMEM] * 2 + [VMEM] * 2,
        flops=10**9,
    )(*windows, diffusivity, decay)
    weights = (to_long, to_across, to_deep, mass)
    first, second, table = pack(REACH, [local], wide, parts, [to_long])
    narrow = exchange("narrow", first, second)
    if by_margins:
        table = call(join_rows, table_shape, [VMEM] * 2)(table, narrow[0])
        parts = (table, two_away("narrow", table))
    else:
        parts = (tell(own_table),)
    row, col = f32(across, deep), f32(long, deep)
    answers = call(
        functools.partial(coarse_corrections, len(parts)),
        f32(8, -(-count // 128) * 128),
        [VMEM] * len(parts),
        [scratch((count, -(-2 * count // 128) * 128))],
    )(*parts)
    iterate, first_row, second_row, first_col, second_col, result = call(
        functools.partial(second_solve, box),
        (cells, row, row, col, col, cells),
        [VMEM] * (12 + N_TABLES),
        [scratch(window.shape), spectral, middle, pltpu.SemaphoreType.DMA((long // 8,))],
        flops=4 * 10**9,
        out_spec=(VMEM,) * 5 + (anywhere,),
    )(local, *wide, *narrow, inverses, answers, *weights, load_window, *tables)
    narrow = exchange("narrow", first_col, second_col)
    wide = exchange("wide", first_row, second_row)
    rows, cols, inner = call(
        functools.partial(inner_residual, box),
        (f32(2, across, deep), f32(2, long, 8, deep), cells),
        [VMEM] * 6,
        [
            scratch((long + 2, box.cols, deep)),
            scratch((long, box.cols, deep)),
            pltpu.SemaphoreType.DMA((long // 8,)),
        ],
        flops=10**9,
        out_spec=(VMEM, VMEM, anywhere),
    )(load, iterate, *weights)
    residual = call(
        functools.partial(outer_residual, box),
        cells,
        [VMEM] * 9 + [anywhere],
        [
            scratch((2, across - 16, deep)),
            scratch((2, long, 8, deep)),
            pltpu.SemaphoreType.DMA((4,)),
        ],
        out_spec=anywhere,
        aliases={9: 0},
    )(iterate, *wide, *narrow, to_long, to_across, rows, cols, inner)
    return result, residual


def solution(mesh):
    split = P(("groups", "wide"), "narrow", None)
    return jax.shard_map(
        on_device,
        mesh=mesh,
        in_specs=(split, split, P(), P(), split),
        out_specs=(split, split),
        check_vma=False,
    )
```

```python
import functools

import jax
import jax.numpy as jnp
import ml_dtypes
import numpy as np
from jax import lax
from jax.experimental import pallas as pl
from jax.experimental.pallas import tpu as pltpu
from jax.sharding import PartitionSpec as P

MARGIN = 4
REACH = MARGIN + 1
EDGE = 8

cheb_center = 1.3
cheb_radius = 1.2
cheb_ratio = 1.3 / 1.2
rho_first = 1.0 / cheb_ratio
rho_second = 1.0 / (2.0 * cheb_ratio - rho_first)
gain = 2.0 * rho_second / cheb_radius

MEANS = range(4)
BOX_DIAGONAL, LONG_HIGH, LONG_LOW, ACROSS_HIGH, ACROSS_LOW, LOAD_SUM = range(4, 10)
IMAGE_SUM, FLOW_LONG_HIGH, FLOW_LONG_LOW, FLOW_ACROSS_HIGH, FLOW_ACROSS_LOW = range(16, 21)

VMEM = pl.BlockSpec(memory_space=pltpu.VMEM)


def sine_basis(length):
    indices = np.arange(1, length + 1)
    phases = indices[:, None] * indices[None, :] % (2 * (length + 1))
    table = np.sqrt(2.0 / (length + 1)) * np.sin(np.pi * phases / (length + 1))
    eigvals = 4.0 * np.sin(np.pi * indices / (2.0 * (length + 1))) ** 2
    return table.astype(np.float32), eigvals.astype(np.float32)


def call(body, out_shape, in_specs, scratch=(), flops=0, out_spec=None, aliases=None):
    return pl.pallas_call(
        body,
        out_shape=out_shape,
        in_specs=in_specs,
        out_specs=out_spec or jax.tree.map(lambda _: VMEM, out_shape),
        scratch_shapes=list(scratch),
        compiler_params=pltpu.CompilerParams(vmem_limit_bytes=30 * 2**20),
        cost_estimate=pl.CostEstimate(flops=flops, bytes_accessed=0, transcendentals=0),
        input_output_aliases=aliases or {},
    )


def f32(*shape):
    return jax.ShapeDtypeStruct(shape, jnp.float32)


class Box:
    def __init__(self, shape):
        self.long, self.across, self.deep = shape
        self.ex = self.long + 2 * MARGIN
        self.ey = self.across + 2 * MARGIN
        self.rows = self.long + 2 * REACH
        self.cols = self.across + 2 * EDGE
        self.flat = self.rows * self.cols


def pieces(values, count):
    parts = []
    for _ in range(count - 1):
        scaled = values * 65537.0
        part = scaled - (scaled - values)
        parts.append(part)
        values = values - part
    return parts + [values]


def left_table(table, depth, count):
    rows, cols = table.shape
    wide = np.zeros((rows, depth), np.float32)
    wide[:, :cols] = table
    parts = []
    rest = wide
    for _ in range(count):
        part = rest.astype(ml_dtypes.bfloat16).astype(np.float32)
        parts.append(part)
        rest = rest - part
    blank = np.zeros_like(parts[0])
    lines = []
    for index in range(count):
        used = count - index if count > 2 else count
        lines.append(np.concatenate([parts[index]] * used + [blank] * (count - used), axis=1))
    return np.concatenate(lines, axis=0)


def right_tables(table):
    rest, parts = table, []
    for _ in range(3):
        part = rest.astype(ml_dtypes.bfloat16).astype(np.float32)
        parts.append(part)
        rest = rest - part
    both = np.concatenate([parts[0], parts[1]], axis=1)
    return np.concatenate([both, both], axis=0), np.concatenate([parts[2], parts[0]], axis=0)


def padded(size):
    return -(-size // 8) * 8


FORWARD, BACKWARD = 2, 3


def tables_of(box):
    sine_x, eig_x = sine_basis(box.ex)
    sine_y, eig_y = sine_basis(box.ey)
    sine_z, eig_z = sine_basis(box.deep)
    in_order_of_steps = np.arange(box.ey).reshape(8, box.ey // 8).T.reshape(-1)
    from_y = sine_y[MARGIN : MARGIN + box.across]
    from_x = sine_x[MARGIN : MARGIN + box.long]
    spread_x = np.broadcast_to(eig_x[:, None], (box.ex, box.deep))
    spread_y = np.broadcast_to(eig_y[:, None], (box.ey, box.deep))
    main_z, rest_z = right_tables(sine_z)
    return [
        jnp.asarray(np.ascontiguousarray(t))
        for t in (
            left_table(sine_y[:, in_order_of_steps], padded(box.ey), FORWARD),
            left_table(sine_x, padded(box.ex), FORWARD),
            left_table(from_x, padded(box.ex), BACKWARD),
            left_table(from_y, padded(box.ey), BACKWARD),
            main_z,
            rest_z,
            spread_x,
            spread_y,
            eig_z[None, :],
        )
    ]


N_TABLES = 9


def one_pass(left, right):
    return lax.dot_general(
        left,
        right,
        (((1,), (0,)), ((), ())),
        precision=lax.Precision.DEFAULT,
        preferred_element_type=jnp.float32,
    )


def dot_left(table, values, count, rows):
    total = one_pass(table, jnp.concatenate(pieces(values, count), axis=0))
    return sum(total[index * rows : (index + 1) * rows] for index in range(1, count)) + total[:rows]


def dot_right(values, main, rest, count):
    deep = values.shape[1]
    parts = pieces(values, count)
    total = one_pass(jnp.concatenate(parts[:2], axis=1), main)
    result = total[:, :deep] + total[:, deep:]
    if count == 3:
        result = result + one_pass(jnp.concatenate([parts[0], parts[2]], axis=1), rest)
    return result


def with_rows(values, rows):
    if values.shape[0] == rows:
        return values
    blank = jnp.zeros((rows - values.shape[0],) + values.shape[1:], values.dtype)
    return jnp.concatenate([values, blank], axis=0)


FORWARD_ROWS, COLS_ABREAST, BACKWARD_ROWS = 24, 40, 32


def fitting(size, wanted):
    return max(part for part in range(8, wanted + 1, 8) if size % part == 0)


def beside(values):
    return jnp.concatenate(values, axis=1)


def apart(values, lanes):
    return [values[:, start : start + lanes] for start in range(0, values.shape[1], lanes)]


def box_solve(box, source, divided, tables, row_mask, col_mask, spectral, middle, emit):
    into_y, into_x, from_x, from_y, main_z, rest_z = tables[:6]
    deep = box.deep
    deep_x, deep_y = padded(box.ex), padded(box.ey)
    into_y, into_x = into_y[...], into_x[...]
    if col_mask is not None:
        mask = jnp.concatenate([col_mask] * FORWARD, axis=1)
        into_y = into_y * mask
        mask = jnp.concatenate([row_mask] * FORWARD, axis=1)
        into_x = into_x * mask
    from_x, from_y, main_z, rest_z = from_x[...], from_y[...], main_z[...], rest_z[...]
    spectral_flat = spectral.reshape(box.ey * deep_x, deep)
    middle_flat = middle.reshape(box.long * deep_y, deep)
    if deep_x > box.ex:
        spectral[:, box.ex :, :] = jnp.zeros((box.ey, deep_x - box.ex, deep), jnp.float32)
    if deep_y > box.ey:
        middle[:, box.ey :, :] = jnp.zeros((box.long, deep_y - box.ey, deep), jnp.float32)
    step = fitting(box.ex, FORWARD_ROWS)
    for start in range(0, box.ex, step):
        block = jnp.concatenate([source(row) for row in range(start, start + step, 8)], axis=0)
        block = dot_right(block.reshape(step * box.ey, deep), main_z, rest_z, FORWARD)
        block = block.reshape(step, box.ey, deep)
        wide = beside([block[row] for row in range(step)])
        wide = dot_left(into_y, with_rows(wide, deep_y), FORWARD, box.ey)
        for row, values in enumerate(apart(wide, deep)):
            spectral_flat[pl.ds(start + row, box.ey, stride=deep_x), :] = values
    step = fitting(box.ey, COLS_ABREAST)
    for start in range(0, box.ey, step):
        wide = beside([spectral[col] for col in range(start, start + step)])
        wide = apart(dot_left(into_x, wide, FORWARD, box.ex), deep)
        wide = beside([divided(values, start + part) for part, values in enumerate(wide)])
        wide = dot_left(from_x, with_rows(wide, deep_x), BACKWARD, box.long)
        for part, values in enumerate(apart(wide, deep)):
            middle_flat[pl.ds(start + part, box.long, stride=deep_y), :] = values
    step = fitting(box.long, BACKWARD_ROWS)
    for start in range(0, box.long, step):
        wide = beside([middle[row] for row in range(start, start + step)])
        parts = apart(dot_left(from_y, wide, BACKWARD, box.across), deep)
        values = dot_right(jnp.concatenate(parts, axis=0), main_z, rest_z, BACKWARD)
        for row in range(0, step, 8):
            emit(start + row, values[row * box.across : (row + 8) * box.across])


def position():
    long_pos, across_pos = lax.axis_index("wide"), lax.axis_index("narrow")
    return long_pos, across_pos, lax.axis_size("wide"), lax.axis_size("narrow")


def as_float(flag):
    return jnp.where(flag, jnp.float32(1.0), jnp.float32(0.0))


def is_even(axis):
    return lax.rem(lax.axis_index(axis), 2) == 0


class Sides:
    def __init__(self, axis, first, second):
        position = lax.axis_index(axis)
        self.even = is_even(axis)
        self.has_low = as_float(position > 0)
        self.has_high = as_float(position < lax.axis_size(axis) - 1)
        self.first, self.second = first, second

    def low(self, *index):
        return jnp.where(self.even, self.second[index], self.first[index]) * self.has_low

    def high(self, *index):
        return jnp.where(self.even, self.first[index], self.second[index]) * self.has_high


def in_order(even, up, down):
    return jnp.where(even, up, down), jnp.where(even, down, up)


def row_of(stride, col, count, first=0):
    return pl.ds(first * stride + col, count, stride=stride)


def pack_columns(box, fields, wide_sides, wide, first, second):
    corner = len(fields) * wide * box.long
    even = is_even("narrow")
    place = 0
    for field, sides in zip(fields, wide_sides):
        for step in range(wide):
            cols = (box.across - wide + step, step)
            values = [field[row_of(box.across, col, box.long), :] for col in cols]
            low = [sides.low(row_of(box.across, col, wide), slice(None)) for col in cols]
            high = [sides.high(row_of(box.across, col, wide), slice(None)) for col in cols]
            at = corner + 2 * REACH * place
            for start, parts in ((place * box.long, values), (at, low), (at + REACH, high)):
                parts = in_order(even, *(part.astype(jnp.float32) for part in parts))
                size = parts[0].shape[0]
                first[start : start + size, :], second[start : start + size, :] = parts
            place += 1


def message_rows(box, count):
    return -(-(count * (box.long + 2 * REACH)) // 8) * 8


def pack_fields(box, wide, fields, tables, after, *refs):
    own, (low, high), refs = refs[:fields], refs[fields : fields + 2], refs[fields + 2 :]
    parts, (first, second, *table) = refs[:tables], refs[tables + after :]
    size = wide * box.across
    flat = [field.reshape(box.long * box.across, box.deep) for field in own]
    low = low.reshape(low.size // box.deep, box.deep)
    high = high.reshape(high.size // box.deep, box.deep)
    sides = [
        Sides("wide", *(ref.at[index * size : (index + 1) * size] for ref in (low, high)))
        for index in range(fields)
    ]
    pack_columns(box, flat, sides, wide, first, second)
    if tables:
        known = last_rows_merged(parts, table[0].shape[0])
        table[0][...] = known
        first[first.shape[0] - known.shape[0] :, :] = known
        second[second.shape[0] - known.shape[0] :, :] = known


def bring_edges(box, zone, scale, load, load_first, load_second, first, second, staged, sems):
    even = is_even("wide")

    def edges(wide):
        up, down = box.long - wide, 0
        return [pl.ds(jnp.where(even, *pair), wide) for pair in ((up, down), (down, up))]

    copies = [
        (zone.at[edges(REACH)[0]], staged.at[0]),
        (zone.at[edges(REACH)[1]], staged.at[1]),
        (load.at[edges(MARGIN)[0]], load_first),
        (load.at[edges(MARGIN)[1]], load_second),
        (scale.at[edges(REACH)[0]], first.at[:REACH]),
        (scale.at[edges(REACH)[1]], second.at[:REACH]),
    ]
    copies = [
        pltpu.make_async_copy(source, target, sems.at[index])
        for index, (source, target) in enumerate(copies)
    ]
    for copy in copies:
        copy.start()
    for copy in copies[:2]:
        copy.wait()
    first[REACH:] = staged[0].astype(jnp.float32)
    second[REACH:] = staged[1].astype(jnp.float32)
    for copy in copies[2:]:
        copy.wait()


def fill_window(box, window, own, wide_sides, narrow_sides, wide, place, total, add=None):
    flat = window.reshape(box.flat, box.deep)
    nothing = jnp.zeros((box.rows, EDGE, box.deep), jnp.float32)
    window[:, :EDGE, :] = nothing
    window[:, EDGE + box.across :, :] = nothing
    if add is None:
        add = lambda values, row_side, col_side: values
    inner = slice(EDGE, EDGE + box.across)
    first, last = REACH, REACH + box.long
    if wide < REACH:
        blank = jnp.zeros((1, box.across, box.deep), jnp.float32)
        window[0:1, inner, :] = blank
        window[box.rows - 1 :, inner, :] = blank
    window[first:last, inner, :] = add(own[...].astype(jnp.float32), 0, 0)
    window[first - wide : first, inner, :] = add(wide_sides.low(Ellipsis), -1, 0)
    window[last : last + wide, inner, :] = add(wide_sides.high(Ellipsis), 1, 0)
    corner = total * box.long
    for step in range(wide):
        for source, col, side in (
            (narrow_sides.low, EDGE - wide + step, -1),
            (narrow_sides.high, EDGE + box.across + step, 1),
        ):
            for start, size, row, row_side in (
                ((place + step) * box.long, box.long, first, 0),
                (corner + 2 * REACH * (place + step), wide, first - wide, -1),
                (corner + 2 * REACH * (place + step) + REACH, wide, last, 1),
            ):
                values = source(slice(start, start + size), slice(None))
                flat[row_of(box.cols, col, size, row), :] = add(values, row_side, side)


def some_cols(box, ref, row, step):
    stride = box.ey // 8
    return ref[row, pl.ds(EDGE - MARGIN + step, 8, stride=stride), :]


def negative_image(box, window, row, at, x, flow_before, weights):
    to_long, to_across, to_deep, mass = weights
    steps = range(box.ey // 8)
    x_next = [some_cols(box, window, row + 1, step) for step in range(-1, len(steps) + 1)]
    flow_long = [
        some_cols(box, to_long, at, step) * (x_next[step + 1] - x[step + 1]) for step in steps
    ]
    flow_across = [
        some_cols(box, to_across, at, step) * (x[step + 2] - x[step + 1])
        for step in range(-1, len(steps))
    ]
    totals = []
    for step in steps:
        here = x[step + 1]
        lanes = here.shape[1]
        flow_deep = some_cols(box, to_deep, at, step) * (pltpu.roll(here, lanes - 1, 1) - here)
        total = flow_long[step] - flow_before[step] - some_cols(box, mass, at, step) * here
        total = total + (flow_across[step + 1] - flow_across[step])
        totals.append(total + (flow_deep - pltpu.roll(flow_deep, 1, 1)))
    return totals, x_next, flow_long


def in_steps(box, refs, rows):
    return jnp.stack(
        [
            jnp.concatenate([some_cols(box, ref, row, step) for step in range(box.ey // 8)], axis=0)
            for ref, row in zip(refs, rows)
        ]
    )


def looked_up(labels, values):
    return jnp.where(labels == 0, values[0], jnp.where(labels == 1, values[1], values[2]))


def at_own_row(line, shape):
    long_pos, across_pos, _, across_count = position()
    rows = lax.broadcasted_iota(jnp.int32, shape, 0)
    own = rows == long_pos * across_count + across_pos
    return jnp.where(own, line[:1], jnp.zeros(shape, jnp.float32))


def merged(table, *others):
    for other in others:
        table = jnp.where(table != 0.0, table, other)
    return table


def last_rows_merged(refs, count):
    return merged(*(ref[ref.shape[0] - count :, :] for ref in refs))


def join_rows(table, message, out):
    out[...] = last_rows_merged((table, message), out.shape[0])


def line_of(numbers, shape):
    count = -(-len(numbers) // 8) * 8
    rows = lax.broadcasted_iota(jnp.int32, (count, shape[1]), 0)
    lanes = lax.broadcasted_iota(jnp.int32, (count, shape[1]), 1)
    stacked = jnp.zeros((count, shape[1]), jnp.float32)
    place = jnp.zeros((count, shape[1]), jnp.bool_)
    for row, (index, values) in enumerate(numbers):
        stacked = jnp.where(rows == row, values, stacked)
        place = place | ((rows == row) & (lanes == index))
    sums = jnp.sum(stacked, axis=1, keepdims=True)
    line = jnp.sum(jnp.where(place, sums, jnp.zeros_like(stacked)), axis=0, keepdims=True)
    return jnp.broadcast_to(line, shape)


def bring_box(
    box, far_load, far_scale, far_zone, after, diffusivity, decay, load, scale, zone, out, table, sems
):
    del after
    size = 8
    copies = []
    for start in range(0, box.long, size):
        rows = slice(start, start + size)
        for source, target in ((far_load, load), (far_scale, scale), (far_zone, zone)):
            copies.append(
                pltpu.make_async_copy(source.at[rows], target.at[rows], sems.at[len(copies)])
            )
            copies[-1].start()
    nothing = jnp.zeros((box.across, box.deep), jnp.float32)
    half = [[0.5 * diffusivity[z : z + 1, d : d + 1] for z in range(3)] for d in range(3)]
    rates = [decay[0:1, z : z + 1] for z in range(3)]

    def halves(row):
        labels, factor = zone[row], scale[row]
        return [looked_up(labels, half[d]) * factor for d in range(3)] + [looked_up(labels, rates)]

    sums = [nothing] * 5
    for start in range(0, box.long, size):
        for copy in copies[start // size * 3 : start // size * 3 + 3]:
            copy.wait()
        for row in range(start, start + size):
            sums = [total + more for total, more in zip(sums, halves(row) + [load[row]])]

    def total(values):
        return jnp.sum(values, axis=0, keepdims=True)

    cells = box.long * box.across * box.deep
    numbers = [(index, total(sums[index]) * (2.0 / cells)) for index in range(3)]
    mass = total(sums[3])
    numbers += [(3, mass / cells)]
    lane = lax.broadcasted_iota(jnp.int32, (1, box.deep), 1)
    ends = jnp.where((lane == 0) | (lane == box.deep - 1), total(sums[2]), 0.0)
    numbers += [
        (BOX_DIAGONAL, mass + ends),
        (LONG_HIGH, total(halves(box.long - 1)[0])),
        (LONG_LOW, total(halves(0)[0])),
        (ACROSS_HIGH, sums[1][box.across - 1 :]),
        (ACROSS_LOW, sums[1][:1]),
        (LOAD_SUM, total(sums[4])),
    ]
    line = line_of(numbers, out.shape)
    out[...] = line
    table[...] = at_own_row(line, table.shape)


def means_of(ref):
    return [ref[0:1, index : index + 1] for index in range(4)]


def first_solve(box, load, low, high, left, right, means, zone, scale, diffusivity, decay, *rest):
    tables = rest[:N_TABLES]
    window, local, image, inverses, first, second, spectral, middle = rest[N_TABLES:]
    spread_x, spread_y, eig_z = tables[6:]
    means = means_of(means)
    base = means[3] + means[0] * spread_x[...] + means[2] * eig_z[...]

    def divided(values, col):
        divisor = base + means[1] * spread_y[col : col + 1, :]
        inverse = pl.reciprocal(divisor, approx=True)
        for _ in range(2):
            inverse = inverse * (2.0 - divisor * inverse)
        inverses[col] = inverse
        return values * inverse

    half = [0.5 * diffusivity[z : z + 1, 2:3] for z in range(3)]
    rates = [decay[0:1, z : z + 1] for z in range(3)]
    lane = lax.broadcasted_iota(jnp.int32, (box.across, box.deep), 1)
    ends = jnp.where((lane == 0) | (lane == box.deep - 1), jnp.float32(1.0), jnp.float32(0.0))
    image[...] = jnp.zeros((box.across, box.deep), jnp.float32)
    wide_sides, narrow_sides = Sides("wide", low, high), Sides("narrow", left, right)
    fill_window(box, window, load, wide_sides, narrow_sides, MARGIN, 0, MARGIN)

    def emit(start, values):
        values = values * (1.0 / cheb_center)
        values = values.reshape(8, box.across, box.deep)
        local[start : start + 8] = values
        total = image[...]
        for row in range(8):
            labels = zone[start + row]
            mass = looked_up(labels, rates) + looked_up(labels, half) * scale[start + row] * ends
            total = total + mass * values[row]
        image[...] = total

    box_solve(
        box,
        lambda start: in_steps(box, [window] * 8, range(1 + start, 9 + start)),
        divided,
        tables,
        None,
        None,
        spectral,
        middle,
        emit,
    )
    even = is_even("wide")
    for target, pair in ((first, (box.long - REACH, 0)), (second, (0, box.long - REACH))):
        rows = local[pl.ds(jnp.where(even, *pair), REACH)]
        target[...] = rows.reshape(REACH * box.across, box.deep)


def side_weights(
    box, zone, scale, low, high, left, right, diffusivity, to_long, to_across, zone_window,
    scale_window
):
    for index, (window, own) in enumerate(((scale_window, scale), (zone_window, zone))):
        start = index * REACH
        wide_sides = Sides("wide", *(ref.at[start : start + REACH] for ref in (low, high)))
        narrow_sides = Sides("narrow", left, right)
        fill_window(box, window, own, wide_sides, narrow_sides, REACH, start, 2 * REACH)
    half = [[0.5 * diffusivity[z : z + 1, d : d + 1] for z in range(3)] for d in range(2)]

    def one_row(row, before):
        labels, factor = zone_window[row], scale_window[row]
        now = [looked_up(labels, half[d]) * factor for d in range(2)]
        to_across[row] = now[1] + pltpu.roll(now[1], box.cols - 1, 0)
        to_long[max(row - 1, 0)] = before + now[0]
        return now[0]

    before = jnp.zeros((box.cols, box.deep), jnp.float32)
    for row in range(box.rows):
        before = one_row(row, before)
    to_long[box.rows - 1] = before


def deep_weights(box, zone_window, scale_window, diffusivity, decay, to_deep, mass):
    half = [0.5 * diffusivity[z : z + 1, 2:3] for z in range(3)]
    rates = [decay[0:1, z : z + 1] for z in range(3)]
    lane = lax.broadcasted_iota(jnp.int32, (box.cols, box.deep), 1)
    ends = jnp.where((lane == 0) | (lane == box.deep - 1), jnp.float32(1.0), jnp.float32(0.0))
    not_last = jnp.where(lane == box.deep - 1, jnp.float32(0.0), jnp.float32(1.0))

    def one_row(row):
        labels = zone_window[row]
        now = looked_up(labels, half) * scale_window[row]
        to_deep[row] = (now + pltpu.roll(now, box.deep - 1, 1)) * not_last
        mass[row] = looked_up(labels, rates) + now * ends

    for row in range(box.rows):
        one_row(row)


def image_sums(
    box, zone, scale, local, image, low, high, left, right, table, diffusivity, out
):
    half = [[0.5 * diffusivity[z : z + 1, d : d + 1] for z in range(3)] for d in range(3)]
    shape = (box.long * box.across, box.deep)
    zone_flat, scale_flat, local_flat = zone.reshape(shape), scale.reshape(shape), local.reshape(shape)
    last_col = row_of(box.across, box.across - 1, box.long)
    first_col = row_of(box.across, 0, box.long)

    wide_sides, narrow_sides = Sides("wide", low, high), Sides("narrow", left, right)

    def side(source, place):
        return source(slice(place * box.long, (place + 1) * box.long), slice(None))

    above, below = wide_sides.high, wide_sides.low
    faces = [
        (0, zone[box.long - 1], scale[box.long - 1], local[box.long - 1], above(REACH), above(0)),
        (0, zone[0], scale[0], local[0], below(2 * REACH - 1), below(REACH - 1)),
        (
            1,
            zone_flat[last_col, :],
            scale_flat[last_col, :],
            local_flat[last_col, :],
            side(narrow_sides.high, REACH),
            side(narrow_sides.high, 0),
        ),
        (
            1,
            zone_flat[first_col, :],
            scale_flat[first_col, :],
            local_flat[first_col, :],
            side(narrow_sides.low, 2 * REACH - 1),
            side(narrow_sides.low, REACH - 1),
        ),
    ]
    flows = []
    for direction, labels, factor, values, far_labels, far_factor in faces:
        weight = looked_up(labels, half[direction]) * factor
        weight = weight + looked_up(far_labels, half[direction]) * far_factor
        flows.append(jnp.sum(weight * values, axis=0, keepdims=True))
    long_pos, across_pos, long_count, across_count = position()
    numbers = [
        (IMAGE_SUM, jnp.sum(image[...], axis=0, keepdims=True) + sum(flows)),
        (FLOW_LONG_HIGH, flows[0] * as_float(long_pos < long_count - 1)),
        (FLOW_LONG_LOW, flows[1] * as_float(long_pos > 0)),
        (FLOW_ACROSS_HIGH, flows[2] * as_float(across_pos < across_count - 1)),
        (FLOW_ACROSS_LOW, flows[3] * as_float(across_pos > 0)),
    ]
    known = table[...] + at_own_row(line_of(numbers, (8, out.shape[1])), out.shape)
    out[...] = known

def column(values, index):
    return values[:, index : index + 1]


def uncoupled_groups(count, across):
    places = np.arange(count)
    long_step = np.abs(places[:, None] // across - places[None, :] // across)
    across_step = np.abs(places[:, None] % across - places[None, :] % across)
    coupled = long_step + across_step == 1
    left = list(range(count))
    groups = []
    while left:
        group = []
        for place in sorted(left, key=lambda p: (coupled[p][left].sum(), p)):
            if not coupled[place][group].any():
                group.append(place)
        left = [place for place in left if place not in group]
        for place in group:
            beside = [other for other in left if coupled[place][other]]
            for other in beside:
                coupled[other][beside] = True
                coupled[other][other] = False
        groups.append(group)
    return groups


def coarse_inverse(numbers, work):
    count, width = work.shape
    across = lax.axis_size("narrow")
    beyond = pltpu.roll(numbers, count - across, 0)
    beside = pltpu.roll(numbers, count - 1, 0)
    before = pltpu.roll(numbers, across, 0)
    ahead = pltpu.roll(numbers, 1, 0)
    place = lax.broadcasted_iota(jnp.int32, (count, 1), 0)
    across_pos = lax.rem(place, across)
    nothing = jnp.zeros((count, 1), jnp.float32)
    couplings = []
    diagonal = column(numbers, BOX_DIAGONAL)
    for own, other, there, inside in (
        (LONG_HIGH, LONG_LOW, beyond, place < count - across),
        (LONG_LOW, LONG_HIGH, before, place >= across),
        (ACROSS_HIGH, ACROSS_LOW, beside, across_pos < across - 1),
        (ACROSS_LOW, ACROSS_HIGH, ahead, across_pos > 0),
    ):
        shared = jnp.where(inside, column(there, other), nothing)
        diagonal = diagonal + column(numbers, own) + shared
        couplings.append(jnp.where(inside, column(numbers, own) + shared, nothing))
    rows = lax.broadcasted_iota(jnp.int32, (count, width), 0)
    cols = lax.broadcasted_iota(jnp.int32, (count, width), 1)
    blank = jnp.zeros((count, width), jnp.float32)
    matrix = jnp.where(cols == rows, diagonal, blank)
    for shift, coupling in zip((across, -across, 1, -1), couplings):
        matrix = matrix - jnp.where((cols == rows + shift) & (cols < count), coupling, blank)
    matrix = jnp.where(cols == rows + count, jnp.ones((count, 1), jnp.float32), matrix)
    if count <= 16:
        for group in uncoupled_groups(count, across):
            rest = matrix
            for step in group:
                pivot_row = matrix[step : step + 1, :] / matrix[step : step + 1, step : step + 1]
                rest = rest - matrix[:, step : step + 1] * pivot_row
                rest = jnp.where(rows == step, pivot_row, rest)
            matrix = rest
        return pltpu.roll(matrix, width - count, 1)
    work[...] = matrix

    def eliminate(step, _):
        values = work[...]
        pivot_row = work[pl.ds(step, 1), :]
        at_step = cols == step
        factors = jnp.sum(jnp.where(at_step, values, blank), axis=1, keepdims=True)
        pivot = jnp.sum(jnp.where(at_step[:1], pivot_row, blank[:1]), axis=1, keepdims=True)
        pivot_row = pivot_row / pivot
        work[...] = jnp.where(rows == step, pivot_row, values - factors * pivot_row)
        return 0

    lax.fori_loop(0, count, eliminate, 0)
    values = work[...]
    if count % 128:
        return pltpu.roll(values, width - count, 1)
    return values[:, count : 2 * count]


def answer(inverse, sums):
    return jnp.sum(inverse * sums, axis=0, keepdims=True)


def at_box(values, row_side, col_side):
    long_pos, across_pos, long_count, across_count = position()
    there_long, there_across = long_pos + row_side, across_pos + col_side
    inside = (
        (there_long >= 0)
        & (there_long < long_count)
        & (there_across >= 0)
        & (there_across < across_count)
    )
    lanes = lax.broadcasted_iota(jnp.int32, values.shape, 1)
    wanted = (lanes == there_long * across_count + there_across) & inside
    return jnp.sum(jnp.where(wanted, values, jnp.zeros_like(values)), axis=1, keepdims=True)


def coarse_corrections(parts, *refs):
    table_parts, (out, work) = refs[:parts], refs[parts:]
    count = work.shape[0]
    numbers = last_rows_merged(table_parts, count)
    across_count = lax.axis_size("narrow")
    inverse = coarse_inverse(numbers, work)
    sums = column(numbers, IMAGE_SUM)
    sums = sums - column(pltpu.roll(numbers, count - across_count, 0), FLOW_LONG_LOW)
    sums = sums - column(pltpu.roll(numbers, across_count, 0), FLOW_LONG_HIGH)
    sums = sums - column(pltpu.roll(numbers, count - 1, 0), FLOW_ACROSS_LOW)
    sums = sums - column(pltpu.roll(numbers, 1, 0), FLOW_ACROSS_HIGH)
    load_sums = column(numbers, LOAD_SUM)
    sums = load_sums * (1.0 - 1.0 / cheb_center) - sums
    out[0:1, :] = answer(inverse, load_sums) * (1.0 / cheb_center)
    out[1:2, :] = answer(inverse, sums) * gain


def second_solve(box, local, low, high, left, right, inverses, answers, *rest):
    to_long, to_across, to_deep, mass, load_window = rest[:5]
    tables = rest[5 : 5 + N_TABLES]
    iterate, top, bottom, last_col, first_col, out = rest[5 + N_TABLES : 11 + N_TABLES]
    window, spectral, middle, sems = rest[11 + N_TABLES :]
    long_pos, across_pos, long_count, across_count = position()
    coarse = answers[0:1, :]
    own_shift = at_box(answers[1:2, :], 0, 0)
    shifts = {
        (row_side, col_side): at_box(coarse, row_side, col_side)
        for row_side in (-1, 0, 1)
        for col_side in (-1, 0, 1)
    }

    def add(values, row_side, col_side):
        shift = shifts[row_side, col_side]
        if values.ndim == 3:
            shift = shift.reshape(1, 1, 1)
        return values + shift

    edge = REACH * box.across
    low, high = (
        ref.at[:edge].reshape(REACH, box.across, box.deep) for ref in (low, high)
    )
    wide_sides, narrow_sides = Sides("wide", low, high), Sides("narrow", left, right)
    fill_window(box, window, local, wide_sides, narrow_sides, REACH, 0, REACH, add)
    weights = (to_long, to_across, to_deep, mass)

    steps = range(box.ey // 8)
    x = [some_cols(box, window, 1, step) for step in range(-1, len(steps) + 1)]
    flow = [
        some_cols(box, to_long, 0, step) * (x[step + 1] - some_cols(box, window, 0, step))
        for step in steps
    ]
    state = [x, flow]

    def divided(values, col):
        return values * inverses[col]

    def residual(start_row):
        rows = []
        for row in range(start_row + 1, start_row + 9):
            image, *state[:] = negative_image(box, window, row, row, *state, weights)
            image = [some_cols(box, load_window, row, step) + image[step] for step in steps]
            rows.append(jnp.concatenate(image, axis=0))
        return jnp.stack(rows)

    inner = slice(EDGE, EDGE + box.across)
    first = REACH
    row_ids = lax.broadcasted_iota(jnp.int32, (1, padded(box.ex)), 1)
    col_ids = lax.broadcasted_iota(jnp.int32, (1, padded(box.ey)), 1)
    col_ids = (col_ids & 7) * (box.ey // 8) + lax.shift_right_logical(col_ids, 3)
    row_mask = jnp.where(row_ids < MARGIN, as_float(long_pos > 0), 1.0)
    row_mask = jnp.where(row_ids >= MARGIN + box.long, as_float(long_pos < long_count - 1), row_mask)
    col_mask = jnp.where(col_ids < MARGIN, as_float(across_pos > 0), 1.0)
    col_mask = jnp.where(
        col_ids >= MARGIN + box.across, as_float(across_pos < across_count - 1), col_mask
    )
    keep = 1.0 + rho_second * rho_first
    copies = []

    def emit(start, values):
        rows = values.reshape(8, box.across, box.deep)
        before = window[first + start : first + start + 8, inner, :]
        shift = own_shift.reshape(1, 1, 1)
        iterate[start : start + 8] = keep * before + (gain * rows + shift)
        copies.append(
            pltpu.make_async_copy(
                iterate.at[start : start + 8], out.at[start : start + 8], sems.at[len(copies)]
            )
        )
        copies[-1].start()

    box_solve(
        box, residual, divided, tables, row_mask, col_mask, spectral, middle, emit
    )
    rows = in_order(is_even("wide"), iterate[box.long - 1], iterate[0])
    top[...], bottom[...] = rows
    flat = iterate.reshape(box.long * box.across, box.deep)
    cols = [flat[row_of(box.across, col, box.long), :] for col in (box.across - 1, 0)]
    last_col[...], first_col[...] = in_order(is_even("narrow"), *cols)
    for copy in copies:
        copy.wait()


def inner_residual(
    box, load, iterate, to_long, to_across, to_deep, mass, rows, cols, out, window, result, sems
):
    inner = slice(EDGE, EDGE + box.across)
    flat = window.reshape((box.long + 2) * box.cols, box.deep)
    iterate_flat = iterate.reshape(box.long * box.across, box.deep)
    blank = jnp.zeros((box.long + 2, EDGE, box.deep), jnp.float32)
    window[:, :EDGE, :] = blank
    window[:, EDGE + box.across :, :] = blank
    window[1 : 1 + box.long, inner, :] = iterate[...]
    window[0, inner, :] = iterate[0]
    window[1 + box.long, inner, :] = iterate[box.long - 1]
    for col, place in ((0, EDGE - 1), (box.across - 1, EDGE + box.across)):
        values = iterate_flat[row_of(box.across, col, box.long), :]
        flat[row_of(box.cols, place, box.long, 1), :] = values
    weights = (to_long, to_across, to_deep, mass)
    steps = range(box.ey // 8)
    x = [some_cols(box, window, 1, step) for step in range(-1, len(steps) + 1)]
    flow = [jnp.zeros((8, box.deep), jnp.float32) for _ in steps]
    middle = slice(8, box.across - 8)
    copies = []
    for row in range(box.long):
        image, x, flow = negative_image(box, window, row + 1, REACH + row, x, flow, weights)
        for step in steps:
            place = pl.ds(EDGE - MARGIN + step, 8, stride=box.ey // 8)
            result[row, place, :] = image[step]
        values = load[row] + result[row, inner]
        result[row, inner] = values
        cols[0, row] = values[:8]
        cols[1, row] = values[box.across - 8 :]
        if row == 0:
            rows[0] = values
        if row == box.long - 1:
            rows[1] = values
        if row % 8 == 7:
            part = slice(row - 7, row + 1)
            copy = pltpu.make_async_copy(
                result.at[part, EDGE + 8 : EDGE + box.across - 8],
                out.at[part, middle],
                sems.at[row // 8],
            )
            copy.start()
            copies.append(copy)
    for copy in copies:
        copy.wait()


def outer_residual(
    box, iterate, low, high, left, right, to_long, to_across, rows, cols, inner_out, out,
    row_part, col_part, sems
):
    del inner_out
    inner = slice(EDGE, EDGE + box.across)
    middle = slice(8, box.across - 8)
    wide_sides, narrow_sides = Sides("wide", low, high), Sides("narrow", left, right)
    last = box.long - 1
    iterate_flat = iterate.reshape(box.long * box.across, box.deep)
    across_flat = to_across.reshape(box.flat, box.deep)
    below = to_long[REACH - 1, inner] * (wide_sides.low(Ellipsis) - iterate[0])
    above = to_long[REACH + last, inner] * (wide_sides.high(Ellipsis) - iterate[last])
    row_part[0] = (rows[0] + below)[middle]
    row_part[1] = (rows[1] + above)[middle]
    copies = [
        pltpu.make_async_copy(row_part.at[0], out.at[0, middle], sems.at[0]),
        pltpu.make_async_copy(row_part.at[1], out.at[last, middle], sems.at[1]),
    ]
    for copy in copies:
        copy.start()
    col_part[...] = cols[...]
    flat = col_part.reshape(2 * box.long * 8, box.deep)
    for side, (from_side, col, face, tile) in enumerate(
        (
            (narrow_sides.low, 0, EDGE - 1, slice(0, 8)),
            (narrow_sides.high, box.across - 1, EDGE + box.across - 1, slice(box.across - 8, None)),
        )
    ):
        weight = across_flat[row_of(box.cols, face, box.long, REACH), :]
        own = iterate_flat[row_of(box.across, col, box.long), :]
        place = pl.ds(side * box.long * 8 + side * 7, box.long, stride=8)
        flat[place, :] = flat[place, :] + weight * (from_side(Ellipsis) - own)
        col_part[side, 0] = col_part[side, 0] + below[tile]
        col_part[side, last] = col_part[side, last] + above[tile]
        first_col = side * (box.across - 8)
        copy = pltpu.make_async_copy(
            col_part.at[side], out.at[:, first_col : first_col + 8], sems.at[2 + side]
        )
        copy.start()
        copies.append(copy)
    for copy in copies:
        copy.wait()


def swaps(axis):
    sizes = (lax.axis_size("wide"), lax.axis_size("narrow"))
    along = ("wide", "narrow").index(axis)
    size, beside = sizes[along], sizes[1 - along]

    def number(place, other_place):
        pair = (place, other_place) if along == 0 else (other_place, place)
        return pair[0] * sizes[1] + pair[1]

    ways = []
    for way in range(2):
        pairs = []
        for place in range(size):
            for other_place in range(beside):
                partner = place + 1 if place % 2 == way else place - 1
                there = other_place
                if not 0 <= partner < size:
                    partner = place
                    there = other_place ^ 1 if beside % 2 == 0 else other_place
                pairs.append((number(place, other_place), number(partner, there)))
        ways.append(pairs)
    return ways


def exchange(axis, first, second):
    ways = swaps(axis)
    axes = ("wide", "narrow")
    return lax.ppermute(first, axes, ways[0]), lax.ppermute(second, axes, ways[1])


def two_away(axis, table):
    size = lax.axis_size(axis)
    return lax.ppermute(table, axis, [(i, (i + 2) % size) for i in range(size)])


def tell(table):
    count = table.shape[0]
    long_pos, across_pos, _, across_count = position()
    own = lax.dynamic_slice_in_dim(table, long_pos * across_count + across_pos, 1, axis=0)
    line = jnp.broadcast_to(own, (count, 1, 128))
    told = lax.all_to_all(line, ("wide", "narrow"), split_axis=0, concat_axis=0, tiled=True)
    return told.reshape(count, 128)


def on_device(zone, scale, diffusivity, decay, load):
    box = Box(load.shape)
    long, across, deep = load.shape
    count = lax.axis_size("wide") * lax.axis_size("narrow")
    by_margins = lax.axis_size("wide") == 4 and lax.axis_size("narrow") == 4
    tables = tables_of(box)
    decay = decay.reshape(1, -1)
    cells = f32(long, across, deep)
    whole_zone = jax.ShapeDtypeStruct(cells.shape, zone.dtype)
    window = f32(box.rows, box.cols, deep)
    table_shape = f32(count, 128)
    anywhere = pl.BlockSpec(memory_space=pl.ANY)
    in_hbm = pl.BlockSpec(memory_space=pltpu.HBM)

    def scratch(shape):
        return pltpu.VMEM(shape, jnp.float32)

    def pinned(field):
        return pltpu.with_memory_space_constraint(field, pltpu.HBM)

    spectral = scratch((box.ey, padded(box.ex), deep))
    middle = scratch((long, padded(box.ey), deep))

    def pack(wide, fields, sides, parts=(), after=()):
        rows = message_rows(box, wide * len(fields)) + (count if parts else 0)
        message = f32(rows, deep)
        body = functools.partial(pack_fields, box, wide, len(fields), len(parts), len(after))
        return call(
            body,
            (message, message) + ((table_shape,) if parts else ()),
            [VMEM] * (len(fields) + 2 + len(parts)) + [anywhere] * len(after),
        )(*fields, *sides, *parts, *after)

    far = f32(2 * REACH, across, deep)
    far_zone, far_scale, far_load = pinned(zone), pinned(scale), pinned(load)
    load_first, load_second, first, second = call(
        functools.partial(bring_edges, box),
        (f32(MARGIN, across, deep),) * 2 + (far, far),
        [in_hbm] * 3,
        [pltpu.VMEM((2, REACH, across, deep), zone.dtype), pltpu.SemaphoreType.DMA((6,))],
    )(far_zone, far_scale, far_load)
    load, scale, zone, sums, table = call(
        functools.partial(bring_box, box),
        (cells, cells, whole_zone, f32(8, 128), table_shape),
        [in_hbm] * 3 + [anywhere] + [VMEM] * 2,
        [pltpu.SemaphoreType.DMA((3 * (long // 8),))],
    )(far_load, far_scale, far_zone, load_first, diffusivity, decay)
    load_wide = exchange("wide", load_first, load_second)
    far_wide = exchange("wide", first, second)
    load_first, load_second = pack(MARGIN, [load], load_wide)
    load_narrow = exchange("narrow", load_first, load_second)
    far_narrow = exchange("narrow", *pack(REACH, [scale, zone], far_wide))
    message = f32(REACH * across, deep)
    load_window, local, image, inverses, first, second = call(
        functools.partial(first_solve, box),
        (window, cells, f32(across, deep), f32(box.ey, box.ex, deep), message, message),
        [VMEM] * 8 + [VMEM] * 2 + [VMEM] * N_TABLES,
        [spectral, middle],
        flops=4 * 10**9,
    )(load, *load_wide, *load_narrow, sums, zone, scale, diffusivity, decay, *tables)
    wide = exchange("wide", first, second)
    table = call(functools.partial(image_sums, box), table_shape, [VMEM] * 10)(
        zone, scale, local, image, *far_wide, *far_narrow, table, diffusivity
    )
    own_table = table
    parts = (table,)
    if by_margins:
        partner = lax.ppermute(table, ("wide", "narrow"), swaps("wide")[0])
        table = call(join_rows, table_shape, [VMEM] * 2)(table, partner)
        parts = (table, two_away("wide", table))
    to_long, to_across, *windows = call(
        functools.partial(side_weights, box),
        (window,) * 4,
        [VMEM] * 6 + [VMEM],
        flops=10**9,
    )(zone, scale, *far_wide, *far_narrow, diffusivity)
    to_deep, mass = call(
        functools.partial(deep_weights, box),
        (window,) * 2,
        [VMEM] * 2 + [VMEM] * 2,
        flops=10**9,
    )(*windows, diffusivity, decay)
    weights = (to_long, to_across, to_deep, mass)
    first, second, table = pack(REACH, [local], wide, parts, [to_long])
    narrow = exchange("narrow", first, second)
    if by_margins:
        table = call(join_rows, table_shape, [VMEM] * 2)(table, narrow[0])
        parts = (table, two_away("narrow", table))
    else:
        parts = (tell(own_table),)
    row, col = f32(across, deep), f32(long, deep)
    answers = call(
        functools.partial(coarse_corrections, len(parts)),
        f32(8, -(-count // 128) * 128),
        [VMEM] * len(parts),
        [scratch((count, -(-2 * count // 128) * 128))],
    )(*parts)
    iterate, first_row, second_row, first_col, second_col, result = call(
        functools.partial(second_solve, box),
        (cells, row, row, col, col, cells),
        [VMEM] * (12 + N_TABLES),
        [scratch(window.shape), spectral, middle, pltpu.SemaphoreType.DMA((long // 8,))],
        flops=4 * 10**9,
        out_spec=(VMEM,) * 5 + (anywhere,),
    )(local, *wide, *narrow, inverses, answers, *weights, load_window, *tables)
    narrow = exchange("narrow", first_col, second_col)
    wide = exchange("wide", first_row, second_row)
    rows, cols, inner = call(
        functools.partial(inner_residual, box),
        (f32(2, across, deep), f32(2, long, 8, deep), cells),
        [VMEM] * 6,
        [
            scratch((long + 2, box.cols, deep)),
            scratch((long, box.cols, deep)),
            pltpu.SemaphoreType.DMA((long // 8,)),
        ],
        flops=10**9,
        out_spec=(VMEM, VMEM, anywhere),
    )(load, iterate, *weights)
    residual = call(
        functools.partial(outer_residual, box),
        cells,
        [VMEM] * 9 + [anywhere],
        [
            scratch((2, across - 16, deep)),
            scratch((2, long, 8, deep)),
            pltpu.SemaphoreType.DMA((4,)),
        ],
        out_spec=anywhere,
        aliases={9: 0},
    )(iterate, *wide, *narrow, to_long, to_across, rows, cols, inner)
    return result, residual


def solution(mesh):
    split = P(("groups", "wide"), "narrow", None)
    return jax.shard_map(
        on_device,
        mesh=mesh,
        in_specs=(split, split, P(), P(), split),
        out_specs=(split, split),
        check_vma=False,
    )
```

```python
import functools

import jax
import jax.numpy as jnp
import ml_dtypes
import numpy as np
from jax import lax
from jax.experimental import pallas as pl
from jax.experimental.pallas import tpu as pltpu
from jax.sharding import PartitionSpec as P

MARGIN = 4
REACH = MARGIN + 1
EDGE = 8

cheb_center = 1.3
cheb_radius = 1.2
cheb_ratio = 1.3 / 1.2
rho_first = 1.0 / cheb_ratio
rho_second = 1.0 / (2.0 * cheb_ratio - rho_first)
gain = 2.0 * rho_second / cheb_radius

MEANS = range(4)
BOX_DIAGONAL, LONG_HIGH, LONG_LOW, ACROSS_HIGH, ACROSS_LOW, LOAD_SUM = range(4, 10)
IMAGE_SUM, FLOW_LONG_HIGH, FLOW_LONG_LOW, FLOW_ACROSS_HIGH, FLOW_ACROSS_LOW = range(16, 21)

VMEM = pl.BlockSpec(memory_space=pltpu.VMEM)


def sine_basis(length):
    indices = np.arange(1, length + 1)
    phases = indices[:, None] * indices[None, :] % (2 * (length + 1))
    table = np.sqrt(2.0 / (length + 1)) * np.sin(np.pi * phases / (length + 1))
    eigvals = 4.0 * np.sin(np.pi * indices / (2.0 * (length + 1))) ** 2
    return table.astype(np.float32), eigvals.astype(np.float32)


def call(body, out_shape, in_specs, scratch=(), flops=0, out_spec=None, aliases=None):
    return pl.pallas_call(
        body,
        out_shape=out_shape,
        in_specs=in_specs,
        out_specs=out_spec or jax.tree.map(lambda _: VMEM, out_shape),
        scratch_shapes=list(scratch),
        compiler_params=pltpu.CompilerParams(vmem_limit_bytes=30 * 2**20),
        cost_estimate=pl.CostEstimate(flops=flops, bytes_accessed=0, transcendentals=0),
        input_output_aliases=aliases or {},
    )


def f32(*shape):
    return jax.ShapeDtypeStruct(shape, jnp.float32)


class Box:
    def __init__(self, shape):
        self.long, self.across, self.deep = shape
        self.ex = self.long + 2 * MARGIN
        self.ey = self.across + 2 * MARGIN
        self.rows = self.long + 2 * REACH
        self.cols = self.across + 2 * EDGE
        self.flat = self.rows * self.cols


def pieces(values, count):
    parts = []
    for _ in range(count - 1):
        scaled = values * 65537.0
        part = scaled - (scaled - values)
        parts.append(part)
        values = values - part
    return parts + [values]


def left_table(table, depth, count):
    rows, cols = table.shape
    wide = np.zeros((rows, depth), np.float32)
    wide[:, :cols] = table
    parts = []
    rest = wide
    for _ in range(count):
        part = rest.astype(ml_dtypes.bfloat16).astype(np.float32)
        parts.append(part)
        rest = rest - part
    blank = np.zeros_like(parts[0])
    lines = []
    for index in range(count):
        used = count - index if count > 2 else count
        lines.append(np.concatenate([parts[index]] * used + [blank] * (count - used), axis=1))
    return np.concatenate(lines, axis=0)


def right_tables(table):
    rest, parts = table, []
    for _ in range(3):
        part = rest.astype(ml_dtypes.bfloat16).astype(np.float32)
        parts.append(part)
        rest = rest - part
    both = np.concatenate([parts[0], parts[1]], axis=1)
    return np.concatenate([both, both], axis=0), np.concatenate([parts[2], parts[0]], axis=0)


def padded(size):
    return -(-size // 8) * 8


FORWARD, BACKWARD = 2, 3


def tables_of(box):
    sine_x, eig_x = sine_basis(box.ex)
    sine_y, eig_y = sine_basis(box.ey)
    sine_z, eig_z = sine_basis(box.deep)
    in_order_of_steps = np.arange(box.ey).reshape(8, box.ey // 8).T.reshape(-1)
    from_y = sine_y[MARGIN : MARGIN + box.across]
    from_x = sine_x[MARGIN : MARGIN + box.long]
    spread_x = np.broadcast_to(eig_x[:, None], (box.ex, box.deep))
    spread_y = np.broadcast_to(eig_y[:, None], (box.ey, box.deep))
    main_z, rest_z = right_tables(sine_z)
    return [
        jnp.asarray(np.ascontiguousarray(t))
        for t in (
            left_table(sine_y[:, in_order_of_steps], padded(box.ey), FORWARD),
            left_table(sine_x, padded(box.ex), FORWARD),
            left_table(from_x, padded(box.ex), BACKWARD),
            left_table(from_y, padded(box.ey), BACKWARD),
            main_z,
            rest_z,
            spread_x,
            spread_y,
            eig_z[None, :],
        )
    ]


N_TABLES = 9


def one_pass(left, right):
    return lax.dot_general(
        left,
        right,
        (((1,), (0,)), ((), ())),
        precision=lax.Precision.DEFAULT,
        preferred_element_type=jnp.float32,
    )


def dot_left(table, values, count, rows):
    total = one_pass(table, jnp.concatenate(pieces(values, count), axis=0))
    return sum(total[index * rows : (index + 1) * rows] for index in range(1, count)) + total[:rows]


def dot_right(values, main, rest, count):
    deep = values.shape[1]
    parts = pieces(values, count)
    total = one_pass(jnp.concatenate(parts[:2], axis=1), main)
    result = total[:, :deep] + total[:, deep:]
    if count == 3:
        result = result + one_pass(jnp.concatenate([parts[0], parts[2]], axis=1), rest)
    return result


def with_rows(values, rows):
    if values.shape[0] == rows:
        return values
    blank = jnp.zeros((rows - values.shape[0],) + values.shape[1:], values.dtype)
    return jnp.concatenate([values, blank], axis=0)


FORWARD_ROWS, COLS_ABREAST, BACKWARD_ROWS = 24, 40, 32


def fitting(size, wanted):
    return max(part for part in range(8, wanted + 1, 8) if size % part == 0)


def beside(values):
    return jnp.concatenate(values, axis=1)


def apart(values, lanes):
    return [values[:, start : start + lanes] for start in range(0, values.shape[1], lanes)]


def box_solve(box, source, divided, tables, row_mask, col_mask, spectral, middle, emit):
    into_y, into_x, from_x, from_y, main_z, rest_z = tables[:6]
    deep = box.deep
    deep_x, deep_y = padded(box.ex), padded(box.ey)
    into_y, into_x = into_y[...], into_x[...]
    if col_mask is not None:
        mask = jnp.concatenate([col_mask] * FORWARD, axis=1)
        into_y = into_y * mask
        mask = jnp.concatenate([row_mask] * FORWARD, axis=1)
        into_x = into_x * mask
    from_x, from_y, main_z, rest_z = from_x[...], from_y[...], main_z[...], rest_z[...]
    spectral_flat = spectral.reshape(box.ey * deep_x, deep)
    middle_flat = middle.reshape(box.long * deep_y, deep)
    if deep_x > box.ex:
        spectral[:, box.ex :, :] = jnp.zeros((box.ey, deep_x - box.ex, deep), jnp.float32)
    if deep_y > box.ey:
        middle[:, box.ey :, :] = jnp.zeros((box.long, deep_y - box.ey, deep), jnp.float32)
    step = fitting(box.ex, FORWARD_ROWS)
    for start in range(0, box.ex, step):
        block = jnp.concatenate([source(row) for row in range(start, start + step, 8)], axis=0)
        block = dot_right(block.reshape(step * box.ey, deep), main_z, rest_z, FORWARD)
        block = block.reshape(step, box.ey, deep)
        wide = beside([block[row] for row in range(step)])
        wide = dot_left(into_y, with_rows(wide, deep_y), FORWARD, box.ey)
        for row, values in enumerate(apart(wide, deep)):
            spectral_flat[pl.ds(start + row, box.ey, stride=deep_x), :] = values
    step = fitting(box.ey, COLS_ABREAST)
    for start in range(0, box.ey, step):
        wide = beside([spectral[col] for col in range(start, start + step)])
        wide = apart(dot_left(into_x, wide, FORWARD, box.ex), deep)
        wide = beside([divided(values, start + part) for part, values in enumerate(wide)])
        wide = dot_left(from_x, with_rows(wide, deep_x), BACKWARD, box.long)
        for part, values in enumerate(apart(wide, deep)):
            middle_flat[pl.ds(start + part, box.long, stride=deep_y), :] = values
    step = fitting(box.long, BACKWARD_ROWS)
    for start in range(0, box.long, step):
        wide = beside([middle[row] for row in range(start, start + step)])
        parts = apart(dot_left(from_y, wide, BACKWARD, box.across), deep)
        values = dot_right(jnp.concatenate(parts, axis=0), main_z, rest_z, BACKWARD)
        for row in range(0, step, 8):
            emit(start + row, values[row * box.across : (row + 8) * box.across])


def position():
    long_pos, across_pos = lax.axis_index("wide"), lax.axis_index("narrow")
    return long_pos, across_pos, lax.axis_size("wide"), lax.axis_size("narrow")


def as_float(flag):
    return jnp.where(flag, jnp.float32(1.0), jnp.float32(0.0))


def is_even(axis):
    return lax.rem(lax.axis_index(axis), 2) == 0


class Sides:
    def __init__(self, axis, first, second):
        position = lax.axis_index(axis)
        self.even = is_even(axis)
        self.has_low = as_float(position > 0)
        self.has_high = as_float(position < lax.axis_size(axis) - 1)
        self.first, self.second = first, second

    def low(self, *index):
        return jnp.where(self.even, self.second[index], self.first[index]) * self.has_low

    def high(self, *index):
        return jnp.where(self.even, self.first[index], self.second[index]) * self.has_high


def in_order(even, up, down):
    return jnp.where(even, up, down), jnp.where(even, down, up)


def row_of(stride, col, count, first=0):
    return pl.ds(first * stride + col, count, stride=stride)


def pack_columns(box, fields, wide_sides, wide, first, second):
    corner = len(fields) * wide * box.long
    even = is_even("narrow")
    place = 0
    for field, sides in zip(fields, wide_sides):
        for step in range(wide):
            cols = (box.across - wide + step, step)
            values = [field[row_of(box.across, col, box.long), :] for col in cols]
            low = [sides.low(row_of(box.across, col, wide), slice(None)) for col in cols]
            high = [sides.high(row_of(box.across, col, wide), slice(None)) for col in cols]
            at = corner + 2 * REACH * place
            for start, parts in ((place * box.long, values), (at, low), (at + REACH, high)):
                parts = in_order(even, *(part.astype(jnp.float32) for part in parts))
                size = parts[0].shape[0]
                first[start : start + size, :], second[start : start + size, :] = parts
            place += 1


def message_rows(box, count):
    return -(-(count * (box.long + 2 * REACH)) // 8) * 8


def pack_fields(box, wide, fields, tables, after, *refs):
    own, (low, high), refs = refs[:fields], refs[fields : fields + 2], refs[fields + 2 :]
    parts, (first, second, *table) = refs[:tables], refs[tables + after :]
    size = wide * box.across
    flat = [field.reshape(box.long * box.across, box.deep) for field in own]
    low = low.reshape(low.size // box.deep, box.deep)
    high = high.reshape(high.size // box.deep, box.deep)
    sides = [
        Sides("wide", *(ref.at[index * size : (index + 1) * size] for ref in (low, high)))
        for index in range(fields)
    ]
    pack_columns(box, flat, sides, wide, first, second)
    if tables:
        known = last_rows_merged(parts, table[0].shape[0])
        table[0][...] = known
        first[first.shape[0] - known.shape[0] :, :] = known
        second[second.shape[0] - known.shape[0] :, :] = known


def bring_edges(box, zone, scale, load, load_first, load_second, first, second, staged, sems):
    even = is_even("wide")

    def edges(wide):
        up, down = box.long - wide, 0
        return [pl.ds(jnp.where(even, *pair), wide) for pair in ((up, down), (down, up))]

    copies = [
        (zone.at[edges(REACH)[0]], staged.at[0]),
        (zone.at[edges(REACH)[1]], staged.at[1]),
        (load.at[edges(MARGIN)[0]], load_first),
        (load.at[edges(MARGIN)[1]], load_second),
        (scale.at[edges(REACH)[0]], first.at[:REACH]),
        (scale.at[edges(REACH)[1]], second.at[:REACH]),
    ]
    copies = [
        pltpu.make_async_copy(source, target, sems.at[index])
        for index, (source, target) in enumerate(copies)
    ]
    for copy in copies:
        copy.start()
    for copy in copies[:2]:
        copy.wait()
    first[REACH:] = staged[0].astype(jnp.float32)
    second[REACH:] = staged[1].astype(jnp.float32)
    for copy in copies[2:]:
        copy.wait()


def fill_window(box, window, own, wide_sides, narrow_sides, wide, place, total, add=None):
    flat = window.reshape(box.flat, box.deep)
    nothing = jnp.zeros((box.rows, EDGE, box.deep), jnp.float32)
    window[:, :EDGE, :] = nothing
    window[:, EDGE + box.across :, :] = nothing
    if add is None:
        add = lambda values, row_side, col_side: values
    inner = slice(EDGE, EDGE + box.across)
    first, last = REACH, REACH + box.long
    if wide < REACH:
        blank = jnp.zeros((1, box.across, box.deep), jnp.float32)
        window[0:1, inner, :] = blank
        window[box.rows - 1 :, inner, :] = blank
    window[first:last, inner, :] = add(own[...].astype(jnp.float32), 0, 0)
    window[first - wide : first, inner, :] = add(wide_sides.low(Ellipsis), -1, 0)
    window[last : last + wide, inner, :] = add(wide_sides.high(Ellipsis), 1, 0)
    corner = total * box.long
    for step in range(wide):
        for source, col, side in (
            (narrow_sides.low, EDGE - wide + step, -1),
            (narrow_sides.high, EDGE + box.across + step, 1),
        ):
            for start, size, row, row_side in (
                ((place + step) * box.long, box.long, first, 0),
                (corner + 2 * REACH * (place + step), wide, first - wide, -1),
                (corner + 2 * REACH * (place + step) + REACH, wide, last, 1),
            ):
                values = source(slice(start, start + size), slice(None))
                flat[row_of(box.cols, col, size, row), :] = add(values, row_side, side)


def some_cols(box, ref, row, step):
    stride = box.ey // 8
    return ref[row, pl.ds(EDGE - MARGIN + step, 8, stride=stride), :]


def negative_image(box, window, row, at, x, flow_before, weights):
    to_long, to_across, to_deep, mass = weights
    steps = range(box.ey // 8)
    x_next = [some_cols(box, window, row + 1, step) for step in range(-1, len(steps) + 1)]
    flow_long = [
        some_cols(box, to_long, at, step) * (x_next[step + 1] - x[step + 1]) for step in steps
    ]
    flow_across = [
        some_cols(box, to_across, at, step) * (x[step + 2] - x[step + 1])
        for step in range(-1, len(steps))
    ]
    totals = []
    for step in steps:
        here = x[step + 1]
        lanes = here.shape[1]
        flow_deep = some_cols(box, to_deep, at, step) * (pltpu.roll(here, lanes - 1, 1) - here)
        total = flow_long[step] - flow_before[step] - some_cols(box, mass, at, step) * here
        total = total + (flow_across[step + 1] - flow_across[step])
        totals.append(total + (flow_deep - pltpu.roll(flow_deep, 1, 1)))
    return totals, x_next, flow_long


def in_steps(box, refs, rows):
    return jnp.stack(
        [
            jnp.concatenate([some_cols(box, ref, row, step) for step in range(box.ey // 8)], axis=0)
            for ref, row in zip(refs, rows)
        ]
    )


def looked_up(labels, values):
    return jnp.where(labels == 0, values[0], jnp.where(labels == 1, values[1], values[2]))


def at_own_row(line, shape):
    long_pos, across_pos, _, across_count = position()
    rows = lax.broadcasted_iota(jnp.int32, shape, 0)
    own = rows == long_pos * across_count + across_pos
    return jnp.where(own, line[:1], jnp.zeros(shape, jnp.float32))


def merged(table, *others):
    for other in others:
        table = jnp.where(table != 0.0, table, other)
    return table


def last_rows_merged(refs, count):
    return merged(*(ref[ref.shape[0] - count :, :] for ref in refs))


def join_rows(table, message, out):
    out[...] = last_rows_merged((table, message), out.shape[0])


def line_of(numbers, shape):
    count = -(-len(numbers) // 8) * 8
    rows = lax.broadcasted_iota(jnp.int32, (count, shape[1]), 0)
    lanes = lax.broadcasted_iota(jnp.int32, (count, shape[1]), 1)
    stacked = jnp.zeros((count, shape[1]), jnp.float32)
    place = jnp.zeros((count, shape[1]), jnp.bool_)
    for row, (index, values) in enumerate(numbers):
        stacked = jnp.where(rows == row, values, stacked)
        place = place | ((rows == row) & (lanes == index))
    sums = jnp.sum(stacked, axis=1, keepdims=True)
    line = jnp.sum(jnp.where(place, sums, jnp.zeros_like(stacked)), axis=0, keepdims=True)
    return jnp.broadcast_to(line, shape)


def bring_box(
    box, far_load, far_scale, far_zone, after, diffusivity, decay, load, scale, zone, out, table, sems
):
    del after
    size = 8
    copies = []
    for start in range(0, box.long, size):
        rows = slice(start, start + size)
        for source, target in ((far_load, load), (far_scale, scale), (far_zone, zone)):
            copies.append(
                pltpu.make_async_copy(source.at[rows], target.at[rows], sems.at[len(copies)])
            )
            copies[-1].start()
    nothing = jnp.zeros((box.across, box.deep), jnp.float32)
    half = [[0.5 * diffusivity[z : z + 1, d : d + 1] for z in range(3)] for d in range(3)]
    rates = [decay[0:1, z : z + 1] for z in range(3)]

    def halves(row):
        labels, factor = zone[row], scale[row]
        return [looked_up(labels, half[d]) * factor for d in range(3)] + [looked_up(labels, rates)]

    sums = [nothing] * 5
    for start in range(0, box.long, size):
        for copy in copies[start // size * 3 : start // size * 3 + 3]:
            copy.wait()
        for row in range(start, start + size):
            sums = [total + more for total, more in zip(sums, halves(row) + [load[row]])]

    def total(values):
        return jnp.sum(values, axis=0, keepdims=True)

    cells = box.long * box.across * box.deep
    numbers = [(index, total(sums[index]) * (2.0 / cells)) for index in range(3)]
    mass = total(sums[3])
    numbers += [(3, mass / cells)]
    lane = lax.broadcasted_iota(jnp.int32, (1, box.deep), 1)
    ends = jnp.where((lane == 0) | (lane == box.deep - 1), total(sums[2]), 0.0)
    numbers += [
        (BOX_DIAGONAL, mass + ends),
        (LONG_HIGH, total(halves(box.long - 1)[0])),
        (LONG_LOW, total(halves(0)[0])),
        (ACROSS_HIGH, sums[1][box.across - 1 :]),
        (ACROSS_LOW, sums[1][:1]),
        (LOAD_SUM, total(sums[4])),
    ]
    line = line_of(numbers, out.shape)
    out[...] = line
    table[...] = at_own_row(line, table.shape)


def means_of(ref):
    return [ref[0:1, index : index + 1] for index in range(4)]


def first_solve(box, load, low, high, left, right, means, zone, scale, diffusivity, decay, *rest):
    tables = rest[:N_TABLES]
    window, local, image, inverses, first, second, spectral, middle = rest[N_TABLES:]
    spread_x, spread_y, eig_z = tables[6:]
    means = means_of(means)
    base = means[3] + means[0] * spread_x[...] + means[2] * eig_z[...]

    def divided(values, col):
        divisor = base + means[1] * spread_y[col : col + 1, :]
        inverse = pl.reciprocal(divisor, approx=True)
        for _ in range(2):
            inverse = inverse * (2.0 - divisor * inverse)
        inverses[col] = inverse
        return values * inverse

    half = [0.5 * diffusivity[z : z + 1, 2:3] for z in range(3)]
    rates = [decay[0:1, z : z + 1] for z in range(3)]
    lane = lax.broadcasted_iota(jnp.int32, (box.across, box.deep), 1)
    ends = jnp.where((lane == 0) | (lane == box.deep - 1), jnp.float32(1.0), jnp.float32(0.0))
    image[...] = jnp.zeros((box.across, box.deep), jnp.float32)
    wide_sides, narrow_sides = Sides("wide", low, high), Sides("narrow", left, right)
    fill_window(box, window, load, wide_sides, narrow_sides, MARGIN, 0, MARGIN)

    def emit(start, values):
        values = values * (1.0 / cheb_center)
        values = values.reshape(8, box.across, box.deep)
        local[start : start + 8] = values
        total = image[...]
        for row in range(8):
            labels = zone[start + row]
            mass = looked_up(labels, rates) + looked_up(labels, half) * scale[start + row] * ends
            total = total + mass * values[row]
        image[...] = total

    box_solve(
        box,
        lambda start: in_steps(box, [window] * 8, range(1 + start, 9 + start)),
        divided,
        tables,
        None,
        None,
        spectral,
        middle,
        emit,
    )
    even = is_even("wide")
    for target, pair in ((first, (box.long - REACH, 0)), (second, (0, box.long - REACH))):
        rows = local[pl.ds(jnp.where(even, *pair), REACH)]
        target[...] = rows.reshape(REACH * box.across, box.deep)


def side_weights(
    box, zone, scale, low, high, left, right, diffusivity, to_long, to_across, zone_window,
    scale_window
):
    for index, (window, own) in enumerate(((scale_window, scale), (zone_window, zone))):
        start = index * REACH
        wide_sides = Sides("wide", *(ref.at[start : start + REACH] for ref in (low, high)))
        narrow_sides = Sides("narrow", left, right)
        fill_window(box, window, own, wide_sides, narrow_sides, REACH, start, 2 * REACH)
    half = [[0.5 * diffusivity[z : z + 1, d : d + 1] for z in range(3)] for d in range(2)]

    def one_row(row, before):
        labels, factor = zone_window[row], scale_window[row]
        now = [looked_up(labels, half[d]) * factor for d in range(2)]
        to_across[row] = now[1] + pltpu.roll(now[1], box.cols - 1, 0)
        to_long[max(row - 1, 0)] = before + now[0]
        return now[0]

    before = jnp.zeros((box.cols, box.deep), jnp.float32)
    for row in range(box.rows):
        before = one_row(row, before)
    to_long[box.rows - 1] = before


def deep_weights(box, zone_window, scale_window, diffusivity, decay, to_deep, mass):
    half = [0.5 * diffusivity[z : z + 1, 2:3] for z in range(3)]
    rates = [decay[0:1, z : z + 1] for z in range(3)]
    lane = lax.broadcasted_iota(jnp.int32, (box.cols, box.deep), 1)
    ends = jnp.where((lane == 0) | (lane == box.deep - 1), jnp.float32(1.0), jnp.float32(0.0))
    not_last = jnp.where(lane == box.deep - 1, jnp.float32(0.0), jnp.float32(1.0))

    def one_row(row):
        labels = zone_window[row]
        now = looked_up(labels, half) * scale_window[row]
        to_deep[row] = (now + pltpu.roll(now, box.deep - 1, 1)) * not_last
        mass[row] = looked_up(labels, rates) + now * ends

    for row in range(box.rows):
        one_row(row)


def image_sums(
    box, zone, scale, local, image, low, high, left, right, table, diffusivity, out
):
    half = [[0.5 * diffusivity[z : z + 1, d : d + 1] for z in range(3)] for d in range(3)]
    shape = (box.long * box.across, box.deep)
    zone_flat, scale_flat, local_flat = zone.reshape(shape), scale.reshape(shape), local.reshape(shape)
    last_col = row_of(box.across, box.across - 1, box.long)
    first_col = row_of(box.across, 0, box.long)

    wide_sides, narrow_sides = Sides("wide", low, high), Sides("narrow", left, right)

    def side(source, place):
        return source(slice(place * box.long, (place + 1) * box.long), slice(None))

    above, below = wide_sides.high, wide_sides.low
    faces = [
        (0, zone[box.long - 1], scale[box.long - 1], local[box.long - 1], above(REACH), above(0)),
        (0, zone[0], scale[0], local[0], below(2 * REACH - 1), below(REACH - 1)),
        (
            1,
            zone_flat[last_col, :],
            scale_flat[last_col, :],
            local_flat[last_col, :],
            side(narrow_sides.high, REACH),
            side(narrow_sides.high, 0),
        ),
        (
            1,
            zone_flat[first_col, :],
            scale_flat[first_col, :],
            local_flat[first_col, :],
            side(narrow_sides.low, 2 * REACH - 1),
            side(narrow_sides.low, REACH - 1),
        ),
    ]
    flows = []
    for direction, labels, factor, values, far_labels, far_factor in faces:
        weight = looked_up(labels, half[direction]) * factor
        weight = weight + looked_up(far_labels, half[direction]) * far_factor
        flows.append(jnp.sum(weight * values, axis=0, keepdims=True))
    long_pos, across_pos, long_count, across_count = position()
    numbers = [
        (IMAGE_SUM, jnp.sum(image[...], axis=0, keepdims=True) + sum(flows)),
        (FLOW_LONG_HIGH, flows[0] * as_float(long_pos < long_count - 1)),
        (FLOW_LONG_LOW, flows[1] * as_float(long_pos > 0)),
        (FLOW_ACROSS_HIGH, flows[2] * as_float(across_pos < across_count - 1)),
        (FLOW_ACROSS_LOW, flows[3] * as_float(across_pos > 0)),
    ]
    known = table[...] + at_own_row(line_of(numbers, (8, out.shape[1])), out.shape)
    out[...] = known

def column(values, index):
    return values[:, index : index + 1]


def uncoupled_groups(count, across):
    places = np.arange(count)
    long_step = np.abs(places[:, None] // across - places[None, :] // across)
    across_step = np.abs(places[:, None] % across - places[None, :] % across)
    coupled = long_step + across_step == 1
    left = list(range(count))
    groups = []
    while left:
        group = []
        for place in sorted(left, key=lambda p: (coupled[p][left].sum(), p)):
            if not coupled[place][group].any():
                group.append(place)
        left = [place for place in left if place not in group]
        for place in group:
            beside = [other for other in left if coupled[place][other]]
            for other in beside:
                coupled[other][beside] = True
                coupled[other][other] = False
        groups.append(group)
    return groups


def coarse_inverse(numbers, work):
    count, width = work.shape
    across = lax.axis_size("narrow")
    beyond = pltpu.roll(numbers, count - across, 0)
    beside = pltpu.roll(numbers, count - 1, 0)
    before = pltpu.roll(numbers, across, 0)
    ahead = pltpu.roll(numbers, 1, 0)
    place = lax.broadcasted_iota(jnp.int32, (count, 1), 0)
    across_pos = lax.rem(place, across)
    nothing = jnp.zeros((count, 1), jnp.float32)
    couplings = []
    diagonal = column(numbers, BOX_DIAGONAL)
    for own, other, there, inside in (
        (LONG_HIGH, LONG_LOW, beyond, place < count - across),
        (LONG_LOW, LONG_HIGH, before, place >= across),
        (ACROSS_HIGH, ACROSS_LOW, beside, across_pos < across - 1),
        (ACROSS_LOW, ACROSS_HIGH, ahead, across_pos > 0),
    ):
        shared = jnp.where(inside, column(there, other), nothing)
        diagonal = diagonal + column(numbers, own) + shared
        couplings.append(jnp.where(inside, column(numbers, own) + shared, nothing))
    rows = lax.broadcasted_iota(jnp.int32, (count, width), 0)
    cols = lax.broadcasted_iota(jnp.int32, (count, width), 1)
    blank = jnp.zeros((count, width), jnp.float32)
    matrix = jnp.where(cols == rows, diagonal, blank)
    for shift, coupling in zip((across, -across, 1, -1), couplings):
        matrix = matrix - jnp.where((cols == rows + shift) & (cols < count), coupling, blank)
    matrix = jnp.where(cols == rows + count, jnp.ones((count, 1), jnp.float32), matrix)
    if count <= 16:
        for group in uncoupled_groups(count, across):
            rest = matrix
            for step in group:
                pivot_row = matrix[step : step + 1, :] / matrix[step : step + 1, step : step + 1]
                rest = rest - matrix[:, step : step + 1] * pivot_row
                rest = jnp.where(rows == step, pivot_row, rest)
            matrix = rest
        return pltpu.roll(matrix, width - count, 1)
    work[...] = matrix

    def eliminate(step, _):
        values = work[...]
        pivot_row = work[pl.ds(step, 1), :]
        at_step = cols == step
        factors = jnp.sum(jnp.where(at_step, values, blank), axis=1, keepdims=True)
        pivot = jnp.sum(jnp.where(at_step[:1], pivot_row, blank[:1]), axis=1, keepdims=True)
        pivot_row = pivot_row / pivot
        work[...] = jnp.where(rows == step, pivot_row, values - factors * pivot_row)
        return 0

    lax.fori_loop(0, count, eliminate, 0)
    values = work[...]
    if count % 128:
        return pltpu.roll(values, width - count, 1)
    return values[:, count : 2 * count]


def answer(inverse, sums):
    return jnp.sum(inverse * sums, axis=0, keepdims=True)


def at_box(values, row_side, col_side):
    long_pos, across_pos, long_count, across_count = position()
    there_long, there_across = long_pos + row_side, across_pos + col_side
    inside = (
        (there_long >= 0)
        & (there_long < long_count)
        & (there_across >= 0)
        & (there_across < across_count)
    )
    lanes = lax.broadcasted_iota(jnp.int32, values.shape, 1)
    wanted = (lanes == there_long * across_count + there_across) & inside
    return jnp.sum(jnp.where(wanted, values, jnp.zeros_like(values)), axis=1, keepdims=True)


def coarse_corrections(parts, *refs):
    table_parts, (out, work) = refs[:parts], refs[parts:]
    count = work.shape[0]
    numbers = last_rows_merged(table_parts, count)
    across_count = lax.axis_size("narrow")
    inverse = coarse_inverse(numbers, work)
    sums = column(numbers, IMAGE_SUM)
    sums = sums - column(pltpu.roll(numbers, count - across_count, 0), FLOW_LONG_LOW)
    sums = sums - column(pltpu.roll(numbers, across_count, 0), FLOW_LONG_HIGH)
    sums = sums - column(pltpu.roll(numbers, count - 1, 0), FLOW_ACROSS_LOW)
    sums = sums - column(pltpu.roll(numbers, 1, 0), FLOW_ACROSS_HIGH)
    load_sums = column(numbers, LOAD_SUM)
    sums = load_sums * (1.0 - 1.0 / cheb_center) - sums
    out[0:1, :] = answer(inverse, load_sums) * (1.0 / cheb_center)
    out[1:2, :] = answer(inverse, sums) * gain


def second_solve(box, local, low, high, left, right, inverses, answers, *rest):
    to_long, to_across, to_deep, mass, load_window = rest[:5]
    tables = rest[5 : 5 + N_TABLES]
    iterate, top, bottom, last_col, first_col, out = rest[5 + N_TABLES : 11 + N_TABLES]
    window, spectral, middle, sems = rest[11 + N_TABLES :]
    long_pos, across_pos, long_count, across_count = position()
    coarse = answers[0:1, :]
    own_shift = at_box(answers[1:2, :], 0, 0)
    shifts = {
        (row_side, col_side): at_box(coarse, row_side, col_side)
        for row_side in (-1, 0, 1)
        for col_side in (-1, 0, 1)
    }

    def add(values, row_side, col_side):
        shift = shifts[row_side, col_side]
        if values.ndim == 3:
            shift = shift.reshape(1, 1, 1)
        return values + shift

    edge = REACH * box.across
    low, high = (
        ref.at[:edge].reshape(REACH, box.across, box.deep) for ref in (low, high)
    )
    wide_sides, narrow_sides = Sides("wide", low, high), Sides("narrow", left, right)
    fill_window(box, window, local, wide_sides, narrow_sides, REACH, 0, REACH, add)
    weights = (to_long, to_across, to_deep, mass)

    steps = range(box.ey // 8)
    x = [some_cols(box, window, 1, step) for step in range(-1, len(steps) + 1)]
    flow = [
        some_cols(box, to_long, 0, step) * (x[step + 1] - some_cols(box, window, 0, step))
        for step in steps
    ]
    state = [x, flow]

    def divided(values, col):
        return values * inverses[col]

    def residual(start_row):
        rows = []
        for row in range(start_row + 1, start_row + 9):
            image, *state[:] = negative_image(box, window, row, row, *state, weights)
            image = [some_cols(box, load_window, row, step) + image[step] for step in steps]
            rows.append(jnp.concatenate(image, axis=0))
        return jnp.stack(rows)

    inner = slice(EDGE, EDGE + box.across)
    first = REACH
    row_ids = lax.broadcasted_iota(jnp.int32, (1, padded(box.ex)), 1)
    col_ids = lax.broadcasted_iota(jnp.int32, (1, padded(box.ey)), 1)
    col_ids = (col_ids & 7) * (box.ey // 8) + lax.shift_right_logical(col_ids, 3)
    row_mask = jnp.where(row_ids < MARGIN, as_float(long_pos > 0), 1.0)
    row_mask = jnp.where(row_ids >= MARGIN + box.long, as_float(long_pos < long_count - 1), row_mask)
    col_mask = jnp.where(col_ids < MARGIN, as_float(across_pos > 0), 1.0)
    col_mask = jnp.where(
        col_ids >= MARGIN + box.across, as_float(across_pos < across_count - 1), col_mask
    )
    keep = 1.0 + rho_second * rho_first
    copies = []

    def emit(start, values):
        rows = values.reshape(8, box.across, box.deep)
        before = window[first + start : first + start + 8, inner, :]
        shift = own_shift.reshape(1, 1, 1)
        iterate[start : start + 8] = keep * before + (gain * rows + shift)
        copies.append(
            pltpu.make_async_copy(
                iterate.at[start : start + 8], out.at[start : start + 8], sems.at[len(copies)]
            )
        )
        copies[-1].start()

    box_solve(
        box, residual, divided, tables, row_mask, col_mask, spectral, middle, emit
    )
    rows = in_order(is_even("wide"), iterate[box.long - 1], iterate[0])
    top[...], bottom[...] = rows
    flat = iterate.reshape(box.long * box.across, box.deep)
    cols = [flat[row_of(box.across, col, box.long), :] for col in (box.across - 1, 0)]
    last_col[...], first_col[...] = in_order(is_even("narrow"), *cols)
    for copy in copies:
        copy.wait()


def inner_residual(
    box, load, iterate, to_long, to_across, to_deep, mass, rows, cols, out, window, result, sems
):
    inner = slice(EDGE, EDGE + box.across)
    flat = window.reshape((box.long + 2) * box.cols, box.deep)
    iterate_flat = iterate.reshape(box.long * box.across, box.deep)
    blank = jnp.zeros((box.long + 2, EDGE, box.deep), jnp.float32)
    window[:, :EDGE, :] = blank
    window[:, EDGE + box.across :, :] = blank
    window[1 : 1 + box.long, inner, :] = iterate[...]
    window[0, inner, :] = iterate[0]
    window[1 + box.long, inner, :] = iterate[box.long - 1]
    for col, place in ((0, EDGE - 1), (box.across - 1, EDGE + box.across)):
        values = iterate_flat[row_of(box.across, col, box.long), :]
        flat[row_of(box.cols, place, box.long, 1), :] = values
    weights = (to_long, to_across, to_deep, mass)
    steps = range(box.ey // 8)
    x = [some_cols(box, window, 1, step) for step in range(-1, len(steps) + 1)]
    flow = [jnp.zeros((8, box.deep), jnp.float32) for _ in steps]
    middle = slice(8, box.across - 8)
    copies = []
    for row in range(box.long):
        image, x, flow = negative_image(box, window, row + 1, REACH + row, x, flow, weights)
        for step in steps:
            place = pl.ds(EDGE - MARGIN + step, 8, stride=box.ey // 8)
            result[row, place, :] = image[step]
        values = load[row] + result[row, inner]
        result[row, inner] = values
        cols[0, row] = values[:8]
        cols[1, row] = values[box.across - 8 :]
        if row == 0:
            rows[0] = values
        if row == box.long - 1:
            rows[1] = values
        if row % 8 == 7:
            part = slice(row - 7, row + 1)
            copy = pltpu.make_async_copy(
                result.at[part, EDGE + 8 : EDGE + box.across - 8],
                out.at[part, middle],
                sems.at[row // 8],
            )
            copy.start()
            copies.append(copy)
    for copy in copies:
        copy.wait()


def outer_residual(
    box, iterate, low, high, left, right, to_long, to_across, rows, cols, inner_out, out,
    row_part, col_part, sems
):
    del inner_out
    inner = slice(EDGE, EDGE + box.across)
    middle = slice(8, box.across - 8)
    wide_sides, narrow_sides = Sides("wide", low, high), Sides("narrow", left, right)
    last = box.long - 1
    iterate_flat = iterate.reshape(box.long * box.across, box.deep)
    across_flat = to_across.reshape(box.flat, box.deep)
    below = to_long[REACH - 1, inner] * (wide_sides.low(Ellipsis) - iterate[0])
    above = to_long[REACH + last, inner] * (wide_sides.high(Ellipsis) - iterate[last])
    row_part[0] = (rows[0] + below)[middle]
    row_part[1] = (rows[1] + above)[middle]
    copies = [
        pltpu.make_async_copy(row_part.at[0], out.at[0, middle], sems.at[0]),
        pltpu.make_async_copy(row_part.at[1], out.at[last, middle], sems.at[1]),
    ]
    for copy in copies:
        copy.start()
    col_part[...] = cols[...]
    flat = col_part.reshape(2 * box.long * 8, box.deep)
    for side, (from_side, col, face, tile) in enumerate(
        (
            (narrow_sides.low, 0, EDGE - 1, slice(0, 8)),
            (narrow_sides.high, box.across - 1, EDGE + box.across - 1, slice(box.across - 8, None)),
        )
    ):
        weight = across_flat[row_of(box.cols, face, box.long, REACH), :]
        own = iterate_flat[row_of(box.across, col, box.long), :]
        place = pl.ds(side * box.long * 8 + side * 7, box.long, stride=8)
        flat[place, :] = flat[place, :] + weight * (from_side(Ellipsis) - own)
        col_part[side, 0] = col_part[side, 0] + below[tile]
        col_part[side, last] = col_part[side, last] + above[tile]
        first_col = side * (box.across - 8)
        copy = pltpu.make_async_copy(
            col_part.at[side], out.at[:, first_col : first_col + 8], sems.at[2 + side]
        )
        copy.start()
        copies.append(copy)
    for copy in copies:
        copy.wait()


def swaps(axis):
    sizes = (lax.axis_size("wide"), lax.axis_size("narrow"))
    along = ("wide", "narrow").index(axis)
    size, beside = sizes[along], sizes[1 - along]

    def number(place, other_place):
        pair = (place, other_place) if along == 0 else (other_place, place)
        return pair[0] * sizes[1] + pair[1]

    ways = []
    for way in range(2):
        pairs = []
        for place in range(size):
            for other_place in range(beside):
                partner = place + 1 if place % 2 == way else place - 1
                there = other_place
                if not 0 <= partner < size:
                    partner = place
                    there = other_place ^ 1 if beside % 2 == 0 else other_place
                pairs.append((number(place, other_place), number(partner, there)))
        ways.append(pairs)
    return ways


def exchange(axis, first, second):
    ways = swaps(axis)
    axes = ("wide", "narrow")
    return lax.ppermute(first, axes, ways[0]), lax.ppermute(second, axes, ways[1])


def two_away(axis, table):
    size = lax.axis_size(axis)
    return lax.ppermute(table, axis, [(i, (i + 2) % size) for i in range(size)])


def tell(table):
    count = table.shape[0]
    long_pos, across_pos, _, across_count = position()
    own = lax.dynamic_slice_in_dim(table, long_pos * across_count + across_pos, 1, axis=0)
    line = jnp.broadcast_to(own, (count, 1, 128))
    told = lax.all_to_all(line, ("wide", "narrow"), split_axis=0, concat_axis=0, tiled=True)
    return told.reshape(count, 128)


def on_device(zone, scale, diffusivity, decay, load):
    box = Box(load.shape)
    long, across, deep = load.shape
    count = lax.axis_size("wide") * lax.axis_size("narrow")
    by_margins = lax.axis_size("wide") == 4 and lax.axis_size("narrow") == 4
    tables = tables_of(box)
    decay = decay.reshape(1, -1)
    cells = f32(long, across, deep)
    whole_zone = jax.ShapeDtypeStruct(cells.shape, zone.dtype)
    window = f32(box.rows, box.cols, deep)
    table_shape = f32(count, 128)
    anywhere = pl.BlockSpec(memory_space=pl.ANY)
    in_hbm = pl.BlockSpec(memory_space=pltpu.HBM)

    def scratch(shape):
        return pltpu.VMEM(shape, jnp.float32)

    def pinned(field):
        return pltpu.with_memory_space_constraint(field, pltpu.HBM)

    spectral = scratch((box.ey, padded(box.ex), deep))
    middle = scratch((long, padded(box.ey), deep))

    def pack(wide, fields, sides, parts=(), after=()):
        rows = message_rows(box, wide * len(fields)) + (count if parts else 0)
        message = f32(rows, deep)
        body = functools.partial(pack_fields, box, wide, len(fields), len(parts), len(after))
        return call(
            body,
            (message, message) + ((table_shape,) if parts else ()),
            [VMEM] * (len(fields) + 2 + len(parts)) + [anywhere] * len(after),
        )(*fields, *sides, *parts, *after)

    far = f32(2 * REACH, across, deep)
    far_zone, far_scale, far_load = pinned(zone), pinned(scale), pinned(load)
    load_first, load_second, first, second = call(
        functools.partial(bring_edges, box),
        (f32(MARGIN, across, deep),) * 2 + (far, far),
        [in_hbm] * 3,
        [pltpu.VMEM((2, REACH, across, deep), zone.dtype), pltpu.SemaphoreType.DMA((6,))],
    )(far_zone, far_scale, far_load)
    load, scale, zone, sums, table = call(
        functools.partial(bring_box, box),
        (cells, cells, whole_zone, f32(8, 128), table_shape),
        [in_hbm] * 3 + [anywhere] + [VMEM] * 2,
        [pltpu.SemaphoreType.DMA((3 * (long // 8),))],
    )(far_load, far_scale, far_zone, load_first, diffusivity, decay)
    load_wide = exchange("wide", load_first, load_second)
    far_wide = exchange("wide", first, second)
    load_first, load_second = pack(MARGIN, [load], load_wide)
    load_narrow = exchange("narrow", load_first, load_second)
    far_narrow = exchange("narrow", *pack(REACH, [scale, zone], far_wide))
    message = f32(REACH * across, deep)
    load_window, local, image, inverses, first, second = call(
        functools.partial(first_solve, box),
        (window, cells, f32(across, deep), f32(box.ey, box.ex, deep), message, message),
        [VMEM] * 8 + [VMEM] * 2 + [VMEM] * N_TABLES,
        [spectral, middle],
        flops=4 * 10**9,
    )(load, *load_wide, *load_narrow, sums, zone, scale, diffusivity, decay, *tables)
    wide = exchange("wide", first, second)
    table = call(functools.partial(image_sums, box), table_shape, [VMEM] * 10)(
        zone, scale, local, image, *far_wide, *far_narrow, table, diffusivity
    )
    own_table = table
    if by_margins:
        more = lax.ppermute(table, ("wide", "narrow"), swaps("narrow")[0])
        table = call(join_rows, table_shape, [VMEM] * 2)(table, more)
        table = call(join_rows, table_shape, [VMEM] * 2)(table, two_away("narrow", table))
        narrow_table = table
        more = lax.ppermute(table, ("wide", "narrow"), swaps("wide")[0])
        table = call(join_rows, table_shape, [VMEM] * 2)(table, more)
        parts = (table, two_away("wide", table))
    else:
        narrow_table = table
        parts = (tell(own_table),)
    to_long, to_across, *windows = call(
        functools.partial(side_weights, box),
        (window,) * 4,
        [VMEM] * 6 + [VMEM],
        flops=10**9,
    )(zone, scale, *far_wide, *far_narrow, diffusivity)
    to_deep, mass = call(
        functools.partial(deep_weights, box),
        (window,) * 2,
        [VMEM] * 2 + [VMEM] * 2,
        flops=10**9,
    )(*windows, diffusivity, decay)
    weights = (to_long, to_across, to_deep, mass)
    first, second = pack(REACH, [local], wide, after=[to_long, narrow_table])
    narrow = exchange("narrow", first, second)
    row, col = f32(across, deep), f32(long, deep)
    answers = call(
        functools.partial(coarse_corrections, len(parts)),
        f32(8, -(-count // 128) * 128),
        [VMEM] * len(parts),
        [scratch((count, -(-2 * count // 128) * 128))],
    )(*parts)
    iterate, first_row, second_row, first_col, second_col, result = call(
        functools.partial(second_solve, box),
        (cells, row, row, col, col, cells),
        [VMEM] * (12 + N_TABLES),
        [scratch(window.shape), spectral, middle, pltpu.SemaphoreType.DMA((long // 8,))],
        flops=4 * 10**9,
        out_spec=(VMEM,) * 5 + (anywhere,),
    )(local, *wide, *narrow, inverses, answers, *weights, load_window, *tables)
    narrow = exchange("narrow", first_col, second_col)
    wide = exchange("wide", first_row, second_row)
    rows, cols, inner = call(
        functools.partial(inner_residual, box),
        (f32(2, across, deep), f32(2, long, 8, deep), cells),
        [VMEM] * 6,
        [
            scratch((long + 2, box.cols, deep)),
            scratch((long, box.cols, deep)),
            pltpu.SemaphoreType.DMA((long // 8,)),
        ],
        flops=10**9,
        out_spec=(VMEM, VMEM, anywhere),
    )(load, iterate, *weights)
    residual = call(
        functools.partial(outer_residual, box),
        cells,
        [VMEM] * 9 + [anywhere],
        [
            scratch((2, across - 16, deep)),
            scratch((2, long, 8, deep)),
            pltpu.SemaphoreType.DMA((4,)),
        ],
        out_spec=anywhere,
        aliases={9: 0},
    )(iterate, *wide, *narrow, to_long, to_across, rows, cols, inner)
    return result, residual


def solution(mesh):
    split = P(("groups", "wide"), "narrow", None)
    return jax.shard_map(
        on_device,
        mesh=mesh,
        in_specs=(split, split, P(), P(), split),
        out_specs=(split, split),
        check_vma=False,
    )
```
